32 devices in a mesh: dp: 4 (over y, core), row: 2 (over x), col: 4 (over z).
Axes of the slice: x: 2, y: 2, z: 4, core: 2. Of those that a mesh axis runs over, the one named last changes fastest.
Arguments:
- tokens: bfloat16 [16, 1024, 2048], P('dp', 'row', 'col'), may hold values from -6 to 6
- cotangent: bfloat16 [16, 1024, 2048], P('dp', 'row', 'col'), may hold values from -6 to 6
- lengths: int32 [16], replicated, may hold values from 512 to 1024, as said below
- deal_order: int32 [16], replicated, may hold values from 0 to 15, as said below
- gain_attn: bfloat16 [2048], replicated, may hold values from 0.25 to 1.75
- gain_ffn: bfloat16 [2048], replicated, may hold values from 0.25 to 1.75
- w_query: bfloat16 [2048, 2048], P('row', 'col'), may hold values from -0.4375 to 0.4375
- key_value_weight: bfloat16 [2048, 2, 512], P('row', None, 'col'), may hold values from -0.4375 to 0.4375
- w_out: bfloat16 [2048, 2048], P('row', 'col'), may hold values from -1.25 to 1.25
- w_gate_up: bfloat16 [2048, 2, 8192], P('row', None, 'col'), may hold values from -0.125 to 0.125
- w_down: bfloat16 [2048, 8192], P('row', 'col'), may hold values from -0.25 to 0.25
Outputs:
- layer_out: float32 [16, 1024, 2048], P('dp', 'row', 'col')
- input_grad: float32 [16, 1024, 2048], P('dp', 'row', 'col')
- grad_query: float32 [2048, 2048], P(('dp', 'row'), 'col')
- grad_kv: float32 [2048, 2, 512], P(('dp', 'row'), None, 'col')
- grad_out: float32 [2048, 2048], P(('dp', 'row'), 'col')
- grad_gate_up: float32 [2048, 2, 8192], P(('dp', 'row'), None, 'col')
- grad_down: float32 [2048, 8192], P(('dp', 'row'), 'col')
- grad_gain_attn: float32 [2048], replicated
- grad_gain_ffn: float32 [2048], replicated
The draws below stay inside these ranges and needn't reach their ends.
Inputs may be any that keep to these rules, and one draw needn't show every extreme that they name: `lengths`: among the 4 sequences that deal_order gives each data group, at least one has length exactly 1024. `deal_order`: A permutation of the sequence numbers.
All inputs are finite; a program needn't handle non-finite values.
Results may differ from the reference program's by a relative error of at most 0.018.
Values may be sent and summed in bfloat16 or wider, within the bound.
A program may use at most 256 MiB of HBM per device.

```python
import jax
import jax.numpy as jnp
from jax import lax

MODEL_WIDTH = 2048
QUERY_HEADS = 32
VALUE_KEY_HEADS = 8
HEAD_SIZE = 64
FF = 8192
SEQ_G = 4
L = 1024
SEQS = 16


def dealing(key):
    return jax.random.permutation(jax.random.fold_in(key, 11), SEQS).astype(jnp.int32)


def draw_deal_order(key, part):
    order = dealing(key)
    return order


def draw_lengths(key, part):
    order = dealing(key)
    key = jax.random.fold_in(key, 2)
    base = jax.random.randint(jax.random.fold_in(key, 3), (SEQS,), L // 2, L + 1)
    picked = jax.random.randint(jax.random.fold_in(key, 4), (SEQS // SEQ_G,), 0, SEQ_G)
    longest = order[jnp.arange(SEQS // SEQ_G) * SEQ_G + picked]
    return base.at[longest].set(L).astype(jnp.int32)


def shard_levels(key, shape, shards, smallest, top_value):
    level = 1.0
    for axis_at, parts in shards:
        steps = jax.random.uniform(jax.random.fold_in(jax.random.fold_in(key, 6), axis_at), (parts,), jnp.float32, smallest / len(shards), top_value / len(shards))
        level = level * jnp.repeat(jnp.exp(steps), shape[axis_at] // parts).reshape((-1,) + (1,) * (len(shape) - 1 - axis_at))
    return level


def normal_values(own_key, extent, scale, limit, cuts=(), held_as=jnp.bfloat16):
    entries = jax.random.normal(own_key, extent, jnp.float32) * scale
    if len(cuts) > 0:
        entries = shard_levels(own_key, extent, cuts, -0.22, 0.18) * entries
    return jnp.clip(entries, min=-limit, max=limit).astype(held_as)


def setup_inputs(seed: int = 0) -> dict:
    keys = jax.random.split(jax.random.key(seed), 12)
    return {
        "tokens": normal_values(keys[0], (SEQS, L, MODEL_WIDTH), 1.0, 6.0, ((0, 4), (1, 2), (2, 4))),
        "cotangent": normal_values(keys[1], (SEQS, L, MODEL_WIDTH), 1.0, 6.0, ((0, 4), (1, 2), (2, 4))),
        "lengths": draw_lengths(jax.random.fold_in(keys[11], 71), 0),
        "deal_order": draw_deal_order(jax.random.fold_in(keys[11], 71), 0),
        "gain_attn": jnp.clip(1.0 + 0.15 * jax.random.normal(keys[4], (MODEL_WIDTH,), jnp.float32), 0.25, 1.75).astype(jnp.bfloat16),
        "gain_ffn": jnp.clip(1.0 + 0.15 * jax.random.normal(keys[5], (MODEL_WIDTH,), jnp.float32), 0.25, 1.75).astype(jnp.bfloat16),
        "w_query": normal_values(keys[6], (MODEL_WIDTH, QUERY_HEADS * HEAD_SIZE), (MODEL_WIDTH // 12) ** -0.5, 0.4375, ((0, 2), (1, 4))),
        "key_value_weight": normal_values(keys[7], (MODEL_WIDTH, 2, VALUE_KEY_HEADS * HEAD_SIZE), (MODEL_WIDTH // 12) ** -0.5, 0.4375, ((0, 2), (2, 4))),
        "w_out": normal_values(keys[8], (MODEL_WIDTH, QUERY_HEADS * HEAD_SIZE), 24 ** -0.5, 1.25, ((0, 2), (1, 4))),
        "w_gate_up": normal_values(keys[9], (MODEL_WIDTH, 2, FF), MODEL_WIDTH ** -0.5, 0.125, ((0, 2), (2, 4))),
        "w_down": normal_values(keys[10], (MODEL_WIDTH, FF), (FF // 16) ** -0.5, 0.25, ((0, 2), (1, 4))),
    }


EPSILON = 1e-05
THETA = 10000000.0
ATTN_MULT = 0.015625
RES_MULT = 0.22
MASKED = -1e+30

@jax.custom_vjp
def lower_precision(v):
    return lax.optimization_barrier(v.astype(jnp.bfloat16)).astype(jnp.float32)

@jax.custom_vjp
def lower_precision_grad(v):
    return v

def low_keep(v):
    return (lower_precision(v), None)

def low_pass(kept, grad):
    return (grad,)

def back_keep(v):
    return (v, None)

def back_low(kept, grad):
    return (lower_precision(grad),)
lower_precision.defvjp(low_keep, low_pass)
lower_precision_grad.defvjp(back_keep, back_low)

def rope_tables(positions, head_size):
    halves = jnp.arange(head_size // 2, dtype=jnp.float32)
    inverse_freq = THETA ** (-(halves * 2.0) / head_size)
    angles = positions.astype(jnp.float32)[:, None] * inverse_freq[None, :]
    return (jnp.cos(angles), jnp.sin(angles))

def rotary_embed(value_rows, cosine_table, sine_table):
    middle = value_rows.shape[-1] // 2
    first_half = value_rows[..., :middle]
    second_half = value_rows[..., middle:]
    cos_part = cosine_table[:, None, :]
    sin_part = sine_table[:, None, :]
    return jnp.concatenate([first_half * cos_part - second_half * sin_part, second_half * cos_part + first_half * sin_part], axis=-1)

def product_highest(left_side, right_side):
    return jnp.dot(left_side, right_side, precision=lax.Precision.HIGHEST)

def attention_block(query_block, key_rows, value_rows, block_start, length):
    key_pos = jnp.arange(key_rows.shape[0], dtype=jnp.int32)
    query_pos = block_start + jnp.arange(query_block.shape[0], dtype=jnp.int32)
    scores = jnp.einsum('qkgd,tkd->kgqt', query_block, key_rows, precision=lax.Precision.HIGHEST) * ATTN_MULT
    scores = lower_precision_grad(scores)
    allowed = (key_pos[None, :] <= query_pos[:, None]) & (key_pos[None, :] < length)
    scores = jnp.where(allowed, scores, MASKED)
    row_max = lax.optimization_barrier(jnp.max(scores, axis=-1, keepdims=True))
    exponent = jnp.exp(scores - row_max)
    weights = exponent / lax.optimization_barrier(jnp.sum(exponent, axis=-1, keepdims=True))
    return jnp.einsum('kgqt,tkd->qkgd', lower_precision(weights), value_rows, precision=lax.Precision.HIGHEST)

def layer(tokens_seq, length, gain_attn, gain_ffn, w_query, key_value_weight, w_out, w_gate_up, w_down):
    sequence_length = tokens_seq.shape[0]
    positions = jnp.arange(sequence_length, dtype=jnp.int32)
    cosine_table, sine_table = rope_tables(positions, HEAD_SIZE)
    live_rows = (positions < length).astype(jnp.float32)[:, None]
    scale_one = lax.rsqrt(lax.optimization_barrier(jnp.mean(tokens_seq * tokens_seq, axis=1, keepdims=True)) + EPSILON)
    first_normed = lower_precision(tokens_seq * scale_one * gain_attn)
    query_rows = lower_precision(rotary_embed(lower_precision_grad(product_highest(first_normed, w_query)).reshape(sequence_length, QUERY_HEADS, HEAD_SIZE), cosine_table, sine_table))
    key_rows = lower_precision(rotary_embed(lower_precision_grad(product_highest(first_normed, key_value_weight[:, 0])).reshape(sequence_length, VALUE_KEY_HEADS, HEAD_SIZE), cosine_table, sine_table))
    value_rows = lower_precision(lower_precision_grad(product_highest(first_normed, key_value_weight[:, 1]))).reshape(sequence_length, VALUE_KEY_HEADS, HEAD_SIZE)
    block_width = min(512, sequence_length)
    query_block_list = query_rows.reshape(sequence_length // block_width, block_width, VALUE_KEY_HEADS, QUERY_HEADS // VALUE_KEY_HEADS, HEAD_SIZE)
    starts = jnp.arange(sequence_length // block_width, dtype=jnp.int32) * block_width

    def one_block(entry):
        return attention_block(entry[0], key_rows, value_rows, entry[1], length)
    mixed_heads = lax.map(jax.checkpoint(one_block), (query_block_list, starts))
    heads_out = lower_precision(lower_precision_grad(mixed_heads.reshape(sequence_length, QUERY_HEADS * HEAD_SIZE)))
    attn_branch = lower_precision_grad(product_highest(heads_out, w_out.T))
    resid = tokens_seq + RES_MULT * attn_branch
    scale_two = lax.rsqrt(lax.optimization_barrier(jnp.mean(resid * resid, axis=1, keepdims=True)) + EPSILON)
    normed_two = lower_precision(resid * scale_two * gain_ffn)
    gate = lower_precision_grad(product_highest(normed_two, w_gate_up[:, 0]))
    upward = lower_precision_grad(product_highest(normed_two, w_gate_up[:, 1]))
    hidden = lower_precision(jax.nn.silu(gate) * upward)
    ffn_branch = lower_precision_grad(product_highest(hidden, w_down.T))
    return live_rows * (resid + RES_MULT * ffn_branch)

def reference(tokens, cotangent, lengths, deal_order, gain_attn, gain_ffn, w_query, key_value_weight, w_out, w_gate_up, w_down):
    params = tuple((item.astype(jnp.float32) for item in (gain_attn, gain_ffn, w_query, key_value_weight, w_out, w_gate_up, w_down)))
    slots = jnp.arange(SEQS, dtype=jnp.int32)
    inverse = lax.optimization_barrier(jnp.sum(jnp.where(deal_order[None, :] == slots[:, None], slots[None, :], 0), axis=1)).astype(jnp.int32)
    given_cot = jnp.take(cotangent, inverse, axis=0)

    def step(totals, entry):
        tokens_seq, cot_seq, length = entry

        def run(tokens_in, *weights):
            return layer(tokens_in, length, *weights)
        output, pull_back = jax.vjp(run, tokens_seq.astype(jnp.float32), *params)
        grads = pull_back(cot_seq.astype(jnp.float32))
        new_totals = tuple((running + fresh for running, fresh in zip(totals, grads[1:])))
        return (new_totals, (output, grads[0]))
    initial = tuple((jnp.zeros_like(item) for item in params))
    totals, (outputs, input_grads) = lax.scan(step, initial, (tokens, given_cot, lengths))
    return (outputs, input_grads, totals[2], totals[3], totals[4], totals[5], totals[6], totals[0], totals[1])
```

```python
import functools

import jax
import jax.numpy as jnp
from jax import lax
from jax.experimental import pallas as pl
from jax.experimental.pallas import tpu as pltpu
from jax.sharding import PartitionSpec as P

HEAD_SIZE = 64


EPSILON = 1e-05
THETA = 10000000.0
ATTN_MULT = 0.015625
RES_MULT = 0.22
MASKED = -1e30


def rope_tables(positions, head_size):
    halves = jnp.arange(head_size // 2, dtype=jnp.float32)
    inverse_freq = THETA ** (-(halves * 2.0) / head_size)
    angles = positions.astype(jnp.float32)[:, None] * inverse_freq[None, :]
    return (jnp.cos(angles), jnp.sin(angles))


def rotary_embed(value_rows, cosine_table, sine_table):
    middle = value_rows.shape[-1] // 2
    first_half = value_rows[..., :middle]
    second_half = value_rows[..., middle:]
    cos_part = cosine_table[:, None, :]
    sin_part = sine_table[:, None, :]
    return jnp.concatenate(
        [
            first_half * cos_part - second_half * sin_part,
            second_half * cos_part + first_half * sin_part,
        ],
        axis=-1,
    )


def widen_cols(value_rows):
    return lax.all_gather(value_rows, "col", axis=1, tiled=True)


def narrow_cols(value_rows):
    return lax.psum_scatter(value_rows, "col", scatter_dimension=1, tiled=True)


def sum_over_cols(value_rows):
    return lax.psum(value_rows, "col")


def contract_local(operand, matrix):
    return lax.dot_general(
        operand, matrix, (((1,), (0,)), ((), ())), preferred_element_type=jnp.float32
    )


def expand_local(operand, matrix):
    trailing = tuple(range(1, operand.ndim))
    return lax.dot_general(
        operand, matrix, ((trailing, trailing), ((), ())), preferred_element_type=jnp.float32
    )


def token_outer(features, grads):
    return lax.dot_general(
        features, grads, (((0,), (0,)), ((), ())), preferred_element_type=jnp.float32
    )


def contract_rows(operand, matrix):
    return contract_local(operand, lax.all_gather(matrix, "row", axis=0, tiled=True))


def expand_rows(operand, matrix):
    return expand_local(operand, lax.all_gather(matrix, "row", axis=0, tiled=True))


def split_keys(key_seq, value_seq, key_pos):
    slot_len = key_seq.shape[0]
    width = min(512, slot_len)
    count = slot_len // width
    return (
        key_seq.reshape(count, width, key_seq.shape[1], key_seq.shape[2]),
        value_seq.reshape(count, width, value_seq.shape[1], value_seq.shape[2]),
        key_pos.reshape(count, width),
    )


def block_scores(query_seq, key_block, pos_block, query_pos, length):
    scores = (
        jnp.einsum("qkgd,tkd->kgqt", query_seq, key_block, preferred_element_type=jnp.float32)
        * ATTN_MULT
    )
    allowed = (pos_block[None, :] <= query_pos[:, None]) & (pos_block[None, :] < length)
    return jnp.where(allowed, scores, MASKED)


def attend(inputs, key_pos, query_pos):
    query_seq, key_seq, value_seq, length = inputs
    key_blocks, value_blocks, pos_blocks = split_keys(key_seq, value_seq, key_pos)
    stat_shape = (query_seq.shape[1], query_seq.shape[2], query_seq.shape[0], 1)

    def gather_stats(carry, entry):
        running_max, running_sum = carry
        key_block, pos_block = entry
        scores = block_scores(query_seq, key_block, pos_block, query_pos, length)
        new_max = jnp.maximum(running_max, jnp.max(scores, axis=-1, keepdims=True))
        new_sum = running_sum * jnp.exp(running_max - new_max) + jnp.sum(
            jnp.exp(scores - new_max), axis=-1, keepdims=True
        )
        return ((new_max, new_sum), None)

    start_stats = (jnp.full(stat_shape, MASKED, jnp.float32), jnp.zeros(stat_shape, jnp.float32))
    (row_max, row_sums), unused = lax.scan(gather_stats, start_stats, (key_blocks, pos_blocks))

    def mix_values(running, entry):
        key_block, value_block, pos_block = entry
        scores = block_scores(query_seq, key_block, pos_block, query_pos, length)
        weights = jnp.exp(scores - row_max) / row_sums
        return (
            running
            + jnp.einsum(
                "kgqt,tkd->qkgd",
                weights.astype(jnp.bfloat16),
                value_block,
                preferred_element_type=jnp.float32,
            ),
            None,
        )

    start_mix = jnp.zeros(query_seq.shape, jnp.float32)
    mixed_heads, unused = lax.scan(mix_values, start_mix, (key_blocks, value_blocks, pos_blocks))
    return (mixed_heads, row_max, row_sums)


def attend_back(inputs, key_pos, query_pos):
    query_seq, key_seq, value_seq, grad_mixed, row_max, row_sums, length = inputs
    key_blocks, value_blocks, pos_blocks = split_keys(key_seq, value_seq, key_pos)

    def block_weights(key_block, value_block, pos_block):
        scores = block_scores(query_seq, key_block, pos_block, query_pos, length)
        weights = jnp.exp(scores - row_max) / row_sums
        grad_weights = jnp.einsum(
            "qkgd,tkd->kgqt", grad_mixed, value_block, preferred_element_type=jnp.float32
        )
        return (weights, grad_weights)

    def gather_centre(running, entry):
        weights, grad_weights = block_weights(*entry)
        return (running + jnp.sum(weights * grad_weights, axis=-1, keepdims=True), None)

    start_centre = jnp.zeros(row_max.shape, jnp.float32)
    centre, unused = lax.scan(gather_centre, start_centre, (key_blocks, value_blocks, pos_blocks))

    def grads_block(running, entry):
        key_block = entry[0]
        weights, grad_weights = block_weights(*entry)
        grad_scores = (weights * (grad_weights - centre)).astype(jnp.bfloat16)
        grad_query = (
            running
            + jnp.einsum(
                "kgqt,tkd->qkgd", grad_scores, key_block, preferred_element_type=jnp.float32
            )
            * ATTN_MULT
        )
        grad_key = (
            jnp.einsum("kgqt,qkgd->tkd", grad_scores, query_seq, preferred_element_type=jnp.float32)
            * ATTN_MULT
        )
        grad_value = jnp.einsum(
            "kgqt,qkgd->tkd",
            weights.astype(jnp.bfloat16),
            grad_mixed,
            preferred_element_type=jnp.float32,
        )
        return (grad_query, (grad_key, grad_value))

    start_query = jnp.zeros(query_seq.shape, jnp.float32)
    grad_query, (grad_key, grad_value) = lax.scan(
        grads_block, start_query, (key_blocks, value_blocks, pos_blocks)
    )
    return (grad_query, grad_key.reshape(key_seq.shape), grad_value.reshape(value_seq.shape))


MESH_IDS = pl.DeviceIdType.MESH
SIBLINGS = [(0, 1), (1, 0), (2, 3), (3, 2)]
OVER_X = [(0, 1), (1, 0)]
CROSSED = [((2 * y + c) * 2 + x, (2 * y + x) * 2 + c) for y in (0, 1) for c in (0, 1) for x in (0, 1)]
SAME_CORE = [[0, 2], [1, 3]]


def bring_cotangent(cotangent, deal_order, first):
    everyone = lax.all_gather(cotangent, "dp", axis=0, tiled=True)
    slots = jnp.arange(deal_order.shape[0], dtype=jnp.int32)
    inverse = jnp.sum(jnp.where(deal_order[None, :] == slots[:, None], slots[None, :], 0), axis=1)
    return jnp.concatenate(
        [
            lax.dynamic_slice_in_dim(
                everyone, lax.dynamic_index_in_dim(inverse, first + at, keepdims=False), 1
            )
            for at in range(cotangent.shape[0])
        ]
    )


def place():
    group = lax.axis_index("dp")
    core = lax.rem(group, 2)
    row = lax.axis_index("row")
    return group, core, group - core + row, row, lax.axis_index("col")


def start_kernel(
    cols, tok_ref, pq_ref, po_ref, x_ref, wq_ref, wo_ref, tok_sems, q_sems, o_sems, qx_sems, ox_sems, local_sems
):
    group, core, mate, row, col = place()
    width = tok_ref.shape[2]
    weight_rows = pq_ref.shape[0]

    def line(step):
        return lax.rem(col + step + cols, cols)

    def start_at(block, size):
        return pl.ds(pl.multiple_of(block * size, size), size)

    barrier = pltpu.get_barrier_semaphore()

    def greet(device):
        pl.semaphore_signal(barrier, inc=1, device_id=device, device_id_type=MESH_IDS)

    for step in range(1, cols):
        greet((mate, core, line(step)))
        greet((group, row, line(step)))
    greet((group, 1 - row, col))

    @pl.when(core != row)
    def _():
        greet((mate, core, col))

    pl.semaphore_wait(barrier, 2 * cols - 1 + (core - row) * (core - row))

    def remote(src, dst, sems, at, device):
        return pltpu.make_async_remote_copy(
            src_ref=src,
            dst_ref=dst,
            send_sem=sems.at[0, at],
            recv_sem=sems.at[1, at],
            device_id=device,
            device_id_type=MESH_IDS,
        )

    def weight_copies(own, full, sems, x_sems):
        wide = own.shape[1]

        def block(of_row, of_col):
            return full.at[start_at(of_row, weight_rows), start_at(of_col, wide)]

        along = [
            remote(own, block(row, col), sems, step, (group, row, line(step)))
            for step in range(1, cols)
        ]
        arrive = [
            remote(own, block(row, line(-step)), sems, step, (group, row, line(step)))
            for step in range(1, cols)
        ]
        across = [remote(own, block(row, col), x_sems, 0, (group, 1 - row, col))] + [
            remote(block(row, line(-step)), block(row, line(-step)), x_sems, step, (group, 1 - row, col))
            for step in range(1, cols)
        ]
        landed = [
            remote(own, block(1 - row, line(-step)), x_sems, step, (group, 1 - row, col))
            for step in range(cols)
        ]
        return along, arrive, across, landed, block(row, col)

    q_along, q_arrive, q_across, q_landed, q_own = weight_copies(pq_ref, wq_ref, q_sems, qx_sems)
    o_along, o_arrive, o_across, o_landed, o_own = weight_copies(po_ref, wo_ref, o_sems, ox_sems)
    own_q = pltpu.make_async_copy(pq_ref, q_own, local_sems.at[0])
    own_o = pltpu.make_async_copy(po_ref, o_own, local_sems.at[1])

    def token_copy(step, into):
        return remote(
            tok_ref.at[line(step)],
            x_ref.at[:, start_at(into, width)],
            tok_sems,
            step,
            (mate, core, line(step)),
        )

    own_tokens = pltpu.make_async_copy(
        tok_ref.at[col], x_ref.at[:, start_at(col, width)], local_sems.at[2]
    )
    for step in range(1, cols):
        token_copy(step, col).start()

    @pl.when(core != row)
    def _():
        token_copy(0, col).start()

    @pl.when(core == row)
    def _():
        own_tokens.start()

    for copy in q_along:
        copy.start()
    q_across[0].start()
    own_q.start()
    own_o.start()
    for copy in o_along:
        copy.start()
    o_across[0].start()
    for step in range(1, cols):
        q_arrive[step - 1].wait_recv()
        q_across[step].start()
    for step in range(1, cols):
        o_arrive[step - 1].wait_recv()
        o_across[step].start()
    for step in range(1, cols):
        token_copy(step, line(-step)).wait_recv()
        token_copy(step, col).wait_send()

    @pl.when(core != row)
    def _():
        token_copy(0, col).wait_recv()
        token_copy(0, col).wait_send()

    @pl.when(core == row)
    def _():
        own_tokens.wait()

    own_q.wait()
    own_o.wait()
    for copy in q_along + o_along + q_across + o_across:
        copy.wait_send()
    for copy in q_landed + o_landed:
        copy.wait_recv()


def start_exchange(tokens, pack_q, pack_o, rows, cols):
    anywhere = pl.BlockSpec(memory_space=pl.ANY)
    seqs, length, width = tokens.shape
    weight_rows = pack_q.shape[0]
    return pl.pallas_call(
        functools.partial(start_kernel, cols),
        out_shape=(
            jax.ShapeDtypeStruct((length, width * cols), tokens.dtype),
            jax.ShapeDtypeStruct((weight_rows * rows, pack_q.shape[1] * cols), pack_q.dtype),
            jax.ShapeDtypeStruct((weight_rows * rows, pack_o.shape[1] * cols), pack_o.dtype),
        ),
        in_specs=[anywhere] * 3,
        out_specs=(anywhere,) * 3,
        scratch_shapes=[pltpu.SemaphoreType.DMA((2, cols))] * 5 + [pltpu.SemaphoreType.DMA((3,))],
        compiler_params=pltpu.CompilerParams(collective_id=1, has_side_effects=True),
        name="start_exchange",
    )(tokens, pack_q, pack_o)


def half_turn(wide):
    lanes = wide.shape[1]
    half = HEAD_SIZE // 2
    lane = lax.broadcasted_iota(jnp.int32, wide.shape, 1)
    return jnp.where(
        lax.rem(lane, HEAD_SIZE) < half,
        pltpu.roll(wide, lanes - half, 1),
        pltpu.roll(wide, half, 1),
    )


def both_heads(pair):
    lane = lax.broadcasted_iota(jnp.int32, pair.shape, 1)
    turned = pltpu.roll(pair, HEAD_SIZE, 1)
    low = lane < HEAD_SIZE
    return jnp.where(low, pair, turned), jnp.where(low, turned, pair)


def keep_head(pair, side):
    lane = lax.broadcasted_iota(jnp.int32, pair.shape, 1)
    mine = lane < HEAD_SIZE if side == 0 else lane >= HEAD_SIZE
    return jnp.where(mine, pair, jnp.zeros_like(pair))


def dot_nn(a, b):
    return lax.dot_general(a, b, (((1,), (0,)), ((), ())), preferred_element_type=jnp.float32)


def dot_nt(a, b):
    return lax.dot_general(a, b, (((1,), (1,)), ((), ())), preferred_element_type=jnp.float32)


def dot_tn(a, b):
    return lax.dot_general(a, b, (((0,), (0,)), ((), ())), preferred_element_type=jnp.float32)


PAIR = 2 * HEAD_SIZE


def attend_kernel(block, len_ref, a_ref, w_ref, cos_ref, sin_ref, qkv_ref, z_ref, q_all, k_two, v_two):
    rows = a_ref.shape[0]
    heads = q_all.shape[0]
    length = len_ref[0]

    @pl.loop(0, rows // block)
    def _(at):
        here = pl.ds(pl.multiple_of(at * block, block), block)
        lin = dot_nn(a_ref[here, :], w_ref[...])
        for part in range(heads // 2 + 1):
            lanes = slice(part * PAIR, (part + 1) * PAIR)
            now = lin[:, lanes]
            now = now * cos_ref[here, lanes] + half_turn(now) * sin_ref[here, lanes]
            qkv_ref[here, lanes] = now.astype(jnp.bfloat16)
            if part < heads // 2:
                for side in range(2):
                    q_all[2 * part + side, here, :] = keep_head(now * ATTN_MULT, side).astype(
                        jnp.bfloat16
                    )
            else:
                keys, values = both_heads(now)
                k_two[here, :] = keys.astype(jnp.bfloat16)
                v_two[here, :] = values.astype(jnp.bfloat16)

    for at in range(rows // block):
        here = slice(at * block, (at + 1) * block)
        upto = (at + 1) * block
        row = lax.broadcasted_iota(jnp.int32, (block, upto), 0) + at * block
        key = lax.broadcasted_iota(jnp.int32, (block, upto), 1)
        allowed = key < jnp.minimum(row + 1, length)

        def one_head(head):
            scores = dot_nt(q_all[head, here, :], k_two[:upto, :])
            scores = jnp.where(allowed, scores, MASKED)
            top = jnp.max(scores, axis=1, keepdims=True)
            power = jnp.exp(scores - top)
            total = jnp.sum(power, axis=1, keepdims=True)
            return dot_nn(power.astype(jnp.bfloat16), v_two[:upto, :]) / total

        for pair in range(heads // 2):
            low = one_head(2 * pair)
            high = one_head(2 * pair + 1)
            lane = lax.broadcasted_iota(jnp.int32, low.shape, 1)
            z_ref[here, pair * PAIR : (pair + 1) * PAIR] = jnp.where(
                lane < HEAD_SIZE, low, high
            ).astype(jnp.bfloat16)


def attend_fast(length, inputs, weights, cosines, sines, groups):
    rows, depth = inputs.shape
    wide = weights.shape[1] // groups
    heads = (wide - PAIR) // HEAD_SIZE
    block = min(256, rows)
    return pl.pallas_call(
        functools.partial(attend_kernel, block),
        grid=(groups,),
        out_shape=(
            jax.ShapeDtypeStruct((rows, groups * wide), jnp.bfloat16),
            jax.ShapeDtypeStruct((rows, groups * heads * HEAD_SIZE), jnp.bfloat16),
        ),
        in_specs=[
            pl.BlockSpec(memory_space=pltpu.SMEM),
            pl.BlockSpec((rows, depth), lambda g: (0, 0)),
            pl.BlockSpec((depth, wide), lambda g: (0, g)),
            pl.BlockSpec((rows, wide), lambda g: (0, 0)),
            pl.BlockSpec((rows, wide), lambda g: (0, 0)),
        ],
        out_specs=(
            pl.BlockSpec((rows, wide), lambda g: (0, g)),
            pl.BlockSpec((rows, heads * HEAD_SIZE), lambda g: (0, g)),
        ),
        scratch_shapes=[
            pltpu.VMEM((heads, rows, PAIR), jnp.bfloat16),
            pltpu.VMEM((rows, PAIR), jnp.bfloat16),
            pltpu.VMEM((rows, PAIR), jnp.bfloat16),
        ],
        compiler_params=pltpu.CompilerParams(vmem_limit_bytes=48 << 20),
        cost_estimate=pl.CostEstimate(
            flops=2 * rows * depth * wide * groups + 2 * groups * heads * rows * rows * 128,
            bytes_accessed=2 * (rows * depth + depth * wide * groups + rows * wide * groups),
            transcendentals=groups * heads * rows * rows // 2,
        ),
        name="attend",
    )(length, inputs, weights, cosines, sines)


def attend_back_kernel(
    block, len_ref, qkv_ref, dz_ref, cos_ref, sin_ref, out_ref, q_all, z_all, k_two, v_two, k_acc, v_acc
):
    rows = qkv_ref.shape[0]
    heads = q_all.shape[0]
    length = len_ref[0]

    @pl.loop(0, rows // block)
    def _(at):
        here = pl.ds(pl.multiple_of(at * block, block), block)
        for part in range(heads // 2):
            lanes = slice(part * PAIR, (part + 1) * PAIR)
            queries = qkv_ref[here, lanes].astype(jnp.float32) * ATTN_MULT
            mixed = dz_ref[here, lanes].astype(jnp.float32)
            for side in range(2):
                q_all[2 * part + side, here, :] = keep_head(queries, side).astype(jnp.bfloat16)
                z_all[2 * part + side, here, :] = keep_head(mixed, side).astype(jnp.bfloat16)
        keys, values = both_heads(qkv_ref[here, heads * HEAD_SIZE :].astype(jnp.float32))
        k_two[here, :] = keys.astype(jnp.bfloat16)
        v_two[here, :] = values.astype(jnp.bfloat16)
        k_acc[here, :] = jnp.zeros((block, PAIR), jnp.float32)
        v_acc[here, :] = jnp.zeros((block, PAIR), jnp.float32)

    def turn_back(now, here, lanes):
        return (now * cos_ref[here, lanes] - half_turn(now) * sin_ref[here, lanes]).astype(
            jnp.bfloat16
        )

    for at in range(rows // block):
        here = slice(at * block, (at + 1) * block)
        upto = (at + 1) * block
        key = lax.broadcasted_iota(jnp.int32, (upto, block), 0)
        query = lax.broadcasted_iota(jnp.int32, (upto, block), 1) + at * block
        allowed = key < jnp.minimum(query + 1, length)

        def one_head(head):
            queries, mixed = q_all[head, here, :], z_all[head, here, :]
            scores = jnp.where(allowed, dot_nt(k_two[:upto, :], queries), MASKED)
            power = jnp.exp(scores - jnp.max(scores, axis=0, keepdims=True))
            weights = power * (1.0 / jnp.sum(power, axis=0, keepdims=True))
            back = dot_nt(v_two[:upto, :], mixed)
            centre = jnp.sum(weights * back, axis=0, keepdims=True)
            slope = (weights * (back - centre)).astype(jnp.bfloat16)
            k_acc[:upto, :] += dot_nn(slope, queries)
            v_acc[:upto, :] += dot_nn(weights.astype(jnp.bfloat16), mixed)
            return dot_tn(slope, k_two[:upto, :]) * ATTN_MULT

        for pair in range(heads // 2):
            low = one_head(2 * pair)
            high = one_head(2 * pair + 1)
            lane = lax.broadcasted_iota(jnp.int32, low.shape, 1)
            lanes = slice(pair * PAIR, (pair + 1) * PAIR)
            out_ref[here, lanes] = turn_back(jnp.where(lane < HEAD_SIZE, low, high), here, lanes)

    @pl.loop(0, rows // block)
    def _(at):
        here = pl.ds(pl.multiple_of(at * block, block), block)
        keys, values = k_acc[here, :], v_acc[here, :]
        keys = keys + pltpu.roll(keys, HEAD_SIZE, 1)
        values = values + pltpu.roll(values, HEAD_SIZE, 1)
        lane = lax.broadcasted_iota(jnp.int32, keys.shape, 1)
        lanes = slice(heads * HEAD_SIZE, heads * HEAD_SIZE + PAIR)
        out_ref[here, lanes] = turn_back(jnp.where(lane < HEAD_SIZE, keys, values), here, lanes)


def attend_back_fast(length, projected, grad_mixed, cosines, sines, groups):
    rows = projected.shape[0]
    wide = projected.shape[1] // groups
    heads = (wide - PAIR) // HEAD_SIZE
    block = min(256, rows)
    return pl.pallas_call(
        functools.partial(attend_back_kernel, block),
        grid=(groups,),
        out_shape=jax.ShapeDtypeStruct((rows, groups * wide), jnp.bfloat16),
        in_specs=[
            pl.BlockSpec(memory_space=pltpu.SMEM),
            pl.BlockSpec((rows, wide), lambda g: (0, g)),
            pl.BlockSpec((rows, heads * HEAD_SIZE), lambda g: (0, g)),
            pl.BlockSpec((rows, wide), lambda g: (0, 0)),
            pl.BlockSpec((rows, wide), lambda g: (0, 0)),
        ],
        out_specs=pl.BlockSpec((rows, wide), lambda g: (0, g)),
        scratch_shapes=[
            pltpu.VMEM((heads, rows, PAIR), jnp.bfloat16),
            pltpu.VMEM((heads, rows, PAIR), jnp.bfloat16),
            pltpu.VMEM((rows, PAIR), jnp.bfloat16),
            pltpu.VMEM((rows, PAIR), jnp.bfloat16),
            pltpu.VMEM((rows, PAIR), jnp.float32),
            pltpu.VMEM((rows, PAIR), jnp.float32),
        ],
        compiler_params=pltpu.CompilerParams(vmem_limit_bytes=48 << 20),
        cost_estimate=pl.CostEstimate(
            flops=5 * groups * heads * rows * rows * 128,
            bytes_accessed=2 * (2 * rows * wide * groups + rows * heads * HEAD_SIZE * groups),
            transcendentals=groups * heads * rows * rows // 2,
        ),
        name="attend_back",
    )(length, projected, grad_mixed, cosines, sines)


def one_sequence_body(
    tokens,
    cotangent,
    lengths,
    deal_order,
    gain_attn,
    gain_ffn,
    w_query,
    key_value_weight,
    w_out,
    w_gate_up,
    w_down,
):
    seq_group, rows_local, width_local = tokens.shape
    row_count = lax.axis_size("row")
    col_count = lax.axis_size("col")
    full_width = width_local * col_count
    slot_len = rows_local * row_count
    group, core, mate, row, col = place()
    query_half = w_query.shape[1] // 2
    kv_half = key_value_weight.shape[2] // 2
    hidden = w_down.shape[1]

    def core_half(matrix, axis):
        width = matrix.shape[axis] // 2
        return lax.dynamic_slice_in_dim(matrix, core * width, width, axis)

    def joined(mine, other, at):
        return jnp.where(
            at == 0, jnp.concatenate([mine, other]), jnp.concatenate([other, mine])
        )

    def from_sibling(value):
        return lax.ppermute(value, "dp", SIBLINGS)

    pack_q = jnp.concatenate(
        [
            core_half(w_query, 1),
            core_half(key_value_weight[:, 0], 1),
            core_half(key_value_weight[:, 1], 1),
        ],
        axis=1,
    )
    pack_o = core_half(w_out, 1)
    own_tokens, weights_qkv, weights_out = start_exchange(
        tokens, pack_q, pack_o, row_count, col_count
    )

    length = lax.dynamic_slice_in_dim(lengths, mate * seq_group + col, 1)
    line_lengths = lax.dynamic_slice_in_dim(lengths, mate * seq_group, seq_group)
    own_pos = core * rows_local + jnp.arange(rows_local, dtype=jnp.int32)
    line_live = (own_pos[None, :] < line_lengths[:, None]).astype(jnp.float32)
    own_live = (own_pos < length).astype(jnp.float32)[:, None]

    def all_rows(matrix):
        count = matrix.shape[0] // 4
        part = lax.dynamic_slice_in_dim(matrix, group * count, count)
        other = lax.all_gather(lax.ppermute(part, "row", OVER_X), "dp", axis=0, tiled=True)
        return joined(matrix, other, row)

    gate_up_weights = all_rows(w_gate_up)
    down_weights = all_rows(w_down)

    given = bring_cotangent(cotangent, deal_order, group * seq_group)
    swapped = lax.ppermute(given, ("dp", "row"), CROSSED)
    line_cot = lax.all_gather(swapped, "col", axis=2, tiled=True)
    line_grad = line_live[:, :, None] * line_cot.astype(jnp.float32)
    grad_ffn = (RES_MULT * line_grad).astype(jnp.bfloat16).reshape(-1, full_width)
    own_grad = own_live * lax.dynamic_index_in_dim(line_cot, col, keepdims=False).astype(
        jnp.float32
    )

    cosine_table, sine_table = rope_tables(jnp.arange(slot_len, dtype=jnp.int32), HEAD_SIZE)
    turns = (query_half + kv_half) // HEAD_SIZE
    cosines = jnp.concatenate(
        [jnp.tile(cosine_table, (1, 2 * turns)), jnp.ones((slot_len, kv_half), jnp.float32)], axis=1
    )
    sines = jnp.concatenate(
        [
            jnp.tile(jnp.concatenate([-sine_table, sine_table], axis=1), (1, turns)),
            jnp.zeros((slot_len, kv_half), jnp.float32),
        ],
        axis=1,
    )

    gain_one = gain_attn.astype(jnp.float32)
    gain_two = gain_ffn.astype(jnp.float32)
    own_float = own_tokens.astype(jnp.float32)
    scale_one = lax.rsqrt(jnp.mean(own_float * own_float, axis=1, keepdims=True) + EPSILON)
    own_input = (own_float * scale_one * gain_one).astype(jnp.bfloat16)
    attn_input = joined(own_input, from_sibling(own_input), core)
    projected, heads_out = attend_fast(
        length, attn_input, weights_qkv, cosines, sines, col_count
    )

    def summed_rows(partial):
        count = partial.shape[0] // 2
        mine = lax.dynamic_slice_in_dim(partial, core * count, count)
        other = lax.dynamic_slice_in_dim(partial, (1 - core) * count, count)
        return mine.astype(jnp.float32) + from_sibling(other).astype(jnp.float32)

    attn_rows = summed_rows(expand_local(heads_out, weights_out).astype(jnp.bfloat16))
    resid = own_float + RES_MULT * attn_rows
    scale_two = lax.rsqrt(jnp.mean(resid * resid, axis=1, keepdims=True) + EPSILON)
    own_ffn = (resid * scale_two * gain_two).astype(jnp.bfloat16)

    ffn_input = lax.all_gather(own_ffn, "col", axis=0, tiled=True)
    gate_up = contract_local(ffn_input, gate_up_weights)
    gate = gate_up[:, 0]
    upward = gate_up[:, 1]
    sigmoid_gate = jax.nn.sigmoid(gate)
    silu_gate = gate * sigmoid_gate
    hidden_rows = (silu_gate * upward).astype(jnp.bfloat16)
    grad_hidden = contract_local(grad_ffn, down_weights)
    slope = sigmoid_gate * (1.0 + gate * (1.0 - sigmoid_gate))
    grad_gate_rows = jnp.stack(
        [grad_hidden * upward * slope, grad_hidden * silu_gate], axis=1
    ).astype(jnp.bfloat16)
    back_partial = expand_local(grad_gate_rows, gate_up_weights).astype(jnp.bfloat16)
    grad_normed_two = lax.psum_scatter(
        back_partial, "col", scatter_dimension=0, tiled=True
    ).astype(jnp.float32)

    mlp_partial = RES_MULT * expand_local(hidden_rows, down_weights)
    is_own = (jnp.arange(col_count) == col).astype(jnp.float32)[:, None, None]
    out_partial = (
        mlp_partial.reshape(col_count, rows_local, full_width) + is_own * resid[None]
    ).astype(jnp.bfloat16)
    out_cols = lax.psum_scatter(out_partial, "col", scatter_dimension=2, tiled=True)
    given_pos = row * rows_local + jnp.arange(rows_local, dtype=jnp.int32)
    given_lengths = lax.dynamic_slice_in_dim(lengths, group * seq_group, seq_group)
    given_live = (given_pos[None, :] < given_lengths[:, None]).astype(jnp.float32)
    layer_out = given_live[:, :, None] * lax.ppermute(
        out_cols, ("dp", "row"), CROSSED
    ).astype(jnp.float32)

    def scatter_rows(matrix):
        return lax.psum_scatter(
            matrix.astype(jnp.bfloat16), ("dp", "row"), scatter_dimension=0, tiled=True
        ).astype(jnp.float32)

    sums_down = scatter_rows(token_outer(grad_ffn, hidden_rows))
    sums_gate_up = scatter_rows(token_outer(ffn_input, grad_gate_rows))

    weighted_two = grad_normed_two * gain_two
    inner_two = jnp.sum(weighted_two * resid, axis=1, keepdims=True)
    grad_resid = (
        own_grad + scale_two * weighted_two - resid * scale_two**3 * inner_two / full_width
    )
    gain_two_part = jnp.sum(grad_normed_two * resid * scale_two, axis=0)
    own_attn_grad = (RES_MULT * grad_resid).astype(jnp.bfloat16)
    grad_attn = joined(own_attn_grad, from_sibling(own_attn_grad), core)
    grad_heads = contract_local(grad_attn, weights_out).astype(jnp.bfloat16)
    grad_out = token_outer(grad_attn, heads_out).astype(jnp.bfloat16)
    grad_projected = attend_back_fast(
        length, projected, grad_heads, cosines, sines, col_count
    )
    grad_normed_one = summed_rows(expand_local(grad_projected, weights_qkv).astype(jnp.bfloat16))
    grad_qkv = token_outer(attn_input, grad_projected).astype(jnp.bfloat16)
    weighted_one = grad_normed_one * gain_one
    inner_one = jnp.sum(weighted_one * own_float, axis=1, keepdims=True)
    own_input_grad = (
        grad_resid
        + scale_one * weighted_one
        - own_float * scale_one**3 * inner_one / full_width
    ).astype(jnp.bfloat16)
    gain_one_part = jnp.sum(grad_normed_one * own_float * scale_one, axis=0)
    given_grad = lax.all_to_all(
        own_input_grad.reshape(rows_local, col_count, width_local), "col", 1, 0
    )
    input_grad = lax.ppermute(given_grad, ("dp", "row"), CROSSED).astype(jnp.float32)
    grad_gain_attn, grad_gain_ffn = lax.psum((gain_one_part, gain_two_part), ("dp", "row", "col"))

    both = jnp.concatenate(
        [
            grad_qkv.reshape(full_width, col_count, -1),
            grad_out.reshape(full_width, col_count, -1),
        ],
        axis=2,
    )
    both = both.reshape(2, 2, row_count, -1, col_count, both.shape[2])
    kept = lax.dynamic_index_in_dim(both, core, 1, keepdims=False)
    sent = from_sibling(lax.dynamic_index_in_dim(both, 1 - core, 1, keepdims=False))
    cores = jnp.where(
        core == 0, jnp.stack([kept, sent], axis=4), jnp.stack([sent, kept], axis=4)
    )
    cores = lax.psum_scatter(
        cores, "row", scatter_dimension=1, tiled=False
    )
    cores = lax.psum_scatter(
        cores, "dp", scatter_dimension=0, axis_index_groups=SAME_CORE, tiled=False
    )
    cores = lax.psum_scatter(cores, "col", scatter_dimension=1, tiled=False).astype(jnp.float32)
    grad_rows = cores.shape[0]
    qk = query_half + kv_half
    out_query = cores[:, :, :query_half].reshape(grad_rows, -1)
    out_kv = jnp.stack(
        [
            cores[:, :, query_half:qk].reshape(grad_rows, -1),
            cores[:, :, qk : qk + kv_half].reshape(grad_rows, -1),
        ],
        axis=1,
    )
    out_out = cores[:, :, qk + kv_half :].reshape(grad_rows, -1)
    return (
        layer_out,
        input_grad,
        out_query,
        out_kv,
        out_out,
        sums_gate_up,
        sums_down,
        grad_gain_attn,
        grad_gain_ffn,
    )


def general_body(
    tokens,
    cotangent,
    lengths,
    deal_order,
    gain_attn,
    gain_ffn,
    w_query,
    key_value_weight,
    w_out,
    w_gate_up,
    w_down,
):
    seq_group, rows_local, width_local = tokens.shape
    row_count = lax.axis_size("row")
    col_count = lax.axis_size("col")
    full_width = width_local * col_count
    slot_len = rows_local * row_count
    total_rows = seq_group * rows_local
    head_size = HEAD_SIZE
    query_width = w_query.shape[1]
    kv_width = key_value_weight.shape[2]
    kv_heads = kv_width // head_size
    group_size = query_width // kv_width
    group_index = lax.axis_index("dp")
    row_index = lax.axis_index("row")
    col_index = lax.axis_index("col")
    matrices = {
        "qkv": jnp.concatenate(
            [w_query, key_value_weight.reshape(key_value_weight.shape[0], 2 * kv_width)], axis=1
        ),
        "out": w_out,
        "gate_up": w_gate_up,
        "down": w_down,
    }

    def contract_with(operand, which_one):
        return contract_rows(operand, matrices[which_one])

    def expand_with(operand, which_one):
        return expand_rows(operand, matrices[which_one])

    own_cotangent = bring_cotangent(cotangent, deal_order, group_index * seq_group)
    own_rows = tokens
    seq_lens = lax.dynamic_slice_in_dim(lengths, group_index * seq_group, seq_group)
    local_pos = row_index * rows_local + jnp.arange(rows_local, dtype=jnp.int32)
    key_pos = jnp.arange(slot_len, dtype=jnp.int32)
    live_rows = (local_pos[None, :] < seq_lens[:, None]).astype(jnp.float32).reshape(total_rows, 1)
    cosine_table, sine_table = rope_tables(jnp.tile(local_pos, seq_group), head_size)
    own_tokens = own_rows.reshape(total_rows, width_local)
    wide_float = widen_cols(own_tokens).astype(jnp.float32)
    scale_one = lax.rsqrt(jnp.mean(wide_float * wide_float, axis=1, keepdims=True) + EPSILON)
    gain_one = gain_attn.astype(jnp.float32)
    first_normed = wide_float * scale_one
    attn_input = (first_normed * gain_one).astype(jnp.bfloat16)
    projected = contract_with(attn_input, "qkv")
    query_lin = projected[:, :query_width].reshape(total_rows, query_width // head_size, head_size)
    key_lin = projected[:, query_width : query_width + kv_width].reshape(
        total_rows, kv_heads, head_size
    )
    value_lin = projected[:, query_width + kv_width :]
    query_rows = rotary_embed(query_lin, cosine_table, sine_table).astype(jnp.bfloat16)
    keys_own = (
        rotary_embed(key_lin, cosine_table, sine_table)
        .astype(jnp.bfloat16)
        .reshape(seq_group, rows_local, kv_width)
    )
    values_own = value_lin.astype(jnp.bfloat16).reshape(seq_group, rows_local, kv_width)
    all_keys, all_values = (
        lax.all_gather(keys_own, "row", axis=1, tiled=True),
        lax.all_gather(values_own, "row", axis=1, tiled=True),
    )
    query_split = query_rows.reshape(seq_group, rows_local, kv_heads, group_size, head_size)
    key_split = all_keys.reshape(seq_group, slot_len, kv_heads, head_size)
    value_split = all_values.reshape(seq_group, slot_len, kv_heads, head_size)

    def forward_seq(inputs):
        return attend(inputs, key_pos, local_pos)

    mixed_heads, row_max, row_sums = lax.map(
        forward_seq, (query_split, key_split, value_split, seq_lens)
    )
    heads_out = mixed_heads.reshape(total_rows, query_width).astype(jnp.bfloat16)
    attn_local = narrow_cols(expand_with(heads_out, "out"))
    resid = own_tokens.astype(jnp.float32) + RES_MULT * attn_local
    gain_two = lax.dynamic_slice_in_dim(
        gain_ffn.astype(jnp.float32), col_index * width_local, width_local
    )
    scale_two = lax.rsqrt(sum_over_cols(jnp.sum(resid * resid, axis=1)) / full_width + EPSILON)[
        :, None
    ]
    normed_two = resid * scale_two
    ffn_input = widen_cols((normed_two * gain_two).astype(jnp.bfloat16))
    gate_up = contract_with(ffn_input, "gate_up")
    gate = gate_up[:, 0]
    upward = gate_up[:, 1]
    sigmoid_gate = jax.nn.sigmoid(gate)
    silu_gate = gate * sigmoid_gate
    hidden = (silu_gate * upward).astype(jnp.bfloat16)
    ffn_local = narrow_cols(expand_with(hidden, "down"))
    layer_out = live_rows * (resid + RES_MULT * ffn_local)
    grad_rows = live_rows * own_cotangent.reshape(total_rows, width_local).astype(jnp.float32)
    grad_ffn = widen_cols((RES_MULT * grad_rows).astype(jnp.bfloat16))
    grad_hidden = contract_with(grad_ffn, "down")
    grad_down = token_outer(grad_ffn, hidden)
    slope = sigmoid_gate * (1.0 + gate * (1.0 - sigmoid_gate))
    grad_gate_rows = jnp.stack(
        [grad_hidden * upward * slope, grad_hidden * silu_gate], axis=1
    ).astype(jnp.bfloat16)
    grad_gate_up = token_outer(ffn_input, grad_gate_rows)
    grad_normed_two = narrow_cols(expand_with(grad_gate_rows, "gate_up"))
    weighted_two = grad_normed_two * gain_two
    inner_two = sum_over_cols(jnp.sum(weighted_two * resid, axis=1))[:, None]
    grad_resid = (
        grad_rows + scale_two * weighted_two - resid * scale_two**3 * inner_two / full_width
    )
    gain_two_part = jnp.sum(grad_normed_two * normed_two, axis=0)
    grad_attn = widen_cols((RES_MULT * grad_resid).astype(jnp.bfloat16))
    grad_heads = contract_with(grad_attn, "out").astype(jnp.bfloat16)
    grad_out = token_outer(grad_attn, heads_out)
    grad_split = grad_heads.reshape(seq_group, rows_local, kv_heads, group_size, head_size)

    def backward_seq(inputs):
        return attend_back(inputs, key_pos, local_pos)

    grad_query, grad_key, grad_value = lax.map(
        backward_seq, (query_split, key_split, value_split, grad_split, row_max, row_sums, seq_lens)
    )
    key_part, value_part = (
        lax.psum_scatter(
            grad_key.reshape(seq_group, slot_len, kv_width).astype(jnp.bfloat16),
            "row",
            scatter_dimension=1,
            tiled=True,
        ).astype(jnp.float32),
        lax.psum_scatter(
            grad_value.reshape(seq_group, slot_len, kv_width).astype(jnp.bfloat16),
            "row",
            scatter_dimension=1,
            tiled=True,
        ).astype(jnp.float32),
    )
    query_back = rotary_embed(
        grad_query.reshape(total_rows, query_width // head_size, head_size),
        cosine_table,
        -sine_table,
    ).reshape(total_rows, query_width)
    key_back = rotary_embed(
        key_part.reshape(total_rows, kv_heads, head_size), cosine_table, -sine_table
    ).reshape(total_rows, kv_width)
    grad_projected = jnp.concatenate(
        [query_back, key_back, value_part.reshape(total_rows, kv_width)], axis=1
    ).astype(jnp.bfloat16)
    grad_qkv = token_outer(attn_input, grad_projected)
    grad_normed_one = expand_with(grad_projected, "qkv")
    weighted_one = grad_normed_one * gain_one
    inner_one = jnp.sum(weighted_one * wide_float, axis=1, keepdims=True)
    input_part = scale_one * weighted_one - wide_float * scale_one**3 * inner_one / full_width
    input_grad = grad_resid + narrow_cols(input_part)
    gain_one_part = jnp.sum(grad_normed_one * first_normed, axis=0)
    gain_two_full = lax.dynamic_update_slice_in_dim(
        jnp.zeros((full_width,), jnp.float32), gain_two_part, col_index * width_local, 0
    )
    grad_gain_attn, grad_gain_ffn = lax.psum((gain_one_part, gain_two_full), ("dp", "row", "col"))
    sums_qkv, sums_out, sums_gate_up, sums_down = (
        lax.psum_scatter(
            grad_qkv.astype(jnp.bfloat16), ("dp", "row"), scatter_dimension=0, tiled=True
        ).astype(jnp.float32),
        lax.psum_scatter(
            grad_out.astype(jnp.bfloat16), ("dp", "row"), scatter_dimension=0, tiled=True
        ).astype(jnp.float32),
        lax.psum_scatter(
            grad_gate_up.astype(jnp.bfloat16), ("dp", "row"), scatter_dimension=0, tiled=True
        ).astype(jnp.float32),
        lax.psum_scatter(
            grad_down.astype(jnp.bfloat16), ("dp", "row"), scatter_dimension=0, tiled=True
        ).astype(jnp.float32),
    )
    out_query = sums_qkv[:, :query_width]
    out_kv = sums_qkv[:, query_width:].reshape(sums_qkv.shape[0], 2, kv_width)
    return (
        layer_out.reshape(seq_group, rows_local, width_local),
        input_grad.reshape(seq_group, rows_local, width_local),
        out_query,
        out_kv,
        sums_out,
        sums_gate_up,
        sums_down,
        grad_gain_attn,
        grad_gain_ffn,
    )


def body(tokens, cotangent, lengths, deal_order, gain_attn, gain_ffn, w_query, key_value_weight, *rest):
    sizes = (lax.axis_size("dp"), lax.axis_size("row"), lax.axis_size("col"))
    one_each = sizes == (4, 2, 4) and tokens.shape[0] == sizes[2]
    pairs = w_query.shape[1] == 8 * HEAD_SIZE and key_value_weight.shape[2] == 2 * HEAD_SIZE
    chosen = one_sequence_body if one_each and pairs else general_body
    return chosen(
        tokens, cotangent, lengths, deal_order, gain_attn, gain_ffn, w_query, key_value_weight, *rest
    )


def solution(mesh):
    placed = (
        P("dp", "row", "col"),
        P("dp", "row", "col"),
        P(),
        P(),
        P(),
        P(),
        P("row", "col"),
        P("row", None, "col"),
        P("row", "col"),
        P("row", None, "col"),
        P("row", "col"),
    )
    return jax.shard_map(
        body,
        mesh=mesh,
        in_specs=placed,
        out_specs=(
            P("dp", "row", "col"),
            P("dp", "row", "col"),
            P(("dp", "row"), "col"),
            P(("dp", "row"), None, "col"),
            P(("dp", "row"), "col"),
            P(("dp", "row"), None, "col"),
            P(("dp", "row"), "col"),
            P(),
            P(),
        ),
        check_vma=False,
    )
```

```python
import functools

import jax
import jax.numpy as jnp
from jax import lax
from jax.experimental import pallas as pl
from jax.experimental.pallas import tpu as pltpu
from jax.sharding import PartitionSpec as P

HEAD_SIZE = 64


EPSILON = 1e-05
THETA = 10000000.0
ATTN_MULT = 0.015625
RES_MULT = 0.22
MASKED = -1e30


def rope_tables(positions, head_size):
    halves = jnp.arange(head_size // 2, dtype=jnp.float32)
    inverse_freq = THETA ** (-(halves * 2.0) / head_size)
    angles = positions.astype(jnp.float32)[:, None] * inverse_freq[None, :]
    return (jnp.cos(angles), jnp.sin(angles))


def rotary_embed(value_rows, cosine_table, sine_table):
    middle = value_rows.shape[-1] // 2
    first_half = value_rows[..., :middle]
    second_half = value_rows[..., middle:]
    cos_part = cosine_table[:, None, :]
    sin_part = sine_table[:, None, :]
    return jnp.concatenate(
        [
            first_half * cos_part - second_half * sin_part,
            second_half * cos_part + first_half * sin_part,
        ],
        axis=-1,
    )


def widen_cols(value_rows):
    return lax.all_gather(value_rows, "col", axis=1, tiled=True)


def narrow_cols(value_rows):
    return lax.psum_scatter(value_rows, "col", scatter_dimension=1, tiled=True)


def sum_over_cols(value_rows):
    return lax.psum(value_rows, "col")


def contract_local(operand, matrix):
    return lax.dot_general(
        operand, matrix, (((1,), (0,)), ((), ())), preferred_element_type=jnp.float32
    )


def expand_local(operand, matrix):
    trailing = tuple(range(1, operand.ndim))
    return lax.dot_general(
        operand, matrix, ((trailing, trailing), ((), ())), preferred_element_type=jnp.float32
    )


def token_outer(features, grads):
    return lax.dot_general(
        features, grads, (((0,), (0,)), ((), ())), preferred_element_type=jnp.float32
    )


def contract_rows(operand, matrix):
    return contract_local(operand, lax.all_gather(matrix, "row", axis=0, tiled=True))


def expand_rows(operand, matrix):
    return expand_local(operand, lax.all_gather(matrix, "row", axis=0, tiled=True))


def split_keys(key_seq, value_seq, key_pos):
    slot_len = key_seq.shape[0]
    width = min(512, slot_len)
    count = slot_len // width
    return (
        key_seq.reshape(count, width, key_seq.shape[1], key_seq.shape[2]),
        value_seq.reshape(count, width, value_seq.shape[1], value_seq.shape[2]),
        key_pos.reshape(count, width),
    )


def block_scores(query_seq, key_block, pos_block, query_pos, length):
    scores = (
        jnp.einsum("qkgd,tkd->kgqt", query_seq, key_block, preferred_element_type=jnp.float32)
        * ATTN_MULT
    )
    allowed = (pos_block[None, :] <= query_pos[:, None]) & (pos_block[None, :] < length)
    return jnp.where(allowed, scores, MASKED)


def attend(inputs, key_pos, query_pos):
    query_seq, key_seq, value_seq, length = inputs
    key_blocks, value_blocks, pos_blocks = split_keys(key_seq, value_seq, key_pos)
    stat_shape = (query_seq.shape[1], query_seq.shape[2], query_seq.shape[0], 1)

    def gather_stats(carry, entry):
        running_max, running_sum = carry
        key_block, pos_block = entry
        scores = block_scores(query_seq, key_block, pos_block, query_pos, length)
        new_max = jnp.maximum(running_max, jnp.max(scores, axis=-1, keepdims=True))
        new_sum = running_sum * jnp.exp(running_max - new_max) + jnp.sum(
            jnp.exp(scores - new_max), axis=-1, keepdims=True
        )
        return ((new_max, new_sum), None)

    start_stats = (jnp.full(stat_shape, MASKED, jnp.float32), jnp.zeros(stat_shape, jnp.float32))
    (row_max, row_sums), unused = lax.scan(gather_stats, start_stats, (key_blocks, pos_blocks))

    def mix_values(running, entry):
        key_block, value_block, pos_block = entry
        scores = block_scores(query_seq, key_block, pos_block, query_pos, length)
        weights = jnp.exp(scores - row_max) / row_sums
        return (
            running
            + jnp.einsum(
                "kgqt,tkd->qkgd",
                weights.astype(jnp.bfloat16),
                value_block,
                preferred_element_type=jnp.float32,
            ),
            None,
        )

    start_mix = jnp.zeros(query_seq.shape, jnp.float32)
    mixed_heads, unused = lax.scan(mix_values, start_mix, (key_blocks, value_blocks, pos_blocks))
    return (mixed_heads, row_max, row_sums)


def attend_back(inputs, key_pos, query_pos):
    query_seq, key_seq, value_seq, grad_mixed, row_max, row_sums, length = inputs
    key_blocks, value_blocks, pos_blocks = split_keys(key_seq, value_seq, key_pos)

    def block_weights(key_block, value_block, pos_block):
        scores = block_scores(query_seq, key_block, pos_block, query_pos, length)
        weights = jnp.exp(scores - row_max) / row_sums
        grad_weights = jnp.einsum(
            "qkgd,tkd->kgqt", grad_mixed, value_block, preferred_element_type=jnp.float32
        )
        return (weights, grad_weights)

    def gather_centre(running, entry):
        weights, grad_weights = block_weights(*entry)
        return (running + jnp.sum(weights * grad_weights, axis=-1, keepdims=True), None)

    start_centre = jnp.zeros(row_max.shape, jnp.float32)
    centre, unused = lax.scan(gather_centre, start_centre, (key_blocks, value_blocks, pos_blocks))

    def grads_block(running, entry):
        key_block = entry[0]
        weights, grad_weights = block_weights(*entry)
        grad_scores = (weights * (grad_weights - centre)).astype(jnp.bfloat16)
        grad_query = (
            running
            + jnp.einsum(
                "kgqt,tkd->qkgd", grad_scores, key_block, preferred_element_type=jnp.float32
            )
            * ATTN_MULT
        )
        grad_key = (
            jnp.einsum("kgqt,qkgd->tkd", grad_scores, query_seq, preferred_element_type=jnp.float32)
            * ATTN_MULT
        )
        grad_value = jnp.einsum(
            "kgqt,qkgd->tkd",
            weights.astype(jnp.bfloat16),
            grad_mixed,
            preferred_element_type=jnp.float32,
        )
        return (grad_query, (grad_key, grad_value))

    start_query = jnp.zeros(query_seq.shape, jnp.float32)
    grad_query, (grad_key, grad_value) = lax.scan(
        grads_block, start_query, (key_blocks, value_blocks, pos_blocks)
    )
    return (grad_query, grad_key.reshape(key_seq.shape), grad_value.reshape(value_seq.shape))


MESH_IDS = pl.DeviceIdType.MESH
SIBLINGS = [(0, 1), (1, 0), (2, 3), (3, 2)]
OVER_X = [(0, 1), (1, 0)]
CROSSED = [((2 * y + c) * 2 + x, (2 * y + x) * 2 + c) for y in (0, 1) for c in (0, 1) for x in (0, 1)]
SAME_CORE = [[0, 2], [1, 3]]


def bring_cotangent(cotangent, deal_order, first):
    everyone = lax.all_gather(cotangent, "dp", axis=0, tiled=True)
    slots = jnp.arange(deal_order.shape[0], dtype=jnp.int32)
    inverse = jnp.sum(jnp.where(deal_order[None, :] == slots[:, None], slots[None, :], 0), axis=1)
    return jnp.concatenate(
        [
            lax.dynamic_slice_in_dim(
                everyone, lax.dynamic_index_in_dim(inverse, first + at, keepdims=False), 1
            )
            for at in range(cotangent.shape[0])
        ]
    )


def place():
    group = lax.axis_index("dp")
    core = lax.rem(group, 2)
    row = lax.axis_index("row")
    return group, core, group - core + row, row, lax.axis_index("col")


def start_kernel(
    cols,
    tok_ref,
    pq_ref,
    po_ref,
    gain_ref,
    x_ref,
    a_ref,
    wq_ref,
    wo_ref,
    x_buf,
    a_buf,
    tok_sems,
    q_sems,
    o_sems,
    qx_sems,
    ox_sems,
    a_sems,
    local_sems,
):
    group, core, mate, row, col = place()
    width = tok_ref.shape[2]
    weight_rows = pq_ref.shape[0]

    def line(step):
        return lax.rem(col + step + cols, cols)

    def start_at(block, size):
        return pl.ds(pl.multiple_of(block * size, size), size)

    barrier = pltpu.get_barrier_semaphore()

    def greet(device):
        pl.semaphore_signal(barrier, inc=1, device_id=device, device_id_type=MESH_IDS)

    for step in range(1, cols):
        greet((mate, core, line(step)))
        greet((group, row, line(step)))
    sibling = (group + 1 - 2 * core, row, col)
    greet((group, 1 - row, col))
    greet(sibling)

    @pl.when(core != row)
    def _():
        greet((mate, core, col))

    pl.semaphore_wait(barrier, 2 * cols + (core - row) * (core - row))

    def remote(src, dst, sems, at, device):
        return pltpu.make_async_remote_copy(
            src_ref=src,
            dst_ref=dst,
            send_sem=sems.at[0, at],
            recv_sem=sems.at[1, at],
            device_id=device,
            device_id_type=MESH_IDS,
        )

    def weight_copies(own, full, sems, x_sems):
        wide = own.shape[1]

        def block(of_row, of_col):
            return full.at[start_at(of_row, weight_rows), start_at(of_col, wide)]

        along = [
            remote(own, block(row, col), sems, step, (group, row, line(step)))
            for step in range(1, cols)
        ]
        arrive = [
            remote(own, block(row, line(-step)), sems, step, (group, row, line(step)))
            for step in range(1, cols)
        ]
        across = [remote(own, block(row, col), x_sems, 0, (group, 1 - row, col))] + [
            remote(block(row, line(-step)), block(row, line(-step)), x_sems, step, (group, 1 - row, col))
            for step in range(1, cols)
        ]
        landed = [
            remote(own, block(1 - row, line(-step)), x_sems, step, (group, 1 - row, col))
            for step in range(cols)
        ]
        return along, arrive, across, landed, block(row, col)

    q_along, q_arrive, q_across, q_landed, q_own = weight_copies(pq_ref, wq_ref, q_sems, qx_sems)
    o_along, o_arrive, o_across, o_landed, o_own = weight_copies(po_ref, wo_ref, o_sems, ox_sems)
    own_q = pltpu.make_async_copy(pq_ref, q_own, local_sems.at[0])
    own_o = pltpu.make_async_copy(po_ref, o_own, local_sems.at[1])

    def token_copy(step, into):
        return remote(
            tok_ref.at[line(step)],
            x_buf.at[:, start_at(into, width)],
            tok_sems,
            step,
            (mate, core, line(step)),
        )

    own_tokens = pltpu.make_async_copy(
        tok_ref.at[col], x_buf.at[:, start_at(col, width)], local_sems.at[2]
    )
    for step in range(1, cols):
        token_copy(step, col).start()

    @pl.when(core != row)
    def _():
        token_copy(0, col).start()

    @pl.when(core == row)
    def _():
        own_tokens.start()

    for copy in q_along:
        copy.start()
    q_across[0].start()
    own_q.start()
    own_o.start()
    for copy in o_along:
        copy.start()
    o_across[0].start()
    for step in range(1, cols):
        token_copy(step, line(-step)).wait_recv()

    @pl.when(core != row)
    def _():
        token_copy(0, col).wait_recv()

    @pl.when(core == row)
    def _():
        own_tokens.wait()

    keep_x = pltpu.make_async_copy(x_buf, x_ref, local_sems.at[3])
    keep_x.start()
    length = x_buf.shape[0]
    tall = min(64, length)

    @pl.loop(0, length // tall)
    def _(at):
        here = pl.ds(pl.multiple_of(at * tall, tall), tall)
        now = x_buf[here, :].astype(jnp.float32)
        scale = lax.rsqrt(jnp.mean(now * now, axis=1, keepdims=True) + EPSILON)
        a_buf[here, :] = (now * scale * gain_ref[...]).astype(jnp.bfloat16)

    def a_copy(of_core):
        return remote(a_buf, a_ref.at[start_at(of_core, length)], a_sems, 0, sibling)

    own_a = pltpu.make_async_copy(a_buf, a_ref.at[start_at(core, length)], local_sems.at[4])
    a_copy(core).start()
    own_a.start()
    for step in range(1, cols):
        q_arrive[step - 1].wait_recv()
        q_across[step].start()
    for step in range(1, cols):
        o_arrive[step - 1].wait_recv()
        o_across[step].start()
    for step in range(1, cols):
        token_copy(step, col).wait_send()

    @pl.when(core != row)
    def _():
        token_copy(0, col).wait_send()

    keep_x.wait()
    own_a.wait()
    a_copy(core).wait_send()
    a_copy(1 - core).wait_recv()
    own_q.wait()
    own_o.wait()
    for copy in q_along + o_along + q_across + o_across:
        copy.wait_send()
    for copy in q_landed + o_landed:
        copy.wait_recv()


def start_exchange(tokens, pack_q, pack_o, gain, rows, cols):
    anywhere = pl.BlockSpec(memory_space=pl.ANY)
    seqs, length, width = tokens.shape
    weight_rows = pack_q.shape[0]
    full = width * cols
    return pl.pallas_call(
        functools.partial(start_kernel, cols),
        out_shape=(
            jax.ShapeDtypeStruct((length, full), tokens.dtype),
            jax.ShapeDtypeStruct((2 * length, full), tokens.dtype),
            jax.ShapeDtypeStruct((weight_rows * rows, pack_q.shape[1] * cols), pack_q.dtype),
            jax.ShapeDtypeStruct((weight_rows * rows, pack_o.shape[1] * cols), pack_o.dtype),
        ),
        in_specs=[anywhere] * 3 + [pl.BlockSpec(memory_space=pltpu.VMEM)],
        out_specs=(anywhere,) * 4,
        scratch_shapes=[
            pltpu.VMEM((length, full), tokens.dtype),
            pltpu.VMEM((length, full), tokens.dtype),
        ]
        + [pltpu.SemaphoreType.DMA((2, cols))] * 5
        + [pltpu.SemaphoreType.DMA((2, 1)), pltpu.SemaphoreType.DMA((5,))],
        compiler_params=pltpu.CompilerParams(
            collective_id=1, has_side_effects=True, vmem_limit_bytes=16 << 20
        ),
        cost_estimate=pl.CostEstimate(flops=0, bytes_accessed=400 << 20, transcendentals=0),
        name="start_exchange",
    )(tokens, pack_q, pack_o, gain.reshape(1, full))


def half_turn(wide):
    lanes = wide.shape[1]
    half = HEAD_SIZE // 2
    lane = lax.broadcasted_iota(jnp.int32, wide.shape, 1)
    return jnp.where(
        lax.rem(lane, HEAD_SIZE) < half,
        pltpu.roll(wide, lanes - half, 1),
        pltpu.roll(wide, half, 1),
    )


def both_heads(pair):
    lane = lax.broadcasted_iota(jnp.int32, pair.shape, 1)
    turned = pltpu.roll(pair, HEAD_SIZE, 1)
    low = lane < HEAD_SIZE
    return jnp.where(low, pair, turned), jnp.where(low, turned, pair)


def keep_head(pair, side):
    lane = lax.broadcasted_iota(jnp.int32, pair.shape, 1)
    mine = lane < HEAD_SIZE if side == 0 else lane >= HEAD_SIZE
    return jnp.where(mine, pair, jnp.zeros_like(pair))


def dot_nn(a, b):
    return lax.dot_general(a, b, (((1,), (0,)), ((), ())), preferred_element_type=jnp.float32)


def dot_nt(a, b):
    return lax.dot_general(a, b, (((1,), (1,)), ((), ())), preferred_element_type=jnp.float32)


def dot_tn(a, b):
    return lax.dot_general(a, b, (((0,), (0,)), ((), ())), preferred_element_type=jnp.float32)


PAIR = 2 * HEAD_SIZE


def attend_kernel(block, len_ref, a_ref, w_ref, cos_ref, sin_ref, qkv_ref, z_ref, q_all, k_two, v_two):
    rows = a_ref.shape[0]
    heads = q_all.shape[0]
    length = len_ref[0]

    @pl.loop(0, rows // block)
    def _(at):
        here = pl.ds(pl.multiple_of(at * block, block), block)
        lin = dot_nn(a_ref[here, :], w_ref[...])
        for part in range(heads // 2 + 1):
            lanes = slice(part * PAIR, (part + 1) * PAIR)
            now = lin[:, lanes]
            table = slice(0, PAIR) if part < heads // 2 else slice(PAIR, 2 * PAIR)
            now = now * cos_ref[here, table] + half_turn(now) * sin_ref[here, table]
            qkv_ref[here, lanes] = now.astype(jnp.bfloat16)
            if part < heads // 2:
                for side in range(2):
                    q_all[2 * part + side, here, :] = keep_head(now * ATTN_MULT, side).astype(
                        jnp.bfloat16
                    )
            else:
                keys, values = both_heads(now)
                k_two[here, :] = keys.astype(jnp.bfloat16)
                v_two[here, :] = values.astype(jnp.bfloat16)

    for at in range(rows // block):
        here = slice(at * block, (at + 1) * block)
        upto = (at + 1) * block
        row = lax.broadcasted_iota(jnp.int32, (block, upto), 0) + at * block
        key = lax.broadcasted_iota(jnp.int32, (block, upto), 1)
        allowed = key < jnp.minimum(row + 1, length)

        def one_head(head):
            scores = dot_nt(q_all[head, here, :], k_two[:upto, :])
            scores = jnp.where(allowed, scores, MASKED)
            top = jnp.max(scores, axis=1, keepdims=True)
            power = jnp.exp(scores - top)
            total = jnp.sum(power, axis=1, keepdims=True)
            return dot_nn(power.astype(jnp.bfloat16), v_two[:upto, :]) / total

        for pair in range(heads // 2):
            low = one_head(2 * pair)
            high = one_head(2 * pair + 1)
            lane = lax.broadcasted_iota(jnp.int32, low.shape, 1)
            z_ref[here, pair * PAIR : (pair + 1) * PAIR] = jnp.where(
                lane < HEAD_SIZE, low, high
            ).astype(jnp.bfloat16)


def attend_fast(length, inputs, weights, cosines, sines, groups):
    rows, depth = inputs.shape
    wide = weights.shape[1] // groups
    heads = (wide - PAIR) // HEAD_SIZE
    block = min(256, rows)
    return pl.pallas_call(
        functools.partial(attend_kernel, block),
        grid=(groups,),
        out_shape=(
            jax.ShapeDtypeStruct((rows, groups * wide), jnp.bfloat16),
            jax.ShapeDtypeStruct((rows, groups * heads * HEAD_SIZE), jnp.bfloat16),
        ),
        in_specs=[
            pl.BlockSpec(memory_space=pltpu.SMEM),
            pl.BlockSpec((rows, depth), lambda g: (0, 0)),
            pl.BlockSpec((depth, wide), lambda g: (0, g)),
            pl.BlockSpec((rows, 2 * PAIR), lambda g: (0, 0)),
            pl.BlockSpec((rows, 2 * PAIR), lambda g: (0, 0)),
        ],
        out_specs=(
            pl.BlockSpec((rows, wide), lambda g: (0, g)),
            pl.BlockSpec((rows, heads * HEAD_SIZE), lambda g: (0, g)),
        ),
        scratch_shapes=[
            pltpu.VMEM((heads, rows, PAIR), jnp.bfloat16),
            pltpu.VMEM((rows, PAIR), jnp.bfloat16),
            pltpu.VMEM((rows, PAIR), jnp.bfloat16),
        ],
        compiler_params=pltpu.CompilerParams(vmem_limit_bytes=48 << 20),
        cost_estimate=pl.CostEstimate(
            flops=2 * rows * depth * wide * groups + 2 * groups * heads * rows * rows * 128,
            bytes_accessed=2 * (rows * depth + depth * wide * groups + rows * wide * groups),
            transcendentals=groups * heads * rows * rows // 2,
        ),
        name="attend",
    )(length, inputs, weights, cosines, sines)


def attend_back_kernel(
    block, len_ref, qkv_ref, dz_ref, cos_ref, sin_ref, out_ref, q_all, z_all, k_two, v_two, k_acc, v_acc
):
    rows = qkv_ref.shape[0]
    heads = q_all.shape[0]
    length = len_ref[0]

    @pl.loop(0, rows // block)
    def _(at):
        here = pl.ds(pl.multiple_of(at * block, block), block)
        for part in range(heads // 2):
            lanes = slice(part * PAIR, (part + 1) * PAIR)
            queries = qkv_ref[here, lanes].astype(jnp.float32) * ATTN_MULT
            mixed = dz_ref[here, lanes].astype(jnp.float32)
            for side in range(2):
                q_all[2 * part + side, here, :] = keep_head(queries, side).astype(jnp.bfloat16)
                z_all[2 * part + side, here, :] = keep_head(mixed, side).astype(jnp.bfloat16)
        keys, values = both_heads(qkv_ref[here, heads * HEAD_SIZE :].astype(jnp.float32))
        k_two[here, :] = keys.astype(jnp.bfloat16)
        v_two[here, :] = values.astype(jnp.bfloat16)
        k_acc[here, :] = jnp.zeros((block, PAIR), jnp.float32)
        v_acc[here, :] = jnp.zeros((block, PAIR), jnp.float32)

    def turn_back(now, here, table):
        return (now * cos_ref[here, table] - half_turn(now) * sin_ref[here, table]).astype(
            jnp.bfloat16
        )

    for at in range(rows // block):
        here = slice(at * block, (at + 1) * block)
        upto = (at + 1) * block
        key = lax.broadcasted_iota(jnp.int32, (upto, block), 0)
        query = lax.broadcasted_iota(jnp.int32, (upto, block), 1) + at * block
        allowed = key < jnp.minimum(query + 1, length)

        def one_head(head):
            queries, mixed = q_all[head, here, :], z_all[head, here, :]
            scores = jnp.where(allowed, dot_nt(k_two[:upto, :], queries), MASKED)
            power = jnp.exp(scores - jnp.max(scores, axis=0, keepdims=True))
            weights = power * (1.0 / jnp.sum(power, axis=0, keepdims=True))
            back = dot_nt(v_two[:upto, :], mixed)
            centre = jnp.sum(weights * back, axis=0, keepdims=True)
            slope = (weights * (back - centre)).astype(jnp.bfloat16)
            k_acc[:upto, :] += dot_nn(slope, queries)
            v_acc[:upto, :] += dot_nn(weights.astype(jnp.bfloat16), mixed)
            return dot_tn(slope, k_two[:upto, :]) * ATTN_MULT

        for pair in range(heads // 2):
            low = one_head(2 * pair)
            high = one_head(2 * pair + 1)
            lane = lax.broadcasted_iota(jnp.int32, low.shape, 1)
            lanes = slice(pair * PAIR, (pair + 1) * PAIR)
            out_ref[here, lanes] = turn_back(
                jnp.where(lane < HEAD_SIZE, low, high), here, slice(0, PAIR)
            )

    @pl.loop(0, rows // block)
    def _(at):
        here = pl.ds(pl.multiple_of(at * block, block), block)
        keys, values = k_acc[here, :], v_acc[here, :]
        keys = keys + pltpu.roll(keys, HEAD_SIZE, 1)
        values = values + pltpu.roll(values, HEAD_SIZE, 1)
        lane = lax.broadcasted_iota(jnp.int32, keys.shape, 1)
        lanes = slice(heads * HEAD_SIZE, heads * HEAD_SIZE + PAIR)
        out_ref[here, lanes] = turn_back(
            jnp.where(lane < HEAD_SIZE, keys, values), here, slice(PAIR, 2 * PAIR)
        )


def attend_back_fast(length, projected, grad_mixed, cosines, sines, groups):
    rows = projected.shape[0]
    wide = projected.shape[1] // groups
    heads = (wide - PAIR) // HEAD_SIZE
    block = min(256, rows)
    return pl.pallas_call(
        functools.partial(attend_back_kernel, block),
        grid=(groups,),
        out_shape=jax.ShapeDtypeStruct((rows, groups * wide), jnp.bfloat16),
        in_specs=[
            pl.BlockSpec(memory_space=pltpu.SMEM),
            pl.BlockSpec((rows, wide), lambda g: (0, g)),
            pl.BlockSpec((rows, heads * HEAD_SIZE), lambda g: (0, g)),
            pl.BlockSpec((rows, 2 * PAIR), lambda g: (0, 0)),
            pl.BlockSpec((rows, 2 * PAIR), lambda g: (0, 0)),
        ],
        out_specs=pl.BlockSpec((rows, wide), lambda g: (0, g)),
        scratch_shapes=[
            pltpu.VMEM((heads, rows, PAIR), jnp.bfloat16),
            pltpu.VMEM((heads, rows, PAIR), jnp.bfloat16),
            pltpu.VMEM((rows, PAIR), jnp.bfloat16),
            pltpu.VMEM((rows, PAIR), jnp.bfloat16),
            pltpu.VMEM((rows, PAIR), jnp.float32),
            pltpu.VMEM((rows, PAIR), jnp.float32),
        ],
        compiler_params=pltpu.CompilerParams(vmem_limit_bytes=48 << 20),
        cost_estimate=pl.CostEstimate(
            flops=5 * groups * heads * rows * rows * 128,
            bytes_accessed=2 * (2 * rows * wide * groups + rows * heads * HEAD_SIZE * groups),
            transcendentals=groups * heads * rows * rows // 2,
        ),
        name="attend_back",
    )(length, projected, grad_mixed, cosines, sines)


def ffn_kernel(
    cols,
    own_ref,
    resid_ref,
    grad_ref,
    wg_own,
    wu_own,
    wd_own,
    wg_far,
    wu_far,
    wd_far,
    wg_sib,
    wu_sib,
    wd_sib,
    b_all,
    u_all,
    dgu_all,
    mlp_all,
    back_all,
    wg,
    wu,
    wd,
    b_buf,
    g_buf,
    u_buf,
    dg_buf,
    du_buf,
    mlp_buf,
    back_buf,
    w_sems,
    ag_send,
    ag_recv,
    back_send,
    back_recv,
    io_sems,
):
    group, core, mate, row, col = place()
    last = cols - 1
    depth = wg_own.shape[0]
    half = depth // 2
    units = wg_own.shape[1]
    tile = min(512, units)

    barrier = pltpu.get_barrier_semaphore()
    for step in range(1, cols):
        pl.semaphore_signal(
            barrier,
            inc=1,
            device_id=(group, row, lax.rem(col + step, cols)),
            device_id_type=MESH_IDS,
        )
    pl.semaphore_wait(barrier, cols - 1)

    def pass_on(src, at, to, way):
        return pltpu.make_async_remote_copy(
            src_ref=src,
            dst_ref=b_all.at[at],
            send_sem=ag_send.at[way, at],
            recv_sem=ag_recv.at[at],
            device_id=(group, row, to),
            device_id_type=MESH_IDS,
        )

    @pl.when(col < last)
    def _():
        pass_on(own_ref, col, col + 1, 0).start()

    @pl.when(col > 0)
    def _():
        pass_on(own_ref, col, col - 1, 1).start()

    def rows_at(first, size):
        return pl.ds(pl.multiple_of(first, half), size)

    own_copy = pltpu.make_async_copy(own_ref, b_all.at[col], io_sems.at[0])
    own_copy.start()
    load_resid = pltpu.make_async_copy(resid_ref, mlp_buf, io_sems.at[8])
    load_resid.start()
    far = (1 - row) * depth
    loads = []
    for at, (full, mine, across, sibling) in enumerate(
        ((wg, wg_own, wg_far, wg_sib), (wu, wu_own, wu_far, wu_sib), (wd, wd_own, wd_far, wd_sib))
    ):
        loads += [
            pltpu.make_async_copy(mine, full.at[rows_at(row * depth, depth)], w_sems.at[3 * at]),
            pltpu.make_async_copy(
                across, full.at[rows_at(far + core * half, half)], w_sems.at[3 * at + 1]
            ),
            pltpu.make_async_copy(
                sibling, full.at[rows_at(far + (1 - core) * half, half)], w_sems.at[3 * at + 2]
            ),
        ]
    for load in loads:
        load.start()
    own_copy.wait()
    for load in loads:
        load.wait()

    def order(at):
        inner_low = jnp.where(at < 2, 1 - at, at)
        inner_high = jnp.where(at == 3, 0, jnp.where(at == 0, 2, jnp.where(at == 1, 1, 3)))
        return jnp.where(
            col == 0,
            at,
            jnp.where(col == last, last - at, jnp.where(col == 1, inner_low, inner_high)),
        )

    def arrive(chunk):
        pass_on(b_all.at[chunk], chunk, col, 0).wait_recv()

        @pl.when((chunk < col) & (col < last))
        def _():
            pass_on(b_all.at[chunk], chunk, col + 1, 0).start()

        @pl.when((chunk > col) & (col > 0))
        def _():
            pass_on(b_all.at[chunk], chunk, col - 1, 1).start()

    def outputs(chunk):
        return (
            pltpu.make_async_copy(u_buf, u_all.at[chunk], io_sems.at[1]),
            pltpu.make_async_copy(dg_buf, dgu_all.at[chunk, :, 0:units], io_sems.at[2]),
            pltpu.make_async_copy(du_buf, dgu_all.at[chunk, :, units : 2 * units], io_sems.at[3]),
        )

    def mlp_out(chunk):
        return pltpu.make_async_copy(mlp_buf, mlp_all.at[chunk], io_sems.at[4])

    def back_out(at, chunk):
        return pltpu.make_async_remote_copy(
            src_ref=back_buf.at[at],
            dst_ref=back_all.at[col],
            send_sem=back_send.at[at],
            recv_sem=back_recv.at[col],
            device_id=(group, row, chunk),
            device_id_type=MESH_IDS,
        )

    own_back = pltpu.make_async_copy(back_buf.at[0], back_all.at[col], io_sems.at[5])
    at_end = (col == 0) | (col == last)

    def one_chunk(at, unused):
        chunk = order(at)

        @pl.when(at_end & (at > 0))
        def _():
            arrive(order(at))

        @pl.when(jnp.logical_not(at_end) & (at == 1))
        def _():
            arrive(order(1))
            arrive(order(2))

        @pl.when(jnp.logical_not(at_end) & (at == 3))
        def _():
            arrive(order(3))

        load_b = pltpu.make_async_copy(b_all.at[chunk], b_buf, io_sems.at[6])
        load_g = pltpu.make_async_copy(grad_ref.at[chunk], g_buf, io_sems.at[7])
        load_b.start()
        load_g.start()

        @pl.when(at > 0)
        def _():
            for copy in outputs(order(at - 1)):
                copy.wait()

        load_b.wait()
        load_g.wait()

        @pl.loop(0, units // tile)
        def _(step):
            lanes = pl.ds(pl.multiple_of(step * tile, tile), tile)
            gate = dot_nn(b_buf[...], wg[:, lanes])
            upward = dot_nn(b_buf[...], wu[:, lanes])
            back = dot_nn(g_buf[...], wd[:, lanes])
            opened = 1.0 / (1.0 + jnp.exp(-gate))
            silu = gate * opened
            u_buf[:, lanes] = (silu * upward).astype(jnp.bfloat16)
            slope = opened * (1.0 + gate * (1.0 - opened))
            dg_buf[:, lanes] = (back * upward * slope).astype(jnp.bfloat16)
            du_buf[:, lanes] = (back * silu).astype(jnp.bfloat16)

        for copy in outputs(chunk):
            copy.start()

        @pl.when(at > 0)
        def _():
            mlp_out(order(at - 1)).wait()

        @pl.when(at == 0)
        def _():
            load_resid.wait()

        @pl.loop(0, 2 * depth // tile)
        def _(step):
            here = pl.ds(pl.multiple_of(step * tile, tile), tile)
            back = dot_nt(dg_buf[...], wg[here, :]) + dot_nt(du_buf[...], wu[here, :])
            back_buf[at, :, here] = back.astype(jnp.bfloat16)
            added = jnp.where(at == 0, mlp_buf[:, here].astype(jnp.float32), 0.0)
            mlp_buf[:, here] = (added + RES_MULT * dot_nt(u_buf[...], wd[here, :])).astype(
                jnp.bfloat16
            )

        mlp_out(chunk).start()

        @pl.when(at == 0)
        def _():
            own_back.start()

        @pl.when(at > 0)
        def _():
            back_out(at, chunk).start()

        return unused

    lax.fori_loop(0, cols, one_chunk, 0)
    for copy in outputs(order(last)):
        copy.wait()
    mlp_out(order(last)).wait()
    own_back.wait()
    for at in range(1, cols):
        back_out(at, order(at)).wait_send()
        source = lax.rem(col + at, cols)
        pltpu.make_async_remote_copy(
            src_ref=back_buf.at[at],
            dst_ref=back_all.at[source],
            send_sem=back_send.at[at],
            recv_sem=back_recv.at[source],
            device_id=(group, row, source),
            device_id_type=MESH_IDS,
        ).wait_recv()
    for chunk in range(cols):

        @pl.when((col >= chunk) & (col < last))
        def _():
            pass_on(own_ref, chunk, col + 1, 0).wait_send()

        @pl.when((col <= chunk) & (col > 0))
        def _():
            pass_on(own_ref, chunk, col - 1, 1).wait_send()


def feed_forward(own_input, resid, grad_rows, weights, cols):
    rows, width = own_input.shape
    units = weights[0].shape[1]
    anywhere = pl.BlockSpec(memory_space=pl.ANY)
    bf16 = jnp.bfloat16
    return pl.pallas_call(
        functools.partial(ffn_kernel, cols),
        out_shape=(
            jax.ShapeDtypeStruct((cols, rows, width), bf16),
            jax.ShapeDtypeStruct((cols, rows, units), bf16),
            jax.ShapeDtypeStruct((cols, rows, 2 * units), bf16),
            jax.ShapeDtypeStruct((cols, rows, width), bf16),
            jax.ShapeDtypeStruct((cols, rows, width), bf16),
        ),
        in_specs=[anywhere] * 12,
        out_specs=(anywhere,) * 5,
        scratch_shapes=[
            pltpu.VMEM((width, units), bf16),
            pltpu.VMEM((width, units), bf16),
            pltpu.VMEM((width, units), bf16),
            pltpu.VMEM((rows, width), bf16),
            pltpu.VMEM((rows, width), bf16),
            pltpu.VMEM((rows, units), bf16),
            pltpu.VMEM((rows, units), bf16),
            pltpu.VMEM((rows, units), bf16),
            pltpu.VMEM((rows, width), bf16),
            pltpu.VMEM((cols, rows, width), bf16),
            pltpu.SemaphoreType.DMA((9,)),
            pltpu.SemaphoreType.DMA((2, cols)),
            pltpu.SemaphoreType.DMA((cols,)),
            pltpu.SemaphoreType.DMA((cols,)),
            pltpu.SemaphoreType.DMA((cols,)),
            pltpu.SemaphoreType.DMA((9,)),
        ],
        compiler_params=pltpu.CompilerParams(
            collective_id=2, has_side_effects=True, vmem_limit_bytes=60 << 20
        ),
        cost_estimate=pl.CostEstimate(
            flops=12 * cols * rows * width * units,
            bytes_accessed=800 << 20,
            transcendentals=cols * rows * units,
        ),
        name="feed_forward",
    )(own_input, resid, grad_rows, *weights)


def finish_kernel(
    cols,
    ig_ref,
    gq_ref,
    go_ref,
    gain_ref,
    gin_ref,
    sq_ref,
    so_ref,
    gsum_ref,
    q_keep,
    q_sib,
    q_a1,
    q_a2,
    q_b1,
    q_b2,
    q_z,
    o_keep,
    o_sib,
    o_a1,
    o_a2,
    o_b1,
    o_b2,
    o_z,
    gain_now,
    gain_in,
    ig_sems,
    gain_sems,
    q_sems,
    o_sems,
    qz_sems,
    oz_sems,
    local_sems,
):
    group, core, mate, row, col = place()
    pair = group - core
    high = pair // 2
    sibling = (pair + 1 - core, row, col)
    over_x = (group, 1 - row, col)
    over_y = (2 * (1 - high) + core, row, col)
    width = gin_ref.shape[2]

    def line(step):
        return lax.rem(col + step + cols, cols)

    barrier = pltpu.get_barrier_semaphore()

    def greet(device):
        pl.semaphore_signal(barrier, inc=1, device_id=device, device_id_type=MESH_IDS)

    greet(sibling)
    greet(over_x)
    greet(over_y)
    for step in range(1, cols):
        greet((mate, core, line(step)))
        greet((group, row, line(step)))

    @pl.when(core != row)
    def _():
        greet((mate, core, col))

    pl.semaphore_wait(barrier, 2 * cols + 1 + (core - row) * (core - row))

    def remote(src, dst, sems, at, device):
        return pltpu.make_async_remote_copy(
            src_ref=src,
            dst_ref=dst,
            send_sem=sems.at[0, at],
            recv_sem=sems.at[1, at],
            device_id=device,
            device_id_type=MESH_IDS,
        )

    def lanes(block, size):
        return pl.ds(pl.multiple_of(block * size, size), size)

    matrices = (
        (gq_ref, sq_ref, q_keep, q_sib, q_a1, q_a2, q_b1, q_b2, q_z, q_sems, qz_sems),
        (go_ref, so_ref, o_keep, o_sib, o_a1, o_a2, o_b1, o_b2, o_z, o_sems, oz_sems),
    )

    def moves(m):
        grads, out, keep, sib, a1, a2, b1, b2, zb, sems, z_sems = matrices[m]
        return dict(
            s0=remote(grads.at[:, 1 - core], sib, sems, 0, sibling),
            a1=remote(grads.at[:, core, 1 - row], a1, sems, 1, over_x),
            a2=remote(keep.at[1 - high, row], a2, sems, 2, over_y),
            b1=remote(sib.at[1 - high], b1, sems, 3, over_y),
            b2=remote(sib.at[high, 1 - row], b2, sems, 4, over_x),
            own=pltpu.make_async_copy(grads.at[:, core], keep, local_sems.at[m]),
        )

    copies = (moves(0), moves(1))

    def rows_plus(into, more):
        rows = into.shape[0]
        step = min(32, rows)

        @pl.loop(0, rows // step)
        def _(at):
            here = pl.ds(pl.multiple_of(at * step, step), step)
            into[here, :] = (
                into[here, :].astype(jnp.float32) + more[here, :].astype(jnp.float32)
            ).astype(into.dtype)

    def token_copy(step, at):
        return remote(
            ig_ref.at[:, lanes(line(step), width)],
            gin_ref.at[at],
            ig_sems,
            step,
            (mate, core, line(step)),
        )

    own_tokens = pltpu.make_async_copy(
        ig_ref.at[:, lanes(col, width)], gin_ref.at[col], local_sems.at[2]
    )

    for m in range(2):
        copies[m]["s0"].start()
        copies[m]["a1"].start()
        copies[m]["own"].start()
    for step in range(1, cols):
        token_copy(step, col).start()

    @pl.when(core != row)
    def _():
        token_copy(0, col).start()

    @pl.when(core == row)
    def _():
        own_tokens.start()

    gain_load = pltpu.make_async_copy(gain_ref, gain_now.at[0], local_sems.at[3])
    gain_load.start()
    gain_load.wait()
    near = (
        sibling,
        over_x,
        over_y,
        (group, row, col + 1 - 2 * lax.rem(col, 2)),
        (group, row, lax.rem(col + cols // 2, cols)),
    )

    def gain_round(at):
        exchange = remote(gain_now.at[at], gain_in.at[at], gain_sems, at, near[at])
        exchange.start()
        exchange.wait()
        gain_now[at + 1] = gain_now[at] + gain_in[at]

    gain_round(0)
    for m in range(2):
        copies[m]["s0"].wait()
        copies[m]["b1"].start()
    gain_round(1)
    for m in range(2):
        grads, out, keep, sib, a1, a2, b1, b2, zb, sems, z_sems = matrices[m]
        copies[m]["own"].wait()
        copies[m]["a1"].wait()
        rows_plus(keep.at[1 - high, row], a1.at[1 - high])
        copies[m]["a2"].start()
    for m in range(2):
        grads, out, keep, sib, a1, a2, b1, b2, zb, sems, z_sems = matrices[m]
        copies[m]["b1"].wait()
        rows_plus(sib.at[high, 1 - row], b1.at[1 - row])
        copies[m]["b2"].start()
    gain_round(2)
    for m in range(2):
        grads, out, keep, sib, a1, a2, b1, b2, zb, sems, z_sems = matrices[m]
        rows_plus(keep.at[high, row], a1.at[high])
        rows_plus(sib.at[high, row], b1.at[row])

    def z_moves(m, side, source):
        grads, out, keep, sib, a1, a2, b1, b2, zb, sems, z_sems = matrices[m]
        held = (keep, sib)[side]
        wide = zb.shape[3]
        return [
            pltpu.make_async_remote_copy(
                src_ref=held.at[high, row, :, lanes(line(step), wide)],
                dst_ref=zb.at[side, line(source(step))],
                send_sem=z_sems.at[0, side, step],
                recv_sem=z_sems.at[1, side, step],
                device_id=(group, row, line(step)),
                device_id_type=MESH_IDS,
            )
            for step in range(1, cols)
        ]

    for side, last_copy in ((0, "a2"), (1, "b2")):
        for m in range(2):
            grads, out, keep, sib, a1, a2, b1, b2, zb, sems, z_sems = matrices[m]
            copies[m][last_copy].wait()
            rows_plus((keep, sib)[side].at[high, row], (a2, b2)[side])
            for copy in z_moves(m, side, lambda step: 0):
                copy.start()
    gain_round(3)
    gain_round(4)
    gsum_ref[...] = gain_now[5]
    for side in range(2):
        for m in range(2):
            grads, out, keep, sib, a1, a2, b1, b2, zb, sems, z_sems = matrices[m]
            for copy in z_moves(m, side, lambda step: 0):
                copy.wait_send()
            for copy in z_moves(m, side, lambda step: -step):
                copy.wait_recv()
            held = (keep, sib)[side]
            wide = zb.shape[3]
            at_core = core if side == 0 else 1 - core
            rows = zb.shape[2]
            tall = min(32, rows)

            @pl.loop(0, rows // tall)
            def _(at):
                here = pl.ds(pl.multiple_of(at * tall, tall), tall)
                total = held[high, row, here, lanes(col, wide)].astype(jnp.float32)
                for step in range(1, cols):
                    total = total + zb[side, line(-step), here, :].astype(jnp.float32)
                out[at_core, here, :] = total

    for step in range(1, cols):
        token_copy(step, line(-step)).wait_recv()
        token_copy(step, col).wait_send()

    @pl.when(core != row)
    def _():
        token_copy(0, col).wait_recv()
        token_copy(0, col).wait_send()

    @pl.when(core == row)
    def _():
        own_tokens.wait()


def finish(input_grad, grad_q, grad_o, gains, cols):
    anywhere = pl.BlockSpec(memory_space=pl.ANY)
    in_vmem = pl.BlockSpec(memory_space=pltpu.VMEM)
    bf16, f32 = jnp.bfloat16, jnp.float32
    length, full = input_grad.shape
    rows = grad_q.shape[0] // 8

    def buffers(wide):
        return [
            pltpu.VMEM((2, 2, rows, wide), bf16),
            pltpu.VMEM((2, 2, rows, wide), bf16),
            pltpu.VMEM((2, rows, wide), bf16),
            pltpu.VMEM((rows, wide), bf16),
            pltpu.VMEM((2, rows, wide), bf16),
            pltpu.VMEM((rows, wide), bf16),
            pltpu.VMEM((2, cols, rows, wide // cols), bf16),
        ]

    wide_q, wide_o = grad_q.shape[1], grad_o.shape[1]
    return pl.pallas_call(
        functools.partial(finish_kernel, cols),
        out_shape=(
            jax.ShapeDtypeStruct((cols, length, full // cols), bf16),
            jax.ShapeDtypeStruct((2, rows, wide_q // cols), f32),
            jax.ShapeDtypeStruct((2, rows, wide_o // cols), f32),
            jax.ShapeDtypeStruct(gains.shape, f32),
        ),
        in_specs=[anywhere] * 4,
        out_specs=(anywhere, in_vmem, in_vmem, in_vmem),
        scratch_shapes=buffers(wide_q)
        + buffers(wide_o)
        + [
            pltpu.VMEM((6,) + gains.shape, f32),
            pltpu.VMEM((5,) + gains.shape, f32),
            pltpu.SemaphoreType.DMA((2, cols)),
            pltpu.SemaphoreType.DMA((2, 5)),
            pltpu.SemaphoreType.DMA((2, 5)),
            pltpu.SemaphoreType.DMA((2, 5)),
            pltpu.SemaphoreType.DMA((2, 2, cols)),
            pltpu.SemaphoreType.DMA((2, 2, cols)),
            pltpu.SemaphoreType.DMA((4,)),
        ],
        compiler_params=pltpu.CompilerParams(
            collective_id=3, has_side_effects=True, vmem_limit_bytes=40 << 20
        ),
        cost_estimate=pl.CostEstimate(flops=0, bytes_accessed=300 << 20, transcendentals=0),
        name="finish",
    )(
        input_grad,
        grad_q.reshape(2, 2, 2, rows, wide_q),
        grad_o.reshape(2, 2, 2, rows, wide_o),
        gains,
    )


def one_sequence_body(
    tokens,
    cotangent,
    lengths,
    deal_order,
    gain_attn,
    gain_ffn,
    w_query,
    key_value_weight,
    w_out,
    w_gate_up,
    w_down,
):
    seq_group, rows_local, width_local = tokens.shape
    row_count = lax.axis_size("row")
    col_count = lax.axis_size("col")
    full_width = width_local * col_count
    slot_len = rows_local * row_count
    group, core, mate, row, col = place()
    query_half = w_query.shape[1] // 2
    kv_half = key_value_weight.shape[2] // 2
    hidden = w_down.shape[1]

    def core_half(matrix, axis):
        width = matrix.shape[axis] // 2
        return lax.dynamic_slice_in_dim(matrix, core * width, width, axis)

    def joined(mine, other, at):
        return jnp.where(
            at == 0, jnp.concatenate([mine, other]), jnp.concatenate([other, mine])
        )

    def from_sibling(value):
        return lax.ppermute(value, "dp", SIBLINGS)

    def half_rows(matrix):
        return core_half(matrix, 0)

    pack_q = jnp.concatenate(
        [
            core_half(w_query, 1),
            core_half(key_value_weight[:, 0], 1),
            core_half(key_value_weight[:, 1], 1),
        ],
        axis=1,
    )
    pack_o = core_half(w_out, 1)
    gain_one = gain_attn.astype(jnp.float32)
    gain_two = gain_ffn.astype(jnp.float32)
    own_tokens, attn_input, weights_qkv, weights_out = start_exchange(
        tokens, pack_q, pack_o, gain_one, row_count, col_count
    )

    length = lax.dynamic_slice_in_dim(lengths, mate * seq_group + col, 1)
    line_lengths = lax.dynamic_slice_in_dim(lengths, mate * seq_group, seq_group)
    own_pos = core * rows_local + jnp.arange(rows_local, dtype=jnp.int32)
    line_live = (own_pos[None, :] < line_lengths[:, None]).astype(jnp.float32)
    own_live = (own_pos < length).astype(jnp.float32)[:, None]

    own_mats = (w_gate_up[:, 0], w_gate_up[:, 1], w_down)
    halves = tuple(half_rows(matrix) for matrix in own_mats)
    halves, attn_input = lax.optimization_barrier((halves, attn_input))
    far_mats = tuple(lax.ppermute(matrix, "row", OVER_X) for matrix in halves)
    sibling_mats = tuple(from_sibling(matrix) for matrix in far_mats)

    given = bring_cotangent(cotangent, deal_order, group * seq_group)
    given, attn_input = lax.optimization_barrier((given, attn_input))
    swapped = lax.ppermute(given, ("dp", "row"), CROSSED)
    line_cot = lax.all_gather(swapped, "col", axis=2, tiled=True)
    line_grad = line_live[:, :, None] * line_cot.astype(jnp.float32)
    grad_ffn = (RES_MULT * line_grad).astype(jnp.bfloat16).reshape(-1, full_width)
    own_grad = own_live * lax.dynamic_index_in_dim(line_cot, col, keepdims=False).astype(
        jnp.float32
    )

    cosine_table, sine_table = rope_tables(jnp.arange(slot_len, dtype=jnp.int32), HEAD_SIZE)
    cosine_table, sine_table = lax.optimization_barrier((cosine_table, sine_table))
    cosines = jnp.concatenate(
        [jnp.tile(cosine_table, (1, 6)), jnp.ones((slot_len, HEAD_SIZE), jnp.float32)], axis=1
    )
    turning = jnp.concatenate([-sine_table, sine_table], axis=1)
    sines = jnp.concatenate(
        [jnp.tile(turning, (1, 3)), jnp.zeros((slot_len, HEAD_SIZE), jnp.float32)], axis=1
    )
    own_float = own_tokens.astype(jnp.float32)
    scale_one = lax.rsqrt(jnp.mean(own_float * own_float, axis=1, keepdims=True) + EPSILON)
    projected, heads_out = attend_fast(
        length, attn_input, weights_qkv, cosines, sines, col_count
    )

    def summed_rows(partial):
        count = partial.shape[0] // 2
        mine = lax.dynamic_slice_in_dim(partial, core * count, count)
        other = lax.dynamic_slice_in_dim(partial, (1 - core) * count, count)
        return mine.astype(jnp.float32) + from_sibling(other).astype(jnp.float32)

    attn_rows = summed_rows(expand_local(heads_out, weights_out).astype(jnp.bfloat16))
    resid = own_float + RES_MULT * attn_rows
    scale_two = lax.rsqrt(jnp.mean(resid * resid, axis=1, keepdims=True) + EPSILON)
    own_ffn = (resid * scale_two * gain_two).astype(jnp.bfloat16)

    ffn_input, hidden_rows, grad_gate_rows, mlp_part, back_part = feed_forward(
        own_ffn,
        resid.astype(jnp.bfloat16),
        grad_ffn.reshape(col_count, rows_local, full_width),
        own_mats + far_mats + sibling_mats,
        col_count,
    )
    ffn_input = ffn_input.reshape(-1, full_width)
    hidden_rows = hidden_rows.reshape(-1, hidden)
    grad_gate_rows = grad_gate_rows.reshape(-1, 2 * hidden)
    grad_normed_two = jnp.sum(back_part.astype(jnp.float32), axis=0)

    out_cols = lax.psum_scatter(mlp_part, "col", scatter_dimension=2, tiled=True)
    given_pos = row * rows_local + jnp.arange(rows_local, dtype=jnp.int32)
    given_lengths = lax.dynamic_slice_in_dim(lengths, group * seq_group, seq_group)
    given_live = (given_pos[None, :] < given_lengths[:, None]).astype(jnp.float32)
    layer_out = given_live[:, :, None] * lax.ppermute(
        out_cols, ("dp", "row"), CROSSED
    ).astype(jnp.float32)

    def scatter_rows(matrix):
        return lax.psum_scatter(
            matrix.astype(jnp.bfloat16), ("dp", "row"), scatter_dimension=0, tiled=True
        ).astype(jnp.float32)

    sums_down = scatter_rows(token_outer(grad_ffn, hidden_rows))
    sums_gate_up = scatter_rows(token_outer(ffn_input, grad_gate_rows))
    sums_gate_up = sums_gate_up.reshape(-1, 2, hidden)

    weighted_two = grad_normed_two * gain_two
    inner_two = jnp.sum(weighted_two * resid, axis=1, keepdims=True)
    grad_resid = (
        own_grad + scale_two * weighted_two - resid * scale_two**3 * inner_two / full_width
    )
    gain_two_part = jnp.sum(grad_normed_two * resid * scale_two, axis=0)
    own_attn_grad = (RES_MULT * grad_resid).astype(jnp.bfloat16)
    grad_attn = joined(own_attn_grad, from_sibling(own_attn_grad), core)
    grad_heads = contract_local(grad_attn, weights_out).astype(jnp.bfloat16)
    grad_out = token_outer(grad_attn, heads_out).astype(jnp.bfloat16)
    grad_projected = attend_back_fast(
        length, projected, grad_heads, cosines, sines, col_count
    )
    grad_normed_one = summed_rows(expand_local(grad_projected, weights_qkv).astype(jnp.bfloat16))
    grad_qkv = token_outer(attn_input, grad_projected).astype(jnp.bfloat16)
    weighted_one = grad_normed_one * gain_one
    inner_one = jnp.sum(weighted_one * own_float, axis=1, keepdims=True)
    own_input_grad = (
        grad_resid
        + scale_one * weighted_one
        - own_float * scale_one**3 * inner_one / full_width
    ).astype(jnp.bfloat16)
    gain_one_part = jnp.sum(grad_normed_one * own_float * scale_one, axis=0)
    gains = jnp.stack([gain_one_part, gain_two_part]).reshape(8, -1)
    given_grad, sums_q, sums_o, gain_sums = finish(
        own_input_grad, grad_qkv, grad_out, gains, col_count
    )
    input_grad = given_grad.astype(jnp.float32)
    grad_gain_attn, grad_gain_ffn = gain_sums.reshape(2, full_width)

    def both_cores(sums):
        return jnp.concatenate([sums[0], sums[1]], axis=1)

    qk = query_half + kv_half
    out_query = both_cores(sums_q[:, :, :query_half])
    out_kv = jnp.stack(
        [
            both_cores(sums_q[:, :, query_half:qk]),
            both_cores(sums_q[:, :, qk:]),
        ],
        axis=1,
    )
    out_out = both_cores(sums_o)
    return (
        layer_out,
        input_grad,
        out_query,
        out_kv,
        out_out,
        sums_gate_up,
        sums_down,
        grad_gain_attn,
        grad_gain_ffn,
    )


def general_body(
    tokens,
    cotangent,
    lengths,
    deal_order,
    gain_attn,
    gain_ffn,
    w_query,
    key_value_weight,
    w_out,
    w_gate_up,
    w_down,
):
    seq_group, rows_local, width_local = tokens.shape
    row_count = lax.axis_size("row")
    col_count = lax.axis_size("col")
    full_width = width_local * col_count
    slot_len = rows_local * row_count
    total_rows = seq_group * rows_local
    head_size = HEAD_SIZE
    query_width = w_query.shape[1]
    kv_width = key_value_weight.shape[2]
    kv_heads = kv_width // head_size
    group_size = query_width // kv_width
    group_index = lax.axis_index("dp")
    row_index = lax.axis_index("row")
    col_index = lax.axis_index("col")
    matrices = {
        "qkv": jnp.concatenate(
            [w_query, key_value_weight.reshape(key_value_weight.shape[0], 2 * kv_width)], axis=1
        ),
        "out": w_out,
        "gate_up": w_gate_up,
        "down": w_down,
    }

    def contract_with(operand, which_one):
        return contract_rows(operand, matrices[which_one])

    def expand_with(operand, which_one):
        return expand_rows(operand, matrices[which_one])

    own_cotangent = bring_cotangent(cotangent, deal_order, group_index * seq_group)
    own_rows = tokens
    seq_lens = lax.dynamic_slice_in_dim(lengths, group_index * seq_group, seq_group)
    local_pos = row_index * rows_local + jnp.arange(rows_local, dtype=jnp.int32)
    key_pos = jnp.arange(slot_len, dtype=jnp.int32)
    live_rows = (local_pos[None, :] < seq_lens[:, None]).astype(jnp.float32).reshape(total_rows, 1)
    cosine_table, sine_table = rope_tables(jnp.tile(local_pos, seq_group), head_size)
    own_tokens = own_rows.reshape(total_rows, width_local)
    wide_float = widen_cols(own_tokens).astype(jnp.float32)
    scale_one = lax.rsqrt(jnp.mean(wide_float * wide_float, axis=1, keepdims=True) + EPSILON)
    gain_one = gain_attn.astype(jnp.float32)
    first_normed = wide_float * scale_one
    attn_input = (first_normed * gain_one).astype(jnp.bfloat16)
    projected = contract_with(attn_input, "qkv")
    query_lin = projected[:, :query_width].reshape(total_rows, query_width // head_size, head_size)
    key_lin = projected[:, query_width : query_width + kv_width].reshape(
        total_rows, kv_heads, head_size
    )
    value_lin = projected[:, query_width + kv_width :]
    query_rows = rotary_embed(query_lin, cosine_table, sine_table).astype(jnp.bfloat16)
    keys_own = (
        rotary_embed(key_lin, cosine_table, sine_table)
        .astype(jnp.bfloat16)
        .reshape(seq_group, rows_local, kv_width)
    )
    values_own = value_lin.astype(jnp.bfloat16).reshape(seq_group, rows_local, kv_width)
    all_keys, all_values = (
        lax.all_gather(keys_own, "row", axis=1, tiled=True),
        lax.all_gather(values_own, "row", axis=1, tiled=True),
    )
    query_split = query_rows.reshape(seq_group, rows_local, kv_heads, group_size, head_size)
    key_split = all_keys.reshape(seq_group, slot_len, kv_heads, head_size)
    value_split = all_values.reshape(seq_group, slot_len, kv_heads, head_size)

    def forward_seq(inputs):
        return attend(inputs, key_pos, local_pos)

    mixed_heads, row_max, row_sums = lax.map(
        forward_seq, (query_split, key_split, value_split, seq_lens)
    )
    heads_out = mixed_heads.reshape(total_rows, query_width).astype(jnp.bfloat16)
    attn_local = narrow_cols(expand_with(heads_out, "out"))
    resid = own_tokens.astype(jnp.float32) + RES_MULT * attn_local
    gain_two = lax.dynamic_slice_in_dim(
        gain_ffn.astype(jnp.float32), col_index * width_local, width_local
    )
    scale_two = lax.rsqrt(sum_over_cols(jnp.sum(resid * resid, axis=1)) / full_width + EPSILON)[
        :, None
    ]
    normed_two = resid * scale_two
    ffn_input = widen_cols((normed_two * gain_two).astype(jnp.bfloat16))
    gate_up = contract_with(ffn_input, "gate_up")
    gate = gate_up[:, 0]
    upward = gate_up[:, 1]
    sigmoid_gate = jax.nn.sigmoid(gate)
    silu_gate = gate * sigmoid_gate
    hidden = (silu_gate * upward).astype(jnp.bfloat16)
    ffn_local = narrow_cols(expand_with(hidden, "down"))
    layer_out = live_rows * (resid + RES_MULT * ffn_local)
    grad_rows = live_rows * own_cotangent.reshape(total_rows, width_local).astype(jnp.float32)
    grad_ffn = widen_cols((RES_MULT * grad_rows).astype(jnp.bfloat16))
    grad_hidden = contract_with(grad_ffn, "down")
    grad_down = token_outer(grad_ffn, hidden)
    slope = sigmoid_gate * (1.0 + gate * (1.0 - sigmoid_gate))
    grad_gate_rows = jnp.stack(
        [grad_hidden * upward * slope, grad_hidden * silu_gate], axis=1
    ).astype(jnp.bfloat16)
    grad_gate_up = token_outer(ffn_input, grad_gate_rows)
    grad_normed_two = narrow_cols(expand_with(grad_gate_rows, "gate_up"))
    weighted_two = grad_normed_two * gain_two
    inner_two = sum_over_cols(jnp.sum(weighted_two * resid, axis=1))[:, None]
    grad_resid = (
        grad_rows + scale_two * weighted_two - resid * scale_two**3 * inner_two / full_width
    )
    gain_two_part = jnp.sum(grad_normed_two * normed_two, axis=0)
    grad_attn = widen_cols((RES_MULT * grad_resid).astype(jnp.bfloat16))
    grad_heads = contract_with(grad_attn, "out").astype(jnp.bfloat16)
    grad_out = token_outer(grad_attn, heads_out)
    grad_split = grad_heads.reshape(seq_group, rows_local, kv_heads, group_size, head_size)

    def backward_seq(inputs):
        return attend_back(inputs, key_pos, local_pos)

    grad_query, grad_key, grad_value = lax.map(
        backward_seq, (query_split, key_split, value_split, grad_split, row_max, row_sums, seq_lens)
    )
    key_part, value_part = (
        lax.psum_scatter(
            grad_key.reshape(seq_group, slot_len, kv_width).astype(jnp.bfloat16),
            "row",
            scatter_dimension=1,
            tiled=True,
        ).astype(jnp.float32),
        lax.psum_scatter(
            grad_value.reshape(seq_group, slot_len, kv_width).astype(jnp.bfloat16),
            "row",
            scatter_dimension=1,
            tiled=True,
        ).astype(jnp.float32),
    )
    query_back = rotary_embed(
        grad_query.reshape(total_rows, query_width // head_size, head_size),
        cosine_table,
        -sine_table,
    ).reshape(total_rows, query_width)
    key_back = rotary_embed(
        key_part.reshape(total_rows, kv_heads, head_size), cosine_table, -sine_table
    ).reshape(total_rows, kv_width)
    grad_projected = jnp.concatenate(
        [query_back, key_back, value_part.reshape(total_rows, kv_width)], axis=1
    ).astype(jnp.bfloat16)
    grad_qkv = token_outer(attn_input, grad_projected)
    grad_normed_one = expand_with(grad_projected, "qkv")
    weighted_one = grad_normed_one * gain_one
    inner_one = jnp.sum(weighted_one * wide_float, axis=1, keepdims=True)
    input_part = scale_one * weighted_one - wide_float * scale_one**3 * inner_one / full_width
    input_grad = grad_resid + narrow_cols(input_part)
    gain_one_part = jnp.sum(grad_normed_one * first_normed, axis=0)
    gain_two_full = lax.dynamic_update_slice_in_dim(
        jnp.zeros((full_width,), jnp.float32), gain_two_part, col_index * width_local, 0
    )
    grad_gain_attn, grad_gain_ffn = lax.psum((gain_one_part, gain_two_full), ("dp", "row", "col"))
    sums_qkv, sums_out, sums_gate_up, sums_down = (
        lax.psum_scatter(
            grad_qkv.astype(jnp.bfloat16), ("dp", "row"), scatter_dimension=0, tiled=True
        ).astype(jnp.float32),
        lax.psum_scatter(
            grad_out.astype(jnp.bfloat16), ("dp", "row"), scatter_dimension=0, tiled=True
        ).astype(jnp.float32),
        lax.psum_scatter(
            grad_gate_up.astype(jnp.bfloat16), ("dp", "row"), scatter_dimension=0, tiled=True
        ).astype(jnp.float32),
        lax.psum_scatter(
            grad_down.astype(jnp.bfloat16), ("dp", "row"), scatter_dimension=0, tiled=True
        ).astype(jnp.float32),
    )
    out_query = sums_qkv[:, :query_width]
    out_kv = sums_qkv[:, query_width:].reshape(sums_qkv.shape[0], 2, kv_width)
    return (
        layer_out.reshape(seq_group, rows_local, width_local),
        input_grad.reshape(seq_group, rows_local, width_local),
        out_query,
        out_kv,
        sums_out,
        sums_gate_up,
        sums_down,
        grad_gain_attn,
        grad_gain_ffn,
    )


def body(tokens, cotangent, lengths, deal_order, gain_attn, gain_ffn, w_query, key_value_weight, *rest):
    sizes = (lax.axis_size("dp"), lax.axis_size("row"), lax.axis_size("col"))
    one_each = sizes == (4, 2, 4) and tokens.shape[0] == sizes[2]
    pairs = w_query.shape[1] == 8 * HEAD_SIZE and key_value_weight.shape[2] == 2 * HEAD_SIZE
    chosen = one_sequence_body if one_each and pairs else general_body
    return chosen(
        tokens, cotangent, lengths, deal_order, gain_attn, gain_ffn, w_query, key_value_weight, *rest
    )


def solution(mesh):
    placed = (
        P("dp", "row", "col"),
        P("dp", "row", "col"),
        P(),
        P(),
        P(),
        P(),
        P("row", "col"),
        P("row", None, "col"),
        P("row", "col"),
        P("row", None, "col"),
        P("row", "col"),
    )
    return jax.shard_map(
        body,
        mesh=mesh,
        in_specs=placed,
        out_specs=(
            P("dp", "row", "col"),
            P("dp", "row", "col"),
            P(("dp", "row"), "col"),
            P(("dp", "row"), None, "col"),
            P(("dp", "row"), "col"),
            P(("dp", "row"), None, "col"),
            P(("dp", "row"), "col"),
            P(),
            P(),
        ),
        check_vma=False,
    )
```

```python
import functools

import jax
import jax.numpy as jnp
from jax import lax
from jax.experimental import pallas as pl
from jax.experimental.pallas import tpu as pltpu
from jax.sharding import PartitionSpec as P

HEAD_SIZE = 64


EPSILON = 1e-05
THETA = 10000000.0
ATTN_MULT = 0.015625
RES_MULT = 0.22
MASKED = -1e30


def rope_tables(positions, head_size):
    halves = jnp.arange(head_size // 2, dtype=jnp.float32)
    inverse_freq = THETA ** (-(halves * 2.0) / head_size)
    angles = positions.astype(jnp.float32)[:, None] * inverse_freq[None, :]
    return (jnp.cos(angles), jnp.sin(angles))


def rotary_embed(value_rows, cosine_table, sine_table):
    middle = value_rows.shape[-1] // 2
    first_half = value_rows[..., :middle]
    second_half = value_rows[..., middle:]
    cos_part = cosine_table[:, None, :]
    sin_part = sine_table[:, None, :]
    return jnp.concatenate(
        [
            first_half * cos_part - second_half * sin_part,
            second_half * cos_part + first_half * sin_part,
        ],
        axis=-1,
    )


def widen_cols(value_rows):
    return lax.all_gather(value_rows, "col", axis=1, tiled=True)


def narrow_cols(value_rows):
    return lax.psum_scatter(value_rows, "col", scatter_dimension=1, tiled=True)


def sum_over_cols(value_rows):
    return lax.psum(value_rows, "col")


def contract_local(operand, matrix):
    return lax.dot_general(
        operand, matrix, (((1,), (0,)), ((), ())), preferred_element_type=jnp.float32
    )


def expand_local(operand, matrix):
    trailing = tuple(range(1, operand.ndim))
    return lax.dot_general(
        operand, matrix, ((trailing, trailing), ((), ())), preferred_element_type=jnp.float32
    )


def token_outer(features, grads):
    return lax.dot_general(
        features, grads, (((0,), (0,)), ((), ())), preferred_element_type=jnp.float32
    )


def contract_rows(operand, matrix):
    return contract_local(operand, lax.all_gather(matrix, "row", axis=0, tiled=True))


def expand_rows(operand, matrix):
    return expand_local(operand, lax.all_gather(matrix, "row", axis=0, tiled=True))


def split_keys(key_seq, value_seq, key_pos):
    slot_len = key_seq.shape[0]
    width = min(512, slot_len)
    count = slot_len // width
    return (
        key_seq.reshape(count, width, key_seq.shape[1], key_seq.shape[2]),
        value_seq.reshape(count, width, value_seq.shape[1], value_seq.shape[2]),
        key_pos.reshape(count, width),
    )


def block_scores(query_seq, key_block, pos_block, query_pos, length):
    scores = (
        jnp.einsum("qkgd,tkd->kgqt", query_seq, key_block, preferred_element_type=jnp.float32)
        * ATTN_MULT
    )
    allowed = (pos_block[None, :] <= query_pos[:, None]) & (pos_block[None, :] < length)
    return jnp.where(allowed, scores, MASKED)


def attend(inputs, key_pos, query_pos):
    query_seq, key_seq, value_seq, length = inputs
    key_blocks, value_blocks, pos_blocks = split_keys(key_seq, value_seq, key_pos)
    stat_shape = (query_seq.shape[1], query_seq.shape[2], query_seq.shape[0], 1)

    def gather_stats(carry, entry):
        running_max, running_sum = carry
        key_block, pos_block = entry
        scores = block_scores(query_seq, key_block, pos_block, query_pos, length)
        new_max = jnp.maximum(running_max, jnp.max(scores, axis=-1, keepdims=True))
        new_sum = running_sum * jnp.exp(running_max - new_max) + jnp.sum(
            jnp.exp(scores - new_max), axis=-1, keepdims=True
        )
        return ((new_max, new_sum), None)

    start_stats = (jnp.full(stat_shape, MASKED, jnp.float32), jnp.zeros(stat_shape, jnp.float32))
    (row_max, row_sums), unused = lax.scan(gather_stats, start_stats, (key_blocks, pos_blocks))

    def mix_values(running, entry):
        key_block, value_block, pos_block = entry
        scores = block_scores(query_seq, key_block, pos_block, query_pos, length)
        weights = jnp.exp(scores - row_max) / row_sums
        return (
            running
            + jnp.einsum(
                "kgqt,tkd->qkgd",
                weights.astype(jnp.bfloat16),
                value_block,
                preferred_element_type=jnp.float32,
            ),
            None,
        )

    start_mix = jnp.zeros(query_seq.shape, jnp.float32)
    mixed_heads, unused = lax.scan(mix_values, start_mix, (key_blocks, value_blocks, pos_blocks))
    return (mixed_heads, row_max, row_sums)


def attend_back(inputs, key_pos, query_pos):
    query_seq, key_seq, value_seq, grad_mixed, row_max, row_sums, length = inputs
    key_blocks, value_blocks, pos_blocks = split_keys(key_seq, value_seq, key_pos)

    def block_weights(key_block, value_block, pos_block):
        scores = block_scores(query_seq, key_block, pos_block, query_pos, length)
        weights = jnp.exp(scores - row_max) / row_sums
        grad_weights = jnp.einsum(
            "qkgd,tkd->kgqt", grad_mixed, value_block, preferred_element_type=jnp.float32
        )
        return (weights, grad_weights)

    def gather_centre(running, entry):
        weights, grad_weights = block_weights(*entry)
        return (running + jnp.sum(weights * grad_weights, axis=-1, keepdims=True), None)

    start_centre = jnp.zeros(row_max.shape, jnp.float32)
    centre, unused = lax.scan(gather_centre, start_centre, (key_blocks, value_blocks, pos_blocks))

    def grads_block(running, entry):
        key_block = entry[0]
        weights, grad_weights = block_weights(*entry)
        grad_scores = (weights * (grad_weights - centre)).astype(jnp.bfloat16)
        grad_query = (
            running
            + jnp.einsum(
                "kgqt,tkd->qkgd", grad_scores, key_block, preferred_element_type=jnp.float32
            )
            * ATTN_MULT
        )
        grad_key = (
            jnp.einsum("kgqt,qkgd->tkd", grad_scores, query_seq, preferred_element_type=jnp.float32)
            * ATTN_MULT
        )
        grad_value = jnp.einsum(
            "kgqt,qkgd->tkd",
            weights.astype(jnp.bfloat16),
            grad_mixed,
            preferred_element_type=jnp.float32,
        )
        return (grad_query, (grad_key, grad_value))

    start_query = jnp.zeros(query_seq.shape, jnp.float32)
    grad_query, (grad_key, grad_value) = lax.scan(
        grads_block, start_query, (key_blocks, value_blocks, pos_blocks)
    )
    return (grad_query, grad_key.reshape(key_seq.shape), grad_value.reshape(value_seq.shape))


MESH_IDS = pl.DeviceIdType.MESH
SIBLINGS = [(0, 1), (1, 0), (2, 3), (3, 2)]
OVER_X = [(0, 1), (1, 0)]
CROSSED = [((2 * y + c) * 2 + x, (2 * y + x) * 2 + c) for y in (0, 1) for c in (0, 1) for x in (0, 1)]


def pick_sequences(everyone, deal_order, first, count):
    slots = jnp.arange(deal_order.shape[0], dtype=jnp.int32)
    inverse = jnp.sum(jnp.where(deal_order[None, :] == slots[:, None], slots[None, :], 0), axis=1)
    return jnp.concatenate(
        [
            lax.dynamic_slice_in_dim(
                everyone, lax.dynamic_index_in_dim(inverse, first + at, keepdims=False), 1
            )
            for at in range(count)
        ]
    )


def bring_cotangent(cotangent, deal_order, first):
    everyone = lax.all_gather(cotangent, "dp", axis=0, tiled=True)
    return pick_sequences(everyone, deal_order, first, cotangent.shape[0])


def place():
    group = lax.axis_index("dp")
    core = lax.rem(group, 2)
    row = lax.axis_index("row")
    return group, core, group - core + row, row, lax.axis_index("col")


def lined(index, step, count):
    return lax.rem(index + step + count, count)


def aligned(block, size):
    return pl.ds(pl.multiple_of(block * size, size), size)


def greet(device):
    pl.semaphore_signal(
        pltpu.get_barrier_semaphore(), inc=1, device_id=device, device_id_type=MESH_IDS
    )


def remote(src, dst, sems, at, device):
    return pltpu.make_async_remote_copy(
        src_ref=src,
        dst_ref=dst,
        send_sem=sems.at[0, at],
        recv_sem=sems.at[1, at],
        device_id=device,
        device_id_type=MESH_IDS,
    )


def weight_copies(cols, own, full, sems, x_sems):
    group, core, mate, row, col = place()
    tall, wide = own.shape

    def block(of_row, of_col):
        return full.at[aligned(of_row, tall), aligned(of_col, wide)]

    def line(step):
        return lined(col, step, cols)

    over = (group, 1 - row, col)
    steps = range(1, cols)
    along = [remote(own, block(row, col), sems, k, (group, row, line(k))) for k in steps]
    arrive = [remote(own, block(row, line(-k)), sems, k, (group, row, line(k))) for k in steps]
    across = [remote(own, block(row, col), x_sems, 0, over)] + [
        remote(block(row, line(-k)), block(row, line(-k)), x_sems, k, over) for k in steps
    ]
    landed = [remote(own, block(1 - row, line(-k)), x_sems, k, over) for k in range(cols)]
    return along, arrive, across, landed, block(row, col)


def start_kernel(
    cols,
    tok_ref,
    pq_ref,
    gain_ref,
    x_ref,
    a_ref,
    wq_ref,
    x_buf,
    a_buf,
    tok_sems,
    q_sems,
    qx_sems,
    a_sems,
    local_sems,
):
    group, core, mate, row, col = place()
    width = tok_ref.shape[2]
    length = x_buf.shape[0]
    sibling = (group + 1 - 2 * core, row, col)

    def line(step):
        return lined(col, step, cols)

    for step in range(1, cols):
        greet((mate, core, line(step)))
        greet((group, row, line(step)))
    greet((group, 1 - row, col))
    greet(sibling)

    @pl.when(core != row)
    def _():
        greet((mate, core, col))

    pl.semaphore_wait(
        pltpu.get_barrier_semaphore(), 2 * cols + (core - row) * (core - row)
    )

    along, arrive, across, landed, own_place = weight_copies(cols, pq_ref, wq_ref, q_sems, qx_sems)
    own_q = pltpu.make_async_copy(pq_ref, own_place, local_sems.at[0])

    def token_copy(step, into):
        return remote(
            tok_ref.at[line(step)],
            x_buf.at[:, aligned(into, width)],
            tok_sems,
            step,
            (mate, core, line(step)),
        )

    own_tokens = pltpu.make_async_copy(
        tok_ref.at[col], x_buf.at[:, aligned(col, width)], local_sems.at[1]
    )
    for step in range(1, cols):
        token_copy(step, col).start()

    @pl.when(core != row)
    def _():
        token_copy(0, col).start()

    @pl.when(core == row)
    def _():
        own_tokens.start()

    for copy in along:
        copy.start()
    across[0].start()
    own_q.start()
    for step in range(1, cols):
        token_copy(step, line(-step)).wait_recv()

    @pl.when(core != row)
    def _():
        token_copy(0, col).wait_recv()

    @pl.when(core == row)
    def _():
        own_tokens.wait()

    keep_x = pltpu.make_async_copy(x_buf, x_ref, local_sems.at[2])
    keep_x.start()
    tall = min(64, length)

    @pl.loop(0, length // tall)
    def _(at):
        here = aligned(at, tall)
        now = x_buf[here, :].astype(jnp.float32)
        scale = lax.rsqrt(jnp.mean(now * now, axis=1, keepdims=True) + EPSILON)
        a_buf[here, :] = (now * scale * gain_ref[...]).astype(jnp.bfloat16)

    def a_copy(of_core):
        return remote(a_buf, a_ref.at[aligned(of_core, length)], a_sems, 0, sibling)

    own_a = pltpu.make_async_copy(a_buf, a_ref.at[aligned(core, length)], local_sems.at[3])
    a_copy(core).start()
    own_a.start()
    for step in range(1, cols):
        arrive[step - 1].wait_recv()
        across[step].start()
    for step in range(1, cols):
        token_copy(step, col).wait_send()

    @pl.when(core != row)
    def _():
        token_copy(0, col).wait_send()

    keep_x.wait()
    own_a.wait()
    a_copy(core).wait_send()
    a_copy(1 - core).wait_recv()
    own_q.wait()
    for copy in along + across:
        copy.wait_send()
    for copy in landed:
        copy.wait_recv()


def start_exchange(tokens, pack_q, gain, rows, cols):
    anywhere = pl.BlockSpec(memory_space=pl.ANY)
    seqs, length, width = tokens.shape
    weight_rows = pack_q.shape[0]
    full = width * cols
    return pl.pallas_call(
        functools.partial(start_kernel, cols),
        out_shape=(
            jax.ShapeDtypeStruct((length, full), tokens.dtype),
            jax.ShapeDtypeStruct((2 * length, full), tokens.dtype),
            jax.ShapeDtypeStruct((weight_rows * rows, pack_q.shape[1] * cols), pack_q.dtype),
        ),
        in_specs=[anywhere] * 2 + [pl.BlockSpec(memory_space=pltpu.VMEM)],
        out_specs=(anywhere,) * 3,
        scratch_shapes=[
            pltpu.VMEM((length, full), tokens.dtype),
            pltpu.VMEM((length, full), tokens.dtype),
        ]
        + [pltpu.SemaphoreType.DMA((2, cols))] * 3
        + [pltpu.SemaphoreType.DMA((2, 1)), pltpu.SemaphoreType.DMA((4,))],
        compiler_params=pltpu.CompilerParams(
            collective_id=1, has_side_effects=True, vmem_limit_bytes=16 << 20
        ),
        cost_estimate=pl.CostEstimate(flops=0, bytes_accessed=400 << 20, transcendentals=0),
        name="start_exchange",
    )(tokens, pack_q, gain.reshape(1, full))


def gather_kernel(cols, own_ref, after_ref, full_ref, sems, x_sems, local_sem):
    group, core, mate, row, col = place()
    for step in range(1, cols):
        greet((group, row, lined(col, step, cols)))
    greet((group, 1 - row, col))
    pl.semaphore_wait(pltpu.get_barrier_semaphore(), cols)
    along, arrive, across, landed, own_place = weight_copies(cols, own_ref, full_ref, sems, x_sems)
    own = pltpu.make_async_copy(own_ref, own_place, local_sem)
    for copy in along:
        copy.start()
    across[0].start()
    own.start()
    for step in range(1, cols):
        arrive[step - 1].wait_recv()
        across[step].start()
    own.wait()
    for copy in along + across:
        copy.wait_send()
    for copy in landed:
        copy.wait_recv()


def gather_weights(own, after, rows, cols):
    anywhere = pl.BlockSpec(memory_space=pl.ANY)
    return pl.pallas_call(
        functools.partial(gather_kernel, cols),
        out_shape=jax.ShapeDtypeStruct((own.shape[0] * rows, own.shape[1] * cols), own.dtype),
        in_specs=[anywhere] * 2,
        out_specs=anywhere,
        scratch_shapes=[
            pltpu.SemaphoreType.DMA((2, cols)),
            pltpu.SemaphoreType.DMA((2, cols)),
            pltpu.SemaphoreType.DMA(()),
        ],
        compiler_params=pltpu.CompilerParams(collective_id=4, has_side_effects=True),
        cost_estimate=pl.CostEstimate(flops=0, bytes_accessed=200 << 20, transcendentals=0),
        name="gather_weights",
    )(own, after)


def half_turn(wide):
    lanes = wide.shape[1]
    half = HEAD_SIZE // 2
    lane = lax.broadcasted_iota(jnp.int32, wide.shape, 1)
    return jnp.where(
        lax.rem(lane, HEAD_SIZE) < half,
        pltpu.roll(wide, lanes - half, 1),
        pltpu.roll(wide, half, 1),
    )


def both_heads(pair):
    lane = lax.broadcasted_iota(jnp.int32, pair.shape, 1)
    turned = pltpu.roll(pair, HEAD_SIZE, 1)
    low = lane < HEAD_SIZE
    return jnp.where(low, pair, turned), jnp.where(low, turned, pair)


def keep_head(pair, side):
    lane = lax.broadcasted_iota(jnp.int32, pair.shape, 1)
    mine = lane < HEAD_SIZE if side == 0 else lane >= HEAD_SIZE
    return jnp.where(mine, pair, jnp.zeros_like(pair))


def dot_nn(a, b):
    return lax.dot_general(a, b, (((1,), (0,)), ((), ())), preferred_element_type=jnp.float32)


def dot_nt(a, b):
    return lax.dot_general(a, b, (((1,), (1,)), ((), ())), preferred_element_type=jnp.float32)


def dot_tn(a, b):
    return lax.dot_general(a, b, (((0,), (0,)), ((), ())), preferred_element_type=jnp.float32)


PAIR = 2 * HEAD_SIZE


def attend_kernel(block, len_ref, a_ref, w_ref, cos_ref, sin_ref, qkv_ref, z_ref, q_all, k_two, v_two):
    rows = a_ref.shape[0]
    heads = q_all.shape[0]
    length = len_ref[0]

    @pl.loop(0, rows // block)
    def _(at):
        here = pl.ds(pl.multiple_of(at * block, block), block)
        lin = dot_nn(a_ref[here, :], w_ref[...])
        for part in range(heads // 2 + 1):
            lanes = slice(part * PAIR, (part + 1) * PAIR)
            now = lin[:, lanes]
            table = slice(0, PAIR) if part < heads // 2 else slice(PAIR, 2 * PAIR)
            now = now * cos_ref[here, table] + half_turn(now) * sin_ref[here, table]
            qkv_ref[here, lanes] = now.astype(jnp.bfloat16)
            if part < heads // 2:
                for side in range(2):
                    q_all[2 * part + side, here, :] = keep_head(now * ATTN_MULT, side).astype(
                        jnp.bfloat16
                    )
            else:
                keys, values = both_heads(now)
                k_two[here, :] = keys.astype(jnp.bfloat16)
                v_two[here, :] = values.astype(jnp.bfloat16)

    for at in range(rows // block):
        here = slice(at * block, (at + 1) * block)
        upto = (at + 1) * block
        row = lax.broadcasted_iota(jnp.int32, (block, upto), 0) + at * block
        key = lax.broadcasted_iota(jnp.int32, (block, upto), 1)
        allowed = key < jnp.minimum(row + 1, length)

        def one_head(head):
            scores = dot_nt(q_all[head, here, :], k_two[:upto, :])
            scores = jnp.where(allowed, scores, MASKED)
            top = jnp.max(scores, axis=1, keepdims=True)
            power = jnp.exp(scores - top)
            total = jnp.sum(power, axis=1, keepdims=True)
            return dot_nn(power.astype(jnp.bfloat16), v_two[:upto, :]) / total

        for pair in range(heads // 2):
            low = one_head(2 * pair)
            high = one_head(2 * pair + 1)
            lane = lax.broadcasted_iota(jnp.int32, low.shape, 1)
            z_ref[here, pair * PAIR : (pair + 1) * PAIR] = jnp.where(
                lane < HEAD_SIZE, low, high
            ).astype(jnp.bfloat16)


def attend_fast(length, inputs, weights, cosines, sines, groups):
    rows, depth = inputs.shape
    wide = weights.shape[1] // groups
    heads = (wide - PAIR) // HEAD_SIZE
    block = min(256, rows)
    return pl.pallas_call(
        functools.partial(attend_kernel, block),
        grid=(groups,),
        out_shape=(
            jax.ShapeDtypeStruct((rows, groups * wide), jnp.bfloat16),
            jax.ShapeDtypeStruct((rows, groups * heads * HEAD_SIZE), jnp.bfloat16),
        ),
        in_specs=[
            pl.BlockSpec(memory_space=pltpu.SMEM),
            pl.BlockSpec((rows, depth), lambda g: (0, 0)),
            pl.BlockSpec((depth, wide), lambda g: (0, g)),
            pl.BlockSpec((rows, 2 * PAIR), lambda g: (0, 0)),
            pl.BlockSpec((rows, 2 * PAIR), lambda g: (0, 0)),
        ],
        out_specs=(
            pl.BlockSpec((rows, wide), lambda g: (0, g)),
            pl.BlockSpec((rows, heads * HEAD_SIZE), lambda g: (0, g)),
        ),
        scratch_shapes=[
            pltpu.VMEM((heads, rows, PAIR), jnp.bfloat16),
            pltpu.VMEM((rows, PAIR), jnp.bfloat16),
            pltpu.VMEM((rows, PAIR), jnp.bfloat16),
        ],
        compiler_params=pltpu.CompilerParams(vmem_limit_bytes=48 << 20),
        cost_estimate=pl.CostEstimate(
            flops=2 * rows * depth * wide * groups + 2 * groups * heads * rows * rows * 128,
            bytes_accessed=2 * (rows * depth + depth * wide * groups + rows * wide * groups),
            transcendentals=groups * heads * rows * rows // 2,
        ),
        name="attend",
    )(length, inputs, weights, cosines, sines)


def attend_back_kernel(
    block, len_ref, qkv_ref, dz_ref, cos_ref, sin_ref, out_ref, q_all, z_all, k_two, v_two, k_acc, v_acc
):
    rows = qkv_ref.shape[0]
    heads = q_all.shape[0]
    length = len_ref[0]

    @pl.loop(0, rows // block)
    def _(at):
        here = pl.ds(pl.multiple_of(at * block, block), block)
        for part in range(heads // 2):
            lanes = slice(part * PAIR, (part + 1) * PAIR)
            queries = qkv_ref[here, lanes].astype(jnp.float32) * ATTN_MULT
            mixed = dz_ref[here, lanes].astype(jnp.float32)
            for side in range(2):
                q_all[2 * part + side, here, :] = keep_head(queries, side).astype(jnp.bfloat16)
                z_all[2 * part + side, here, :] = keep_head(mixed, side).astype(jnp.bfloat16)
        keys, values = both_heads(qkv_ref[here, heads * HEAD_SIZE :].astype(jnp.float32))
        k_two[here, :] = keys.astype(jnp.bfloat16)
        v_two[here, :] = values.astype(jnp.bfloat16)
        k_acc[here, :] = jnp.zeros((block, PAIR), jnp.float32)
        v_acc[here, :] = jnp.zeros((block, PAIR), jnp.float32)

    def turn_back(now, here, table):
        return (now * cos_ref[here, table] - half_turn(now) * sin_ref[here, table]).astype(
            jnp.bfloat16
        )

    for at in range(rows // block):
        here = slice(at * block, (at + 1) * block)
        upto = (at + 1) * block
        key = lax.broadcasted_iota(jnp.int32, (upto, block), 0)
        query = lax.broadcasted_iota(jnp.int32, (upto, block), 1) + at * block
        allowed = key < jnp.minimum(query + 1, length)

        def one_head(head):
            queries, mixed = q_all[head, here, :], z_all[head, here, :]
            scores = jnp.where(allowed, dot_nt(k_two[:upto, :], queries), MASKED)
            power = jnp.exp(scores - jnp.max(scores, axis=0, keepdims=True))
            weights = power * (1.0 / jnp.sum(power, axis=0, keepdims=True))
            back = dot_nt(v_two[:upto, :], mixed)
            centre = jnp.sum(weights * back, axis=0, keepdims=True)
            slope = (weights * (back - centre)).astype(jnp.bfloat16)
            k_acc[:upto, :] += dot_nn(slope, queries)
            v_acc[:upto, :] += dot_nn(weights.astype(jnp.bfloat16), mixed)
            return dot_tn(slope, k_two[:upto, :]) * ATTN_MULT

        for pair in range(heads // 2):
            low = one_head(2 * pair)
            high = one_head(2 * pair + 1)
            lane = lax.broadcasted_iota(jnp.int32, low.shape, 1)
            lanes = slice(pair * PAIR, (pair + 1) * PAIR)
            out_ref[here, lanes] = turn_back(
                jnp.where(lane < HEAD_SIZE, low, high), here, slice(0, PAIR)
            )

    @pl.loop(0, rows // block)
    def _(at):
        here = pl.ds(pl.multiple_of(at * block, block), block)
        keys, values = k_acc[here, :], v_acc[here, :]
        keys = keys + pltpu.roll(keys, HEAD_SIZE, 1)
        values = values + pltpu.roll(values, HEAD_SIZE, 1)
        lane = lax.broadcasted_iota(jnp.int32, keys.shape, 1)
        lanes = slice(heads * HEAD_SIZE, heads * HEAD_SIZE + PAIR)
        out_ref[here, lanes] = turn_back(
            jnp.where(lane < HEAD_SIZE, keys, values), here, slice(PAIR, 2 * PAIR)
        )


def attend_back_fast(length, projected, grad_mixed, cosines, sines, groups):
    rows = projected.shape[0]
    wide = projected.shape[1] // groups
    heads = (wide - PAIR) // HEAD_SIZE
    block = min(256, rows)
    return pl.pallas_call(
        functools.partial(attend_back_kernel, block),
        grid=(groups,),
        out_shape=jax.ShapeDtypeStruct((rows, groups * wide), jnp.bfloat16),
        in_specs=[
            pl.BlockSpec(memory_space=pltpu.SMEM),
            pl.BlockSpec((rows, wide), lambda g: (0, g)),
            pl.BlockSpec((rows, heads * HEAD_SIZE), lambda g: (0, g)),
            pl.BlockSpec((rows, 2 * PAIR), lambda g: (0, 0)),
            pl.BlockSpec((rows, 2 * PAIR), lambda g: (0, 0)),
        ],
        out_specs=pl.BlockSpec((rows, wide), lambda g: (0, g)),
        scratch_shapes=[
            pltpu.VMEM((heads, rows, PAIR), jnp.bfloat16),
            pltpu.VMEM((heads, rows, PAIR), jnp.bfloat16),
            pltpu.VMEM((rows, PAIR), jnp.bfloat16),
            pltpu.VMEM((rows, PAIR), jnp.bfloat16),
            pltpu.VMEM((rows, PAIR), jnp.float32),
            pltpu.VMEM((rows, PAIR), jnp.float32),
        ],
        compiler_params=pltpu.CompilerParams(vmem_limit_bytes=48 << 20),
        cost_estimate=pl.CostEstimate(
            flops=5 * groups * heads * rows * rows * 128,
            bytes_accessed=2 * (2 * rows * wide * groups + rows * heads * HEAD_SIZE * groups),
            transcendentals=groups * heads * rows * rows // 2,
        ),
        name="attend_back",
    )(length, projected, grad_mixed, cosines, sines)


def ffn_kernel(
    cols,
    own_ref,
    resid_ref,
    grad_ref,
    wg_own,
    wu_own,
    wd_own,
    wg_far,
    wu_far,
    wd_far,
    wg_sib,
    wu_sib,
    wd_sib,
    b_all,
    u_all,
    dgu_all,
    mlp_all,
    back_all,
    ggu_ref,
    gdn_ref,
    wg,
    wu,
    wd,
    b_buf,
    g_buf,
    u_buf,
    dg_buf,
    du_buf,
    mlp_buf,
    back_buf,
    turn_buf,
    w_sems,
    ag_send,
    ag_recv,
    back_send,
    back_recv,
    io_sems,
):
    group, core, mate, row, col = place()
    last = cols - 1
    depth = wg_own.shape[0]
    half = depth // 2
    units = wg_own.shape[1]
    tile = min(512, units)

    barrier = pltpu.get_barrier_semaphore()
    for step in range(1, cols):
        pl.semaphore_signal(
            barrier,
            inc=1,
            device_id=(group, row, lax.rem(col + step, cols)),
            device_id_type=MESH_IDS,
        )
    pl.semaphore_wait(barrier, cols - 1)

    def pass_on(src, at, to, way):
        return pltpu.make_async_remote_copy(
            src_ref=src,
            dst_ref=b_all.at[at],
            send_sem=ag_send.at[way, at],
            recv_sem=ag_recv.at[at],
            device_id=(group, row, to),
            device_id_type=MESH_IDS,
        )

    @pl.when(col < last)
    def _():
        pass_on(own_ref, col, col + 1, 0).start()

    @pl.when(col > 0)
    def _():
        pass_on(own_ref, col, col - 1, 1).start()

    def rows_at(first, size):
        return pl.ds(pl.multiple_of(first, half), size)

    own_copy = pltpu.make_async_copy(own_ref, b_all.at[col], io_sems.at[0])
    own_copy.start()
    load_resid = pltpu.make_async_copy(resid_ref, mlp_buf, io_sems.at[8])
    load_resid.start()
    far = (1 - row) * depth
    loads = []
    for at, (full, mine, across, sibling) in enumerate(
        ((wg, wg_own, wg_far, wg_sib), (wu, wu_own, wu_far, wu_sib), (wd, wd_own, wd_far, wd_sib))
    ):
        loads += [
            pltpu.make_async_copy(mine, full.at[rows_at(row * depth, depth)], w_sems.at[3 * at]),
            pltpu.make_async_copy(
                across, full.at[rows_at(far + core * half, half)], w_sems.at[3 * at + 1]
            ),
            pltpu.make_async_copy(
                sibling, full.at[rows_at(far + (1 - core) * half, half)], w_sems.at[3 * at + 2]
            ),
        ]
    for load in loads:
        load.start()
    own_copy.wait()
    for load in loads:
        load.wait()

    def order(at):
        inner_low = jnp.where(at < 2, 1 - at, at)
        inner_high = jnp.where(at == 3, 0, jnp.where(at == 0, 2, jnp.where(at == 1, 1, 3)))
        return jnp.where(
            col == 0,
            at,
            jnp.where(col == last, last - at, jnp.where(col == 1, inner_low, inner_high)),
        )

    def arrive(chunk):
        pass_on(b_all.at[chunk], chunk, col, 0).wait_recv()

        @pl.when((chunk < col) & (col < last))
        def _():
            pass_on(b_all.at[chunk], chunk, col + 1, 0).start()

        @pl.when((chunk > col) & (col > 0))
        def _():
            pass_on(b_all.at[chunk], chunk, col - 1, 1).start()

    def outputs(chunk):
        return (
            pltpu.make_async_copy(u_buf, u_all.at[chunk], io_sems.at[1]),
            pltpu.make_async_copy(dg_buf, dgu_all.at[chunk, :, 0:units], io_sems.at[2]),
            pltpu.make_async_copy(du_buf, dgu_all.at[chunk, :, units : 2 * units], io_sems.at[3]),
        )

    def mlp_out(chunk):
        return pltpu.make_async_copy(mlp_buf, mlp_all.at[chunk], io_sems.at[4])

    def back_out(at, chunk):
        return pltpu.make_async_remote_copy(
            src_ref=back_buf.at[slot_of(at)],
            dst_ref=back_all.at[col],
            send_sem=back_send.at[at],
            recv_sem=back_recv.at[col],
            device_id=(group, row, chunk),
            device_id_type=MESH_IDS,
        )

    def slot_of(at):
        return lax.rem(at, cols - 1)

    own_back = pltpu.make_async_copy(back_buf.at[0], back_all.at[col], io_sems.at[5])
    at_end = (col == 0) | (col == last)

    def one_chunk(at, unused):
        chunk = order(at)

        @pl.when(at_end & (at > 0))
        def _():
            arrive(order(at))

        @pl.when(jnp.logical_not(at_end) & (at == 1))
        def _():
            arrive(order(1))
            arrive(order(2))

        @pl.when(jnp.logical_not(at_end) & (at == 3))
        def _():
            arrive(order(3))

        load_b = pltpu.make_async_copy(b_all.at[chunk], b_buf, io_sems.at[6])
        load_g = pltpu.make_async_copy(grad_ref.at[chunk], g_buf, io_sems.at[7])
        load_b.start()
        load_g.start()

        @pl.when(at > 0)
        def _():
            for copy in outputs(order(at - 1)):
                copy.wait()

        load_b.wait()
        load_g.wait()

        @pl.loop(0, units // tile)
        def _(step):
            lanes = pl.ds(pl.multiple_of(step * tile, tile), tile)
            gate = dot_nn(b_buf[...], wg[:, lanes])
            upward = dot_nn(b_buf[...], wu[:, lanes])
            back = dot_nn(g_buf[...], wd[:, lanes])
            opened = 1.0 / (1.0 + jnp.exp(-gate))
            silu = gate * opened
            u_buf[:, lanes] = (silu * upward).astype(jnp.bfloat16)
            slope = opened * (1.0 + gate * (1.0 - opened))
            dg_buf[:, lanes] = (back * upward * slope).astype(jnp.bfloat16)
            du_buf[:, lanes] = (back * silu).astype(jnp.bfloat16)

        for copy in outputs(chunk):
            copy.start()

        @pl.when(at > 0)
        def _():
            mlp_out(order(at - 1)).wait()

        @pl.when(at == 0)
        def _():
            load_resid.wait()

        @pl.when(at == last)
        def _():
            own_back.wait()

        @pl.loop(0, 2 * depth // tile)
        def _(step):
            here = pl.ds(pl.multiple_of(step * tile, tile), tile)
            back = dot_nt(dg_buf[...], wg[here, :]) + dot_nt(du_buf[...], wu[here, :])
            back_buf[slot_of(at), :, here] = back.astype(jnp.bfloat16)
            added = jnp.where(at == 0, mlp_buf[:, here].astype(jnp.float32), 0.0)
            mlp_buf[:, here] = (added + RES_MULT * dot_nt(u_buf[...], wd[here, :])).astype(
                jnp.bfloat16
            )

        mlp_out(chunk).start()

        @pl.when(at == 0)
        def _():
            own_back.start()

        @pl.when(at > 0)
        def _():
            back_out(at, chunk).start()

        return unused

    lax.fori_loop(0, cols, one_chunk, 0)
    for copy in outputs(order(last)):
        copy.wait()
    mlp_out(order(last)).wait()

    rows = b_buf.shape[0]
    loads = []
    for chunk in range(cols):
        here = slice(chunk * rows, (chunk + 1) * rows)
        loads += [
            pltpu.make_async_copy(
                dgu_all.at[chunk, :, 0:units], wg.at[here], w_sems.at[chunk]
            ),
            pltpu.make_async_copy(
                dgu_all.at[chunk, :, units : 2 * units], wu.at[here], w_sems.at[cols + chunk]
            ),
            pltpu.make_async_copy(u_all.at[chunk], wd.at[here], w_sems.at[2 * cols + chunk]),
        ]
    for load in loads:
        load.start()
    for load in loads:
        load.wait()

    def results(at):
        here = aligned(at, rows)
        return (
            pltpu.make_async_copy(dg_buf, ggu_ref.at[here, 0:units], io_sems.at[1]),
            pltpu.make_async_copy(du_buf, ggu_ref.at[here, units : 2 * units], io_sems.at[2]),
            pltpu.make_async_copy(u_buf, gdn_ref.at[here], io_sems.at[3]),
        )

    def turned(source, into, at):
        load = pltpu.make_async_copy(source.at[:, :, aligned(at, rows)], turn_buf, io_sems.at[4])
        load.start()
        load.wait()
        for chunk in range(cols):
            into[:, chunk * rows : (chunk + 1) * rows] = turn_buf[chunk].T

    def one_block(at, unused):
        turned(b_all, b_buf, at)
        turned(grad_ref, g_buf, at)

        @pl.when(at > 0)
        def _():
            for copy in results(at - 1):
                copy.wait()

        @pl.loop(0, units // tile)
        def _(step):
            lanes = aligned(step, tile)
            dg_buf[:, lanes] = dot_nn(b_buf[...], wg[:, lanes]).astype(jnp.bfloat16)
            du_buf[:, lanes] = dot_nn(b_buf[...], wu[:, lanes]).astype(jnp.bfloat16)
            u_buf[:, lanes] = dot_nn(g_buf[...], wd[:, lanes]).astype(jnp.bfloat16)

        for copy in results(at):
            copy.start()
        return unused

    lax.fori_loop(0, cols, one_block, 0)
    for copy in results(last):
        copy.wait()
    for at in range(1, cols):
        back_out(at, order(at)).wait_send()
        source = lax.rem(col + at, cols)
        pltpu.make_async_remote_copy(
            src_ref=back_buf.at[slot_of(at)],
            dst_ref=back_all.at[source],
            send_sem=back_send.at[at],
            recv_sem=back_recv.at[source],
            device_id=(group, row, source),
            device_id_type=MESH_IDS,
        ).wait_recv()
    for chunk in range(cols):

        @pl.when((col >= chunk) & (col < last))
        def _():
            pass_on(own_ref, chunk, col + 1, 0).wait_send()

        @pl.when((col <= chunk) & (col > 0))
        def _():
            pass_on(own_ref, chunk, col - 1, 1).wait_send()


def feed_forward(own_input, resid, grad_rows, weights, cols):
    rows, width = own_input.shape
    units = weights[0].shape[1]
    anywhere = pl.BlockSpec(memory_space=pl.ANY)
    bf16 = jnp.bfloat16
    return pl.pallas_call(
        functools.partial(ffn_kernel, cols),
        out_shape=(
            jax.ShapeDtypeStruct((cols, rows, width), bf16),
            jax.ShapeDtypeStruct((cols, rows, units), bf16),
            jax.ShapeDtypeStruct((cols, rows, 2 * units), bf16),
            jax.ShapeDtypeStruct((cols, rows, width), bf16),
            jax.ShapeDtypeStruct((cols, rows, width), bf16),
            jax.ShapeDtypeStruct((width, 2 * units), bf16),
            jax.ShapeDtypeStruct((width, units), bf16),
        ),
        in_specs=[anywhere] * 12,
        out_specs=(anywhere,) * 7,
        scratch_shapes=[
            pltpu.VMEM((width, units), bf16),
            pltpu.VMEM((width, units), bf16),
            pltpu.VMEM((width, units), bf16),
            pltpu.VMEM((rows, width), bf16),
            pltpu.VMEM((rows, width), bf16),
            pltpu.VMEM((rows, units), bf16),
            pltpu.VMEM((rows, units), bf16),
            pltpu.VMEM((rows, units), bf16),
            pltpu.VMEM((rows, width), bf16),
            pltpu.VMEM((cols - 1, rows, width), bf16),
            pltpu.VMEM((cols, rows, rows), bf16),
            pltpu.SemaphoreType.DMA((12,)),
            pltpu.SemaphoreType.DMA((2, cols)),
            pltpu.SemaphoreType.DMA((cols,)),
            pltpu.SemaphoreType.DMA((cols,)),
            pltpu.SemaphoreType.DMA((cols,)),
            pltpu.SemaphoreType.DMA((9,)),
        ],
        compiler_params=pltpu.CompilerParams(
            collective_id=2, has_side_effects=True, vmem_limit_bytes=60 << 20
        ),
        cost_estimate=pl.CostEstimate(
            flops=18 * cols * rows * width * units,
            bytes_accessed=800 << 20,
            transcendentals=cols * rows * units,
        ),
        name="feed_forward",
    )(own_input, resid, grad_rows, *weights)


def finish_kernel(
    cols,
    ig_ref,
    gq_ref,
    go_ref,
    gain_ref,
    gin_ref,
    sq_ref,
    so_ref,
    gsum_ref,
    q_keep,
    q_sib,
    q_a1,
    q_a2,
    q_b1,
    q_b2,
    q_z,
    o_keep,
    o_sib,
    o_a1,
    o_a2,
    o_b1,
    o_b2,
    o_z,
    gain_now,
    gain_in,
    ig_sems,
    gain_sems,
    q_sems,
    o_sems,
    qz_sems,
    oz_sems,
    local_sems,
):
    group, core, mate, row, col = place()
    pair = group - core
    high = pair // 2
    sibling = (pair + 1 - core, row, col)
    over_x = (group, 1 - row, col)
    over_y = (2 * (1 - high) + core, row, col)
    width = gin_ref.shape[2]

    def line(step):
        return lax.rem(col + step + cols, cols)

    barrier = pltpu.get_barrier_semaphore()

    def greet(device):
        pl.semaphore_signal(barrier, inc=1, device_id=device, device_id_type=MESH_IDS)

    greet(sibling)
    greet(over_x)
    greet(over_y)
    for step in range(1, cols):
        greet((mate, core, line(step)))
        greet((group, row, line(step)))

    @pl.when(core != row)
    def _():
        greet((mate, core, col))

    pl.semaphore_wait(barrier, 2 * cols + 1 + (core - row) * (core - row))

    def remote(src, dst, sems, at, device):
        return pltpu.make_async_remote_copy(
            src_ref=src,
            dst_ref=dst,
            send_sem=sems.at[0, at],
            recv_sem=sems.at[1, at],
            device_id=device,
            device_id_type=MESH_IDS,
        )

    def lanes(block, size):
        return pl.ds(pl.multiple_of(block * size, size), size)

    matrices = (
        (gq_ref, sq_ref, q_keep, q_sib, q_a1, q_a2, q_b1, q_b2, q_z, q_sems, qz_sems),
        (go_ref, so_ref, o_keep, o_sib, o_a1, o_a2, o_b1, o_b2, o_z, o_sems, oz_sems),
    )

    def moves(m):
        grads, out, keep, sib, a1, a2, b1, b2, zb, sems, z_sems = matrices[m]
        return dict(
            s0=remote(grads.at[:, 1 - core], sib, sems, 0, sibling),
            a1=remote(grads.at[:, core, 1 - row], a1, sems, 1, over_x),
            a2=remote(keep.at[1 - high, row], a2, sems, 2, over_y),
            b1=remote(sib.at[1 - high], b1, sems, 3, over_y),
            b2=remote(sib.at[high, 1 - row], b2, sems, 4, over_x),
            own=pltpu.make_async_copy(grads.at[:, core], keep, local_sems.at[m]),
        )

    copies = (moves(0), moves(1))

    def rows_plus(into, more):
        rows = into.shape[0]
        step = min(32, rows)

        @pl.loop(0, rows // step)
        def _(at):
            here = pl.ds(pl.multiple_of(at * step, step), step)
            into[here, :] = (
                into[here, :].astype(jnp.float32) + more[here, :].astype(jnp.float32)
            ).astype(into.dtype)

    def token_copy(step, at):
        return remote(
            ig_ref.at[:, lanes(line(step), width)],
            gin_ref.at[at],
            ig_sems,
            step,
            (mate, core, line(step)),
        )

    own_tokens = pltpu.make_async_copy(
        ig_ref.at[:, lanes(col, width)], gin_ref.at[col], local_sems.at[2]
    )

    for m in range(2):
        copies[m]["s0"].start()
        copies[m]["a1"].start()
        copies[m]["own"].start()
    for step in range(1, cols):
        token_copy(step, col).start()

    @pl.when(core != row)
    def _():
        token_copy(0, col).start()

    @pl.when(core == row)
    def _():
        own_tokens.start()

    gain_load = pltpu.make_async_copy(gain_ref, gain_now.at[0], local_sems.at[3])
    gain_load.start()
    gain_load.wait()
    near = (
        sibling,
        over_x,
        over_y,
        (group, row, col + 1 - 2 * lax.rem(col, 2)),
        (group, row, lax.rem(col + cols // 2, cols)),
    )

    def gain_round(at):
        exchange = remote(gain_now.at[at], gain_in.at[at], gain_sems, at, near[at])
        exchange.start()
        exchange.wait()
        gain_now[at + 1] = gain_now[at] + gain_in[at]

    gain_round(0)
    for m in range(2):
        copies[m]["s0"].wait()
        copies[m]["b1"].start()
    gain_round(1)
    for m in range(2):
        grads, out, keep, sib, a1, a2, b1, b2, zb, sems, z_sems = matrices[m]
        copies[m]["own"].wait()
        copies[m]["a1"].wait()
        rows_plus(keep.at[1 - high, row], a1.at[1 - high])
        copies[m]["a2"].start()
    for m in range(2):
        grads, out, keep, sib, a1, a2, b1, b2, zb, sems, z_sems = matrices[m]
        copies[m]["b1"].wait()
        rows_plus(sib.at[high, 1 - row], b1.at[1 - row])
        copies[m]["b2"].start()
    gain_round(2)
    for m in range(2):
        grads, out, keep, sib, a1, a2, b1, b2, zb, sems, z_sems = matrices[m]
        rows_plus(keep.at[high, row], a1.at[high])
        rows_plus(sib.at[high, row], b1.at[row])

    def z_moves(m, side, source):
        grads, out, keep, sib, a1, a2, b1, b2, zb, sems, z_sems = matrices[m]
        held = (keep, sib)[side]
        wide = zb.shape[3]
        return [
            pltpu.make_async_remote_copy(
                src_ref=held.at[high, row, :, lanes(line(step), wide)],
                dst_ref=zb.at[side, line(source(step))],
                send_sem=z_sems.at[0, side, step],
                recv_sem=z_sems.at[1, side, step],
                device_id=(group, row, line(step)),
                device_id_type=MESH_IDS,
            )
            for step in range(1, cols)
        ]

    for side, last_copy in ((0, "a2"), (1, "b2")):
        for m in range(2):
            grads, out, keep, sib, a1, a2, b1, b2, zb, sems, z_sems = matrices[m]
            copies[m][last_copy].wait()
            rows_plus((keep, sib)[side].at[high, row], (a2, b2)[side])
            for copy in z_moves(m, side, lambda step: 0):
                copy.start()
    gain_round(3)
    gain_round(4)
    gsum_ref[...] = gain_now[5]
    for side in range(2):
        for m in range(2):
            grads, out, keep, sib, a1, a2, b1, b2, zb, sems, z_sems = matrices[m]
            for copy in z_moves(m, side, lambda step: 0):
                copy.wait_send()
            for copy in z_moves(m, side, lambda step: -step):
                copy.wait_recv()
            held = (keep, sib)[side]
            wide = zb.shape[3]
            at_core = core if side == 0 else 1 - core
            rows = zb.shape[2]
            tall = min(32, rows)

            @pl.loop(0, rows // tall)
            def _(at):
                here = pl.ds(pl.multiple_of(at * tall, tall), tall)
                total = held[high, row, here, lanes(col, wide)].astype(jnp.float32)
                for step in range(1, cols):
                    total = total + zb[side, line(-step), here, :].astype(jnp.float32)
                out[at_core, here, :] = total

    for step in range(1, cols):
        token_copy(step, line(-step)).wait_recv()
        token_copy(step, col).wait_send()

    @pl.when(core != row)
    def _():
        token_copy(0, col).wait_recv()
        token_copy(0, col).wait_send()

    @pl.when(core == row)
    def _():
        own_tokens.wait()


def finish(input_grad, grad_q, grad_o, gains, cols):
    anywhere = pl.BlockSpec(memory_space=pl.ANY)
    in_vmem = pl.BlockSpec(memory_space=pltpu.VMEM)
    bf16, f32 = jnp.bfloat16, jnp.float32
    length, full = input_grad.shape
    rows = grad_q.shape[0] // 8

    def buffers(wide):
        return [
            pltpu.VMEM((2, 2, rows, wide), bf16),
            pltpu.VMEM((2, 2, rows, wide), bf16),
            pltpu.VMEM((2, rows, wide), bf16),
            pltpu.VMEM((rows, wide), bf16),
            pltpu.VMEM((2, rows, wide), bf16),
            pltpu.VMEM((rows, wide), bf16),
            pltpu.VMEM((2, cols, rows, wide // cols), bf16),
        ]

    wide_q, wide_o = grad_q.shape[1], grad_o.shape[1]
    return pl.pallas_call(
        functools.partial(finish_kernel, cols),
        out_shape=(
            jax.ShapeDtypeStruct((cols, length, full // cols), bf16),
            jax.ShapeDtypeStruct((2, rows, wide_q // cols), f32),
            jax.ShapeDtypeStruct((2, rows, wide_o // cols), f32),
            jax.ShapeDtypeStruct(gains.shape, f32),
        ),
        in_specs=[anywhere] * 4,
        out_specs=(anywhere, in_vmem, in_vmem, in_vmem),
        scratch_shapes=buffers(wide_q)
        + buffers(wide_o)
        + [
            pltpu.VMEM((6,) + gains.shape, f32),
            pltpu.VMEM((5,) + gains.shape, f32),
            pltpu.SemaphoreType.DMA((2, cols)),
            pltpu.SemaphoreType.DMA((2, 5)),
            pltpu.SemaphoreType.DMA((2, 5)),
            pltpu.SemaphoreType.DMA((2, 5)),
            pltpu.SemaphoreType.DMA((2, 2, cols)),
            pltpu.SemaphoreType.DMA((2, 2, cols)),
            pltpu.SemaphoreType.DMA((4,)),
        ],
        compiler_params=pltpu.CompilerParams(
            collective_id=3, has_side_effects=True, vmem_limit_bytes=40 << 20
        ),
        cost_estimate=pl.CostEstimate(flops=0, bytes_accessed=300 << 20, transcendentals=0),
        name="finish",
    )(
        input_grad,
        grad_q.reshape(2, 2, 2, rows, wide_q),
        grad_o.reshape(2, 2, 2, rows, wide_o),
        gains,
    )


def one_sequence_body(
    tokens,
    cotangent,
    lengths,
    deal_order,
    gain_attn,
    gain_ffn,
    w_query,
    key_value_weight,
    w_out,
    w_gate_up,
    w_down,
):
    seq_group, rows_local, width_local = tokens.shape
    row_count = lax.axis_size("row")
    col_count = lax.axis_size("col")
    full_width = width_local * col_count
    slot_len = rows_local * row_count
    group, core, mate, row, col = place()
    query_half = w_query.shape[1] // 2
    kv_half = key_value_weight.shape[2] // 2
    hidden = w_down.shape[1]

    def core_half(matrix, axis):
        width = matrix.shape[axis] // 2
        return lax.dynamic_slice_in_dim(matrix, core * width, width, axis)

    def joined(mine, other, at):
        return jnp.where(
            at == 0, jnp.concatenate([mine, other]), jnp.concatenate([other, mine])
        )

    def from_sibling(value):
        return lax.ppermute(value, "dp", SIBLINGS)

    def half_rows(matrix):
        return core_half(matrix, 0)

    pack_q = jnp.concatenate(
        [
            core_half(w_query, 1),
            core_half(key_value_weight[:, 0], 1),
            core_half(key_value_weight[:, 1], 1),
        ],
        axis=1,
    )
    pack_o = core_half(w_out, 1)
    gain_one = gain_attn.astype(jnp.float32)
    gain_two = gain_ffn.astype(jnp.float32)
    own_tokens, attn_input, weights_qkv = start_exchange(
        tokens, pack_q, gain_one, row_count, col_count
    )

    length = lax.dynamic_slice_in_dim(lengths, mate * seq_group + col, 1)
    line_lengths = lax.dynamic_slice_in_dim(lengths, mate * seq_group, seq_group)
    own_pos = core * rows_local + jnp.arange(rows_local, dtype=jnp.int32)
    line_live = (own_pos[None, :] < line_lengths[:, None]).astype(jnp.float32)
    own_live = (own_pos < length).astype(jnp.float32)[:, None]

    w_gate_up, attn_input = lax.optimization_barrier((w_gate_up, attn_input))
    own_mats = (w_gate_up[:, 0], w_gate_up[:, 1], w_down)
    halves = tuple(half_rows(matrix) for matrix in own_mats)
    halves, attn_input = lax.optimization_barrier((halves, attn_input))
    far_mats = tuple(lax.ppermute(matrix, "row", OVER_X) for matrix in halves)
    sibling_mats = tuple(from_sibling(matrix) for matrix in far_mats)

    everyone = lax.all_gather(cotangent, "dp", axis=0, tiled=True)
    everyone, attn_input = lax.optimization_barrier((everyone, attn_input))
    given = lax.ppermute(
        pick_sequences(everyone, deal_order, group * seq_group, seq_group), ("dp", "row"), CROSSED
    )
    line_cot = lax.all_gather(given, "col", axis=2, tiled=True)
    line_grad = line_live[:, :, None] * line_cot.astype(jnp.float32)
    grad_ffn = (RES_MULT * line_grad).astype(jnp.bfloat16).reshape(-1, full_width)
    own_grad = own_live * lax.dynamic_index_in_dim(line_cot, col, keepdims=False).astype(
        jnp.float32
    )

    cosine_table, sine_table = rope_tables(jnp.arange(slot_len, dtype=jnp.int32), HEAD_SIZE)
    cosine_table, sine_table = lax.optimization_barrier((cosine_table, sine_table))
    cosines = jnp.concatenate(
        [jnp.tile(cosine_table, (1, 6)), jnp.ones((slot_len, HEAD_SIZE), jnp.float32)], axis=1
    )
    turning = jnp.concatenate([-sine_table, sine_table], axis=1)
    sines = jnp.concatenate(
        [jnp.tile(turning, (1, 3)), jnp.zeros((slot_len, HEAD_SIZE), jnp.float32)], axis=1
    )
    own_float = own_tokens.astype(jnp.float32)
    scale_one = lax.rsqrt(jnp.mean(own_float * own_float, axis=1, keepdims=True) + EPSILON)
    projected, heads_out = attend_fast(
        length, attn_input, weights_qkv, cosines, sines, col_count
    )

    def summed_rows(partial):
        count = partial.shape[0] // 2
        mine = lax.dynamic_slice_in_dim(partial, core * count, count)
        other = lax.dynamic_slice_in_dim(partial, (1 - core) * count, count)
        return mine.astype(jnp.float32) + from_sibling(other).astype(jnp.float32)

    weights_out = gather_weights(pack_o, heads_out, row_count, col_count)
    attn_rows = summed_rows(expand_local(heads_out, weights_out).astype(jnp.bfloat16))
    resid = own_float + RES_MULT * attn_rows
    scale_two = lax.rsqrt(jnp.mean(resid * resid, axis=1, keepdims=True) + EPSILON)
    own_ffn = (resid * scale_two * gain_two).astype(jnp.bfloat16)

    unused_b, unused_u, unused_gu, mlp_part, back_part, grad_gu, grad_dn = feed_forward(
        own_ffn,
        resid.astype(jnp.bfloat16),
        grad_ffn.reshape(col_count, rows_local, full_width),
        own_mats + far_mats + sibling_mats,
        col_count,
    )
    grad_normed_two = jnp.sum(back_part.astype(jnp.float32), axis=0)

    out_cols = lax.psum_scatter(mlp_part, "col", scatter_dimension=2, tiled=True)
    given_pos = row * rows_local + jnp.arange(rows_local, dtype=jnp.int32)
    given_lengths = lax.dynamic_slice_in_dim(lengths, group * seq_group, seq_group)
    given_live = (given_pos[None, :] < given_lengths[:, None]).astype(jnp.float32)
    layer_out = given_live[:, :, None] * lax.ppermute(
        out_cols, ("dp", "row"), CROSSED
    ).astype(jnp.float32)

    def scatter_rows(matrix):
        return lax.psum_scatter(
            matrix, ("dp", "row"), scatter_dimension=0, tiled=True
        ).astype(jnp.float32)

    sums_down = scatter_rows(grad_dn)
    sums_gate_up = scatter_rows(grad_gu)
    sums_gate_up = sums_gate_up.reshape(-1, 2, hidden)

    weighted_two = grad_normed_two * gain_two
    inner_two = jnp.sum(weighted_two * resid, axis=1, keepdims=True)
    grad_resid = (
        own_grad + scale_two * weighted_two - resid * scale_two**3 * inner_two / full_width
    )
    gain_two_part = jnp.sum(grad_normed_two * resid * scale_two, axis=0)
    own_attn_grad = (RES_MULT * grad_resid).astype(jnp.bfloat16)
    grad_attn = joined(own_attn_grad, from_sibling(own_attn_grad), core)
    grad_heads = contract_local(grad_attn, weights_out).astype(jnp.bfloat16)
    grad_out = token_outer(grad_attn, heads_out).astype(jnp.bfloat16)
    grad_projected = attend_back_fast(
        length, projected, grad_heads, cosines, sines, col_count
    )
    grad_normed_one = summed_rows(expand_local(grad_projected, weights_qkv).astype(jnp.bfloat16))
    grad_qkv = token_outer(attn_input, grad_projected).astype(jnp.bfloat16)
    weighted_one = grad_normed_one * gain_one
    inner_one = jnp.sum(weighted_one * own_float, axis=1, keepdims=True)
    own_input_grad = (
        grad_resid
        + scale_one * weighted_one
        - own_float * scale_one**3 * inner_one / full_width
    ).astype(jnp.bfloat16)
    gain_one_part = jnp.sum(grad_normed_one * own_float * scale_one, axis=0)
    gains = jnp.stack([gain_one_part, gain_two_part]).reshape(8, -1)
    given_grad, sums_q, sums_o, gain_sums = finish(
        own_input_grad, grad_qkv, grad_out, gains, col_count
    )
    input_grad = given_grad.astype(jnp.float32)
    grad_gain_attn, grad_gain_ffn = gain_sums.reshape(2, full_width)

    def both_cores(sums):
        return jnp.concatenate([sums[0], sums[1]], axis=1)

    qk = query_half + kv_half
    out_query = both_cores(sums_q[:, :, :query_half])
    out_kv = jnp.stack(
        [
            both_cores(sums_q[:, :, query_half:qk]),
            both_cores(sums_q[:, :, qk:]),
        ],
        axis=1,
    )
    out_out = both_cores(sums_o)
    return (
        layer_out,
        input_grad,
        out_query,
        out_kv,
        out_out,
        sums_gate_up,
        sums_down,
        grad_gain_attn,
        grad_gain_ffn,
    )


def general_body(
    tokens,
    cotangent,
    lengths,
    deal_order,
    gain_attn,
    gain_ffn,
    w_query,
    key_value_weight,
    w_out,
    w_gate_up,
    w_down,
):
    seq_group, rows_local, width_local = tokens.shape
    row_count = lax.axis_size("row")
    col_count = lax.axis_size("col")
    full_width = width_local * col_count
    slot_len = rows_local * row_count
    total_rows = seq_group * rows_local
    head_size = HEAD_SIZE
    query_width = w_query.shape[1]
    kv_width = key_value_weight.shape[2]
    kv_heads = kv_width // head_size
    group_size = query_width // kv_width
    group_index = lax.axis_index("dp")
    row_index = lax.axis_index("row")
    col_index = lax.axis_index("col")
    matrices = {
        "qkv": jnp.concatenate(
            [w_query, key_value_weight.reshape(key_value_weight.shape[0], 2 * kv_width)], axis=1
        ),
        "out": w_out,
        "gate_up": w_gate_up,
        "down": w_down,
    }

    def contract_with(operand, which_one):
        return contract_rows(operand, matrices[which_one])

    def expand_with(operand, which_one):
        return expand_rows(operand, matrices[which_one])

    own_cotangent = bring_cotangent(cotangent, deal_order, group_index * seq_group)
    own_rows = tokens
    seq_lens = lax.dynamic_slice_in_dim(lengths, group_index * seq_group, seq_group)
    local_pos = row_index * rows_local + jnp.arange(rows_local, dtype=jnp.int32)
    key_pos = jnp.arange(slot_len, dtype=jnp.int32)
    live_rows = (local_pos[None, :] < seq_lens[:, None]).astype(jnp.float32).reshape(total_rows, 1)
    cosine_table, sine_table = rope_tables(jnp.tile(local_pos, seq_group), head_size)
    own_tokens = own_rows.reshape(total_rows, width_local)
    wide_float = widen_cols(own_tokens).astype(jnp.float32)
    scale_one = lax.rsqrt(jnp.mean(wide_float * wide_float, axis=1, keepdims=True) + EPSILON)
    gain_one = gain_attn.astype(jnp.float32)
    first_normed = wide_float * scale_one
    attn_input = (first_normed * gain_one).astype(jnp.bfloat16)
    projected = contract_with(attn_input, "qkv")
    query_lin = projected[:, :query_width].reshape(total_rows, query_width // head_size, head_size)
    key_lin = projected[:, query_width : query_width + kv_width].reshape(
        total_rows, kv_heads, head_size
    )
    value_lin = projected[:, query_width + kv_width :]
    query_rows = rotary_embed(query_lin, cosine_table, sine_table).astype(jnp.bfloat16)
    keys_own = (
        rotary_embed(key_lin, cosine_table, sine_table)
        .astype(jnp.bfloat16)
        .reshape(seq_group, rows_local, kv_width)
    )
    values_own = value_lin.astype(jnp.bfloat16).reshape(seq_group, rows_local, kv_width)
    all_keys, all_values = (
        lax.all_gather(keys_own, "row", axis=1, tiled=True),
        lax.all_gather(values_own, "row", axis=1, tiled=True),
    )
    query_split = query_rows.reshape(seq_group, rows_local, kv_heads, group_size, head_size)
    key_split = all_keys.reshape(seq_group, slot_len, kv_heads, head_size)
    value_split = all_values.reshape(seq_group, slot_len, kv_heads, head_size)

    def forward_seq(inputs):
        return attend(inputs, key_pos, local_pos)

    mixed_heads, row_max, row_sums = lax.map(
        forward_seq, (query_split, key_split, value_split, seq_lens)
    )
    heads_out = mixed_heads.reshape(total_rows, query_width).astype(jnp.bfloat16)
    attn_local = narrow_cols(expand_with(heads_out, "out"))
    resid = own_tokens.astype(jnp.float32) + RES_MULT * attn_local
    gain_two = lax.dynamic_slice_in_dim(
        gain_ffn.astype(jnp.float32), col_index * width_local, width_local
    )
    scale_two = lax.rsqrt(sum_over_cols(jnp.sum(resid * resid, axis=1)) / full_width + EPSILON)[
        :, None
    ]
    normed_two = resid * scale_two
    ffn_input = widen_cols((normed_two * gain_two).astype(jnp.bfloat16))
    gate_up = contract_with(ffn_input, "gate_up")
    gate = gate_up[:, 0]
    upward = gate_up[:, 1]
    sigmoid_gate = jax.nn.sigmoid(gate)
    silu_gate = gate * sigmoid_gate
    hidden = (silu_gate * upward).astype(jnp.bfloat16)
    ffn_local = narrow_cols(expand_with(hidden, "down"))
    layer_out = live_rows * (resid + RES_MULT * ffn_local)
    grad_rows = live_rows * own_cotangent.reshape(total_rows, width_local).astype(jnp.float32)
    grad_ffn = widen_cols((RES_MULT * grad_rows).astype(jnp.bfloat16))
    grad_hidden = contract_with(grad_ffn, "down")
    grad_down = token_outer(grad_ffn, hidden)
    slope = sigmoid_gate * (1.0 + gate * (1.0 - sigmoid_gate))
    grad_gate_rows = jnp.stack(
        [grad_hidden * upward * slope, grad_hidden * silu_gate], axis=1
    ).astype(jnp.bfloat16)
    grad_gate_up = token_outer(ffn_input, grad_gate_rows)
    grad_normed_two = narrow_cols(expand_with(grad_gate_rows, "gate_up"))
    weighted_two = grad_normed_two * gain_two
    inner_two = sum_over_cols(jnp.sum(weighted_two * resid, axis=1))[:, None]
    grad_resid = (
        grad_rows + scale_two * weighted_two - resid * scale_two**3 * inner_two / full_width
    )
    gain_two_part = jnp.sum(grad_normed_two * normed_two, axis=0)
    grad_attn = widen_cols((RES_MULT * grad_resid).astype(jnp.bfloat16))
    grad_heads = contract_with(grad_attn, "out").astype(jnp.bfloat16)
    grad_out = token_outer(grad_attn, heads_out)
    grad_split = grad_heads.reshape(seq_group, rows_local, kv_heads, group_size, head_size)

    def backward_seq(inputs):
        return attend_back(inputs, key_pos, local_pos)

    grad_query, grad_key, grad_value = lax.map(
        backward_seq, (query_split, key_split, value_split, grad_split, row_max, row_sums, seq_lens)
    )
    key_part, value_part = (
        lax.psum_scatter(
            grad_key.reshape(seq_group, slot_len, kv_width).astype(jnp.bfloat16),
            "row",
            scatter_dimension=1,
            tiled=True,
        ).astype(jnp.float32),
        lax.psum_scatter(
            grad_value.reshape(seq_group, slot_len, kv_width).astype(jnp.bfloat16),
            "row",
            scatter_dimension=1,
            tiled=True,
        ).astype(jnp.float32),
    )
    query_back = rotary_embed(
        grad_query.reshape(total_rows, query_width // head_size, head_size),
        cosine_table,
        -sine_table,
    ).reshape(total_rows, query_width)
    key_back = rotary_embed(
        key_part.reshape(total_rows, kv_heads, head_size), cosine_table, -sine_table
    ).reshape(total_rows, kv_width)
    grad_projected = jnp.concatenate(
        [query_back, key_back, value_part.reshape(total_rows, kv_width)], axis=1
    ).astype(jnp.bfloat16)
    grad_qkv = token_outer(attn_input, grad_projected)
    grad_normed_one = expand_with(grad_projected, "qkv")
    weighted_one = grad_normed_one * gain_one
    inner_one = jnp.sum(weighted_one * wide_float, axis=1, keepdims=True)
    input_part = scale_one * weighted_one - wide_float * scale_one**3 * inner_one / full_width
    input_grad = grad_resid + narrow_cols(input_part)
    gain_one_part = jnp.sum(grad_normed_one * first_normed, axis=0)
    gain_two_full = lax.dynamic_update_slice_in_dim(
        jnp.zeros((full_width,), jnp.float32), gain_two_part, col_index * width_local, 0
    )
    grad_gain_attn, grad_gain_ffn = lax.psum((gain_one_part, gain_two_full), ("dp", "row", "col"))
    sums_qkv, sums_out, sums_gate_up, sums_down = (
        lax.psum_scatter(
            grad_qkv.astype(jnp.bfloat16), ("dp", "row"), scatter_dimension=0, tiled=True
        ).astype(jnp.float32),
        lax.psum_scatter(
            grad_out.astype(jnp.bfloat16), ("dp", "row"), scatter_dimension=0, tiled=True
        ).astype(jnp.float32),
        lax.psum_scatter(
            grad_gate_up.astype(jnp.bfloat16), ("dp", "row"), scatter_dimension=0, tiled=True
        ).astype(jnp.float32),
        lax.psum_scatter(
            grad_down.astype(jnp.bfloat16), ("dp", "row"), scatter_dimension=0, tiled=True
        ).astype(jnp.float32),
    )
    out_query = sums_qkv[:, :query_width]
    out_kv = sums_qkv[:, query_width:].reshape(sums_qkv.shape[0], 2, kv_width)
    return (
        layer_out.reshape(seq_group, rows_local, width_local),
        input_grad.reshape(seq_group, rows_local, width_local),
        out_query,
        out_kv,
        sums_out,
        sums_gate_up,
        sums_down,
        grad_gain_attn,
        grad_gain_ffn,
    )


def body(tokens, cotangent, lengths, deal_order, gain_attn, gain_ffn, w_query, key_value_weight, *rest):
    sizes = (lax.axis_size("dp"), lax.axis_size("row"), lax.axis_size("col"))
    one_each = sizes == (4, 2, 4) and tokens.shape[0] == sizes[2]
    pairs = w_query.shape[1] == 8 * HEAD_SIZE and key_value_weight.shape[2] == 2 * HEAD_SIZE
    chosen = one_sequence_body if one_each and pairs else general_body
    return chosen(
        tokens, cotangent, lengths, deal_order, gain_attn, gain_ffn, w_query, key_value_weight, *rest
    )


def solution(mesh):
    placed = (
        P("dp", "row", "col"),
        P("dp", "row", "col"),
        P(),
        P(),
        P(),
        P(),
        P("row", "col"),
        P("row", None, "col"),
        P("row", "col"),
        P("row", None, "col"),
        P("row", "col"),
    )
    return jax.shard_map(
        body,
        mesh=mesh,
        in_specs=placed,
        out_specs=(
            P("dp", "row", "col"),
            P("dp", "row", "col"),
            P(("dp", "row"), "col"),
            P(("dp", "row"), None, "col"),
            P(("dp", "row"), "col"),
            P(("dp", "row"), None, "col"),
            P(("dp", "row"), "col"),
            P(),
            P(),
        ),
        check_vma=False,
    )
```

```python
import functools

import jax
import jax.numpy as jnp
from jax import lax
from jax.experimental import pallas as pl
from jax.experimental.pallas import tpu as pltpu
from jax.sharding import PartitionSpec as P

HEAD_SIZE = 64


EPSILON = 1e-05
THETA = 10000000.0
ATTN_MULT = 0.015625
RES_MULT = 0.22
MASKED = -1e30


def rope_tables(positions, head_size):
    halves = jnp.arange(head_size // 2, dtype=jnp.float32)
    inverse_freq = THETA ** (-(halves * 2.0) / head_size)
    angles = positions.astype(jnp.float32)[:, None] * inverse_freq[None, :]
    return (jnp.cos(angles), jnp.sin(angles))


def rotary_embed(value_rows, cosine_table, sine_table):
    middle = value_rows.shape[-1] // 2
    first_half = value_rows[..., :middle]
    second_half = value_rows[..., middle:]
    cos_part = cosine_table[:, None, :]
    sin_part = sine_table[:, None, :]
    return jnp.concatenate(
        [
            first_half * cos_part - second_half * sin_part,
            second_half * cos_part + first_half * sin_part,
        ],
        axis=-1,
    )


def widen_cols(value_rows):
    return lax.all_gather(value_rows, "col", axis=1, tiled=True)


def narrow_cols(value_rows):
    return lax.psum_scatter(value_rows, "col", scatter_dimension=1, tiled=True)


def sum_over_cols(value_rows):
    return lax.psum(value_rows, "col")


def contract_local(operand, matrix):
    return lax.dot_general(
        operand, matrix, (((1,), (0,)), ((), ())), preferred_element_type=jnp.float32
    )


def expand_local(operand, matrix):
    trailing = tuple(range(1, operand.ndim))
    return lax.dot_general(
        operand, matrix, ((trailing, trailing), ((), ())), preferred_element_type=jnp.float32
    )


def token_outer(features, grads):
    return lax.dot_general(
        features, grads, (((0,), (0,)), ((), ())), preferred_element_type=jnp.float32
    )


def contract_rows(operand, matrix):
    return contract_local(operand, lax.all_gather(matrix, "row", axis=0, tiled=True))


def expand_rows(operand, matrix):
    return expand_local(operand, lax.all_gather(matrix, "row", axis=0, tiled=True))


def split_keys(key_seq, value_seq, key_pos):
    slot_len = key_seq.shape[0]
    width = min(512, slot_len)
    count = slot_len // width
    return (
        key_seq.reshape(count, width, key_seq.shape[1], key_seq.shape[2]),
        value_seq.reshape(count, width, value_seq.shape[1], value_seq.shape[2]),
        key_pos.reshape(count, width),
    )


def block_scores(query_seq, key_block, pos_block, query_pos, length):
    scores = (
        jnp.einsum("qkgd,tkd->kgqt", query_seq, key_block, preferred_element_type=jnp.float32)
        * ATTN_MULT
    )
    allowed = (pos_block[None, :] <= query_pos[:, None]) & (pos_block[None, :] < length)
    return jnp.where(allowed, scores, MASKED)


def attend(inputs, key_pos, query_pos):
    query_seq, key_seq, value_seq, length = inputs
    key_blocks, value_blocks, pos_blocks = split_keys(key_seq, value_seq, key_pos)
    stat_shape = (query_seq.shape[1], query_seq.shape[2], query_seq.shape[0], 1)

    def gather_stats(carry, entry):
        running_max, running_sum = carry
        key_block, pos_block = entry
        scores = block_scores(query_seq, key_block, pos_block, query_pos, length)
        new_max = jnp.maximum(running_max, jnp.max(scores, axis=-1, keepdims=True))
        new_sum = running_sum * jnp.exp(running_max - new_max) + jnp.sum(
            jnp.exp(scores - new_max), axis=-1, keepdims=True
        )
        return ((new_max, new_sum), None)

    start_stats = (jnp.full(stat_shape, MASKED, jnp.float32), jnp.zeros(stat_shape, jnp.float32))
    (row_max, row_sums), unused = lax.scan(gather_stats, start_stats, (key_blocks, pos_blocks))

    def mix_values(running, entry):
        key_block, value_block, pos_block = entry
        scores = block_scores(query_seq, key_block, pos_block, query_pos, length)
        weights = jnp.exp(scores - row_max) / row_sums
        return (
            running
            + jnp.einsum(
                "kgqt,tkd->qkgd",
                weights.astype(jnp.bfloat16),
                value_block,
                preferred_element_type=jnp.float32,
            ),
            None,
        )

    start_mix = jnp.zeros(query_seq.shape, jnp.float32)
    mixed_heads, unused = lax.scan(mix_values, start_mix, (key_blocks, value_blocks, pos_blocks))
    return (mixed_heads, row_max, row_sums)


def attend_back(inputs, key_pos, query_pos):
    query_seq, key_seq, value_seq, grad_mixed, row_max, row_sums, length = inputs
    key_blocks, value_blocks, pos_blocks = split_keys(key_seq, value_seq, key_pos)

    def block_weights(key_block, value_block, pos_block):
        scores = block_scores(query_seq, key_block, pos_block, query_pos, length)
        weights = jnp.exp(scores - row_max) / row_sums
        grad_weights = jnp.einsum(
            "qkgd,tkd->kgqt", grad_mixed, value_block, preferred_element_type=jnp.float32
        )
        return (weights, grad_weights)

    def gather_centre(running, entry):
        weights, grad_weights = block_weights(*entry)
        return (running + jnp.sum(weights * grad_weights, axis=-1, keepdims=True), None)

    start_centre = jnp.zeros(row_max.shape, jnp.float32)
    centre, unused = lax.scan(gather_centre, start_centre, (key_blocks, value_blocks, pos_blocks))

    def grads_block(running, entry):
        key_block = entry[0]
        weights, grad_weights = block_weights(*entry)
        grad_scores = (weights * (grad_weights - centre)).astype(jnp.bfloat16)
        grad_query = (
            running
            + jnp.einsum(
                "kgqt,tkd->qkgd", grad_scores, key_block, preferred_element_type=jnp.float32
            )
            * ATTN_MULT
        )
        grad_key = (
            jnp.einsum("kgqt,qkgd->tkd", grad_scores, query_seq, preferred_element_type=jnp.float32)
            * ATTN_MULT
        )
        grad_value = jnp.einsum(
            "kgqt,qkgd->tkd",
            weights.astype(jnp.bfloat16),
            grad_mixed,
            preferred_element_type=jnp.float32,
        )
        return (grad_query, (grad_key, grad_value))

    start_query = jnp.zeros(query_seq.shape, jnp.float32)
    grad_query, (grad_key, grad_value) = lax.scan(
        grads_block, start_query, (key_blocks, value_blocks, pos_blocks)
    )
    return (grad_query, grad_key.reshape(key_seq.shape), grad_value.reshape(value_seq.shape))


MESH_IDS = pl.DeviceIdType.MESH
CORES = [[(2 * y + c) * 2 + x for y in (0, 1) for x in (0, 1)] for c in (0, 1)]
SIBLINGS = [(0, 1), (1, 0), (2, 3), (3, 2)]
OVER_X = [(0, 1), (1, 0)]
CROSSED = [((2 * y + c) * 2 + x, (2 * y + x) * 2 + c) for y in (0, 1) for c in (0, 1) for x in (0, 1)]


def pick_sequences(everyone, deal_order, first, count):
    slots = jnp.arange(deal_order.shape[0], dtype=jnp.int32)
    inverse = jnp.sum(jnp.where(deal_order[None, :] == slots[:, None], slots[None, :], 0), axis=1)
    return jnp.concatenate(
        [
            lax.dynamic_slice_in_dim(
                everyone, lax.dynamic_index_in_dim(inverse, first + at, keepdims=False), 1
            )
            for at in range(count)
        ]
    )


def bring_cotangent(cotangent, deal_order, first):
    everyone = lax.all_gather(cotangent, "dp", axis=0, tiled=True)
    return pick_sequences(everyone, deal_order, first, cotangent.shape[0])


def place():
    group = lax.axis_index("dp")
    core = lax.rem(group, 2)
    row = lax.axis_index("row")
    return group, core, group - core + row, row, lax.axis_index("col")


def lined(index, step, count):
    return lax.rem(index + step + count, count)


def aligned(block, size):
    return pl.ds(pl.multiple_of(block * size, size), size)


def greet(device):
    pl.semaphore_signal(
        pltpu.get_barrier_semaphore(), inc=1, device_id=device, device_id_type=MESH_IDS
    )


def remote(src, dst, sems, at, device):
    return pltpu.make_async_remote_copy(
        src_ref=src,
        dst_ref=dst,
        send_sem=sems.at[0, at],
        recv_sem=sems.at[1, at],
        device_id=device,
        device_id_type=MESH_IDS,
    )


def weight_copies(cols, own, full, sems, x_sems):
    group, core, mate, row, col = place()
    tall, wide = own.shape

    def block(of_row, of_col):
        return full.at[aligned(of_row, tall), aligned(of_col, wide)]

    def line(step):
        return lined(col, step, cols)

    over = (group, 1 - row, col)
    steps = range(1, cols)
    along = [remote(own, block(row, col), sems, k, (group, row, line(k))) for k in steps]
    arrive = [remote(own, block(row, line(-k)), sems, k, (group, row, line(k))) for k in steps]
    across = [remote(own, block(row, col), x_sems, 0, over)] + [
        remote(block(row, line(-k)), block(row, line(-k)), x_sems, k, over) for k in steps
    ]
    landed = [remote(own, block(1 - row, line(-k)), x_sems, k, over) for k in range(cols)]
    return along, arrive, across, landed, block(row, col)


def start_kernel(
    cols,
    tok_ref,
    pq_ref,
    gain_ref,
    x_ref,
    a_ref,
    wq_ref,
    x_buf,
    a_buf,
    tok_sems,
    q_sems,
    qx_sems,
    a_sems,
    local_sems,
):
    group, core, mate, row, col = place()
    width = tok_ref.shape[2]
    length = x_buf.shape[0]
    sibling = (group + 1 - 2 * core, row, col)

    def line(step):
        return lined(col, step, cols)

    for step in range(1, cols):
        greet((mate, core, line(step)))
        greet((group, row, line(step)))
    greet((group, 1 - row, col))
    greet(sibling)

    @pl.when(core != row)
    def _():
        greet((mate, core, col))

    pl.semaphore_wait(
        pltpu.get_barrier_semaphore(), 2 * cols + (core - row) * (core - row)
    )

    along, arrive, across, landed, own_place = weight_copies(cols, pq_ref, wq_ref, q_sems, qx_sems)
    own_q = pltpu.make_async_copy(pq_ref, own_place, local_sems.at[0])

    def token_copy(step, into):
        return remote(
            tok_ref.at[line(step)],
            x_buf.at[:, aligned(into, width)],
            tok_sems,
            step,
            (mate, core, line(step)),
        )

    own_tokens = pltpu.make_async_copy(
        tok_ref.at[col], x_buf.at[:, aligned(col, width)], local_sems.at[1]
    )
    for step in range(1, cols):
        token_copy(step, col).start()

    @pl.when(core != row)
    def _():
        token_copy(0, col).start()

    @pl.when(core == row)
    def _():
        own_tokens.start()

    for copy in along:
        copy.start()
    across[0].start()
    own_q.start()
    for step in range(1, cols):
        token_copy(step, line(-step)).wait_recv()

    @pl.when(core != row)
    def _():
        token_copy(0, col).wait_recv()

    @pl.when(core == row)
    def _():
        own_tokens.wait()

    keep_x = pltpu.make_async_copy(x_buf, x_ref, local_sems.at[2])
    keep_x.start()
    tall = min(64, length)

    @pl.loop(0, length // tall)
    def _(at):
        here = aligned(at, tall)
        now = x_buf[here, :].astype(jnp.float32)
        scale = lax.rsqrt(jnp.mean(now * now, axis=1, keepdims=True) + EPSILON)
        a_buf[here, :] = (now * scale * gain_ref[...]).astype(jnp.bfloat16)

    def a_copy(of_core):
        return remote(a_buf, a_ref.at[aligned(of_core, length)], a_sems, 0, sibling)

    own_a = pltpu.make_async_copy(a_buf, a_ref.at[aligned(core, length)], local_sems.at[3])
    a_copy(core).start()
    own_a.start()
    for step in range(1, cols):
        arrive[step - 1].wait_recv()
        across[step].start()
    for step in range(1, cols):
        token_copy(step, col).wait_send()

    @pl.when(core != row)
    def _():
        token_copy(0, col).wait_send()

    keep_x.wait()
    own_a.wait()
    a_copy(core).wait_send()
    a_copy(1 - core).wait_recv()
    own_q.wait()
    for copy in along + across:
        copy.wait_send()
    for copy in landed:
        copy.wait_recv()


def start_exchange(tokens, pack_q, gain, rows, cols):
    anywhere = pl.BlockSpec(memory_space=pl.ANY)
    seqs, length, width = tokens.shape
    weight_rows = pack_q.shape[0]
    full = width * cols
    return pl.pallas_call(
        functools.partial(start_kernel, cols),
        out_shape=(
            jax.ShapeDtypeStruct((length, full), tokens.dtype),
            jax.ShapeDtypeStruct((2 * length, full), tokens.dtype),
            jax.ShapeDtypeStruct((weight_rows * rows, pack_q.shape[1] * cols), pack_q.dtype),
        ),
        in_specs=[anywhere] * 2 + [pl.BlockSpec(memory_space=pltpu.VMEM)],
        out_specs=(anywhere,) * 3,
        scratch_shapes=[
            pltpu.VMEM((length, full), tokens.dtype),
            pltpu.VMEM((length, full), tokens.dtype),
        ]
        + [pltpu.SemaphoreType.DMA((2, cols))] * 3
        + [pltpu.SemaphoreType.DMA((2, 1)), pltpu.SemaphoreType.DMA((4,))],
        compiler_params=pltpu.CompilerParams(
            collective_id=1, has_side_effects=True, vmem_limit_bytes=16 << 20
        ),
        cost_estimate=pl.CostEstimate(flops=0, bytes_accessed=400 << 20, transcendentals=0),
        name="start_exchange",
    )(tokens, pack_q, gain.reshape(1, full))


def gather_kernel(cols, own_ref, after_ref, full_ref, sems, x_sems, local_sem):
    group, core, mate, row, col = place()
    for step in range(1, cols):
        greet((group, row, lined(col, step, cols)))
    greet((group, 1 - row, col))
    pl.semaphore_wait(pltpu.get_barrier_semaphore(), cols)
    along, arrive, across, landed, own_place = weight_copies(cols, own_ref, full_ref, sems, x_sems)
    own = pltpu.make_async_copy(own_ref, own_place, local_sem)
    for copy in along:
        copy.start()
    across[0].start()
    own.start()
    for step in range(1, cols):
        arrive[step - 1].wait_recv()
        across[step].start()
    own.wait()
    for copy in along + across:
        copy.wait_send()
    for copy in landed:
        copy.wait_recv()


def gather_weights(own, after, rows, cols):
    anywhere = pl.BlockSpec(memory_space=pl.ANY)
    return pl.pallas_call(
        functools.partial(gather_kernel, cols),
        out_shape=jax.ShapeDtypeStruct((own.shape[0] * rows, own.shape[1] * cols), own.dtype),
        in_specs=[anywhere] * 2,
        out_specs=anywhere,
        scratch_shapes=[
            pltpu.SemaphoreType.DMA((2, cols)),
            pltpu.SemaphoreType.DMA((2, cols)),
            pltpu.SemaphoreType.DMA(()),
        ],
        compiler_params=pltpu.CompilerParams(collective_id=4, has_side_effects=True),
        cost_estimate=pl.CostEstimate(flops=0, bytes_accessed=200 << 20, transcendentals=0),
        name="gather_weights",
    )(own, after)


def half_turn(wide):
    lanes = wide.shape[1]
    half = HEAD_SIZE // 2
    lane = lax.broadcasted_iota(jnp.int32, wide.shape, 1)
    return jnp.where(
        lax.rem(lane, HEAD_SIZE) < half,
        pltpu.roll(wide, lanes - half, 1),
        pltpu.roll(wide, half, 1),
    )


def both_heads(pair):
    lane = lax.broadcasted_iota(jnp.int32, pair.shape, 1)
    turned = pltpu.roll(pair, HEAD_SIZE, 1)
    low = lane < HEAD_SIZE
    return jnp.where(low, pair, turned), jnp.where(low, turned, pair)


def keep_head(pair, side):
    lane = lax.broadcasted_iota(jnp.int32, pair.shape, 1)
    mine = lane < HEAD_SIZE if side == 0 else lane >= HEAD_SIZE
    return jnp.where(mine, pair, jnp.zeros_like(pair))


def dot_nn(a, b):
    return lax.dot_general(a, b, (((1,), (0,)), ((), ())), preferred_element_type=jnp.float32)


def dot_nt(a, b):
    return lax.dot_general(a, b, (((1,), (1,)), ((), ())), preferred_element_type=jnp.float32)


def dot_tn(a, b):
    return lax.dot_general(a, b, (((0,), (0,)), ((), ())), preferred_element_type=jnp.float32)


PAIR = 2 * HEAD_SIZE


def attend_kernel(block, len_ref, a_ref, w_ref, cos_ref, sin_ref, qkv_ref, z_ref, q_all, k_two, v_two):
    rows = a_ref.shape[0]
    heads = q_all.shape[0]
    length = len_ref[0]

    @pl.loop(0, rows // block)
    def _(at):
        here = pl.ds(pl.multiple_of(at * block, block), block)
        lin = dot_nn(a_ref[here, :], w_ref[...])
        for part in range(heads // 2 + 1):
            lanes = slice(part * PAIR, (part + 1) * PAIR)
            now = lin[:, lanes]
            table = slice(0, PAIR) if part < heads // 2 else slice(PAIR, 2 * PAIR)
            now = now * cos_ref[here, table] + half_turn(now) * sin_ref[here, table]
            qkv_ref[here, lanes] = now.astype(jnp.bfloat16)
            if part < heads // 2:
                for side in range(2):
                    q_all[2 * part + side, here, :] = keep_head(now * ATTN_MULT, side).astype(
                        jnp.bfloat16
                    )
            else:
                keys, values = both_heads(now)
                k_two[here, :] = keys.astype(jnp.bfloat16)
                v_two[here, :] = values.astype(jnp.bfloat16)

    for at in range(rows // block):
        here = slice(at * block, (at + 1) * block)
        upto = (at + 1) * block
        row = lax.broadcasted_iota(jnp.int32, (block, upto), 0) + at * block
        key = lax.broadcasted_iota(jnp.int32, (block, upto), 1)
        allowed = key < jnp.minimum(row + 1, length)

        def one_head(head):
            scores = dot_nt(q_all[head, here, :], k_two[:upto, :])
            scores = jnp.where(allowed, scores, MASKED)
            top = jnp.max(scores, axis=1, keepdims=True)
            power = jnp.exp(scores - top)
            total = jnp.sum(power, axis=1, keepdims=True)
            return dot_nn(power.astype(jnp.bfloat16), v_two[:upto, :]) / total

        for pair in range(heads // 2):
            low = one_head(2 * pair)
            high = one_head(2 * pair + 1)
            lane = lax.broadcasted_iota(jnp.int32, low.shape, 1)
            z_ref[here, pair * PAIR : (pair + 1) * PAIR] = jnp.where(
                lane < HEAD_SIZE, low, high
            ).astype(jnp.bfloat16)


def attend_fast(length, inputs, weights, cosines, sines, groups):
    rows, depth = inputs.shape
    wide = weights.shape[1] // groups
    heads = (wide - PAIR) // HEAD_SIZE
    block = min(256, rows)
    return pl.pallas_call(
        functools.partial(attend_kernel, block),
        grid=(groups,),
        out_shape=(
            jax.ShapeDtypeStruct((rows, groups * wide), jnp.bfloat16),
            jax.ShapeDtypeStruct((rows, groups * heads * HEAD_SIZE), jnp.bfloat16),
        ),
        in_specs=[
            pl.BlockSpec(memory_space=pltpu.SMEM),
            pl.BlockSpec((rows, depth), lambda g: (0, 0)),
            pl.BlockSpec((depth, wide), lambda g: (0, g)),
            pl.BlockSpec((rows, 2 * PAIR), lambda g: (0, 0)),
            pl.BlockSpec((rows, 2 * PAIR), lambda g: (0, 0)),
        ],
        out_specs=(
            pl.BlockSpec((rows, wide), lambda g: (0, g)),
            pl.BlockSpec((rows, heads * HEAD_SIZE), lambda g: (0, g)),
        ),
        scratch_shapes=[
            pltpu.VMEM((heads, rows, PAIR), jnp.bfloat16),
            pltpu.VMEM((rows, PAIR), jnp.bfloat16),
            pltpu.VMEM((rows, PAIR), jnp.bfloat16),
        ],
        compiler_params=pltpu.CompilerParams(vmem_limit_bytes=48 << 20),
        cost_estimate=pl.CostEstimate(
            flops=2 * rows * depth * wide * groups + 2 * groups * heads * rows * rows * 128,
            bytes_accessed=2 * (rows * depth + depth * wide * groups + rows * wide * groups),
            transcendentals=groups * heads * rows * rows // 2,
        ),
        name="attend",
    )(length, inputs, weights, cosines, sines)


def attend_back_kernel(
    block, len_ref, qkv_ref, dz_ref, cos_ref, sin_ref, out_ref, q_all, z_all, k_two, v_two, k_acc, v_acc
):
    rows = qkv_ref.shape[0]
    heads = q_all.shape[0]
    length = len_ref[0]

    @pl.loop(0, rows // block)
    def _(at):
        here = pl.ds(pl.multiple_of(at * block, block), block)
        for part in range(heads // 2):
            lanes = slice(part * PAIR, (part + 1) * PAIR)
            queries = qkv_ref[here, lanes].astype(jnp.float32) * ATTN_MULT
            mixed = dz_ref[here, lanes].astype(jnp.float32)
            for side in range(2):
                q_all[2 * part + side, here, :] = keep_head(queries, side).astype(jnp.bfloat16)
                z_all[2 * part + side, here, :] = keep_head(mixed, side).astype(jnp.bfloat16)
        keys, values = both_heads(qkv_ref[here, heads * HEAD_SIZE :].astype(jnp.float32))
        k_two[here, :] = keys.astype(jnp.bfloat16)
        v_two[here, :] = values.astype(jnp.bfloat16)
        k_acc[here, :] = jnp.zeros((block, PAIR), jnp.float32)
        v_acc[here, :] = jnp.zeros((block, PAIR), jnp.float32)

    def turn_back(now, here, table):
        return (now * cos_ref[here, table] - half_turn(now) * sin_ref[here, table]).astype(
            jnp.bfloat16
        )

    for at in range(rows // block):
        here = slice(at * block, (at + 1) * block)
        upto = (at + 1) * block
        key = lax.broadcasted_iota(jnp.int32, (upto, block), 0)
        query = lax.broadcasted_iota(jnp.int32, (upto, block), 1) + at * block
        allowed = key < jnp.minimum(query + 1, length)

        def one_head(head):
            queries, mixed = q_all[head, here, :], z_all[head, here, :]
            scores = jnp.where(allowed, dot_nt(k_two[:upto, :], queries), MASKED)
            power = jnp.exp(scores - jnp.max(scores, axis=0, keepdims=True))
            weights = power * (1.0 / jnp.sum(power, axis=0, keepdims=True))
            back = dot_nt(v_two[:upto, :], mixed)
            centre = jnp.sum(weights * back, axis=0, keepdims=True)
            slope = (weights * (back - centre)).astype(jnp.bfloat16)
            k_acc[:upto, :] += dot_nn(slope, queries)
            v_acc[:upto, :] += dot_nn(weights.astype(jnp.bfloat16), mixed)
            return dot_tn(slope, k_two[:upto, :]) * ATTN_MULT

        for pair in range(heads // 2):
            low = one_head(2 * pair)
            high = one_head(2 * pair + 1)
            lane = lax.broadcasted_iota(jnp.int32, low.shape, 1)
            lanes = slice(pair * PAIR, (pair + 1) * PAIR)
            out_ref[here, lanes] = turn_back(
                jnp.where(lane < HEAD_SIZE, low, high), here, slice(0, PAIR)
            )

    @pl.loop(0, rows // block)
    def _(at):
        here = pl.ds(pl.multiple_of(at * block, block), block)
        keys, values = k_acc[here, :], v_acc[here, :]
        keys = keys + pltpu.roll(keys, HEAD_SIZE, 1)
        values = values + pltpu.roll(values, HEAD_SIZE, 1)
        lane = lax.broadcasted_iota(jnp.int32, keys.shape, 1)
        lanes = slice(heads * HEAD_SIZE, heads * HEAD_SIZE + PAIR)
        out_ref[here, lanes] = turn_back(
            jnp.where(lane < HEAD_SIZE, keys, values), here, slice(PAIR, 2 * PAIR)
        )


def attend_back_fast(length, projected, grad_mixed, cosines, sines, groups):
    rows = projected.shape[0]
    wide = projected.shape[1] // groups
    heads = (wide - PAIR) // HEAD_SIZE
    block = min(256, rows)
    return pl.pallas_call(
        functools.partial(attend_back_kernel, block),
        grid=(groups,),
        out_shape=jax.ShapeDtypeStruct((rows, groups * wide), jnp.bfloat16),
        in_specs=[
            pl.BlockSpec(memory_space=pltpu.SMEM),
            pl.BlockSpec((rows, wide), lambda g: (0, g)),
            pl.BlockSpec((rows, heads * HEAD_SIZE), lambda g: (0, g)),
            pl.BlockSpec((rows, 2 * PAIR), lambda g: (0, 0)),
            pl.BlockSpec((rows, 2 * PAIR), lambda g: (0, 0)),
        ],
        out_specs=pl.BlockSpec((rows, wide), lambda g: (0, g)),
        scratch_shapes=[
            pltpu.VMEM((heads, rows, PAIR), jnp.bfloat16),
            pltpu.VMEM((heads, rows, PAIR), jnp.bfloat16),
            pltpu.VMEM((rows, PAIR), jnp.bfloat16),
            pltpu.VMEM((rows, PAIR), jnp.bfloat16),
            pltpu.VMEM((rows, PAIR), jnp.float32),
            pltpu.VMEM((rows, PAIR), jnp.float32),
        ],
        compiler_params=pltpu.CompilerParams(vmem_limit_bytes=48 << 20),
        cost_estimate=pl.CostEstimate(
            flops=5 * groups * heads * rows * rows * 128,
            bytes_accessed=2 * (2 * rows * wide * groups + rows * heads * HEAD_SIZE * groups),
            transcendentals=groups * heads * rows * rows // 2,
        ),
        name="attend_back",
    )(length, projected, grad_mixed, cosines, sines)


def ffn_kernel(
    cols,
    own_ref,
    resid_ref,
    grad_ref,
    wg_own,
    wu_own,
    wd_own,
    wg_far,
    wu_far,
    wd_far,
    wg_sib,
    wu_sib,
    wd_sib,
    b_all,
    u_all,
    dgu_all,
    mlp_all,
    back_all,
    land_ref,
    sums_ref,
    wg,
    wu,
    wd,
    b_buf,
    g_buf,
    u_buf,
    dg_buf,
    du_buf,
    mlp_buf,
    back_buf,
    turn_buf,
    w_sems,
    ag_send,
    ag_recv,
    back_send,
    back_recv,
    pair_sems,
    io_sems,
):
    group, core, mate, row, col = place()
    sibling = (group + 1 - 2 * core, row, col)
    last = cols - 1
    depth = wg_own.shape[0]
    half = depth // 2
    units = wg_own.shape[1]
    tile = min(512, units)

    barrier = pltpu.get_barrier_semaphore()
    for step in range(1, cols):
        pl.semaphore_signal(
            barrier,
            inc=1,
            device_id=(group, row, lax.rem(col + step, cols)),
            device_id_type=MESH_IDS,
        )
    greet(sibling)
    pl.semaphore_wait(barrier, cols)

    def pass_on(src, at, to, way):
        return pltpu.make_async_remote_copy(
            src_ref=src,
            dst_ref=b_all.at[at],
            send_sem=ag_send.at[way, at],
            recv_sem=ag_recv.at[at],
            device_id=(group, row, to),
            device_id_type=MESH_IDS,
        )

    @pl.when(col < last)
    def _():
        pass_on(own_ref, col, col + 1, 0).start()

    @pl.when(col > 0)
    def _():
        pass_on(own_ref, col, col - 1, 1).start()

    def rows_at(first, size):
        return pl.ds(pl.multiple_of(first, half), size)

    own_copy = pltpu.make_async_copy(own_ref, b_all.at[col], io_sems.at[0])
    own_copy.start()
    load_resid = pltpu.make_async_copy(resid_ref, mlp_buf, io_sems.at[8])
    load_resid.start()
    far = (1 - row) * depth
    loads = []
    for at, (full, mine, across, shared) in enumerate(
        ((wg, wg_own, wg_far, wg_sib), (wu, wu_own, wu_far, wu_sib), (wd, wd_own, wd_far, wd_sib))
    ):
        loads += [
            pltpu.make_async_copy(mine, full.at[rows_at(row * depth, depth)], w_sems.at[3 * at]),
            pltpu.make_async_copy(
                across, full.at[rows_at(far + core * half, half)], w_sems.at[3 * at + 1]
            ),
            pltpu.make_async_copy(
                shared, full.at[rows_at(far + (1 - core) * half, half)], w_sems.at[3 * at + 2]
            ),
        ]
    for load in loads:
        load.start()
    own_copy.wait()
    for load in loads:
        load.wait()

    def order(at):
        inner_low = jnp.where(at < 2, 1 - at, at)
        inner_high = jnp.where(at == 3, 0, jnp.where(at == 0, 2, jnp.where(at == 1, 1, 3)))
        return jnp.where(
            col == 0,
            at,
            jnp.where(col == last, last - at, jnp.where(col == 1, inner_low, inner_high)),
        )

    def arrive(chunk):
        pass_on(b_all.at[chunk], chunk, col, 0).wait_recv()

        @pl.when((chunk < col) & (col < last))
        def _():
            pass_on(b_all.at[chunk], chunk, col + 1, 0).start()

        @pl.when((chunk > col) & (col > 0))
        def _():
            pass_on(b_all.at[chunk], chunk, col - 1, 1).start()

    def outputs(chunk):
        return (
            pltpu.make_async_copy(u_buf, u_all.at[chunk], io_sems.at[1]),
            pltpu.make_async_copy(dg_buf, dgu_all.at[chunk, :, 0:units], io_sems.at[2]),
            pltpu.make_async_copy(du_buf, dgu_all.at[chunk, :, units : 2 * units], io_sems.at[3]),
        )

    def mlp_out(chunk):
        return pltpu.make_async_copy(mlp_buf, mlp_all.at[chunk], io_sems.at[4])

    def back_out(at, chunk):
        return pltpu.make_async_remote_copy(
            src_ref=back_buf.at[slot_of(at)],
            dst_ref=back_all.at[col],
            send_sem=back_send.at[at],
            recv_sem=back_recv.at[col],
            device_id=(group, row, chunk),
            device_id_type=MESH_IDS,
        )

    def slot_of(at):
        return lax.rem(at, cols - 1)

    own_back = pltpu.make_async_copy(back_buf.at[0], back_all.at[col], io_sems.at[5])
    at_end = (col == 0) | (col == last)

    def one_chunk(at, unused):
        chunk = order(at)

        @pl.when(at_end & (at > 0))
        def _():
            arrive(order(at))

        @pl.when(jnp.logical_not(at_end) & (at == 1))
        def _():
            arrive(order(1))
            arrive(order(2))

        @pl.when(jnp.logical_not(at_end) & (at == 3))
        def _():
            arrive(order(3))

        load_b = pltpu.make_async_copy(b_all.at[chunk], b_buf, io_sems.at[6])
        load_g = pltpu.make_async_copy(grad_ref.at[chunk], g_buf, io_sems.at[7])
        load_b.start()
        load_g.start()

        @pl.when(at > 0)
        def _():
            for copy in outputs(order(at - 1)):
                copy.wait()

        load_b.wait()
        load_g.wait()

        @pl.loop(0, units // tile)
        def _(step):
            lanes = pl.ds(pl.multiple_of(step * tile, tile), tile)
            gate = dot_nn(b_buf[...], wg[:, lanes])
            upward = dot_nn(b_buf[...], wu[:, lanes])
            back = RES_MULT * dot_nn(g_buf[...], wd[:, lanes])
            opened = 1.0 / (1.0 + jnp.exp(-gate))
            silu = gate * opened
            u_buf[:, lanes] = (silu * upward).astype(jnp.bfloat16)
            slope = opened * (1.0 + gate * (1.0 - opened))
            dg_buf[:, lanes] = (back * upward * slope).astype(jnp.bfloat16)
            du_buf[:, lanes] = (back * silu).astype(jnp.bfloat16)

        for copy in outputs(chunk):
            copy.start()

        @pl.when(at > 0)
        def _():
            mlp_out(order(at - 1)).wait()

        @pl.when(at == 0)
        def _():
            load_resid.wait()

        @pl.when(at == last)
        def _():
            own_back.wait()

        @pl.loop(0, 2 * depth // tile)
        def _(step):
            here = pl.ds(pl.multiple_of(step * tile, tile), tile)
            back = dot_nt(dg_buf[...], wg[here, :]) + dot_nt(du_buf[...], wu[here, :])
            back_buf[slot_of(at), :, here] = back.astype(jnp.bfloat16)
            added = jnp.where(at == 0, mlp_buf[:, here].astype(jnp.float32), 0.0)
            mlp_buf[:, here] = (added + RES_MULT * dot_nt(u_buf[...], wd[here, :])).astype(
                jnp.bfloat16
            )

        mlp_out(chunk).start()

        @pl.when(at == 0)
        def _():
            own_back.start()

        @pl.when(at > 0)
        def _():
            back_out(at, chunk).start()

        return unused

    lax.fori_loop(0, cols, one_chunk, 0)
    for copy in outputs(order(last)):
        copy.wait()
    mlp_out(order(last)).wait()

    rows = b_buf.shape[0]
    loads = []
    for chunk in range(cols):
        here = slice(chunk * rows, (chunk + 1) * rows)
        loads += [
            pltpu.make_async_copy(
                dgu_all.at[chunk, :, 0:units], wg.at[here], w_sems.at[chunk]
            ),
            pltpu.make_async_copy(
                dgu_all.at[chunk, :, units : 2 * units], wu.at[here], w_sems.at[cols + chunk]
            ),
            pltpu.make_async_copy(u_all.at[chunk], wd.at[here], w_sems.at[2 * cols + chunk]),
        ]
    for load in loads:
        load.start()
    for load in loads:
        load.wait()

    buffers = (dg_buf, du_buf, u_buf)

    def to_sibling(at, part):
        return pltpu.make_async_remote_copy(
            src_ref=buffers[part],
            dst_ref=land_ref.at[at, part],
            send_sem=pair_sems.at[0, at, part],
            recv_sem=pair_sems.at[1, at, part],
            device_id=sibling,
            device_id_type=MESH_IDS,
        )

    def landed(at, part):
        return pltpu.make_async_copy(land_ref.at[at, part], buffers[part], io_sems.at[5 + part])

    def results(at, part):
        here = slice(part * units, (part + 1) * units)
        return pltpu.make_async_copy(
            buffers[part], sums_ref.at[at, :, here], io_sems.at[1 + part]
        )

    def turned(source, into, at):
        load = pltpu.make_async_copy(source.at[:, :, aligned(at, rows)], turn_buf, io_sems.at[4])
        load.start()
        load.wait()
        for chunk in range(cols):
            into[:, chunk * rows : (chunk + 1) * rows] = turn_buf[chunk].T

    parts = range(3)

    def one_block(at, unused):
        high = lax.rem(at, 2)
        is_own = at >= 2
        block = 2 * high + jnp.where(is_own, core, 1 - core)
        turned(b_all, b_buf, block)
        turned(grad_ref, g_buf, block)

        @pl.when((at == 1) | (at == 2))
        def _():
            for part in parts:
                to_sibling(at - 1, part).wait_send()

        @pl.when(at == 3)
        def _():
            for part in parts:
                results(0, part).wait()

        @pl.when(is_own)
        def _():
            for part in parts:
                to_sibling(high, part).wait_recv()
                landed(high, part).start()
            for part in parts:
                landed(high, part).wait()

        @pl.loop(0, units // tile)
        def _(step):
            lanes = aligned(step, tile)

            def put(buffer, value):
                other = jnp.where(is_own, buffer[:, lanes].astype(jnp.float32), 0.0)
                buffer[:, lanes] = (other + value).astype(jnp.bfloat16)

            put(dg_buf, dot_nn(b_buf[...], wg[:, lanes]))
            put(du_buf, dot_nn(b_buf[...], wu[:, lanes]))
            put(u_buf, RES_MULT * dot_nn(g_buf[...], wd[:, lanes]))

        @pl.when(jnp.logical_not(is_own))
        def _():
            for part in parts:
                to_sibling(at, part).start()

        @pl.when(is_own)
        def _():
            for part in parts:
                results(high, part).start()

        return unused

    lax.fori_loop(0, 4, one_block, 0)
    for part in parts:
        results(1, part).wait()
    for at in range(1, cols):
        back_out(at, order(at)).wait_send()
        source = lax.rem(col + at, cols)
        pltpu.make_async_remote_copy(
            src_ref=back_buf.at[slot_of(at)],
            dst_ref=back_all.at[source],
            send_sem=back_send.at[at],
            recv_sem=back_recv.at[source],
            device_id=(group, row, source),
            device_id_type=MESH_IDS,
        ).wait_recv()
    for chunk in range(cols):

        @pl.when((col >= chunk) & (col < last))
        def _():
            pass_on(own_ref, chunk, col + 1, 0).wait_send()

        @pl.when((col <= chunk) & (col > 0))
        def _():
            pass_on(own_ref, chunk, col - 1, 1).wait_send()


def feed_forward(own_input, resid, grad_rows, weights, cols):
    rows, width = own_input.shape
    units = weights[0].shape[1]
    anywhere = pl.BlockSpec(memory_space=pl.ANY)
    bf16 = jnp.bfloat16
    return pl.pallas_call(
        functools.partial(ffn_kernel, cols),
        out_shape=(
            jax.ShapeDtypeStruct((cols, rows, width), bf16),
            jax.ShapeDtypeStruct((cols, rows, units), bf16),
            jax.ShapeDtypeStruct((cols, rows, 2 * units), bf16),
            jax.ShapeDtypeStruct((cols, rows, width), bf16),
            jax.ShapeDtypeStruct((cols, rows, width), bf16),
            jax.ShapeDtypeStruct((2, 3, rows, units), bf16),
            jax.ShapeDtypeStruct((2, rows, 3 * units), bf16),
        ),
        in_specs=[anywhere] * 12,
        out_specs=(anywhere,) * 7,
        scratch_shapes=[
            pltpu.VMEM((width, units), bf16),
            pltpu.VMEM((width, units), bf16),
            pltpu.VMEM((width, units), bf16),
            pltpu.VMEM((rows, width), bf16),
            pltpu.VMEM((rows, width), bf16),
            pltpu.VMEM((rows, units), bf16),
            pltpu.VMEM((rows, units), bf16),
            pltpu.VMEM((rows, units), bf16),
            pltpu.VMEM((rows, width), bf16),
            pltpu.VMEM((cols - 1, rows, width), bf16),
            pltpu.VMEM((cols, rows, rows), bf16),
            pltpu.SemaphoreType.DMA((12,)),
            pltpu.SemaphoreType.DMA((2, cols)),
            pltpu.SemaphoreType.DMA((cols,)),
            pltpu.SemaphoreType.DMA((cols,)),
            pltpu.SemaphoreType.DMA((cols,)),
            pltpu.SemaphoreType.DMA((2, 2, 3)),
            pltpu.SemaphoreType.DMA((9,)),
        ],
        compiler_params=pltpu.CompilerParams(
            collective_id=2, has_side_effects=True, vmem_limit_bytes=60 << 20
        ),
        cost_estimate=pl.CostEstimate(
            flops=18 * cols * rows * width * units,
            bytes_accessed=800 << 20,
            transcendentals=cols * rows * units,
        ),
        name="feed_forward",
    )(own_input, resid, grad_rows, *weights)


def finish_kernel(
    cols,
    ig_ref,
    gq_ref,
    go_ref,
    gain_ref,
    gin_ref,
    sq_ref,
    so_ref,
    gsum_ref,
    q_keep,
    q_sib,
    q_a1,
    q_a2,
    q_b1,
    q_b2,
    q_z,
    o_keep,
    o_sib,
    o_a1,
    o_a2,
    o_b1,
    o_b2,
    o_z,
    gain_now,
    gain_in,
    ig_sems,
    gain_sems,
    q_sems,
    o_sems,
    qz_sems,
    oz_sems,
    local_sems,
):
    group, core, mate, row, col = place()
    pair = group - core
    high = pair // 2
    sibling = (pair + 1 - core, row, col)
    over_x = (group, 1 - row, col)
    over_y = (2 * (1 - high) + core, row, col)
    width = gin_ref.shape[2]

    def line(step):
        return lax.rem(col + step + cols, cols)

    barrier = pltpu.get_barrier_semaphore()

    def greet(device):
        pl.semaphore_signal(barrier, inc=1, device_id=device, device_id_type=MESH_IDS)

    greet(sibling)
    greet(over_x)
    greet(over_y)
    for step in range(1, cols):
        greet((mate, core, line(step)))
        greet((group, row, line(step)))

    @pl.when(core != row)
    def _():
        greet((mate, core, col))

    pl.semaphore_wait(barrier, 2 * cols + 1 + (core - row) * (core - row))

    def remote(src, dst, sems, at, device):
        return pltpu.make_async_remote_copy(
            src_ref=src,
            dst_ref=dst,
            send_sem=sems.at[0, at],
            recv_sem=sems.at[1, at],
            device_id=device,
            device_id_type=MESH_IDS,
        )

    def lanes(block, size):
        return pl.ds(pl.multiple_of(block * size, size), size)

    matrices = (
        (gq_ref, sq_ref, q_keep, q_sib, q_a1, q_a2, q_b1, q_b2, q_z, q_sems, qz_sems),
        (go_ref, so_ref, o_keep, o_sib, o_a1, o_a2, o_b1, o_b2, o_z, o_sems, oz_sems),
    )

    def moves(m):
        grads, out, keep, sib, a1, a2, b1, b2, zb, sems, z_sems = matrices[m]
        return dict(
            s0=remote(grads.at[:, 1 - core], sib, sems, 0, sibling),
            a1=remote(grads.at[:, core, 1 - row], a1, sems, 1, over_x),
            a2=remote(keep.at[1 - high, row], a2, sems, 2, over_y),
            b1=remote(sib.at[1 - high], b1, sems, 3, over_y),
            b2=remote(sib.at[high, 1 - row], b2, sems, 4, over_x),
            own=pltpu.make_async_copy(grads.at[:, core], keep, local_sems.at[m]),
        )

    copies = (moves(0), moves(1))

    def rows_plus(into, more):
        rows = into.shape[0]
        step = min(32, rows)

        @pl.loop(0, rows // step)
        def _(at):
            here = pl.ds(pl.multiple_of(at * step, step), step)
            into[here, :] = (
                into[here, :].astype(jnp.float32) + more[here, :].astype(jnp.float32)
            ).astype(into.dtype)

    def token_copy(step, at):
        return remote(
            ig_ref.at[:, lanes(line(step), width)],
            gin_ref.at[at],
            ig_sems,
            step,
            (mate, core, line(step)),
        )

    own_tokens = pltpu.make_async_copy(
        ig_ref.at[:, lanes(col, width)], gin_ref.at[col], local_sems.at[2]
    )

    for m in range(2):
        copies[m]["s0"].start()
        copies[m]["a1"].start()
        copies[m]["own"].start()
    for step in range(1, cols):
        token_copy(step, col).start()

    @pl.when(core != row)
    def _():
        token_copy(0, col).start()

    @pl.when(core == row)
    def _():
        own_tokens.start()

    gain_load = pltpu.make_async_copy(gain_ref, gain_now.at[0], local_sems.at[3])
    gain_load.start()
    gain_load.wait()
    near = (
        sibling,
        over_x,
        over_y,
        (group, row, col + 1 - 2 * lax.rem(col, 2)),
        (group, row, lax.rem(col + cols // 2, cols)),
    )

    def gain_round(at):
        exchange = remote(gain_now.at[at], gain_in.at[at], gain_sems, at, near[at])
        exchange.start()
        exchange.wait()
        gain_now[at + 1] = gain_now[at] + gain_in[at]

    gain_round(0)
    for m in range(2):
        copies[m]["s0"].wait()
        copies[m]["b1"].start()
    gain_round(1)
    for m in range(2):
        grads, out, keep, sib, a1, a2, b1, b2, zb, sems, z_sems = matrices[m]
        copies[m]["own"].wait()
        copies[m]["a1"].wait()
        rows_plus(keep.at[1 - high, row], a1.at[1 - high])
        copies[m]["a2"].start()
    for m in range(2):
        grads, out, keep, sib, a1, a2, b1, b2, zb, sems, z_sems = matrices[m]
        copies[m]["b1"].wait()
        rows_plus(sib.at[high, 1 - row], b1.at[1 - row])
        copies[m]["b2"].start()
    gain_round(2)
    for m in range(2):
        grads, out, keep, sib, a1, a2, b1, b2, zb, sems, z_sems = matrices[m]
        rows_plus(keep.at[high, row], a1.at[high])
        rows_plus(sib.at[high, row], b1.at[row])

    def z_moves(m, side, source):
        grads, out, keep, sib, a1, a2, b1, b2, zb, sems, z_sems = matrices[m]
        held = (keep, sib)[side]
        wide = zb.shape[3]
        return [
            pltpu.make_async_remote_copy(
                src_ref=held.at[high, row, :, lanes(line(step), wide)],
                dst_ref=zb.at[side, line(source(step))],
                send_sem=z_sems.at[0, side, step],
                recv_sem=z_sems.at[1, side, step],
                device_id=(group, row, line(step)),
                device_id_type=MESH_IDS,
            )
            for step in range(1, cols)
        ]

    for side, last_copy in ((0, "a2"), (1, "b2")):
        for m in range(2):
            grads, out, keep, sib, a1, a2, b1, b2, zb, sems, z_sems = matrices[m]
            copies[m][last_copy].wait()
            rows_plus((keep, sib)[side].at[high, row], (a2, b2)[side])
            for copy in z_moves(m, side, lambda step: 0):
                copy.start()
    gain_round(3)
    gain_round(4)
    gsum_ref[...] = gain_now[5]
    for side in range(2):
        for m in range(2):
            grads, out, keep, sib, a1, a2, b1, b2, zb, sems, z_sems = matrices[m]
            for copy in z_moves(m, side, lambda step: 0):
                copy.wait_send()
            for copy in z_moves(m, side, lambda step: -step):
                copy.wait_recv()
            held = (keep, sib)[side]
            wide = zb.shape[3]
            at_core = core if side == 0 else 1 - core
            rows = zb.shape[2]
            tall = min(32, rows)

            @pl.loop(0, rows // tall)
            def _(at):
                here = pl.ds(pl.multiple_of(at * tall, tall), tall)
                total = held[high, row, here, lanes(col, wide)].astype(jnp.float32)
                for step in range(1, cols):
                    total = total + zb[side, line(-step), here, :].astype(jnp.float32)
                out[at_core, here, :] = total

    for step in range(1, cols):
        token_copy(step, line(-step)).wait_recv()
        token_copy(step, col).wait_send()

    @pl.when(core != row)
    def _():
        token_copy(0, col).wait_recv()
        token_copy(0, col).wait_send()

    @pl.when(core == row)
    def _():
        own_tokens.wait()


def finish(input_grad, grad_q, grad_o, gains, cols):
    anywhere = pl.BlockSpec(memory_space=pl.ANY)
    in_vmem = pl.BlockSpec(memory_space=pltpu.VMEM)
    bf16, f32 = jnp.bfloat16, jnp.float32
    length, full = input_grad.shape
    rows = grad_q.shape[0] // 8

    def buffers(wide):
        return [
            pltpu.VMEM((2, 2, rows, wide), bf16),
            pltpu.VMEM((2, 2, rows, wide), bf16),
            pltpu.VMEM((2, rows, wide), bf16),
            pltpu.VMEM((rows, wide), bf16),
            pltpu.VMEM((2, rows, wide), bf16),
            pltpu.VMEM((rows, wide), bf16),
            pltpu.VMEM((2, cols, rows, wide // cols), bf16),
        ]

    wide_q, wide_o = grad_q.shape[1], grad_o.shape[1]
    return pl.pallas_call(
        functools.partial(finish_kernel, cols),
        out_shape=(
            jax.ShapeDtypeStruct((cols, length, full // cols), bf16),
            jax.ShapeDtypeStruct((2, rows, wide_q // cols), f32),
            jax.ShapeDtypeStruct((2, rows, wide_o // cols), f32),
            jax.ShapeDtypeStruct(gains.shape, f32),
        ),
        in_specs=[anywhere] * 4,
        out_specs=(anywhere, in_vmem, in_vmem, in_vmem),
        scratch_shapes=buffers(wide_q)
        + buffers(wide_o)
        + [
            pltpu.VMEM((6,) + gains.shape, f32),
            pltpu.VMEM((5,) + gains.shape, f32),
            pltpu.SemaphoreType.DMA((2, cols)),
            pltpu.SemaphoreType.DMA((2, 5)),
            pltpu.SemaphoreType.DMA((2, 5)),
            pltpu.SemaphoreType.DMA((2, 5)),
            pltpu.SemaphoreType.DMA((2, 2, cols)),
            pltpu.SemaphoreType.DMA((2, 2, cols)),
            pltpu.SemaphoreType.DMA((4,)),
        ],
        compiler_params=pltpu.CompilerParams(
            collective_id=3, has_side_effects=True, vmem_limit_bytes=40 << 20
        ),
        cost_estimate=pl.CostEstimate(flops=0, bytes_accessed=300 << 20, transcendentals=0),
        name="finish",
    )(
        input_grad,
        grad_q.reshape(2, 2, 2, rows, wide_q),
        grad_o.reshape(2, 2, 2, rows, wide_o),
        gains,
    )


def one_sequence_body(
    tokens,
    cotangent,
    lengths,
    deal_order,
    gain_attn,
    gain_ffn,
    w_query,
    key_value_weight,
    w_out,
    w_gate_up,
    w_down,
):
    seq_group, rows_local, width_local = tokens.shape
    row_count = lax.axis_size("row")
    col_count = lax.axis_size("col")
    full_width = width_local * col_count
    slot_len = rows_local * row_count
    group, core, mate, row, col = place()
    query_half = w_query.shape[1] // 2
    kv_half = key_value_weight.shape[2] // 2
    hidden = w_down.shape[1]

    def core_half(matrix, axis):
        width = matrix.shape[axis] // 2
        return lax.dynamic_slice_in_dim(matrix, core * width, width, axis)

    def joined(mine, other, at):
        return jnp.where(
            at == 0, jnp.concatenate([mine, other]), jnp.concatenate([other, mine])
        )

    def from_sibling(value):
        return lax.ppermute(value, "dp", SIBLINGS)

    def half_rows(matrix):
        return core_half(matrix, 0)

    pack_q = jnp.concatenate(
        [
            core_half(w_query, 1),
            core_half(key_value_weight[:, 0], 1),
            core_half(key_value_weight[:, 1], 1),
        ],
        axis=1,
    )
    pack_o = core_half(w_out, 1)
    gain_one = gain_attn.astype(jnp.float32)
    gain_two = gain_ffn.astype(jnp.float32)
    own_tokens, attn_input, weights_qkv = start_exchange(
        tokens, pack_q, gain_one, row_count, col_count
    )

    length = lax.dynamic_slice_in_dim(lengths, mate * seq_group + col, 1)
    given_pos = row * rows_local + jnp.arange(rows_local, dtype=jnp.int32)
    given_lengths = lax.dynamic_slice_in_dim(lengths, group * seq_group, seq_group)
    given_live = given_pos[None, :, None] < given_lengths[:, None, None]
    everyone = lax.all_gather(cotangent, "dp", axis=0, tiled=True)
    everyone, attn_input = lax.optimization_barrier((everyone, attn_input))
    picked = pick_sequences(everyone, deal_order, group * seq_group, seq_group)
    picked = jnp.where(given_live, picked, jnp.zeros_like(picked))
    given = lax.ppermute(picked, ("dp", "row"), CROSSED)
    weights_out = gather_weights(pack_o, picked, row_count, col_count)
    given, weights_out = lax.optimization_barrier((given, weights_out))
    line_cot = lax.all_gather(given, "col", axis=2, tiled=True)
    own_grad = lax.dynamic_index_in_dim(line_cot, col, keepdims=False).astype(jnp.float32)

    w_gate_up, w_down, attn_input, weights_out = lax.optimization_barrier(
        (w_gate_up, w_down, attn_input, weights_out)
    )
    far_gate_up = lax.ppermute(half_rows(w_gate_up), "row", OVER_X)
    far_down = lax.ppermute(half_rows(w_down), "row", OVER_X)
    own_mats = (w_gate_up[:, 0], w_gate_up[:, 1], w_down)
    far_mats = (far_gate_up[:, 0], far_gate_up[:, 1], far_down)
    sibling_mats = tuple(from_sibling(matrix) for matrix in far_mats)

    cosine_table, sine_table = rope_tables(jnp.arange(slot_len, dtype=jnp.int32), HEAD_SIZE)
    cosine_table, sine_table = lax.optimization_barrier((cosine_table, sine_table))
    cosines = jnp.concatenate(
        [jnp.tile(cosine_table, (1, 6)), jnp.ones((slot_len, HEAD_SIZE), jnp.float32)], axis=1
    )
    turning = jnp.concatenate([-sine_table, sine_table], axis=1)
    sines = jnp.concatenate(
        [jnp.tile(turning, (1, 3)), jnp.zeros((slot_len, HEAD_SIZE), jnp.float32)], axis=1
    )
    own_float = own_tokens.astype(jnp.float32)
    scale_one = lax.rsqrt(jnp.mean(own_float * own_float, axis=1, keepdims=True) + EPSILON)
    projected, heads_out = attend_fast(
        length, attn_input, weights_qkv, cosines, sines, col_count
    )

    def summed_rows(partial):
        count = partial.shape[0] // 2
        mine = lax.dynamic_slice_in_dim(partial, core * count, count)
        other = lax.dynamic_slice_in_dim(partial, (1 - core) * count, count)
        return mine.astype(jnp.float32) + from_sibling(other).astype(jnp.float32)

    attn_rows = summed_rows(expand_local(heads_out, weights_out).astype(jnp.bfloat16))
    resid = own_float + RES_MULT * attn_rows
    scale_two = lax.rsqrt(jnp.mean(resid * resid, axis=1, keepdims=True) + EPSILON)
    own_ffn = (resid * scale_two * gain_two).astype(jnp.bfloat16)

    unused_b, unused_u, unused_gu, mlp_part, back_part, unused_land, grad_sums = feed_forward(
        own_ffn,
        resid.astype(jnp.bfloat16),
        line_cot,
        own_mats + far_mats + sibling_mats,
        col_count,
    )
    grad_normed_two = jnp.sum(back_part.astype(jnp.float32), axis=0)

    sums_ffn = lax.psum_scatter(
        grad_sums.reshape(-1, 3 * hidden),
        ("dp", "row"),
        scatter_dimension=0,
        axis_index_groups=CORES,
        tiled=True,
    )

    weighted_two = grad_normed_two * gain_two
    inner_two = jnp.sum(weighted_two * resid, axis=1, keepdims=True)
    grad_resid = (
        own_grad + scale_two * weighted_two - resid * scale_two**3 * inner_two / full_width
    )
    gain_two_part = jnp.sum(grad_normed_two * resid * scale_two, axis=0)
    own_attn_grad = (RES_MULT * grad_resid).astype(jnp.bfloat16)
    grad_attn = joined(own_attn_grad, from_sibling(own_attn_grad), core)
    grad_heads = contract_local(grad_attn, weights_out).astype(jnp.bfloat16)
    grad_out = token_outer(grad_attn, heads_out).astype(jnp.bfloat16)
    grad_projected = attend_back_fast(
        length, projected, grad_heads, cosines, sines, col_count
    )
    mlp_part, sums_ffn, grad_projected = lax.optimization_barrier(
        (mlp_part, sums_ffn, grad_projected)
    )
    out_cols = lax.psum_scatter(mlp_part, "col", scatter_dimension=2, tiled=True)
    grad_normed_one = summed_rows(expand_local(grad_projected, weights_qkv).astype(jnp.bfloat16))
    grad_qkv = token_outer(attn_input, grad_projected).astype(jnp.bfloat16)
    weighted_one = grad_normed_one * gain_one
    inner_one = jnp.sum(weighted_one * own_float, axis=1, keepdims=True)
    own_input_grad = (
        grad_resid
        + scale_one * weighted_one
        - own_float * scale_one**3 * inner_one / full_width
    ).astype(jnp.bfloat16)
    gain_one_part = jnp.sum(grad_normed_one * own_float * scale_one, axis=0)
    sums_ffn = sums_ffn.astype(jnp.float32)
    sums_gate_up = sums_ffn[:, : 2 * hidden].reshape(-1, 2, hidden)
    sums_down = sums_ffn[:, 2 * hidden :]
    gains = jnp.stack([gain_one_part, gain_two_part]).reshape(8, -1)
    given_grad, sums_q, sums_o, gain_sums = finish(
        own_input_grad, grad_qkv, grad_out, gains, col_count
    )
    out_cols, given_grad = lax.optimization_barrier((out_cols, given_grad))
    layer_out = jnp.where(
        given_live, lax.ppermute(out_cols, ("dp", "row"), CROSSED).astype(jnp.float32), 0.0
    )
    input_grad = given_grad.astype(jnp.float32)
    grad_gain_attn, grad_gain_ffn = gain_sums.reshape(2, full_width)

    def both_cores(sums):
        return jnp.concatenate([sums[0], sums[1]], axis=1)

    qk = query_half + kv_half
    out_query = both_cores(sums_q[:, :, :query_half])
    out_kv = jnp.stack(
        [
            both_cores(sums_q[:, :, query_half:qk]),
            both_cores(sums_q[:, :, qk:]),
        ],
        axis=1,
    )
    out_out = both_cores(sums_o)
    return (
        layer_out,
        input_grad,
        out_query,
        out_kv,
        out_out,
        sums_gate_up,
        sums_down,
        grad_gain_attn,
        grad_gain_ffn,
    )


def general_body(
    tokens,
    cotangent,
    lengths,
    deal_order,
    gain_attn,
    gain_ffn,
    w_query,
    key_value_weight,
    w_out,
    w_gate_up,
    w_down,
):
    seq_group, rows_local, width_local = tokens.shape
    row_count = lax.axis_size("row")
    col_count = lax.axis_size("col")
    full_width = width_local * col_count
    slot_len = rows_local * row_count
    total_rows = seq_group * rows_local
    head_size = HEAD_SIZE
    query_width = w_query.shape[1]
    kv_width = key_value_weight.shape[2]
    kv_heads = kv_width // head_size
    group_size = query_width // kv_width
    group_index = lax.axis_index("dp")
    row_index = lax.axis_index("row")
    col_index = lax.axis_index("col")
    matrices = {
        "qkv": jnp.concatenate(
            [w_query, key_value_weight.reshape(key_value_weight.shape[0], 2 * kv_width)], axis=1
        ),
        "out": w_out,
        "gate_up": w_gate_up,
        "down": w_down,
    }

    def contract_with(operand, which_one):
        return contract_rows(operand, matrices[which_one])

    def expand_with(operand, which_one):
        return expand_rows(operand, matrices[which_one])

    own_cotangent = bring_cotangent(cotangent, deal_order, group_index * seq_group)
    own_rows = tokens
    seq_lens = lax.dynamic_slice_in_dim(lengths, group_index * seq_group, seq_group)
    local_pos = row_index * rows_local + jnp.arange(rows_local, dtype=jnp.int32)
    key_pos = jnp.arange(slot_len, dtype=jnp.int32)
    live_rows = (local_pos[None, :] < seq_lens[:, None]).astype(jnp.float32).reshape(total_rows, 1)
    cosine_table, sine_table = rope_tables(jnp.tile(local_pos, seq_group), head_size)
    own_tokens = own_rows.reshape(total_rows, width_local)
    wide_float = widen_cols(own_tokens).astype(jnp.float32)
    scale_one = lax.rsqrt(jnp.mean(wide_float * wide_float, axis=1, keepdims=True) + EPSILON)
    gain_one = gain_attn.astype(jnp.float32)
    first_normed = wide_float * scale_one
    attn_input = (first_normed * gain_one).astype(jnp.bfloat16)
    projected = contract_with(attn_input, "qkv")
    query_lin = projected[:, :query_width].reshape(total_rows, query_width // head_size, head_size)
    key_lin = projected[:, query_width : query_width + kv_width].reshape(
        total_rows, kv_heads, head_size
    )
    value_lin = projected[:, query_width + kv_width :]
    query_rows = rotary_embed(query_lin, cosine_table, sine_table).astype(jnp.bfloat16)
    keys_own = (
        rotary_embed(key_lin, cosine_table, sine_table)
        .astype(jnp.bfloat16)
        .reshape(seq_group, rows_local, kv_width)
    )
    values_own = value_lin.astype(jnp.bfloat16).reshape(seq_group, rows_local, kv_width)
    all_keys, all_values = (
        lax.all_gather(keys_own, "row", axis=1, tiled=True),
        lax.all_gather(values_own, "row", axis=1, tiled=True),
    )
    query_split = query_rows.reshape(seq_group, rows_local, kv_heads, group_size, head_size)
    key_split = all_keys.reshape(seq_group, slot_len, kv_heads, head_size)
    value_split = all_values.reshape(seq_group, slot_len, kv_heads, head_size)

    def forward_seq(inputs):
        return attend(inputs, key_pos, local_pos)

    mixed_heads, row_max, row_sums = lax.map(
        forward_seq, (query_split, key_split, value_split, seq_lens)
    )
    heads_out = mixed_heads.reshape(total_rows, query_width).astype(jnp.bfloat16)
    attn_local = narrow_cols(expand_with(heads_out, "out"))
    resid = own_tokens.astype(jnp.float32) + RES_MULT * attn_local
    gain_two = lax.dynamic_slice_in_dim(
        gain_ffn.astype(jnp.float32), col_index * width_local, width_local
    )
    scale_two = lax.rsqrt(sum_over_cols(jnp.sum(resid * resid, axis=1)) / full_width + EPSILON)[
        :, None
    ]
    normed_two = resid * scale_two
    ffn_input = widen_cols((normed_two * gain_two).astype(jnp.bfloat16))
    gate_up = contract_with(ffn_input, "gate_up")
    gate = gate_up[:, 0]
    upward = gate_up[:, 1]
    sigmoid_gate = jax.nn.sigmoid(gate)
    silu_gate = gate * sigmoid_gate
    hidden = (silu_gate * upward).astype(jnp.bfloat16)
    ffn_local = narrow_cols(expand_with(hidden, "down"))
    layer_out = live_rows * (resid + RES_MULT * ffn_local)
    grad_rows = live_rows * own_cotangent.reshape(total_rows, width_local).astype(jnp.float32)
    grad_ffn = widen_cols((RES_MULT * grad_rows).astype(jnp.bfloat16))
    grad_hidden = contract_with(grad_ffn, "down")
    grad_down = token_outer(grad_ffn, hidden)
    slope = sigmoid_gate * (1.0 + gate * (1.0 - sigmoid_gate))
    grad_gate_rows = jnp.stack(
        [grad_hidden * upward * slope, grad_hidden * silu_gate], axis=1
    ).astype(jnp.bfloat16)
    grad_gate_up = token_outer(ffn_input, grad_gate_rows)
    grad_normed_two = narrow_cols(expand_with(grad_gate_rows, "gate_up"))
    weighted_two = grad_normed_two * gain_two
    inner_two = sum_over_cols(jnp.sum(weighted_two * resid, axis=1))[:, None]
    grad_resid = (
        grad_rows + scale_two * weighted_two - resid * scale_two**3 * inner_two / full_width
    )
    gain_two_part = jnp.sum(grad_normed_two * normed_two, axis=0)
    grad_attn = widen_cols((RES_MULT * grad_resid).astype(jnp.bfloat16))
    grad_heads = contract_with(grad_attn, "out").astype(jnp.bfloat16)
    grad_out = token_outer(grad_attn, heads_out)
    grad_split = grad_heads.reshape(seq_group, rows_local, kv_heads, group_size, head_size)

    def backward_seq(inputs):
        return attend_back(inputs, key_pos, local_pos)

    grad_query, grad_key, grad_value = lax.map(
        backward_seq, (query_split, key_split, value_split, grad_split, row_max, row_sums, seq_lens)
    )
    key_part, value_part = (
        lax.psum_scatter(
            grad_key.reshape(seq_group, slot_len, kv_width).astype(jnp.bfloat16),
            "row",
            scatter_dimension=1,
            tiled=True,
        ).astype(jnp.float32),
        lax.psum_scatter(
            grad_value.reshape(seq_group, slot_len, kv_width).astype(jnp.bfloat16),
            "row",
            scatter_dimension=1,
            tiled=True,
        ).astype(jnp.float32),
    )
    query_back = rotary_embed(
        grad_query.reshape(total_rows, query_width // head_size, head_size),
        cosine_table,
        -sine_table,
    ).reshape(total_rows, query_width)
    key_back = rotary_embed(
        key_part.reshape(total_rows, kv_heads, head_size), cosine_table, -sine_table
    ).reshape(total_rows, kv_width)
    grad_projected = jnp.concatenate(
        [query_back, key_back, value_part.reshape(total_rows, kv_width)], axis=1
    ).astype(jnp.bfloat16)
    grad_qkv = token_outer(attn_input, grad_projected)
    grad_normed_one = expand_with(grad_projected, "qkv")
    weighted_one = grad_normed_one * gain_one
    inner_one = jnp.sum(weighted_one * wide_float, axis=1, keepdims=True)
    input_part = scale_one * weighted_one - wide_float * scale_one**3 * inner_one / full_width
    input_grad = grad_resid + narrow_cols(input_part)
    gain_one_part = jnp.sum(grad_normed_one * first_normed, axis=0)
    gain_two_full = lax.dynamic_update_slice_in_dim(
        jnp.zeros((full_width,), jnp.float32), gain_two_part, col_index * width_local, 0
    )
    grad_gain_attn, grad_gain_ffn = lax.psum((gain_one_part, gain_two_full), ("dp", "row", "col"))
    sums_qkv, sums_out, sums_gate_up, sums_down = (
        lax.psum_scatter(
            grad_qkv.astype(jnp.bfloat16), ("dp", "row"), scatter_dimension=0, tiled=True
        ).astype(jnp.float32),
        lax.psum_scatter(
            grad_out.astype(jnp.bfloat16), ("dp", "row"), scatter_dimension=0, tiled=True
        ).astype(jnp.float32),
        lax.psum_scatter(
            grad_gate_up.astype(jnp.bfloat16), ("dp", "row"), scatter_dimension=0, tiled=True
        ).astype(jnp.float32),
        lax.psum_scatter(
            grad_down.astype(jnp.bfloat16), ("dp", "row"), scatter_dimension=0, tiled=True
        ).astype(jnp.float32),
    )
    out_query = sums_qkv[:, :query_width]
    out_kv = sums_qkv[:, query_width:].reshape(sums_qkv.shape[0], 2, kv_width)
    return (
        layer_out.reshape(seq_group, rows_local, width_local),
        input_grad.reshape(seq_group, rows_local, width_local),
        out_query,
        out_kv,
        sums_out,
        sums_gate_up,
        sums_down,
        grad_gain_attn,
        grad_gain_ffn,
    )


def body(tokens, cotangent, lengths, deal_order, gain_attn, gain_ffn, w_query, key_value_weight, *rest):
    sizes = (lax.axis_size("dp"), lax.axis_size("row"), lax.axis_size("col"))
    one_each = sizes == (4, 2, 4) and tokens.shape[0] == sizes[2]
    pairs = w_query.shape[1] == 8 * HEAD_SIZE and key_value_weight.shape[2] == 2 * HEAD_SIZE
    chosen = one_sequence_body if one_each and pairs else general_body
    return chosen(
        tokens, cotangent, lengths, deal_order, gain_attn, gain_ffn, w_query, key_value_weight, *rest
    )


def solution(mesh):
    placed = (
        P("dp", "row", "col"),
        P("dp", "row", "col"),
        P(),
        P(),
        P(),
        P(),
        P("row", "col"),
        P("row", None, "col"),
        P("row", "col"),
        P("row", None, "col"),
        P("row", "col"),
    )
    return jax.shard_map(
        body,
        mesh=mesh,
        in_specs=placed,
        out_specs=(
            P("dp", "row", "col"),
            P("dp", "row", "col"),
            P(("dp", "row"), "col"),
            P(("dp", "row"), None, "col"),
            P(("dp", "row"), "col"),
            P(("dp", "row"), None, "col"),
            P(("dp", "row"), "col"),
            P(),
            P(),
        ),
        check_vma=False,
    )
```

```python
import functools

import jax
import jax.numpy as jnp
from jax import lax
from jax.experimental import pallas as pl
from jax.experimental.pallas import tpu as pltpu
from jax.sharding import PartitionSpec as P

HEAD_SIZE = 64


EPSILON = 1e-05
THETA = 10000000.0
ATTN_MULT = 0.015625
RES_MULT = 0.22
MASKED = -1e30


def rope_tables(positions, head_size):
    halves = jnp.arange(head_size // 2, dtype=jnp.float32)
    inverse_freq = THETA ** (-(halves * 2.0) / head_size)
    angles = positions.astype(jnp.float32)[:, None] * inverse_freq[None, :]
    return (jnp.cos(angles), jnp.sin(angles))


def rotary_embed(value_rows, cosine_table, sine_table):
    middle = value_rows.shape[-1] // 2
    first_half = value_rows[..., :middle]
    second_half = value_rows[..., middle:]
    cos_part = cosine_table[:, None, :]
    sin_part = sine_table[:, None, :]
    return jnp.concatenate(
        [
            first_half * cos_part - second_half * sin_part,
            second_half * cos_part + first_half * sin_part,
        ],
        axis=-1,
    )


def widen_cols(value_rows):
    return lax.all_gather(value_rows, "col", axis=1, tiled=True)


def narrow_cols(value_rows):
    return lax.psum_scatter(value_rows, "col", scatter_dimension=1, tiled=True)


def sum_over_cols(value_rows):
    return lax.psum(value_rows, "col")


def contract_local(operand, matrix):
    return lax.dot_general(
        operand, matrix, (((1,), (0,)), ((), ())), preferred_element_type=jnp.float32
    )


def expand_local(operand, matrix):
    trailing = tuple(range(1, operand.ndim))
    return lax.dot_general(
        operand, matrix, ((trailing, trailing), ((), ())), preferred_element_type=jnp.float32
    )


def token_outer(features, grads):
    return lax.dot_general(
        features, grads, (((0,), (0,)), ((), ())), preferred_element_type=jnp.float32
    )


def contract_rows(operand, matrix):
    return contract_local(operand, lax.all_gather(matrix, "row", axis=0, tiled=True))


def expand_rows(operand, matrix):
    return expand_local(operand, lax.all_gather(matrix, "row", axis=0, tiled=True))


def split_keys(key_seq, value_seq, key_pos):
    slot_len = key_seq.shape[0]
    width = min(512, slot_len)
    count = slot_len // width
    return (
        key_seq.reshape(count, width, key_seq.shape[1], key_seq.shape[2]),
        value_seq.reshape(count, width, value_seq.shape[1], value_seq.shape[2]),
        key_pos.reshape(count, width),
    )


def block_scores(query_seq, key_block, pos_block, query_pos, length):
    scores = (
        jnp.einsum("qkgd,tkd->kgqt", query_seq, key_block, preferred_element_type=jnp.float32)
        * ATTN_MULT
    )
    allowed = (pos_block[None, :] <= query_pos[:, None]) & (pos_block[None, :] < length)
    return jnp.where(allowed, scores, MASKED)


def attend(inputs, key_pos, query_pos):
    query_seq, key_seq, value_seq, length = inputs
    key_blocks, value_blocks, pos_blocks = split_keys(key_seq, value_seq, key_pos)
    stat_shape = (query_seq.shape[1], query_seq.shape[2], query_seq.shape[0], 1)

    def gather_stats(carry, entry):
        running_max, running_sum = carry
        key_block, pos_block = entry
        scores = block_scores(query_seq, key_block, pos_block, query_pos, length)
        new_max = jnp.maximum(running_max, jnp.max(scores, axis=-1, keepdims=True))
        new_sum = running_sum * jnp.exp(running_max - new_max) + jnp.sum(
            jnp.exp(scores - new_max), axis=-1, keepdims=True
        )
        return ((new_max, new_sum), None)

    start_stats = (jnp.full(stat_shape, MASKED, jnp.float32), jnp.zeros(stat_shape, jnp.float32))
    (row_max, row_sums), unused = lax.scan(gather_stats, start_stats, (key_blocks, pos_blocks))

    def mix_values(running, entry):
        key_block, value_block, pos_block = entry
        scores = block_scores(query_seq, key_block, pos_block, query_pos, length)
        weights = jnp.exp(scores - row_max) / row_sums
        return (
            running
            + jnp.einsum(
                "kgqt,tkd->qkgd",
                weights.astype(jnp.bfloat16),
                value_block,
                preferred_element_type=jnp.float32,
            ),
            None,
        )

    start_mix = jnp.zeros(query_seq.shape, jnp.float32)
    mixed_heads, unused = lax.scan(mix_values, start_mix, (key_blocks, value_blocks, pos_blocks))
    return (mixed_heads, row_max, row_sums)


def attend_back(inputs, key_pos, query_pos):
    query_seq, key_seq, value_seq, grad_mixed, row_max, row_sums, length = inputs
    key_blocks, value_blocks, pos_blocks = split_keys(key_seq, value_seq, key_pos)

    def block_weights(key_block, value_block, pos_block):
        scores = block_scores(query_seq, key_block, pos_block, query_pos, length)
        weights = jnp.exp(scores - row_max) / row_sums
        grad_weights = jnp.einsum(
            "qkgd,tkd->kgqt", grad_mixed, value_block, preferred_element_type=jnp.float32
        )
        return (weights, grad_weights)

    def gather_centre(running, entry):
        weights, grad_weights = block_weights(*entry)
        return (running + jnp.sum(weights * grad_weights, axis=-1, keepdims=True), None)

    start_centre = jnp.zeros(row_max.shape, jnp.float32)
    centre, unused = lax.scan(gather_centre, start_centre, (key_blocks, value_blocks, pos_blocks))

    def grads_block(running, entry):
        key_block = entry[0]
        weights, grad_weights = block_weights(*entry)
        grad_scores = (weights * (grad_weights - centre)).astype(jnp.bfloat16)
        grad_query = (
            running
            + jnp.einsum(
                "kgqt,tkd->qkgd", grad_scores, key_block, preferred_element_type=jnp.float32
            )
            * ATTN_MULT
        )
        grad_key = (
            jnp.einsum("kgqt,qkgd->tkd", grad_scores, query_seq, preferred_element_type=jnp.float32)
            * ATTN_MULT
        )
        grad_value = jnp.einsum(
            "kgqt,qkgd->tkd",
            weights.astype(jnp.bfloat16),
            grad_mixed,
            preferred_element_type=jnp.float32,
        )
        return (grad_query, (grad_key, grad_value))

    start_query = jnp.zeros(query_seq.shape, jnp.float32)
    grad_query, (grad_key, grad_value) = lax.scan(
        grads_block, start_query, (key_blocks, value_blocks, pos_blocks)
    )
    return (grad_query, grad_key.reshape(key_seq.shape), grad_value.reshape(value_seq.shape))


MESH_IDS = pl.DeviceIdType.MESH
SIBLINGS = [(0, 1), (1, 0), (2, 3), (3, 2)]
OVER_X = [(0, 1), (1, 0)]
OVER_Y = [(0, 2), (2, 0), (1, 3), (3, 1)]
CROSSED = [((2 * y + c) * 2 + x, (2 * y + x) * 2 + c) for y in (0, 1) for c in (0, 1) for x in (0, 1)]


def pick_sequences(everyone, deal_order, first, count):
    slots = jnp.arange(deal_order.shape[0], dtype=jnp.int32)
    inverse = jnp.sum(jnp.where(deal_order[None, :] == slots[:, None], slots[None, :], 0), axis=1)
    return jnp.concatenate(
        [
            lax.dynamic_slice_in_dim(
                everyone, lax.dynamic_index_in_dim(inverse, first + at, keepdims=False), 1
            )
            for at in range(count)
        ]
    )


def bring_cotangent(cotangent, deal_order, first):
    everyone = lax.all_gather(cotangent, "dp", axis=0, tiled=True)
    return pick_sequences(everyone, deal_order, first, cotangent.shape[0])


def place():
    group = lax.axis_index("dp")
    core = lax.rem(group, 2)
    row = lax.axis_index("row")
    return group, core, group - core + row, row, lax.axis_index("col")


def lined(index, step, count):
    return lax.rem(index + step + count, count)


def aligned(block, size):
    return pl.ds(pl.multiple_of(block * size, size), size)


def greet(device):
    pl.semaphore_signal(
        pltpu.get_barrier_semaphore(), inc=1, device_id=device, device_id_type=MESH_IDS
    )


def remote(src, dst, sems, at, device):
    return pltpu.make_async_remote_copy(
        src_ref=src,
        dst_ref=dst,
        send_sem=sems.at[0, at],
        recv_sem=sems.at[1, at],
        device_id=device,
        device_id_type=MESH_IDS,
    )


def line_order(col, last, at):
    inner_low = jnp.where(at < 2, 1 - at, at)
    inner_high = jnp.where(at == 3, 0, jnp.where(at == 0, 2, jnp.where(at == 1, 1, 3)))
    return jnp.where(
        col == 0, at, jnp.where(col == last, last - at, jnp.where(col == 1, inner_low, inner_high))
    )


def start_kernel(
    cols, tok_ref, gain_ref, x_ref, a_ref, x_buf, a_buf, tok_sems, a_sems, local_sems
):
    group, core, mate, row, col = place()
    width = tok_ref.shape[2]
    length = x_buf.shape[0]
    sibling = (group + 1 - 2 * core, row, col)

    def line(step):
        return lined(col, step, cols)

    for step in range(1, cols):
        greet((mate, core, line(step)))
    greet(sibling)

    @pl.when(core != row)
    def _():
        greet((mate, core, col))

    pl.semaphore_wait(pltpu.get_barrier_semaphore(), cols + (core - row) * (core - row))

    def token_copy(step, into):
        return remote(
            tok_ref.at[line(step)],
            x_buf.at[:, aligned(into, width)],
            tok_sems,
            step,
            (mate, core, line(step)),
        )

    own_tokens = pltpu.make_async_copy(
        tok_ref.at[col], x_buf.at[:, aligned(col, width)], local_sems.at[0]
    )
    for step in range(1, cols):
        token_copy(step, col).start()

    @pl.when(core != row)
    def _():
        token_copy(0, col).start()

    @pl.when(core == row)
    def _():
        own_tokens.start()

    for step in range(1, cols):
        token_copy(step, line(-step)).wait_recv()

    @pl.when(core != row)
    def _():
        token_copy(0, col).wait_recv()

    @pl.when(core == row)
    def _():
        own_tokens.wait()

    keep_x = pltpu.make_async_copy(x_buf, x_ref, local_sems.at[1])
    keep_x.start()
    tall = min(64, length)

    @pl.loop(0, length // tall)
    def _(at):
        here = aligned(at, tall)
        now = x_buf[here, :].astype(jnp.float32)
        scale = lax.rsqrt(jnp.mean(now * now, axis=1, keepdims=True) + EPSILON)
        a_buf[here, :] = (now * scale * gain_ref[...]).astype(jnp.bfloat16)

    def a_copy(of_core):
        return remote(a_buf, a_ref.at[aligned(of_core, length)], a_sems, 0, sibling)

    own_a = pltpu.make_async_copy(a_buf, a_ref.at[aligned(core, length)], local_sems.at[2])
    a_copy(core).start()
    own_a.start()
    for step in range(1, cols):
        token_copy(step, col).wait_send()

    @pl.when(core != row)
    def _():
        token_copy(0, col).wait_send()

    keep_x.wait()
    own_a.wait()
    a_copy(core).wait_send()
    a_copy(1 - core).wait_recv()


def start_exchange(tokens, gain, cols):
    anywhere = pl.BlockSpec(memory_space=pl.ANY)
    seqs, length, width = tokens.shape
    full = width * cols
    return pl.pallas_call(
        functools.partial(start_kernel, cols),
        out_shape=(
            jax.ShapeDtypeStruct((length, full), tokens.dtype),
            jax.ShapeDtypeStruct((2 * length, full), tokens.dtype),
        ),
        in_specs=[anywhere, pl.BlockSpec(memory_space=pltpu.VMEM)],
        out_specs=(anywhere,) * 2,
        scratch_shapes=[
            pltpu.VMEM((length, full), tokens.dtype),
            pltpu.VMEM((length, full), tokens.dtype),
            pltpu.SemaphoreType.DMA((2, cols)),
            pltpu.SemaphoreType.DMA((2, 1)),
            pltpu.SemaphoreType.DMA((3,)),
        ],
        compiler_params=pltpu.CompilerParams(
            collective_id=1, has_side_effects=True, vmem_limit_bytes=16 << 20
        ),
        cost_estimate=pl.CostEstimate(flops=0, bytes_accessed=200 << 20, transcendentals=0),
        name="start_exchange",
    )(tokens, gain.reshape(1, full))


def gather_kernel(
    cols, q_ref, o_ref, after_ref, wq_ref, wo_ref, q_send, q_recv, q_over, o_send, o_recv, o_over, local_sems
):
    group, core, mate, row, col = place()
    last = cols - 1
    over = (group, 1 - row, col)
    greet(over)

    @pl.when(col < last)
    def _():
        greet((group, row, col + 1))

    @pl.when(col > 0)
    def _():
        greet((group, row, col - 1))

    pl.semaphore_wait(
        pltpu.get_barrier_semaphore(),
        1 + jnp.minimum(col, 1) + jnp.minimum(last - col, 1),
    )

    def moves(own, full, send, recv, over_sems):
        tall, wide = own.shape

        def block(of_row, of_col):
            return full.at[aligned(of_row, tall), aligned(of_col, wide)]

        def along(src, chunk, to, way):
            return pltpu.make_async_remote_copy(
                src_ref=src,
                dst_ref=block(row, chunk),
                send_sem=send.at[way, chunk],
                recv_sem=recv.at[chunk],
                device_id=(group, row, to),
                device_id_type=MESH_IDS,
            )

        def across(src, of_row, chunk):
            return remote(src, block(of_row, chunk), over_sems, chunk, over)

        return block, along, across

    both = (
        (q_ref, moves(q_ref, wq_ref, q_send, q_recv, q_over)),
        (o_ref, moves(o_ref, wo_ref, o_send, o_recv, o_over)),
    )
    own_copies = []
    for at, (own, (block, along, across)) in enumerate(both):

        @pl.when(col < last)
        def _():
            along(own, col, col + 1, 0).start()

        @pl.when(col > 0)
        def _():
            along(own, col, col - 1, 1).start()

        across(own, row, col).start()
        own_copies.append(pltpu.make_async_copy(own, block(row, col), local_sems.at[at]))
        own_copies[-1].start()
    for at in range(1, cols):
        chunk = line_order(col, last, at)
        for own, (block, along, across) in both:
            along(own, chunk, col, 0).wait_recv()

            @pl.when((chunk < col) & (col < last))
            def _():
                along(block(row, chunk), chunk, col + 1, 0).start()

            @pl.when((chunk > col) & (col > 0))
            def _():
                along(block(row, chunk), chunk, col - 1, 1).start()

            across(block(row, chunk), row, chunk).start()
    for copy in own_copies:
        copy.wait()
    for own, (block, along, across) in both:
        for chunk in range(cols):

            @pl.when((col >= chunk) & (col < last))
            def _():
                along(own, chunk, col + 1, 0).wait_send()

            @pl.when((col <= chunk) & (col > 0))
            def _():
                along(own, chunk, col - 1, 1).wait_send()

            across(own, row, chunk).wait_send()
            across(own, 1 - row, chunk).wait_recv()


def gather_weights(own_q, own_o, after, rows, cols):
    anywhere = pl.BlockSpec(memory_space=pl.ANY)

    def whole(own):
        return jax.ShapeDtypeStruct((own.shape[0] * rows, own.shape[1] * cols), own.dtype)

    return pl.pallas_call(
        functools.partial(gather_kernel, cols),
        out_shape=(whole(own_q), whole(own_o)),
        in_specs=[anywhere] * 3,
        out_specs=(anywhere,) * 2,
        scratch_shapes=[
            pltpu.SemaphoreType.DMA((2, cols)),
            pltpu.SemaphoreType.DMA((cols,)),
            pltpu.SemaphoreType.DMA((2, cols)),
        ]
        * 2
        + [pltpu.SemaphoreType.DMA((2,))],
        compiler_params=pltpu.CompilerParams(collective_id=4, has_side_effects=True),
        cost_estimate=pl.CostEstimate(flops=0, bytes_accessed=300 << 20, transcendentals=0),
        name="gather_weights",
    )(own_q, own_o, after)


def half_turn(wide):
    lanes = wide.shape[1]
    half = HEAD_SIZE // 2
    lane = lax.broadcasted_iota(jnp.int32, wide.shape, 1)
    return jnp.where(
        lax.rem(lane, HEAD_SIZE) < half,
        pltpu.roll(wide, lanes - half, 1),
        pltpu.roll(wide, half, 1),
    )


def both_heads(pair):
    lane = lax.broadcasted_iota(jnp.int32, pair.shape, 1)
    turned = pltpu.roll(pair, HEAD_SIZE, 1)
    low = lane < HEAD_SIZE
    return jnp.where(low, pair, turned), jnp.where(low, turned, pair)


def keep_head(pair, side):
    lane = lax.broadcasted_iota(jnp.int32, pair.shape, 1)
    mine = lane < HEAD_SIZE if side == 0 else lane >= HEAD_SIZE
    return jnp.where(mine, pair, jnp.zeros_like(pair))


def dot_nn(a, b):
    return lax.dot_general(a, b, (((1,), (0,)), ((), ())), preferred_element_type=jnp.float32)


def dot_nt(a, b):
    return lax.dot_general(a, b, (((1,), (1,)), ((), ())), preferred_element_type=jnp.float32)


def dot_tn(a, b):
    return lax.dot_general(a, b, (((0,), (0,)), ((), ())), preferred_element_type=jnp.float32)


PAIR = 2 * HEAD_SIZE


def attend_kernel(block, len_ref, a_ref, w_ref, cos_ref, sin_ref, qkv_ref, z_ref, q_all, k_two, v_two):
    rows = a_ref.shape[0]
    heads = q_all.shape[0]
    length = len_ref[0]

    @pl.loop(0, rows // block)
    def _(at):
        here = pl.ds(pl.multiple_of(at * block, block), block)
        lin = dot_nn(a_ref[here, :], w_ref[...])
        for part in range(heads // 2 + 1):
            lanes = slice(part * PAIR, (part + 1) * PAIR)
            now = lin[:, lanes]
            table = slice(0, PAIR) if part < heads // 2 else slice(PAIR, 2 * PAIR)
            now = now * cos_ref[here, table] + half_turn(now) * sin_ref[here, table]
            qkv_ref[here, lanes] = now.astype(jnp.bfloat16)
            if part < heads // 2:
                for side in range(2):
                    q_all[2 * part + side, here, :] = keep_head(now * ATTN_MULT, side).astype(
                        jnp.bfloat16
                    )
            else:
                keys, values = both_heads(now)
                k_two[here, :] = keys.astype(jnp.bfloat16)
                v_two[here, :] = values.astype(jnp.bfloat16)

    for at in range(rows // block):
        here = slice(at * block, (at + 1) * block)
        upto = (at + 1) * block
        row = lax.broadcasted_iota(jnp.int32, (block, upto), 0) + at * block
        key = lax.broadcasted_iota(jnp.int32, (block, upto), 1)
        allowed = key < jnp.minimum(row + 1, length)

        def one_head(head):
            scores = dot_nt(q_all[head, here, :], k_two[:upto, :])
            scores = jnp.where(allowed, scores, MASKED)
            top = jnp.max(scores, axis=1, keepdims=True)
            power = jnp.exp(scores - top)
            total = jnp.sum(power, axis=1, keepdims=True)
            return dot_nn(power.astype(jnp.bfloat16), v_two[:upto, :]) / total

        for pair in range(heads // 2):
            low = one_head(2 * pair)
            high = one_head(2 * pair + 1)
            lane = lax.broadcasted_iota(jnp.int32, low.shape, 1)
            z_ref[here, pair * PAIR : (pair + 1) * PAIR] = jnp.where(
                lane < HEAD_SIZE, low, high
            ).astype(jnp.bfloat16)


def attend_fast(length, inputs, weights, cosines, sines, groups):
    rows, depth = inputs.shape
    wide = weights.shape[1] // groups
    heads = (wide - PAIR) // HEAD_SIZE
    block = min(256, rows)
    return pl.pallas_call(
        functools.partial(attend_kernel, block),
        grid=(groups,),
        out_shape=(
            jax.ShapeDtypeStruct((rows, groups * wide), jnp.bfloat16),
            jax.ShapeDtypeStruct((rows, groups * heads * HEAD_SIZE), jnp.bfloat16),
        ),
        in_specs=[
            pl.BlockSpec(memory_space=pltpu.SMEM),
            pl.BlockSpec((rows, depth), lambda g: (0, 0)),
            pl.BlockSpec((depth, wide), lambda g: (0, g)),
            pl.BlockSpec((rows, 2 * PAIR), lambda g: (0, 0)),
            pl.BlockSpec((rows, 2 * PAIR), lambda g: (0, 0)),
        ],
        out_specs=(
            pl.BlockSpec((rows, wide), lambda g: (0, g)),
            pl.BlockSpec((rows, heads * HEAD_SIZE), lambda g: (0, g)),
        ),
        scratch_shapes=[
            pltpu.VMEM((heads, rows, PAIR), jnp.bfloat16),
            pltpu.VMEM((rows, PAIR), jnp.bfloat16),
            pltpu.VMEM((rows, PAIR), jnp.bfloat16),
        ],
        compiler_params=pltpu.CompilerParams(vmem_limit_bytes=48 << 20),
        cost_estimate=pl.CostEstimate(
            flops=2 * rows * depth * wide * groups + 2 * groups * heads * rows * rows * 128,
            bytes_accessed=2 * (rows * depth + depth * wide * groups + rows * wide * groups),
            transcendentals=groups * heads * rows * rows // 2,
        ),
        name="attend",
    )(length, inputs, weights, cosines, sines)


def attend_back_kernel(
    block, len_ref, qkv_ref, dz_ref, cos_ref, sin_ref, out_ref, q_all, z_all, k_two, v_two, k_acc, v_acc
):
    rows = qkv_ref.shape[0]
    heads = q_all.shape[0]
    length = len_ref[0]

    @pl.loop(0, rows // block)
    def _(at):
        here = pl.ds(pl.multiple_of(at * block, block), block)
        for part in range(heads // 2):
            lanes = slice(part * PAIR, (part + 1) * PAIR)
            queries = qkv_ref[here, lanes].astype(jnp.float32) * ATTN_MULT
            mixed = dz_ref[here, lanes].astype(jnp.float32)
            for side in range(2):
                q_all[2 * part + side, here, :] = keep_head(queries, side).astype(jnp.bfloat16)
                z_all[2 * part + side, here, :] = keep_head(mixed, side).astype(jnp.bfloat16)
        keys, values = both_heads(qkv_ref[here, heads * HEAD_SIZE :].astype(jnp.float32))
        k_two[here, :] = keys.astype(jnp.bfloat16)
        v_two[here, :] = values.astype(jnp.bfloat16)
        k_acc[here, :] = jnp.zeros((block, PAIR), jnp.float32)
        v_acc[here, :] = jnp.zeros((block, PAIR), jnp.float32)

    def turn_back(now, here, table):
        return (now * cos_ref[here, table] - half_turn(now) * sin_ref[here, table]).astype(
            jnp.bfloat16
        )

    for at in range(rows // block):
        here = slice(at * block, (at + 1) * block)
        upto = (at + 1) * block
        key = lax.broadcasted_iota(jnp.int32, (upto, block), 0)
        query = lax.broadcasted_iota(jnp.int32, (upto, block), 1) + at * block
        allowed = key < jnp.minimum(query + 1, length)

        def one_head(head):
            queries, mixed = q_all[head, here, :], z_all[head, here, :]
            scores = jnp.where(allowed, dot_nt(k_two[:upto, :], queries), MASKED)
            power = jnp.exp(scores - jnp.max(scores, axis=0, keepdims=True))
            weights = power * (1.0 / jnp.sum(power, axis=0, keepdims=True))
            back = dot_nt(v_two[:upto, :], mixed)
            centre = jnp.sum(weights * back, axis=0, keepdims=True)
            slope = (weights * (back - centre)).astype(jnp.bfloat16)
            k_acc[:upto, :] += dot_nn(slope, queries)
            v_acc[:upto, :] += dot_nn(weights.astype(jnp.bfloat16), mixed)
            return dot_tn(slope, k_two[:upto, :]) * ATTN_MULT

        for pair in range(heads // 2):
            low = one_head(2 * pair)
            high = one_head(2 * pair + 1)
            lane = lax.broadcasted_iota(jnp.int32, low.shape, 1)
            lanes = slice(pair * PAIR, (pair + 1) * PAIR)
            out_ref[here, lanes] = turn_back(
                jnp.where(lane < HEAD_SIZE, low, high), here, slice(0, PAIR)
            )

    @pl.loop(0, rows // block)
    def _(at):
        here = pl.ds(pl.multiple_of(at * block, block), block)
        keys, values = k_acc[here, :], v_acc[here, :]
        keys = keys + pltpu.roll(keys, HEAD_SIZE, 1)
        values = values + pltpu.roll(values, HEAD_SIZE, 1)
        lane = lax.broadcasted_iota(jnp.int32, keys.shape, 1)
        lanes = slice(heads * HEAD_SIZE, heads * HEAD_SIZE + PAIR)
        out_ref[here, lanes] = turn_back(
            jnp.where(lane < HEAD_SIZE, keys, values), here, slice(PAIR, 2 * PAIR)
        )


def attend_back_fast(length, projected, grad_mixed, cosines, sines, groups):
    rows = projected.shape[0]
    wide = projected.shape[1] // groups
    heads = (wide - PAIR) // HEAD_SIZE
    block = min(256, rows)
    return pl.pallas_call(
        functools.partial(attend_back_kernel, block),
        grid=(groups,),
        out_shape=jax.ShapeDtypeStruct((rows, groups * wide), jnp.bfloat16),
        in_specs=[
            pl.BlockSpec(memory_space=pltpu.SMEM),
            pl.BlockSpec((rows, wide), lambda g: (0, g)),
            pl.BlockSpec((rows, heads * HEAD_SIZE), lambda g: (0, g)),
            pl.BlockSpec((rows, 2 * PAIR), lambda g: (0, 0)),
            pl.BlockSpec((rows, 2 * PAIR), lambda g: (0, 0)),
        ],
        out_specs=pl.BlockSpec((rows, wide), lambda g: (0, g)),
        scratch_shapes=[
            pltpu.VMEM((heads, rows, PAIR), jnp.bfloat16),
            pltpu.VMEM((heads, rows, PAIR), jnp.bfloat16),
            pltpu.VMEM((rows, PAIR), jnp.bfloat16),
            pltpu.VMEM((rows, PAIR), jnp.bfloat16),
            pltpu.VMEM((rows, PAIR), jnp.float32),
            pltpu.VMEM((rows, PAIR), jnp.float32),
        ],
        compiler_params=pltpu.CompilerParams(vmem_limit_bytes=48 << 20),
        cost_estimate=pl.CostEstimate(
            flops=5 * groups * heads * rows * rows * 128,
            bytes_accessed=2 * (2 * rows * wide * groups + rows * heads * HEAD_SIZE * groups),
            transcendentals=groups * heads * rows * rows // 2,
        ),
        name="attend_back",
    )(length, projected, grad_mixed, cosines, sines)


def ffn_kernel(
    cols,
    own_ref,
    resid_ref,
    grad_ref,
    wg_own,
    wu_own,
    wd_own,
    wg_far,
    wu_far,
    wd_far,
    wg_sib,
    wu_sib,
    wd_sib,
    b_all,
    u_all,
    dgu_all,
    mlp_all,
    back_all,
    land_ref,
    a_keep,
    a_send,
    b_keep,
    b_send,
    wg,
    wu,
    wd,
    b_buf,
    g_buf,
    u_buf,
    dg_buf,
    du_buf,
    mlp_buf,
    back_buf,
    turn_buf,
    w_sems,
    ag_send,
    ag_recv,
    back_send,
    back_recv,
    pair_sems,
    lane_sems,
    io_sems,
):
    group, core, mate, row, col = place()
    sibling = (group + 1 - 2 * core, row, col)
    last = cols - 1
    depth = wg_own.shape[0]
    half = depth // 2
    units = wg_own.shape[1]
    tile = min(512, units)

    barrier = pltpu.get_barrier_semaphore()
    for step in range(1, cols):
        pl.semaphore_signal(
            barrier,
            inc=1,
            device_id=(group, row, lax.rem(col + step, cols)),
            device_id_type=MESH_IDS,
        )
    greet(sibling)
    pl.semaphore_wait(barrier, cols)

    def pass_on(src, at, to, way):
        return pltpu.make_async_remote_copy(
            src_ref=src,
            dst_ref=b_all.at[at],
            send_sem=ag_send.at[way, at],
            recv_sem=ag_recv.at[at],
            device_id=(group, row, to),
            device_id_type=MESH_IDS,
        )

    @pl.when(col < last)
    def _():
        pass_on(own_ref, col, col + 1, 0).start()

    @pl.when(col > 0)
    def _():
        pass_on(own_ref, col, col - 1, 1).start()

    def rows_at(first, size):
        return pl.ds(pl.multiple_of(first, half), size)

    own_copy = pltpu.make_async_copy(own_ref, b_all.at[col], io_sems.at[0])
    own_copy.start()
    load_resid = pltpu.make_async_copy(resid_ref, mlp_buf, io_sems.at[8])
    load_resid.start()
    far = (1 - row) * depth
    loads = []
    for at, (full, mine, across, shared) in enumerate(
        ((wg, wg_own, wg_far, wg_sib), (wu, wu_own, wu_far, wu_sib), (wd, wd_own, wd_far, wd_sib))
    ):
        loads += [
            pltpu.make_async_copy(mine, full.at[rows_at(row * depth, depth)], w_sems.at[3 * at]),
            pltpu.make_async_copy(
                across, full.at[rows_at(far + core * half, half)], w_sems.at[3 * at + 1]
            ),
            pltpu.make_async_copy(
                shared, full.at[rows_at(far + (1 - core) * half, half)], w_sems.at[3 * at + 2]
            ),
        ]
    for load in loads:
        load.start()
    own_copy.wait()
    for load in loads:
        load.wait()

    def order(at):
        return line_order(col, last, at)

    def arrive(chunk):
        pass_on(b_all.at[chunk], chunk, col, 0).wait_recv()

        @pl.when((chunk < col) & (col < last))
        def _():
            pass_on(b_all.at[chunk], chunk, col + 1, 0).start()

        @pl.when((chunk > col) & (col > 0))
        def _():
            pass_on(b_all.at[chunk], chunk, col - 1, 1).start()

    def outputs(chunk):
        return (
            pltpu.make_async_copy(u_buf, u_all.at[chunk], io_sems.at[1]),
            pltpu.make_async_copy(dg_buf, dgu_all.at[chunk, :, 0:units], io_sems.at[2]),
            pltpu.make_async_copy(du_buf, dgu_all.at[chunk, :, units : 2 * units], io_sems.at[3]),
        )

    def mlp_out(chunk):
        return pltpu.make_async_copy(mlp_buf, mlp_all.at[chunk], io_sems.at[4])

    def back_out(at, chunk):
        return pltpu.make_async_remote_copy(
            src_ref=back_buf.at[slot_of(at)],
            dst_ref=back_all.at[col],
            send_sem=back_send.at[at],
            recv_sem=back_recv.at[col],
            device_id=(group, row, chunk),
            device_id_type=MESH_IDS,
        )

    def slot_of(at):
        return lax.rem(at, cols - 1)

    own_back = pltpu.make_async_copy(back_buf.at[0], back_all.at[col], io_sems.at[5])
    at_end = (col == 0) | (col == last)

    def one_chunk(at, unused):
        chunk = order(at)

        @pl.when(at_end & (at > 0))
        def _():
            arrive(order(at))

        @pl.when(jnp.logical_not(at_end) & (at == 1))
        def _():
            arrive(order(1))
            arrive(order(2))

        @pl.when(jnp.logical_not(at_end) & (at == 3))
        def _():
            arrive(order(3))

        load_b = pltpu.make_async_copy(b_all.at[chunk], b_buf, io_sems.at[6])
        load_g = pltpu.make_async_copy(grad_ref.at[chunk], g_buf, io_sems.at[7])
        load_b.start()
        load_g.start()

        @pl.when(at > 0)
        def _():
            for copy in outputs(order(at - 1)):
                copy.wait()

        load_b.wait()
        load_g.wait()

        @pl.loop(0, units // tile)
        def _(step):
            lanes = pl.ds(pl.multiple_of(step * tile, tile), tile)
            gate = dot_nn(b_buf[...], wg[:, lanes])
            upward = dot_nn(b_buf[...], wu[:, lanes])
            back = RES_MULT * dot_nn(g_buf[...], wd[:, lanes])
            opened = 1.0 / (1.0 + jnp.exp(-gate))
            silu = gate * opened
            u_buf[:, lanes] = (silu * upward).astype(jnp.bfloat16)
            slope = opened * (1.0 + gate * (1.0 - opened))
            dg_buf[:, lanes] = (back * upward * slope).astype(jnp.bfloat16)
            du_buf[:, lanes] = (back * silu).astype(jnp.bfloat16)

        for copy in outputs(chunk):
            copy.start()

        @pl.when(at > 0)
        def _():
            mlp_out(order(at - 1)).wait()

        @pl.when(at == 0)
        def _():
            load_resid.wait()

        @pl.when(at == last)
        def _():
            own_back.wait()

        @pl.loop(0, 2 * depth // tile)
        def _(step):
            here = pl.ds(pl.multiple_of(step * tile, tile), tile)
            back = dot_nt(dg_buf[...], wg[here, :]) + dot_nt(du_buf[...], wu[here, :])
            back_buf[slot_of(at), :, here] = back.astype(jnp.bfloat16)
            added = jnp.where(at == 0, mlp_buf[:, here].astype(jnp.float32), 0.0)
            mlp_buf[:, here] = (added + RES_MULT * dot_nt(u_buf[...], wd[here, :])).astype(
                jnp.bfloat16
            )

        mlp_out(chunk).start()

        @pl.when(at == 0)
        def _():
            own_back.start()

        @pl.when(at > 0)
        def _():
            back_out(at, chunk).start()

        return unused

    lax.fori_loop(0, cols, one_chunk, 0)
    for copy in outputs(order(last)):
        copy.wait()
    mlp_out(order(last)).wait()

    rows = b_buf.shape[0]
    loads = []
    for chunk in range(cols):
        here = slice(chunk * rows, (chunk + 1) * rows)
        loads += [
            pltpu.make_async_copy(
                dgu_all.at[chunk, :, 0:units], wg.at[here], w_sems.at[chunk]
            ),
            pltpu.make_async_copy(
                dgu_all.at[chunk, :, units : 2 * units], wu.at[here], w_sems.at[cols + chunk]
            ),
            pltpu.make_async_copy(u_all.at[chunk], wd.at[here], w_sems.at[2 * cols + chunk]),
        ]
    for load in loads:
        load.start()
    for load in loads:
        load.wait()

    buffers = (dg_buf, du_buf, u_buf)

    def to_sibling(at, part):
        return pltpu.make_async_remote_copy(
            src_ref=buffers[part],
            dst_ref=land_ref.at[at, part],
            send_sem=pair_sems.at[0, at, part],
            recv_sem=pair_sems.at[1, at, part],
            device_id=sibling,
            device_id_type=MESH_IDS,
        )

    def landed(at, part):
        return pltpu.make_async_copy(land_ref.at[at, part], buffers[part], io_sems.at[5 + part])

    halfway = units // 2
    small = rows // 2
    mine, others = aligned(row, small), aligned(1 - row, small)

    def x_lane(high):
        return (
            pltpu.make_async_copy(
                dg_buf.at[mine], a_keep.at[high, :, 0:units], lane_sems.at[0]
            ),
            pltpu.make_async_copy(
                dg_buf.at[others], a_send.at[high, :, 0:units], lane_sems.at[1]
            ),
            pltpu.make_async_copy(
                u_buf.at[mine, 0:halfway],
                a_keep.at[high, :, units : units + halfway],
                lane_sems.at[2],
            ),
            pltpu.make_async_copy(
                u_buf.at[others, 0:halfway],
                a_send.at[high, :, units : units + halfway],
                lane_sems.at[3],
            ),
        )

    def y_lane(target):
        copies = []
        for side in range(2):
            here = slice(side * small, (side + 1) * small)
            copies += [
                pltpu.make_async_copy(
                    du_buf.at[here], target.at[side, :, 0:units], lane_sems.at[4 + 2 * side]
                ),
                pltpu.make_async_copy(
                    u_buf.at[here, halfway:units],
                    target.at[side, :, units : units + halfway],
                    lane_sems.at[5 + 2 * side],
                ),
            ]
        return copies

    def put_results(high, act):
        for copy in x_lane(high):
            act(copy)

        @pl.when(high == (group - core) // 2)
        def _():
            for copy in y_lane(b_keep):
                act(copy)

        @pl.when(high != (group - core) // 2)
        def _():
            for copy in y_lane(b_send):
                act(copy)

    def start_it(copy):
        copy.start()

    def wait_for(copy):
        copy.wait()

    def turned(source, into, at):
        load = pltpu.make_async_copy(source.at[:, :, aligned(at, rows)], turn_buf, io_sems.at[4])
        load.start()
        load.wait()
        for chunk in range(cols):
            into[:, chunk * rows : (chunk + 1) * rows] = turn_buf[chunk].T

    parts = range(3)

    def one_block(at, unused):
        high = lax.rem(at, 2)
        is_own = at >= 2
        block = 2 * high + jnp.where(is_own, core, 1 - core)
        turned(b_all, b_buf, block)
        turned(grad_ref, g_buf, block)

        @pl.when((at == 1) | (at == 2))
        def _():
            for part in parts:
                to_sibling(at - 1, part).wait_send()

        @pl.when(at == 3)
        def _():
            put_results(0, wait_for)

        @pl.when(is_own)
        def _():
            for part in parts:
                to_sibling(high, part).wait_recv()
                landed(high, part).start()
            for part in parts:
                landed(high, part).wait()

        @pl.loop(0, units // tile)
        def _(step):
            lanes = aligned(step, tile)

            def put(buffer, value):
                other = jnp.where(is_own, buffer[:, lanes].astype(jnp.float32), 0.0)
                buffer[:, lanes] = (other + value).astype(jnp.bfloat16)

            put(dg_buf, dot_nn(b_buf[...], wg[:, lanes]))
            put(du_buf, dot_nn(b_buf[...], wu[:, lanes]))
            put(u_buf, RES_MULT * dot_nn(g_buf[...], wd[:, lanes]))

        @pl.when(jnp.logical_not(is_own))
        def _():
            for part in parts:
                to_sibling(at, part).start()

        @pl.when(is_own)
        def _():
            put_results(high, start_it)

        return unused

    lax.fori_loop(0, 4, one_block, 0)
    put_results(1, wait_for)
    for at in range(1, cols):
        back_out(at, order(at)).wait_send()
        source = lax.rem(col + at, cols)
        pltpu.make_async_remote_copy(
            src_ref=back_buf.at[slot_of(at)],
            dst_ref=back_all.at[source],
            send_sem=back_send.at[at],
            recv_sem=back_recv.at[source],
            device_id=(group, row, source),
            device_id_type=MESH_IDS,
        ).wait_recv()
    for chunk in range(cols):

        @pl.when((col >= chunk) & (col < last))
        def _():
            pass_on(own_ref, chunk, col + 1, 0).wait_send()

        @pl.when((col <= chunk) & (col > 0))
        def _():
            pass_on(own_ref, chunk, col - 1, 1).wait_send()


def feed_forward(own_input, resid, grad_rows, weights, cols):
    rows, width = own_input.shape
    units = weights[0].shape[1]
    anywhere = pl.BlockSpec(memory_space=pl.ANY)
    bf16 = jnp.bfloat16
    return pl.pallas_call(
        functools.partial(ffn_kernel, cols),
        out_shape=(
            jax.ShapeDtypeStruct((cols, rows, width), bf16),
            jax.ShapeDtypeStruct((cols, rows, units), bf16),
            jax.ShapeDtypeStruct((cols, rows, 2 * units), bf16),
            jax.ShapeDtypeStruct((cols, rows, width), bf16),
            jax.ShapeDtypeStruct((cols, rows, width), bf16),
            jax.ShapeDtypeStruct((2, 3, rows, units), bf16),
        )
        + (jax.ShapeDtypeStruct((2, rows // 2, units + units // 2), bf16),) * 4,
        in_specs=[anywhere] * 12,
        out_specs=(anywhere,) * 10,
        scratch_shapes=[
            pltpu.VMEM((width, units), bf16),
            pltpu.VMEM((width, units), bf16),
            pltpu.VMEM((width, units), bf16),
            pltpu.VMEM((rows, width), bf16),
            pltpu.VMEM((rows, width), bf16),
            pltpu.VMEM((rows, units), bf16),
            pltpu.VMEM((rows, units), bf16),
            pltpu.VMEM((rows, units), bf16),
            pltpu.VMEM((rows, width), bf16),
            pltpu.VMEM((cols - 1, rows, width), bf16),
            pltpu.VMEM((cols, rows, rows), bf16),
            pltpu.SemaphoreType.DMA((12,)),
            pltpu.SemaphoreType.DMA((2, cols)),
            pltpu.SemaphoreType.DMA((cols,)),
            pltpu.SemaphoreType.DMA((cols,)),
            pltpu.SemaphoreType.DMA((cols,)),
            pltpu.SemaphoreType.DMA((2, 2, 3)),
            pltpu.SemaphoreType.DMA((8,)),
            pltpu.SemaphoreType.DMA((9,)),
        ],
        compiler_params=pltpu.CompilerParams(
            collective_id=2, has_side_effects=True, vmem_limit_bytes=60 << 20
        ),
        cost_estimate=pl.CostEstimate(
            flops=18 * cols * rows * width * units,
            bytes_accessed=800 << 20,
            transcendentals=cols * rows * units,
        ),
        name="feed_forward",
    )(own_input, resid, grad_rows, *weights)


def finish_kernel(
    cols,
    ig_ref,
    gq_ref,
    go_ref,
    gain_ref,
    out_ref,
    gin_ref,
    crossed_ref,
    sq_ref,
    so_ref,
    gsum_ref,
    q_keep,
    q_sib,
    q_a1,
    q_a2,
    q_b1,
    q_b2,
    q_z,
    o_keep,
    o_sib,
    o_a1,
    o_a2,
    o_b1,
    o_b2,
    o_z,
    gain_now,
    gain_in,
    ig_sems,
    gain_sems,
    q_sems,
    o_sems,
    qz_sems,
    oz_sems,
    cross_sems,
    local_sems,
):
    group, core, mate, row, col = place()
    pair = group - core
    high = pair // 2
    sibling = (pair + 1 - core, row, col)
    over_x = (group, 1 - row, col)
    over_y = (2 * (1 - high) + core, row, col)
    width = gin_ref.shape[2]

    def line(step):
        return lax.rem(col + step + cols, cols)

    barrier = pltpu.get_barrier_semaphore()

    def greet(device):
        pl.semaphore_signal(barrier, inc=1, device_id=device, device_id_type=MESH_IDS)

    greet(sibling)
    greet(over_x)
    greet(over_y)
    for step in range(1, cols):
        greet((mate, core, line(step)))
        greet((group, row, line(step)))

    @pl.when(core != row)
    def _():
        greet((mate, core, col))

    pl.semaphore_wait(barrier, 2 * cols + 1 + (core - row) * (core - row))

    def remote(src, dst, sems, at, device):
        return pltpu.make_async_remote_copy(
            src_ref=src,
            dst_ref=dst,
            send_sem=sems.at[0, at],
            recv_sem=sems.at[1, at],
            device_id=device,
            device_id_type=MESH_IDS,
        )

    def lanes(block, size):
        return pl.ds(pl.multiple_of(block * size, size), size)

    matrices = (
        (gq_ref, sq_ref, q_keep, q_sib, q_a1, q_a2, q_b1, q_b2, q_z, q_sems, qz_sems),
        (go_ref, so_ref, o_keep, o_sib, o_a1, o_a2, o_b1, o_b2, o_z, o_sems, oz_sems),
    )

    def moves(m):
        grads, out, keep, sib, a1, a2, b1, b2, zb, sems, z_sems = matrices[m]
        return dict(
            s0=remote(grads.at[:, 1 - core], sib, sems, 0, sibling),
            a1=remote(grads.at[:, core, 1 - row], a1, sems, 1, over_x),
            a2=remote(keep.at[1 - high, row], a2, sems, 2, over_y),
            b1=remote(sib.at[1 - high], b1, sems, 3, over_y),
            b2=remote(sib.at[high, 1 - row], b2, sems, 4, over_x),
            own=pltpu.make_async_copy(grads.at[:, core], keep, local_sems.at[m]),
        )

    copies = (moves(0), moves(1))

    def rows_plus(into, more):
        rows = into.shape[0]
        step = min(32, rows)

        @pl.loop(0, rows // step)
        def _(at):
            here = pl.ds(pl.multiple_of(at * step, step), step)
            into[here, :] = (
                into[here, :].astype(jnp.float32) + more[here, :].astype(jnp.float32)
            ).astype(into.dtype)

    def token_copy(step, at):
        return remote(
            ig_ref.at[:, lanes(line(step), width)],
            gin_ref.at[at],
            ig_sems,
            step,
            (mate, core, line(step)),
        )

    own_tokens = pltpu.make_async_copy(
        ig_ref.at[:, lanes(col, width)], gin_ref.at[col], local_sems.at[2]
    )

    cross = remote(out_ref, crossed_ref, cross_sems, 0, (mate, core, col))
    stay = pltpu.make_async_copy(out_ref, crossed_ref, local_sems.at[4])
    for m in range(2):
        copies[m]["s0"].start()
        copies[m]["a1"].start()
        copies[m]["own"].start()
    for step in range(1, cols):
        token_copy(step, col).start()

    @pl.when(core != row)
    def _():
        token_copy(0, col).start()
        cross.start()

    @pl.when(core == row)
    def _():
        own_tokens.start()
        stay.start()

    gain_load = pltpu.make_async_copy(gain_ref, gain_now.at[0], local_sems.at[3])
    gain_load.start()
    gain_load.wait()
    near = (
        sibling,
        over_x,
        over_y,
        (group, row, col + 1 - 2 * lax.rem(col, 2)),
        (group, row, lax.rem(col + cols // 2, cols)),
    )

    def gain_round(at):
        exchange = remote(gain_now.at[at], gain_in.at[at], gain_sems, at, near[at])
        exchange.start()
        exchange.wait()
        gain_now[at + 1] = gain_now[at] + gain_in[at]

    gain_round(0)
    for m in range(2):
        copies[m]["s0"].wait()
        copies[m]["b1"].start()
    gain_round(1)
    for m in range(2):
        grads, out, keep, sib, a1, a2, b1, b2, zb, sems, z_sems = matrices[m]
        copies[m]["own"].wait()
        copies[m]["a1"].wait()
        rows_plus(keep.at[1 - high, row], a1.at[1 - high])
        copies[m]["a2"].start()
    for m in range(2):
        grads, out, keep, sib, a1, a2, b1, b2, zb, sems, z_sems = matrices[m]
        copies[m]["b1"].wait()
        rows_plus(sib.at[high, 1 - row], b1.at[1 - row])
        copies[m]["b2"].start()
    gain_round(2)
    for m in range(2):
        grads, out, keep, sib, a1, a2, b1, b2, zb, sems, z_sems = matrices[m]
        rows_plus(keep.at[high, row], a1.at[high])
        rows_plus(sib.at[high, row], b1.at[row])

    def z_moves(m, side, source):
        grads, out, keep, sib, a1, a2, b1, b2, zb, sems, z_sems = matrices[m]
        held = (keep, sib)[side]
        wide = zb.shape[3]
        return [
            pltpu.make_async_remote_copy(
                src_ref=held.at[high, row, :, lanes(line(step), wide)],
                dst_ref=zb.at[side, line(source(step))],
                send_sem=z_sems.at[0, side, step],
                recv_sem=z_sems.at[1, side, step],
                device_id=(group, row, line(step)),
                device_id_type=MESH_IDS,
            )
            for step in range(1, cols)
        ]

    for side, last_copy in ((0, "a2"), (1, "b2")):
        for m in range(2):
            grads, out, keep, sib, a1, a2, b1, b2, zb, sems, z_sems = matrices[m]
            copies[m][last_copy].wait()
            rows_plus((keep, sib)[side].at[high, row], (a2, b2)[side])
            for copy in z_moves(m, side, lambda step: 0):
                copy.start()
    gain_round(3)
    gain_round(4)
    gsum_ref[...] = gain_now[5]
    for side in range(2):
        for m in range(2):
            grads, out, keep, sib, a1, a2, b1, b2, zb, sems, z_sems = matrices[m]
            for copy in z_moves(m, side, lambda step: 0):
                copy.wait_send()
            for copy in z_moves(m, side, lambda step: -step):
                copy.wait_recv()
            held = (keep, sib)[side]
            wide = zb.shape[3]
            at_core = core if side == 0 else 1 - core
            rows = zb.shape[2]
            tall = min(32, rows)

            @pl.loop(0, rows // tall)
            def _(at):
                here = pl.ds(pl.multiple_of(at * tall, tall), tall)
                total = held[high, row, here, lanes(col, wide)].astype(jnp.float32)
                for step in range(1, cols):
                    total = total + zb[side, line(-step), here, :].astype(jnp.float32)
                out[at_core, here, :] = total

    for step in range(1, cols):
        token_copy(step, line(-step)).wait_recv()
        token_copy(step, col).wait_send()

    @pl.when(core != row)
    def _():
        token_copy(0, col).wait_recv()
        token_copy(0, col).wait_send()
        cross.wait()

    @pl.when(core == row)
    def _():
        own_tokens.wait()
        stay.wait()


def finish(input_grad, grad_q, grad_o, gains, output, cols):
    anywhere = pl.BlockSpec(memory_space=pl.ANY)
    in_vmem = pl.BlockSpec(memory_space=pltpu.VMEM)
    bf16, f32 = jnp.bfloat16, jnp.float32
    length, full = input_grad.shape
    rows = grad_q.shape[0] // 8

    def buffers(wide):
        return [
            pltpu.VMEM((2, 2, rows, wide), bf16),
            pltpu.VMEM((2, 2, rows, wide), bf16),
            pltpu.VMEM((2, rows, wide), bf16),
            pltpu.VMEM((rows, wide), bf16),
            pltpu.VMEM((2, rows, wide), bf16),
            pltpu.VMEM((rows, wide), bf16),
            pltpu.VMEM((2, cols, rows, wide // cols), bf16),
        ]

    wide_q, wide_o = grad_q.shape[1], grad_o.shape[1]
    return pl.pallas_call(
        functools.partial(finish_kernel, cols),
        out_shape=(
            jax.ShapeDtypeStruct((cols, length, full // cols), bf16),
            jax.ShapeDtypeStruct(output.shape, bf16),
            jax.ShapeDtypeStruct((2, rows, wide_q // cols), f32),
            jax.ShapeDtypeStruct((2, rows, wide_o // cols), f32),
            jax.ShapeDtypeStruct(gains.shape, f32),
        ),
        in_specs=[anywhere] * 5,
        out_specs=(anywhere, anywhere, in_vmem, in_vmem, in_vmem),
        scratch_shapes=buffers(wide_q)
        + buffers(wide_o)
        + [
            pltpu.VMEM((6,) + gains.shape, f32),
            pltpu.VMEM((5,) + gains.shape, f32),
            pltpu.SemaphoreType.DMA((2, cols)),
            pltpu.SemaphoreType.DMA((2, 5)),
            pltpu.SemaphoreType.DMA((2, 5)),
            pltpu.SemaphoreType.DMA((2, 5)),
            pltpu.SemaphoreType.DMA((2, 2, cols)),
            pltpu.SemaphoreType.DMA((2, 2, cols)),
            pltpu.SemaphoreType.DMA((2, 1)),
            pltpu.SemaphoreType.DMA((5,)),
        ],
        compiler_params=pltpu.CompilerParams(
            collective_id=3, has_side_effects=True, vmem_limit_bytes=40 << 20
        ),
        cost_estimate=pl.CostEstimate(flops=0, bytes_accessed=300 << 20, transcendentals=0),
        name="finish",
    )(
        input_grad,
        grad_q.reshape(2, 2, 2, rows, wide_q),
        grad_o.reshape(2, 2, 2, rows, wide_o),
        gains,
        output,
    )


def one_sequence_body(
    tokens,
    cotangent,
    lengths,
    deal_order,
    gain_attn,
    gain_ffn,
    w_query,
    key_value_weight,
    w_out,
    w_gate_up,
    w_down,
):
    seq_group, rows_local, width_local = tokens.shape
    row_count = lax.axis_size("row")
    col_count = lax.axis_size("col")
    full_width = width_local * col_count
    slot_len = rows_local * row_count
    group, core, mate, row, col = place()
    query_half = w_query.shape[1] // 2
    kv_half = key_value_weight.shape[2] // 2
    hidden = w_down.shape[1]

    def core_half(matrix, axis):
        width = matrix.shape[axis] // 2
        return lax.dynamic_slice_in_dim(matrix, core * width, width, axis)

    def joined(mine, other, at):
        return jnp.where(
            at == 0, jnp.concatenate([mine, other]), jnp.concatenate([other, mine])
        )

    def from_sibling(value):
        return lax.ppermute(value, "dp", SIBLINGS)

    def half_rows(matrix):
        return core_half(matrix, 0)

    pack_q = jnp.concatenate(
        [
            core_half(w_query, 1),
            core_half(key_value_weight[:, 0], 1),
            core_half(key_value_weight[:, 1], 1),
        ],
        axis=1,
    )
    pack_o = core_half(w_out, 1)
    gain_one = gain_attn.astype(jnp.float32)
    gain_two = gain_ffn.astype(jnp.float32)
    own_tokens, attn_input = start_exchange(tokens, gain_one, col_count)

    length = lax.dynamic_slice_in_dim(lengths, mate * seq_group + col, 1)
    given_pos = row * rows_local + jnp.arange(rows_local, dtype=jnp.int32)
    given_lengths = lax.dynamic_slice_in_dim(lengths, group * seq_group, seq_group)
    given_live = given_pos[None, :, None] < given_lengths[:, None, None]
    everyone = lax.all_gather(cotangent, "dp", axis=0, tiled=True)
    everyone, attn_input = lax.optimization_barrier((everyone, attn_input))
    picked = pick_sequences(everyone, deal_order, group * seq_group, seq_group)
    picked = jnp.where(given_live, picked, jnp.zeros_like(picked))
    given = lax.ppermute(picked, ("dp", "row"), CROSSED)
    weights_qkv, weights_out = gather_weights(pack_q, pack_o, picked, row_count, col_count)
    given, weights_qkv = lax.optimization_barrier((given, weights_qkv))
    line_cot = lax.all_gather(given, "col", axis=2, tiled=True)
    own_grad = lax.dynamic_index_in_dim(line_cot, col, keepdims=False).astype(jnp.float32)

    w_gate_up, w_down, weights_qkv = lax.optimization_barrier((w_gate_up, w_down, weights_qkv))
    far_gate_up = lax.ppermute(half_rows(w_gate_up), "row", OVER_X)
    far_down = lax.ppermute(half_rows(w_down), "row", OVER_X)
    own_mats = (w_gate_up[:, 0], w_gate_up[:, 1], w_down)
    far_mats = (far_gate_up[:, 0], far_gate_up[:, 1], far_down)
    sibling_mats = tuple(from_sibling(matrix) for matrix in far_mats)

    cosine_table, sine_table = rope_tables(jnp.arange(slot_len, dtype=jnp.int32), HEAD_SIZE)
    cosine_table, sine_table = lax.optimization_barrier((cosine_table, sine_table))
    cosines = jnp.concatenate(
        [jnp.tile(cosine_table, (1, 6)), jnp.ones((slot_len, HEAD_SIZE), jnp.float32)], axis=1
    )
    turning = jnp.concatenate([-sine_table, sine_table], axis=1)
    sines = jnp.concatenate(
        [jnp.tile(turning, (1, 3)), jnp.zeros((slot_len, HEAD_SIZE), jnp.float32)], axis=1
    )
    own_float = own_tokens.astype(jnp.float32)
    scale_one = lax.rsqrt(jnp.mean(own_float * own_float, axis=1, keepdims=True) + EPSILON)
    projected, heads_out = attend_fast(
        length, attn_input, weights_qkv, cosines, sines, col_count
    )

    def summed_rows(partial):
        count = partial.shape[0] // 2
        mine = lax.dynamic_slice_in_dim(partial, core * count, count)
        other = lax.dynamic_slice_in_dim(partial, (1 - core) * count, count)
        return mine.astype(jnp.float32) + from_sibling(other).astype(jnp.float32)

    attn_rows = summed_rows(expand_local(heads_out, weights_out).astype(jnp.bfloat16))
    resid = own_float + RES_MULT * attn_rows
    scale_two = lax.rsqrt(jnp.mean(resid * resid, axis=1, keepdims=True) + EPSILON)
    own_ffn = (resid * scale_two * gain_two).astype(jnp.bfloat16)

    *unused, a_keep, a_send, b_keep, b_send = feed_forward(
        own_ffn,
        resid.astype(jnp.bfloat16),
        line_cot,
        own_mats + far_mats + sibling_mats,
        col_count,
    )
    mlp_part, back_part = unused[3:5]
    grad_normed_two = jnp.sum(back_part.astype(jnp.float32), axis=0)
    out_cols = lax.psum_scatter(mlp_part, "col", scatter_dimension=2, tiled=True)

    def plus(kept, came):
        return (kept.astype(jnp.float32) + came.astype(jnp.float32)).astype(jnp.bfloat16)

    a_came = lax.ppermute(a_send, "row", OVER_X)
    b_came = lax.ppermute(b_send, "dp", OVER_Y)

    weighted_two = grad_normed_two * gain_two
    inner_two = jnp.sum(weighted_two * resid, axis=1, keepdims=True)
    grad_resid = (
        own_grad + scale_two * weighted_two - resid * scale_two**3 * inner_two / full_width
    )
    gain_two_part = jnp.sum(grad_normed_two * resid * scale_two, axis=0)
    own_attn_grad = (RES_MULT * grad_resid).astype(jnp.bfloat16)
    grad_attn = joined(own_attn_grad, from_sibling(own_attn_grad), core)
    grad_heads = contract_local(grad_attn, weights_out).astype(jnp.bfloat16)
    grad_out = token_outer(grad_attn, heads_out).astype(jnp.bfloat16)
    grad_projected = attend_back_fast(
        length, projected, grad_heads, cosines, sines, col_count
    )
    grad_normed_one = summed_rows(expand_local(grad_projected, weights_qkv).astype(jnp.bfloat16))
    grad_qkv = token_outer(attn_input, grad_projected).astype(jnp.bfloat16)
    weighted_one = grad_normed_one * gain_one
    inner_one = jnp.sum(weighted_one * own_float, axis=1, keepdims=True)
    own_input_grad = (
        grad_resid
        + scale_one * weighted_one
        - own_float * scale_one**3 * inner_one / full_width
    ).astype(jnp.bfloat16)
    gain_one_part = jnp.sum(grad_normed_one * own_float * scale_one, axis=0)
    a_sum, b_sum, own_input_grad = lax.optimization_barrier(
        (plus(a_keep, a_came), plus(b_keep, b_came), own_input_grad)
    )
    high = group // 2

    def one_of(pair, at):
        return lax.dynamic_index_in_dim(pair, at, keepdims=False)

    a_last = lax.ppermute(one_of(a_sum, 1 - high), "dp", OVER_Y)
    b_last = lax.ppermute(one_of(b_sum, 1 - row), "row", OVER_X)
    gains = jnp.stack([gain_one_part, gain_two_part]).reshape(8, -1)
    given_grad, given_out, sums_q, sums_o, gain_sums = finish(
        own_input_grad, grad_qkv, grad_out, gains, out_cols, col_count
    )
    layer_out = jnp.where(given_live, given_out.astype(jnp.float32), 0.0)
    input_grad = given_grad.astype(jnp.float32)
    a_total = one_of(a_sum, high).astype(jnp.float32) + a_last.astype(jnp.float32)
    b_total = one_of(b_sum, row).astype(jnp.float32) + b_last.astype(jnp.float32)
    sums_gate_up = jnp.stack([a_total[:, :hidden], b_total[:, :hidden]], axis=1)
    sums_down = jnp.concatenate([a_total[:, hidden:], b_total[:, hidden:]], axis=1)
    grad_gain_attn, grad_gain_ffn = gain_sums.reshape(2, full_width)

    def both_cores(sums):
        return jnp.concatenate([sums[0], sums[1]], axis=1)

    qk = query_half + kv_half
    out_query = both_cores(sums_q[:, :, :query_half])
    out_kv = jnp.stack(
        [
            both_cores(sums_q[:, :, query_half:qk]),
            both_cores(sums_q[:, :, qk:]),
        ],
        axis=1,
    )
    out_out = both_cores(sums_o)
    return (
        layer_out,
        input_grad,
        out_query,
        out_kv,
        out_out,
        sums_gate_up,
        sums_down,
        grad_gain_attn,
        grad_gain_ffn,
    )


def general_body(
    tokens,
    cotangent,
    lengths,
    deal_order,
    gain_attn,
    gain_ffn,
    w_query,
    key_value_weight,
    w_out,
    w_gate_up,
    w_down,
):
    seq_group, rows_local, width_local = tokens.shape
    row_count = lax.axis_size("row")
    col_count = lax.axis_size("col")
    full_width = width_local * col_count
    slot_len = rows_local * row_count
    total_rows = seq_group * rows_local
    head_size = HEAD_SIZE
    query_width = w_query.shape[1]
    kv_width = key_value_weight.shape[2]
    kv_heads = kv_width // head_size
    group_size = query_width // kv_width
    group_index = lax.axis_index("dp")
    row_index = lax.axis_index("row")
    col_index = lax.axis_index("col")
    matrices = {
        "qkv": jnp.concatenate(
            [w_query, key_value_weight.reshape(key_value_weight.shape[0], 2 * kv_width)], axis=1
        ),
        "out": w_out,
        "gate_up": w_gate_up,
        "down": w_down,
    }

    def contract_with(operand, which_one):
        return contract_rows(operand, matrices[which_one])

    def expand_with(operand, which_one):
        return expand_rows(operand, matrices[which_one])

    own_cotangent = bring_cotangent(cotangent, deal_order, group_index * seq_group)
    own_rows = tokens
    seq_lens = lax.dynamic_slice_in_dim(lengths, group_index * seq_group, seq_group)
    local_pos = row_index * rows_local + jnp.arange(rows_local, dtype=jnp.int32)
    key_pos = jnp.arange(slot_len, dtype=jnp.int32)
    live_rows = (local_pos[None, :] < seq_lens[:, None]).astype(jnp.float32).reshape(total_rows, 1)
    cosine_table, sine_table = rope_tables(jnp.tile(local_pos, seq_group), head_size)
    own_tokens = own_rows.reshape(total_rows, width_local)
    wide_float = widen_cols(own_tokens).astype(jnp.float32)
    scale_one = lax.rsqrt(jnp.mean(wide_float * wide_float, axis=1, keepdims=True) + EPSILON)
    gain_one = gain_attn.astype(jnp.float32)
    first_normed = wide_float * scale_one
    attn_input = (first_normed * gain_one).astype(jnp.bfloat16)
    projected = contract_with(attn_input, "qkv")
    query_lin = projected[:, :query_width].reshape(total_rows, query_width // head_size, head_size)
    key_lin = projected[:, query_width : query_width + kv_width].reshape(
        total_rows, kv_heads, head_size
    )
    value_lin = projected[:, query_width + kv_width :]
    query_rows = rotary_embed(query_lin, cosine_table, sine_table).astype(jnp.bfloat16)
    keys_own = (
        rotary_embed(key_lin, cosine_table, sine_table)
        .astype(jnp.bfloat16)
        .reshape(seq_group, rows_local, kv_width)
    )
    values_own = value_lin.astype(jnp.bfloat16).reshape(seq_group, rows_local, kv_width)
    all_keys, all_values = (
        lax.all_gather(keys_own, "row", axis=1, tiled=True),
        lax.all_gather(values_own, "row", axis=1, tiled=True),
    )
    query_split = query_rows.reshape(seq_group, rows_local, kv_heads, group_size, head_size)
    key_split = all_keys.reshape(seq_group, slot_len, kv_heads, head_size)
    value_split = all_values.reshape(seq_group, slot_len, kv_heads, head_size)

    def forward_seq(inputs):
        return attend(inputs, key_pos, local_pos)

    mixed_heads, row_max, row_sums = lax.map(
        forward_seq, (query_split, key_split, value_split, seq_lens)
    )
    heads_out = mixed_heads.reshape(total_rows, query_width).astype(jnp.bfloat16)
    attn_local = narrow_cols(expand_with(heads_out, "out"))
    resid = own_tokens.astype(jnp.float32) + RES_MULT * attn_local
    gain_two = lax.dynamic_slice_in_dim(
        gain_ffn.astype(jnp.float32), col_index * width_local, width_local
    )
    scale_two = lax.rsqrt(sum_over_cols(jnp.sum(resid * resid, axis=1)) / full_width + EPSILON)[
        :, None
    ]
    normed_two = resid * scale_two
    ffn_input = widen_cols((normed_two * gain_two).astype(jnp.bfloat16))
    gate_up = contract_with(ffn_input, "gate_up")
    gate = gate_up[:, 0]
    upward = gate_up[:, 1]
    sigmoid_gate = jax.nn.sigmoid(gate)
    silu_gate = gate * sigmoid_gate
    hidden = (silu_gate * upward).astype(jnp.bfloat16)
    ffn_local = narrow_cols(expand_with(hidden, "down"))
    layer_out = live_rows * (resid + RES_MULT * ffn_local)
    grad_rows = live_rows * own_cotangent.reshape(total_rows, width_local).astype(jnp.float32)
    grad_ffn = widen_cols((RES_MULT * grad_rows).astype(jnp.bfloat16))
    grad_hidden = contract_with(grad_ffn, "down")
    grad_down = token_outer(grad_ffn, hidden)
    slope = sigmoid_gate * (1.0 + gate * (1.0 - sigmoid_gate))
    grad_gate_rows = jnp.stack(
        [grad_hidden * upward * slope, grad_hidden * silu_gate], axis=1
    ).astype(jnp.bfloat16)
    grad_gate_up = token_outer(ffn_input, grad_gate_rows)
    grad_normed_two = narrow_cols(expand_with(grad_gate_rows, "gate_up"))
    weighted_two = grad_normed_two * gain_two
    inner_two = sum_over_cols(jnp.sum(weighted_two * resid, axis=1))[:, None]
    grad_resid = (
        grad_rows + scale_two * weighted_two - resid * scale_two**3 * inner_two / full_width
    )
    gain_two_part = jnp.sum(grad_normed_two * normed_two, axis=0)
    grad_attn = widen_cols((RES_MULT * grad_resid).astype(jnp.bfloat16))
    grad_heads = contract_with(grad_attn, "out").astype(jnp.bfloat16)
    grad_out = token_outer(grad_attn, heads_out)
    grad_split = grad_heads.reshape(seq_group, rows_local, kv_heads, group_size, head_size)

    def backward_seq(inputs):
        return attend_back(inputs, key_pos, local_pos)

    grad_query, grad_key, grad_value = lax.map(
        backward_seq, (query_split, key_split, value_split, grad_split, row_max, row_sums, seq_lens)
    )
    key_part, value_part = (
        lax.psum_scatter(
            grad_key.reshape(seq_group, slot_len, kv_width).astype(jnp.bfloat16),
            "row",
            scatter_dimension=1,
            tiled=True,
        ).astype(jnp.float32),
        lax.psum_scatter(
            grad_value.reshape(seq_group, slot_len, kv_width).astype(jnp.bfloat16),
            "row",
            scatter_dimension=1,
            tiled=True,
        ).astype(jnp.float32),
    )
    query_back = rotary_embed(
        grad_query.reshape(total_rows, query_width // head_size, head_size),
        cosine_table,
        -sine_table,
    ).reshape(total_rows, query_width)
    key_back = rotary_embed(
        key_part.reshape(total_rows, kv_heads, head_size), cosine_table, -sine_table
    ).reshape(total_rows, kv_width)
    grad_projected = jnp.concatenate(
        [query_back, key_back, value_part.reshape(total_rows, kv_width)], axis=1
    ).astype(jnp.bfloat16)
    grad_qkv = token_outer(attn_input, grad_projected)
    grad_normed_one = expand_with(grad_projected, "qkv")
    weighted_one = grad_normed_one * gain_one
    inner_one = jnp.sum(weighted_one * wide_float, axis=1, keepdims=True)
    input_part = scale_one * weighted_one - wide_float * scale_one**3 * inner_one / full_width
    input_grad = grad_resid + narrow_cols(input_part)
    gain_one_part = jnp.sum(grad_normed_one * first_normed, axis=0)
    gain_two_full = lax.dynamic_update_slice_in_dim(
        jnp.zeros((full_width,), jnp.float32), gain_two_part, col_index * width_local, 0
    )
    grad_gain_attn, grad_gain_ffn = lax.psum((gain_one_part, gain_two_full), ("dp", "row", "col"))
    sums_qkv, sums_out, sums_gate_up, sums_down = (
        lax.psum_scatter(
            grad_qkv.astype(jnp.bfloat16), ("dp", "row"), scatter_dimension=0, tiled=True
        ).astype(jnp.float32),
        lax.psum_scatter(
            grad_out.astype(jnp.bfloat16), ("dp", "row"), scatter_dimension=0, tiled=True
        ).astype(jnp.float32),
        lax.psum_scatter(
            grad_gate_up.astype(jnp.bfloat16), ("dp", "row"), scatter_dimension=0, tiled=True
        ).astype(jnp.float32),
        lax.psum_scatter(
            grad_down.astype(jnp.bfloat16), ("dp", "row"), scatter_dimension=0, tiled=True
        ).astype(jnp.float32),
    )
    out_query = sums_qkv[:, :query_width]
    out_kv = sums_qkv[:, query_width:].reshape(sums_qkv.shape[0], 2, kv_width)
    return (
        layer_out.reshape(seq_group, rows_local, width_local),
        input_grad.reshape(seq_group, rows_local, width_local),
        out_query,
        out_kv,
        sums_out,
        sums_gate_up,
        sums_down,
        grad_gain_attn,
        grad_gain_ffn,
    )


def body(tokens, cotangent, lengths, deal_order, gain_attn, gain_ffn, w_query, key_value_weight, *rest):
    sizes = (lax.axis_size("dp"), lax.axis_size("row"), lax.axis_size("col"))
    one_each = sizes == (4, 2, 4) and tokens.shape[0] == sizes[2]
    pairs = w_query.shape[1] == 8 * HEAD_SIZE and key_value_weight.shape[2] == 2 * HEAD_SIZE
    chosen = one_sequence_body if one_each and pairs else general_body
    return chosen(
        tokens, cotangent, lengths, deal_order, gain_attn, gain_ffn, w_query, key_value_weight, *rest
    )


def solution(mesh):
    placed = (
        P("dp", "row", "col"),
        P("dp", "row", "col"),
        P(),
        P(),
        P(),
        P(),
        P("row", "col"),
        P("row", None, "col"),
        P("row", "col"),
        P("row", None, "col"),
        P("row", "col"),
    )
    return jax.shard_map(
        body,
        mesh=mesh,
        in_specs=placed,
        out_specs=(
            P("dp", "row", "col"),
            P("dp", "row", "col"),
            P(("dp", "row"), "col"),
            P(("dp", "row"), None, "col"),
            P(("dp", "row"), "col"),
            P(("dp", "row"), None, "col"),
            P(("dp", "row"), "col"),
            P(),
            P(),
        ),
        check_vma=False,
    )
```

```python
import functools

import jax
import jax.numpy as jnp
from jax import lax
from jax.experimental import pallas as pl
from jax.experimental.pallas import tpu as pltpu
from jax.sharding import PartitionSpec as P

HEAD_SIZE = 64


EPSILON = 1e-05
THETA = 10000000.0
ATTN_MULT = 0.015625
RES_MULT = 0.22
MASKED = -1e30


def rope_tables(positions, head_size):
    halves = jnp.arange(head_size // 2, dtype=jnp.float32)
    inverse_freq = THETA ** (-(halves * 2.0) / head_size)
    angles = positions.astype(jnp.float32)[:, None] * inverse_freq[None, :]
    return (jnp.cos(angles), jnp.sin(angles))


def rotary_embed(value_rows, cosine_table, sine_table):
    middle = value_rows.shape[-1] // 2
    first_half = value_rows[..., :middle]
    second_half = value_rows[..., middle:]
    cos_part = cosine_table[:, None, :]
    sin_part = sine_table[:, None, :]
    return jnp.concatenate(
        [
            first_half * cos_part - second_half * sin_part,
            second_half * cos_part + first_half * sin_part,
        ],
        axis=-1,
    )


def widen_cols(value_rows):
    return lax.all_gather(value_rows, "col", axis=1, tiled=True)


def narrow_cols(value_rows):
    return lax.psum_scatter(value_rows, "col", scatter_dimension=1, tiled=True)


def sum_over_cols(value_rows):
    return lax.psum(value_rows, "col")


def contract_local(operand, matrix):
    return lax.dot_general(
        operand, matrix, (((1,), (0,)), ((), ())), preferred_element_type=jnp.float32
    )


def expand_local(operand, matrix):
    trailing = tuple(range(1, operand.ndim))
    return lax.dot_general(
        operand, matrix, ((trailing, trailing), ((), ())), preferred_element_type=jnp.float32
    )


def token_outer(features, grads):
    return lax.dot_general(
        features, grads, (((0,), (0,)), ((), ())), preferred_element_type=jnp.float32
    )


def contract_rows(operand, matrix):
    return contract_local(operand, lax.all_gather(matrix, "row", axis=0, tiled=True))


def expand_rows(operand, matrix):
    return expand_local(operand, lax.all_gather(matrix, "row", axis=0, tiled=True))


def split_keys(key_seq, value_seq, key_pos):
    slot_len = key_seq.shape[0]
    width = min(512, slot_len)
    count = slot_len // width
    return (
        key_seq.reshape(count, width, key_seq.shape[1], key_seq.shape[2]),
        value_seq.reshape(count, width, value_seq.shape[1], value_seq.shape[2]),
        key_pos.reshape(count, width),
    )


def block_scores(query_seq, key_block, pos_block, query_pos, length):
    scores = (
        jnp.einsum("qkgd,tkd->kgqt", query_seq, key_block, preferred_element_type=jnp.float32)
        * ATTN_MULT
    )
    allowed = (pos_block[None, :] <= query_pos[:, None]) & (pos_block[None, :] < length)
    return jnp.where(allowed, scores, MASKED)


def attend(inputs, key_pos, query_pos):
    query_seq, key_seq, value_seq, length = inputs
    key_blocks, value_blocks, pos_blocks = split_keys(key_seq, value_seq, key_pos)
    stat_shape = (query_seq.shape[1], query_seq.shape[2], query_seq.shape[0], 1)

    def gather_stats(carry, entry):
        running_max, running_sum = carry
        key_block, pos_block = entry
        scores = block_scores(query_seq, key_block, pos_block, query_pos, length)
        new_max = jnp.maximum(running_max, jnp.max(scores, axis=-1, keepdims=True))
        new_sum = running_sum * jnp.exp(running_max - new_max) + jnp.sum(
            jnp.exp(scores - new_max), axis=-1, keepdims=True
        )
        return ((new_max, new_sum), None)

    start_stats = (jnp.full(stat_shape, MASKED, jnp.float32), jnp.zeros(stat_shape, jnp.float32))
    (row_max, row_sums), unused = lax.scan(gather_stats, start_stats, (key_blocks, pos_blocks))

    def mix_values(running, entry):
        key_block, value_block, pos_block = entry
        scores = block_scores(query_seq, key_block, pos_block, query_pos, length)
        weights = jnp.exp(scores - row_max) / row_sums
        return (
            running
            + jnp.einsum(
                "kgqt,tkd->qkgd",
                weights.astype(jnp.bfloat16),
                value_block,
                preferred_element_type=jnp.float32,
            ),
            None,
        )

    start_mix = jnp.zeros(query_seq.shape, jnp.float32)
    mixed_heads, unused = lax.scan(mix_values, start_mix, (key_blocks, value_blocks, pos_blocks))
    return (mixed_heads, row_max, row_sums)


def attend_back(inputs, key_pos, query_pos):
    query_seq, key_seq, value_seq, grad_mixed, row_max, row_sums, length = inputs
    key_blocks, value_blocks, pos_blocks = split_keys(key_seq, value_seq, key_pos)

    def block_weights(key_block, value_block, pos_block):
        scores = block_scores(query_seq, key_block, pos_block, query_pos, length)
        weights = jnp.exp(scores - row_max) / row_sums
        grad_weights = jnp.einsum(
            "qkgd,tkd->kgqt", grad_mixed, value_block, preferred_element_type=jnp.float32
        )
        return (weights, grad_weights)

    def gather_centre(running, entry):
        weights, grad_weights = block_weights(*entry)
        return (running + jnp.sum(weights * grad_weights, axis=-1, keepdims=True), None)

    start_centre = jnp.zeros(row_max.shape, jnp.float32)
    centre, unused = lax.scan(gather_centre, start_centre, (key_blocks, value_blocks, pos_blocks))

    def grads_block(running, entry):
        key_block = entry[0]
        weights, grad_weights = block_weights(*entry)
        grad_scores = (weights * (grad_weights - centre)).astype(jnp.bfloat16)
        grad_query = (
            running
            + jnp.einsum(
                "kgqt,tkd->qkgd", grad_scores, key_block, preferred_element_type=jnp.float32
            )
            * ATTN_MULT
        )
        grad_key = (
            jnp.einsum("kgqt,qkgd->tkd", grad_scores, query_seq, preferred_element_type=jnp.float32)
            * ATTN_MULT
        )
        grad_value = jnp.einsum(
            "kgqt,qkgd->tkd",
            weights.astype(jnp.bfloat16),
            grad_mixed,
            preferred_element_type=jnp.float32,
        )
        return (grad_query, (grad_key, grad_value))

    start_query = jnp.zeros(query_seq.shape, jnp.float32)
    grad_query, (grad_key, grad_value) = lax.scan(
        grads_block, start_query, (key_blocks, value_blocks, pos_blocks)
    )
    return (grad_query, grad_key.reshape(key_seq.shape), grad_value.reshape(value_seq.shape))


MESH_IDS = pl.DeviceIdType.MESH
SIBLINGS = [(0, 1), (1, 0), (2, 3), (3, 2)]
OVER_X = [(0, 1), (1, 0)]
OVER_Y = [(0, 2), (2, 0), (1, 3), (3, 1)]
CROSSED = [((2 * y + c) * 2 + x, (2 * y + x) * 2 + c) for y in (0, 1) for c in (0, 1) for x in (0, 1)]


def pick_sequences(everyone, deal_order, first, count):
    slots = jnp.arange(deal_order.shape[0], dtype=jnp.int32)
    inverse = jnp.sum(jnp.where(deal_order[None, :] == slots[:, None], slots[None, :], 0), axis=1)
    return jnp.concatenate(
        [
            lax.dynamic_slice_in_dim(
                everyone, lax.dynamic_index_in_dim(inverse, first + at, keepdims=False), 1
            )
            for at in range(count)
        ]
    )


def bring_cotangent(cotangent, deal_order, first):
    everyone = lax.all_gather(cotangent, "dp", axis=0, tiled=True)
    return pick_sequences(everyone, deal_order, first, cotangent.shape[0])


def place():
    group = lax.axis_index("dp")
    core = lax.rem(group, 2)
    row = lax.axis_index("row")
    return group, core, group - core + row, row, lax.axis_index("col")


def lined(index, step, count):
    return lax.rem(index + step + count, count)


def aligned(block, size):
    return pl.ds(pl.multiple_of(block * size, size), size)


def greet(device):
    pl.semaphore_signal(
        pltpu.get_barrier_semaphore(), inc=1, device_id=device, device_id_type=MESH_IDS
    )


def remote(src, dst, sems, at, device):
    return pltpu.make_async_remote_copy(
        src_ref=src,
        dst_ref=dst,
        send_sem=sems.at[0, at],
        recv_sem=sems.at[1, at],
        device_id=device,
        device_id_type=MESH_IDS,
    )


def line_order(col, last, at):
    inner_low = jnp.where(at < 2, 1 - at, at)
    inner_high = jnp.where(at == 3, 0, jnp.where(at == 0, 2, jnp.where(at == 1, 1, 3)))
    return jnp.where(
        col == 0, at, jnp.where(col == last, last - at, jnp.where(col == 1, inner_low, inner_high))
    )


def start_kernel(
    cols, tok_ref, gain_ref, x_ref, a_ref, x_buf, a_buf, tok_sems, a_sems, local_sems
):
    group, core, mate, row, col = place()
    width = tok_ref.shape[2]
    length = x_buf.shape[0]
    sibling = (group + 1 - 2 * core, row, col)

    def line(step):
        return lined(col, step, cols)

    for step in range(1, cols):
        greet((mate, core, line(step)))
    greet(sibling)

    @pl.when(core != row)
    def _():
        greet((mate, core, col))

    pl.semaphore_wait(pltpu.get_barrier_semaphore(), cols + (core - row) * (core - row))

    def token_copy(step, into):
        return remote(
            tok_ref.at[line(step)],
            x_buf.at[:, aligned(into, width)],
            tok_sems,
            step,
            (mate, core, line(step)),
        )

    own_tokens = pltpu.make_async_copy(
        tok_ref.at[col], x_buf.at[:, aligned(col, width)], local_sems.at[0]
    )
    for step in range(1, cols):
        token_copy(step, col).start()

    @pl.when(core != row)
    def _():
        token_copy(0, col).start()

    @pl.when(core == row)
    def _():
        own_tokens.start()

    for step in range(1, cols):
        token_copy(step, line(-step)).wait_recv()

    @pl.when(core != row)
    def _():
        token_copy(0, col).wait_recv()

    @pl.when(core == row)
    def _():
        own_tokens.wait()

    keep_x = pltpu.make_async_copy(x_buf, x_ref, local_sems.at[1])
    keep_x.start()
    tall = min(64, length)

    @pl.loop(0, length // tall)
    def _(at):
        here = aligned(at, tall)
        now = x_buf[here, :].astype(jnp.float32)
        scale = lax.rsqrt(jnp.mean(now * now, axis=1, keepdims=True) + EPSILON)
        a_buf[here, :] = (now * scale * gain_ref[...]).astype(jnp.bfloat16)

    def a_copy(of_core):
        return remote(a_buf, a_ref.at[aligned(of_core, length)], a_sems, 0, sibling)

    own_a = pltpu.make_async_copy(a_buf, a_ref.at[aligned(core, length)], local_sems.at[2])
    a_copy(core).start()
    own_a.start()
    for step in range(1, cols):
        token_copy(step, col).wait_send()

    @pl.when(core != row)
    def _():
        token_copy(0, col).wait_send()

    keep_x.wait()
    own_a.wait()
    a_copy(core).wait_send()
    a_copy(1 - core).wait_recv()


def start_exchange(tokens, gain, cols):
    anywhere = pl.BlockSpec(memory_space=pl.ANY)
    seqs, length, width = tokens.shape
    full = width * cols
    return pl.pallas_call(
        functools.partial(start_kernel, cols),
        out_shape=(
            jax.ShapeDtypeStruct((length, full), tokens.dtype),
            jax.ShapeDtypeStruct((2 * length, full), tokens.dtype),
        ),
        in_specs=[anywhere, pl.BlockSpec(memory_space=pltpu.VMEM)],
        out_specs=(anywhere,) * 2,
        scratch_shapes=[
            pltpu.VMEM((length, full), tokens.dtype),
            pltpu.VMEM((length, full), tokens.dtype),
            pltpu.SemaphoreType.DMA((2, cols)),
            pltpu.SemaphoreType.DMA((2, 1)),
            pltpu.SemaphoreType.DMA((3,)),
        ],
        compiler_params=pltpu.CompilerParams(
            collective_id=1, has_side_effects=True, vmem_limit_bytes=16 << 20
        ),
        cost_estimate=pl.CostEstimate(flops=0, bytes_accessed=200 << 20, transcendentals=0),
        name="start_exchange",
    )(tokens, gain.reshape(1, full))


def gather_kernel(
    cols, q_ref, o_ref, after_ref, wq_ref, wo_ref, q_send, q_recv, q_over, o_send, o_recv, o_over, local_sems
):
    group, core, mate, row, col = place()
    last = cols - 1
    over = (group, 1 - row, col)
    greet(over)

    @pl.when(col < last)
    def _():
        greet((group, row, col + 1))

    @pl.when(col > 0)
    def _():
        greet((group, row, col - 1))

    pl.semaphore_wait(
        pltpu.get_barrier_semaphore(),
        1 + jnp.minimum(col, 1) + jnp.minimum(last - col, 1),
    )

    def moves(own, full, send, recv, over_sems):
        tall, wide = own.shape

        def block(of_row, of_col):
            return full.at[aligned(of_row, tall), aligned(of_col, wide)]

        def along(src, chunk, to, way):
            return pltpu.make_async_remote_copy(
                src_ref=src,
                dst_ref=block(row, chunk),
                send_sem=send.at[way, chunk],
                recv_sem=recv.at[chunk],
                device_id=(group, row, to),
                device_id_type=MESH_IDS,
            )

        def across(src, of_row, chunk):
            return remote(src, block(of_row, chunk), over_sems, chunk, over)

        return block, along, across

    both = (
        (q_ref, moves(q_ref, wq_ref, q_send, q_recv, q_over)),
        (o_ref, moves(o_ref, wo_ref, o_send, o_recv, o_over)),
    )
    own_copies = []
    for at, (own, (block, along, across)) in enumerate(both):

        @pl.when(col < last)
        def _():
            along(own, col, col + 1, 0).start()

        @pl.when(col > 0)
        def _():
            along(own, col, col - 1, 1).start()

        across(own, row, col).start()
        own_copies.append(pltpu.make_async_copy(own, block(row, col), local_sems.at[at]))
        own_copies[-1].start()
    for at in range(1, cols):
        chunk = line_order(col, last, at)
        for own, (block, along, across) in both:
            along(own, chunk, col, 0).wait_recv()

            @pl.when((chunk < col) & (col < last))
            def _():
                along(block(row, chunk), chunk, col + 1, 0).start()

            @pl.when((chunk > col) & (col > 0))
            def _():
                along(block(row, chunk), chunk, col - 1, 1).start()

            across(block(row, chunk), row, chunk).start()
    for copy in own_copies:
        copy.wait()
    for own, (block, along, across) in both:
        for chunk in range(cols):

            @pl.when((col >= chunk) & (col < last))
            def _():
                along(own, chunk, col + 1, 0).wait_send()

            @pl.when((col <= chunk) & (col > 0))
            def _():
                along(own, chunk, col - 1, 1).wait_send()

            across(own, row, chunk).wait_send()
            across(own, 1 - row, chunk).wait_recv()


def gather_weights(own_q, own_o, after, rows, cols):
    anywhere = pl.BlockSpec(memory_space=pl.ANY)

    def whole(own):
        return jax.ShapeDtypeStruct((own.shape[0] * rows, own.shape[1] * cols), own.dtype)

    return pl.pallas_call(
        functools.partial(gather_kernel, cols),
        out_shape=(whole(own_q), whole(own_o)),
        in_specs=[anywhere] * 3,
        out_specs=(anywhere,) * 2,
        scratch_shapes=[
            pltpu.SemaphoreType.DMA((2, cols)),
            pltpu.SemaphoreType.DMA((cols,)),
            pltpu.SemaphoreType.DMA((2, cols)),
        ]
        * 2
        + [pltpu.SemaphoreType.DMA((2,))],
        compiler_params=pltpu.CompilerParams(collective_id=4, has_side_effects=True),
        cost_estimate=pl.CostEstimate(flops=0, bytes_accessed=300 << 20, transcendentals=0),
        name="gather_weights",
    )(own_q, own_o, after)


def half_turn(wide):
    lanes = wide.shape[1]
    half = HEAD_SIZE // 2
    lane = lax.broadcasted_iota(jnp.int32, wide.shape, 1)
    return jnp.where(
        lax.rem(lane, HEAD_SIZE) < half,
        pltpu.roll(wide, lanes - half, 1),
        pltpu.roll(wide, half, 1),
    )


def both_heads(pair):
    lane = lax.broadcasted_iota(jnp.int32, pair.shape, 1)
    turned = pltpu.roll(pair, HEAD_SIZE, 1)
    low = lane < HEAD_SIZE
    return jnp.where(low, pair, turned), jnp.where(low, turned, pair)


def keep_head(pair, side):
    lane = lax.broadcasted_iota(jnp.int32, pair.shape, 1)
    mine = lane < HEAD_SIZE if side == 0 else lane >= HEAD_SIZE
    return jnp.where(mine, pair, jnp.zeros_like(pair))


def dot_nn(a, b):
    return lax.dot_general(a, b, (((1,), (0,)), ((), ())), preferred_element_type=jnp.float32)


def dot_nt(a, b):
    return lax.dot_general(a, b, (((1,), (1,)), ((), ())), preferred_element_type=jnp.float32)


def dot_tn(a, b):
    return lax.dot_general(a, b, (((0,), (0,)), ((), ())), preferred_element_type=jnp.float32)


PAIR = 2 * HEAD_SIZE


def attend_kernel(block, len_ref, a_ref, w_ref, cos_ref, sin_ref, qkv_ref, z_ref, q_all, k_two, v_two):
    rows = a_ref.shape[0]
    heads = q_all.shape[0]
    length = len_ref[0]

    @pl.loop(0, rows // block)
    def _(at):
        here = pl.ds(pl.multiple_of(at * block, block), block)
        lin = dot_nn(a_ref[here, :], w_ref[...])
        for part in range(heads // 2 + 1):
            lanes = slice(part * PAIR, (part + 1) * PAIR)
            now = lin[:, lanes]
            table = slice(0, PAIR) if part < heads // 2 else slice(PAIR, 2 * PAIR)
            now = now * cos_ref[here, table] + half_turn(now) * sin_ref[here, table]
            qkv_ref[here, lanes] = now.astype(jnp.bfloat16)
            if part < heads // 2:
                for side in range(2):
                    q_all[2 * part + side, here, :] = keep_head(now * ATTN_MULT, side).astype(
                        jnp.bfloat16
                    )
            else:
                keys, values = both_heads(now)
                k_two[here, :] = keys.astype(jnp.bfloat16)
                v_two[here, :] = values.astype(jnp.bfloat16)

    for at in range(rows // block):
        here = slice(at * block, (at + 1) * block)
        upto = (at + 1) * block
        row = lax.broadcasted_iota(jnp.int32, (block, upto), 0) + at * block
        key = lax.broadcasted_iota(jnp.int32, (block, upto), 1)
        allowed = key < jnp.minimum(row + 1, length)

        def one_head(head):
            scores = dot_nt(q_all[head, here, :], k_two[:upto, :])
            scores = jnp.where(allowed, scores, MASKED)
            top = jnp.max(scores, axis=1, keepdims=True)
            power = jnp.exp(scores - top)
            total = jnp.sum(power, axis=1, keepdims=True)
            return dot_nn(power.astype(jnp.bfloat16), v_two[:upto, :]) / total

        for pair in range(heads // 2):
            low = one_head(2 * pair)
            high = one_head(2 * pair + 1)
            lane = lax.broadcasted_iota(jnp.int32, low.shape, 1)
            z_ref[here, pair * PAIR : (pair + 1) * PAIR] = jnp.where(
                lane < HEAD_SIZE, low, high
            ).astype(jnp.bfloat16)


def attend_fast(length, inputs, weights, cosines, sines, groups):
    rows, depth = inputs.shape
    wide = weights.shape[1] // groups
    heads = (wide - PAIR) // HEAD_SIZE
    block = min(256, rows)
    return pl.pallas_call(
        functools.partial(attend_kernel, block),
        grid=(groups,),
        out_shape=(
            jax.ShapeDtypeStruct((rows, groups * wide), jnp.bfloat16),
            jax.ShapeDtypeStruct((rows, groups * heads * HEAD_SIZE), jnp.bfloat16),
        ),
        in_specs=[
            pl.BlockSpec(memory_space=pltpu.SMEM),
            pl.BlockSpec((rows, depth), lambda g: (0, 0)),
            pl.BlockSpec((depth, wide), lambda g: (0, g)),
            pl.BlockSpec((rows, 2 * PAIR), lambda g: (0, 0)),
            pl.BlockSpec((rows, 2 * PAIR), lambda g: (0, 0)),
        ],
        out_specs=(
            pl.BlockSpec((rows, wide), lambda g: (0, g)),
            pl.BlockSpec((rows, heads * HEAD_SIZE), lambda g: (0, g)),
        ),
        scratch_shapes=[
            pltpu.VMEM((heads, rows, PAIR), jnp.bfloat16),
            pltpu.VMEM((rows, PAIR), jnp.bfloat16),
            pltpu.VMEM((rows, PAIR), jnp.bfloat16),
        ],
        compiler_params=pltpu.CompilerParams(vmem_limit_bytes=48 << 20),
        cost_estimate=pl.CostEstimate(
            flops=2 * rows * depth * wide * groups + 2 * groups * heads * rows * rows * 128,
            bytes_accessed=2 * (rows * depth + depth * wide * groups + rows * wide * groups),
            transcendentals=groups * heads * rows * rows // 2,
        ),
        name="attend",
    )(length, inputs, weights, cosines, sines)


def attend_back_kernel(
    block, len_ref, qkv_ref, dz_ref, cos_ref, sin_ref, out_ref, q_all, z_all, k_two, v_two, k_acc, v_acc
):
    rows = qkv_ref.shape[0]
    heads = q_all.shape[0]
    length = len_ref[0]

    @pl.loop(0, rows // block)
    def _(at):
        here = pl.ds(pl.multiple_of(at * block, block), block)
        for part in range(heads // 2):
            lanes = slice(part * PAIR, (part + 1) * PAIR)
            queries = qkv_ref[here, lanes].astype(jnp.float32) * ATTN_MULT
            mixed = dz_ref[here, lanes].astype(jnp.float32)
            for side in range(2):
                q_all[2 * part + side, here, :] = keep_head(queries, side).astype(jnp.bfloat16)
                z_all[2 * part + side, here, :] = keep_head(mixed, side).astype(jnp.bfloat16)
        keys, values = both_heads(qkv_ref[here, heads * HEAD_SIZE :].astype(jnp.float32))
        k_two[here, :] = keys.astype(jnp.bfloat16)
        v_two[here, :] = values.astype(jnp.bfloat16)
        k_acc[here, :] = jnp.zeros((block, PAIR), jnp.float32)
        v_acc[here, :] = jnp.zeros((block, PAIR), jnp.float32)

    def turn_back(now, here, table):
        return (now * cos_ref[here, table] - half_turn(now) * sin_ref[here, table]).astype(
            jnp.bfloat16
        )

    for at in range(rows // block):
        here = slice(at * block, (at + 1) * block)
        upto = (at + 1) * block
        key = lax.broadcasted_iota(jnp.int32, (upto, block), 0)
        query = lax.broadcasted_iota(jnp.int32, (upto, block), 1) + at * block
        allowed = key < jnp.minimum(query + 1, length)

        def one_head(head):
            queries, mixed = q_all[head, here, :], z_all[head, here, :]
            scores = jnp.where(allowed, dot_nt(k_two[:upto, :], queries), MASKED)
            power = jnp.exp(scores - jnp.max(scores, axis=0, keepdims=True))
            weights = power * (1.0 / jnp.sum(power, axis=0, keepdims=True))
            back = dot_nt(v_two[:upto, :], mixed)
            centre = jnp.sum(weights * back, axis=0, keepdims=True)
            slope = (weights * (back - centre)).astype(jnp.bfloat16)
            k_acc[:upto, :] += dot_nn(slope, queries)
            v_acc[:upto, :] += dot_nn(weights.astype(jnp.bfloat16), mixed)
            return dot_tn(slope, k_two[:upto, :]) * ATTN_MULT

        for pair in range(heads // 2):
            low = one_head(2 * pair)
            high = one_head(2 * pair + 1)
            lane = lax.broadcasted_iota(jnp.int32, low.shape, 1)
            lanes = slice(pair * PAIR, (pair + 1) * PAIR)
            out_ref[here, lanes] = turn_back(
                jnp.where(lane < HEAD_SIZE, low, high), here, slice(0, PAIR)
            )

    @pl.loop(0, rows // block)
    def _(at):
        here = pl.ds(pl.multiple_of(at * block, block), block)
        keys, values = k_acc[here, :], v_acc[here, :]
        keys = keys + pltpu.roll(keys, HEAD_SIZE, 1)
        values = values + pltpu.roll(values, HEAD_SIZE, 1)
        lane = lax.broadcasted_iota(jnp.int32, keys.shape, 1)
        lanes = slice(heads * HEAD_SIZE, heads * HEAD_SIZE + PAIR)
        out_ref[here, lanes] = turn_back(
            jnp.where(lane < HEAD_SIZE, keys, values), here, slice(PAIR, 2 * PAIR)
        )


def attend_back_fast(length, projected, grad_mixed, cosines, sines, groups):
    rows = projected.shape[0]
    wide = projected.shape[1] // groups
    heads = (wide - PAIR) // HEAD_SIZE
    block = min(256, rows)
    return pl.pallas_call(
        functools.partial(attend_back_kernel, block),
        grid=(groups,),
        out_shape=jax.ShapeDtypeStruct((rows, groups * wide), jnp.bfloat16),
        in_specs=[
            pl.BlockSpec(memory_space=pltpu.SMEM),
            pl.BlockSpec((rows, wide), lambda g: (0, g)),
            pl.BlockSpec((rows, heads * HEAD_SIZE), lambda g: (0, g)),
            pl.BlockSpec((rows, 2 * PAIR), lambda g: (0, 0)),
            pl.BlockSpec((rows, 2 * PAIR), lambda g: (0, 0)),
        ],
        out_specs=pl.BlockSpec((rows, wide), lambda g: (0, g)),
        scratch_shapes=[
            pltpu.VMEM((heads, rows, PAIR), jnp.bfloat16),
            pltpu.VMEM((heads, rows, PAIR), jnp.bfloat16),
            pltpu.VMEM((rows, PAIR), jnp.bfloat16),
            pltpu.VMEM((rows, PAIR), jnp.bfloat16),
            pltpu.VMEM((rows, PAIR), jnp.float32),
            pltpu.VMEM((rows, PAIR), jnp.float32),
        ],
        compiler_params=pltpu.CompilerParams(vmem_limit_bytes=48 << 20),
        cost_estimate=pl.CostEstimate(
            flops=5 * groups * heads * rows * rows * 128,
            bytes_accessed=2 * (2 * rows * wide * groups + rows * heads * HEAD_SIZE * groups),
            transcendentals=groups * heads * rows * rows // 2,
        ),
        name="attend_back",
    )(length, projected, grad_mixed, cosines, sines)


def ffn_kernel(
    cols,
    own_ref,
    resid_ref,
    grad_ref,
    wg_own,
    wu_own,
    wd_own,
    wg_far,
    wu_far,
    wd_far,
    wg_sib,
    wu_sib,
    wd_sib,
    u_all,
    dgu_all,
    mlp_all,
    back_all,
    relay_ref,
    land_ref,
    a_keep,
    a_send,
    b_keep,
    b_send,
    wg,
    wu,
    wd,
    b_all,
    b_turn,
    g_two,
    u_buf,
    dg_buf,
    du_buf,
    mlp_buf,
    back_buf,
    w_sems,
    ag_send,
    ag_recv,
    back_send,
    back_recv,
    relay_recv,
    pair_sems,
    lane_sems,
    io_sems,
):
    group, core, mate, row, col = place()
    sibling = (group + 1 - 2 * core, row, col)
    last = cols - 1
    depth = wg_own.shape[0]
    half = depth // 2
    units = wg_own.shape[1]
    rows = own_ref.shape[0]
    tile = min(512, units)
    beside = col + 1 - 2 * lax.rem(col, 2)
    facing = last - col
    inner = (col > 0) & (col < last)

    for step in range(1, cols):
        greet((group, row, lined(col, step, cols)))
    greet(sibling)
    pl.semaphore_wait(pltpu.get_barrier_semaphore(), cols)

    def pass_on(src, at, to, way):
        return pltpu.make_async_remote_copy(
            src_ref=src,
            dst_ref=b_all.at[at],
            send_sem=ag_send.at[way, at],
            recv_sem=ag_recv.at[at],
            device_id=(group, row, to),
            device_id_type=MESH_IDS,
        )

    @pl.when(col < last)
    def _():
        pass_on(own_ref, col, col + 1, 0).start()

    @pl.when(col > 0)
    def _():
        pass_on(own_ref, col, col - 1, 1).start()

    def order(at):
        return line_order(col, last, at)

    def load_g(at):
        side = lax.rem(at, 2)
        return pltpu.make_async_copy(grad_ref.at[order(at)], g_two.at[side], io_sems.at[6 + side])

    def rows_at(first, size):
        return pl.ds(pl.multiple_of(first, half), size)

    own_copy = pltpu.make_async_copy(own_ref, b_all.at[col], io_sems.at[0])
    own_copy.start()
    load_resid = pltpu.make_async_copy(resid_ref, mlp_buf, io_sems.at[8])
    far = (1 - row) * depth
    loads = []
    for at, (full, mine, across, shared) in enumerate(
        ((wg, wg_own, wg_far, wg_sib), (wu, wu_own, wu_far, wu_sib), (wd, wd_own, wd_far, wd_sib))
    ):
        loads += [
            pltpu.make_async_copy(mine, full.at[rows_at(row * depth, depth)], w_sems.at[3 * at]),
            pltpu.make_async_copy(
                across, full.at[rows_at(far + core * half, half)], w_sems.at[3 * at + 1]
            ),
            pltpu.make_async_copy(
                shared, full.at[rows_at(far + (1 - core) * half, half)], w_sems.at[3 * at + 2]
            ),
        ]
    for load in loads:
        load.start()
    load_g(0).start()
    load_resid.start()
    own_copy.wait()
    for load in loads:
        load.wait()

    def arrive(chunk):
        pass_on(b_all.at[chunk], chunk, col, 0).wait_recv()

        @pl.when((chunk < col) & (col < last))
        def _():
            pass_on(b_all.at[chunk], chunk, col + 1, 0).start()

        @pl.when((chunk > col) & (col > 0))
        def _():
            pass_on(b_all.at[chunk], chunk, col - 1, 1).start()

    def outputs(chunk):
        return (
            pltpu.make_async_copy(u_buf, u_all.at[chunk], io_sems.at[1]),
            pltpu.make_async_copy(dg_buf, dgu_all.at[chunk, :, 0:units], io_sems.at[2]),
            pltpu.make_async_copy(du_buf, dgu_all.at[chunk, :, units : 2 * units], io_sems.at[3]),
        )

    def mlp_out(chunk):
        return pltpu.make_async_copy(mlp_buf, mlp_all.at[chunk], io_sems.at[4])

    def slot_of(at):
        return lax.rem(at, cols - 1)

    def deliver(slot, to, place_there, at):
        return pltpu.make_async_remote_copy(
            src_ref=back_buf.at[slot],
            dst_ref=back_all.at[place_there],
            send_sem=back_send.at[at],
            recv_sem=back_recv.at[place_there],
            device_id=(group, row, to),
            device_id_type=MESH_IDS,
        )

    def hand_over(slot, to, box, at):
        return pltpu.make_async_remote_copy(
            src_ref=back_buf.at[slot],
            dst_ref=relay_ref.at[box],
            send_sem=back_send.at[at],
            recv_sem=relay_recv.at[box],
            device_id=(group, row, to),
            device_id_type=MESH_IDS,
        )

    own_back = pltpu.make_async_copy(back_buf.at[0], back_all.at[0], io_sems.at[5])
    at_end = jnp.logical_not(inner)

    def one_chunk(at, unused):
        chunk = order(at)
        side = lax.rem(at, 2)

        @pl.when(at_end & (at > 0))
        def _():
            arrive(order(at))

        @pl.when(inner & (at == 1))
        def _():
            arrive(order(1))
            arrive(order(2))

        @pl.when(inner & (at == 3))
        def _():
            arrive(order(3))

        load_g(at).wait()

        @pl.when(at < last)
        def _():
            load_g(at + 1).start()

        @pl.when(at > 0)
        def _():
            for copy in outputs(order(at - 1)):
                copy.wait()

        @pl.loop(0, units // tile)
        def _(step):
            lanes = aligned(step, tile)
            gate = dot_nn(b_all[chunk], wg[:, lanes])
            upward = dot_nn(b_all[chunk], wu[:, lanes])
            back = RES_MULT * dot_nn(g_two[side], wd[:, lanes])
            opened = 1.0 / (1.0 + jnp.exp(-gate))
            silu = gate * opened
            u_buf[:, lanes] = (silu * upward).astype(jnp.bfloat16)
            slope = opened * (1.0 + gate * (1.0 - opened))
            dg_buf[:, lanes] = (back * upward * slope).astype(jnp.bfloat16)
            du_buf[:, lanes] = (back * silu).astype(jnp.bfloat16)

        for copy in outputs(chunk):
            copy.start()

        @pl.when(at > 0)
        def _():
            mlp_out(order(at - 1)).wait()

        @pl.when(at == 0)
        def _():
            load_resid.wait()

        @pl.when(at == last)
        def _():
            own_back.wait()

        @pl.loop(0, 2 * depth // tile)
        def _(step):
            here = aligned(step, tile)
            back = dot_nt(dg_buf[...], wg[here, :]) + dot_nt(du_buf[...], wu[here, :])
            back_buf[slot_of(at), :, here] = back.astype(jnp.bfloat16)
            added = jnp.where(at == 0, mlp_buf[:, here].astype(jnp.float32), 0.0)
            mlp_buf[:, here] = (added + RES_MULT * dot_nt(u_buf[...], wd[here, :])).astype(
                jnp.bfloat16
            )

        mlp_out(chunk).start()

        @pl.when(at == 0)
        def _():
            own_back.start()

        @pl.when(at_end & (at == 1))
        def _():
            deliver(1, beside, 1, 1).start()

        @pl.when(at_end & (at == 2))
        def _():
            hand_over(2, beside, 1, 2).start()

        @pl.when(at_end & (at == 3))
        def _():
            deliver(0, facing, 2, 3).start()

        @pl.when(inner & (at == 3))
        def _():
            hand_over(0, facing, 0, 3).start()

        return unused

    lax.fori_loop(0, cols, one_chunk, 0)
    for copy in outputs(order(last)):
        copy.wait()
    mlp_out(order(last)).wait()

    loads = []
    for chunk in range(cols):
        here = slice(chunk * rows, (chunk + 1) * rows)
        loads += [
            pltpu.make_async_copy(
                dgu_all.at[chunk, :, 0:units], wg.at[here], w_sems.at[chunk]
            ),
            pltpu.make_async_copy(
                dgu_all.at[chunk, :, units : 2 * units], wu.at[here], w_sems.at[cols + chunk]
            ),
            pltpu.make_async_copy(u_all.at[chunk], wd.at[here], w_sems.at[2 * cols + chunk]),
        ]
    for load in loads:
        load.start()
    for load in loads:
        load.wait()

    def relay(box, slot):
        hand_over(slot, facing, box, 3).wait_recv()
        load = pltpu.make_async_copy(relay_ref.at[box], mlp_buf, io_sems.at[4])
        load.start()
        load.wait()
        tall = min(64, rows)

        @pl.loop(0, rows // tall)
        def _(at):
            here = aligned(at, tall)
            back_buf[slot, here, :] = (
                back_buf[slot, here, :].astype(jnp.float32)
                + mlp_buf[here, :].astype(jnp.float32)
            ).astype(jnp.bfloat16)

    buffers = (dg_buf, du_buf, u_buf)

    def to_sibling(at, part):
        return pltpu.make_async_remote_copy(
            src_ref=buffers[part],
            dst_ref=land_ref.at[at, part],
            send_sem=pair_sems.at[0, at, part],
            recv_sem=pair_sems.at[1, at, part],
            device_id=sibling,
            device_id_type=MESH_IDS,
        )

    def landed(at, part):
        return pltpu.make_async_copy(land_ref.at[at, part], buffers[part], io_sems.at[1 + part])

    halfway = units // 2
    small = rows // 2
    mine, others = aligned(row, small), aligned(1 - row, small)

    def x_lane(high):
        return (
            pltpu.make_async_copy(
                dg_buf.at[mine], a_keep.at[high, :, 0:units], lane_sems.at[0]
            ),
            pltpu.make_async_copy(
                dg_buf.at[others], a_send.at[high, :, 0:units], lane_sems.at[1]
            ),
            pltpu.make_async_copy(
                u_buf.at[mine, 0:halfway],
                a_keep.at[high, :, units : units + halfway],
                lane_sems.at[2],
            ),
            pltpu.make_async_copy(
                u_buf.at[others, 0:halfway],
                a_send.at[high, :, units : units + halfway],
                lane_sems.at[3],
            ),
        )

    def y_lane(target):
        copies = []
        for side in range(2):
            here = slice(side * small, (side + 1) * small)
            copies += [
                pltpu.make_async_copy(
                    du_buf.at[here], target.at[side, :, 0:units], lane_sems.at[4 + 2 * side]
                ),
                pltpu.make_async_copy(
                    u_buf.at[here, halfway:units],
                    target.at[side, :, units : units + halfway],
                    lane_sems.at[5 + 2 * side],
                ),
            ]
        return copies

    def put_results(high, act):
        for copy in x_lane(high):
            act(copy)

        @pl.when(high == (group - core) // 2)
        def _():
            for copy in y_lane(b_keep):
                act(copy)

        @pl.when(high != (group - core) // 2)
        def _():
            for copy in y_lane(b_send):
                act(copy)

    def start_it(copy):
        copy.start()

    def wait_for(copy):
        copy.wait()

    def part_of(chunk):
        return slice(chunk * rows, (chunk + 1) * rows)

    def grad_tile(block, chunk):
        return pltpu.make_async_copy(
            grad_ref.at[chunk, :, aligned(block, rows)],
            mlp_buf.at[:, part_of(chunk)],
            w_sems.at[chunk],
        )

    parts = range(3)

    def one_block(at, unused):
        high = lax.rem(at, 2)
        is_own = at >= 2
        block = 2 * high + jnp.where(is_own, core, 1 - core)

        @pl.when(inner & (at == 1))
        def _():
            relay(0, col)
            deliver(col, beside, 1, 1).start()
            relay(1, last - col)
            deliver(last - col, facing, 2, 2).start()

        for chunk in range(cols):
            grad_tile(block, chunk).start()
        for chunk in range(cols):
            b_turn[:, part_of(chunk)] = b_all[chunk, :, aligned(block, rows)].T
        for chunk in range(cols):
            grad_tile(block, chunk).wait()
        for chunk in range(cols):
            g_two[0, :, part_of(chunk)] = mlp_buf[:, part_of(chunk)].T

        @pl.when((at == 1) | (at == 2))
        def _():
            for part in parts:
                to_sibling(at - 1, part).wait_send()

        @pl.when(at == 3)
        def _():
            put_results(0, wait_for)

        @pl.when(is_own)
        def _():
            for part in parts:
                to_sibling(high, part).wait_recv()
                landed(high, part).start()
            for part in parts:
                landed(high, part).wait()

        @pl.loop(0, units // tile)
        def _(step):
            lanes = aligned(step, tile)

            def put(buffer, value):
                other = jnp.where(is_own, buffer[:, lanes].astype(jnp.float32), 0.0)
                buffer[:, lanes] = (other + value).astype(jnp.bfloat16)

            put(dg_buf, dot_nn(b_turn[...], wg[:, lanes]))
            put(du_buf, dot_nn(b_turn[...], wu[:, lanes]))
            put(u_buf, RES_MULT * dot_nn(g_two[0], wd[:, lanes]))

        @pl.when(jnp.logical_not(is_own))
        def _():
            for part in parts:
                to_sibling(at, part).start()

        @pl.when(is_own)
        def _():
            put_results(high, start_it)

        return unused

    lax.fori_loop(0, 4, one_block, 0)
    put_results(1, wait_for)
    for at in range(1, cols):
        deliver(0, beside, 1, at).wait_send()
    for at in range(1, 3):
        deliver(0, beside, at, at).wait_recv()
    for chunk in range(cols):

        @pl.when((col >= chunk) & (col < last))
        def _():
            pass_on(own_ref, chunk, col + 1, 0).wait_send()

        @pl.when((col <= chunk) & (col > 0))
        def _():
            pass_on(own_ref, chunk, col - 1, 1).wait_send()


def feed_forward(own_input, resid, grad_rows, weights, cols):
    rows, width = own_input.shape
    units = weights[0].shape[1]
    anywhere = pl.BlockSpec(memory_space=pl.ANY)
    bf16 = jnp.bfloat16
    lane = jax.ShapeDtypeStruct((2, rows // 2, units + units // 2), bf16)
    return pl.pallas_call(
        functools.partial(ffn_kernel, cols),
        out_shape=(
            jax.ShapeDtypeStruct((cols, rows, units), bf16),
            jax.ShapeDtypeStruct((cols, rows, 2 * units), bf16),
            jax.ShapeDtypeStruct((cols, rows, width), bf16),
            jax.ShapeDtypeStruct((3, rows, width), bf16),
            jax.ShapeDtypeStruct((2, rows, width), bf16),
            jax.ShapeDtypeStruct((2, 3, rows, units), bf16),
        )
        + (lane,) * 4,
        in_specs=[anywhere] * 12,
        out_specs=(anywhere,) * 10,
        scratch_shapes=[
            pltpu.VMEM((width, units), bf16),
            pltpu.VMEM((width, units), bf16),
            pltpu.VMEM((width, units), bf16),
            pltpu.VMEM((cols, rows, width), bf16),
            pltpu.VMEM((rows, width), bf16),
            pltpu.VMEM((2, rows, width), bf16),
            pltpu.VMEM((rows, units), bf16),
            pltpu.VMEM((rows, units), bf16),
            pltpu.VMEM((rows, units), bf16),
            pltpu.VMEM((rows, width), bf16),
            pltpu.VMEM((cols - 1, rows, width), bf16),
            pltpu.SemaphoreType.DMA((12,)),
            pltpu.SemaphoreType.DMA((2, cols)),
            pltpu.SemaphoreType.DMA((cols,)),
            pltpu.SemaphoreType.DMA((cols,)),
            pltpu.SemaphoreType.DMA((cols,)),
            pltpu.SemaphoreType.DMA((2,)),
            pltpu.SemaphoreType.DMA((2, 2, 3)),
            pltpu.SemaphoreType.DMA((8,)),
            pltpu.SemaphoreType.DMA((9,)),
        ],
        compiler_params=pltpu.CompilerParams(
            collective_id=2, has_side_effects=True, vmem_limit_bytes=60 << 20
        ),
        cost_estimate=pl.CostEstimate(
            flops=18 * cols * rows * width * units,
            bytes_accessed=800 << 20,
            transcendentals=cols * rows * units,
        ),
        name="feed_forward",
    )(own_input, resid, grad_rows, *weights)


def finish_kernel(
    cols,
    ig_ref,
    gq_ref,
    go_ref,
    gain_ref,
    out_ref,
    gin_ref,
    crossed_ref,
    sq_ref,
    so_ref,
    gsum_ref,
    q_keep,
    q_sib,
    q_a1,
    q_a2,
    q_b1,
    q_b2,
    q_z,
    o_keep,
    o_sib,
    o_a1,
    o_a2,
    o_b1,
    o_b2,
    o_z,
    gain_now,
    gain_in,
    ig_sems,
    gain_sems,
    q_sems,
    o_sems,
    qz_sems,
    oz_sems,
    cross_sems,
    local_sems,
):
    group, core, mate, row, col = place()
    pair = group - core
    high = pair // 2
    sibling = (pair + 1 - core, row, col)
    over_x = (group, 1 - row, col)
    over_y = (2 * (1 - high) + core, row, col)
    width = gin_ref.shape[2]

    def line(step):
        return lax.rem(col + step + cols, cols)

    barrier = pltpu.get_barrier_semaphore()

    def greet(device):
        pl.semaphore_signal(barrier, inc=1, device_id=device, device_id_type=MESH_IDS)

    greet(sibling)
    greet(over_x)
    greet(over_y)
    for step in range(1, cols):
        greet((mate, core, line(step)))
        greet((group, row, line(step)))

    @pl.when(core != row)
    def _():
        greet((mate, core, col))

    pl.semaphore_wait(barrier, 2 * cols + 1 + (core - row) * (core - row))

    def remote(src, dst, sems, at, device):
        return pltpu.make_async_remote_copy(
            src_ref=src,
            dst_ref=dst,
            send_sem=sems.at[0, at],
            recv_sem=sems.at[1, at],
            device_id=device,
            device_id_type=MESH_IDS,
        )

    def lanes(block, size):
        return pl.ds(pl.multiple_of(block * size, size), size)

    matrices = (
        (gq_ref, sq_ref, q_keep, q_sib, q_a1, q_a2, q_b1, q_b2, q_z, q_sems, qz_sems),
        (go_ref, so_ref, o_keep, o_sib, o_a1, o_a2, o_b1, o_b2, o_z, o_sems, oz_sems),
    )

    def moves(m):
        grads, out, keep, sib, a1, a2, b1, b2, zb, sems, z_sems = matrices[m]
        return dict(
            s0=remote(grads.at[:, 1 - core], sib, sems, 0, sibling),
            a1=remote(grads.at[:, core, 1 - row], a1, sems, 1, over_x),
            a2=remote(keep.at[1 - high, row], a2, sems, 2, over_y),
            b1=remote(sib.at[1 - high], b1, sems, 3, over_y),
            b2=remote(sib.at[high, 1 - row], b2, sems, 4, over_x),
            own=pltpu.make_async_copy(grads.at[:, core], keep, local_sems.at[m]),
        )

    copies = (moves(0), moves(1))

    def rows_plus(into, more):
        rows = into.shape[0]
        step = min(32, rows)

        @pl.loop(0, rows // step)
        def _(at):
            here = pl.ds(pl.multiple_of(at * step, step), step)
            into[here, :] = (
                into[here, :].astype(jnp.float32) + more[here, :].astype(jnp.float32)
            ).astype(into.dtype)

    def token_copy(step, at):
        return remote(
            ig_ref.at[:, lanes(line(step), width)],
            gin_ref.at[at],
            ig_sems,
            step,
            (mate, core, line(step)),
        )

    own_tokens = pltpu.make_async_copy(
        ig_ref.at[:, lanes(col, width)], gin_ref.at[col], local_sems.at[2]
    )

    cross = remote(out_ref, crossed_ref, cross_sems, 0, (mate, core, col))
    stay = pltpu.make_async_copy(out_ref, crossed_ref, local_sems.at[4])
    for m in range(2):
        copies[m]["s0"].start()
        copies[m]["a1"].start()
        copies[m]["own"].start()
    @pl.when(core == row)
    def _():
        own_tokens.start()
        stay.start()
        for step in range(1, cols):
            token_copy(step, col).start()

    gain_load = pltpu.make_async_copy(gain_ref, gain_now.at[0], local_sems.at[3])
    gain_load.start()
    gain_load.wait()
    near = (
        sibling,
        over_x,
        over_y,
        (group, row, col + 1 - 2 * lax.rem(col, 2)),
        (group, row, lax.rem(col + cols // 2, cols)),
    )

    def gain_round(at):
        exchange = remote(gain_now.at[at], gain_in.at[at], gain_sems, at, near[at])
        exchange.start()
        exchange.wait()
        gain_now[at + 1] = gain_now[at] + gain_in[at]

    gain_round(0)
    for m in range(2):
        copies[m]["s0"].wait()
        copies[m]["b1"].start()
    gain_round(1)
    for m in range(2):
        grads, out, keep, sib, a1, a2, b1, b2, zb, sems, z_sems = matrices[m]
        copies[m]["own"].wait()
        copies[m]["a1"].wait()
        rows_plus(keep.at[1 - high, row], a1.at[1 - high])
        copies[m]["a2"].start()
    for m in range(2):
        grads, out, keep, sib, a1, a2, b1, b2, zb, sems, z_sems = matrices[m]
        copies[m]["b1"].wait()
        rows_plus(sib.at[high, 1 - row], b1.at[1 - row])
        copies[m]["b2"].start()

    @pl.when(core != row)
    def _():
        for step in range(cols):
            token_copy(step, col).start()
        cross.start()

    gain_round(2)
    for m in range(2):
        grads, out, keep, sib, a1, a2, b1, b2, zb, sems, z_sems = matrices[m]
        rows_plus(keep.at[high, row], a1.at[high])
        rows_plus(sib.at[high, row], b1.at[row])

    def z_moves(m, side, source):
        grads, out, keep, sib, a1, a2, b1, b2, zb, sems, z_sems = matrices[m]
        held = (keep, sib)[side]
        wide = zb.shape[3]
        return [
            pltpu.make_async_remote_copy(
                src_ref=held.at[high, row, :, lanes(line(step), wide)],
                dst_ref=zb.at[side, line(source(step))],
                send_sem=z_sems.at[0, side, step],
                recv_sem=z_sems.at[1, side, step],
                device_id=(group, row, line(step)),
                device_id_type=MESH_IDS,
            )
            for step in range(1, cols)
        ]

    for side, last_copy in ((0, "a2"), (1, "b2")):
        for m in range(2):
            grads, out, keep, sib, a1, a2, b1, b2, zb, sems, z_sems = matrices[m]
            copies[m][last_copy].wait()
            rows_plus((keep, sib)[side].at[high, row], (a2, b2)[side])
            for copy in z_moves(m, side, lambda step: 0):
                copy.start()
    gain_round(3)
    gain_round(4)
    gsum_ref[...] = gain_now[5]
    for side in range(2):
        for m in range(2):
            grads, out, keep, sib, a1, a2, b1, b2, zb, sems, z_sems = matrices[m]
            for copy in z_moves(m, side, lambda step: 0):
                copy.wait_send()
            for copy in z_moves(m, side, lambda step: -step):
                copy.wait_recv()
            held = (keep, sib)[side]
            wide = zb.shape[3]
            at_core = core if side == 0 else 1 - core
            rows = zb.shape[2]
            tall = min(32, rows)

            @pl.loop(0, rows // tall)
            def _(at):
                here = pl.ds(pl.multiple_of(at * tall, tall), tall)
                total = held[high, row, here, lanes(col, wide)].astype(jnp.float32)
                for step in range(1, cols):
                    total = total + zb[side, line(-step), here, :].astype(jnp.float32)
                out[at_core, here, :] = total

    for step in range(1, cols):
        token_copy(step, line(-step)).wait_recv()
        token_copy(step, col).wait_send()

    @pl.when(core != row)
    def _():
        token_copy(0, col).wait_recv()
        token_copy(0, col).wait_send()
        cross.wait()

    @pl.when(core == row)
    def _():
        own_tokens.wait()
        stay.wait()


def finish(input_grad, grad_q, grad_o, gains, output, cols):
    anywhere = pl.BlockSpec(memory_space=pl.ANY)
    in_vmem = pl.BlockSpec(memory_space=pltpu.VMEM)
    bf16, f32 = jnp.bfloat16, jnp.float32
    length, full = input_grad.shape
    rows = grad_q.shape[0] // 8

    def buffers(wide):
        return [
            pltpu.VMEM((2, 2, rows, wide), bf16),
            pltpu.VMEM((2, 2, rows, wide), bf16),
            pltpu.VMEM((2, rows, wide), bf16),
            pltpu.VMEM((rows, wide), bf16),
            pltpu.VMEM((2, rows, wide), bf16),
            pltpu.VMEM((rows, wide), bf16),
            pltpu.VMEM((2, cols, rows, wide // cols), bf16),
        ]

    wide_q, wide_o = grad_q.shape[1], grad_o.shape[1]
    return pl.pallas_call(
        functools.partial(finish_kernel, cols),
        out_shape=(
            jax.ShapeDtypeStruct((cols, length, full // cols), bf16),
            jax.ShapeDtypeStruct(output.shape, bf16),
            jax.ShapeDtypeStruct((2, rows, wide_q // cols), f32),
            jax.ShapeDtypeStruct((2, rows, wide_o // cols), f32),
            jax.ShapeDtypeStruct(gains.shape, f32),
        ),
        in_specs=[anywhere] * 5,
        out_specs=(anywhere, anywhere, in_vmem, in_vmem, in_vmem),
        scratch_shapes=buffers(wide_q)
        + buffers(wide_o)
        + [
            pltpu.VMEM((6,) + gains.shape, f32),
            pltpu.VMEM((5,) + gains.shape, f32),
            pltpu.SemaphoreType.DMA((2, cols)),
            pltpu.SemaphoreType.DMA((2, 5)),
            pltpu.SemaphoreType.DMA((2, 5)),
            pltpu.SemaphoreType.DMA((2, 5)),
            pltpu.SemaphoreType.DMA((2, 2, cols)),
            pltpu.SemaphoreType.DMA((2, 2, cols)),
            pltpu.SemaphoreType.DMA((2, 1)),
            pltpu.SemaphoreType.DMA((5,)),
        ],
        compiler_params=pltpu.CompilerParams(
            collective_id=3, has_side_effects=True, vmem_limit_bytes=40 << 20
        ),
        cost_estimate=pl.CostEstimate(flops=0, bytes_accessed=300 << 20, transcendentals=0),
        name="finish",
    )(
        input_grad,
        grad_q.reshape(2, 2, 2, rows, wide_q),
        grad_o.reshape(2, 2, 2, rows, wide_o),
        gains,
        output,
    )


def one_sequence_body(
    tokens,
    cotangent,
    lengths,
    deal_order,
    gain_attn,
    gain_ffn,
    w_query,
    key_value_weight,
    w_out,
    w_gate_up,
    w_down,
):
    seq_group, rows_local, width_local = tokens.shape
    row_count = lax.axis_size("row")
    col_count = lax.axis_size("col")
    full_width = width_local * col_count
    slot_len = rows_local * row_count
    group, core, mate, row, col = place()
    query_half = w_query.shape[1] // 2
    kv_half = key_value_weight.shape[2] // 2
    hidden = w_down.shape[1]

    def core_half(matrix, axis):
        width = matrix.shape[axis] // 2
        return lax.dynamic_slice_in_dim(matrix, core * width, width, axis)

    def joined(mine, other, at):
        return jnp.where(
            at == 0, jnp.concatenate([mine, other]), jnp.concatenate([other, mine])
        )

    def from_sibling(value):
        return lax.ppermute(value, "dp", SIBLINGS)

    def half_rows(matrix):
        return core_half(matrix, 0)

    pack_q = jnp.concatenate(
        [
            core_half(w_query, 1),
            core_half(key_value_weight[:, 0], 1),
            core_half(key_value_weight[:, 1], 1),
        ],
        axis=1,
    )
    pack_o = core_half(w_out, 1)
    gain_one = gain_attn.astype(jnp.float32)
    gain_two = gain_ffn.astype(jnp.float32)
    own_tokens, attn_input = start_exchange(tokens, gain_one, col_count)

    length = lax.dynamic_slice_in_dim(lengths, mate * seq_group + col, 1)
    given_pos = row * rows_local + jnp.arange(rows_local, dtype=jnp.int32)
    given_lengths = lax.dynamic_slice_in_dim(lengths, group * seq_group, seq_group)
    given_live = given_pos[None, :, None] < given_lengths[:, None, None]
    everyone = lax.all_gather(cotangent, "dp", axis=0, tiled=True)
    everyone, attn_input = lax.optimization_barrier((everyone, attn_input))
    picked = pick_sequences(everyone, deal_order, group * seq_group, seq_group)
    picked = jnp.where(given_live, picked, jnp.zeros_like(picked))
    given = lax.ppermute(picked, ("dp", "row"), CROSSED)
    weights_qkv, weights_out = gather_weights(pack_q, pack_o, picked, row_count, col_count)
    given, weights_qkv = lax.optimization_barrier((given, weights_qkv))
    line_cot = lax.all_gather(given, "col", axis=2, tiled=True)
    own_grad = lax.dynamic_index_in_dim(line_cot, col, keepdims=False).astype(jnp.float32)

    w_gate_up, w_down, weights_qkv = lax.optimization_barrier((w_gate_up, w_down, weights_qkv))
    far_gate_up = lax.ppermute(half_rows(w_gate_up), "row", OVER_X)
    far_down = lax.ppermute(half_rows(w_down), "row", OVER_X)
    own_mats = (w_gate_up[:, 0], w_gate_up[:, 1], w_down)

    cosine_table, sine_table = rope_tables(jnp.arange(slot_len, dtype=jnp.int32), HEAD_SIZE)
    cosine_table, sine_table = lax.optimization_barrier((cosine_table, sine_table))
    cosines = jnp.concatenate(
        [jnp.tile(cosine_table, (1, 6)), jnp.ones((slot_len, HEAD_SIZE), jnp.float32)], axis=1
    )
    turning = jnp.concatenate([-sine_table, sine_table], axis=1)
    sines = jnp.concatenate(
        [jnp.tile(turning, (1, 3)), jnp.zeros((slot_len, HEAD_SIZE), jnp.float32)], axis=1
    )
    own_float = own_tokens.astype(jnp.float32)
    scale_one = lax.rsqrt(jnp.mean(own_float * own_float, axis=1, keepdims=True) + EPSILON)
    projected, heads_out = attend_fast(
        length, attn_input, weights_qkv, cosines, sines, col_count
    )

    def summed_rows(partial):
        count = partial.shape[0] // 2
        mine = lax.dynamic_slice_in_dim(partial, core * count, count)
        other = lax.dynamic_slice_in_dim(partial, (1 - core) * count, count)
        return mine.astype(jnp.float32) + from_sibling(other).astype(jnp.float32)

    attn_rows = summed_rows(expand_local(heads_out, weights_out).astype(jnp.bfloat16))
    resid = own_float + RES_MULT * attn_rows
    scale_two = lax.rsqrt(jnp.mean(resid * resid, axis=1, keepdims=True) + EPSILON)
    own_ffn = (resid * scale_two * gain_two).astype(jnp.bfloat16)

    far_gate_up, far_down, own_ffn, own_mats = lax.optimization_barrier(
        (far_gate_up, far_down, own_ffn, own_mats)
    )
    far_mats = (far_gate_up[:, 0], far_gate_up[:, 1], far_down)
    sibling_mats = tuple(from_sibling(matrix) for matrix in far_mats)
    *unused, a_keep, a_send, b_keep, b_send = feed_forward(
        own_ffn,
        resid.astype(jnp.bfloat16),
        line_cot,
        own_mats + far_mats + sibling_mats,
        col_count,
    )
    mlp_part, back_part = unused[2:4]
    grad_normed_two = jnp.sum(back_part.astype(jnp.float32), axis=0)
    out_cols = lax.psum_scatter(mlp_part, "col", scatter_dimension=2, tiled=True)

    def plus(kept, came):
        return (kept.astype(jnp.float32) + came.astype(jnp.float32)).astype(jnp.bfloat16)

    a_came = lax.ppermute(a_send, "row", OVER_X)
    b_came = lax.ppermute(b_send, "dp", OVER_Y)

    weighted_two = grad_normed_two * gain_two
    inner_two = jnp.sum(weighted_two * resid, axis=1, keepdims=True)
    grad_resid = (
        own_grad + scale_two * weighted_two - resid * scale_two**3 * inner_two / full_width
    )
    gain_two_part = jnp.sum(grad_normed_two * resid * scale_two, axis=0)
    own_attn_grad = (RES_MULT * grad_resid).astype(jnp.bfloat16)
    grad_attn = joined(own_attn_grad, from_sibling(own_attn_grad), core)
    grad_heads = contract_local(grad_attn, weights_out).astype(jnp.bfloat16)
    grad_out = token_outer(grad_attn, heads_out).astype(jnp.bfloat16)
    grad_projected = attend_back_fast(
        length, projected, grad_heads, cosines, sines, col_count
    )
    grad_normed_one = summed_rows(expand_local(grad_projected, weights_qkv).astype(jnp.bfloat16))
    grad_qkv = token_outer(attn_input, grad_projected).astype(jnp.bfloat16)
    weighted_one = grad_normed_one * gain_one
    inner_one = jnp.sum(weighted_one * own_float, axis=1, keepdims=True)
    own_input_grad = (
        grad_resid
        + scale_one * weighted_one
        - own_float * scale_one**3 * inner_one / full_width
    ).astype(jnp.bfloat16)
    gain_one_part = jnp.sum(grad_normed_one * own_float * scale_one, axis=0)
    a_sum, b_sum, own_input_grad = lax.optimization_barrier(
        (plus(a_keep, a_came), plus(b_keep, b_came), own_input_grad)
    )
    high = group // 2

    def one_of(pair, at):
        return lax.dynamic_index_in_dim(pair, at, keepdims=False)

    a_last = lax.ppermute(one_of(a_sum, 1 - high), "dp", OVER_Y)
    b_last = lax.ppermute(one_of(b_sum, 1 - row), "row", OVER_X)
    gains = jnp.stack([gain_one_part, gain_two_part]).reshape(8, -1)
    given_grad, given_out, sums_q, sums_o, gain_sums = finish(
        own_input_grad, grad_qkv, grad_out, gains, out_cols, col_count
    )
    layer_out = jnp.where(given_live, given_out.astype(jnp.float32), 0.0)
    input_grad = given_grad.astype(jnp.float32)
    a_total = one_of(a_sum, high).astype(jnp.float32) + a_last.astype(jnp.float32)
    b_total = one_of(b_sum, row).astype(jnp.float32) + b_last.astype(jnp.float32)
    sums_gate_up = jnp.stack([a_total[:, :hidden], b_total[:, :hidden]], axis=1)
    sums_down = jnp.concatenate([a_total[:, hidden:], b_total[:, hidden:]], axis=1)
    grad_gain_attn, grad_gain_ffn = gain_sums.reshape(2, full_width)

    def both_cores(sums):
        return jnp.concatenate([sums[0], sums[1]], axis=1)

    qk = query_half + kv_half
    out_query = both_cores(sums_q[:, :, :query_half])
    out_kv = jnp.stack(
        [
            both_cores(sums_q[:, :, query_half:qk]),
            both_cores(sums_q[:, :, qk:]),
        ],
        axis=1,
    )
    out_out = both_cores(sums_o)
    return (
        layer_out,
        input_grad,
        out_query,
        out_kv,
        out_out,
        sums_gate_up,
        sums_down,
        grad_gain_attn,
        grad_gain_ffn,
    )


def general_body(
    tokens,
    cotangent,
    lengths,
    deal_order,
    gain_attn,
    gain_ffn,
    w_query,
    key_value_weight,
    w_out,
    w_gate_up,
    w_down,
):
    seq_group, rows_local, width_local = tokens.shape
    row_count = lax.axis_size("row")
    col_count = lax.axis_size("col")
    full_width = width_local * col_count
    slot_len = rows_local * row_count
    total_rows = seq_group * rows_local
    head_size = HEAD_SIZE
    query_width = w_query.shape[1]
    kv_width = key_value_weight.shape[2]
    kv_heads = kv_width // head_size
    group_size = query_width // kv_width
    group_index = lax.axis_index("dp")
    row_index = lax.axis_index("row")
    col_index = lax.axis_index("col")
    matrices = {
        "qkv": jnp.concatenate(
            [w_query, key_value_weight.reshape(key_value_weight.shape[0], 2 * kv_width)], axis=1
        ),
        "out": w_out,
        "gate_up": w_gate_up,
        "down": w_down,
    }

    def contract_with(operand, which_one):
        return contract_rows(operand, matrices[which_one])

    def expand_with(operand, which_one):
        return expand_rows(operand, matrices[which_one])

    own_cotangent = bring_cotangent(cotangent, deal_order, group_index * seq_group)
    own_rows = tokens
    seq_lens = lax.dynamic_slice_in_dim(lengths, group_index * seq_group, seq_group)
    local_pos = row_index * rows_local + jnp.arange(rows_local, dtype=jnp.int32)
    key_pos = jnp.arange(slot_len, dtype=jnp.int32)
    live_rows = (local_pos[None, :] < seq_lens[:, None]).astype(jnp.float32).reshape(total_rows, 1)
    cosine_table, sine_table = rope_tables(jnp.tile(local_pos, seq_group), head_size)
    own_tokens = own_rows.reshape(total_rows, width_local)
    wide_float = widen_cols(own_tokens).astype(jnp.float32)
    scale_one = lax.rsqrt(jnp.mean(wide_float * wide_float, axis=1, keepdims=True) + EPSILON)
    gain_one = gain_attn.astype(jnp.float32)
    first_normed = wide_float * scale_one
    attn_input = (first_normed * gain_one).astype(jnp.bfloat16)
    projected = contract_with(attn_input, "qkv")
    query_lin = projected[:, :query_width].reshape(total_rows, query_width // head_size, head_size)
    key_lin = projected[:, query_width : query_width + kv_width].reshape(
        total_rows, kv_heads, head_size
    )
    value_lin = projected[:, query_width + kv_width :]
    query_rows = rotary_embed(query_lin, cosine_table, sine_table).astype(jnp.bfloat16)
    keys_own = (
        rotary_embed(key_lin, cosine_table, sine_table)
        .astype(jnp.bfloat16)
        .reshape(seq_group, rows_local, kv_width)
    )
    values_own = value_lin.astype(jnp.bfloat16).reshape(seq_group, rows_local, kv_width)
    all_keys, all_values = (
        lax.all_gather(keys_own, "row", axis=1, tiled=True),
        lax.all_gather(values_own, "row", axis=1, tiled=True),
    )
    query_split = query_rows.reshape(seq_group, rows_local, kv_heads, group_size, head_size)
    key_split = all_keys.reshape(seq_group, slot_len, kv_heads, head_size)
    value_split = all_values.reshape(seq_group, slot_len, kv_heads, head_size)

    def forward_seq(inputs):
        return attend(inputs, key_pos, local_pos)

    mixed_heads, row_max, row_sums = lax.map(
        forward_seq, (query_split, key_split, value_split, seq_lens)
    )
    heads_out = mixed_heads.reshape(total_rows, query_width).astype(jnp.bfloat16)
    attn_local = narrow_cols(expand_with(heads_out, "out"))
    resid = own_tokens.astype(jnp.float32) + RES_MULT * attn_local
    gain_two = lax.dynamic_slice_in_dim(
        gain_ffn.astype(jnp.float32), col_index * width_local, width_local
    )
    scale_two = lax.rsqrt(sum_over_cols(jnp.sum(resid * resid, axis=1)) / full_width + EPSILON)[
        :, None
    ]
    normed_two = resid * scale_two
    ffn_input = widen_cols((normed_two * gain_two).astype(jnp.bfloat16))
    gate_up = contract_with(ffn_input, "gate_up")
    gate = gate_up[:, 0]
    upward = gate_up[:, 1]
    sigmoid_gate = jax.nn.sigmoid(gate)
    silu_gate = gate * sigmoid_gate
    hidden = (silu_gate * upward).astype(jnp.bfloat16)
    ffn_local = narrow_cols(expand_with(hidden, "down"))
    layer_out = live_rows * (resid + RES_MULT * ffn_local)
    grad_rows = live_rows * own_cotangent.reshape(total_rows, width_local).astype(jnp.float32)
    grad_ffn = widen_cols((RES_MULT * grad_rows).astype(jnp.bfloat16))
    grad_hidden = contract_with(grad_ffn, "down")
    grad_down = token_outer(grad_ffn, hidden)
    slope = sigmoid_gate * (1.0 + gate * (1.0 - sigmoid_gate))
    grad_gate_rows = jnp.stack(
        [grad_hidden * upward * slope, grad_hidden * silu_gate], axis=1
    ).astype(jnp.bfloat16)
    grad_gate_up = token_outer(ffn_input, grad_gate_rows)
    grad_normed_two = narrow_cols(expand_with(grad_gate_rows, "gate_up"))
    weighted_two = grad_normed_two * gain_two
    inner_two = sum_over_cols(jnp.sum(weighted_two * resid, axis=1))[:, None]
    grad_resid = (
        grad_rows + scale_two * weighted_two - resid * scale_two**3 * inner_two / full_width
    )
    gain_two_part = jnp.sum(grad_normed_two * normed_two, axis=0)
    grad_attn = widen_cols((RES_MULT * grad_resid).astype(jnp.bfloat16))
    grad_heads = contract_with(grad_attn, "out").astype(jnp.bfloat16)
    grad_out = token_outer(grad_attn, heads_out)
    grad_split = grad_heads.reshape(seq_group, rows_local, kv_heads, group_size, head_size)

    def backward_seq(inputs):
        return attend_back(inputs, key_pos, local_pos)

    grad_query, grad_key, grad_value = lax.map(
        backward_seq, (query_split, key_split, value_split, grad_split, row_max, row_sums, seq_lens)
    )
    key_part, value_part = (
        lax.psum_scatter(
            grad_key.reshape(seq_group, slot_len, kv_width).astype(jnp.bfloat16),
            "row",
            scatter_dimension=1,
            tiled=True,
        ).astype(jnp.float32),
        lax.psum_scatter(
            grad_value.reshape(seq_group, slot_len, kv_width).astype(jnp.bfloat16),
            "row",
            scatter_dimension=1,
            tiled=True,
        ).astype(jnp.float32),
    )
    query_back = rotary_embed(
        grad_query.reshape(total_rows, query_width // head_size, head_size),
        cosine_table,
        -sine_table,
    ).reshape(total_rows, query_width)
    key_back = rotary_embed(
        key_part.reshape(total_rows, kv_heads, head_size), cosine_table, -sine_table
    ).reshape(total_rows, kv_width)
    grad_projected = jnp.concatenate(
        [query_back, key_back, value_part.reshape(total_rows, kv_width)], axis=1
    ).astype(jnp.bfloat16)
    grad_qkv = token_outer(attn_input, grad_projected)
    grad_normed_one = expand_with(grad_projected, "qkv")
    weighted_one = grad_normed_one * gain_one
    inner_one = jnp.sum(weighted_one * wide_float, axis=1, keepdims=True)
    input_part = scale_one * weighted_one - wide_float * scale_one**3 * inner_one / full_width
    input_grad = grad_resid + narrow_cols(input_part)
    gain_one_part = jnp.sum(grad_normed_one * first_normed, axis=0)
    gain_two_full = lax.dynamic_update_slice_in_dim(
        jnp.zeros((full_width,), jnp.float32), gain_two_part, col_index * width_local, 0
    )
    grad_gain_attn, grad_gain_ffn = lax.psum((gain_one_part, gain_two_full), ("dp", "row", "col"))
    sums_qkv, sums_out, sums_gate_up, sums_down = (
        lax.psum_scatter(
            grad_qkv.astype(jnp.bfloat16), ("dp", "row"), scatter_dimension=0, tiled=True
        ).astype(jnp.float32),
        lax.psum_scatter(
            grad_out.astype(jnp.bfloat16), ("dp", "row"), scatter_dimension=0, tiled=True
        ).astype(jnp.float32),
        lax.psum_scatter(
            grad_gate_up.astype(jnp.bfloat16), ("dp", "row"), scatter_dimension=0, tiled=True
        ).astype(jnp.float32),
        lax.psum_scatter(
            grad_down.astype(jnp.bfloat16), ("dp", "row"), scatter_dimension=0, tiled=True
        ).astype(jnp.float32),
    )
    out_query = sums_qkv[:, :query_width]
    out_kv = sums_qkv[:, query_width:].reshape(sums_qkv.shape[0], 2, kv_width)
    return (
        layer_out.reshape(seq_group, rows_local, width_local),
        input_grad.reshape(seq_group, rows_local, width_local),
        out_query,
        out_kv,
        sums_out,
        sums_gate_up,
        sums_down,
        grad_gain_attn,
        grad_gain_ffn,
    )


def body(tokens, cotangent, lengths, deal_order, gain_attn, gain_ffn, w_query, key_value_weight, *rest):
    sizes = (lax.axis_size("dp"), lax.axis_size("row"), lax.axis_size("col"))
    one_each = sizes == (4, 2, 4) and tokens.shape[0] == sizes[2]
    pairs = w_query.shape[1] == 8 * HEAD_SIZE and key_value_weight.shape[2] == 2 * HEAD_SIZE
    chosen = one_sequence_body if one_each and pairs else general_body
    return chosen(
        tokens, cotangent, lengths, deal_order, gain_attn, gain_ffn, w_query, key_value_weight, *rest
    )


def solution(mesh):
    placed = (
        P("dp", "row", "col"),
        P("dp", "row", "col"),
        P(),
        P(),
        P(),
        P(),
        P("row", "col"),
        P("row", None, "col"),
        P("row", "col"),
        P("row", None, "col"),
        P("row", "col"),
    )
    return jax.shard_map(
        body,
        mesh=mesh,
        in_specs=placed,
        out_specs=(
            P("dp", "row", "col"),
            P("dp", "row", "col"),
            P(("dp", "row"), "col"),
            P(("dp", "row"), None, "col"),
            P(("dp", "row"), "col"),
            P(("dp", "row"), None, "col"),
            P(("dp", "row"), "col"),
            P(),
            P(),
        ),
        check_vma=False,
    )
```

```python
import functools

import jax
import jax.numpy as jnp
from jax import lax
from jax.experimental import pallas as pl
from jax.experimental.pallas import tpu as pltpu
from jax.sharding import PartitionSpec as P

HEAD_SIZE = 64


EPSILON = 1e-05
THETA = 10000000.0
ATTN_MULT = 0.015625
RES_MULT = 0.22
MASKED = -1e30


def rope_tables(positions, head_size):
    halves = jnp.arange(head_size // 2, dtype=jnp.float32)
    inverse_freq = THETA ** (-(halves * 2.0) / head_size)
    angles = positions.astype(jnp.float32)[:, None] * inverse_freq[None, :]
    return (jnp.cos(angles), jnp.sin(angles))


def rotary_embed(value_rows, cosine_table, sine_table):
    middle = value_rows.shape[-1] // 2
    first_half = value_rows[..., :middle]
    second_half = value_rows[..., middle:]
    cos_part = cosine_table[:, None, :]
    sin_part = sine_table[:, None, :]
    return jnp.concatenate(
        [
            first_half * cos_part - second_half * sin_part,
            second_half * cos_part + first_half * sin_part,
        ],
        axis=-1,
    )


def widen_cols(value_rows):
    return lax.all_gather(value_rows, "col", axis=1, tiled=True)


def narrow_cols(value_rows):
    return lax.psum_scatter(value_rows, "col", scatter_dimension=1, tiled=True)


def sum_over_cols(value_rows):
    return lax.psum(value_rows, "col")


def contract_local(operand, matrix):
    return lax.dot_general(
        operand, matrix, (((1,), (0,)), ((), ())), preferred_element_type=jnp.float32
    )


def expand_local(operand, matrix):
    trailing = tuple(range(1, operand.ndim))
    return lax.dot_general(
        operand, matrix, ((trailing, trailing), ((), ())), preferred_element_type=jnp.float32
    )


def token_outer(features, grads):
    return lax.dot_general(
        features, grads, (((0,), (0,)), ((), ())), preferred_element_type=jnp.float32
    )


def contract_rows(operand, matrix):
    return contract_local(operand, lax.all_gather(matrix, "row", axis=0, tiled=True))


def expand_rows(operand, matrix):
    return expand_local(operand, lax.all_gather(matrix, "row", axis=0, tiled=True))


def split_keys(key_seq, value_seq, key_pos):
    slot_len = key_seq.shape[0]
    width = min(512, slot_len)
    count = slot_len // width
    return (
        key_seq.reshape(count, width, key_seq.shape[1], key_seq.shape[2]),
        value_seq.reshape(count, width, value_seq.shape[1], value_seq.shape[2]),
        key_pos.reshape(count, width),
    )


def block_scores(query_seq, key_block, pos_block, query_pos, length):
    scores = (
        jnp.einsum("qkgd,tkd->kgqt", query_seq, key_block, preferred_element_type=jnp.float32)
        * ATTN_MULT
    )
    allowed = (pos_block[None, :] <= query_pos[:, None]) & (pos_block[None, :] < length)
    return jnp.where(allowed, scores, MASKED)


def attend(inputs, key_pos, query_pos):
    query_seq, key_seq, value_seq, length = inputs
    key_blocks, value_blocks, pos_blocks = split_keys(key_seq, value_seq, key_pos)
    stat_shape = (query_seq.shape[1], query_seq.shape[2], query_seq.shape[0], 1)

    def gather_stats(carry, entry):
        running_max, running_sum = carry
        key_block, pos_block = entry
        scores = block_scores(query_seq, key_block, pos_block, query_pos, length)
        new_max = jnp.maximum(running_max, jnp.max(scores, axis=-1, keepdims=True))
        new_sum = running_sum * jnp.exp(running_max - new_max) + jnp.sum(
            jnp.exp(scores - new_max), axis=-1, keepdims=True
        )
        return ((new_max, new_sum), None)

    start_stats = (jnp.full(stat_shape, MASKED, jnp.float32), jnp.zeros(stat_shape, jnp.float32))
    (row_max, row_sums), unused = lax.scan(gather_stats, start_stats, (key_blocks, pos_blocks))

    def mix_values(running, entry):
        key_block, value_block, pos_block = entry
        scores = block_scores(query_seq, key_block, pos_block, query_pos, length)
        weights = jnp.exp(scores - row_max) / row_sums
        return (
            running
            + jnp.einsum(
                "kgqt,tkd->qkgd",
                weights.astype(jnp.bfloat16),
                value_block,
                preferred_element_type=jnp.float32,
            ),
            None,
        )

    start_mix = jnp.zeros(query_seq.shape, jnp.float32)
    mixed_heads, unused = lax.scan(mix_values, start_mix, (key_blocks, value_blocks, pos_blocks))
    return (mixed_heads, row_max, row_sums)


def attend_back(inputs, key_pos, query_pos):
    query_seq, key_seq, value_seq, grad_mixed, row_max, row_sums, length = inputs
    key_blocks, value_blocks, pos_blocks = split_keys(key_seq, value_seq, key_pos)

    def block_weights(key_block, value_block, pos_block):
        scores = block_scores(query_seq, key_block, pos_block, query_pos, length)
        weights = jnp.exp(scores - row_max) / row_sums
        grad_weights = jnp.einsum(
            "qkgd,tkd->kgqt", grad_mixed, value_block, preferred_element_type=jnp.float32
        )
        return (weights, grad_weights)

    def gather_centre(running, entry):
        weights, grad_weights = block_weights(*entry)
        return (running + jnp.sum(weights * grad_weights, axis=-1, keepdims=True), None)

    start_centre = jnp.zeros(row_max.shape, jnp.float32)
    centre, unused = lax.scan(gather_centre, start_centre, (key_blocks, value_blocks, pos_blocks))

    def grads_block(running, entry):
        key_block = entry[0]
        weights, grad_weights = block_weights(*entry)
        grad_scores = (weights * (grad_weights - centre)).astype(jnp.bfloat16)
        grad_query = (
            running
            + jnp.einsum(
                "kgqt,tkd->qkgd", grad_scores, key_block, preferred_element_type=jnp.float32
            )
            * ATTN_MULT
        )
        grad_key = (
            jnp.einsum("kgqt,qkgd->tkd", grad_scores, query_seq, preferred_element_type=jnp.float32)
            * ATTN_MULT
        )
        grad_value = jnp.einsum(
            "kgqt,qkgd->tkd",
            weights.astype(jnp.bfloat16),
            grad_mixed,
            preferred_element_type=jnp.float32,
        )
        return (grad_query, (grad_key, grad_value))

    start_query = jnp.zeros(query_seq.shape, jnp.float32)
    grad_query, (grad_key, grad_value) = lax.scan(
        grads_block, start_query, (key_blocks, value_blocks, pos_blocks)
    )
    return (grad_query, grad_key.reshape(key_seq.shape), grad_value.reshape(value_seq.shape))


MESH_IDS = pl.DeviceIdType.MESH
SIBLINGS = [(0, 1), (1, 0), (2, 3), (3, 2)]
OVER_X = [(0, 1), (1, 0)]
OVER_Y = [(0, 2), (2, 0), (1, 3), (3, 1)]
CROSSED = [((2 * y + c) * 2 + x, (2 * y + x) * 2 + c) for y in (0, 1) for c in (0, 1) for x in (0, 1)]


def pick_sequences(everyone, deal_order, first, count):
    slots = jnp.arange(deal_order.shape[0], dtype=jnp.int32)
    inverse = jnp.sum(jnp.where(deal_order[None, :] == slots[:, None], slots[None, :], 0), axis=1)
    return jnp.concatenate(
        [
            lax.dynamic_slice_in_dim(
                everyone, lax.dynamic_index_in_dim(inverse, first + at, keepdims=False), 1
            )
            for at in range(count)
        ]
    )


def bring_cotangent(cotangent, deal_order, first):
    everyone = lax.all_gather(cotangent, "dp", axis=0, tiled=True)
    return pick_sequences(everyone, deal_order, first, cotangent.shape[0])


def place():
    group = lax.axis_index("dp")
    core = lax.rem(group, 2)
    row = lax.axis_index("row")
    return group, core, group - core + row, row, lax.axis_index("col")


def lined(index, step, count):
    return lax.rem(index + step + count, count)


def aligned(block, size):
    return pl.ds(pl.multiple_of(block * size, size), size)


def greet(device):
    pl.semaphore_signal(
        pltpu.get_barrier_semaphore(), inc=1, device_id=device, device_id_type=MESH_IDS
    )


def remote(src, dst, sems, at, device):
    return pltpu.make_async_remote_copy(
        src_ref=src,
        dst_ref=dst,
        send_sem=sems.at[0, at],
        recv_sem=sems.at[1, at],
        device_id=device,
        device_id_type=MESH_IDS,
    )


def line_order(col, last, at):
    inner_low = jnp.where(at < 2, 1 - at, at)
    inner_high = jnp.where(at == 3, 0, jnp.where(at == 0, 2, jnp.where(at == 1, 1, 3)))
    return jnp.where(
        col == 0, at, jnp.where(col == last, last - at, jnp.where(col == 1, inner_low, inner_high))
    )


def start_kernel(
    cols, tok_ref, gain_ref, x_ref, a_ref, x_buf, a_buf, tok_sems, a_sems, local_sems
):
    group, core, mate, row, col = place()
    width = tok_ref.shape[2]
    length = x_buf.shape[0]
    sibling = (group + 1 - 2 * core, row, col)

    def line(step):
        return lined(col, step, cols)

    for step in range(1, cols):
        greet((mate, core, line(step)))
    greet(sibling)

    @pl.when(core != row)
    def _():
        greet((mate, core, col))

    pl.semaphore_wait(pltpu.get_barrier_semaphore(), cols + (core - row) * (core - row))

    def token_copy(step, into):
        return remote(
            tok_ref.at[line(step)],
            x_buf.at[:, aligned(into, width)],
            tok_sems,
            step,
            (mate, core, line(step)),
        )

    own_tokens = pltpu.make_async_copy(
        tok_ref.at[col], x_buf.at[:, aligned(col, width)], local_sems.at[0]
    )
    for step in range(1, cols):
        token_copy(step, col).start()

    @pl.when(core != row)
    def _():
        token_copy(0, col).start()

    @pl.when(core == row)
    def _():
        own_tokens.start()

    for step in range(1, cols):
        token_copy(step, line(-step)).wait_recv()

    @pl.when(core != row)
    def _():
        token_copy(0, col).wait_recv()

    @pl.when(core == row)
    def _():
        own_tokens.wait()

    keep_x = pltpu.make_async_copy(x_buf, x_ref, local_sems.at[1])
    keep_x.start()
    tall = min(64, length)

    @pl.loop(0, length // tall)
    def _(at):
        here = aligned(at, tall)
        now = x_buf[here, :].astype(jnp.float32)
        scale = lax.rsqrt(jnp.mean(now * now, axis=1, keepdims=True) + EPSILON)
        a_buf[here, :] = (now * scale * gain_ref[...]).astype(jnp.bfloat16)

    def a_copy(of_core):
        return remote(a_buf, a_ref.at[aligned(of_core, length)], a_sems, 0, sibling)

    own_a = pltpu.make_async_copy(a_buf, a_ref.at[aligned(core, length)], local_sems.at[2])
    a_copy(core).start()
    own_a.start()
    for step in range(1, cols):
        token_copy(step, col).wait_send()

    @pl.when(core != row)
    def _():
        token_copy(0, col).wait_send()

    keep_x.wait()
    own_a.wait()
    a_copy(core).wait_send()
    a_copy(1 - core).wait_recv()


def start_exchange(tokens, gain, cols):
    anywhere = pl.BlockSpec(memory_space=pl.ANY)
    seqs, length, width = tokens.shape
    full = width * cols
    return pl.pallas_call(
        functools.partial(start_kernel, cols),
        out_shape=(
            jax.ShapeDtypeStruct((length, full), tokens.dtype),
            jax.ShapeDtypeStruct((2 * length, full), tokens.dtype),
        ),
        in_specs=[anywhere, pl.BlockSpec(memory_space=pltpu.VMEM)],
        out_specs=(anywhere,) * 2,
        scratch_shapes=[
            pltpu.VMEM((length, full), tokens.dtype),
            pltpu.VMEM((length, full), tokens.dtype),
            pltpu.SemaphoreType.DMA((2, cols)),
            pltpu.SemaphoreType.DMA((2, 1)),
            pltpu.SemaphoreType.DMA((3,)),
        ],
        compiler_params=pltpu.CompilerParams(
            collective_id=1, has_side_effects=True, vmem_limit_bytes=16 << 20
        ),
        cost_estimate=pl.CostEstimate(flops=0, bytes_accessed=200 << 20, transcendentals=0),
        name="start_exchange",
    )(tokens, gain.reshape(1, full))


def gather_kernel(cols, own_ref, after_ref, full_ref, send, recv, over_sems, local_sem):
    group, core, mate, row, col = place()
    last = cols - 1
    over = (group, 1 - row, col)
    tall, wide = own_ref.shape
    greet(over)

    @pl.when(col < last)
    def _():
        greet((group, row, col + 1))

    @pl.when(col > 0)
    def _():
        greet((group, row, col - 1))

    pl.semaphore_wait(
        pltpu.get_barrier_semaphore(),
        1 + jnp.minimum(col, 1) + jnp.minimum(last - col, 1),
    )

    def block(of_row, of_col):
        return full_ref.at[aligned(of_row, tall), aligned(of_col, wide)]

    def along(src, chunk, to, way):
        return pltpu.make_async_remote_copy(
            src_ref=src,
            dst_ref=block(row, chunk),
            send_sem=send.at[way, chunk],
            recv_sem=recv.at[chunk],
            device_id=(group, row, to),
            device_id_type=MESH_IDS,
        )

    def across(src, of_row, chunk):
        return remote(src, block(of_row, chunk), over_sems, chunk, over)

    @pl.when(col < last)
    def _():
        along(own_ref, col, col + 1, 0).start()

    @pl.when(col > 0)
    def _():
        along(own_ref, col, col - 1, 1).start()

    across(own_ref, row, col).start()
    own_copy = pltpu.make_async_copy(own_ref, block(row, col), local_sem)
    own_copy.start()
    for at in range(1, cols):
        chunk = line_order(col, last, at)
        along(own_ref, chunk, col, 0).wait_recv()

        @pl.when((chunk < col) & (col < last))
        def _():
            along(block(row, chunk), chunk, col + 1, 0).start()

        @pl.when((chunk > col) & (col > 0))
        def _():
            along(block(row, chunk), chunk, col - 1, 1).start()

        across(block(row, chunk), row, chunk).start()
    own_copy.wait()
    for chunk in range(cols):

        @pl.when((col >= chunk) & (col < last))
        def _():
            along(own_ref, chunk, col + 1, 0).wait_send()

        @pl.when((col <= chunk) & (col > 0))
        def _():
            along(own_ref, chunk, col - 1, 1).wait_send()

        across(own_ref, row, chunk).wait_send()
        across(own_ref, 1 - row, chunk).wait_recv()


def gather_weights(own, after, rows, cols, collective_id):
    anywhere = pl.BlockSpec(memory_space=pl.ANY)
    return pl.pallas_call(
        functools.partial(gather_kernel, cols),
        out_shape=jax.ShapeDtypeStruct((own.shape[0] * rows, own.shape[1] * cols), own.dtype),
        in_specs=[anywhere] * 2,
        out_specs=anywhere,
        scratch_shapes=[
            pltpu.SemaphoreType.DMA((2, cols)),
            pltpu.SemaphoreType.DMA((cols,)),
            pltpu.SemaphoreType.DMA((2, cols)),
            pltpu.SemaphoreType.DMA(()),
        ],
        compiler_params=pltpu.CompilerParams(collective_id=collective_id, has_side_effects=True),
        cost_estimate=pl.CostEstimate(flops=0, bytes_accessed=200 << 20, transcendentals=0),
        name="gather_weights",
    )(own, after)


def half_turn(wide):
    lanes = wide.shape[1]
    half = HEAD_SIZE // 2
    lane = lax.broadcasted_iota(jnp.int32, wide.shape, 1)
    return jnp.where(
        lax.rem(lane, HEAD_SIZE) < half,
        pltpu.roll(wide, lanes - half, 1),
        pltpu.roll(wide, half, 1),
    )


def both_heads(pair):
    lane = lax.broadcasted_iota(jnp.int32, pair.shape, 1)
    turned = pltpu.roll(pair, HEAD_SIZE, 1)
    low = lane < HEAD_SIZE
    return jnp.where(low, pair, turned), jnp.where(low, turned, pair)


def keep_head(pair, side):
    lane = lax.broadcasted_iota(jnp.int32, pair.shape, 1)
    mine = lane < HEAD_SIZE if side == 0 else lane >= HEAD_SIZE
    return jnp.where(mine, pair, jnp.zeros_like(pair))


def dot_nn(a, b):
    return lax.dot_general(a, b, (((1,), (0,)), ((), ())), preferred_element_type=jnp.float32)


def dot_nt(a, b):
    return lax.dot_general(a, b, (((1,), (1,)), ((), ())), preferred_element_type=jnp.float32)


def dot_tn(a, b):
    return lax.dot_general(a, b, (((0,), (0,)), ((), ())), preferred_element_type=jnp.float32)


PAIR = 2 * HEAD_SIZE


def attend_kernel(block, len_ref, a_ref, w_ref, cos_ref, sin_ref, qkv_ref, z_ref, q_all, k_two, v_two):
    rows = a_ref.shape[0]
    heads = q_all.shape[0]
    length = len_ref[0]

    @pl.loop(0, rows // block)
    def _(at):
        here = pl.ds(pl.multiple_of(at * block, block), block)
        lin = dot_nn(a_ref[here, :], w_ref[...])
        for part in range(heads // 2 + 1):
            lanes = slice(part * PAIR, (part + 1) * PAIR)
            now = lin[:, lanes]
            table = slice(0, PAIR) if part < heads // 2 else slice(PAIR, 2 * PAIR)
            now = now * cos_ref[here, table] + half_turn(now) * sin_ref[here, table]
            qkv_ref[here, lanes] = now.astype(jnp.bfloat16)
            if part < heads // 2:
                for side in range(2):
                    q_all[2 * part + side, here, :] = keep_head(now * ATTN_MULT, side).astype(
                        jnp.bfloat16
                    )
            else:
                keys, values = both_heads(now)
                k_two[here, :] = keys.astype(jnp.bfloat16)
                v_two[here, :] = values.astype(jnp.bfloat16)

    for at in range(rows // block):
        here = slice(at * block, (at + 1) * block)
        upto = (at + 1) * block
        row = lax.broadcasted_iota(jnp.int32, (block, upto), 0) + at * block
        key = lax.broadcasted_iota(jnp.int32, (block, upto), 1)
        allowed = key < jnp.minimum(row + 1, length)

        def one_head(head):
            scores = dot_nt(q_all[head, here, :], k_two[:upto, :])
            scores = jnp.where(allowed, scores, MASKED)
            top = jnp.max(scores, axis=1, keepdims=True)
            power = jnp.exp(scores - top)
            total = jnp.sum(power, axis=1, keepdims=True)
            return dot_nn(power.astype(jnp.bfloat16), v_two[:upto, :]) / total

        for pair in range(heads // 2):
            low = one_head(2 * pair)
            high = one_head(2 * pair + 1)
            lane = lax.broadcasted_iota(jnp.int32, low.shape, 1)
            z_ref[here, pair * PAIR : (pair + 1) * PAIR] = jnp.where(
                lane < HEAD_SIZE, low, high
            ).astype(jnp.bfloat16)


def attend_fast(length, inputs, weights, cosines, sines, groups):
    rows, depth = inputs.shape
    wide = weights.shape[1] // groups
    heads = (wide - PAIR) // HEAD_SIZE
    block = min(256, rows)
    return pl.pallas_call(
        functools.partial(attend_kernel, block),
        grid=(groups,),
        out_shape=(
            jax.ShapeDtypeStruct((rows, groups * wide), jnp.bfloat16),
            jax.ShapeDtypeStruct((rows, groups * heads * HEAD_SIZE), jnp.bfloat16),
        ),
        in_specs=[
            pl.BlockSpec(memory_space=pltpu.SMEM),
            pl.BlockSpec((rows, depth), lambda g: (0, 0)),
            pl.BlockSpec((depth, wide), lambda g: (0, g)),
            pl.BlockSpec((rows, 2 * PAIR), lambda g: (0, 0)),
            pl.BlockSpec((rows, 2 * PAIR), lambda g: (0, 0)),
        ],
        out_specs=(
            pl.BlockSpec((rows, wide), lambda g: (0, g)),
            pl.BlockSpec((rows, heads * HEAD_SIZE), lambda g: (0, g)),
        ),
        scratch_shapes=[
            pltpu.VMEM((heads, rows, PAIR), jnp.bfloat16),
            pltpu.VMEM((rows, PAIR), jnp.bfloat16),
            pltpu.VMEM((rows, PAIR), jnp.bfloat16),
        ],
        compiler_params=pltpu.CompilerParams(vmem_limit_bytes=48 << 20),
        cost_estimate=pl.CostEstimate(
            flops=2 * rows * depth * wide * groups + 2 * groups * heads * rows * rows * 128,
            bytes_accessed=2 * (rows * depth + depth * wide * groups + rows * wide * groups),
            transcendentals=groups * heads * rows * rows // 2,
        ),
        name="attend",
    )(length, inputs, weights, cosines, sines)


def attend_back_kernel(
    block, len_ref, qkv_ref, dz_ref, cos_ref, sin_ref, out_ref, q_all, z_all, k_two, v_two, k_acc, v_acc
):
    rows = qkv_ref.shape[0]
    heads = q_all.shape[0]
    length = len_ref[0]

    @pl.loop(0, rows // block)
    def _(at):
        here = pl.ds(pl.multiple_of(at * block, block), block)
        for part in range(heads // 2):
            lanes = slice(part * PAIR, (part + 1) * PAIR)
            queries = qkv_ref[here, lanes].astype(jnp.float32) * ATTN_MULT
            mixed = dz_ref[here, lanes].astype(jnp.float32)
            for side in range(2):
                q_all[2 * part + side, here, :] = keep_head(queries, side).astype(jnp.bfloat16)
                z_all[2 * part + side, here, :] = keep_head(mixed, side).astype(jnp.bfloat16)
        keys, values = both_heads(qkv_ref[here, heads * HEAD_SIZE :].astype(jnp.float32))
        k_two[here, :] = keys.astype(jnp.bfloat16)
        v_two[here, :] = values.astype(jnp.bfloat16)
        k_acc[here, :] = jnp.zeros((block, PAIR), jnp.float32)
        v_acc[here, :] = jnp.zeros((block, PAIR), jnp.float32)

    def turn_back(now, here, table):
        return (now * cos_ref[here, table] - half_turn(now) * sin_ref[here, table]).astype(
            jnp.bfloat16
        )

    for at in range(rows // block):
        here = slice(at * block, (at + 1) * block)
        upto = (at + 1) * block
        key = lax.broadcasted_iota(jnp.int32, (upto, block), 0)
        query = lax.broadcasted_iota(jnp.int32, (upto, block), 1) + at * block
        allowed = key < jnp.minimum(query + 1, length)

        def one_head(head):
            queries, mixed = q_all[head, here, :], z_all[head, here, :]
            scores = jnp.where(allowed, dot_nt(k_two[:upto, :], queries), MASKED)
            power = jnp.exp(scores - jnp.max(scores, axis=0, keepdims=True))
            weights = power * (1.0 / jnp.sum(power, axis=0, keepdims=True))
            back = dot_nt(v_two[:upto, :], mixed)
            centre = jnp.sum(weights * back, axis=0, keepdims=True)
            slope = (weights * (back - centre)).astype(jnp.bfloat16)
            k_acc[:upto, :] += dot_nn(slope, queries)
            v_acc[:upto, :] += dot_nn(weights.astype(jnp.bfloat16), mixed)
            return dot_tn(slope, k_two[:upto, :]) * ATTN_MULT

        for pair in range(heads // 2):
            low = one_head(2 * pair)
            high = one_head(2 * pair + 1)
            lane = lax.broadcasted_iota(jnp.int32, low.shape, 1)
            lanes = slice(pair * PAIR, (pair + 1) * PAIR)
            out_ref[here, lanes] = turn_back(
                jnp.where(lane < HEAD_SIZE, low, high), here, slice(0, PAIR)
            )

    @pl.loop(0, rows // block)
    def _(at):
        here = pl.ds(pl.multiple_of(at * block, block), block)
        keys, values = k_acc[here, :], v_acc[here, :]
        keys = keys + pltpu.roll(keys, HEAD_SIZE, 1)
        values = values + pltpu.roll(values, HEAD_SIZE, 1)
        lane = lax.broadcasted_iota(jnp.int32, keys.shape, 1)
        lanes = slice(heads * HEAD_SIZE, heads * HEAD_SIZE + PAIR)
        out_ref[here, lanes] = turn_back(
            jnp.where(lane < HEAD_SIZE, keys, values), here, slice(PAIR, 2 * PAIR)
        )


def attend_back_fast(length, projected, grad_mixed, cosines, sines, groups):
    rows = projected.shape[0]
    wide = projected.shape[1] // groups
    heads = (wide - PAIR) // HEAD_SIZE
    block = min(256, rows)
    return pl.pallas_call(
        functools.partial(attend_back_kernel, block),
        grid=(groups,),
        out_shape=jax.ShapeDtypeStruct((rows, groups * wide), jnp.bfloat16),
        in_specs=[
            pl.BlockSpec(memory_space=pltpu.SMEM),
            pl.BlockSpec((rows, wide), lambda g: (0, g)),
            pl.BlockSpec((rows, heads * HEAD_SIZE), lambda g: (0, g)),
            pl.BlockSpec((rows, 2 * PAIR), lambda g: (0, 0)),
            pl.BlockSpec((rows, 2 * PAIR), lambda g: (0, 0)),
        ],
        out_specs=pl.BlockSpec((rows, wide), lambda g: (0, g)),
        scratch_shapes=[
            pltpu.VMEM((heads, rows, PAIR), jnp.bfloat16),
            pltpu.VMEM((heads, rows, PAIR), jnp.bfloat16),
            pltpu.VMEM((rows, PAIR), jnp.bfloat16),
            pltpu.VMEM((rows, PAIR), jnp.bfloat16),
            pltpu.VMEM((rows, PAIR), jnp.float32),
            pltpu.VMEM((rows, PAIR), jnp.float32),
        ],
        compiler_params=pltpu.CompilerParams(vmem_limit_bytes=48 << 20),
        cost_estimate=pl.CostEstimate(
            flops=5 * groups * heads * rows * rows * 128,
            bytes_accessed=2 * (2 * rows * wide * groups + rows * heads * HEAD_SIZE * groups),
            transcendentals=groups * heads * rows * rows // 2,
        ),
        name="attend_back",
    )(length, projected, grad_mixed, cosines, sines)


def ffn_kernel(
    cols,
    own_ref,
    resid_ref,
    grad_ref,
    wg_own,
    wu_own,
    wd_own,
    wg_far,
    wu_far,
    wd_far,
    wg_sib,
    wu_sib,
    wd_sib,
    u_all,
    dgu_all,
    mlp_all,
    back_all,
    relay_ref,
    land_ref,
    a_keep,
    a_send,
    b_keep,
    b_send,
    wg,
    wu,
    wd,
    b_all,
    b_turn,
    g_two,
    u_buf,
    dg_buf,
    du_buf,
    mlp_buf,
    back_buf,
    w_sems,
    ag_send,
    ag_recv,
    back_send,
    back_recv,
    relay_recv,
    pair_sems,
    lane_sems,
    tile_sems,
    io_sems,
):
    group, core, mate, row, col = place()
    sibling = (group + 1 - 2 * core, row, col)
    last = cols - 1
    depth = wg_own.shape[0]
    half = depth // 2
    units = wg_own.shape[1]
    rows = own_ref.shape[0]
    tile = units // cols
    beside = col + 1 - 2 * lax.rem(col, 2)
    facing = last - col
    inner = (col > 0) & (col < last)

    for step in range(1, cols):
        greet((group, row, lined(col, step, cols)))
    greet(sibling)
    pl.semaphore_wait(pltpu.get_barrier_semaphore(), cols)

    def pass_on(src, at, to, way):
        return pltpu.make_async_remote_copy(
            src_ref=src,
            dst_ref=b_all.at[at],
            send_sem=ag_send.at[way, at],
            recv_sem=ag_recv.at[at],
            device_id=(group, row, to),
            device_id_type=MESH_IDS,
        )

    @pl.when(col < last)
    def _():
        pass_on(own_ref, col, col + 1, 0).start()

    @pl.when(col > 0)
    def _():
        pass_on(own_ref, col, col - 1, 1).start()

    def order(at):
        return line_order(col, last, at)

    def load_g(at):
        side = lax.rem(at, 2)
        return pltpu.make_async_copy(grad_ref.at[order(at)], g_two.at[side], io_sems.at[6 + side])

    def rows_at(first, size):
        return pl.ds(pl.multiple_of(first, half), size)

    own_copy = pltpu.make_async_copy(own_ref, b_all.at[col], io_sems.at[0])
    own_copy.start()
    load_resid = pltpu.make_async_copy(resid_ref, mlp_buf, io_sems.at[8])
    far = (1 - row) * depth
    loads = []
    for at, (full, mine, across, shared) in enumerate(
        ((wg, wg_own, wg_far, wg_sib), (wu, wu_own, wu_far, wu_sib), (wd, wd_own, wd_far, wd_sib))
    ):
        loads += [
            pltpu.make_async_copy(mine, full.at[rows_at(row * depth, depth)], w_sems.at[3 * at]),
            pltpu.make_async_copy(
                across, full.at[rows_at(far + core * half, half)], w_sems.at[3 * at + 1]
            ),
            pltpu.make_async_copy(
                shared, full.at[rows_at(far + (1 - core) * half, half)], w_sems.at[3 * at + 2]
            ),
        ]
    for load in loads:
        load.start()
    load_g(0).start()
    load_resid.start()
    own_copy.wait()
    for load in loads:
        load.wait()

    def arrive(chunk):
        pass_on(b_all.at[chunk], chunk, col, 0).wait_recv()

        @pl.when((chunk < col) & (col < last))
        def _():
            pass_on(b_all.at[chunk], chunk, col + 1, 0).start()

        @pl.when((chunk > col) & (col > 0))
        def _():
            pass_on(b_all.at[chunk], chunk, col - 1, 1).start()

    def outputs(chunk):
        return (
            pltpu.make_async_copy(u_buf, u_all.at[chunk], io_sems.at[1]),
            pltpu.make_async_copy(dg_buf, dgu_all.at[chunk, :, 0:units], io_sems.at[2]),
            pltpu.make_async_copy(du_buf, dgu_all.at[chunk, :, units : 2 * units], io_sems.at[3]),
        )

    def mlp_out(chunk):
        return pltpu.make_async_copy(mlp_buf, mlp_all.at[chunk], io_sems.at[4])

    def slot_of(at):
        return lax.rem(at, cols - 1)

    def deliver(slot, to, place_there, at):
        return pltpu.make_async_remote_copy(
            src_ref=back_buf.at[slot],
            dst_ref=back_all.at[place_there],
            send_sem=back_send.at[at],
            recv_sem=back_recv.at[place_there],
            device_id=(group, row, to),
            device_id_type=MESH_IDS,
        )

    def hand_over(slot, to, box, at):
        return pltpu.make_async_remote_copy(
            src_ref=back_buf.at[slot],
            dst_ref=relay_ref.at[box],
            send_sem=back_send.at[at],
            recv_sem=relay_recv.at[box],
            device_id=(group, row, to),
            device_id_type=MESH_IDS,
        )

    own_back = pltpu.make_async_copy(back_buf.at[0], back_all.at[0], io_sems.at[5])
    at_end = jnp.logical_not(inner)

    def one_chunk(at, unused):
        chunk = order(at)
        side = lax.rem(at, 2)

        @pl.when(at_end & (at > 0))
        def _():
            arrive(order(at))

        @pl.when(inner & (at == 1))
        def _():
            arrive(order(1))
            arrive(order(2))

        @pl.when(inner & (at == 3))
        def _():
            arrive(order(3))

        load_g(at).wait()

        @pl.when(at < last)
        def _():
            load_g(at + 1).start()

        @pl.when(at > 0)
        def _():
            for copy in outputs(order(at - 1)):
                copy.wait()

        @pl.loop(0, units // tile)
        def _(step):
            lanes = aligned(step, tile)
            gate = dot_nn(b_all[chunk], wg[:, lanes])
            upward = dot_nn(b_all[chunk], wu[:, lanes])
            back = RES_MULT * dot_nn(g_two[side], wd[:, lanes])
            opened = 1.0 / (1.0 + jnp.exp(-gate))
            silu = gate * opened
            u_buf[:, lanes] = (silu * upward).astype(jnp.bfloat16)
            slope = opened * (1.0 + gate * (1.0 - opened))
            dg_buf[:, lanes] = (back * upward * slope).astype(jnp.bfloat16)
            du_buf[:, lanes] = (back * silu).astype(jnp.bfloat16)

        for copy in outputs(chunk):
            copy.start()

        @pl.when(at > 0)
        def _():
            mlp_out(order(at - 1)).wait()

        @pl.when(at == 0)
        def _():
            load_resid.wait()

        @pl.when(at == last)
        def _():
            own_back.wait()

        @pl.loop(0, 2 * depth // tile)
        def _(step):
            here = aligned(step, tile)
            back = dot_nt(dg_buf[...], wg[here, :]) + dot_nt(du_buf[...], wu[here, :])
            back_buf[slot_of(at), :, here] = back.astype(jnp.bfloat16)
            added = jnp.where(at == 0, mlp_buf[:, here].astype(jnp.float32), 0.0)
            mlp_buf[:, here] = (added + RES_MULT * dot_nt(u_buf[...], wd[here, :])).astype(
                jnp.bfloat16
            )

        mlp_out(chunk).start()

        @pl.when(at == 0)
        def _():
            own_back.start()

        @pl.when(at_end & (at == 1))
        def _():
            deliver(1, beside, 1, 1).start()

        @pl.when(at_end & (at == 2))
        def _():
            hand_over(2, beside, 1, 2).start()

        @pl.when(at_end & (at == 3))
        def _():
            deliver(0, facing, 2, 3).start()

        @pl.when(inner & (at == 3))
        def _():
            hand_over(0, facing, 0, 3).start()

        return unused

    lax.fori_loop(0, cols, one_chunk, 0)
    for copy in outputs(order(last)):
        copy.wait()
    mlp_out(order(last)).wait()

    loads = []
    for chunk in range(cols):
        here = slice(chunk * rows, (chunk + 1) * rows)
        loads += [
            pltpu.make_async_copy(
                dgu_all.at[chunk, :, 0:units], wg.at[here], w_sems.at[chunk]
            ),
            pltpu.make_async_copy(
                dgu_all.at[chunk, :, units : 2 * units], wu.at[here], w_sems.at[cols + chunk]
            ),
            pltpu.make_async_copy(u_all.at[chunk], wd.at[here], w_sems.at[2 * cols + chunk]),
        ]
    for load in loads:
        load.start()

    def relay(box, slot):
        hand_over(slot, facing, box, 3).wait_recv()
        load = pltpu.make_async_copy(relay_ref.at[box], mlp_buf, io_sems.at[4])
        load.start()
        load.wait()
        tall = min(64, rows)

        @pl.loop(0, rows // tall)
        def _(at):
            here = aligned(at, tall)
            back_buf[slot, here, :] = (
                back_buf[slot, here, :].astype(jnp.float32)
                + mlp_buf[here, :].astype(jnp.float32)
            ).astype(jnp.bfloat16)

    buffers = (dg_buf, du_buf, u_buf)

    def to_sibling(at, part):
        return pltpu.make_async_remote_copy(
            src_ref=buffers[part],
            dst_ref=land_ref.at[at, part],
            send_sem=pair_sems.at[0, at, part],
            recv_sem=pair_sems.at[1, at, part],
            device_id=sibling,
            device_id_type=MESH_IDS,
        )

    def landed(at, part):
        return pltpu.make_async_copy(land_ref.at[at, part], buffers[part], io_sems.at[1 + part])

    halfway = units // 2
    small = rows // 2
    mine, others = aligned(row, small), aligned(1 - row, small)

    def x_lane(high):
        return (
            pltpu.make_async_copy(
                dg_buf.at[mine], a_keep.at[high, :, 0:units], lane_sems.at[0]
            ),
            pltpu.make_async_copy(
                dg_buf.at[others], a_send.at[high, :, 0:units], lane_sems.at[1]
            ),
            pltpu.make_async_copy(
                u_buf.at[mine, 0:halfway],
                a_keep.at[high, :, units : units + halfway],
                lane_sems.at[2],
            ),
            pltpu.make_async_copy(
                u_buf.at[others, 0:halfway],
                a_send.at[high, :, units : units + halfway],
                lane_sems.at[3],
            ),
        )

    def y_lane(target):
        copies = []
        for side in range(2):
            here = slice(side * small, (side + 1) * small)
            copies += [
                pltpu.make_async_copy(
                    du_buf.at[here], target.at[side, :, 0:units], lane_sems.at[4 + 2 * side]
                ),
                pltpu.make_async_copy(
                    u_buf.at[here, halfway:units],
                    target.at[side, :, units : units + halfway],
                    lane_sems.at[5 + 2 * side],
                ),
            ]
        return copies

    def put_results(high, act):
        for copy in x_lane(high):
            act(copy)

        @pl.when(high == (group - core) // 2)
        def _():
            for copy in y_lane(b_keep):
                act(copy)

        @pl.when(high != (group - core) // 2)
        def _():
            for copy in y_lane(b_send):
                act(copy)

    def start_it(copy):
        copy.start()

    def wait_for(copy):
        copy.wait()

    def part_of(chunk):
        return slice(chunk * rows, (chunk + 1) * rows)

    def grad_tile(block, chunk):
        return pltpu.make_async_copy(
            grad_ref.at[chunk, :, aligned(block, rows)],
            mlp_buf.at[:, part_of(chunk)],
            tile_sems.at[chunk],
        )

    parts = range(3)

    def block_of(at):
        return 2 * lax.rem(at, 2) + jnp.where(at >= 2, core, 1 - core)

    for chunk in range(cols):
        grad_tile(block_of(0), chunk).start()
    for chunk in range(cols):
        b_turn[0, :, part_of(chunk)] = b_all[chunk, :, aligned(block_of(0), rows)].T
    for chunk in range(cols):
        grad_tile(block_of(0), chunk).wait()
    for chunk in range(cols):
        g_two[0, :, part_of(chunk)] = mlp_buf[:, part_of(chunk)].T
    for load in loads:
        load.wait()

    def one_block(at, unused):
        high = lax.rem(at, 2)
        is_own = at >= 2
        side = lax.rem(at, 2)
        following = block_of(jnp.minimum(at + 1, 3))

        @pl.when(inner & (at == 1))
        def _():
            relay(0, col)
            deliver(col, beside, 1, 1).start()
            relay(1, last - col)
            deliver(last - col, facing, 2, 2).start()

        @pl.when(at < 3)
        def _():
            for chunk in range(cols):
                grad_tile(following, chunk).start()

        @pl.when((at == 1) | (at == 2))
        def _():
            for part in parts:
                to_sibling(at - 1, part).wait_send()

        @pl.when(at == 3)
        def _():
            put_results(0, wait_for)

        @pl.when(is_own)
        def _():
            for part in parts:
                to_sibling(high, part).wait_recv()
                landed(high, part).start()
            for part in parts:
                landed(high, part).wait()

        @pl.when(at < 3)
        def _():
            for chunk in range(cols):
                grad_tile(following, chunk).wait()

        @pl.loop(0, cols)
        def _(step):
            lanes = aligned(step, tile)
            tokens = aligned(step, rows)

            def put(buffer, value):
                other = jnp.where(is_own, buffer[:, lanes].astype(jnp.float32), 0.0)
                buffer[:, lanes] = (other + value).astype(jnp.bfloat16)

            put(dg_buf, dot_nn(b_turn[side], wg[:, lanes]))
            b_turn[1 - side, :, tokens] = b_all[step, :, aligned(following, rows)].T
            put(du_buf, dot_nn(b_turn[side], wu[:, lanes]))
            g_two[1 - side, :, tokens] = mlp_buf[:, tokens].T
            put(u_buf, RES_MULT * dot_nn(g_two[side], wd[:, lanes]))

        @pl.when(jnp.logical_not(is_own))
        def _():
            for part in parts:
                to_sibling(at, part).start()

        @pl.when(is_own)
        def _():
            put_results(high, start_it)

        return unused

    lax.fori_loop(0, 4, one_block, 0)
    put_results(1, wait_for)
    for at in range(1, cols):
        deliver(0, beside, 1, at).wait_send()
    for at in range(1, 3):
        deliver(0, beside, at, at).wait_recv()
    for chunk in range(cols):

        @pl.when((col >= chunk) & (col < last))
        def _():
            pass_on(own_ref, chunk, col + 1, 0).wait_send()

        @pl.when((col <= chunk) & (col > 0))
        def _():
            pass_on(own_ref, chunk, col - 1, 1).wait_send()


def feed_forward(own_input, resid, grad_rows, weights, cols):
    rows, width = own_input.shape
    units = weights[0].shape[1]
    anywhere = pl.BlockSpec(memory_space=pl.ANY)
    bf16 = jnp.bfloat16
    lane = jax.ShapeDtypeStruct((2, rows // 2, units + units // 2), bf16)
    return pl.pallas_call(
        functools.partial(ffn_kernel, cols),
        out_shape=(
            jax.ShapeDtypeStruct((cols, rows, units), bf16),
            jax.ShapeDtypeStruct((cols, rows, 2 * units), bf16),
            jax.ShapeDtypeStruct((cols, rows, width), bf16),
            jax.ShapeDtypeStruct((3, rows, width), bf16),
            jax.ShapeDtypeStruct((2, rows, width), bf16),
            jax.ShapeDtypeStruct((2, 3, rows, units), bf16),
        )
        + (lane,) * 4,
        in_specs=[anywhere] * 12,
        out_specs=(anywhere,) * 10,
        scratch_shapes=[
            pltpu.VMEM((width, units), bf16),
            pltpu.VMEM((width, units), bf16),
            pltpu.VMEM((width, units), bf16),
            pltpu.VMEM((cols, rows, width), bf16),
            pltpu.VMEM((2, rows, width), bf16),
            pltpu.VMEM((2, rows, width), bf16),
            pltpu.VMEM((rows, units), bf16),
            pltpu.VMEM((rows, units), bf16),
            pltpu.VMEM((rows, units), bf16),
            pltpu.VMEM((rows, width), bf16),
            pltpu.VMEM((cols - 1, rows, width), bf16),
            pltpu.SemaphoreType.DMA((12,)),
            pltpu.SemaphoreType.DMA((2, cols)),
            pltpu.SemaphoreType.DMA((cols,)),
            pltpu.SemaphoreType.DMA((cols,)),
            pltpu.SemaphoreType.DMA((cols,)),
            pltpu.SemaphoreType.DMA((2,)),
            pltpu.SemaphoreType.DMA((2, 2, 3)),
            pltpu.SemaphoreType.DMA((8,)),
            pltpu.SemaphoreType.DMA((cols,)),
            pltpu.SemaphoreType.DMA((9,)),
        ],
        compiler_params=pltpu.CompilerParams(
            collective_id=2, has_side_effects=True, vmem_limit_bytes=60 << 20
        ),
        cost_estimate=pl.CostEstimate(
            flops=18 * cols * rows * width * units,
            bytes_accessed=800 << 20,
            transcendentals=cols * rows * units,
        ),
        name="feed_forward",
    )(own_input, resid, grad_rows, *weights)


def finish_kernel(
    cols,
    ig_ref,
    gq_ref,
    go_ref,
    gain_ref,
    gin_ref,
    sq_ref,
    so_ref,
    gsum_ref,
    q_keep,
    q_sib,
    q_a1,
    q_a2,
    q_b1,
    q_b2,
    q_z,
    o_keep,
    o_sib,
    o_a1,
    o_a2,
    o_b1,
    o_b2,
    o_z,
    gain_now,
    gain_in,
    ig_sems,
    gain_sems,
    q_sems,
    o_sems,
    qz_sems,
    oz_sems,
    local_sems,
):
    group, core, mate, row, col = place()
    pair = group - core
    high = pair // 2
    sibling = (pair + 1 - core, row, col)
    over_x = (group, 1 - row, col)
    over_y = (2 * (1 - high) + core, row, col)
    width = gin_ref.shape[2]

    def line(step):
        return lax.rem(col + step + cols, cols)

    barrier = pltpu.get_barrier_semaphore()

    def greet(device):
        pl.semaphore_signal(barrier, inc=1, device_id=device, device_id_type=MESH_IDS)

    greet(sibling)
    greet(over_x)
    greet(over_y)
    for step in range(1, cols):
        greet((mate, core, line(step)))
        greet((group, row, line(step)))

    @pl.when(core != row)
    def _():
        greet((mate, core, col))

    pl.semaphore_wait(barrier, 2 * cols + 1 + (core - row) * (core - row))

    def remote(src, dst, sems, at, device):
        return pltpu.make_async_remote_copy(
            src_ref=src,
            dst_ref=dst,
            send_sem=sems.at[0, at],
            recv_sem=sems.at[1, at],
            device_id=device,
            device_id_type=MESH_IDS,
        )

    def lanes(block, size):
        return pl.ds(pl.multiple_of(block * size, size), size)

    matrices = (
        (gq_ref, sq_ref, q_keep, q_sib, q_a1, q_a2, q_b1, q_b2, q_z, q_sems, qz_sems),
        (go_ref, so_ref, o_keep, o_sib, o_a1, o_a2, o_b1, o_b2, o_z, o_sems, oz_sems),
    )

    def moves(m):
        grads, out, keep, sib, a1, a2, b1, b2, zb, sems, z_sems = matrices[m]
        return dict(
            s0=remote(grads.at[:, 1 - core], sib, sems, 0, sibling),
            a1=remote(grads.at[:, core, 1 - row], a1, sems, 1, over_x),
            a2=remote(keep.at[1 - high, row], a2, sems, 2, over_y),
            b1=remote(sib.at[1 - high], b1, sems, 3, over_y),
            b2=remote(sib.at[high, 1 - row], b2, sems, 4, over_x),
            own=pltpu.make_async_copy(grads.at[:, core], keep, local_sems.at[m]),
        )

    copies = (moves(0), moves(1))

    def rows_plus(into, more):
        rows = into.shape[0]
        step = min(32, rows)

        @pl.loop(0, rows // step)
        def _(at):
            here = pl.ds(pl.multiple_of(at * step, step), step)
            into[here, :] = (
                into[here, :].astype(jnp.float32) + more[here, :].astype(jnp.float32)
            ).astype(into.dtype)

    def token_copy(step, at):
        return remote(
            ig_ref.at[:, lanes(line(step), width)],
            gin_ref.at[at],
            ig_sems,
            step,
            (mate, core, line(step)),
        )

    own_tokens = pltpu.make_async_copy(
        ig_ref.at[:, lanes(col, width)], gin_ref.at[col], local_sems.at[2]
    )

    for m in range(2):
        copies[m]["s0"].start()
        copies[m]["a1"].start()
        copies[m]["own"].start()
    @pl.when(core == row)
    def _():
        own_tokens.start()
        for step in range(1, cols):
            token_copy(step, col).start()

    gain_load = pltpu.make_async_copy(gain_ref, gain_now.at[0], local_sems.at[3])
    gain_load.start()
    gain_load.wait()
    near = (
        sibling,
        over_x,
        over_y,
        (group, row, col + 1 - 2 * lax.rem(col, 2)),
        (group, row, lax.rem(col + cols // 2, cols)),
    )

    def gain_round(at):
        exchange = remote(gain_now.at[at], gain_in.at[at], gain_sems, at, near[at])
        exchange.start()
        exchange.wait()
        gain_now[at + 1] = gain_now[at] + gain_in[at]

    gain_round(0)
    for m in range(2):
        copies[m]["s0"].wait()
        copies[m]["b1"].start()
    gain_round(1)
    for m in range(2):
        grads, out, keep, sib, a1, a2, b1, b2, zb, sems, z_sems = matrices[m]
        copies[m]["own"].wait()
        copies[m]["a1"].wait()
        rows_plus(keep.at[1 - high, row], a1.at[1 - high])
        copies[m]["a2"].start()
    for m in range(2):
        grads, out, keep, sib, a1, a2, b1, b2, zb, sems, z_sems = matrices[m]
        copies[m]["b1"].wait()
        rows_plus(sib.at[high, 1 - row], b1.at[1 - row])
        copies[m]["b2"].start()

    @pl.when(core != row)
    def _():
        for step in range(cols):
            token_copy(step, col).start()

    gain_round(2)
    for m in range(2):
        grads, out, keep, sib, a1, a2, b1, b2, zb, sems, z_sems = matrices[m]
        rows_plus(keep.at[high, row], a1.at[high])
        rows_plus(sib.at[high, row], b1.at[row])

    def z_moves(m, side, source):
        grads, out, keep, sib, a1, a2, b1, b2, zb, sems, z_sems = matrices[m]
        held = (keep, sib)[side]
        wide = zb.shape[3]
        return [
            pltpu.make_async_remote_copy(
                src_ref=held.at[high, row, :, lanes(line(step), wide)],
                dst_ref=zb.at[side, line(source(step))],
                send_sem=z_sems.at[0, side, step],
                recv_sem=z_sems.at[1, side, step],
                device_id=(group, row, line(step)),
                device_id_type=MESH_IDS,
            )
            for step in range(1, cols)
        ]

    for side, last_copy in ((0, "a2"), (1, "b2")):
        for m in range(2):
            grads, out, keep, sib, a1, a2, b1, b2, zb, sems, z_sems = matrices[m]
            copies[m][last_copy].wait()
            rows_plus((keep, sib)[side].at[high, row], (a2, b2)[side])
            for copy in z_moves(m, side, lambda step: 0):
                copy.start()
    gain_round(3)
    gain_round(4)
    gsum_ref[...] = gain_now[5]
    for side in range(2):
        for m in range(2):
            grads, out, keep, sib, a1, a2, b1, b2, zb, sems, z_sems = matrices[m]
            for copy in z_moves(m, side, lambda step: 0):
                copy.wait_send()
            for copy in z_moves(m, side, lambda step: -step):
                copy.wait_recv()
            held = (keep, sib)[side]
            wide = zb.shape[3]
            at_core = core if side == 0 else 1 - core
            rows = zb.shape[2]
            tall = min(32, rows)

            @pl.loop(0, rows // tall)
            def _(at):
                here = pl.ds(pl.multiple_of(at * tall, tall), tall)
                total = held[high, row, here, lanes(col, wide)].astype(jnp.float32)
                for step in range(1, cols):
                    total = total + zb[side, line(-step), here, :].astype(jnp.float32)
                out[at_core, here, :] = total

    for step in range(1, cols):
        token_copy(step, line(-step)).wait_recv()
        token_copy(step, col).wait_send()

    @pl.when(core != row)
    def _():
        token_copy(0, col).wait_recv()
        token_copy(0, col).wait_send()

    @pl.when(core == row)
    def _():
        own_tokens.wait()


def finish(input_grad, grad_q, grad_o, gains, cols):
    anywhere = pl.BlockSpec(memory_space=pl.ANY)
    in_vmem = pl.BlockSpec(memory_space=pltpu.VMEM)
    bf16, f32 = jnp.bfloat16, jnp.float32
    length, full = input_grad.shape
    rows = grad_q.shape[0] // 8

    def buffers(wide):
        return [
            pltpu.VMEM((2, 2, rows, wide), bf16),
            pltpu.VMEM((2, 2, rows, wide), bf16),
            pltpu.VMEM((2, rows, wide), bf16),
            pltpu.VMEM((rows, wide), bf16),
            pltpu.VMEM((2, rows, wide), bf16),
            pltpu.VMEM((rows, wide), bf16),
            pltpu.VMEM((2, cols, rows, wide // cols), bf16),
        ]

    wide_q, wide_o = grad_q.shape[1], grad_o.shape[1]
    return pl.pallas_call(
        functools.partial(finish_kernel, cols),
        out_shape=(
            jax.ShapeDtypeStruct((cols, length, full // cols), bf16),
            jax.ShapeDtypeStruct((2, rows, wide_q // cols), f32),
            jax.ShapeDtypeStruct((2, rows, wide_o // cols), f32),
            jax.ShapeDtypeStruct(gains.shape, f32),
        ),
        in_specs=[anywhere] * 4,
        out_specs=(anywhere, in_vmem, in_vmem, in_vmem),
        scratch_shapes=buffers(wide_q)
        + buffers(wide_o)
        + [
            pltpu.VMEM((6,) + gains.shape, f32),
            pltpu.VMEM((5,) + gains.shape, f32),
            pltpu.SemaphoreType.DMA((2, cols)),
            pltpu.SemaphoreType.DMA((2, 5)),
            pltpu.SemaphoreType.DMA((2, 5)),
            pltpu.SemaphoreType.DMA((2, 5)),
            pltpu.SemaphoreType.DMA((2, 2, cols)),
            pltpu.SemaphoreType.DMA((2, 2, cols)),
            pltpu.SemaphoreType.DMA((4,)),
        ],
        compiler_params=pltpu.CompilerParams(
            collective_id=3, has_side_effects=True, vmem_limit_bytes=40 << 20
        ),
        cost_estimate=pl.CostEstimate(flops=0, bytes_accessed=300 << 20, transcendentals=0),
        name="finish",
    )(
        input_grad,
        grad_q.reshape(2, 2, 2, rows, wide_q),
        grad_o.reshape(2, 2, 2, rows, wide_o),
        gains,
    )


def one_sequence_body(
    tokens,
    cotangent,
    lengths,
    deal_order,
    gain_attn,
    gain_ffn,
    w_query,
    key_value_weight,
    w_out,
    w_gate_up,
    w_down,
):
    seq_group, rows_local, width_local = tokens.shape
    row_count = lax.axis_size("row")
    col_count = lax.axis_size("col")
    full_width = width_local * col_count
    slot_len = rows_local * row_count
    group, core, mate, row, col = place()
    query_half = w_query.shape[1] // 2
    kv_half = key_value_weight.shape[2] // 2
    hidden = w_down.shape[1]

    def core_half(matrix, axis):
        width = matrix.shape[axis] // 2
        return lax.dynamic_slice_in_dim(matrix, core * width, width, axis)

    def joined(mine, other, at):
        return jnp.where(
            at == 0, jnp.concatenate([mine, other]), jnp.concatenate([other, mine])
        )

    def from_sibling(value):
        return lax.ppermute(value, "dp", SIBLINGS)

    def half_rows(matrix):
        return core_half(matrix, 0)

    pack_q = jnp.concatenate(
        [
            core_half(w_query, 1),
            core_half(key_value_weight[:, 0], 1),
            core_half(key_value_weight[:, 1], 1),
        ],
        axis=1,
    )
    pack_o = core_half(w_out, 1)
    gain_one = gain_attn.astype(jnp.float32)
    gain_two = gain_ffn.astype(jnp.float32)
    own_tokens, attn_input = start_exchange(tokens, gain_one, col_count)

    length = lax.dynamic_slice_in_dim(lengths, mate * seq_group + col, 1)
    given_pos = row * rows_local + jnp.arange(rows_local, dtype=jnp.int32)
    given_lengths = lax.dynamic_slice_in_dim(lengths, group * seq_group, seq_group)
    given_live = given_pos[None, :, None] < given_lengths[:, None, None]
    everyone = lax.all_gather(cotangent, "dp", axis=0, tiled=True)
    everyone, attn_input = lax.optimization_barrier((everyone, attn_input))
    picked = pick_sequences(everyone, deal_order, group * seq_group, seq_group)
    picked = jnp.where(given_live, picked, jnp.zeros_like(picked))
    given = lax.ppermute(picked, ("dp", "row"), CROSSED)
    weights_qkv = gather_weights(pack_q, picked, row_count, col_count, 4)
    given, weights_qkv = lax.optimization_barrier((given, weights_qkv))
    line_cot = lax.all_gather(given, "col", axis=2, tiled=True)
    own_grad = lax.dynamic_index_in_dim(line_cot, col, keepdims=False).astype(jnp.float32)

    w_gate_up, w_down, weights_qkv = lax.optimization_barrier((w_gate_up, w_down, weights_qkv))
    far_gate_up = lax.ppermute(half_rows(w_gate_up), "row", OVER_X)
    far_down = lax.ppermute(half_rows(w_down), "row", OVER_X)
    own_mats = (w_gate_up[:, 0], w_gate_up[:, 1], w_down)

    cosine_table, sine_table = rope_tables(jnp.arange(slot_len, dtype=jnp.int32), HEAD_SIZE)
    cosine_table, sine_table = lax.optimization_barrier((cosine_table, sine_table))
    cosines = jnp.concatenate(
        [jnp.tile(cosine_table, (1, 6)), jnp.ones((slot_len, HEAD_SIZE), jnp.float32)], axis=1
    )
    turning = jnp.concatenate([-sine_table, sine_table], axis=1)
    sines = jnp.concatenate(
        [jnp.tile(turning, (1, 3)), jnp.zeros((slot_len, HEAD_SIZE), jnp.float32)], axis=1
    )
    own_float = own_tokens.astype(jnp.float32)
    scale_one = lax.rsqrt(jnp.mean(own_float * own_float, axis=1, keepdims=True) + EPSILON)
    projected, heads_out = attend_fast(
        length, attn_input, weights_qkv, cosines, sines, col_count
    )

    def summed_rows(partial):
        count = partial.shape[0] // 2
        mine = lax.dynamic_slice_in_dim(partial, core * count, count)
        other = lax.dynamic_slice_in_dim(partial, (1 - core) * count, count)
        return mine.astype(jnp.float32) + from_sibling(other).astype(jnp.float32)

    weights_out = gather_weights(pack_o, heads_out, row_count, col_count, 5)
    attn_rows = summed_rows(expand_local(heads_out, weights_out).astype(jnp.bfloat16))
    resid = own_float + RES_MULT * attn_rows
    scale_two = lax.rsqrt(jnp.mean(resid * resid, axis=1, keepdims=True) + EPSILON)
    own_ffn = (resid * scale_two * gain_two).astype(jnp.bfloat16)

    far_gate_up, far_down, own_ffn, own_mats = lax.optimization_barrier(
        (far_gate_up, far_down, own_ffn, own_mats)
    )
    far_mats = (far_gate_up[:, 0], far_gate_up[:, 1], far_down)
    sibling_mats = tuple(from_sibling(matrix) for matrix in far_mats)
    *unused, a_keep, a_send, b_keep, b_send = feed_forward(
        own_ffn,
        resid.astype(jnp.bfloat16),
        line_cot,
        own_mats + far_mats + sibling_mats,
        col_count,
    )
    mlp_part, back_part = unused[2:4]
    grad_normed_two = jnp.sum(back_part.astype(jnp.float32), axis=0)
    out_cols = lax.psum_scatter(mlp_part, "col", scatter_dimension=2, tiled=True)

    def plus(kept, came):
        return (kept.astype(jnp.float32) + came.astype(jnp.float32)).astype(jnp.bfloat16)

    a_came = lax.ppermute(a_send, "row", OVER_X)
    b_came = lax.ppermute(b_send, "dp", OVER_Y)

    weighted_two = grad_normed_two * gain_two
    inner_two = jnp.sum(weighted_two * resid, axis=1, keepdims=True)
    grad_resid = (
        own_grad + scale_two * weighted_two - resid * scale_two**3 * inner_two / full_width
    )
    gain_two_part = jnp.sum(grad_normed_two * resid * scale_two, axis=0)
    own_attn_grad = (RES_MULT * grad_resid).astype(jnp.bfloat16)
    grad_attn = joined(own_attn_grad, from_sibling(own_attn_grad), core)
    grad_heads = contract_local(grad_attn, weights_out).astype(jnp.bfloat16)
    grad_out = token_outer(grad_attn, heads_out).astype(jnp.bfloat16)
    grad_projected = attend_back_fast(
        length, projected, grad_heads, cosines, sines, col_count
    )
    grad_normed_one = summed_rows(expand_local(grad_projected, weights_qkv).astype(jnp.bfloat16))
    grad_qkv = token_outer(attn_input, grad_projected).astype(jnp.bfloat16)
    weighted_one = grad_normed_one * gain_one
    inner_one = jnp.sum(weighted_one * own_float, axis=1, keepdims=True)
    own_input_grad = (
        grad_resid
        + scale_one * weighted_one
        - own_float * scale_one**3 * inner_one / full_width
    ).astype(jnp.bfloat16)
    gain_one_part = jnp.sum(grad_normed_one * own_float * scale_one, axis=0)
    a_sum, b_sum, own_input_grad = lax.optimization_barrier(
        (plus(a_keep, a_came), plus(b_keep, b_came), own_input_grad)
    )
    high = group // 2

    def one_of(pair, at):
        return lax.dynamic_index_in_dim(pair, at, keepdims=False)

    a_last = lax.ppermute(one_of(a_sum, 1 - high), "dp", OVER_Y)
    b_last = lax.ppermute(one_of(b_sum, 1 - row), "row", OVER_X)
    gains = jnp.stack([gain_one_part, gain_two_part]).reshape(8, -1)
    given_grad, sums_q, sums_o, gain_sums = finish(
        own_input_grad, grad_qkv, grad_out, gains, col_count
    )
    out_cols, a_last, b_last, a_sum, b_sum, given_grad = lax.optimization_barrier(
        (out_cols, a_last, b_last, a_sum, b_sum, given_grad)
    )
    given_out = lax.ppermute(out_cols, ("dp", "row"), CROSSED)
    layer_out = jnp.where(given_live, given_out.astype(jnp.float32), 0.0)
    input_grad = given_grad.astype(jnp.float32)
    a_total = one_of(a_sum, high).astype(jnp.float32) + a_last.astype(jnp.float32)
    b_total = one_of(b_sum, row).astype(jnp.float32) + b_last.astype(jnp.float32)
    sums_gate_up = jnp.stack([a_total[:, :hidden], b_total[:, :hidden]], axis=1)
    sums_down = jnp.concatenate([a_total[:, hidden:], b_total[:, hidden:]], axis=1)
    grad_gain_attn, grad_gain_ffn = gain_sums.reshape(2, full_width)

    def both_cores(sums):
        return jnp.concatenate([sums[0], sums[1]], axis=1)

    qk = query_half + kv_half
    out_query = both_cores(sums_q[:, :, :query_half])
    out_kv = jnp.stack(
        [
            both_cores(sums_q[:, :, query_half:qk]),
            both_cores(sums_q[:, :, qk:]),
        ],
        axis=1,
    )
    out_out = both_cores(sums_o)
    return (
        layer_out,
        input_grad,
        out_query,
        out_kv,
        out_out,
        sums_gate_up,
        sums_down,
        grad_gain_attn,
        grad_gain_ffn,
    )


def general_body(
    tokens,
    cotangent,
    lengths,
    deal_order,
    gain_attn,
    gain_ffn,
    w_query,
    key_value_weight,
    w_out,
    w_gate_up,
    w_down,
):
    seq_group, rows_local, width_local = tokens.shape
    row_count = lax.axis_size("row")
    col_count = lax.axis_size("col")
    full_width = width_local * col_count
    slot_len = rows_local * row_count
    total_rows = seq_group * rows_local
    head_size = HEAD_SIZE
    query_width = w_query.shape[1]
    kv_width = key_value_weight.shape[2]
    kv_heads = kv_width // head_size
    group_size = query_width // kv_width
    group_index = lax.axis_index("dp")
    row_index = lax.axis_index("row")
    col_index = lax.axis_index("col")
    matrices = {
        "qkv": jnp.concatenate(
            [w_query, key_value_weight.reshape(key_value_weight.shape[0], 2 * kv_width)], axis=1
        ),
        "out": w_out,
        "gate_up": w_gate_up,
        "down": w_down,
    }

    def contract_with(operand, which_one):
        return contract_rows(operand, matrices[which_one])

    def expand_with(operand, which_one):
        return expand_rows(operand, matrices[which_one])

    own_cotangent = bring_cotangent(cotangent, deal_order, group_index * seq_group)
    own_rows = tokens
    seq_lens = lax.dynamic_slice_in_dim(lengths, group_index * seq_group, seq_group)
    local_pos = row_index * rows_local + jnp.arange(rows_local, dtype=jnp.int32)
    key_pos = jnp.arange(slot_len, dtype=jnp.int32)
    live_rows = (local_pos[None, :] < seq_lens[:, None]).astype(jnp.float32).reshape(total_rows, 1)
    cosine_table, sine_table = rope_tables(jnp.tile(local_pos, seq_group), head_size)
    own_tokens = own_rows.reshape(total_rows, width_local)
    wide_float = widen_cols(own_tokens).astype(jnp.float32)
    scale_one = lax.rsqrt(jnp.mean(wide_float * wide_float, axis=1, keepdims=True) + EPSILON)
    gain_one = gain_attn.astype(jnp.float32)
    first_normed = wide_float * scale_one
    attn_input = (first_normed * gain_one).astype(jnp.bfloat16)
    projected = contract_with(attn_input, "qkv")
    query_lin = projected[:, :query_width].reshape(total_rows, query_width // head_size, head_size)
    key_lin = projected[:, query_width : query_width + kv_width].reshape(
        total_rows, kv_heads, head_size
    )
    value_lin = projected[:, query_width + kv_width :]
    query_rows = rotary_embed(query_lin, cosine_table, sine_table).astype(jnp.bfloat16)
    keys_own = (
        rotary_embed(key_lin, cosine_table, sine_table)
        .astype(jnp.bfloat16)
        .reshape(seq_group, rows_local, kv_width)
    )
    values_own = value_lin.astype(jnp.bfloat16).reshape(seq_group, rows_local, kv_width)
    all_keys, all_values = (
        lax.all_gather(keys_own, "row", axis=1, tiled=True),
        lax.all_gather(values_own, "row", axis=1, tiled=True),
    )
    query_split = query_rows.reshape(seq_group, rows_local, kv_heads, group_size, head_size)
    key_split = all_keys.reshape(seq_group, slot_len, kv_heads, head_size)
    value_split = all_values.reshape(seq_group, slot_len, kv_heads, head_size)

    def forward_seq(inputs):
        return attend(inputs, key_pos, local_pos)

    mixed_heads, row_max, row_sums = lax.map(
        forward_seq, (query_split, key_split, value_split, seq_lens)
    )
    heads_out = mixed_heads.reshape(total_rows, query_width).astype(jnp.bfloat16)
    attn_local = narrow_cols(expand_with(heads_out, "out"))
    resid = own_tokens.astype(jnp.float32) + RES_MULT * attn_local
    gain_two = lax.dynamic_slice_in_dim(
        gain_ffn.astype(jnp.float32), col_index * width_local, width_local
    )
    scale_two = lax.rsqrt(sum_over_cols(jnp.sum(resid * resid, axis=1)) / full_width + EPSILON)[
        :, None
    ]
    normed_two = resid * scale_two
    ffn_input = widen_cols((normed_two * gain_two).astype(jnp.bfloat16))
    gate_up = contract_with(ffn_input, "gate_up")
    gate = gate_up[:, 0]
    upward = gate_up[:, 1]
    sigmoid_gate = jax.nn.sigmoid(gate)
    silu_gate = gate * sigmoid_gate
    hidden = (silu_gate * upward).astype(jnp.bfloat16)
    ffn_local = narrow_cols(expand_with(hidden, "down"))
    layer_out = live_rows * (resid + RES_MULT * ffn_local)
    grad_rows = live_rows * own_cotangent.reshape(total_rows, width_local).astype(jnp.float32)
    grad_ffn = widen_cols((RES_MULT * grad_rows).astype(jnp.bfloat16))
    grad_hidden = contract_with(grad_ffn, "down")
    grad_down = token_outer(grad_ffn, hidden)
    slope = sigmoid_gate * (1.0 + gate * (1.0 - sigmoid_gate))
    grad_gate_rows = jnp.stack(
        [grad_hidden * upward * slope, grad_hidden * silu_gate], axis=1
    ).astype(jnp.bfloat16)
    grad_gate_up = token_outer(ffn_input, grad_gate_rows)
    grad_normed_two = narrow_cols(expand_with(grad_gate_rows, "gate_up"))
    weighted_two = grad_normed_two * gain_two
    inner_two = sum_over_cols(jnp.sum(weighted_two * resid, axis=1))[:, None]
    grad_resid = (
        grad_rows + scale_two * weighted_two - resid * scale_two**3 * inner_two / full_width
    )
    gain_two_part = jnp.sum(grad_normed_two * normed_two, axis=0)
    grad_attn = widen_cols((RES_MULT * grad_resid).astype(jnp.bfloat16))
    grad_heads = contract_with(grad_attn, "out").astype(jnp.bfloat16)
    grad_out = token_outer(grad_attn, heads_out)
    grad_split = grad_heads.reshape(seq_group, rows_local, kv_heads, group_size, head_size)

    def backward_seq(inputs):
        return attend_back(inputs, key_pos, local_pos)

    grad_query, grad_key, grad_value = lax.map(
        backward_seq, (query_split, key_split, value_split, grad_split, row_max, row_sums, seq_lens)
    )
    key_part, value_part = (
        lax.psum_scatter(
            grad_key.reshape(seq_group, slot_len, kv_width).astype(jnp.bfloat16),
            "row",
            scatter_dimension=1,
            tiled=True,
        ).astype(jnp.float32),
        lax.psum_scatter(
            grad_value.reshape(seq_group, slot_len, kv_width).astype(jnp.bfloat16),
            "row",
            scatter_dimension=1,
            tiled=True,
        ).astype(jnp.float32),
    )
    query_back = rotary_embed(
        grad_query.reshape(total_rows, query_width // head_size, head_size),
        cosine_table,
        -sine_table,
    ).reshape(total_rows, query_width)
    key_back = rotary_embed(
        key_part.reshape(total_rows, kv_heads, head_size), cosine_table, -sine_table
    ).reshape(total_rows, kv_width)
    grad_projected = jnp.concatenate(
        [query_back, key_back, value_part.reshape(total_rows, kv_width)], axis=1
    ).astype(jnp.bfloat16)
    grad_qkv = token_outer(attn_input, grad_projected)
    grad_normed_one = expand_with(grad_projected, "qkv")
    weighted_one = grad_normed_one * gain_one
    inner_one = jnp.sum(weighted_one * wide_float, axis=1, keepdims=True)
    input_part = scale_one * weighted_one - wide_float * scale_one**3 * inner_one / full_width
    input_grad = grad_resid + narrow_cols(input_part)
    gain_one_part = jnp.sum(grad_normed_one * first_normed, axis=0)
    gain_two_full = lax.dynamic_update_slice_in_dim(
        jnp.zeros((full_width,), jnp.float32), gain_two_part, col_index * width_local, 0
    )
    grad_gain_attn, grad_gain_ffn = lax.psum((gain_one_part, gain_two_full), ("dp", "row", "col"))
    sums_qkv, sums_out, sums_gate_up, sums_down = (
        lax.psum_scatter(
            grad_qkv.astype(jnp.bfloat16), ("dp", "row"), scatter_dimension=0, tiled=True
        ).astype(jnp.float32),
        lax.psum_scatter(
            grad_out.astype(jnp.bfloat16), ("dp", "row"), scatter_dimension=0, tiled=True
        ).astype(jnp.float32),
        lax.psum_scatter(
            grad_gate_up.astype(jnp.bfloat16), ("dp", "row"), scatter_dimension=0, tiled=True
        ).astype(jnp.float32),
        lax.psum_scatter(
            grad_down.astype(jnp.bfloat16), ("dp", "row"), scatter_dimension=0, tiled=True
        ).astype(jnp.float32),
    )
    out_query = sums_qkv[:, :query_width]
    out_kv = sums_qkv[:, query_width:].reshape(sums_qkv.shape[0], 2, kv_width)
    return (
        layer_out.reshape(seq_group, rows_local, width_local),
        input_grad.reshape(seq_group, rows_local, width_local),
        out_query,
        out_kv,
        sums_out,
        sums_gate_up,
        sums_down,
        grad_gain_attn,
        grad_gain_ffn,
    )


def body(tokens, cotangent, lengths, deal_order, gain_attn, gain_ffn, w_query, key_value_weight, *rest):
    sizes = (lax.axis_size("dp"), lax.axis_size("row"), lax.axis_size("col"))
    one_each = sizes == (4, 2, 4) and tokens.shape[0] == sizes[2]
    pairs = w_query.shape[1] == 8 * HEAD_SIZE and key_value_weight.shape[2] == 2 * HEAD_SIZE
    chosen = one_sequence_body if one_each and pairs else general_body
    return chosen(
        tokens, cotangent, lengths, deal_order, gain_attn, gain_ffn, w_query, key_value_weight, *rest
    )


def solution(mesh):
    placed = (
        P("dp", "row", "col"),
        P("dp", "row", "col"),
        P(),
        P(),
        P(),
        P(),
        P("row", "col"),
        P("row", None, "col"),
        P("row", "col"),
        P("row", None, "col"),
        P("row", "col"),
    )
    return jax.shard_map(
        body,
        mesh=mesh,
        in_specs=placed,
        out_specs=(
            P("dp", "row", "col"),
            P("dp", "row", "col"),
            P(("dp", "row"), "col"),
            P(("dp", "row"), None, "col"),
            P(("dp", "row"), "col"),
            P(("dp", "row"), None, "col"),
            P(("dp", "row"), "col"),
            P(),
            P(),
        ),
        check_vma=False,
    )
```

```python
import functools

import jax
import jax.numpy as jnp
from jax import lax
from jax.experimental import pallas as pl
from jax.experimental.pallas import tpu as pltpu
from jax.sharding import PartitionSpec as P

HEAD_SIZE = 64


EPSILON = 1e-05
THETA = 10000000.0
ATTN_MULT = 0.015625
RES_MULT = 0.22
MASKED = -1e30


def rope_tables(positions, head_size):
    halves = jnp.arange(head_size // 2, dtype=jnp.float32)
    inverse_freq = THETA ** (-(halves * 2.0) / head_size)
    angles = positions.astype(jnp.float32)[:, None] * inverse_freq[None, :]
    return (jnp.cos(angles), jnp.sin(angles))


def rotary_embed(value_rows, cosine_table, sine_table):
    middle = value_rows.shape[-1] // 2
    first_half = value_rows[..., :middle]
    second_half = value_rows[..., middle:]
    cos_part = cosine_table[:, None, :]
    sin_part = sine_table[:, None, :]
    return jnp.concatenate(
        [
            first_half * cos_part - second_half * sin_part,
            second_half * cos_part + first_half * sin_part,
        ],
        axis=-1,
    )


def widen_cols(value_rows):
    return lax.all_gather(value_rows, "col", axis=1, tiled=True)


def narrow_cols(value_rows):
    return lax.psum_scatter(value_rows, "col", scatter_dimension=1, tiled=True)


def sum_over_cols(value_rows):
    return lax.psum(value_rows, "col")


def contract_local(operand, matrix):
    return lax.dot_general(
        operand, matrix, (((1,), (0,)), ((), ())), preferred_element_type=jnp.float32
    )


def expand_local(operand, matrix):
    trailing = tuple(range(1, operand.ndim))
    return lax.dot_general(
        operand, matrix, ((trailing, trailing), ((), ())), preferred_element_type=jnp.float32
    )


def token_outer(features, grads):
    return lax.dot_general(
        features, grads, (((0,), (0,)), ((), ())), preferred_element_type=jnp.float32
    )


def contract_rows(operand, matrix):
    return contract_local(operand, lax.all_gather(matrix, "row", axis=0, tiled=True))


def expand_rows(operand, matrix):
    return expand_local(operand, lax.all_gather(matrix, "row", axis=0, tiled=True))


def split_keys(key_seq, value_seq, key_pos):
    slot_len = key_seq.shape[0]
    width = min(512, slot_len)
    count = slot_len // width
    return (
        key_seq.reshape(count, width, key_seq.shape[1], key_seq.shape[2]),
        value_seq.reshape(count, width, value_seq.shape[1], value_seq.shape[2]),
        key_pos.reshape(count, width),
    )


def block_scores(query_seq, key_block, pos_block, query_pos, length):
    scores = (
        jnp.einsum("qkgd,tkd->kgqt", query_seq, key_block, preferred_element_type=jnp.float32)
        * ATTN_MULT
    )
    allowed = (pos_block[None, :] <= query_pos[:, None]) & (pos_block[None, :] < length)
    return jnp.where(allowed, scores, MASKED)


def attend(inputs, key_pos, query_pos):
    query_seq, key_seq, value_seq, length = inputs
    key_blocks, value_blocks, pos_blocks = split_keys(key_seq, value_seq, key_pos)
    stat_shape = (query_seq.shape[1], query_seq.shape[2], query_seq.shape[0], 1)

    def gather_stats(carry, entry):
        running_max, running_sum = carry
        key_block, pos_block = entry
        scores = block_scores(query_seq, key_block, pos_block, query_pos, length)
        new_max = jnp.maximum(running_max, jnp.max(scores, axis=-1, keepdims=True))
        new_sum = running_sum * jnp.exp(running_max - new_max) + jnp.sum(
            jnp.exp(scores - new_max), axis=-1, keepdims=True
        )
        return ((new_max, new_sum), None)

    start_stats = (jnp.full(stat_shape, MASKED, jnp.float32), jnp.zeros(stat_shape, jnp.float32))
    (row_max, row_sums), unused = lax.scan(gather_stats, start_stats, (key_blocks, pos_blocks))

    def mix_values(running, entry):
        key_block, value_block, pos_block = entry
        scores = block_scores(query_seq, key_block, pos_block, query_pos, length)
        weights = jnp.exp(scores - row_max) / row_sums
        return (
            running
            + jnp.einsum(
                "kgqt,tkd->qkgd",
                weights.astype(jnp.bfloat16),
                value_block,
                preferred_element_type=jnp.float32,
            ),
            None,
        )

    start_mix = jnp.zeros(query_seq.shape, jnp.float32)
    mixed_heads, unused = lax.scan(mix_values, start_mix, (key_blocks, value_blocks, pos_blocks))
    return (mixed_heads, row_max, row_sums)


def attend_back(inputs, key_pos, query_pos):
    query_seq, key_seq, value_seq, grad_mixed, row_max, row_sums, length = inputs
    key_blocks, value_blocks, pos_blocks = split_keys(key_seq, value_seq, key_pos)

    def block_weights(key_block, value_block, pos_block):
        scores = block_scores(query_seq, key_block, pos_block, query_pos, length)
        weights = jnp.exp(scores - row_max) / row_sums
        grad_weights = jnp.einsum(
            "qkgd,tkd->kgqt", grad_mixed, value_block, preferred_element_type=jnp.float32
        )
        return (weights, grad_weights)

    def gather_centre(running, entry):
        weights, grad_weights = block_weights(*entry)
        return (running + jnp.sum(weights * grad_weights, axis=-1, keepdims=True), None)

    start_centre = jnp.zeros(row_max.shape, jnp.float32)
    centre, unused = lax.scan(gather_centre, start_centre, (key_blocks, value_blocks, pos_blocks))

    def grads_block(running, entry):
        key_block = entry[0]
        weights, grad_weights = block_weights(*entry)
        grad_scores = (weights * (grad_weights - centre)).astype(jnp.bfloat16)
        grad_query = (
            running
            + jnp.einsum(
                "kgqt,tkd->qkgd", grad_scores, key_block, preferred_element_type=jnp.float32
            )
            * ATTN_MULT
        )
        grad_key = (
            jnp.einsum("kgqt,qkgd->tkd", grad_scores, query_seq, preferred_element_type=jnp.float32)
            * ATTN_MULT
        )
        grad_value = jnp.einsum(
            "kgqt,qkgd->tkd",
            weights.astype(jnp.bfloat16),
            grad_mixed,
            preferred_element_type=jnp.float32,
        )
        return (grad_query, (grad_key, grad_value))

    start_query = jnp.zeros(query_seq.shape, jnp.float32)
    grad_query, (grad_key, grad_value) = lax.scan(
        grads_block, start_query, (key_blocks, value_blocks, pos_blocks)
    )
    return (grad_query, grad_key.reshape(key_seq.shape), grad_value.reshape(value_seq.shape))


MESH_IDS = pl.DeviceIdType.MESH
SIBLINGS = [(0, 1), (1, 0), (2, 3), (3, 2)]
OVER_X = [(0, 1), (1, 0)]
OVER_Y = [(0, 2), (2, 0), (1, 3), (3, 1)]
CROSSED = [((2 * y + c) * 2 + x, (2 * y + x) * 2 + c) for y in (0, 1) for c in (0, 1) for x in (0, 1)]


def pick_sequences(everyone, deal_order, first, count):
    slots = jnp.arange(deal_order.shape[0], dtype=jnp.int32)
    inverse = jnp.sum(jnp.where(deal_order[None, :] == slots[:, None], slots[None, :], 0), axis=1)
    return jnp.concatenate(
        [
            lax.dynamic_slice_in_dim(
                everyone, lax.dynamic_index_in_dim(inverse, first + at, keepdims=False), 1
            )
            for at in range(count)
        ]
    )


def bring_cotangent(cotangent, deal_order, first):
    everyone = lax.all_gather(cotangent, "dp", axis=0, tiled=True)
    return pick_sequences(everyone, deal_order, first, cotangent.shape[0])


def place():
    group = lax.axis_index("dp")
    core = lax.rem(group, 2)
    row = lax.axis_index("row")
    return group, core, group - core + row, row, lax.axis_index("col")


def lined(index, step, count):
    return lax.rem(index + step + count, count)


def aligned(block, size):
    return pl.ds(pl.multiple_of(block * size, size), size)


def greet(device):
    pl.semaphore_signal(
        pltpu.get_barrier_semaphore(), inc=1, device_id=device, device_id_type=MESH_IDS
    )


def remote(src, dst, sems, at, device):
    return pltpu.make_async_remote_copy(
        src_ref=src,
        dst_ref=dst,
        send_sem=sems.at[0, at],
        recv_sem=sems.at[1, at],
        device_id=device,
        device_id_type=MESH_IDS,
    )


def line_order(col, last, at):
    inner_low = jnp.where(at < 2, 1 - at, at)
    inner_high = jnp.where(at == 3, 0, jnp.where(at == 0, 2, jnp.where(at == 1, 1, 3)))
    return jnp.where(
        col == 0, at, jnp.where(col == last, last - at, jnp.where(col == 1, inner_low, inner_high))
    )


def start_kernel(
    cols, tok_ref, gain_ref, x_ref, a_ref, x_buf, a_buf, tok_sems, a_sems, local_sems
):
    group, core, mate, row, col = place()
    width = tok_ref.shape[2]
    length = x_buf.shape[0]
    sibling = (group + 1 - 2 * core, row, col)

    def line(step):
        return lined(col, step, cols)

    for step in range(1, cols):
        greet((mate, core, line(step)))
    greet(sibling)

    @pl.when(core != row)
    def _():
        greet((mate, core, col))

    pl.semaphore_wait(pltpu.get_barrier_semaphore(), cols + (core - row) * (core - row))

    def token_copy(step, into):
        return remote(
            tok_ref.at[line(step)],
            x_buf.at[:, aligned(into, width)],
            tok_sems,
            step,
            (mate, core, line(step)),
        )

    own_tokens = pltpu.make_async_copy(
        tok_ref.at[col], x_buf.at[:, aligned(col, width)], local_sems.at[0]
    )
    for step in range(1, cols):
        token_copy(step, col).start()

    @pl.when(core != row)
    def _():
        token_copy(0, col).start()

    @pl.when(core == row)
    def _():
        own_tokens.start()

    for step in range(1, cols):
        token_copy(step, line(-step)).wait_recv()

    @pl.when(core != row)
    def _():
        token_copy(0, col).wait_recv()

    @pl.when(core == row)
    def _():
        own_tokens.wait()

    keep_x = pltpu.make_async_copy(x_buf, x_ref, local_sems.at[1])
    keep_x.start()
    tall = min(64, length)

    @pl.loop(0, length // tall)
    def _(at):
        here = aligned(at, tall)
        now = x_buf[here, :].astype(jnp.float32)
        scale = lax.rsqrt(jnp.mean(now * now, axis=1, keepdims=True) + EPSILON)
        a_buf[here, :] = (now * scale * gain_ref[...]).astype(jnp.bfloat16)

    def a_copy(of_core):
        return remote(a_buf, a_ref.at[aligned(of_core, length)], a_sems, 0, sibling)

    own_a = pltpu.make_async_copy(a_buf, a_ref.at[aligned(core, length)], local_sems.at[2])
    a_copy(core).start()
    own_a.start()
    for step in range(1, cols):
        token_copy(step, col).wait_send()

    @pl.when(core != row)
    def _():
        token_copy(0, col).wait_send()

    keep_x.wait()
    own_a.wait()
    a_copy(core).wait_send()
    a_copy(1 - core).wait_recv()


def start_exchange(tokens, gain, cols):
    anywhere = pl.BlockSpec(memory_space=pl.ANY)
    seqs, length, width = tokens.shape
    full = width * cols
    return pl.pallas_call(
        functools.partial(start_kernel, cols),
        out_shape=(
            jax.ShapeDtypeStruct((length, full), tokens.dtype),
            jax.ShapeDtypeStruct((2 * length, full), tokens.dtype),
        ),
        in_specs=[anywhere, pl.BlockSpec(memory_space=pltpu.VMEM)],
        out_specs=(anywhere,) * 2,
        scratch_shapes=[
            pltpu.VMEM((length, full), tokens.dtype),
            pltpu.VMEM((length, full), tokens.dtype),
            pltpu.SemaphoreType.DMA((2, cols)),
            pltpu.SemaphoreType.DMA((2, 1)),
            pltpu.SemaphoreType.DMA((3,)),
        ],
        compiler_params=pltpu.CompilerParams(
            collective_id=1, has_side_effects=True, vmem_limit_bytes=16 << 20
        ),
        cost_estimate=pl.CostEstimate(flops=0, bytes_accessed=200 << 20, transcendentals=0),
        name="start_exchange",
    )(tokens, gain.reshape(1, full))


def gather_kernel(
    cols,
    q_ref,
    o_ref,
    rows_ref,
    wq_ref,
    wo_ref,
    crossed_ref,
    q_send,
    q_recv,
    q_over,
    o_send,
    o_recv,
    o_over,
    cross_sems,
    local_sems,
):
    group, core, mate, row, col = place()
    last = cols - 1
    over = (group, 1 - row, col)
    greet(over)

    @pl.when(core != row)
    def _():
        greet((mate, core, col))

    @pl.when(col < last)
    def _():
        greet((group, row, col + 1))

    @pl.when(col > 0)
    def _():
        greet((group, row, col - 1))

    pl.semaphore_wait(
        pltpu.get_barrier_semaphore(),
        1 + jnp.minimum(col, 1) + jnp.minimum(last - col, 1) + (core - row) * (core - row),
    )
    cross = remote(rows_ref, crossed_ref, cross_sems, 0, (mate, core, col))
    stay = pltpu.make_async_copy(rows_ref, crossed_ref, local_sems.at[2])

    def moves(own, full, send, recv, over_sems):
        tall, wide = own.shape

        def block(of_row, of_col):
            return full.at[aligned(of_row, tall), aligned(of_col, wide)]

        def along(src, chunk, to, way):
            return pltpu.make_async_remote_copy(
                src_ref=src,
                dst_ref=block(row, chunk),
                send_sem=send.at[way, chunk],
                recv_sem=recv.at[chunk],
                device_id=(group, row, to),
                device_id_type=MESH_IDS,
            )

        def across(src, of_row, chunk):
            return remote(src, block(of_row, chunk), over_sems, chunk, over)

        return block, along, across

    both = (
        (q_ref, moves(q_ref, wq_ref, q_send, q_recv, q_over)),
        (o_ref, moves(o_ref, wo_ref, o_send, o_recv, o_over)),
    )
    own_copies = []
    for at, (own, (block, along, across)) in enumerate(both):

        @pl.when(col < last)
        def _():
            along(own, col, col + 1, 0).start()

        @pl.when(col > 0)
        def _():
            along(own, col, col - 1, 1).start()

        across(own, row, col).start()
        own_copies.append(pltpu.make_async_copy(own, block(row, col), local_sems.at[at]))
        own_copies[-1].start()

    @pl.when(core != row)
    def _():
        cross.start()

    @pl.when(core == row)
    def _():
        stay.start()

    for at in range(1, cols):
        chunk = line_order(col, last, at)
        for own, (block, along, across) in both:
            along(own, chunk, col, 0).wait_recv()

            @pl.when((chunk < col) & (col < last))
            def _():
                along(block(row, chunk), chunk, col + 1, 0).start()

            @pl.when((chunk > col) & (col > 0))
            def _():
                along(block(row, chunk), chunk, col - 1, 1).start()

            across(block(row, chunk), row, chunk).start()
    for copy in own_copies:
        copy.wait()

    @pl.when(core != row)
    def _():
        cross.wait()

    @pl.when(core == row)
    def _():
        stay.wait()

    for own, (block, along, across) in both:
        for chunk in range(cols):

            @pl.when((col >= chunk) & (col < last))
            def _():
                along(own, chunk, col + 1, 0).wait_send()

            @pl.when((col <= chunk) & (col > 0))
            def _():
                along(own, chunk, col - 1, 1).wait_send()

            across(own, row, chunk).wait_send()
            across(own, 1 - row, chunk).wait_recv()


def gather_weights(own_q, own_o, token_rows, rows, cols):
    anywhere = pl.BlockSpec(memory_space=pl.ANY)

    def whole(own):
        return jax.ShapeDtypeStruct((own.shape[0] * rows, own.shape[1] * cols), own.dtype)

    return pl.pallas_call(
        functools.partial(gather_kernel, cols),
        out_shape=(
            whole(own_q),
            whole(own_o),
            jax.ShapeDtypeStruct(token_rows.shape, token_rows.dtype),
        ),
        in_specs=[anywhere] * 3,
        out_specs=(anywhere,) * 3,
        scratch_shapes=[
            pltpu.SemaphoreType.DMA((2, cols)),
            pltpu.SemaphoreType.DMA((cols,)),
            pltpu.SemaphoreType.DMA((2, cols)),
        ]
        * 2
        + [pltpu.SemaphoreType.DMA((2, 1)), pltpu.SemaphoreType.DMA((3,))],
        compiler_params=pltpu.CompilerParams(collective_id=4, has_side_effects=True),
        cost_estimate=pl.CostEstimate(flops=0, bytes_accessed=300 << 20, transcendentals=0),
        name="gather_weights",
    )(own_q, own_o, token_rows)


def half_turn(wide):
    lanes = wide.shape[1]
    half = HEAD_SIZE // 2
    lane = lax.broadcasted_iota(jnp.int32, wide.shape, 1)
    return jnp.where(
        lax.rem(lane, HEAD_SIZE) < half,
        pltpu.roll(wide, lanes - half, 1),
        pltpu.roll(wide, half, 1),
    )


def both_heads(pair):
    lane = lax.broadcasted_iota(jnp.int32, pair.shape, 1)
    turned = pltpu.roll(pair, HEAD_SIZE, 1)
    low = lane < HEAD_SIZE
    return jnp.where(low, pair, turned), jnp.where(low, turned, pair)


def keep_head(pair, side):
    lane = lax.broadcasted_iota(jnp.int32, pair.shape, 1)
    mine = lane < HEAD_SIZE if side == 0 else lane >= HEAD_SIZE
    return jnp.where(mine, pair, jnp.zeros_like(pair))


def dot_nn(a, b):
    return lax.dot_general(a, b, (((1,), (0,)), ((), ())), preferred_element_type=jnp.float32)


def dot_nt(a, b):
    return lax.dot_general(a, b, (((1,), (1,)), ((), ())), preferred_element_type=jnp.float32)


def dot_tn(a, b):
    return lax.dot_general(a, b, (((0,), (0,)), ((), ())), preferred_element_type=jnp.float32)


PAIR = 2 * HEAD_SIZE


def attend_kernel(block, len_ref, a_ref, w_ref, cos_ref, sin_ref, qkv_ref, z_ref, q_all, k_two, v_two):
    rows = a_ref.shape[0]
    heads = q_all.shape[0]
    length = len_ref[0]

    @pl.loop(0, rows // block)
    def _(at):
        here = pl.ds(pl.multiple_of(at * block, block), block)
        lin = dot_nn(a_ref[here, :], w_ref[...])
        for part in range(heads // 2 + 1):
            lanes = slice(part * PAIR, (part + 1) * PAIR)
            now = lin[:, lanes]
            table = slice(0, PAIR) if part < heads // 2 else slice(PAIR, 2 * PAIR)
            now = now * cos_ref[here, table] + half_turn(now) * sin_ref[here, table]
            qkv_ref[here, lanes] = now.astype(jnp.bfloat16)
            if part < heads // 2:
                for side in range(2):
                    q_all[2 * part + side, here, :] = keep_head(now * ATTN_MULT, side).astype(
                        jnp.bfloat16
                    )
            else:
                keys, values = both_heads(now)
                k_two[here, :] = keys.astype(jnp.bfloat16)
                v_two[here, :] = values.astype(jnp.bfloat16)

    for at in range(rows // block):
        here = slice(at * block, (at + 1) * block)
        upto = (at + 1) * block
        row = lax.broadcasted_iota(jnp.int32, (block, upto), 0) + at * block
        key = lax.broadcasted_iota(jnp.int32, (block, upto), 1)
        allowed = key < jnp.minimum(row + 1, length)

        def one_head(head):
            scores = dot_nt(q_all[head, here, :], k_two[:upto, :])
            scores = jnp.where(allowed, scores, MASKED)
            top = jnp.max(scores, axis=1, keepdims=True)
            power = jnp.exp(scores - top)
            total = jnp.sum(power, axis=1, keepdims=True)
            return dot_nn(power.astype(jnp.bfloat16), v_two[:upto, :]) / total

        for pair in range(heads // 2):
            low = one_head(2 * pair)
            high = one_head(2 * pair + 1)
            lane = lax.broadcasted_iota(jnp.int32, low.shape, 1)
            z_ref[here, pair * PAIR : (pair + 1) * PAIR] = jnp.where(
                lane < HEAD_SIZE, low, high
            ).astype(jnp.bfloat16)


def attend_fast(length, inputs, weights, cosines, sines, groups):
    rows, depth = inputs.shape
    wide = weights.shape[1] // groups
    heads = (wide - PAIR) // HEAD_SIZE
    block = min(256, rows)
    return pl.pallas_call(
        functools.partial(attend_kernel, block),
        grid=(groups,),
        out_shape=(
            jax.ShapeDtypeStruct((rows, groups * wide), jnp.bfloat16),
            jax.ShapeDtypeStruct((rows, groups * heads * HEAD_SIZE), jnp.bfloat16),
        ),
        in_specs=[
            pl.BlockSpec(memory_space=pltpu.SMEM),
            pl.BlockSpec((rows, depth), lambda g: (0, 0)),
            pl.BlockSpec((depth, wide), lambda g: (0, g)),
            pl.BlockSpec((rows, 2 * PAIR), lambda g: (0, 0)),
            pl.BlockSpec((rows, 2 * PAIR), lambda g: (0, 0)),
        ],
        out_specs=(
            pl.BlockSpec((rows, wide), lambda g: (0, g)),
            pl.BlockSpec((rows, heads * HEAD_SIZE), lambda g: (0, g)),
        ),
        scratch_shapes=[
            pltpu.VMEM((heads, rows, PAIR), jnp.bfloat16),
            pltpu.VMEM((rows, PAIR), jnp.bfloat16),
            pltpu.VMEM((rows, PAIR), jnp.bfloat16),
        ],
        compiler_params=pltpu.CompilerParams(vmem_limit_bytes=48 << 20),
        cost_estimate=pl.CostEstimate(
            flops=2 * rows * depth * wide * groups + 2 * groups * heads * rows * rows * 128,
            bytes_accessed=2 * (rows * depth + depth * wide * groups + rows * wide * groups),
            transcendentals=groups * heads * rows * rows // 2,
        ),
        name="attend",
    )(length, inputs, weights, cosines, sines)


def attend_back_kernel(
    block, len_ref, qkv_ref, dz_ref, cos_ref, sin_ref, out_ref, q_all, z_all, k_two, v_two, k_acc, v_acc
):
    rows = qkv_ref.shape[0]
    heads = q_all.shape[0]
    length = len_ref[0]

    @pl.loop(0, rows // block)
    def _(at):
        here = pl.ds(pl.multiple_of(at * block, block), block)
        for part in range(heads // 2):
            lanes = slice(part * PAIR, (part + 1) * PAIR)
            queries = qkv_ref[here, lanes].astype(jnp.float32) * ATTN_MULT
            mixed = dz_ref[here, lanes].astype(jnp.float32)
            for side in range(2):
                q_all[2 * part + side, here, :] = keep_head(queries, side).astype(jnp.bfloat16)
                z_all[2 * part + side, here, :] = keep_head(mixed, side).astype(jnp.bfloat16)
        keys, values = both_heads(qkv_ref[here, heads * HEAD_SIZE :].astype(jnp.float32))
        k_two[here, :] = keys.astype(jnp.bfloat16)
        v_two[here, :] = values.astype(jnp.bfloat16)
        k_acc[here, :] = jnp.zeros((block, PAIR), jnp.float32)
        v_acc[here, :] = jnp.zeros((block, PAIR), jnp.float32)

    def turn_back(now, here, table):
        return (now * cos_ref[here, table] - half_turn(now) * sin_ref[here, table]).astype(
            jnp.bfloat16
        )

    for at in range(rows // block):
        here = slice(at * block, (at + 1) * block)
        upto = (at + 1) * block
        key = lax.broadcasted_iota(jnp.int32, (upto, block), 0)
        query = lax.broadcasted_iota(jnp.int32, (upto, block), 1) + at * block
        allowed = key < jnp.minimum(query + 1, length)

        def one_head(head):
            queries, mixed = q_all[head, here, :], z_all[head, here, :]
            scores = jnp.where(allowed, dot_nt(k_two[:upto, :], queries), MASKED)
            power = jnp.exp(scores - jnp.max(scores, axis=0, keepdims=True))
            weights = power * (1.0 / jnp.sum(power, axis=0, keepdims=True))
            back = dot_nt(v_two[:upto, :], mixed)
            centre = jnp.sum(weights * back, axis=0, keepdims=True)
            slope = (weights * (back - centre)).astype(jnp.bfloat16)
            k_acc[:upto, :] += dot_nn(slope, queries)
            v_acc[:upto, :] += dot_nn(weights.astype(jnp.bfloat16), mixed)
            return dot_tn(slope, k_two[:upto, :]) * ATTN_MULT

        for pair in range(heads // 2):
            low = one_head(2 * pair)
            high = one_head(2 * pair + 1)
            lane = lax.broadcasted_iota(jnp.int32, low.shape, 1)
            lanes = slice(pair * PAIR, (pair + 1) * PAIR)
            out_ref[here, lanes] = turn_back(
                jnp.where(lane < HEAD_SIZE, low, high), here, slice(0, PAIR)
            )

    @pl.loop(0, rows // block)
    def _(at):
        here = pl.ds(pl.multiple_of(at * block, block), block)
        keys, values = k_acc[here, :], v_acc[here, :]
        keys = keys + pltpu.roll(keys, HEAD_SIZE, 1)
        values = values + pltpu.roll(values, HEAD_SIZE, 1)
        lane = lax.broadcasted_iota(jnp.int32, keys.shape, 1)
        lanes = slice(heads * HEAD_SIZE, heads * HEAD_SIZE + PAIR)
        out_ref[here, lanes] = turn_back(
            jnp.where(lane < HEAD_SIZE, keys, values), here, slice(PAIR, 2 * PAIR)
        )


def attend_back_fast(length, projected, grad_mixed, cosines, sines, groups):
    rows = projected.shape[0]
    wide = projected.shape[1] // groups
    heads = (wide - PAIR) // HEAD_SIZE
    block = min(256, rows)
    return pl.pallas_call(
        functools.partial(attend_back_kernel, block),
        grid=(groups,),
        out_shape=jax.ShapeDtypeStruct((rows, groups * wide), jnp.bfloat16),
        in_specs=[
            pl.BlockSpec(memory_space=pltpu.SMEM),
            pl.BlockSpec((rows, wide), lambda g: (0, g)),
            pl.BlockSpec((rows, heads * HEAD_SIZE), lambda g: (0, g)),
            pl.BlockSpec((rows, 2 * PAIR), lambda g: (0, 0)),
            pl.BlockSpec((rows, 2 * PAIR), lambda g: (0, 0)),
        ],
        out_specs=pl.BlockSpec((rows, wide), lambda g: (0, g)),
        scratch_shapes=[
            pltpu.VMEM((heads, rows, PAIR), jnp.bfloat16),
            pltpu.VMEM((heads, rows, PAIR), jnp.bfloat16),
            pltpu.VMEM((rows, PAIR), jnp.bfloat16),
            pltpu.VMEM((rows, PAIR), jnp.bfloat16),
            pltpu.VMEM((rows, PAIR), jnp.float32),
            pltpu.VMEM((rows, PAIR), jnp.float32),
        ],
        compiler_params=pltpu.CompilerParams(vmem_limit_bytes=48 << 20),
        cost_estimate=pl.CostEstimate(
            flops=5 * groups * heads * rows * rows * 128,
            bytes_accessed=2 * (2 * rows * wide * groups + rows * heads * HEAD_SIZE * groups),
            transcendentals=groups * heads * rows * rows // 2,
        ),
        name="attend_back",
    )(length, projected, grad_mixed, cosines, sines)


def ffn_kernel(
    cols,
    own_ref,
    resid_ref,
    grad_ref,
    wg_own,
    wu_own,
    wd_own,
    wg_far,
    wu_far,
    wd_far,
    wg_sib,
    wu_sib,
    wd_sib,
    u_all,
    dgu_all,
    mlp_all,
    back_all,
    relay_ref,
    land_ref,
    a_keep,
    a_send,
    b_keep,
    b_send,
    wg,
    wu,
    wd,
    b_all,
    b_turn,
    g_two,
    u_buf,
    dg_buf,
    du_buf,
    mlp_buf,
    back_buf,
    w_sems,
    ag_send,
    ag_recv,
    back_send,
    back_recv,
    relay_recv,
    pair_sems,
    lane_sems,
    tile_sems,
    io_sems,
):
    group, core, mate, row, col = place()
    sibling = (group + 1 - 2 * core, row, col)
    last = cols - 1
    depth = wg_own.shape[0]
    half = depth // 2
    units = wg_own.shape[1]
    rows = own_ref.shape[0]
    tile = units // cols
    beside = col + 1 - 2 * lax.rem(col, 2)
    facing = last - col
    inner = (col > 0) & (col < last)

    for step in range(1, cols):
        greet((group, row, lined(col, step, cols)))
    greet(sibling)
    pl.semaphore_wait(pltpu.get_barrier_semaphore(), cols)

    def pass_on(src, at, to, way):
        return pltpu.make_async_remote_copy(
            src_ref=src,
            dst_ref=b_all.at[at],
            send_sem=ag_send.at[way, at],
            recv_sem=ag_recv.at[at],
            device_id=(group, row, to),
            device_id_type=MESH_IDS,
        )

    @pl.when(col < last)
    def _():
        pass_on(own_ref, col, col + 1, 0).start()

    @pl.when(col > 0)
    def _():
        pass_on(own_ref, col, col - 1, 1).start()

    def order(at):
        return line_order(col, last, at)

    def load_g(at):
        side = lax.rem(at, 2)
        return pltpu.make_async_copy(grad_ref.at[order(at)], g_two.at[side], io_sems.at[6 + side])

    def rows_at(first, size):
        return pl.ds(pl.multiple_of(first, half), size)

    own_copy = pltpu.make_async_copy(own_ref, b_all.at[col], io_sems.at[0])
    own_copy.start()
    load_resid = pltpu.make_async_copy(resid_ref, mlp_buf, io_sems.at[8])
    far = (1 - row) * depth
    loads = []
    for at, (full, mine, across, shared) in enumerate(
        ((wg, wg_own, wg_far, wg_sib), (wu, wu_own, wu_far, wu_sib), (wd, wd_own, wd_far, wd_sib))
    ):
        loads += [
            pltpu.make_async_copy(mine, full.at[rows_at(row * depth, depth)], w_sems.at[3 * at]),
            pltpu.make_async_copy(
                across, full.at[rows_at(far + core * half, half)], w_sems.at[3 * at + 1]
            ),
            pltpu.make_async_copy(
                shared, full.at[rows_at(far + (1 - core) * half, half)], w_sems.at[3 * at + 2]
            ),
        ]
    for load in loads:
        load.start()
    load_g(0).start()
    load_resid.start()
    own_copy.wait()
    for load in loads:
        load.wait()

    def arrive(chunk):
        pass_on(b_all.at[chunk], chunk, col, 0).wait_recv()

        @pl.when((chunk < col) & (col < last))
        def _():
            pass_on(b_all.at[chunk], chunk, col + 1, 0).start()

        @pl.when((chunk > col) & (col > 0))
        def _():
            pass_on(b_all.at[chunk], chunk, col - 1, 1).start()

    def outputs(chunk):
        return (
            pltpu.make_async_copy(u_buf, u_all.at[chunk], io_sems.at[1]),
            pltpu.make_async_copy(dg_buf, dgu_all.at[chunk, :, 0:units], io_sems.at[2]),
            pltpu.make_async_copy(du_buf, dgu_all.at[chunk, :, units : 2 * units], io_sems.at[3]),
        )

    def mlp_out(chunk):
        return pltpu.make_async_copy(mlp_buf, mlp_all.at[chunk], io_sems.at[4])

    def slot_of(at):
        return lax.rem(at, cols - 1)

    def deliver(slot, to, place_there, at):
        return pltpu.make_async_remote_copy(
            src_ref=back_buf.at[slot],
            dst_ref=back_all.at[place_there],
            send_sem=back_send.at[at],
            recv_sem=back_recv.at[place_there],
            device_id=(group, row, to),
            device_id_type=MESH_IDS,
        )

    def hand_over(slot, to, box, at):
        return pltpu.make_async_remote_copy(
            src_ref=back_buf.at[slot],
            dst_ref=relay_ref.at[box],
            send_sem=back_send.at[at],
            recv_sem=relay_recv.at[box],
            device_id=(group, row, to),
            device_id_type=MESH_IDS,
        )

    own_back = pltpu.make_async_copy(back_buf.at[0], back_all.at[0], io_sems.at[5])
    at_end = jnp.logical_not(inner)

    def one_chunk(at, unused):
        chunk = order(at)
        side = lax.rem(at, 2)

        @pl.when(at_end & (at > 0))
        def _():
            arrive(order(at))

        @pl.when(inner & (at == 1))
        def _():
            arrive(order(1))
            arrive(order(2))

        @pl.when(inner & (at == 3))
        def _():
            arrive(order(3))

        load_g(at).wait()

        @pl.when(at < last)
        def _():
            load_g(at + 1).start()

        @pl.when(at > 0)
        def _():
            for copy in outputs(order(at - 1)):
                copy.wait()

        @pl.loop(0, units // tile)
        def _(step):
            lanes = aligned(step, tile)
            gate = dot_nn(b_all[chunk], wg[:, lanes])
            upward = dot_nn(b_all[chunk], wu[:, lanes])
            back = RES_MULT * dot_nn(g_two[side], wd[:, lanes])
            opened = 1.0 / (1.0 + jnp.exp(-gate))
            silu = gate * opened
            u_buf[:, lanes] = (silu * upward).astype(jnp.bfloat16)
            slope = opened * (1.0 + gate * (1.0 - opened))
            dg_buf[:, lanes] = (back * upward * slope).astype(jnp.bfloat16)
            du_buf[:, lanes] = (back * silu).astype(jnp.bfloat16)

        for copy in outputs(chunk):
            copy.start()

        @pl.when(at > 0)
        def _():
            mlp_out(order(at - 1)).wait()

        @pl.when(at == 0)
        def _():
            load_resid.wait()

        @pl.when(at == last)
        def _():
            own_back.wait()

        @pl.loop(0, 2 * depth // tile)
        def _(step):
            here = aligned(step, tile)
            back = dot_nt(dg_buf[...], wg[here, :]) + dot_nt(du_buf[...], wu[here, :])
            back_buf[slot_of(at), :, here] = back.astype(jnp.bfloat16)
            added = jnp.where(at == 0, mlp_buf[:, here].astype(jnp.float32), 0.0)
            mlp_buf[:, here] = (added + RES_MULT * dot_nt(u_buf[...], wd[here, :])).astype(
                jnp.bfloat16
            )

        mlp_out(chunk).start()

        @pl.when(at == 0)
        def _():
            own_back.start()

        @pl.when(at_end & (at == 1))
        def _():
            deliver(1, beside, 1, 1).start()

        @pl.when(at_end & (at == 2))
        def _():
            hand_over(2, beside, 1, 2).start()

        @pl.when(at_end & (at == 3))
        def _():
            deliver(0, facing, 2, 3).start()

        @pl.when(inner & (at == 3))
        def _():
            hand_over(0, facing, 0, 3).start()

        return unused

    lax.fori_loop(0, cols, one_chunk, 0)
    for copy in outputs(order(last)):
        copy.wait()
    mlp_out(order(last)).wait()

    loads = []
    for chunk in range(cols):
        here = slice(chunk * rows, (chunk + 1) * rows)
        loads += [
            pltpu.make_async_copy(
                dgu_all.at[chunk, :, 0:units], wg.at[here], w_sems.at[chunk]
            ),
            pltpu.make_async_copy(
                dgu_all.at[chunk, :, units : 2 * units], wu.at[here], w_sems.at[cols + chunk]
            ),
            pltpu.make_async_copy(u_all.at[chunk], wd.at[here], w_sems.at[2 * cols + chunk]),
        ]
    for load in loads:
        load.start()

    def relay(box, slot):
        hand_over(slot, facing, box, 3).wait_recv()
        load = pltpu.make_async_copy(relay_ref.at[box], mlp_buf, io_sems.at[4])
        load.start()
        load.wait()
        tall = min(64, rows)

        @pl.loop(0, rows // tall)
        def _(at):
            here = aligned(at, tall)
            back_buf[slot, here, :] = (
                back_buf[slot, here, :].astype(jnp.float32)
                + mlp_buf[here, :].astype(jnp.float32)
            ).astype(jnp.bfloat16)

    buffers = (dg_buf, du_buf, u_buf)

    def to_sibling(at, part):
        return pltpu.make_async_remote_copy(
            src_ref=buffers[part],
            dst_ref=land_ref.at[at, part],
            send_sem=pair_sems.at[0, at, part],
            recv_sem=pair_sems.at[1, at, part],
            device_id=sibling,
            device_id_type=MESH_IDS,
        )

    def landed(at, part):
        return pltpu.make_async_copy(land_ref.at[at, part], buffers[part], io_sems.at[1 + part])

    halfway = units // 2
    small = rows // 2
    mine, others = aligned(row, small), aligned(1 - row, small)

    def x_lane(high):
        return (
            pltpu.make_async_copy(
                dg_buf.at[mine], a_keep.at[high, :, 0:units], lane_sems.at[0]
            ),
            pltpu.make_async_copy(
                dg_buf.at[others], a_send.at[high, :, 0:units], lane_sems.at[1]
            ),
            pltpu.make_async_copy(
                u_buf.at[mine, 0:halfway],
                a_keep.at[high, :, units : units + halfway],
                lane_sems.at[2],
            ),
            pltpu.make_async_copy(
                u_buf.at[others, 0:halfway],
                a_send.at[high, :, units : units + halfway],
                lane_sems.at[3],
            ),
        )

    def y_lane(target):
        copies = []
        for side in range(2):
            here = slice(side * small, (side + 1) * small)
            copies += [
                pltpu.make_async_copy(
                    du_buf.at[here], target.at[side, :, 0:units], lane_sems.at[4 + 2 * side]
                ),
                pltpu.make_async_copy(
                    u_buf.at[here, halfway:units],
                    target.at[side, :, units : units + halfway],
                    lane_sems.at[5 + 2 * side],
                ),
            ]
        return copies

    def put_results(high, act):
        for copy in x_lane(high):
            act(copy)

        @pl.when(high == (group - core) // 2)
        def _():
            for copy in y_lane(b_keep):
                act(copy)

        @pl.when(high != (group - core) // 2)
        def _():
            for copy in y_lane(b_send):
                act(copy)

    def start_it(copy):
        copy.start()

    def wait_for(copy):
        copy.wait()

    def part_of(chunk):
        return slice(chunk * rows, (chunk + 1) * rows)

    def grad_tile(block, chunk):
        return pltpu.make_async_copy(
            grad_ref.at[chunk, :, aligned(block, rows)],
            mlp_buf.at[:, part_of(chunk)],
            tile_sems.at[chunk],
        )

    parts = range(3)

    def block_of(at):
        return 2 * lax.rem(at, 2) + jnp.where(at >= 2, core, 1 - core)

    for chunk in range(cols):
        grad_tile(block_of(0), chunk).start()
    for chunk in range(cols):
        b_turn[0, :, part_of(chunk)] = b_all[chunk, :, aligned(block_of(0), rows)].T
    for chunk in range(cols):
        grad_tile(block_of(0), chunk).wait()
    for chunk in range(cols):
        g_two[0, :, part_of(chunk)] = mlp_buf[:, part_of(chunk)].T
    for load in loads:
        load.wait()

    def one_block(at, unused):
        high = lax.rem(at, 2)
        is_own = at >= 2
        side = lax.rem(at, 2)
        following = block_of(jnp.minimum(at + 1, 3))

        @pl.when(inner & (at == 1))
        def _():
            relay(0, col)
            deliver(col, beside, 1, 1).start()
            relay(1, last - col)
            deliver(last - col, facing, 2, 2).start()

        @pl.when(at < 3)
        def _():
            for chunk in range(cols):
                grad_tile(following, chunk).start()

        @pl.when((at == 1) | (at == 2))
        def _():
            for part in parts:
                to_sibling(at - 1, part).wait_send()

        @pl.when(at == 3)
        def _():
            put_results(0, wait_for)

        @pl.when(is_own)
        def _():
            for part in parts:
                to_sibling(high, part).wait_recv()
                landed(high, part).start()
            for part in parts:
                landed(high, part).wait()

        @pl.when(at < 3)
        def _():
            for chunk in range(cols):
                grad_tile(following, chunk).wait()

        @pl.loop(0, cols)
        def _(step):
            lanes = aligned(step, tile)
            tokens = aligned(step, rows)

            def put(buffer, value):
                other = jnp.where(is_own, buffer[:, lanes].astype(jnp.float32), 0.0)
                buffer[:, lanes] = (other + value).astype(jnp.bfloat16)

            put(dg_buf, dot_nn(b_turn[side], wg[:, lanes]))
            b_turn[1 - side, :, tokens] = b_all[step, :, aligned(following, rows)].T
            put(du_buf, dot_nn(b_turn[side], wu[:, lanes]))
            g_two[1 - side, :, tokens] = mlp_buf[:, tokens].T
            put(u_buf, RES_MULT * dot_nn(g_two[side], wd[:, lanes]))

        @pl.when(jnp.logical_not(is_own))
        def _():
            for part in parts:
                to_sibling(at, part).start()

        @pl.when(is_own)
        def _():
            put_results(high, start_it)

        return unused

    lax.fori_loop(0, 4, one_block, 0)
    put_results(1, wait_for)
    for at in range(1, cols):
        deliver(0, beside, 1, at).wait_send()
    for at in range(1, 3):
        deliver(0, beside, at, at).wait_recv()
    for chunk in range(cols):

        @pl.when((col >= chunk) & (col < last))
        def _():
            pass_on(own_ref, chunk, col + 1, 0).wait_send()

        @pl.when((col <= chunk) & (col > 0))
        def _():
            pass_on(own_ref, chunk, col - 1, 1).wait_send()


def feed_forward(own_input, resid, grad_rows, weights, cols):
    rows, width = own_input.shape
    units = weights[0].shape[1]
    anywhere = pl.BlockSpec(memory_space=pl.ANY)
    bf16 = jnp.bfloat16
    lane = jax.ShapeDtypeStruct((2, rows // 2, units + units // 2), bf16)
    return pl.pallas_call(
        functools.partial(ffn_kernel, cols),
        out_shape=(
            jax.ShapeDtypeStruct((cols, rows, units), bf16),
            jax.ShapeDtypeStruct((cols, rows, 2 * units), bf16),
            jax.ShapeDtypeStruct((cols, rows, width), bf16),
            jax.ShapeDtypeStruct((3, rows, width), bf16),
            jax.ShapeDtypeStruct((2, rows, width), bf16),
            jax.ShapeDtypeStruct((2, 3, rows, units), bf16),
        )
        + (lane,) * 4,
        in_specs=[anywhere] * 12,
        out_specs=(anywhere,) * 10,
        scratch_shapes=[
            pltpu.VMEM((width, units), bf16),
            pltpu.VMEM((width, units), bf16),
            pltpu.VMEM((width, units), bf16),
            pltpu.VMEM((cols, rows, width), bf16),
            pltpu.VMEM((2, rows, width), bf16),
            pltpu.VMEM((2, rows, width), bf16),
            pltpu.VMEM((rows, units), bf16),
            pltpu.VMEM((rows, units), bf16),
            pltpu.VMEM((rows, units), bf16),
            pltpu.VMEM((rows, width), bf16),
            pltpu.VMEM((cols - 1, rows, width), bf16),
            pltpu.SemaphoreType.DMA((12,)),
            pltpu.SemaphoreType.DMA((2, cols)),
            pltpu.SemaphoreType.DMA((cols,)),
            pltpu.SemaphoreType.DMA((cols,)),
            pltpu.SemaphoreType.DMA((cols,)),
            pltpu.SemaphoreType.DMA((2,)),
            pltpu.SemaphoreType.DMA((2, 2, 3)),
            pltpu.SemaphoreType.DMA((8,)),
            pltpu.SemaphoreType.DMA((cols,)),
            pltpu.SemaphoreType.DMA((9,)),
        ],
        compiler_params=pltpu.CompilerParams(
            collective_id=2, has_side_effects=True, vmem_limit_bytes=60 << 20
        ),
        cost_estimate=pl.CostEstimate(
            flops=18 * cols * rows * width * units,
            bytes_accessed=800 << 20,
            transcendentals=cols * rows * units,
        ),
        name="feed_forward",
    )(own_input, resid, grad_rows, *weights)


def finish_kernel(
    cols,
    ig_ref,
    gq_ref,
    go_ref,
    gain_ref,
    gin_ref,
    sq_ref,
    so_ref,
    gsum_ref,
    q_keep,
    q_sib,
    q_a1,
    q_a2,
    q_b1,
    q_b2,
    q_z,
    o_keep,
    o_sib,
    o_a1,
    o_a2,
    o_b1,
    o_b2,
    o_z,
    gain_now,
    gain_in,
    ig_sems,
    gain_sems,
    q_sems,
    o_sems,
    qz_sems,
    oz_sems,
    local_sems,
):
    group, core, mate, row, col = place()
    pair = group - core
    high = pair // 2
    sibling = (pair + 1 - core, row, col)
    over_x = (group, 1 - row, col)
    over_y = (2 * (1 - high) + core, row, col)
    width = gin_ref.shape[2]

    def line(step):
        return lax.rem(col + step + cols, cols)

    barrier = pltpu.get_barrier_semaphore()

    def greet(device):
        pl.semaphore_signal(barrier, inc=1, device_id=device, device_id_type=MESH_IDS)

    greet(sibling)
    greet(over_x)
    greet(over_y)
    for step in range(1, cols):
        greet((mate, core, line(step)))
        greet((group, row, line(step)))

    @pl.when(core != row)
    def _():
        greet((mate, core, col))

    pl.semaphore_wait(barrier, 2 * cols + 1 + (core - row) * (core - row))

    def remote(src, dst, sems, at, device):
        return pltpu.make_async_remote_copy(
            src_ref=src,
            dst_ref=dst,
            send_sem=sems.at[0, at],
            recv_sem=sems.at[1, at],
            device_id=device,
            device_id_type=MESH_IDS,
        )

    def lanes(block, size):
        return pl.ds(pl.multiple_of(block * size, size), size)

    matrices = (
        (gq_ref, sq_ref, q_keep, q_sib, q_a1, q_a2, q_b1, q_b2, q_z, q_sems, qz_sems),
        (go_ref, so_ref, o_keep, o_sib, o_a1, o_a2, o_b1, o_b2, o_z, o_sems, oz_sems),
    )

    def moves(m):
        grads, out, keep, sib, a1, a2, b1, b2, zb, sems, z_sems = matrices[m]
        return dict(
            s0=remote(grads.at[:, 1 - core], sib, sems, 0, sibling),
            a1=remote(grads.at[:, core, 1 - row], a1, sems, 1, over_x),
            a2=remote(keep.at[1 - high, row], a2, sems, 2, over_y),
            b1=remote(sib.at[1 - high], b1, sems, 3, over_y),
            b2=remote(sib.at[high, 1 - row], b2, sems, 4, over_x),
            own=pltpu.make_async_copy(grads.at[:, core], keep, local_sems.at[m]),
        )

    copies = (moves(0), moves(1))

    def rows_plus(into, more):
        rows = into.shape[0]
        step = min(32, rows)

        @pl.loop(0, rows // step)
        def _(at):
            here = pl.ds(pl.multiple_of(at * step, step), step)
            into[here, :] = (
                into[here, :].astype(jnp.float32) + more[here, :].astype(jnp.float32)
            ).astype(into.dtype)

    def token_copy(step, at):
        return remote(
            ig_ref.at[:, lanes(line(step), width)],
            gin_ref.at[at],
            ig_sems,
            step,
            (mate, core, line(step)),
        )

    own_tokens = pltpu.make_async_copy(
        ig_ref.at[:, lanes(col, width)], gin_ref.at[col], local_sems.at[2]
    )

    for m in range(2):
        copies[m]["s0"].start()
        copies[m]["a1"].start()
        copies[m]["own"].start()
    @pl.when(core == row)
    def _():
        own_tokens.start()
        for step in range(1, cols):
            token_copy(step, col).start()

    gain_load = pltpu.make_async_copy(gain_ref, gain_now.at[0], local_sems.at[3])
    gain_load.start()
    gain_load.wait()
    near = (
        sibling,
        over_x,
        over_y,
        (group, row, col + 1 - 2 * lax.rem(col, 2)),
        (group, row, lax.rem(col + cols // 2, cols)),
    )

    def gain_round(at):
        exchange = remote(gain_now.at[at], gain_in.at[at], gain_sems, at, near[at])
        exchange.start()
        exchange.wait()
        gain_now[at + 1] = gain_now[at] + gain_in[at]

    gain_round(0)
    for m in range(2):
        copies[m]["s0"].wait()
        copies[m]["b1"].start()
    gain_round(1)
    for m in range(2):
        grads, out, keep, sib, a1, a2, b1, b2, zb, sems, z_sems = matrices[m]
        copies[m]["own"].wait()
        copies[m]["a1"].wait()
        rows_plus(keep.at[1 - high, row], a1.at[1 - high])
        copies[m]["a2"].start()
    for m in range(2):
        grads, out, keep, sib, a1, a2, b1, b2, zb, sems, z_sems = matrices[m]
        copies[m]["b1"].wait()
        rows_plus(sib.at[high, 1 - row], b1.at[1 - row])
        copies[m]["b2"].start()

    @pl.when(core != row)
    def _():
        for step in range(cols):
            token_copy(step, col).start()

    gain_round(2)
    for m in range(2):
        grads, out, keep, sib, a1, a2, b1, b2, zb, sems, z_sems = matrices[m]
        rows_plus(keep.at[high, row], a1.at[high])
        rows_plus(sib.at[high, row], b1.at[row])

    def z_moves(m, side, source):
        grads, out, keep, sib, a1, a2, b1, b2, zb, sems, z_sems = matrices[m]
        held = (keep, sib)[side]
        wide = zb.shape[3]
        return [
            pltpu.make_async_remote_copy(
                src_ref=held.at[high, row, :, lanes(line(step), wide)],
                dst_ref=zb.at[side, line(source(step))],
                send_sem=z_sems.at[0, side, step],
                recv_sem=z_sems.at[1, side, step],
                device_id=(group, row, line(step)),
                device_id_type=MESH_IDS,
            )
            for step in range(1, cols)
        ]

    for side, last_copy in ((0, "a2"), (1, "b2")):
        for m in range(2):
            grads, out, keep, sib, a1, a2, b1, b2, zb, sems, z_sems = matrices[m]
            copies[m][last_copy].wait()
            rows_plus((keep, sib)[side].at[high, row], (a2, b2)[side])
            for copy in z_moves(m, side, lambda step: 0):
                copy.start()
    gain_round(3)
    gain_round(4)
    gsum_ref[...] = gain_now[5]
    for side in range(2):
        for m in range(2):
            grads, out, keep, sib, a1, a2, b1, b2, zb, sems, z_sems = matrices[m]
            for copy in z_moves(m, side, lambda step: 0):
                copy.wait_send()
            for copy in z_moves(m, side, lambda step: -step):
                copy.wait_recv()
            held = (keep, sib)[side]
            wide = zb.shape[3]
            at_core = core if side == 0 else 1 - core
            rows = zb.shape[2]
            tall = min(32, rows)

            @pl.loop(0, rows // tall)
            def _(at):
                here = pl.ds(pl.multiple_of(at * tall, tall), tall)
                total = held[high, row, here, lanes(col, wide)].astype(jnp.float32)
                for step in range(1, cols):
                    total = total + zb[side, line(-step), here, :].astype(jnp.float32)
                out[at_core, here, :] = total

    for step in range(1, cols):
        token_copy(step, line(-step)).wait_recv()
        token_copy(step, col).wait_send()

    @pl.when(core != row)
    def _():
        token_copy(0, col).wait_recv()
        token_copy(0, col).wait_send()

    @pl.when(core == row)
    def _():
        own_tokens.wait()


def finish(input_grad, grad_q, grad_o, gains, cols):
    anywhere = pl.BlockSpec(memory_space=pl.ANY)
    in_vmem = pl.BlockSpec(memory_space=pltpu.VMEM)
    bf16, f32 = jnp.bfloat16, jnp.float32
    length, full = input_grad.shape
    rows = grad_q.shape[0] // 8

    def buffers(wide):
        return [
            pltpu.VMEM((2, 2, rows, wide), bf16),
            pltpu.VMEM((2, 2, rows, wide), bf16),
            pltpu.VMEM((2, rows, wide), bf16),
            pltpu.VMEM((rows, wide), bf16),
            pltpu.VMEM((2, rows, wide), bf16),
            pltpu.VMEM((rows, wide), bf16),
            pltpu.VMEM((2, cols, rows, wide // cols), bf16),
        ]

    wide_q, wide_o = grad_q.shape[1], grad_o.shape[1]
    return pl.pallas_call(
        functools.partial(finish_kernel, cols),
        out_shape=(
            jax.ShapeDtypeStruct((cols, length, full // cols), bf16),
            jax.ShapeDtypeStruct((2, rows, wide_q // cols), f32),
            jax.ShapeDtypeStruct((2, rows, wide_o // cols), f32),
            jax.ShapeDtypeStruct(gains.shape, f32),
        ),
        in_specs=[anywhere] * 4,
        out_specs=(anywhere, in_vmem, in_vmem, in_vmem),
        scratch_shapes=buffers(wide_q)
        + buffers(wide_o)
        + [
            pltpu.VMEM((6,) + gains.shape, f32),
            pltpu.VMEM((5,) + gains.shape, f32),
            pltpu.SemaphoreType.DMA((2, cols)),
            pltpu.SemaphoreType.DMA((2, 5)),
            pltpu.SemaphoreType.DMA((2, 5)),
            pltpu.SemaphoreType.DMA((2, 5)),
            pltpu.SemaphoreType.DMA((2, 2, cols)),
            pltpu.SemaphoreType.DMA((2, 2, cols)),
            pltpu.SemaphoreType.DMA((4,)),
        ],
        compiler_params=pltpu.CompilerParams(
            collective_id=3, has_side_effects=True, vmem_limit_bytes=40 << 20
        ),
        cost_estimate=pl.CostEstimate(flops=0, bytes_accessed=300 << 20, transcendentals=0),
        name="finish",
    )(
        input_grad,
        grad_q.reshape(2, 2, 2, rows, wide_q),
        grad_o.reshape(2, 2, 2, rows, wide_o),
        gains,
    )


def one_sequence_body(
    tokens,
    cotangent,
    lengths,
    deal_order,
    gain_attn,
    gain_ffn,
    w_query,
    key_value_weight,
    w_out,
    w_gate_up,
    w_down,
):
    seq_group, rows_local, width_local = tokens.shape
    row_count = lax.axis_size("row")
    col_count = lax.axis_size("col")
    full_width = width_local * col_count
    slot_len = rows_local * row_count
    group, core, mate, row, col = place()
    query_half = w_query.shape[1] // 2
    kv_half = key_value_weight.shape[2] // 2
    hidden = w_down.shape[1]

    def core_half(matrix, axis):
        width = matrix.shape[axis] // 2
        return lax.dynamic_slice_in_dim(matrix, core * width, width, axis)

    def joined(mine, other, at):
        return jnp.where(
            at == 0, jnp.concatenate([mine, other]), jnp.concatenate([other, mine])
        )

    def from_sibling(value):
        return lax.ppermute(value, "dp", SIBLINGS)

    def half_rows(matrix):
        return core_half(matrix, 0)

    pack_q = jnp.concatenate(
        [
            core_half(w_query, 1),
            core_half(key_value_weight[:, 0], 1),
            core_half(key_value_weight[:, 1], 1),
        ],
        axis=1,
    )
    pack_o = core_half(w_out, 1)
    gain_one = gain_attn.astype(jnp.float32)
    gain_two = gain_ffn.astype(jnp.float32)
    own_tokens, attn_input = start_exchange(tokens, gain_one, col_count)

    length = lax.dynamic_slice_in_dim(lengths, mate * seq_group + col, 1)
    given_pos = row * rows_local + jnp.arange(rows_local, dtype=jnp.int32)
    given_lengths = lax.dynamic_slice_in_dim(lengths, group * seq_group, seq_group)
    given_live = given_pos[None, :, None] < given_lengths[:, None, None]
    everyone = lax.all_gather(cotangent, "dp", axis=0, tiled=True)
    everyone, attn_input = lax.optimization_barrier((everyone, attn_input))
    picked = pick_sequences(everyone, deal_order, group * seq_group, seq_group)
    picked = jnp.where(given_live, picked, jnp.zeros_like(picked))
    weights_qkv, weights_out, given = gather_weights(
        pack_q, pack_o, picked, row_count, col_count
    )
    line_cot = lax.all_gather(given, "col", axis=2, tiled=True)
    own_grad = lax.dynamic_index_in_dim(line_cot, col, keepdims=False).astype(jnp.float32)

    w_gate_up, w_down, weights_qkv = lax.optimization_barrier((w_gate_up, w_down, weights_qkv))
    far_gate_up = lax.ppermute(half_rows(w_gate_up), "row", OVER_X)
    far_down = lax.ppermute(half_rows(w_down), "row", OVER_X)
    own_mats = (w_gate_up[:, 0], w_gate_up[:, 1], w_down)

    cosine_table, sine_table = rope_tables(jnp.arange(slot_len, dtype=jnp.int32), HEAD_SIZE)
    cosine_table, sine_table = lax.optimization_barrier((cosine_table, sine_table))
    cosines = jnp.concatenate(
        [jnp.tile(cosine_table, (1, 6)), jnp.ones((slot_len, HEAD_SIZE), jnp.float32)], axis=1
    )
    turning = jnp.concatenate([-sine_table, sine_table], axis=1)
    sines = jnp.concatenate(
        [jnp.tile(turning, (1, 3)), jnp.zeros((slot_len, HEAD_SIZE), jnp.float32)], axis=1
    )
    own_float = own_tokens.astype(jnp.float32)
    scale_one = lax.rsqrt(jnp.mean(own_float * own_float, axis=1, keepdims=True) + EPSILON)
    projected, heads_out = attend_fast(
        length, attn_input, weights_qkv, cosines, sines, col_count
    )

    def summed_rows(partial):
        count = partial.shape[0] // 2
        mine = lax.dynamic_slice_in_dim(partial, core * count, count)
        other = lax.dynamic_slice_in_dim(partial, (1 - core) * count, count)
        return mine.astype(jnp.float32) + from_sibling(other).astype(jnp.float32)

    attn_rows = summed_rows(expand_local(heads_out, weights_out).astype(jnp.bfloat16))
    resid = own_float + RES_MULT * attn_rows
    scale_two = lax.rsqrt(jnp.mean(resid * resid, axis=1, keepdims=True) + EPSILON)
    own_ffn = (resid * scale_two * gain_two).astype(jnp.bfloat16)

    far_gate_up, far_down, own_ffn, own_mats = lax.optimization_barrier(
        (far_gate_up, far_down, own_ffn, own_mats)
    )
    far_mats = (far_gate_up[:, 0], far_gate_up[:, 1], far_down)
    sibling_mats = tuple(from_sibling(matrix) for matrix in far_mats)
    *unused, a_keep, a_send, b_keep, b_send = feed_forward(
        own_ffn,
        resid.astype(jnp.bfloat16),
        line_cot,
        own_mats + far_mats + sibling_mats,
        col_count,
    )
    mlp_part, back_part = unused[2:4]
    grad_normed_two = jnp.sum(back_part.astype(jnp.float32), axis=0)
    out_cols = lax.psum_scatter(mlp_part, "col", scatter_dimension=2, tiled=True)

    def plus(kept, came):
        return (kept.astype(jnp.float32) + came.astype(jnp.float32)).astype(jnp.bfloat16)

    a_came = lax.ppermute(a_send, "row", OVER_X)
    b_came = lax.ppermute(b_send, "dp", OVER_Y)

    weighted_two = grad_normed_two * gain_two
    inner_two = jnp.sum(weighted_two * resid, axis=1, keepdims=True)
    grad_resid = (
        own_grad + scale_two * weighted_two - resid * scale_two**3 * inner_two / full_width
    )
    gain_two_part = jnp.sum(grad_normed_two * resid * scale_two, axis=0)
    own_attn_grad = (RES_MULT * grad_resid).astype(jnp.bfloat16)
    grad_attn = joined(own_attn_grad, from_sibling(own_attn_grad), core)
    grad_heads = contract_local(grad_attn, weights_out).astype(jnp.bfloat16)
    grad_out = token_outer(grad_attn, heads_out).astype(jnp.bfloat16)
    grad_projected = attend_back_fast(
        length, projected, grad_heads, cosines, sines, col_count
    )
    a_sum, b_sum, grad_projected = lax.optimization_barrier(
        (plus(a_keep, a_came), plus(b_keep, b_came), grad_projected)
    )
    high = group // 2

    def one_of(pair, at):
        return lax.dynamic_index_in_dim(pair, at, keepdims=False)

    a_last = lax.ppermute(one_of(a_sum, 1 - high), "dp", OVER_Y)
    b_last = lax.ppermute(one_of(b_sum, 1 - row), "row", OVER_X)
    grad_normed_one = summed_rows(expand_local(grad_projected, weights_qkv).astype(jnp.bfloat16))
    grad_qkv = token_outer(attn_input, grad_projected).astype(jnp.bfloat16)
    weighted_one = grad_normed_one * gain_one
    inner_one = jnp.sum(weighted_one * own_float, axis=1, keepdims=True)
    own_input_grad = (
        grad_resid
        + scale_one * weighted_one
        - own_float * scale_one**3 * inner_one / full_width
    ).astype(jnp.bfloat16)
    gain_one_part = jnp.sum(grad_normed_one * own_float * scale_one, axis=0)
    a_last, b_last, own_input_grad = lax.optimization_barrier((a_last, b_last, own_input_grad))
    gains = jnp.stack([gain_one_part, gain_two_part]).reshape(8, -1)
    given_grad, sums_q, sums_o, gain_sums = finish(
        own_input_grad, grad_qkv, grad_out, gains, col_count
    )
    out_cols, a_last, b_last, a_sum, b_sum, given_grad = lax.optimization_barrier(
        (out_cols, a_last, b_last, a_sum, b_sum, given_grad)
    )
    given_out = lax.ppermute(out_cols, ("dp", "row"), CROSSED)
    layer_out = jnp.where(given_live, given_out.astype(jnp.float32), 0.0)
    input_grad = given_grad.astype(jnp.float32)
    a_total = one_of(a_sum, high).astype(jnp.float32) + a_last.astype(jnp.float32)
    b_total = one_of(b_sum, row).astype(jnp.float32) + b_last.astype(jnp.float32)
    sums_gate_up = jnp.stack([a_total[:, :hidden], b_total[:, :hidden]], axis=1)
    sums_down = jnp.concatenate([a_total[:, hidden:], b_total[:, hidden:]], axis=1)
    grad_gain_attn, grad_gain_ffn = gain_sums.reshape(2, full_width)

    def both_cores(sums):
        return jnp.concatenate([sums[0], sums[1]], axis=1)

    qk = query_half + kv_half
    out_query = both_cores(sums_q[:, :, :query_half])
    out_kv = jnp.stack(
        [
            both_cores(sums_q[:, :, query_half:qk]),
            both_cores(sums_q[:, :, qk:]),
        ],
        axis=1,
    )
    out_out = both_cores(sums_o)
    return (
        layer_out,
        input_grad,
        out_query,
        out_kv,
        out_out,
        sums_gate_up,
        sums_down,
        grad_gain_attn,
        grad_gain_ffn,
    )


def general_body(
    tokens,
    cotangent,
    lengths,
    deal_order,
    gain_attn,
    gain_ffn,
    w_query,
    key_value_weight,
    w_out,
    w_gate_up,
    w_down,
):
    seq_group, rows_local, width_local = tokens.shape
    row_count = lax.axis_size("row")
    col_count = lax.axis_size("col")
    full_width = width_local * col_count
    slot_len = rows_local * row_count
    total_rows = seq_group * rows_local
    head_size = HEAD_SIZE
    query_width = w_query.shape[1]
    kv_width = key_value_weight.shape[2]
    kv_heads = kv_width // head_size
    group_size = query_width // kv_width
    group_index = lax.axis_index("dp")
    row_index = lax.axis_index("row")
    col_index = lax.axis_index("col")
    matrices = {
        "qkv": jnp.concatenate(
            [w_query, key_value_weight.reshape(key_value_weight.shape[0], 2 * kv_width)], axis=1
        ),
        "out": w_out,
        "gate_up": w_gate_up,
        "down": w_down,
    }

    def contract_with(operand, which_one):
        return contract_rows(operand, matrices[which_one])

    def expand_with(operand, which_one):
        return expand_rows(operand, matrices[which_one])

    own_cotangent = bring_cotangent(cotangent, deal_order, group_index * seq_group)
    own_rows = tokens
    seq_lens = lax.dynamic_slice_in_dim(lengths, group_index * seq_group, seq_group)
    local_pos = row_index * rows_local + jnp.arange(rows_local, dtype=jnp.int32)
    key_pos = jnp.arange(slot_len, dtype=jnp.int32)
    live_rows = (local_pos[None, :] < seq_lens[:, None]).astype(jnp.float32).reshape(total_rows, 1)
    cosine_table, sine_table = rope_tables(jnp.tile(local_pos, seq_group), head_size)
    own_tokens = own_rows.reshape(total_rows, width_local)
    wide_float = widen_cols(own_tokens).astype(jnp.float32)
    scale_one = lax.rsqrt(jnp.mean(wide_float * wide_float, axis=1, keepdims=True) + EPSILON)
    gain_one = gain_attn.astype(jnp.float32)
    first_normed = wide_float * scale_one
    attn_input = (first_normed * gain_one).astype(jnp.bfloat16)
    projected = contract_with(attn_input, "qkv")
    query_lin = projected[:, :query_width].reshape(total_rows, query_width // head_size, head_size)
    key_lin = projected[:, query_width : query_width + kv_width].reshape(
        total_rows, kv_heads, head_size
    )
    value_lin = projected[:, query_width + kv_width :]
    query_rows = rotary_embed(query_lin, cosine_table, sine_table).astype(jnp.bfloat16)
    keys_own = (
        rotary_embed(key_lin, cosine_table, sine_table)
        .astype(jnp.bfloat16)
        .reshape(seq_group, rows_local, kv_width)
    )
    values_own = value_lin.astype(jnp.bfloat16).reshape(seq_group, rows_local, kv_width)
    all_keys, all_values = (
        lax.all_gather(keys_own, "row", axis=1, tiled=True),
        lax.all_gather(values_own, "row", axis=1, tiled=True),
    )
    query_split = query_rows.reshape(seq_group, rows_local, kv_heads, group_size, head_size)
    key_split = all_keys.reshape(seq_group, slot_len, kv_heads, head_size)
    value_split = all_values.reshape(seq_group, slot_len, kv_heads, head_size)

    def forward_seq(inputs):
        return attend(inputs, key_pos, local_pos)

    mixed_heads, row_max, row_sums = lax.map(
        forward_seq, (query_split, key_split, value_split, seq_lens)
    )
    heads_out = mixed_heads.reshape(total_rows, query_width).astype(jnp.bfloat16)
    attn_local = narrow_cols(expand_with(heads_out, "out"))
    resid = own_tokens.astype(jnp.float32) + RES_MULT * attn_local
    gain_two = lax.dynamic_slice_in_dim(
        gain_ffn.astype(jnp.float32), col_index * width_local, width_local
    )
    scale_two = lax.rsqrt(sum_over_cols(jnp.sum(resid * resid, axis=1)) / full_width + EPSILON)[
        :, None
    ]
    normed_two = resid * scale_two
    ffn_input = widen_cols((normed_two * gain_two).astype(jnp.bfloat16))
    gate_up = contract_with(ffn_input, "gate_up")
    gate = gate_up[:, 0]
    upward = gate_up[:, 1]
    sigmoid_gate = jax.nn.sigmoid(gate)
    silu_gate = gate * sigmoid_gate
    hidden = (silu_gate * upward).astype(jnp.bfloat16)
    ffn_local = narrow_cols(expand_with(hidden, "down"))
    layer_out = live_rows * (resid + RES_MULT * ffn_local)
    grad_rows = live_rows * own_cotangent.reshape(total_rows, width_local).astype(jnp.float32)
    grad_ffn = widen_cols((RES_MULT * grad_rows).astype(jnp.bfloat16))
    grad_hidden = contract_with(grad_ffn, "down")
    grad_down = token_outer(grad_ffn, hidden)
    slope = sigmoid_gate * (1.0 + gate * (1.0 - sigmoid_gate))
    grad_gate_rows = jnp.stack(
        [grad_hidden * upward * slope, grad_hidden * silu_gate], axis=1
    ).astype(jnp.bfloat16)
    grad_gate_up = token_outer(ffn_input, grad_gate_rows)
    grad_normed_two = narrow_cols(expand_with(grad_gate_rows, "gate_up"))
    weighted_two = grad_normed_two * gain_two
    inner_two = sum_over_cols(jnp.sum(weighted_two * resid, axis=1))[:, None]
    grad_resid = (
        grad_rows + scale_two * weighted_two - resid * scale_two**3 * inner_two / full_width
    )
    gain_two_part = jnp.sum(grad_normed_two * normed_two, axis=0)
    grad_attn = widen_cols((RES_MULT * grad_resid).astype(jnp.bfloat16))
    grad_heads = contract_with(grad_attn, "out").astype(jnp.bfloat16)
    grad_out = token_outer(grad_attn, heads_out)
    grad_split = grad_heads.reshape(seq_group, rows_local, kv_heads, group_size, head_size)

    def backward_seq(inputs):
        return attend_back(inputs, key_pos, local_pos)

    grad_query, grad_key, grad_value = lax.map(
        backward_seq, (query_split, key_split, value_split, grad_split, row_max, row_sums, seq_lens)
    )
    key_part, value_part = (
        lax.psum_scatter(
            grad_key.reshape(seq_group, slot_len, kv_width).astype(jnp.bfloat16),
            "row",
            scatter_dimension=1,
            tiled=True,
        ).astype(jnp.float32),
        lax.psum_scatter(
            grad_value.reshape(seq_group, slot_len, kv_width).astype(jnp.bfloat16),
            "row",
            scatter_dimension=1,
            tiled=True,
        ).astype(jnp.float32),
    )
    query_back = rotary_embed(
        grad_query.reshape(total_rows, query_width // head_size, head_size),
        cosine_table,
        -sine_table,
    ).reshape(total_rows, query_width)
    key_back = rotary_embed(
        key_part.reshape(total_rows, kv_heads, head_size), cosine_table, -sine_table
    ).reshape(total_rows, kv_width)
    grad_projected = jnp.concatenate(
        [query_back, key_back, value_part.reshape(total_rows, kv_width)], axis=1
    ).astype(jnp.bfloat16)
    grad_qkv = token_outer(attn_input, grad_projected)
    grad_normed_one = expand_with(grad_projected, "qkv")
    weighted_one = grad_normed_one * gain_one
    inner_one = jnp.sum(weighted_one * wide_float, axis=1, keepdims=True)
    input_part = scale_one * weighted_one - wide_float * scale_one**3 * inner_one / full_width
    input_grad = grad_resid + narrow_cols(input_part)
    gain_one_part = jnp.sum(grad_normed_one * first_normed, axis=0)
    gain_two_full = lax.dynamic_update_slice_in_dim(
        jnp.zeros((full_width,), jnp.float32), gain_two_part, col_index * width_local, 0
    )
    grad_gain_attn, grad_gain_ffn = lax.psum((gain_one_part, gain_two_full), ("dp", "row", "col"))
    sums_qkv, sums_out, sums_gate_up, sums_down = (
        lax.psum_scatter(
            grad_qkv.astype(jnp.bfloat16), ("dp", "row"), scatter_dimension=0, tiled=True
        ).astype(jnp.float32),
        lax.psum_scatter(
            grad_out.astype(jnp.bfloat16), ("dp", "row"), scatter_dimension=0, tiled=True
        ).astype(jnp.float32),
        lax.psum_scatter(
            grad_gate_up.astype(jnp.bfloat16), ("dp", "row"), scatter_dimension=0, tiled=True
        ).astype(jnp.float32),
        lax.psum_scatter(
            grad_down.astype(jnp.bfloat16), ("dp", "row"), scatter_dimension=0, tiled=True
        ).astype(jnp.float32),
    )
    out_query = sums_qkv[:, :query_width]
    out_kv = sums_qkv[:, query_width:].reshape(sums_qkv.shape[0], 2, kv_width)
    return (
        layer_out.reshape(seq_group, rows_local, width_local),
        input_grad.reshape(seq_group, rows_local, width_local),
        out_query,
        out_kv,
        sums_out,
        sums_gate_up,
        sums_down,
        grad_gain_attn,
        grad_gain_ffn,
    )


def body(tokens, cotangent, lengths, deal_order, gain_attn, gain_ffn, w_query, key_value_weight, *rest):
    sizes = (lax.axis_size("dp"), lax.axis_size("row"), lax.axis_size("col"))
    one_each = sizes == (4, 2, 4) and tokens.shape[0] == sizes[2]
    pairs = w_query.shape[1] == 8 * HEAD_SIZE and key_value_weight.shape[2] == 2 * HEAD_SIZE
    chosen = one_sequence_body if one_each and pairs else general_body
    return chosen(
        tokens, cotangent, lengths, deal_order, gain_attn, gain_ffn, w_query, key_value_weight, *rest
    )


def solution(mesh):
    placed = (
        P("dp", "row", "col"),
        P("dp", "row", "col"),
        P(),
        P(),
        P(),
        P(),
        P("row", "col"),
        P("row", None, "col"),
        P("row", "col"),
        P("row", None, "col"),
        P("row", "col"),
    )
    return jax.shard_map(
        body,
        mesh=mesh,
        in_specs=placed,
        out_specs=(
            P("dp", "row", "col"),
            P("dp", "row", "col"),
            P(("dp", "row"), "col"),
            P(("dp", "row"), None, "col"),
            P(("dp", "row"), "col"),
            P(("dp", "row"), None, "col"),
            P(("dp", "row"), "col"),
            P(),
            P(),
        ),
        check_vma=False,
    )
```

```python
import functools

import jax
import jax.numpy as jnp
from jax import lax
from jax.experimental import pallas as pl
from jax.experimental.pallas import tpu as pltpu
from jax.sharding import PartitionSpec as P

HEAD_SIZE = 64


EPSILON = 1e-05
THETA = 10000000.0
ATTN_MULT = 0.015625
RES_MULT = 0.22
MASKED = -1e30


def rope_tables(positions, head_size):
    halves = jnp.arange(head_size // 2, dtype=jnp.float32)
    inverse_freq = THETA ** (-(halves * 2.0) / head_size)
    angles = positions.astype(jnp.float32)[:, None] * inverse_freq[None, :]
    return (jnp.cos(angles), jnp.sin(angles))


def rotary_embed(value_rows, cosine_table, sine_table):
    middle = value_rows.shape[-1] // 2
    first_half = value_rows[..., :middle]
    second_half = value_rows[..., middle:]
    cos_part = cosine_table[:, None, :]
    sin_part = sine_table[:, None, :]
    return jnp.concatenate(
        [
            first_half * cos_part - second_half * sin_part,
            second_half * cos_part + first_half * sin_part,
        ],
        axis=-1,
    )


def widen_cols(value_rows):
    return lax.all_gather(value_rows, "col", axis=1, tiled=True)


def narrow_cols(value_rows):
    return lax.psum_scatter(value_rows, "col", scatter_dimension=1, tiled=True)


def sum_over_cols(value_rows):
    return lax.psum(value_rows, "col")


def contract_local(operand, matrix):
    return lax.dot_general(
        operand, matrix, (((1,), (0,)), ((), ())), preferred_element_type=jnp.float32
    )


def expand_local(operand, matrix):
    trailing = tuple(range(1, operand.ndim))
    return lax.dot_general(
        operand, matrix, ((trailing, trailing), ((), ())), preferred_element_type=jnp.float32
    )


def token_outer(features, grads):
    return lax.dot_general(
        features, grads, (((0,), (0,)), ((), ())), preferred_element_type=jnp.float32
    )


def contract_rows(operand, matrix):
    return contract_local(operand, lax.all_gather(matrix, "row", axis=0, tiled=True))


def expand_rows(operand, matrix):
    return expand_local(operand, lax.all_gather(matrix, "row", axis=0, tiled=True))


def split_keys(key_seq, value_seq, key_pos):
    slot_len = key_seq.shape[0]
    width = min(512, slot_len)
    count = slot_len // width
    return (
        key_seq.reshape(count, width, key_seq.shape[1], key_seq.shape[2]),
        value_seq.reshape(count, width, value_seq.shape[1], value_seq.shape[2]),
        key_pos.reshape(count, width),
    )


def block_scores(query_seq, key_block, pos_block, query_pos, length):
    scores = (
        jnp.einsum("qkgd,tkd->kgqt", query_seq, key_block, preferred_element_type=jnp.float32)
        * ATTN_MULT
    )
    allowed = (pos_block[None, :] <= query_pos[:, None]) & (pos_block[None, :] < length)
    return jnp.where(allowed, scores, MASKED)


def attend(inputs, key_pos, query_pos):
    query_seq, key_seq, value_seq, length = inputs
    key_blocks, value_blocks, pos_blocks = split_keys(key_seq, value_seq, key_pos)
    stat_shape = (query_seq.shape[1], query_seq.shape[2], query_seq.shape[0], 1)

    def gather_stats(carry, entry):
        running_max, running_sum = carry
        key_block, pos_block = entry
        scores = block_scores(query_seq, key_block, pos_block, query_pos, length)
        new_max = jnp.maximum(running_max, jnp.max(scores, axis=-1, keepdims=True))
        new_sum = running_sum * jnp.exp(running_max - new_max) + jnp.sum(
            jnp.exp(scores - new_max), axis=-1, keepdims=True
        )
        return ((new_max, new_sum), None)

    start_stats = (jnp.full(stat_shape, MASKED, jnp.float32), jnp.zeros(stat_shape, jnp.float32))
    (row_max, row_sums), unused = lax.scan(gather_stats, start_stats, (key_blocks, pos_blocks))

    def mix_values(running, entry):
        key_block, value_block, pos_block = entry
        scores = block_scores(query_seq, key_block, pos_block, query_pos, length)
        weights = jnp.exp(scores - row_max) / row_sums
        return (
            running
            + jnp.einsum(
                "kgqt,tkd->qkgd",
                weights.astype(jnp.bfloat16),
                value_block,
                preferred_element_type=jnp.float32,
            ),
            None,
        )

    start_mix = jnp.zeros(query_seq.shape, jnp.float32)
    mixed_heads, unused = lax.scan(mix_values, start_mix, (key_blocks, value_blocks, pos_blocks))
    return (mixed_heads, row_max, row_sums)


def attend_back(inputs, key_pos, query_pos):
    query_seq, key_seq, value_seq, grad_mixed, row_max, row_sums, length = inputs
    key_blocks, value_blocks, pos_blocks = split_keys(key_seq, value_seq, key_pos)

    def block_weights(key_block, value_block, pos_block):
        scores = block_scores(query_seq, key_block, pos_block, query_pos, length)
        weights = jnp.exp(scores - row_max) / row_sums
        grad_weights = jnp.einsum(
            "qkgd,tkd->kgqt", grad_mixed, value_block, preferred_element_type=jnp.float32
        )
        return (weights, grad_weights)

    def gather_centre(running, entry):
        weights, grad_weights = block_weights(*entry)
        return (running + jnp.sum(weights * grad_weights, axis=-1, keepdims=True), None)

    start_centre = jnp.zeros(row_max.shape, jnp.float32)
    centre, unused = lax.scan(gather_centre, start_centre, (key_blocks, value_blocks, pos_blocks))

    def grads_block(running, entry):
        key_block = entry[0]
        weights, grad_weights = block_weights(*entry)
        grad_scores = (weights * (grad_weights - centre)).astype(jnp.bfloat16)
        grad_query = (
            running
            + jnp.einsum(
                "kgqt,tkd->qkgd", grad_scores, key_block, preferred_element_type=jnp.float32
            )
            * ATTN_MULT
        )
        grad_key = (
            jnp.einsum("kgqt,qkgd->tkd", grad_scores, query_seq, preferred_element_type=jnp.float32)
            * ATTN_MULT
        )
        grad_value = jnp.einsum(
            "kgqt,qkgd->tkd",
            weights.astype(jnp.bfloat16),
            grad_mixed,
            preferred_element_type=jnp.float32,
        )
        return (grad_query, (grad_key, grad_value))

    start_query = jnp.zeros(query_seq.shape, jnp.float32)
    grad_query, (grad_key, grad_value) = lax.scan(
        grads_block, start_query, (key_blocks, value_blocks, pos_blocks)
    )
    return (grad_query, grad_key.reshape(key_seq.shape), grad_value.reshape(value_seq.shape))


MESH_IDS = pl.DeviceIdType.MESH
SIBLINGS = [(0, 1), (1, 0), (2, 3), (3, 2)]
OVER_X = [(0, 1), (1, 0)]
OVER_Y = [(0, 2), (2, 0), (1, 3), (3, 1)]
CROSSED = [((2 * y + c) * 2 + x, (2 * y + x) * 2 + c) for y in (0, 1) for c in (0, 1) for x in (0, 1)]


def pick_sequences(everyone, deal_order, first, count):
    slots = jnp.arange(deal_order.shape[0], dtype=jnp.int32)
    inverse = jnp.sum(jnp.where(deal_order[None, :] == slots[:, None], slots[None, :], 0), axis=1)
    return jnp.concatenate(
        [
            lax.dynamic_slice_in_dim(
                everyone, lax.dynamic_index_in_dim(inverse, first + at, keepdims=False), 1
            )
            for at in range(count)
        ]
    )


def bring_cotangent(cotangent, deal_order, first):
    everyone = lax.all_gather(cotangent, "dp", axis=0, tiled=True)
    return pick_sequences(everyone, deal_order, first, cotangent.shape[0])


def place():
    group = lax.axis_index("dp")
    core = lax.rem(group, 2)
    row = lax.axis_index("row")
    return group, core, group - core + row, row, lax.axis_index("col")


def lined(index, step, count):
    return lax.rem(index + step + count, count)


def aligned(block, size):
    return pl.ds(pl.multiple_of(block * size, size), size)


def greet(device):
    pl.semaphore_signal(
        pltpu.get_barrier_semaphore(), inc=1, device_id=device, device_id_type=MESH_IDS
    )


def remote(src, dst, sems, at, device):
    return pltpu.make_async_remote_copy(
        src_ref=src,
        dst_ref=dst,
        send_sem=sems.at[0, at],
        recv_sem=sems.at[1, at],
        device_id=device,
        device_id_type=MESH_IDS,
    )


def line_order(col, last, at):
    inner_low = jnp.where(at < 2, 1 - at, at)
    inner_high = jnp.where(at == 3, 0, jnp.where(at == 0, 2, jnp.where(at == 1, 1, 3)))
    return jnp.where(
        col == 0, at, jnp.where(col == last, last - at, jnp.where(col == 1, inner_low, inner_high))
    )


def start_kernel(
    cols, tok_ref, gain_ref, x_ref, a_ref, x_buf, a_buf, tok_sems, a_sems, local_sems
):
    group, core, mate, row, col = place()
    width = tok_ref.shape[2]
    length = x_buf.shape[0]
    sibling = (group + 1 - 2 * core, row, col)

    def line(step):
        return lined(col, step, cols)

    for step in range(1, cols):
        greet((mate, core, line(step)))
    greet(sibling)

    @pl.when(core != row)
    def _():
        greet((mate, core, col))

    pl.semaphore_wait(pltpu.get_barrier_semaphore(), cols + (core - row) * (core - row))

    def token_copy(step, into):
        return remote(
            tok_ref.at[line(step)],
            x_buf.at[:, aligned(into, width)],
            tok_sems,
            step,
            (mate, core, line(step)),
        )

    own_tokens = pltpu.make_async_copy(
        tok_ref.at[col], x_buf.at[:, aligned(col, width)], local_sems.at[0]
    )
    for step in range(1, cols):
        token_copy(step, col).start()

    @pl.when(core != row)
    def _():
        token_copy(0, col).start()

    @pl.when(core == row)
    def _():
        own_tokens.start()

    for step in range(1, cols):
        token_copy(step, line(-step)).wait_recv()

    @pl.when(core != row)
    def _():
        token_copy(0, col).wait_recv()

    @pl.when(core == row)
    def _():
        own_tokens.wait()

    keep_x = pltpu.make_async_copy(x_buf, x_ref, local_sems.at[1])
    keep_x.start()
    tall = min(64, length)

    @pl.loop(0, length // tall)
    def _(at):
        here = aligned(at, tall)
        now = x_buf[here, :].astype(jnp.float32)
        scale = lax.rsqrt(jnp.mean(now * now, axis=1, keepdims=True) + EPSILON)
        a_buf[here, :] = (now * scale * gain_ref[...]).astype(jnp.bfloat16)

    def a_copy(of_core):
        return remote(a_buf, a_ref.at[aligned(of_core, length)], a_sems, 0, sibling)

    own_a = pltpu.make_async_copy(a_buf, a_ref.at[aligned(core, length)], local_sems.at[2])
    a_copy(core).start()
    own_a.start()
    for step in range(1, cols):
        token_copy(step, col).wait_send()

    @pl.when(core != row)
    def _():
        token_copy(0, col).wait_send()

    keep_x.wait()
    own_a.wait()
    a_copy(core).wait_send()
    a_copy(1 - core).wait_recv()


def start_exchange(tokens, gain, cols):
    anywhere = pl.BlockSpec(memory_space=pl.ANY)
    seqs, length, width = tokens.shape
    full = width * cols
    return pl.pallas_call(
        functools.partial(start_kernel, cols),
        out_shape=(
            jax.ShapeDtypeStruct((length, full), tokens.dtype),
            jax.ShapeDtypeStruct((2 * length, full), tokens.dtype),
        ),
        in_specs=[anywhere, pl.BlockSpec(memory_space=pltpu.VMEM)],
        out_specs=(anywhere,) * 2,
        scratch_shapes=[
            pltpu.VMEM((length, full), tokens.dtype),
            pltpu.VMEM((length, full), tokens.dtype),
            pltpu.SemaphoreType.DMA((2, cols)),
            pltpu.SemaphoreType.DMA((2, 1)),
            pltpu.SemaphoreType.DMA((3,)),
        ],
        compiler_params=pltpu.CompilerParams(
            collective_id=1, has_side_effects=True, vmem_limit_bytes=16 << 20
        ),
        cost_estimate=pl.CostEstimate(flops=0, bytes_accessed=200 << 20, transcendentals=0),
        name="start_exchange",
    )(tokens, gain.reshape(1, full))


def gather_kernel(
    cols,
    q_ref,
    o_ref,
    rows_ref,
    wq_ref,
    wo_ref,
    crossed_ref,
    q_send,
    q_recv,
    q_over,
    q_shared,
    o_send,
    o_recv,
    o_over,
    o_shared,
    cross_sems,
    local_sems,
):
    group, core, mate, row, col = place()
    last = cols - 1
    over = (group, 1 - row, col)
    high = (group - core) // 2
    other_plane = (2 * (1 - high) + core, row, col)
    greet(over)
    greet(other_plane)

    @pl.when(core != row)
    def _():
        greet((mate, core, col))

    @pl.when(col < last)
    def _():
        greet((group, row, col + 1))

    @pl.when(col > 0)
    def _():
        greet((group, row, col - 1))

    pl.semaphore_wait(
        pltpu.get_barrier_semaphore(),
        2 + jnp.minimum(col, 1) + jnp.minimum(last - col, 1) + (core - row) * (core - row),
    )
    cross = remote(rows_ref, crossed_ref, cross_sems, 0, (mate, core, col))
    stay = pltpu.make_async_copy(rows_ref, crossed_ref, local_sems.at[2])

    def moves(own, full, send, recv, over_sems, shared_sems):
        tall, wide = own.shape

        def block(of_row, of_col):
            return full.at[aligned(of_row, tall), aligned(of_col, wide)]

        def along(src, chunk, to, way):
            return pltpu.make_async_remote_copy(
                src_ref=src,
                dst_ref=block(row, chunk),
                send_sem=send.at[way, chunk],
                recv_sem=recv.at[chunk],
                device_id=(group, row, to),
                device_id_type=MESH_IDS,
            )

        def across(src, of_row, chunk):
            return remote(src, block(of_row, chunk), over_sems, chunk, over)

        def share(chunk):
            place_there = block(1 - row, chunk)
            return remote(place_there, place_there, shared_sems, chunk, other_plane)

        return block, along, across, share

    both = (
        (q_ref, moves(q_ref, wq_ref, q_send, q_recv, q_over, q_shared)),
        (o_ref, moves(o_ref, wo_ref, o_send, o_recv, o_over, o_shared)),
    )
    own_copies = []
    for at, (own, (block, along, across, share)) in enumerate(both):

        @pl.when(col < last)
        def _():
            along(own, col, col + 1, 0).start()

        @pl.when(col > 0)
        def _():
            along(own, col, col - 1, 1).start()

        @pl.when(lax.rem(col, 2) == high)
        def _():
            across(own, row, col).start()

        own_copies.append(pltpu.make_async_copy(own, block(row, col), local_sems.at[at]))
        own_copies[-1].start()

    @pl.when(core != row)
    def _():
        cross.start()

    @pl.when(core == row)
    def _():
        stay.start()

    for at in range(1, cols):
        chunk = line_order(col, last, at)
        for own, (block, along, across, share) in both:
            along(own, chunk, col, 0).wait_recv()

            @pl.when((chunk < col) & (col < last))
            def _():
                along(block(row, chunk), chunk, col + 1, 0).start()

            @pl.when((chunk > col) & (col > 0))
            def _():
                along(block(row, chunk), chunk, col - 1, 1).start()

            @pl.when(lax.rem(chunk, 2) == high)
            def _():
                across(block(row, chunk), row, chunk).start()

    for at in range(cols // 2):
        for own, (block, along, across, share) in both:
            chunk = 2 * at + high
            across(own, 1 - row, chunk).wait_recv()
            share(chunk).start()
    for copy in own_copies:
        copy.wait()

    @pl.when(core != row)
    def _():
        cross.wait()

    @pl.when(core == row)
    def _():
        stay.wait()

    for own, (block, along, across, share) in both:
        for chunk in range(cols):

            @pl.when((col >= chunk) & (col < last))
            def _():
                along(own, chunk, col + 1, 0).wait_send()

            @pl.when((col <= chunk) & (col > 0))
            def _():
                along(own, chunk, col - 1, 1).wait_send()

        for at in range(cols // 2):
            across(own, row, 2 * at + high).wait_send()
            share(2 * at + high).wait_send()
            share(2 * at + 1 - high).wait_recv()


def gather_weights(own_q, own_o, token_rows, rows, cols):
    anywhere = pl.BlockSpec(memory_space=pl.ANY)

    def whole(own):
        return jax.ShapeDtypeStruct((own.shape[0] * rows, own.shape[1] * cols), own.dtype)

    return pl.pallas_call(
        functools.partial(gather_kernel, cols),
        out_shape=(
            whole(own_q),
            whole(own_o),
            jax.ShapeDtypeStruct(token_rows.shape, token_rows.dtype),
        ),
        in_specs=[anywhere] * 3,
        out_specs=(anywhere,) * 3,
        scratch_shapes=[
            pltpu.SemaphoreType.DMA((2, cols)),
            pltpu.SemaphoreType.DMA((cols,)),
            pltpu.SemaphoreType.DMA((2, cols)),
            pltpu.SemaphoreType.DMA((2, cols)),
        ]
        * 2
        + [pltpu.SemaphoreType.DMA((2, 1)), pltpu.SemaphoreType.DMA((3,))],
        compiler_params=pltpu.CompilerParams(collective_id=4, has_side_effects=True),
        cost_estimate=pl.CostEstimate(flops=0, bytes_accessed=300 << 20, transcendentals=0),
        name="gather_weights",
    )(own_q, own_o, token_rows)


def half_turn(wide):
    lanes = wide.shape[1]
    half = HEAD_SIZE // 2
    lane = lax.broadcasted_iota(jnp.int32, wide.shape, 1)
    return jnp.where(
        lax.rem(lane, HEAD_SIZE) < half,
        pltpu.roll(wide, lanes - half, 1),
        pltpu.roll(wide, half, 1),
    )


def both_heads(pair):
    lane = lax.broadcasted_iota(jnp.int32, pair.shape, 1)
    turned = pltpu.roll(pair, HEAD_SIZE, 1)
    low = lane < HEAD_SIZE
    return jnp.where(low, pair, turned), jnp.where(low, turned, pair)


def keep_head(pair, side):
    lane = lax.broadcasted_iota(jnp.int32, pair.shape, 1)
    mine = lane < HEAD_SIZE if side == 0 else lane >= HEAD_SIZE
    return jnp.where(mine, pair, jnp.zeros_like(pair))


def dot_nn(a, b):
    return lax.dot_general(a, b, (((1,), (0,)), ((), ())), preferred_element_type=jnp.float32)


def dot_nt(a, b):
    return lax.dot_general(a, b, (((1,), (1,)), ((), ())), preferred_element_type=jnp.float32)


def dot_tn(a, b):
    return lax.dot_general(a, b, (((0,), (0,)), ((), ())), preferred_element_type=jnp.float32)


PAIR = 2 * HEAD_SIZE


def attend_kernel(block, len_ref, a_ref, w_ref, cos_ref, sin_ref, qkv_ref, z_ref, q_all, k_two, v_two):
    rows = a_ref.shape[0]
    heads = q_all.shape[0]
    length = len_ref[0]

    @pl.loop(0, rows // block)
    def _(at):
        here = pl.ds(pl.multiple_of(at * block, block), block)
        lin = dot_nn(a_ref[here, :], w_ref[...])
        for part in range(heads // 2 + 1):
            lanes = slice(part * PAIR, (part + 1) * PAIR)
            now = lin[:, lanes]
            table = slice(0, PAIR) if part < heads // 2 else slice(PAIR, 2 * PAIR)
            now = now * cos_ref[here, table] + half_turn(now) * sin_ref[here, table]
            qkv_ref[here, lanes] = now.astype(jnp.bfloat16)
            if part < heads // 2:
                for side in range(2):
                    q_all[2 * part + side, here, :] = keep_head(now * ATTN_MULT, side).astype(
                        jnp.bfloat16
                    )
            else:
                keys, values = both_heads(now)
                k_two[here, :] = keys.astype(jnp.bfloat16)
                v_two[here, :] = values.astype(jnp.bfloat16)

    for at in range(rows // block):
        here = slice(at * block, (at + 1) * block)
        upto = (at + 1) * block
        row = lax.broadcasted_iota(jnp.int32, (block, upto), 0) + at * block
        key = lax.broadcasted_iota(jnp.int32, (block, upto), 1)
        allowed = key < jnp.minimum(row + 1, length)

        def one_head(head):
            scores = dot_nt(q_all[head, here, :], k_two[:upto, :])
            scores = jnp.where(allowed, scores, MASKED)
            top = jnp.max(scores, axis=1, keepdims=True)
            power = jnp.exp(scores - top)
            total = jnp.sum(power, axis=1, keepdims=True)
            return dot_nn(power.astype(jnp.bfloat16), v_two[:upto, :]) / total

        for pair in range(heads // 2):
            low = one_head(2 * pair)
            high = one_head(2 * pair + 1)
            lane = lax.broadcasted_iota(jnp.int32, low.shape, 1)
            z_ref[here, pair * PAIR : (pair + 1) * PAIR] = jnp.where(
                lane < HEAD_SIZE, low, high
            ).astype(jnp.bfloat16)


def attend_fast(length, inputs, weights, cosines, sines, groups):
    rows, depth = inputs.shape
    wide = weights.shape[1] // groups
    heads = (wide - PAIR) // HEAD_SIZE
    block = min(256, rows)
    return pl.pallas_call(
        functools.partial(attend_kernel, block),
        grid=(groups,),
        out_shape=(
            jax.ShapeDtypeStruct((rows, groups * wide), jnp.bfloat16),
            jax.ShapeDtypeStruct((rows, groups * heads * HEAD_SIZE), jnp.bfloat16),
        ),
        in_specs=[
            pl.BlockSpec(memory_space=pltpu.SMEM),
            pl.BlockSpec((rows, depth), lambda g: (0, 0)),
            pl.BlockSpec((depth, wide), lambda g: (0, g)),
            pl.BlockSpec((rows, 2 * PAIR), lambda g: (0, 0)),
            pl.BlockSpec((rows, 2 * PAIR), lambda g: (0, 0)),
        ],
        out_specs=(
            pl.BlockSpec((rows, wide), lambda g: (0, g)),
            pl.BlockSpec((rows, heads * HEAD_SIZE), lambda g: (0, g)),
        ),
        scratch_shapes=[
            pltpu.VMEM((heads, rows, PAIR), jnp.bfloat16),
            pltpu.VMEM((rows, PAIR), jnp.bfloat16),
            pltpu.VMEM((rows, PAIR), jnp.bfloat16),
        ],
        compiler_params=pltpu.CompilerParams(vmem_limit_bytes=48 << 20),
        cost_estimate=pl.CostEstimate(
            flops=2 * rows * depth * wide * groups + 2 * groups * heads * rows * rows * 128,
            bytes_accessed=2 * (rows * depth + depth * wide * groups + rows * wide * groups),
            transcendentals=groups * heads * rows * rows // 2,
        ),
        name="attend",
    )(length, inputs, weights, cosines, sines)


def attend_back_kernel(
    block, len_ref, qkv_ref, dz_ref, cos_ref, sin_ref, out_ref, q_all, z_all, k_two, v_two, k_acc, v_acc
):
    rows = qkv_ref.shape[0]
    heads = q_all.shape[0]
    length = len_ref[0]

    @pl.loop(0, rows // block)
    def _(at):
        here = pl.ds(pl.multiple_of(at * block, block), block)
        for part in range(heads // 2):
            lanes = slice(part * PAIR, (part + 1) * PAIR)
            queries = qkv_ref[here, lanes].astype(jnp.float32) * ATTN_MULT
            mixed = dz_ref[here, lanes].astype(jnp.float32)
            for side in range(2):
                q_all[2 * part + side, here, :] = keep_head(queries, side).astype(jnp.bfloat16)
                z_all[2 * part + side, here, :] = keep_head(mixed, side).astype(jnp.bfloat16)
        keys, values = both_heads(qkv_ref[here, heads * HEAD_SIZE :].astype(jnp.float32))
        k_two[here, :] = keys.astype(jnp.bfloat16)
        v_two[here, :] = values.astype(jnp.bfloat16)
        k_acc[here, :] = jnp.zeros((block, PAIR), jnp.float32)
        v_acc[here, :] = jnp.zeros((block, PAIR), jnp.float32)

    def turn_back(now, here, table):
        return (now * cos_ref[here, table] - half_turn(now) * sin_ref[here, table]).astype(
            jnp.bfloat16
        )

    for at in range(rows // block):
        here = slice(at * block, (at + 1) * block)
        upto = (at + 1) * block
        key = lax.broadcasted_iota(jnp.int32, (upto, block), 0)
        query = lax.broadcasted_iota(jnp.int32, (upto, block), 1) + at * block
        allowed = key < jnp.minimum(query + 1, length)

        def one_head(head):
            queries, mixed = q_all[head, here, :], z_all[head, here, :]
            scores = jnp.where(allowed, dot_nt(k_two[:upto, :], queries), MASKED)
            power = jnp.exp(scores - jnp.max(scores, axis=0, keepdims=True))
            weights = power * (1.0 / jnp.sum(power, axis=0, keepdims=True))
            back = dot_nt(v_two[:upto, :], mixed)
            centre = jnp.sum(weights * back, axis=0, keepdims=True)
            slope = (weights * (back - centre)).astype(jnp.bfloat16)
            k_acc[:upto, :] += dot_nn(slope, queries)
            v_acc[:upto, :] += dot_nn(weights.astype(jnp.bfloat16), mixed)
            return dot_tn(slope, k_two[:upto, :]) * ATTN_MULT

        for pair in range(heads // 2):
            low = one_head(2 * pair)
            high = one_head(2 * pair + 1)
            lane = lax.broadcasted_iota(jnp.int32, low.shape, 1)
            lanes = slice(pair * PAIR, (pair + 1) * PAIR)
            out_ref[here, lanes] = turn_back(
                jnp.where(lane < HEAD_SIZE, low, high), here, slice(0, PAIR)
            )

    @pl.loop(0, rows // block)
    def _(at):
        here = pl.ds(pl.multiple_of(at * block, block), block)
        keys, values = k_acc[here, :], v_acc[here, :]
        keys = keys + pltpu.roll(keys, HEAD_SIZE, 1)
        values = values + pltpu.roll(values, HEAD_SIZE, 1)
        lane = lax.broadcasted_iota(jnp.int32, keys.shape, 1)
        lanes = slice(heads * HEAD_SIZE, heads * HEAD_SIZE + PAIR)
        out_ref[here, lanes] = turn_back(
            jnp.where(lane < HEAD_SIZE, keys, values), here, slice(PAIR, 2 * PAIR)
        )


def attend_back_fast(length, projected, grad_mixed, cosines, sines, groups):
    rows = projected.shape[0]
    wide = projected.shape[1] // groups
    heads = (wide - PAIR) // HEAD_SIZE
    block = min(256, rows)
    return pl.pallas_call(
        functools.partial(attend_back_kernel, block),
        grid=(groups,),
        out_shape=jax.ShapeDtypeStruct((rows, groups * wide), jnp.bfloat16),
        in_specs=[
            pl.BlockSpec(memory_space=pltpu.SMEM),
            pl.BlockSpec((rows, wide), lambda g: (0, g)),
            pl.BlockSpec((rows, heads * HEAD_SIZE), lambda g: (0, g)),
            pl.BlockSpec((rows, 2 * PAIR), lambda g: (0, 0)),
            pl.BlockSpec((rows, 2 * PAIR), lambda g: (0, 0)),
        ],
        out_specs=pl.BlockSpec((rows, wide), lambda g: (0, g)),
        scratch_shapes=[
            pltpu.VMEM((heads, rows, PAIR), jnp.bfloat16),
            pltpu.VMEM((heads, rows, PAIR), jnp.bfloat16),
            pltpu.VMEM((rows, PAIR), jnp.bfloat16),
            pltpu.VMEM((rows, PAIR), jnp.bfloat16),
            pltpu.VMEM((rows, PAIR), jnp.float32),
            pltpu.VMEM((rows, PAIR), jnp.float32),
        ],
        compiler_params=pltpu.CompilerParams(vmem_limit_bytes=48 << 20),
        cost_estimate=pl.CostEstimate(
            flops=5 * groups * heads * rows * rows * 128,
            bytes_accessed=2 * (2 * rows * wide * groups + rows * heads * HEAD_SIZE * groups),
            transcendentals=groups * heads * rows * rows // 2,
        ),
        name="attend_back",
    )(length, projected, grad_mixed, cosines, sines)


def ffn_kernel(
    cols,
    own_ref,
    resid_ref,
    grad_ref,
    wg_own,
    wu_own,
    wd_own,
    wg_far,
    wu_far,
    wd_far,
    wg_far_y,
    wu_far_y,
    wd_far_y,
    wg_sib,
    wu_sib,
    wd_sib,
    wg_sib_y,
    wu_sib_y,
    wd_sib_y,
    u_all,
    dgu_all,
    mlp_all,
    back_all,
    relay_ref,
    land_ref,
    a_keep,
    a_send,
    b_keep,
    b_send,
    wg,
    wu,
    wd,
    b_all,
    b_turn,
    g_two,
    u_buf,
    dg_buf,
    du_buf,
    mlp_buf,
    back_buf,
    w_sems,
    ag_send,
    ag_recv,
    back_send,
    back_recv,
    relay_recv,
    pair_sems,
    lane_sems,
    tile_sems,
    io_sems,
):
    group, core, mate, row, col = place()
    sibling = (group + 1 - 2 * core, row, col)
    last = cols - 1
    depth = wg_own.shape[0]
    half = depth // 2
    units = wg_own.shape[1]
    rows = own_ref.shape[0]
    tile = units // cols
    beside = col + 1 - 2 * lax.rem(col, 2)
    facing = last - col
    inner = (col > 0) & (col < last)

    for step in range(1, cols):
        greet((group, row, lined(col, step, cols)))
    greet(sibling)
    pl.semaphore_wait(pltpu.get_barrier_semaphore(), cols)

    def pass_on(src, at, to, way):
        return pltpu.make_async_remote_copy(
            src_ref=src,
            dst_ref=b_all.at[at],
            send_sem=ag_send.at[way, at],
            recv_sem=ag_recv.at[at],
            device_id=(group, row, to),
            device_id_type=MESH_IDS,
        )

    @pl.when(col < last)
    def _():
        pass_on(own_ref, col, col + 1, 0).start()

    @pl.when(col > 0)
    def _():
        pass_on(own_ref, col, col - 1, 1).start()

    def order(at):
        return line_order(col, last, at)

    def load_g(at):
        side = lax.rem(at, 2)
        return pltpu.make_async_copy(grad_ref.at[order(at)], g_two.at[side], io_sems.at[6 + side])

    quarter = half // 2
    high = (group - core) // 2

    def rows_at(first, size):
        return pl.ds(pl.multiple_of(first, quarter), size)

    own_copy = pltpu.make_async_copy(own_ref, b_all.at[col], io_sems.at[0])
    own_copy.start()
    load_resid = pltpu.make_async_copy(resid_ref, mlp_buf, io_sems.at[8])
    far = (1 - row) * depth
    loads = []
    for full, mine, pieces in (
        (wg, wg_own, (wg_far, wg_far_y, wg_sib, wg_sib_y)),
        (wu, wu_own, (wu_far, wu_far_y, wu_sib, wu_sib_y)),
        (wd, wd_own, (wd_far, wd_far_y, wd_sib, wd_sib_y)),
    ):
        places = [
            far + of_core * half + of_plane * quarter
            for of_core in (core, 1 - core)
            for of_plane in (high, 1 - high)
        ]
        loads.append(
            pltpu.make_async_copy(
                mine, full.at[rows_at(row * depth, depth)], w_sems.at[len(loads)]
            )
        )
        for piece, first in zip(pieces, places):
            loads.append(
                pltpu.make_async_copy(
                    piece, full.at[rows_at(first, quarter)], w_sems.at[len(loads)]
                )
            )
    for load in loads:
        load.start()
    load_g(0).start()
    load_resid.start()
    own_copy.wait()
    for load in loads:
        load.wait()

    def arrive(chunk):
        pass_on(b_all.at[chunk], chunk, col, 0).wait_recv()

        @pl.when((chunk < col) & (col < last))
        def _():
            pass_on(b_all.at[chunk], chunk, col + 1, 0).start()

        @pl.when((chunk > col) & (col > 0))
        def _():
            pass_on(b_all.at[chunk], chunk, col - 1, 1).start()

    def outputs(chunk):
        return (
            pltpu.make_async_copy(u_buf, u_all.at[chunk], io_sems.at[1]),
            pltpu.make_async_copy(dg_buf, dgu_all.at[chunk, :, 0:units], io_sems.at[2]),
            pltpu.make_async_copy(du_buf, dgu_all.at[chunk, :, units : 2 * units], io_sems.at[3]),
        )

    def mlp_out(chunk):
        return pltpu.make_async_copy(mlp_buf, mlp_all.at[chunk], io_sems.at[4])

    def slot_of(at):
        return lax.rem(at, cols - 1)

    def deliver(slot, to, place_there, at):
        return pltpu.make_async_remote_copy(
            src_ref=back_buf.at[slot],
            dst_ref=back_all.at[place_there],
            send_sem=back_send.at[at],
            recv_sem=back_recv.at[place_there],
            device_id=(group, row, to),
            device_id_type=MESH_IDS,
        )

    def hand_over(slot, to, box, at):
        return pltpu.make_async_remote_copy(
            src_ref=back_buf.at[slot],
            dst_ref=relay_ref.at[box],
            send_sem=back_send.at[at],
            recv_sem=relay_recv.at[box],
            device_id=(group, row, to),
            device_id_type=MESH_IDS,
        )

    own_back = pltpu.make_async_copy(back_buf.at[0], back_all.at[0], io_sems.at[5])
    at_end = jnp.logical_not(inner)

    def one_chunk(at, unused):
        chunk = order(at)
        side = lax.rem(at, 2)

        @pl.when(at_end & (at > 0))
        def _():
            arrive(order(at))

        @pl.when(inner & (at == 1))
        def _():
            arrive(order(1))
            arrive(order(2))

        @pl.when(inner & (at == 3))
        def _():
            arrive(order(3))

        load_g(at).wait()

        @pl.when(at < last)
        def _():
            load_g(at + 1).start()

        @pl.when(at > 0)
        def _():
            for copy in outputs(order(at - 1)):
                copy.wait()

        @pl.loop(0, units // tile)
        def _(step):
            lanes = aligned(step, tile)
            gate = dot_nn(b_all[chunk], wg[:, lanes])
            upward = dot_nn(b_all[chunk], wu[:, lanes])
            back = RES_MULT * dot_nn(g_two[side], wd[:, lanes])
            opened = 1.0 / (1.0 + jnp.exp(-gate))
            silu = gate * opened
            u_buf[:, lanes] = (silu * upward).astype(jnp.bfloat16)
            slope = opened * (1.0 + gate * (1.0 - opened))
            dg_buf[:, lanes] = (back * upward * slope).astype(jnp.bfloat16)
            du_buf[:, lanes] = (back * silu).astype(jnp.bfloat16)

        for copy in outputs(chunk):
            copy.start()

        @pl.when(at > 0)
        def _():
            mlp_out(order(at - 1)).wait()

        @pl.when(at == 0)
        def _():
            load_resid.wait()

        @pl.when(at == last)
        def _():
            own_back.wait()

        @pl.loop(0, 2 * depth // tile)
        def _(step):
            here = aligned(step, tile)
            back = dot_nt(dg_buf[...], wg[here, :]) + dot_nt(du_buf[...], wu[here, :])
            back_buf[slot_of(at), :, here] = back.astype(jnp.bfloat16)
            added = jnp.where(at == 0, mlp_buf[:, here].astype(jnp.float32), 0.0)
            mlp_buf[:, here] = (added + RES_MULT * dot_nt(u_buf[...], wd[here, :])).astype(
                jnp.bfloat16
            )

        mlp_out(chunk).start()

        @pl.when(at == 0)
        def _():
            own_back.start()

        @pl.when(at_end & (at == 1))
        def _():
            deliver(1, beside, 1, 1).start()

        @pl.when(at_end & (at == 2))
        def _():
            hand_over(2, beside, 1, 2).start()

        @pl.when(at_end & (at == 3))
        def _():
            deliver(0, facing, 2, 3).start()

        @pl.when(inner & (at == 3))
        def _():
            hand_over(0, facing, 0, 3).start()

        return unused

    lax.fori_loop(0, cols, one_chunk, 0)
    for copy in outputs(order(last)):
        copy.wait()
    mlp_out(order(last)).wait()

    loads = []
    for chunk in range(cols):
        here = slice(chunk * rows, (chunk + 1) * rows)
        loads += [
            pltpu.make_async_copy(
                dgu_all.at[chunk, :, 0:units], wg.at[here], w_sems.at[chunk]
            ),
            pltpu.make_async_copy(
                dgu_all.at[chunk, :, units : 2 * units], wu.at[here], w_sems.at[cols + chunk]
            ),
            pltpu.make_async_copy(u_all.at[chunk], wd.at[here], w_sems.at[2 * cols + chunk]),
        ]
    for load in loads:
        load.start()

    def relay(box, slot):
        hand_over(slot, facing, box, 3).wait_recv()
        load = pltpu.make_async_copy(relay_ref.at[box], mlp_buf, io_sems.at[4])
        load.start()
        load.wait()
        tall = min(64, rows)

        @pl.loop(0, rows // tall)
        def _(at):
            here = aligned(at, tall)
            back_buf[slot, here, :] = (
                back_buf[slot, here, :].astype(jnp.float32)
                + mlp_buf[here, :].astype(jnp.float32)
            ).astype(jnp.bfloat16)

    buffers = (dg_buf, du_buf, u_buf)

    def to_sibling(at, part):
        return pltpu.make_async_remote_copy(
            src_ref=buffers[part],
            dst_ref=land_ref.at[at, part],
            send_sem=pair_sems.at[0, at, part],
            recv_sem=pair_sems.at[1, at, part],
            device_id=sibling,
            device_id_type=MESH_IDS,
        )

    def landed(at, part):
        return pltpu.make_async_copy(land_ref.at[at, part], buffers[part], io_sems.at[1 + part])

    halfway = units // 2
    small = rows // 2
    mine, others = aligned(row, small), aligned(1 - row, small)

    def x_lane(high):
        return (
            pltpu.make_async_copy(
                dg_buf.at[mine], a_keep.at[high, :, 0:units], lane_sems.at[0]
            ),
            pltpu.make_async_copy(
                dg_buf.at[others], a_send.at[high, :, 0:units], lane_sems.at[1]
            ),
            pltpu.make_async_copy(
                u_buf.at[mine, 0:halfway],
                a_keep.at[high, :, units : units + halfway],
                lane_sems.at[2],
            ),
            pltpu.make_async_copy(
                u_buf.at[others, 0:halfway],
                a_send.at[high, :, units : units + halfway],
                lane_sems.at[3],
            ),
        )

    def y_lane(target):
        copies = []
        for side in range(2):
            here = slice(side * small, (side + 1) * small)
            copies += [
                pltpu.make_async_copy(
                    du_buf.at[here], target.at[side, :, 0:units], lane_sems.at[4 + 2 * side]
                ),
                pltpu.make_async_copy(
                    u_buf.at[here, halfway:units],
                    target.at[side, :, units : units + halfway],
                    lane_sems.at[5 + 2 * side],
                ),
            ]
        return copies

    def put_results(high, act):
        for copy in x_lane(high):
            act(copy)

        @pl.when(high == (group - core) // 2)
        def _():
            for copy in y_lane(b_keep):
                act(copy)

        @pl.when(high != (group - core) // 2)
        def _():
            for copy in y_lane(b_send):
                act(copy)

    def start_it(copy):
        copy.start()

    def wait_for(copy):
        copy.wait()

    def part_of(chunk):
        return slice(chunk * rows, (chunk + 1) * rows)

    def grad_tile(block, chunk):
        return pltpu.make_async_copy(
            grad_ref.at[chunk, :, aligned(block, rows)],
            mlp_buf.at[:, part_of(chunk)],
            tile_sems.at[chunk],
        )

    parts = range(3)

    def block_of(at):
        return 2 * lax.rem(at, 2) + jnp.where(at >= 2, core, 1 - core)

    for chunk in range(cols):
        grad_tile(block_of(0), chunk).start()
    for chunk in range(cols):
        b_turn[0, :, part_of(chunk)] = b_all[chunk, :, aligned(block_of(0), rows)].T
    for chunk in range(cols):
        grad_tile(block_of(0), chunk).wait()
    for chunk in range(cols):
        g_two[0, :, part_of(chunk)] = mlp_buf[:, part_of(chunk)].T
    for load in loads:
        load.wait()

    def one_block(at, unused):
        high = lax.rem(at, 2)
        is_own = at >= 2
        side = lax.rem(at, 2)
        following = block_of(jnp.minimum(at + 1, 3))

        @pl.when(inner & (at == 1))
        def _():
            relay(0, col)
            deliver(col, beside, 1, 1).start()
            relay(1, last - col)
            deliver(last - col, facing, 2, 2).start()

        @pl.when(at < 3)
        def _():
            for chunk in range(cols):
                grad_tile(following, chunk).start()

        @pl.when((at == 1) | (at == 2))
        def _():
            for part in parts:
                to_sibling(at - 1, part).wait_send()

        @pl.when(at == 3)
        def _():
            put_results(0, wait_for)

        @pl.when(is_own)
        def _():
            for part in parts:
                to_sibling(high, part).wait_recv()
                landed(high, part).start()
            for part in parts:
                landed(high, part).wait()

        @pl.when(at < 3)
        def _():
            for chunk in range(cols):
                grad_tile(following, chunk).wait()

        @pl.loop(0, cols)
        def _(step):
            lanes = aligned(step, tile)
            tokens = aligned(step, rows)

            def put(buffer, value):
                other = jnp.where(is_own, buffer[:, lanes].astype(jnp.float32), 0.0)
                buffer[:, lanes] = (other + value).astype(jnp.bfloat16)

            put(dg_buf, dot_nn(b_turn[side], wg[:, lanes]))
            b_turn[1 - side, :, tokens] = b_all[step, :, aligned(following, rows)].T
            put(du_buf, dot_nn(b_turn[side], wu[:, lanes]))
            g_two[1 - side, :, tokens] = mlp_buf[:, tokens].T
            put(u_buf, RES_MULT * dot_nn(g_two[side], wd[:, lanes]))

        @pl.when(jnp.logical_not(is_own))
        def _():
            for part in parts:
                to_sibling(at, part).start()

        @pl.when(is_own)
        def _():
            put_results(high, start_it)

        return unused

    lax.fori_loop(0, 4, one_block, 0)
    put_results(1, wait_for)
    for at in range(1, cols):
        deliver(0, beside, 1, at).wait_send()
    for at in range(1, 3):
        deliver(0, beside, at, at).wait_recv()
    for chunk in range(cols):

        @pl.when((col >= chunk) & (col < last))
        def _():
            pass_on(own_ref, chunk, col + 1, 0).wait_send()

        @pl.when((col <= chunk) & (col > 0))
        def _():
            pass_on(own_ref, chunk, col - 1, 1).wait_send()


def feed_forward(own_input, resid, grad_rows, weights, cols):
    rows, width = own_input.shape
    units = weights[0].shape[1]
    anywhere = pl.BlockSpec(memory_space=pl.ANY)
    bf16 = jnp.bfloat16
    lane = jax.ShapeDtypeStruct((2, rows // 2, units + units // 2), bf16)
    return pl.pallas_call(
        functools.partial(ffn_kernel, cols),
        out_shape=(
            jax.ShapeDtypeStruct((cols, rows, units), bf16),
            jax.ShapeDtypeStruct((cols, rows, 2 * units), bf16),
            jax.ShapeDtypeStruct((cols, rows, width), bf16),
            jax.ShapeDtypeStruct((3, rows, width), bf16),
            jax.ShapeDtypeStruct((2, rows, width), bf16),
            jax.ShapeDtypeStruct((2, 3, rows, units), bf16),
        )
        + (lane,) * 4,
        in_specs=[anywhere] * 18,
        out_specs=(anywhere,) * 10,
        scratch_shapes=[
            pltpu.VMEM((width, units), bf16),
            pltpu.VMEM((width, units), bf16),
            pltpu.VMEM((width, units), bf16),
            pltpu.VMEM((cols, rows, width), bf16),
            pltpu.VMEM((2, rows, width), bf16),
            pltpu.VMEM((2, rows, width), bf16),
            pltpu.VMEM((rows, units), bf16),
            pltpu.VMEM((rows, units), bf16),
            pltpu.VMEM((rows, units), bf16),
            pltpu.VMEM((rows, width), bf16),
            pltpu.VMEM((cols - 1, rows, width), bf16),
            pltpu.SemaphoreType.DMA((15,)),
            pltpu.SemaphoreType.DMA((2, cols)),
            pltpu.SemaphoreType.DMA((cols,)),
            pltpu.SemaphoreType.DMA((cols,)),
            pltpu.SemaphoreType.DMA((cols,)),
            pltpu.SemaphoreType.DMA((2,)),
            pltpu.SemaphoreType.DMA((2, 2, 3)),
            pltpu.SemaphoreType.DMA((8,)),
            pltpu.SemaphoreType.DMA((cols,)),
            pltpu.SemaphoreType.DMA((9,)),
        ],
        compiler_params=pltpu.CompilerParams(
            collective_id=2, has_side_effects=True, vmem_limit_bytes=60 << 20
        ),
        cost_estimate=pl.CostEstimate(
            flops=18 * cols * rows * width * units,
            bytes_accessed=800 << 20,
            transcendentals=cols * rows * units,
        ),
        name="feed_forward",
    )(own_input, resid, grad_rows, *weights)


def finish_kernel(
    cols,
    ig_ref,
    gq_ref,
    go_ref,
    gain_ref,
    out_ref,
    gin_ref,
    crossed_ref,
    sq_ref,
    so_ref,
    gsum_ref,
    q_keep,
    q_sib,
    q_a1,
    q_a2,
    q_b1,
    q_b2,
    q_z,
    o_keep,
    o_sib,
    o_a1,
    o_a2,
    o_b1,
    o_b2,
    o_z,
    gain_now,
    gain_in,
    ig_sems,
    gain_sems,
    q_sems,
    o_sems,
    qz_sems,
    oz_sems,
    cross_sems,
    local_sems,
):
    group, core, mate, row, col = place()
    pair = group - core
    high = pair // 2
    sibling = (pair + 1 - core, row, col)
    over_x = (group, 1 - row, col)
    over_y = (2 * (1 - high) + core, row, col)
    width = gin_ref.shape[2]

    def line(step):
        return lax.rem(col + step + cols, cols)

    barrier = pltpu.get_barrier_semaphore()

    def greet(device):
        pl.semaphore_signal(barrier, inc=1, device_id=device, device_id_type=MESH_IDS)

    greet(sibling)
    greet(over_x)
    greet(over_y)
    for step in range(1, cols):
        greet((mate, core, line(step)))
        greet((group, row, line(step)))

    @pl.when(core != row)
    def _():
        greet((mate, core, col))

    pl.semaphore_wait(barrier, 2 * cols + 1 + (core - row) * (core - row))

    def remote(src, dst, sems, at, device):
        return pltpu.make_async_remote_copy(
            src_ref=src,
            dst_ref=dst,
            send_sem=sems.at[0, at],
            recv_sem=sems.at[1, at],
            device_id=device,
            device_id_type=MESH_IDS,
        )

    def lanes(block, size):
        return pl.ds(pl.multiple_of(block * size, size), size)

    matrices = (
        (gq_ref, sq_ref, q_keep, q_sib, q_a1, q_a2, q_b1, q_b2, q_z, q_sems, qz_sems),
        (go_ref, so_ref, o_keep, o_sib, o_a1, o_a2, o_b1, o_b2, o_z, o_sems, oz_sems),
    )

    def moves(m):
        grads, out, keep, sib, a1, a2, b1, b2, zb, sems, z_sems = matrices[m]
        return dict(
            s0=remote(grads.at[:, 1 - core], sib, sems, 0, sibling),
            a1=remote(grads.at[:, core, 1 - row], a1, sems, 1, over_x),
            a2=remote(keep.at[1 - high, row], a2, sems, 2, over_y),
            b1=remote(sib.at[1 - high], b1, sems, 3, over_y),
            b2=remote(sib.at[high, 1 - row], b2, sems, 4, over_x),
            own=pltpu.make_async_copy(grads.at[:, core], keep, local_sems.at[m]),
        )

    copies = (moves(0), moves(1))

    def rows_plus(into, more):
        rows = into.shape[0]
        step = min(32, rows)

        @pl.loop(0, rows // step)
        def _(at):
            here = pl.ds(pl.multiple_of(at * step, step), step)
            into[here, :] = (
                into[here, :].astype(jnp.float32) + more[here, :].astype(jnp.float32)
            ).astype(into.dtype)

    def token_copy(step, at):
        return remote(
            ig_ref.at[:, lanes(line(step), width)],
            gin_ref.at[at],
            ig_sems,
            step,
            (mate, core, line(step)),
        )

    own_tokens = pltpu.make_async_copy(
        ig_ref.at[:, lanes(col, width)], gin_ref.at[col], local_sems.at[2]
    )

    cross = remote(out_ref, crossed_ref, cross_sems, 0, (mate, core, col))
    stay = pltpu.make_async_copy(out_ref, crossed_ref, local_sems.at[4])
    for m in range(2):
        copies[m]["s0"].start()
        copies[m]["a1"].start()
        copies[m]["own"].start()
    @pl.when(core == row)
    def _():
        own_tokens.start()
        stay.start()
        for step in range(1, cols):
            token_copy(step, col).start()

    gain_load = pltpu.make_async_copy(gain_ref, gain_now.at[0], local_sems.at[3])
    gain_load.start()
    gain_load.wait()
    near = (
        sibling,
        over_x,
        over_y,
        (group, row, col + 1 - 2 * lax.rem(col, 2)),
        (group, row, lax.rem(col + cols // 2, cols)),
    )

    def gain_round(at):
        exchange = remote(gain_now.at[at], gain_in.at[at], gain_sems, at, near[at])
        exchange.start()
        exchange.wait()
        gain_now[at + 1] = gain_now[at] + gain_in[at]

    gain_round(0)
    for m in range(2):
        copies[m]["s0"].wait()
        copies[m]["b1"].start()
    gain_round(1)
    for m in range(2):
        grads, out, keep, sib, a1, a2, b1, b2, zb, sems, z_sems = matrices[m]
        copies[m]["own"].wait()
        copies[m]["a1"].wait()
        rows_plus(keep.at[1 - high, row], a1.at[1 - high])
        copies[m]["a2"].start()
    for m in range(2):
        grads, out, keep, sib, a1, a2, b1, b2, zb, sems, z_sems = matrices[m]
        copies[m]["b1"].wait()
        rows_plus(sib.at[high, 1 - row], b1.at[1 - row])
        copies[m]["b2"].start()

    @pl.when(core != row)
    def _():
        for step in range(cols):
            token_copy(step, col).start()
        cross.start()

    gain_round(2)
    for m in range(2):
        grads, out, keep, sib, a1, a2, b1, b2, zb, sems, z_sems = matrices[m]
        rows_plus(keep.at[high, row], a1.at[high])
        rows_plus(sib.at[high, row], b1.at[row])

    def z_moves(m, side, source):
        grads, out, keep, sib, a1, a2, b1, b2, zb, sems, z_sems = matrices[m]
        held = (keep, sib)[side]
        wide = zb.shape[3]
        return [
            pltpu.make_async_remote_copy(
                src_ref=held.at[high, row, :, lanes(line(step), wide)],
                dst_ref=zb.at[side, line(source(step))],
                send_sem=z_sems.at[0, side, step],
                recv_sem=z_sems.at[1, side, step],
                device_id=(group, row, line(step)),
                device_id_type=MESH_IDS,
            )
            for step in range(1, cols)
        ]

    for side, last_copy in ((0, "a2"), (1, "b2")):
        for m in range(2):
            grads, out, keep, sib, a1, a2, b1, b2, zb, sems, z_sems = matrices[m]
            copies[m][last_copy].wait()
            rows_plus((keep, sib)[side].at[high, row], (a2, b2)[side])
            for copy in z_moves(m, side, lambda step: 0):
                copy.start()
    gain_round(3)
    gain_round(4)
    gsum_ref[...] = gain_now[5]
    for side in range(2):
        for m in range(2):
            grads, out, keep, sib, a1, a2, b1, b2, zb, sems, z_sems = matrices[m]
            for copy in z_moves(m, side, lambda step: 0):
                copy.wait_send()
            for copy in z_moves(m, side, lambda step: -step):
                copy.wait_recv()
            held = (keep, sib)[side]
            wide = zb.shape[3]
            at_core = core if side == 0 else 1 - core
            rows = zb.shape[2]
            tall = min(32, rows)

            @pl.loop(0, rows // tall)
            def _(at):
                here = pl.ds(pl.multiple_of(at * tall, tall), tall)
                total = held[high, row, here, lanes(col, wide)].astype(jnp.float32)
                for step in range(1, cols):
                    total = total + zb[side, line(-step), here, :].astype(jnp.float32)
                out[at_core, here, :] = total

    for step in range(1, cols):
        token_copy(step, line(-step)).wait_recv()
        token_copy(step, col).wait_send()

    @pl.when(core != row)
    def _():
        token_copy(0, col).wait_recv()
        token_copy(0, col).wait_send()
        cross.wait()

    @pl.when(core == row)
    def _():
        own_tokens.wait()
        stay.wait()


def finish(input_grad, grad_q, grad_o, gains, output, cols):
    anywhere = pl.BlockSpec(memory_space=pl.ANY)
    in_vmem = pl.BlockSpec(memory_space=pltpu.VMEM)
    bf16, f32 = jnp.bfloat16, jnp.float32
    length, full = input_grad.shape
    rows = grad_q.shape[0] // 8

    def buffers(wide):
        return [
            pltpu.VMEM((2, 2, rows, wide), bf16),
            pltpu.VMEM((2, 2, rows, wide), bf16),
            pltpu.VMEM((2, rows, wide), bf16),
            pltpu.VMEM((rows, wide), bf16),
            pltpu.VMEM((2, rows, wide), bf16),
            pltpu.VMEM((rows, wide), bf16),
            pltpu.VMEM((2, cols, rows, wide // cols), bf16),
        ]

    wide_q, wide_o = grad_q.shape[1], grad_o.shape[1]
    return pl.pallas_call(
        functools.partial(finish_kernel, cols),
        out_shape=(
            jax.ShapeDtypeStruct((cols, length, full // cols), bf16),
            jax.ShapeDtypeStruct(output.shape, bf16),
            jax.ShapeDtypeStruct((2, rows, wide_q // cols), f32),
            jax.ShapeDtypeStruct((2, rows, wide_o // cols), f32),
            jax.ShapeDtypeStruct(gains.shape, f32),
        ),
        in_specs=[anywhere] * 5,
        out_specs=(anywhere, anywhere, in_vmem, in_vmem, in_vmem),
        scratch_shapes=buffers(wide_q)
        + buffers(wide_o)
        + [
            pltpu.VMEM((6,) + gains.shape, f32),
            pltpu.VMEM((5,) + gains.shape, f32),
            pltpu.SemaphoreType.DMA((2, cols)),
            pltpu.SemaphoreType.DMA((2, 5)),
            pltpu.SemaphoreType.DMA((2, 5)),
            pltpu.SemaphoreType.DMA((2, 5)),
            pltpu.SemaphoreType.DMA((2, 2, cols)),
            pltpu.SemaphoreType.DMA((2, 2, cols)),
            pltpu.SemaphoreType.DMA((2, 1)),
            pltpu.SemaphoreType.DMA((5,)),
        ],
        compiler_params=pltpu.CompilerParams(
            collective_id=3, has_side_effects=True, vmem_limit_bytes=40 << 20
        ),
        cost_estimate=pl.CostEstimate(flops=0, bytes_accessed=300 << 20, transcendentals=0),
        name="finish",
    )(
        input_grad,
        grad_q.reshape(2, 2, 2, rows, wide_q),
        grad_o.reshape(2, 2, 2, rows, wide_o),
        gains,
        output,
    )


def one_sequence_body(
    tokens,
    cotangent,
    lengths,
    deal_order,
    gain_attn,
    gain_ffn,
    w_query,
    key_value_weight,
    w_out,
    w_gate_up,
    w_down,
):
    seq_group, rows_local, width_local = tokens.shape
    row_count = lax.axis_size("row")
    col_count = lax.axis_size("col")
    full_width = width_local * col_count
    slot_len = rows_local * row_count
    group, core, mate, row, col = place()
    query_half = w_query.shape[1] // 2
    kv_half = key_value_weight.shape[2] // 2
    hidden = w_down.shape[1]

    def core_half(matrix, axis):
        width = matrix.shape[axis] // 2
        return lax.dynamic_slice_in_dim(matrix, core * width, width, axis)

    def joined(mine, other, at):
        return jnp.where(
            at == 0, jnp.concatenate([mine, other]), jnp.concatenate([other, mine])
        )

    def from_sibling(value):
        return lax.ppermute(value, "dp", SIBLINGS)

    def half_rows(matrix):
        return core_half(matrix, 0)

    pack_q = jnp.concatenate(
        [
            core_half(w_query, 1),
            core_half(key_value_weight[:, 0], 1),
            core_half(key_value_weight[:, 1], 1),
        ],
        axis=1,
    )
    pack_o = core_half(w_out, 1)
    gain_one = gain_attn.astype(jnp.float32)
    gain_two = gain_ffn.astype(jnp.float32)
    own_tokens, attn_input = start_exchange(tokens, gain_one, col_count)

    length = lax.dynamic_slice_in_dim(lengths, mate * seq_group + col, 1)
    given_pos = row * rows_local + jnp.arange(rows_local, dtype=jnp.int32)
    given_lengths = lax.dynamic_slice_in_dim(lengths, group * seq_group, seq_group)
    given_live = given_pos[None, :, None] < given_lengths[:, None, None]
    everyone = lax.all_gather(cotangent, "dp", axis=0, tiled=True)
    everyone, attn_input = lax.optimization_barrier((everyone, attn_input))
    picked = pick_sequences(everyone, deal_order, group * seq_group, seq_group)
    picked = jnp.where(given_live, picked, jnp.zeros_like(picked))
    weights_qkv, weights_out, given = gather_weights(
        pack_q, pack_o, picked, row_count, col_count
    )
    line_cot = lax.all_gather(given, "col", axis=2, tiled=True)
    own_grad = lax.dynamic_index_in_dim(line_cot, col, keepdims=False).astype(jnp.float32)

    w_gate_up, w_down, weights_qkv = lax.optimization_barrier((w_gate_up, w_down, weights_qkv))
    def quarter_rows(matrix):
        count = matrix.shape[0] // 4
        return lax.dynamic_slice_in_dim(matrix, (2 * core + group // 2) * count, count)

    far_gate_up = lax.ppermute(quarter_rows(w_gate_up), "row", OVER_X)
    far_down = lax.ppermute(quarter_rows(w_down), "row", OVER_X)
    own_mats = (w_gate_up[:, 0], w_gate_up[:, 1], w_down)

    cosine_table, sine_table = rope_tables(jnp.arange(slot_len, dtype=jnp.int32), HEAD_SIZE)
    cosine_table, sine_table = lax.optimization_barrier((cosine_table, sine_table))
    cosines = jnp.concatenate(
        [jnp.tile(cosine_table, (1, 6)), jnp.ones((slot_len, HEAD_SIZE), jnp.float32)], axis=1
    )
    turning = jnp.concatenate([-sine_table, sine_table], axis=1)
    sines = jnp.concatenate(
        [jnp.tile(turning, (1, 3)), jnp.zeros((slot_len, HEAD_SIZE), jnp.float32)], axis=1
    )
    own_float = own_tokens.astype(jnp.float32)
    scale_one = lax.rsqrt(jnp.mean(own_float * own_float, axis=1, keepdims=True) + EPSILON)
    projected, heads_out = attend_fast(
        length, attn_input, weights_qkv, cosines, sines, col_count
    )

    def summed_rows(partial):
        count = partial.shape[0] // 2
        mine = lax.dynamic_slice_in_dim(partial, core * count, count)
        other = lax.dynamic_slice_in_dim(partial, (1 - core) * count, count)
        return mine.astype(jnp.float32) + from_sibling(other).astype(jnp.float32)

    attn_rows = summed_rows(expand_local(heads_out, weights_out).astype(jnp.bfloat16))
    resid = own_float + RES_MULT * attn_rows
    scale_two = lax.rsqrt(jnp.mean(resid * resid, axis=1, keepdims=True) + EPSILON)
    own_ffn = (resid * scale_two * gain_two).astype(jnp.bfloat16)

    shared_gate_up = lax.ppermute(far_gate_up, "dp", OVER_Y)
    shared_down = lax.ppermute(far_down, "dp", OVER_Y)
    own_ffn, own_mats, far_gate_up, far_down, shared_gate_up, shared_down = (
        lax.optimization_barrier(
            (own_ffn, own_mats, far_gate_up, far_down, shared_gate_up, shared_down)
        )
    )
    far_mats = (far_gate_up[:, 0], far_gate_up[:, 1], far_down)
    far_mats += (shared_gate_up[:, 0], shared_gate_up[:, 1], shared_down)
    sibling_mats = tuple(from_sibling(matrix) for matrix in far_mats)
    *unused, a_keep, a_send, b_keep, b_send = feed_forward(
        own_ffn,
        resid.astype(jnp.bfloat16),
        line_cot,
        own_mats + far_mats + sibling_mats,
        col_count,
    )
    mlp_part, back_part = unused[2:4]
    grad_normed_two = jnp.sum(back_part.astype(jnp.float32), axis=0)
    out_cols = lax.psum_scatter(mlp_part, "col", scatter_dimension=2, tiled=True)

    def plus(kept, came):
        return (kept.astype(jnp.float32) + came.astype(jnp.float32)).astype(jnp.bfloat16)

    a_came = lax.ppermute(a_send, "row", OVER_X)
    b_came = lax.ppermute(b_send, "dp", OVER_Y)

    weighted_two = grad_normed_two * gain_two
    inner_two = jnp.sum(weighted_two * resid, axis=1, keepdims=True)
    grad_resid = (
        own_grad + scale_two * weighted_two - resid * scale_two**3 * inner_two / full_width
    )
    gain_two_part = jnp.sum(grad_normed_two * resid * scale_two, axis=0)
    own_attn_grad = (RES_MULT * grad_resid).astype(jnp.bfloat16)
    grad_attn = joined(own_attn_grad, from_sibling(own_attn_grad), core)
    grad_heads = contract_local(grad_attn, weights_out).astype(jnp.bfloat16)
    grad_out = token_outer(grad_attn, heads_out).astype(jnp.bfloat16)
    grad_projected = attend_back_fast(
        length, projected, grad_heads, cosines, sines, col_count
    )
    a_sum, b_sum, grad_projected = lax.optimization_barrier(
        (plus(a_keep, a_came), plus(b_keep, b_came), grad_projected)
    )
    high = group // 2

    def one_of(pair, at):
        return lax.dynamic_index_in_dim(pair, at, keepdims=False)

    a_last = lax.ppermute(one_of(a_sum, 1 - high), "dp", OVER_Y)
    b_last = lax.ppermute(one_of(b_sum, 1 - row), "row", OVER_X)
    grad_normed_one = summed_rows(expand_local(grad_projected, weights_qkv).astype(jnp.bfloat16))
    grad_qkv = token_outer(attn_input, grad_projected).astype(jnp.bfloat16)
    weighted_one = grad_normed_one * gain_one
    inner_one = jnp.sum(weighted_one * own_float, axis=1, keepdims=True)
    own_input_grad = (
        grad_resid
        + scale_one * weighted_one
        - own_float * scale_one**3 * inner_one / full_width
    ).astype(jnp.bfloat16)
    gain_one_part = jnp.sum(grad_normed_one * own_float * scale_one, axis=0)
    a_last, b_last, own_input_grad = lax.optimization_barrier((a_last, b_last, own_input_grad))
    gains = jnp.stack([gain_one_part, gain_two_part]).reshape(8, -1)
    given_grad, given_out, sums_q, sums_o, gain_sums = finish(
        own_input_grad, grad_qkv, grad_out, gains, out_cols, col_count
    )
    a_last, b_last, a_sum, b_sum, given_grad = lax.optimization_barrier(
        (a_last, b_last, a_sum, b_sum, given_grad)
    )
    layer_out = jnp.where(given_live, given_out.astype(jnp.float32), 0.0)
    input_grad = given_grad.astype(jnp.float32)
    a_total = one_of(a_sum, high).astype(jnp.float32) + a_last.astype(jnp.float32)
    b_total = one_of(b_sum, row).astype(jnp.float32) + b_last.astype(jnp.float32)
    sums_gate_up = jnp.stack([a_total[:, :hidden], b_total[:, :hidden]], axis=1)
    sums_down = jnp.concatenate([a_total[:, hidden:], b_total[:, hidden:]], axis=1)
    grad_gain_attn, grad_gain_ffn = gain_sums.reshape(2, full_width)

    def both_cores(sums):
        return jnp.concatenate([sums[0], sums[1]], axis=1)

    qk = query_half + kv_half
    out_query = both_cores(sums_q[:, :, :query_half])
    out_kv = jnp.stack(
        [
            both_cores(sums_q[:, :, query_half:qk]),
            both_cores(sums_q[:, :, qk:]),
        ],
        axis=1,
    )
    out_out = both_cores(sums_o)
    return (
        layer_out,
        input_grad,
        out_query,
        out_kv,
        out_out,
        sums_gate_up,
        sums_down,
        grad_gain_attn,
        grad_gain_ffn,
    )


def general_body(
    tokens,
    cotangent,
    lengths,
    deal_order,
    gain_attn,
    gain_ffn,
    w_query,
    key_value_weight,
    w_out,
    w_gate_up,
    w_down,
):
    seq_group, rows_local, width_local = tokens.shape
    row_count = lax.axis_size("row")
    col_count = lax.axis_size("col")
    full_width = width_local * col_count
    slot_len = rows_local * row_count
    total_rows = seq_group * rows_local
    head_size = HEAD_SIZE
    query_width = w_query.shape[1]
    kv_width = key_value_weight.shape[2]
    kv_heads = kv_width // head_size
    group_size = query_width // kv_width
    group_index = lax.axis_index("dp")
    row_index = lax.axis_index("row")
    col_index = lax.axis_index("col")
    matrices = {
        "qkv": jnp.concatenate(
            [w_query, key_value_weight.reshape(key_value_weight.shape[0], 2 * kv_width)], axis=1
        ),
        "out": w_out,
        "gate_up": w_gate_up,
        "down": w_down,
    }

    def contract_with(operand, which_one):
        return contract_rows(operand, matrices[which_one])

    def expand_with(operand, which_one):
        return expand_rows(operand, matrices[which_one])

    own_cotangent = bring_cotangent(cotangent, deal_order, group_index * seq_group)
    own_rows = tokens
    seq_lens = lax.dynamic_slice_in_dim(lengths, group_index * seq_group, seq_group)
    local_pos = row_index * rows_local + jnp.arange(rows_local, dtype=jnp.int32)
    key_pos = jnp.arange(slot_len, dtype=jnp.int32)
    live_rows = (local_pos[None, :] < seq_lens[:, None]).astype(jnp.float32).reshape(total_rows, 1)
    cosine_table, sine_table = rope_tables(jnp.tile(local_pos, seq_group), head_size)
    own_tokens = own_rows.reshape(total_rows, width_local)
    wide_float = widen_cols(own_tokens).astype(jnp.float32)
    scale_one = lax.rsqrt(jnp.mean(wide_float * wide_float, axis=1, keepdims=True) + EPSILON)
    gain_one = gain_attn.astype(jnp.float32)
    first_normed = wide_float * scale_one
    attn_input = (first_normed * gain_one).astype(jnp.bfloat16)
    projected = contract_with(attn_input, "qkv")
    query_lin = projected[:, :query_width].reshape(total_rows, query_width // head_size, head_size)
    key_lin = projected[:, query_width : query_width + kv_width].reshape(
        total_rows, kv_heads, head_size
    )
    value_lin = projected[:, query_width + kv_width :]
    query_rows = rotary_embed(query_lin, cosine_table, sine_table).astype(jnp.bfloat16)
    keys_own = (
        rotary_embed(key_lin, cosine_table, sine_table)
        .astype(jnp.bfloat16)
        .reshape(seq_group, rows_local, kv_width)
    )
    values_own = value_lin.astype(jnp.bfloat16).reshape(seq_group, rows_local, kv_width)
    all_keys, all_values = (
        lax.all_gather(keys_own, "row", axis=1, tiled=True),
        lax.all_gather(values_own, "row", axis=1, tiled=True),
    )
    query_split = query_rows.reshape(seq_group, rows_local, kv_heads, group_size, head_size)
    key_split = all_keys.reshape(seq_group, slot_len, kv_heads, head_size)
    value_split = all_values.reshape(seq_group, slot_len, kv_heads, head_size)

    def forward_seq(inputs):
        return attend(inputs, key_pos, local_pos)

    mixed_heads, row_max, row_sums = lax.map(
        forward_seq, (query_split, key_split, value_split, seq_lens)
    )
    heads_out = mixed_heads.reshape(total_rows, query_width).astype(jnp.bfloat16)
    attn_local = narrow_cols(expand_with(heads_out, "out"))
    resid = own_tokens.astype(jnp.float32) + RES_MULT * attn_local
    gain_two = lax.dynamic_slice_in_dim(
        gain_ffn.astype(jnp.float32), col_index * width_local, width_local
    )
    scale_two = lax.rsqrt(sum_over_cols(jnp.sum(resid * resid, axis=1)) / full_width + EPSILON)[
        :, None
    ]
    normed_two = resid * scale_two
    ffn_input = widen_cols((normed_two * gain_two).astype(jnp.bfloat16))
    gate_up = contract_with(ffn_input, "gate_up")
    gate = gate_up[:, 0]
    upward = gate_up[:, 1]
    sigmoid_gate = jax.nn.sigmoid(gate)
    silu_gate = gate * sigmoid_gate
    hidden = (silu_gate * upward).astype(jnp.bfloat16)
    ffn_local = narrow_cols(expand_with(hidden, "down"))
    layer_out = live_rows * (resid + RES_MULT * ffn_local)
    grad_rows = live_rows * own_cotangent.reshape(total_rows, width_local).astype(jnp.float32)
    grad_ffn = widen_cols((RES_MULT * grad_rows).astype(jnp.bfloat16))
    grad_hidden = contract_with(grad_ffn, "down")
    grad_down = token_outer(grad_ffn, hidden)
    slope = sigmoid_gate * (1.0 + gate * (1.0 - sigmoid_gate))
    grad_gate_rows = jnp.stack(
        [grad_hidden * upward * slope, grad_hidden * silu_gate], axis=1
    ).astype(jnp.bfloat16)
    grad_gate_up = token_outer(ffn_input, grad_gate_rows)
    grad_normed_two = narrow_cols(expand_with(grad_gate_rows, "gate_up"))
    weighted_two = grad_normed_two * gain_two
    inner_two = sum_over_cols(jnp.sum(weighted_two * resid, axis=1))[:, None]
    grad_resid = (
        grad_rows + scale_two * weighted_two - resid * scale_two**3 * inner_two / full_width
    )
    gain_two_part = jnp.sum(grad_normed_two * normed_two, axis=0)
    grad_attn = widen_cols((RES_MULT * grad_resid).astype(jnp.bfloat16))
    grad_heads = contract_with(grad_attn, "out").astype(jnp.bfloat16)
    grad_out = token_outer(grad_attn, heads_out)
    grad_split = grad_heads.reshape(seq_group, rows_local, kv_heads, group_size, head_size)

    def backward_seq(inputs):
        return attend_back(inputs, key_pos, local_pos)

    grad_query, grad_key, grad_value = lax.map(
        backward_seq, (query_split, key_split, value_split, grad_split, row_max, row_sums, seq_lens)
    )
    key_part, value_part = (
        lax.psum_scatter(
            grad_key.reshape(seq_group, slot_len, kv_width).astype(jnp.bfloat16),
            "row",
            scatter_dimension=1,
            tiled=True,
        ).astype(jnp.float32),
        lax.psum_scatter(
            grad_value.reshape(seq_group, slot_len, kv_width).astype(jnp.bfloat16),
            "row",
            scatter_dimension=1,
            tiled=True,
        ).astype(jnp.float32),
    )
    query_back = rotary_embed(
        grad_query.reshape(total_rows, query_width // head_size, head_size),
        cosine_table,
        -sine_table,
    ).reshape(total_rows, query_width)
    key_back = rotary_embed(
        key_part.reshape(total_rows, kv_heads, head_size), cosine_table, -sine_table
    ).reshape(total_rows, kv_width)
    grad_projected = jnp.concatenate(
        [query_back, key_back, value_part.reshape(total_rows, kv_width)], axis=1
    ).astype(jnp.bfloat16)
    grad_qkv = token_outer(attn_input, grad_projected)
    grad_normed_one = expand_with(grad_projected, "qkv")
    weighted_one = grad_normed_one * gain_one
    inner_one = jnp.sum(weighted_one * wide_float, axis=1, keepdims=True)
    input_part = scale_one * weighted_one - wide_float * scale_one**3 * inner_one / full_width
    input_grad = grad_resid + narrow_cols(input_part)
    gain_one_part = jnp.sum(grad_normed_one * first_normed, axis=0)
    gain_two_full = lax.dynamic_update_slice_in_dim(
        jnp.zeros((full_width,), jnp.float32), gain_two_part, col_index * width_local, 0
    )
    grad_gain_attn, grad_gain_ffn = lax.psum((gain_one_part, gain_two_full), ("dp", "row", "col"))
    sums_qkv, sums_out, sums_gate_up, sums_down = (
        lax.psum_scatter(
            grad_qkv.astype(jnp.bfloat16), ("dp", "row"), scatter_dimension=0, tiled=True
        ).astype(jnp.float32),
        lax.psum_scatter(
            grad_out.astype(jnp.bfloat16), ("dp", "row"), scatter_dimension=0, tiled=True
        ).astype(jnp.float32),
        lax.psum_scatter(
            grad_gate_up.astype(jnp.bfloat16), ("dp", "row"), scatter_dimension=0, tiled=True
        ).astype(jnp.float32),
        lax.psum_scatter(
            grad_down.astype(jnp.bfloat16), ("dp", "row"), scatter_dimension=0, tiled=True
        ).astype(jnp.float32),
    )
    out_query = sums_qkv[:, :query_width]
    out_kv = sums_qkv[:, query_width:].reshape(sums_qkv.shape[0], 2, kv_width)
    return (
        layer_out.reshape(seq_group, rows_local, width_local),
        input_grad.reshape(seq_group, rows_local, width_local),
        out_query,
        out_kv,
        sums_out,
        sums_gate_up,
        sums_down,
        grad_gain_attn,
        grad_gain_ffn,
    )


def body(tokens, cotangent, lengths, deal_order, gain_attn, gain_ffn, w_query, key_value_weight, *rest):
    sizes = (lax.axis_size("dp"), lax.axis_size("row"), lax.axis_size("col"))
    one_each = sizes == (4, 2, 4) and tokens.shape[0] == sizes[2]
    pairs = w_query.shape[1] == 8 * HEAD_SIZE and key_value_weight.shape[2] == 2 * HEAD_SIZE
    chosen = one_sequence_body if one_each and pairs else general_body
    return chosen(
        tokens, cotangent, lengths, deal_order, gain_attn, gain_ffn, w_query, key_value_weight, *rest
    )


def solution(mesh):
    placed = (
        P("dp", "row", "col"),
        P("dp", "row", "col"),
        P(),
        P(),
        P(),
        P(),
        P("row", "col"),
        P("row", None, "col"),
        P("row", "col"),
        P("row", None, "col"),
        P("row", "col"),
    )
    return jax.shard_map(
        body,
        mesh=mesh,
        in_specs=placed,
        out_specs=(
            P("dp", "row", "col"),
            P("dp", "row", "col"),
            P(("dp", "row"), "col"),
            P(("dp", "row"), None, "col"),
            P(("dp", "row"), "col"),
            P(("dp", "row"), None, "col"),
            P(("dp", "row"), "col"),
            P(),
            P(),
        ),
        check_vma=False,
    )
```

```python
import functools

import jax
import jax.numpy as jnp
from jax import lax
from jax.experimental import pallas as pl
from jax.experimental.pallas import tpu as pltpu
from jax.sharding import PartitionSpec as P

HEAD_SIZE = 64


EPSILON = 1e-05
THETA = 10000000.0
ATTN_MULT = 0.015625
RES_MULT = 0.22
MASKED = -1e30


def rope_tables(positions, head_size):
    halves = jnp.arange(head_size // 2, dtype=jnp.float32)
    inverse_freq = THETA ** (-(halves * 2.0) / head_size)
    angles = positions.astype(jnp.float32)[:, None] * inverse_freq[None, :]
    return (jnp.cos(angles), jnp.sin(angles))


def rotary_embed(value_rows, cosine_table, sine_table):
    middle = value_rows.shape[-1] // 2
    first_half = value_rows[..., :middle]
    second_half = value_rows[..., middle:]
    cos_part = cosine_table[:, None, :]
    sin_part = sine_table[:, None, :]
    return jnp.concatenate(
        [
            first_half * cos_part - second_half * sin_part,
            second_half * cos_part + first_half * sin_part,
        ],
        axis=-1,
    )


def widen_cols(value_rows):
    return lax.all_gather(value_rows, "col", axis=1, tiled=True)


def narrow_cols(value_rows):
    return lax.psum_scatter(value_rows, "col", scatter_dimension=1, tiled=True)


def sum_over_cols(value_rows):
    return lax.psum(value_rows, "col")


def contract_local(operand, matrix):
    return lax.dot_general(
        operand, matrix, (((1,), (0,)), ((), ())), preferred_element_type=jnp.float32
    )


def expand_local(operand, matrix):
    trailing = tuple(range(1, operand.ndim))
    return lax.dot_general(
        operand, matrix, ((trailing, trailing), ((), ())), preferred_element_type=jnp.float32
    )


def token_outer(features, grads):
    return lax.dot_general(
        features, grads, (((0,), (0,)), ((), ())), preferred_element_type=jnp.float32
    )


def contract_rows(operand, matrix):
    return contract_local(operand, lax.all_gather(matrix, "row", axis=0, tiled=True))


def expand_rows(operand, matrix):
    return expand_local(operand, lax.all_gather(matrix, "row", axis=0, tiled=True))


def split_keys(key_seq, value_seq, key_pos):
    slot_len = key_seq.shape[0]
    width = min(512, slot_len)
    count = slot_len // width
    return (
        key_seq.reshape(count, width, key_seq.shape[1], key_seq.shape[2]),
        value_seq.reshape(count, width, value_seq.shape[1], value_seq.shape[2]),
        key_pos.reshape(count, width),
    )


def block_scores(query_seq, key_block, pos_block, query_pos, length):
    scores = (
        jnp.einsum("qkgd,tkd->kgqt", query_seq, key_block, preferred_element_type=jnp.float32)
        * ATTN_MULT
    )
    allowed = (pos_block[None, :] <= query_pos[:, None]) & (pos_block[None, :] < length)
    return jnp.where(allowed, scores, MASKED)


def attend(inputs, key_pos, query_pos):
    query_seq, key_seq, value_seq, length = inputs
    key_blocks, value_blocks, pos_blocks = split_keys(key_seq, value_seq, key_pos)
    stat_shape = (query_seq.shape[1], query_seq.shape[2], query_seq.shape[0], 1)

    def gather_stats(carry, entry):
        running_max, running_sum = carry
        key_block, pos_block = entry
        scores = block_scores(query_seq, key_block, pos_block, query_pos, length)
        new_max = jnp.maximum(running_max, jnp.max(scores, axis=-1, keepdims=True))
        new_sum = running_sum * jnp.exp(running_max - new_max) + jnp.sum(
            jnp.exp(scores - new_max), axis=-1, keepdims=True
        )
        return ((new_max, new_sum), None)

    start_stats = (jnp.full(stat_shape, MASKED, jnp.float32), jnp.zeros(stat_shape, jnp.float32))
    (row_max, row_sums), unused = lax.scan(gather_stats, start_stats, (key_blocks, pos_blocks))

    def mix_values(running, entry):
        key_block, value_block, pos_block = entry
        scores = block_scores(query_seq, key_block, pos_block, query_pos, length)
        weights = jnp.exp(scores - row_max) / row_sums
        return (
            running
            + jnp.einsum(
                "kgqt,tkd->qkgd",
                weights.astype(jnp.bfloat16),
                value_block,
                preferred_element_type=jnp.float32,
            ),
            None,
        )

    start_mix = jnp.zeros(query_seq.shape, jnp.float32)
    mixed_heads, unused = lax.scan(mix_values, start_mix, (key_blocks, value_blocks, pos_blocks))
    return (mixed_heads, row_max, row_sums)


def attend_back(inputs, key_pos, query_pos):
    query_seq, key_seq, value_seq, grad_mixed, row_max, row_sums, length = inputs
    key_blocks, value_blocks, pos_blocks = split_keys(key_seq, value_seq, key_pos)

    def block_weights(key_block, value_block, pos_block):
        scores = block_scores(query_seq, key_block, pos_block, query_pos, length)
        weights = jnp.exp(scores - row_max) / row_sums
        grad_weights = jnp.einsum(
            "qkgd,tkd->kgqt", grad_mixed, value_block, preferred_element_type=jnp.float32
        )
        return (weights, grad_weights)

    def gather_centre(running, entry):
        weights, grad_weights = block_weights(*entry)
        return (running + jnp.sum(weights * grad_weights, axis=-1, keepdims=True), None)

    start_centre = jnp.zeros(row_max.shape, jnp.float32)
    centre, unused = lax.scan(gather_centre, start_centre, (key_blocks, value_blocks, pos_blocks))

    def grads_block(running, entry):
        key_block = entry[0]
        weights, grad_weights = block_weights(*entry)
        grad_scores = (weights * (grad_weights - centre)).astype(jnp.bfloat16)
        grad_query = (
            running
            + jnp.einsum(
                "kgqt,tkd->qkgd", grad_scores, key_block, preferred_element_type=jnp.float32
            )
            * ATTN_MULT
        )
        grad_key = (
            jnp.einsum("kgqt,qkgd->tkd", grad_scores, query_seq, preferred_element_type=jnp.float32)
            * ATTN_MULT
        )
        grad_value = jnp.einsum(
            "kgqt,qkgd->tkd",
            weights.astype(jnp.bfloat16),
            grad_mixed,
            preferred_element_type=jnp.float32,
        )
        return (grad_query, (grad_key, grad_value))

    start_query = jnp.zeros(query_seq.shape, jnp.float32)
    grad_query, (grad_key, grad_value) = lax.scan(
        grads_block, start_query, (key_blocks, value_blocks, pos_blocks)
    )
    return (grad_query, grad_key.reshape(key_seq.shape), grad_value.reshape(value_seq.shape))


MESH_IDS = pl.DeviceIdType.MESH
SIBLINGS = [(0, 1), (1, 0), (2, 3), (3, 2)]
OVER_X = [(0, 1), (1, 0)]
OVER_Y = [(0, 2), (2, 0), (1, 3), (3, 1)]
CROSSED = [((2 * y + c) * 2 + x, (2 * y + x) * 2 + c) for y in (0, 1) for c in (0, 1) for x in (0, 1)]


def pick_sequences(everyone, deal_order, first, count):
    slots = jnp.arange(deal_order.shape[0], dtype=jnp.int32)
    inverse = jnp.sum(jnp.where(deal_order[None, :] == slots[:, None], slots[None, :], 0), axis=1)
    return jnp.concatenate(
        [
            lax.dynamic_slice_in_dim(
                everyone, lax.dynamic_index_in_dim(inverse, first + at, keepdims=False), 1
            )
            for at in range(count)
        ]
    )


def bring_cotangent(cotangent, deal_order, first):
    everyone = lax.all_gather(cotangent, "dp", axis=0, tiled=True)
    return pick_sequences(everyone, deal_order, first, cotangent.shape[0])


def place():
    group = lax.axis_index("dp")
    core = lax.rem(group, 2)
    row = lax.axis_index("row")
    return group, core, group - core + row, row, lax.axis_index("col")


def lined(index, step, count):
    return lax.rem(index + step + count, count)


def aligned(block, size):
    return pl.ds(pl.multiple_of(block * size, size), size)


def greet(device):
    pl.semaphore_signal(
        pltpu.get_barrier_semaphore(), inc=1, device_id=device, device_id_type=MESH_IDS
    )


def remote(src, dst, sems, at, device):
    return pltpu.make_async_remote_copy(
        src_ref=src,
        dst_ref=dst,
        send_sem=sems.at[0, at],
        recv_sem=sems.at[1, at],
        device_id=device,
        device_id_type=MESH_IDS,
    )


def line_order(col, last, at):
    inner_low = jnp.where(at < 2, 1 - at, at)
    inner_high = jnp.where(at == 3, 0, jnp.where(at == 0, 2, jnp.where(at == 1, 1, 3)))
    return jnp.where(
        col == 0, at, jnp.where(col == last, last - at, jnp.where(col == 1, inner_low, inner_high))
    )


def start_kernel(
    cols, tok_ref, gain_ref, x_ref, a_ref, x_buf, a_buf, tok_sems, a_sems, local_sems
):
    group, core, mate, row, col = place()
    width = tok_ref.shape[2]
    length = x_buf.shape[0]
    sibling = (group + 1 - 2 * core, row, col)

    def line(step):
        return lined(col, step, cols)

    for step in range(1, cols):
        greet((mate, core, line(step)))
    greet(sibling)

    @pl.when(core != row)
    def _():
        greet((mate, core, col))

    pl.semaphore_wait(pltpu.get_barrier_semaphore(), cols + (core - row) * (core - row))

    def token_copy(step, into):
        return remote(
            tok_ref.at[line(step)],
            x_buf.at[:, aligned(into, width)],
            tok_sems,
            step,
            (mate, core, line(step)),
        )

    own_tokens = pltpu.make_async_copy(
        tok_ref.at[col], x_buf.at[:, aligned(col, width)], local_sems.at[0]
    )
    for step in range(1, cols):
        token_copy(step, col).start()

    @pl.when(core != row)
    def _():
        token_copy(0, col).start()

    @pl.when(core == row)
    def _():
        own_tokens.start()

    for step in range(1, cols):
        token_copy(step, line(-step)).wait_recv()

    @pl.when(core != row)
    def _():
        token_copy(0, col).wait_recv()

    @pl.when(core == row)
    def _():
        own_tokens.wait()

    keep_x = pltpu.make_async_copy(x_buf, x_ref, local_sems.at[1])
    keep_x.start()
    tall = min(64, length)

    @pl.loop(0, length // tall)
    def _(at):
        here = aligned(at, tall)
        now = x_buf[here, :].astype(jnp.float32)
        scale = lax.rsqrt(jnp.mean(now * now, axis=1, keepdims=True) + EPSILON)
        a_buf[here, :] = (now * scale * gain_ref[...]).astype(jnp.bfloat16)

    def a_copy(of_core):
        return remote(a_buf, a_ref.at[aligned(of_core, length)], a_sems, 0, sibling)

    own_a = pltpu.make_async_copy(a_buf, a_ref.at[aligned(core, length)], local_sems.at[2])
    a_copy(core).start()
    own_a.start()
    for step in range(1, cols):
        token_copy(step, col).wait_send()

    @pl.when(core != row)
    def _():
        token_copy(0, col).wait_send()

    keep_x.wait()
    own_a.wait()
    a_copy(core).wait_send()
    a_copy(1 - core).wait_recv()


def start_exchange(tokens, gain, cols):
    anywhere = pl.BlockSpec(memory_space=pl.ANY)
    seqs, length, width = tokens.shape
    full = width * cols
    return pl.pallas_call(
        functools.partial(start_kernel, cols),
        out_shape=(
            jax.ShapeDtypeStruct((length, full), tokens.dtype),
            jax.ShapeDtypeStruct((2 * length, full), tokens.dtype),
        ),
        in_specs=[anywhere, pl.BlockSpec(memory_space=pltpu.VMEM)],
        out_specs=(anywhere,) * 2,
        scratch_shapes=[
            pltpu.VMEM((length, full), tokens.dtype),
            pltpu.VMEM((length, full), tokens.dtype),
            pltpu.SemaphoreType.DMA((2, cols)),
            pltpu.SemaphoreType.DMA((2, 1)),
            pltpu.SemaphoreType.DMA((3,)),
        ],
        compiler_params=pltpu.CompilerParams(
            collective_id=1, has_side_effects=True, vmem_limit_bytes=16 << 20
        ),
        cost_estimate=pl.CostEstimate(flops=0, bytes_accessed=200 << 20, transcendentals=0),
        name="start_exchange",
    )(tokens, gain.reshape(1, full))


def gather_kernel(
    cols, q_ref, o_ref, after_ref, wq_ref, wo_ref, q_send, q_recv, q_over, o_send, o_recv, o_over, local_sems
):
    group, core, mate, row, col = place()
    last = cols - 1
    over = (group, 1 - row, col)
    greet(over)

    @pl.when(col < last)
    def _():
        greet((group, row, col + 1))

    @pl.when(col > 0)
    def _():
        greet((group, row, col - 1))

    pl.semaphore_wait(
        pltpu.get_barrier_semaphore(),
        1 + jnp.minimum(col, 1) + jnp.minimum(last - col, 1),
    )

    def moves(own, full, send, recv, over_sems):
        tall, wide = own.shape

        def block(of_row, of_col):
            return full.at[aligned(of_row, tall), aligned(of_col, wide)]

        def along(src, chunk, to, way):
            return pltpu.make_async_remote_copy(
                src_ref=src,
                dst_ref=block(row, chunk),
                send_sem=send.at[way, chunk],
                recv_sem=recv.at[chunk],
                device_id=(group, row, to),
                device_id_type=MESH_IDS,
            )

        def across(src, of_row, chunk):
            return remote(src, block(of_row, chunk), over_sems, chunk, over)

        return block, along, across

    both = (
        (q_ref, moves(q_ref, wq_ref, q_send, q_recv, q_over)),
        (o_ref, moves(o_ref, wo_ref, o_send, o_recv, o_over)),
    )
    own_copies = []
    for at, (own, (block, along, across)) in enumerate(both):

        @pl.when(col < last)
        def _():
            along(own, col, col + 1, 0).start()

        @pl.when(col > 0)
        def _():
            along(own, col, col - 1, 1).start()

        across(own, row, col).start()
        own_copies.append(pltpu.make_async_copy(own, block(row, col), local_sems.at[at]))
        own_copies[-1].start()
    for at in range(1, cols):
        chunk = line_order(col, last, at)
        for own, (block, along, across) in both:
            along(own, chunk, col, 0).wait_recv()

            @pl.when((chunk < col) & (col < last))
            def _():
                along(block(row, chunk), chunk, col + 1, 0).start()

            @pl.when((chunk > col) & (col > 0))
            def _():
                along(block(row, chunk), chunk, col - 1, 1).start()

            across(block(row, chunk), row, chunk).start()
    for copy in own_copies:
        copy.wait()
    for own, (block, along, across) in both:
        for chunk in range(cols):

            @pl.when((col >= chunk) & (col < last))
            def _():
                along(own, chunk, col + 1, 0).wait_send()

            @pl.when((col <= chunk) & (col > 0))
            def _():
                along(own, chunk, col - 1, 1).wait_send()

            across(own, row, chunk).wait_send()
            across(own, 1 - row, chunk).wait_recv()


def gather_weights(own_q, own_o, after, rows, cols):
    anywhere = pl.BlockSpec(memory_space=pl.ANY)

    def whole(own):
        return jax.ShapeDtypeStruct((own.shape[0] * rows, own.shape[1] * cols), own.dtype)

    return pl.pallas_call(
        functools.partial(gather_kernel, cols),
        out_shape=(whole(own_q), whole(own_o)),
        in_specs=[anywhere] * 3,
        out_specs=(anywhere,) * 2,
        scratch_shapes=[
            pltpu.SemaphoreType.DMA((2, cols)),
            pltpu.SemaphoreType.DMA((cols,)),
            pltpu.SemaphoreType.DMA((2, cols)),
        ]
        * 2
        + [pltpu.SemaphoreType.DMA((2,))],
        compiler_params=pltpu.CompilerParams(collective_id=4, has_side_effects=True),
        cost_estimate=pl.CostEstimate(flops=0, bytes_accessed=300 << 20, transcendentals=0),
        name="gather_weights",
    )(own_q, own_o, after)


def half_turn(wide):
    lanes = wide.shape[1]
    half = HEAD_SIZE // 2
    lane = lax.broadcasted_iota(jnp.int32, wide.shape, 1)
    return jnp.where(
        lax.rem(lane, HEAD_SIZE) < half,
        pltpu.roll(wide, lanes - half, 1),
        pltpu.roll(wide, half, 1),
    )


def both_heads(pair):
    lane = lax.broadcasted_iota(jnp.int32, pair.shape, 1)
    turned = pltpu.roll(pair, HEAD_SIZE, 1)
    low = lane < HEAD_SIZE
    return jnp.where(low, pair, turned), jnp.where(low, turned, pair)


def keep_head(pair, side):
    lane = lax.broadcasted_iota(jnp.int32, pair.shape, 1)
    mine = lane < HEAD_SIZE if side == 0 else lane >= HEAD_SIZE
    return jnp.where(mine, pair, jnp.zeros_like(pair))


def dot_nn(a, b):
    return lax.dot_general(a, b, (((1,), (0,)), ((), ())), preferred_element_type=jnp.float32)


def dot_nt(a, b):
    return lax.dot_general(a, b, (((1,), (1,)), ((), ())), preferred_element_type=jnp.float32)


def dot_tn(a, b):
    return lax.dot_general(a, b, (((0,), (0,)), ((), ())), preferred_element_type=jnp.float32)


PAIR = 2 * HEAD_SIZE


def attend_kernel(block, len_ref, a_ref, w_ref, cos_ref, sin_ref, qkv_ref, z_ref, q_all, k_two, v_two):
    rows = a_ref.shape[0]
    heads = q_all.shape[0]
    length = len_ref[0]

    @pl.loop(0, rows // block)
    def _(at):
        here = pl.ds(pl.multiple_of(at * block, block), block)
        lin = dot_nn(a_ref[here, :], w_ref[...])
        for part in range(heads // 2 + 1):
            lanes = slice(part * PAIR, (part + 1) * PAIR)
            now = lin[:, lanes]
            table = slice(0, PAIR) if part < heads // 2 else slice(PAIR, 2 * PAIR)
            now = now * cos_ref[here, table] + half_turn(now) * sin_ref[here, table]
            qkv_ref[here, lanes] = now.astype(jnp.bfloat16)
            if part < heads // 2:
                for side in range(2):
                    q_all[2 * part + side, here, :] = keep_head(now * ATTN_MULT, side).astype(
                        jnp.bfloat16
                    )
            else:
                keys, values = both_heads(now)
                k_two[here, :] = keys.astype(jnp.bfloat16)
                v_two[here, :] = values.astype(jnp.bfloat16)

    for at in range(rows // block):
        here = slice(at * block, (at + 1) * block)
        upto = (at + 1) * block
        row = lax.broadcasted_iota(jnp.int32, (block, upto), 0) + at * block
        key = lax.broadcasted_iota(jnp.int32, (block, upto), 1)
        allowed = key < jnp.minimum(row + 1, length)

        def one_head(head):
            scores = dot_nt(q_all[head, here, :], k_two[:upto, :])
            scores = jnp.where(allowed, scores, MASKED)
            top = jnp.max(scores, axis=1, keepdims=True)
            power = jnp.exp(scores - top)
            total = jnp.sum(power, axis=1, keepdims=True)
            return dot_nn(power.astype(jnp.bfloat16), v_two[:upto, :]) / total

        for pair in range(heads // 2):
            low = one_head(2 * pair)
            high = one_head(2 * pair + 1)
            lane = lax.broadcasted_iota(jnp.int32, low.shape, 1)
            z_ref[here, pair * PAIR : (pair + 1) * PAIR] = jnp.where(
                lane < HEAD_SIZE, low, high
            ).astype(jnp.bfloat16)


def attend_fast(length, inputs, weights, cosines, sines, groups):
    rows, depth = inputs.shape
    wide = weights.shape[1] // groups
    heads = (wide - PAIR) // HEAD_SIZE
    block = min(256, rows)
    return pl.pallas_call(
        functools.partial(attend_kernel, block),
        grid=(groups,),
        out_shape=(
            jax.ShapeDtypeStruct((rows, groups * wide), jnp.bfloat16),
            jax.ShapeDtypeStruct((rows, groups * heads * HEAD_SIZE), jnp.bfloat16),
        ),
        in_specs=[
            pl.BlockSpec(memory_space=pltpu.SMEM),
            pl.BlockSpec((rows, depth), lambda g: (0, 0)),
            pl.BlockSpec((depth, wide), lambda g: (0, g)),
            pl.BlockSpec((rows, 2 * PAIR), lambda g: (0, 0)),
            pl.BlockSpec((rows, 2 * PAIR), lambda g: (0, 0)),
        ],
        out_specs=(
            pl.BlockSpec((rows, wide), lambda g: (0, g)),
            pl.BlockSpec((rows, heads * HEAD_SIZE), lambda g: (0, g)),
        ),
        scratch_shapes=[
            pltpu.VMEM((heads, rows, PAIR), jnp.bfloat16),
            pltpu.VMEM((rows, PAIR), jnp.bfloat16),
            pltpu.VMEM((rows, PAIR), jnp.bfloat16),
        ],
        compiler_params=pltpu.CompilerParams(vmem_limit_bytes=48 << 20),
        cost_estimate=pl.CostEstimate(
            flops=2 * rows * depth * wide * groups + 2 * groups * heads * rows * rows * 128,
            bytes_accessed=2 * (rows * depth + depth * wide * groups + rows * wide * groups),
            transcendentals=groups * heads * rows * rows // 2,
        ),
        name="attend",
    )(length, inputs, weights, cosines, sines)


def attend_back_kernel(
    block, len_ref, qkv_ref, dz_ref, cos_ref, sin_ref, out_ref, q_all, z_all, k_two, v_two, k_acc, v_acc
):
    rows = qkv_ref.shape[0]
    heads = q_all.shape[0]
    length = len_ref[0]

    @pl.loop(0, rows // block)
    def _(at):
        here = pl.ds(pl.multiple_of(at * block, block), block)
        for part in range(heads // 2):
            lanes = slice(part * PAIR, (part + 1) * PAIR)
            queries = qkv_ref[here, lanes].astype(jnp.float32) * ATTN_MULT
            mixed = dz_ref[here, lanes].astype(jnp.float32)
            for side in range(2):
                q_all[2 * part + side, here, :] = keep_head(queries, side).astype(jnp.bfloat16)
                z_all[2 * part + side, here, :] = keep_head(mixed, side).astype(jnp.bfloat16)
        keys, values = both_heads(qkv_ref[here, heads * HEAD_SIZE :].astype(jnp.float32))
        k_two[here, :] = keys.astype(jnp.bfloat16)
        v_two[here, :] = values.astype(jnp.bfloat16)
        k_acc[here, :] = jnp.zeros((block, PAIR), jnp.float32)
        v_acc[here, :] = jnp.zeros((block, PAIR), jnp.float32)

    def turn_back(now, here, table):
        return (now * cos_ref[here, table] - half_turn(now) * sin_ref[here, table]).astype(
            jnp.bfloat16
        )

    for at in range(rows // block):
        here = slice(at * block, (at + 1) * block)
        upto = (at + 1) * block
        key = lax.broadcasted_iota(jnp.int32, (upto, block), 0)
        query = lax.broadcasted_iota(jnp.int32, (upto, block), 1) + at * block
        allowed = key < jnp.minimum(query + 1, length)

        def one_head(head):
            queries, mixed = q_all[head, here, :], z_all[head, here, :]
            scores = jnp.where(allowed, dot_nt(k_two[:upto, :], queries), MASKED)
            power = jnp.exp(scores - jnp.max(scores, axis=0, keepdims=True))
            weights = power * (1.0 / jnp.sum(power, axis=0, keepdims=True))
            back = dot_nt(v_two[:upto, :], mixed)
            centre = jnp.sum(weights * back, axis=0, keepdims=True)
            slope = (weights * (back - centre)).astype(jnp.bfloat16)
            k_acc[:upto, :] += dot_nn(slope, queries)
            v_acc[:upto, :] += dot_nn(weights.astype(jnp.bfloat16), mixed)
            return dot_tn(slope, k_two[:upto, :]) * ATTN_MULT

        for pair in range(heads // 2):
            low = one_head(2 * pair)
            high = one_head(2 * pair + 1)
            lane = lax.broadcasted_iota(jnp.int32, low.shape, 1)
            lanes = slice(pair * PAIR, (pair + 1) * PAIR)
            out_ref[here, lanes] = turn_back(
                jnp.where(lane < HEAD_SIZE, low, high), here, slice(0, PAIR)
            )

    @pl.loop(0, rows // block)
    def _(at):
        here = pl.ds(pl.multiple_of(at * block, block), block)
        keys, values = k_acc[here, :], v_acc[here, :]
        keys = keys + pltpu.roll(keys, HEAD_SIZE, 1)
        values = values + pltpu.roll(values, HEAD_SIZE, 1)
        lane = lax.broadcasted_iota(jnp.int32, keys.shape, 1)
        lanes = slice(heads * HEAD_SIZE, heads * HEAD_SIZE + PAIR)
        out_ref[here, lanes] = turn_back(
            jnp.where(lane < HEAD_SIZE, keys, values), here, slice(PAIR, 2 * PAIR)
        )


def attend_back_fast(length, projected, grad_mixed, cosines, sines, groups):
    rows = projected.shape[0]
    wide = projected.shape[1] // groups
    heads = (wide - PAIR) // HEAD_SIZE
    block = min(256, rows)
    return pl.pallas_call(
        functools.partial(attend_back_kernel, block),
        grid=(groups,),
        out_shape=jax.ShapeDtypeStruct((rows, groups * wide), jnp.bfloat16),
        in_specs=[
            pl.BlockSpec(memory_space=pltpu.SMEM),
            pl.BlockSpec((rows, wide), lambda g: (0, g)),
            pl.BlockSpec((rows, heads * HEAD_SIZE), lambda g: (0, g)),
            pl.BlockSpec((rows, 2 * PAIR), lambda g: (0, 0)),
            pl.BlockSpec((rows, 2 * PAIR), lambda g: (0, 0)),
        ],
        out_specs=pl.BlockSpec((rows, wide), lambda g: (0, g)),
        scratch_shapes=[
            pltpu.VMEM((heads, rows, PAIR), jnp.bfloat16),
            pltpu.VMEM((heads, rows, PAIR), jnp.bfloat16),
            pltpu.VMEM((rows, PAIR), jnp.bfloat16),
            pltpu.VMEM((rows, PAIR), jnp.bfloat16),
            pltpu.VMEM((rows, PAIR), jnp.float32),
            pltpu.VMEM((rows, PAIR), jnp.float32),
        ],
        compiler_params=pltpu.CompilerParams(vmem_limit_bytes=48 << 20),
        cost_estimate=pl.CostEstimate(
            flops=5 * groups * heads * rows * rows * 128,
            bytes_accessed=2 * (2 * rows * wide * groups + rows * heads * HEAD_SIZE * groups),
            transcendentals=groups * heads * rows * rows // 2,
        ),
        name="attend_back",
    )(length, projected, grad_mixed, cosines, sines)


def ffn_kernel(
    cols,
    own_ref,
    resid_ref,
    grad_ref,
    wg_own,
    wu_own,
    wd_own,
    wg_far,
    wu_far,
    wd_far,
    wg_far_y,
    wu_far_y,
    wd_far_y,
    wg_sib,
    wu_sib,
    wd_sib,
    wg_sib_y,
    wu_sib_y,
    wd_sib_y,
    u_all,
    dgu_all,
    mlp_all,
    back_all,
    relay_ref,
    land_ref,
    a_keep,
    a_send,
    b_keep,
    b_send,
    wg,
    wu,
    wd,
    b_all,
    b_turn,
    g_two,
    u_buf,
    dg_buf,
    du_buf,
    mlp_buf,
    back_buf,
    w_sems,
    ag_send,
    ag_recv,
    back_send,
    back_recv,
    relay_recv,
    pair_sems,
    lane_sems,
    tile_sems,
    io_sems,
):
    group, core, mate, row, col = place()
    sibling = (group + 1 - 2 * core, row, col)
    last = cols - 1
    depth = wg_own.shape[0]
    half = depth // 2
    units = wg_own.shape[1]
    rows = own_ref.shape[0]
    tile = units // cols
    beside = col + 1 - 2 * lax.rem(col, 2)
    facing = last - col
    inner = (col > 0) & (col < last)

    for step in range(1, cols):
        greet((group, row, lined(col, step, cols)))
    greet(sibling)
    pl.semaphore_wait(pltpu.get_barrier_semaphore(), cols)

    def pass_on(src, at, to, way):
        return pltpu.make_async_remote_copy(
            src_ref=src,
            dst_ref=b_all.at[at],
            send_sem=ag_send.at[way, at],
            recv_sem=ag_recv.at[at],
            device_id=(group, row, to),
            device_id_type=MESH_IDS,
        )

    @pl.when(col < last)
    def _():
        pass_on(own_ref, col, col + 1, 0).start()

    @pl.when(col > 0)
    def _():
        pass_on(own_ref, col, col - 1, 1).start()

    def order(at):
        return line_order(col, last, at)

    def load_g(at):
        side = lax.rem(at, 2)
        return pltpu.make_async_copy(grad_ref.at[order(at)], g_two.at[side], io_sems.at[6 + side])

    quarter = half // 2
    high = (group - core) // 2

    def rows_at(first, size):
        return pl.ds(pl.multiple_of(first, quarter), size)

    own_copy = pltpu.make_async_copy(own_ref, b_all.at[col], io_sems.at[0])
    own_copy.start()
    load_resid = pltpu.make_async_copy(resid_ref, mlp_buf, io_sems.at[8])
    far = (1 - row) * depth
    loads = []
    for full, mine, pieces in (
        (wg, wg_own, (wg_far, wg_far_y, wg_sib, wg_sib_y)),
        (wu, wu_own, (wu_far, wu_far_y, wu_sib, wu_sib_y)),
        (wd, wd_own, (wd_far, wd_far_y, wd_sib, wd_sib_y)),
    ):
        places = [
            far + of_core * half + of_plane * quarter
            for of_core in (core, 1 - core)
            for of_plane in (high, 1 - high)
        ]
        loads.append(
            pltpu.make_async_copy(
                mine, full.at[rows_at(row * depth, depth)], w_sems.at[len(loads)]
            )
        )
        for piece, first in zip(pieces, places):
            loads.append(
                pltpu.make_async_copy(
                    piece, full.at[rows_at(first, quarter)], w_sems.at[len(loads)]
                )
            )
    for load in loads:
        load.start()
    load_g(0).start()
    load_resid.start()
    own_copy.wait()
    for load in loads:
        load.wait()

    def arrive(chunk):
        pass_on(b_all.at[chunk], chunk, col, 0).wait_recv()

        @pl.when((chunk < col) & (col < last))
        def _():
            pass_on(b_all.at[chunk], chunk, col + 1, 0).start()

        @pl.when((chunk > col) & (col > 0))
        def _():
            pass_on(b_all.at[chunk], chunk, col - 1, 1).start()

    def outputs(chunk):
        return (
            pltpu.make_async_copy(u_buf, u_all.at[chunk], io_sems.at[1]),
            pltpu.make_async_copy(dg_buf, dgu_all.at[chunk, :, 0:units], io_sems.at[2]),
            pltpu.make_async_copy(du_buf, dgu_all.at[chunk, :, units : 2 * units], io_sems.at[3]),
        )

    def mlp_out(chunk):
        return pltpu.make_async_copy(mlp_buf, mlp_all.at[chunk], io_sems.at[4])

    def slot_of(at):
        return lax.rem(at, cols - 1)

    def deliver(slot, to, place_there, at):
        return pltpu.make_async_remote_copy(
            src_ref=back_buf.at[slot],
            dst_ref=back_all.at[place_there],
            send_sem=back_send.at[at],
            recv_sem=back_recv.at[place_there],
            device_id=(group, row, to),
            device_id_type=MESH_IDS,
        )

    def hand_over(slot, to, box, at):
        return pltpu.make_async_remote_copy(
            src_ref=back_buf.at[slot],
            dst_ref=relay_ref.at[box],
            send_sem=back_send.at[at],
            recv_sem=relay_recv.at[box],
            device_id=(group, row, to),
            device_id_type=MESH_IDS,
        )

    own_back = pltpu.make_async_copy(back_buf.at[0], back_all.at[0], io_sems.at[5])
    at_end = jnp.logical_not(inner)

    def one_chunk(at, unused):
        chunk = order(at)
        side = lax.rem(at, 2)

        @pl.when(at_end & (at > 0))
        def _():
            arrive(order(at))

        @pl.when(inner & (at == 1))
        def _():
            arrive(order(1))
            arrive(order(2))

        @pl.when(inner & (at == 3))
        def _():
            arrive(order(3))

        load_g(at).wait()

        @pl.when(at < last)
        def _():
            load_g(at + 1).start()

        @pl.when(at > 0)
        def _():
            for copy in outputs(order(at - 1)):
                copy.wait()

        @pl.loop(0, units // tile)
        def _(step):
            lanes = aligned(step, tile)
            gate = dot_nn(b_all[chunk], wg[:, lanes])
            upward = dot_nn(b_all[chunk], wu[:, lanes])
            back = RES_MULT * dot_nn(g_two[side], wd[:, lanes])
            opened = 1.0 / (1.0 + jnp.exp(-gate))
            silu = gate * opened
            u_buf[:, lanes] = (silu * upward).astype(jnp.bfloat16)
            slope = opened * (1.0 + gate * (1.0 - opened))
            dg_buf[:, lanes] = (back * upward * slope).astype(jnp.bfloat16)
            du_buf[:, lanes] = (back * silu).astype(jnp.bfloat16)

        for copy in outputs(chunk):
            copy.start()

        @pl.when(at > 0)
        def _():
            mlp_out(order(at - 1)).wait()

        @pl.when(at == 0)
        def _():
            load_resid.wait()

        @pl.when(at == last)
        def _():
            own_back.wait()

        @pl.loop(0, 2 * depth // tile)
        def _(step):
            here = aligned(step, tile)
            back = dot_nt(dg_buf[...], wg[here, :]) + dot_nt(du_buf[...], wu[here, :])
            back_buf[slot_of(at), :, here] = back.astype(jnp.bfloat16)
            added = jnp.where(at == 0, mlp_buf[:, here].astype(jnp.float32), 0.0)
            mlp_buf[:, here] = (added + RES_MULT * dot_nt(u_buf[...], wd[here, :])).astype(
                jnp.bfloat16
            )

        mlp_out(chunk).start()

        @pl.when(at == 0)
        def _():
            own_back.start()

        @pl.when(at_end & (at == 1))
        def _():
            deliver(1, beside, 1, 1).start()

        @pl.when(at_end & (at == 2))
        def _():
            hand_over(2, beside, 1, 2).start()

        @pl.when(at_end & (at == 3))
        def _():
            deliver(0, facing, 2, 3).start()

        @pl.when(inner & (at == 3))
        def _():
            hand_over(0, facing, 0, 3).start()

        return unused

    lax.fori_loop(0, cols, one_chunk, 0)
    for copy in outputs(order(last)):
        copy.wait()
    mlp_out(order(last)).wait()

    loads = []
    for chunk in range(cols):
        here = slice(chunk * rows, (chunk + 1) * rows)
        loads += [
            pltpu.make_async_copy(
                dgu_all.at[chunk, :, 0:units], wg.at[here], w_sems.at[chunk]
            ),
            pltpu.make_async_copy(
                dgu_all.at[chunk, :, units : 2 * units], wu.at[here], w_sems.at[cols + chunk]
            ),
            pltpu.make_async_copy(u_all.at[chunk], wd.at[here], w_sems.at[2 * cols + chunk]),
        ]
    for load in loads:
        load.start()

    def relay(box, slot):
        hand_over(slot, facing, box, 3).wait_recv()
        load = pltpu.make_async_copy(relay_ref.at[box], mlp_buf, io_sems.at[4])
        load.start()
        load.wait()
        tall = min(64, rows)

        @pl.loop(0, rows // tall)
        def _(at):
            here = aligned(at, tall)
            back_buf[slot, here, :] = (
                back_buf[slot, here, :].astype(jnp.float32)
                + mlp_buf[here, :].astype(jnp.float32)
            ).astype(jnp.bfloat16)

    buffers = (dg_buf, du_buf, u_buf)

    def to_sibling(at, part):
        return pltpu.make_async_remote_copy(
            src_ref=buffers[part],
            dst_ref=land_ref.at[at, part],
            send_sem=pair_sems.at[0, at, part],
            recv_sem=pair_sems.at[1, at, part],
            device_id=sibling,
            device_id_type=MESH_IDS,
        )

    def landed(at, part):
        return pltpu.make_async_copy(land_ref.at[at, part], buffers[part], io_sems.at[1 + part])

    halfway = units // 2
    small = rows // 2
    mine, others = aligned(row, small), aligned(1 - row, small)

    def x_lane(high):
        return (
            pltpu.make_async_copy(
                dg_buf.at[mine], a_keep.at[high, :, 0:units], lane_sems.at[0]
            ),
            pltpu.make_async_copy(
                dg_buf.at[others], a_send.at[high, :, 0:units], lane_sems.at[1]
            ),
            pltpu.make_async_copy(
                u_buf.at[mine, 0:halfway],
                a_keep.at[high, :, units : units + halfway],
                lane_sems.at[2],
            ),
            pltpu.make_async_copy(
                u_buf.at[others, 0:halfway],
                a_send.at[high, :, units : units + halfway],
                lane_sems.at[3],
            ),
        )

    def y_lane(target):
        copies = []
        for side in range(2):
            here = slice(side * small, (side + 1) * small)
            copies += [
                pltpu.make_async_copy(
                    du_buf.at[here], target.at[side, :, 0:units], lane_sems.at[4 + 2 * side]
                ),
                pltpu.make_async_copy(
                    u_buf.at[here, halfway:units],
                    target.at[side, :, units : units + halfway],
                    lane_sems.at[5 + 2 * side],
                ),
            ]
        return copies

    def put_results(high, act):
        for copy in x_lane(high):
            act(copy)

        @pl.when(high == (group - core) // 2)
        def _():
            for copy in y_lane(b_keep):
                act(copy)

        @pl.when(high != (group - core) // 2)
        def _():
            for copy in y_lane(b_send):
                act(copy)

    def start_it(copy):
        copy.start()

    def wait_for(copy):
        copy.wait()

    def part_of(chunk):
        return slice(chunk * rows, (chunk + 1) * rows)

    def grad_tile(block, chunk):
        return pltpu.make_async_copy(
            grad_ref.at[chunk, :, aligned(block, rows)],
            mlp_buf.at[:, part_of(chunk)],
            tile_sems.at[chunk],
        )

    parts = range(3)

    def block_of(at):
        return 2 * lax.rem(at, 2) + jnp.where(at >= 2, core, 1 - core)

    for chunk in range(cols):
        grad_tile(block_of(0), chunk).start()
    for chunk in range(cols):
        b_turn[0, :, part_of(chunk)] = b_all[chunk, :, aligned(block_of(0), rows)].T
    for chunk in range(cols):
        grad_tile(block_of(0), chunk).wait()
    for chunk in range(cols):
        g_two[0, :, part_of(chunk)] = mlp_buf[:, part_of(chunk)].T
    for load in loads:
        load.wait()

    def one_block(at, unused):
        high = lax.rem(at, 2)
        is_own = at >= 2
        side = lax.rem(at, 2)
        following = block_of(jnp.minimum(at + 1, 3))

        @pl.when(inner & (at == 1))
        def _():
            relay(0, col)
            deliver(col, beside, 1, 1).start()
            relay(1, last - col)
            deliver(last - col, facing, 2, 2).start()

        @pl.when(at < 3)
        def _():
            for chunk in range(cols):
                grad_tile(following, chunk).start()

        @pl.when((at == 1) | (at == 2))
        def _():
            for part in parts:
                to_sibling(at - 1, part).wait_send()

        @pl.when(at == 3)
        def _():
            put_results(0, wait_for)

        @pl.when(is_own)
        def _():
            for part in parts:
                to_sibling(high, part).wait_recv()
                landed(high, part).start()
            for part in parts:
                landed(high, part).wait()

        @pl.when(at < 3)
        def _():
            for chunk in range(cols):
                grad_tile(following, chunk).wait()

        @pl.loop(0, cols)
        def _(step):
            lanes = aligned(step, tile)
            tokens = aligned(step, rows)

            def put(buffer, value):
                other = jnp.where(is_own, buffer[:, lanes].astype(jnp.float32), 0.0)
                buffer[:, lanes] = (other + value).astype(jnp.bfloat16)

            put(dg_buf, dot_nn(b_turn[side], wg[:, lanes]))
            b_turn[1 - side, :, tokens] = b_all[step, :, aligned(following, rows)].T
            put(du_buf, dot_nn(b_turn[side], wu[:, lanes]))
            g_two[1 - side, :, tokens] = mlp_buf[:, tokens].T
            put(u_buf, RES_MULT * dot_nn(g_two[side], wd[:, lanes]))

        @pl.when(jnp.logical_not(is_own))
        def _():
            for part in parts:
                to_sibling(at, part).start()

        @pl.when(is_own)
        def _():
            put_results(high, start_it)

        return unused

    lax.fori_loop(0, 4, one_block, 0)
    put_results(1, wait_for)
    for at in range(1, cols):
        deliver(0, beside, 1, at).wait_send()
    for at in range(1, 3):
        deliver(0, beside, at, at).wait_recv()
    for chunk in range(cols):

        @pl.when((col >= chunk) & (col < last))
        def _():
            pass_on(own_ref, chunk, col + 1, 0).wait_send()

        @pl.when((col <= chunk) & (col > 0))
        def _():
            pass_on(own_ref, chunk, col - 1, 1).wait_send()


def feed_forward(own_input, resid, grad_rows, weights, cols):
    rows, width = own_input.shape
    units = weights[0].shape[1]
    anywhere = pl.BlockSpec(memory_space=pl.ANY)
    bf16 = jnp.bfloat16
    lane = jax.ShapeDtypeStruct((2, rows // 2, units + units // 2), bf16)
    return pl.pallas_call(
        functools.partial(ffn_kernel, cols),
        out_shape=(
            jax.ShapeDtypeStruct((cols, rows, units), bf16),
            jax.ShapeDtypeStruct((cols, rows, 2 * units), bf16),
            jax.ShapeDtypeStruct((cols, rows, width), bf16),
            jax.ShapeDtypeStruct((3, rows, width), bf16),
            jax.ShapeDtypeStruct((2, rows, width), bf16),
            jax.ShapeDtypeStruct((2, 3, rows, units), bf16),
        )
        + (lane,) * 4,
        in_specs=[anywhere] * 18,
        out_specs=(anywhere,) * 10,
        scratch_shapes=[
            pltpu.VMEM((width, units), bf16),
            pltpu.VMEM((width, units), bf16),
            pltpu.VMEM((width, units), bf16),
            pltpu.VMEM((cols, rows, width), bf16),
            pltpu.VMEM((2, rows, width), bf16),
            pltpu.VMEM((2, rows, width), bf16),
            pltpu.VMEM((rows, units), bf16),
            pltpu.VMEM((rows, units), bf16),
            pltpu.VMEM((rows, units), bf16),
            pltpu.VMEM((rows, width), bf16),
            pltpu.VMEM((cols - 1, rows, width), bf16),
            pltpu.SemaphoreType.DMA((15,)),
            pltpu.SemaphoreType.DMA((2, cols)),
            pltpu.SemaphoreType.DMA((cols,)),
            pltpu.SemaphoreType.DMA((cols,)),
            pltpu.SemaphoreType.DMA((cols,)),
            pltpu.SemaphoreType.DMA((2,)),
            pltpu.SemaphoreType.DMA((2, 2, 3)),
            pltpu.SemaphoreType.DMA((8,)),
            pltpu.SemaphoreType.DMA((cols,)),
            pltpu.SemaphoreType.DMA((9,)),
        ],
        compiler_params=pltpu.CompilerParams(
            collective_id=2, has_side_effects=True, vmem_limit_bytes=60 << 20
        ),
        cost_estimate=pl.CostEstimate(
            flops=18 * cols * rows * width * units,
            bytes_accessed=800 << 20,
            transcendentals=cols * rows * units,
        ),
        name="feed_forward",
    )(own_input, resid, grad_rows, *weights)


def finish_kernel(
    cols,
    ig_ref,
    gq_ref,
    go_ref,
    gain_ref,
    out_ref,
    gin_ref,
    crossed_ref,
    sq_ref,
    so_ref,
    gsum_ref,
    q_keep,
    q_sib,
    q_a1,
    q_a2,
    q_b1,
    q_b2,
    q_z,
    o_keep,
    o_sib,
    o_a1,
    o_a2,
    o_b1,
    o_b2,
    o_z,
    gain_now,
    gain_in,
    ig_sems,
    gain_sems,
    q_sems,
    o_sems,
    qz_sems,
    oz_sems,
    cross_sems,
    local_sems,
):
    group, core, mate, row, col = place()
    pair = group - core
    high = pair // 2
    sibling = (pair + 1 - core, row, col)
    over_x = (group, 1 - row, col)
    over_y = (2 * (1 - high) + core, row, col)
    width = gin_ref.shape[2]

    def line(step):
        return lax.rem(col + step + cols, cols)

    barrier = pltpu.get_barrier_semaphore()

    def greet(device):
        pl.semaphore_signal(barrier, inc=1, device_id=device, device_id_type=MESH_IDS)

    greet(sibling)
    greet(over_x)
    greet(over_y)
    for step in range(1, cols):
        greet((mate, core, line(step)))
        greet((group, row, line(step)))

    @pl.when(core != row)
    def _():
        greet((mate, core, col))

    pl.semaphore_wait(barrier, 2 * cols + 1 + (core - row) * (core - row))

    def remote(src, dst, sems, at, device):
        return pltpu.make_async_remote_copy(
            src_ref=src,
            dst_ref=dst,
            send_sem=sems.at[0, at],
            recv_sem=sems.at[1, at],
            device_id=device,
            device_id_type=MESH_IDS,
        )

    def lanes(block, size):
        return pl.ds(pl.multiple_of(block * size, size), size)

    matrices = (
        (gq_ref, sq_ref, q_keep, q_sib, q_a1, q_a2, q_b1, q_b2, q_z, q_sems, qz_sems),
        (go_ref, so_ref, o_keep, o_sib, o_a1, o_a2, o_b1, o_b2, o_z, o_sems, oz_sems),
    )

    def moves(m):
        grads, out, keep, sib, a1, a2, b1, b2, zb, sems, z_sems = matrices[m]
        return dict(
            s0=remote(grads.at[:, 1 - core], sib, sems, 0, sibling),
            a1=remote(grads.at[:, core, 1 - row], a1, sems, 1, over_x),
            a2=remote(keep.at[1 - high, row], a2, sems, 2, over_y),
            b1=remote(sib.at[1 - high], b1, sems, 3, over_y),
            b2=remote(sib.at[high, 1 - row], b2, sems, 4, over_x),
            own=pltpu.make_async_copy(grads.at[:, core], keep, local_sems.at[m]),
        )

    copies = (moves(0), moves(1))

    def rows_plus(into, more):
        rows = into.shape[0]
        step = min(32, rows)

        @pl.loop(0, rows // step)
        def _(at):
            here = pl.ds(pl.multiple_of(at * step, step), step)
            into[here, :] = (
                into[here, :].astype(jnp.float32) + more[here, :].astype(jnp.float32)
            ).astype(into.dtype)

    def token_copy(step, at):
        return remote(
            ig_ref.at[:, lanes(line(step), width)],
            gin_ref.at[at],
            ig_sems,
            step,
            (mate, core, line(step)),
        )

    own_tokens = pltpu.make_async_copy(
        ig_ref.at[:, lanes(col, width)], gin_ref.at[col], local_sems.at[2]
    )

    cross = remote(out_ref, crossed_ref, cross_sems, 0, (mate, core, col))
    stay = pltpu.make_async_copy(out_ref, crossed_ref, local_sems.at[4])
    for m in (1, 0):
        copies[m]["s0"].start()
        copies[m]["own"].start()
    copies[1]["a1"].start()
    @pl.when(core == row)
    def _():
        own_tokens.start()
        stay.start()
        for step in range(1, cols):
            token_copy(step, col).start()

    gain_load = pltpu.make_async_copy(gain_ref, gain_now.at[0], local_sems.at[3])
    gain_load.start()
    gain_load.wait()
    near = (
        sibling,
        over_x,
        over_y,
        (group, row, col + 1 - 2 * lax.rem(col, 2)),
        (group, row, lax.rem(col + cols // 2, cols)),
    )

    def gain_round(at):
        exchange = remote(gain_now.at[at], gain_in.at[at], gain_sems, at, near[at])
        exchange.start()
        exchange.wait()
        gain_now[at + 1] = gain_now[at] + gain_in[at]

    def z_moves(m, side, source):
        grads, out, keep, sib, a1, a2, b1, b2, zb, sems, z_sems = matrices[m]
        held = (keep, sib)[side]
        wide = zb.shape[3]
        return [
            pltpu.make_async_remote_copy(
                src_ref=held.at[high, row, :, lanes(line(step), wide)],
                dst_ref=zb.at[side, line(source(step))],
                send_sem=z_sems.at[0, side, step],
                recv_sem=z_sems.at[1, side, step],
                device_id=(group, row, line(step)),
                device_id_type=MESH_IDS,
            )
            for step in range(1, cols)
        ]

    def first_sums(m):
        grads, out, keep, sib, a1, a2, b1, b2, zb, sems, z_sems = matrices[m]
        copies[m]["own"].wait()
        copies[m]["a1"].wait()
        if m == 1:
            copies[0]["a1"].start()
        rows_plus(keep.at[1 - high, row], a1.at[1 - high])
        copies[m]["a2"].start()
        copies[m]["b1"].wait()
        if m == 1:
            copies[0]["b1"].start()
        rows_plus(sib.at[high, 1 - row], b1.at[1 - row])
        copies[m]["b2"].start()

    def last_sums(m):
        grads, out, keep, sib, a1, a2, b1, b2, zb, sems, z_sems = matrices[m]
        rows_plus(keep.at[high, row], a1.at[high])
        rows_plus(sib.at[high, row], b1.at[row])
        for side, last_copy in ((0, "a2"), (1, "b2")):
            copies[m][last_copy].wait()
            rows_plus((keep, sib)[side].at[high, row], (a2, b2)[side])
            for copy in z_moves(m, side, lambda step: 0):
                copy.start()

    copies[1]["s0"].wait()
    copies[1]["b1"].start()
    gain_round(0)
    copies[0]["s0"].wait()
    first_sums(1)
    gain_round(1)
    last_sums(1)
    gain_round(2)
    first_sums(0)

    @pl.when(core != row)
    def _():
        for step in range(cols):
            token_copy(step, col).start()
        cross.start()

    gain_round(3)
    last_sums(0)
    gain_round(4)
    gsum_ref[...] = gain_now[5]
    for m in (1, 0):
        for side in range(2):
            grads, out, keep, sib, a1, a2, b1, b2, zb, sems, z_sems = matrices[m]
            for copy in z_moves(m, side, lambda step: 0):
                copy.wait_send()
            for copy in z_moves(m, side, lambda step: -step):
                copy.wait_recv()
            held = (keep, sib)[side]
            wide = zb.shape[3]
            at_core = core if side == 0 else 1 - core
            rows = zb.shape[2]
            tall = min(32, rows)

            @pl.loop(0, rows // tall)
            def _(at):
                here = pl.ds(pl.multiple_of(at * tall, tall), tall)
                total = held[high, row, here, lanes(col, wide)].astype(jnp.float32)
                for step in range(1, cols):
                    total = total + zb[side, line(-step), here, :].astype(jnp.float32)
                out[at_core, here, :] = total

    for step in range(1, cols):
        token_copy(step, line(-step)).wait_recv()
        token_copy(step, col).wait_send()

    @pl.when(core != row)
    def _():
        token_copy(0, col).wait_recv()
        token_copy(0, col).wait_send()
        cross.wait()

    @pl.when(core == row)
    def _():
        own_tokens.wait()
        stay.wait()


def finish(input_grad, grad_q, grad_o, gains, output, cols):
    anywhere = pl.BlockSpec(memory_space=pl.ANY)
    in_vmem = pl.BlockSpec(memory_space=pltpu.VMEM)
    bf16, f32 = jnp.bfloat16, jnp.float32
    length, full = input_grad.shape
    rows = grad_q.shape[0] // 8

    def buffers(wide):
        return [
            pltpu.VMEM((2, 2, rows, wide), bf16),
            pltpu.VMEM((2, 2, rows, wide), bf16),
            pltpu.VMEM((2, rows, wide), bf16),
            pltpu.VMEM((rows, wide), bf16),
            pltpu.VMEM((2, rows, wide), bf16),
            pltpu.VMEM((rows, wide), bf16),
            pltpu.VMEM((2, cols, rows, wide // cols), bf16),
        ]

    wide_q, wide_o = grad_q.shape[1], grad_o.shape[1]
    return pl.pallas_call(
        functools.partial(finish_kernel, cols),
        out_shape=(
            jax.ShapeDtypeStruct((cols, length, full // cols), bf16),
            jax.ShapeDtypeStruct(output.shape, bf16),
            jax.ShapeDtypeStruct((2, rows, wide_q // cols), f32),
            jax.ShapeDtypeStruct((2, rows, wide_o // cols), f32),
            jax.ShapeDtypeStruct(gains.shape, f32),
        ),
        in_specs=[anywhere] * 5,
        out_specs=(anywhere, anywhere, in_vmem, in_vmem, in_vmem),
        scratch_shapes=buffers(wide_q)
        + buffers(wide_o)
        + [
            pltpu.VMEM((6,) + gains.shape, f32),
            pltpu.VMEM((5,) + gains.shape, f32),
            pltpu.SemaphoreType.DMA((2, cols)),
            pltpu.SemaphoreType.DMA((2, 5)),
            pltpu.SemaphoreType.DMA((2, 5)),
            pltpu.SemaphoreType.DMA((2, 5)),
            pltpu.SemaphoreType.DMA((2, 2, cols)),
            pltpu.SemaphoreType.DMA((2, 2, cols)),
            pltpu.SemaphoreType.DMA((2, 1)),
            pltpu.SemaphoreType.DMA((5,)),
        ],
        compiler_params=pltpu.CompilerParams(
            collective_id=3, has_side_effects=True, vmem_limit_bytes=40 << 20
        ),
        cost_estimate=pl.CostEstimate(flops=0, bytes_accessed=300 << 20, transcendentals=0),
        name="finish",
    )(
        input_grad,
        grad_q.reshape(2, 2, 2, rows, wide_q),
        grad_o.reshape(2, 2, 2, rows, wide_o),
        gains,
        output,
    )


def one_sequence_body(
    tokens,
    cotangent,
    lengths,
    deal_order,
    gain_attn,
    gain_ffn,
    w_query,
    key_value_weight,
    w_out,
    w_gate_up,
    w_down,
):
    seq_group, rows_local, width_local = tokens.shape
    row_count = lax.axis_size("row")
    col_count = lax.axis_size("col")
    full_width = width_local * col_count
    slot_len = rows_local * row_count
    group, core, mate, row, col = place()
    query_half = w_query.shape[1] // 2
    kv_half = key_value_weight.shape[2] // 2
    hidden = w_down.shape[1]

    def core_half(matrix, axis):
        width = matrix.shape[axis] // 2
        return lax.dynamic_slice_in_dim(matrix, core * width, width, axis)

    def joined(mine, other, at):
        return jnp.where(
            at == 0, jnp.concatenate([mine, other]), jnp.concatenate([other, mine])
        )

    def from_sibling(value):
        return lax.ppermute(value, "dp", SIBLINGS)

    def half_rows(matrix):
        return core_half(matrix, 0)

    pack_q = jnp.concatenate(
        [
            core_half(w_query, 1),
            core_half(key_value_weight[:, 0], 1),
            core_half(key_value_weight[:, 1], 1),
        ],
        axis=1,
    )
    pack_o = core_half(w_out, 1)
    gain_one = gain_attn.astype(jnp.float32)
    gain_two = gain_ffn.astype(jnp.float32)
    own_tokens, attn_input = start_exchange(tokens, gain_one, col_count)

    length = lax.dynamic_slice_in_dim(lengths, mate * seq_group + col, 1)
    given_pos = row * rows_local + jnp.arange(rows_local, dtype=jnp.int32)
    given_lengths = lax.dynamic_slice_in_dim(lengths, group * seq_group, seq_group)
    given_live = given_pos[None, :, None] < given_lengths[:, None, None]
    everyone = lax.all_gather(cotangent, "dp", axis=0, tiled=True)
    everyone, attn_input = lax.optimization_barrier((everyone, attn_input))
    picked = pick_sequences(everyone, deal_order, group * seq_group, seq_group)
    picked = jnp.where(given_live, picked, jnp.zeros_like(picked))
    given = lax.ppermute(picked, ("dp", "row"), CROSSED)
    weights_qkv, weights_out = gather_weights(pack_q, pack_o, picked, row_count, col_count)
    given, weights_qkv = lax.optimization_barrier((given, weights_qkv))
    line_cot = lax.all_gather(given, "col", axis=2, tiled=True)
    own_grad = lax.dynamic_index_in_dim(line_cot, col, keepdims=False).astype(jnp.float32)

    w_gate_up, w_down, weights_qkv = lax.optimization_barrier((w_gate_up, w_down, weights_qkv))
    def quarter_rows(matrix):
        count = matrix.shape[0] // 4
        return lax.dynamic_slice_in_dim(matrix, (2 * core + group // 2) * count, count)

    far_gate_up = lax.ppermute(quarter_rows(w_gate_up), "row", OVER_X)
    far_down = lax.ppermute(quarter_rows(w_down), "row", OVER_X)
    own_mats = (w_gate_up[:, 0], w_gate_up[:, 1], w_down)

    cosine_table, sine_table = rope_tables(jnp.arange(slot_len, dtype=jnp.int32), HEAD_SIZE)
    cosine_table, sine_table = lax.optimization_barrier((cosine_table, sine_table))
    cosines = jnp.concatenate(
        [jnp.tile(cosine_table, (1, 6)), jnp.ones((slot_len, HEAD_SIZE), jnp.float32)], axis=1
    )
    turning = jnp.concatenate([-sine_table, sine_table], axis=1)
    sines = jnp.concatenate(
        [jnp.tile(turning, (1, 3)), jnp.zeros((slot_len, HEAD_SIZE), jnp.float32)], axis=1
    )
    own_float = own_tokens.astype(jnp.float32)
    scale_one = lax.rsqrt(jnp.mean(own_float * own_float, axis=1, keepdims=True) + EPSILON)
    projected, heads_out = attend_fast(
        length, attn_input, weights_qkv, cosines, sines, col_count
    )

    def summed_rows(partial):
        count = partial.shape[0] // 2
        mine = lax.dynamic_slice_in_dim(partial, core * count, count)
        other = lax.dynamic_slice_in_dim(partial, (1 - core) * count, count)
        return mine.astype(jnp.float32) + from_sibling(other).astype(jnp.float32)

    attn_rows = summed_rows(expand_local(heads_out, weights_out).astype(jnp.bfloat16))
    resid = own_float + RES_MULT * attn_rows
    scale_two = lax.rsqrt(jnp.mean(resid * resid, axis=1, keepdims=True) + EPSILON)
    own_ffn = (resid * scale_two * gain_two).astype(jnp.bfloat16)

    shared_gate_up = lax.ppermute(far_gate_up, "dp", OVER_Y)
    shared_down = lax.ppermute(far_down, "dp", OVER_Y)
    own_ffn, own_mats, far_gate_up, far_down, shared_gate_up, shared_down = (
        lax.optimization_barrier(
            (own_ffn, own_mats, far_gate_up, far_down, shared_gate_up, shared_down)
        )
    )
    far_mats = (far_gate_up[:, 0], far_gate_up[:, 1], far_down)
    far_mats += (shared_gate_up[:, 0], shared_gate_up[:, 1], shared_down)
    sibling_mats = tuple(from_sibling(matrix) for matrix in far_mats)
    *unused, a_keep, a_send, b_keep, b_send = feed_forward(
        own_ffn,
        resid.astype(jnp.bfloat16),
        line_cot,
        own_mats + far_mats + sibling_mats,
        col_count,
    )
    mlp_part, back_part = unused[2:4]
    grad_normed_two = jnp.sum(back_part.astype(jnp.float32), axis=0)
    out_cols = lax.psum_scatter(mlp_part, "col", scatter_dimension=2, tiled=True)

    def plus(kept, came):
        return (kept.astype(jnp.float32) + came.astype(jnp.float32)).astype(jnp.bfloat16)

    a_came = lax.ppermute(a_send, "row", OVER_X)
    b_came = lax.ppermute(b_send, "dp", OVER_Y)

    weighted_two = grad_normed_two * gain_two
    inner_two = jnp.sum(weighted_two * resid, axis=1, keepdims=True)
    grad_resid = (
        own_grad + scale_two * weighted_two - resid * scale_two**3 * inner_two / full_width
    )
    gain_two_part = jnp.sum(grad_normed_two * resid * scale_two, axis=0)
    own_attn_grad = (RES_MULT * grad_resid).astype(jnp.bfloat16)
    grad_attn = joined(own_attn_grad, from_sibling(own_attn_grad), core)
    grad_heads = contract_local(grad_attn, weights_out).astype(jnp.bfloat16)
    grad_out = token_outer(grad_attn, heads_out).astype(jnp.bfloat16)
    grad_projected = attend_back_fast(
        length, projected, grad_heads, cosines, sines, col_count
    )
    a_sum, b_sum, grad_projected = lax.optimization_barrier(
        (plus(a_keep, a_came), plus(b_keep, b_came), grad_projected)
    )
    high = group // 2

    def one_of(pair, at):
        return lax.dynamic_index_in_dim(pair, at, keepdims=False)

    a_last = lax.ppermute(one_of(a_sum, 1 - high), "dp", OVER_Y)
    b_last = lax.ppermute(one_of(b_sum, 1 - row), "row", OVER_X)
    grad_normed_one = summed_rows(expand_local(grad_projected, weights_qkv).astype(jnp.bfloat16))
    grad_qkv = token_outer(attn_input, grad_projected).astype(jnp.bfloat16)
    weighted_one = grad_normed_one * gain_one
    inner_one = jnp.sum(weighted_one * own_float, axis=1, keepdims=True)
    own_input_grad = (
        grad_resid
        + scale_one * weighted_one
        - own_float * scale_one**3 * inner_one / full_width
    ).astype(jnp.bfloat16)
    gain_one_part = jnp.sum(grad_normed_one * own_float * scale_one, axis=0)
    a_last, b_last, own_input_grad = lax.optimization_barrier((a_last, b_last, own_input_grad))
    gains = jnp.stack([gain_one_part, gain_two_part]).reshape(8, -1)
    given_grad, given_out, sums_q, sums_o, gain_sums = finish(
        own_input_grad, grad_qkv, grad_out, gains, out_cols, col_count
    )
    a_last, b_last, a_sum, b_sum, given_grad = lax.optimization_barrier(
        (a_last, b_last, a_sum, b_sum, given_grad)
    )
    layer_out = jnp.where(given_live, given_out.astype(jnp.float32), 0.0)
    input_grad = given_grad.astype(jnp.float32)
    a_total = one_of(a_sum, high).astype(jnp.float32) + a_last.astype(jnp.float32)
    b_total = one_of(b_sum, row).astype(jnp.float32) + b_last.astype(jnp.float32)
    sums_gate_up = jnp.stack([a_total[:, :hidden], b_total[:, :hidden]], axis=1)
    sums_down = jnp.concatenate([a_total[:, hidden:], b_total[:, hidden:]], axis=1)
    grad_gain_attn, grad_gain_ffn = gain_sums.reshape(2, full_width)

    def both_cores(sums):
        return jnp.concatenate([sums[0], sums[1]], axis=1)

    qk = query_half + kv_half
    out_query = both_cores(sums_q[:, :, :query_half])
    out_kv = jnp.stack(
        [
            both_cores(sums_q[:, :, query_half:qk]),
            both_cores(sums_q[:, :, qk:]),
        ],
        axis=1,
    )
    out_out = both_cores(sums_o)
    return (
        layer_out,
        input_grad,
        out_query,
        out_kv,
        out_out,
        sums_gate_up,
        sums_down,
        grad_gain_attn,
        grad_gain_ffn,
    )


def general_body(
    tokens,
    cotangent,
    lengths,
    deal_order,
    gain_attn,
    gain_ffn,
    w_query,
    key_value_weight,
    w_out,
    w_gate_up,
    w_down,
):
    seq_group, rows_local, width_local = tokens.shape
    row_count = lax.axis_size("row")
    col_count = lax.axis_size("col")
    full_width = width_local * col_count
    slot_len = rows_local * row_count
    total_rows = seq_group * rows_local
    head_size = HEAD_SIZE
    query_width = w_query.shape[1]
    kv_width = key_value_weight.shape[2]
    kv_heads = kv_width // head_size
    group_size = query_width // kv_width
    group_index = lax.axis_index("dp")
    row_index = lax.axis_index("row")
    col_index = lax.axis_index("col")
    matrices = {
        "qkv": jnp.concatenate(
            [w_query, key_value_weight.reshape(key_value_weight.shape[0], 2 * kv_width)], axis=1
        ),
        "out": w_out,
        "gate_up": w_gate_up,
        "down": w_down,
    }

    def contract_with(operand, which_one):
        return contract_rows(operand, matrices[which_one])

    def expand_with(operand, which_one):
        return expand_rows(operand, matrices[which_one])

    own_cotangent = bring_cotangent(cotangent, deal_order, group_index * seq_group)
    own_rows = tokens
    seq_lens = lax.dynamic_slice_in_dim(lengths, group_index * seq_group, seq_group)
    local_pos = row_index * rows_local + jnp.arange(rows_local, dtype=jnp.int32)
    key_pos = jnp.arange(slot_len, dtype=jnp.int32)
    live_rows = (local_pos[None, :] < seq_lens[:, None]).astype(jnp.float32).reshape(total_rows, 1)
    cosine_table, sine_table = rope_tables(jnp.tile(local_pos, seq_group), head_size)
    own_tokens = own_rows.reshape(total_rows, width_local)
    wide_float = widen_cols(own_tokens).astype(jnp.float32)
    scale_one = lax.rsqrt(jnp.mean(wide_float * wide_float, axis=1, keepdims=True) + EPSILON)
    gain_one = gain_attn.astype(jnp.float32)
    first_normed = wide_float * scale_one
    attn_input = (first_normed * gain_one).astype(jnp.bfloat16)
    projected = contract_with(attn_input, "qkv")
    query_lin = projected[:, :query_width].reshape(total_rows, query_width // head_size, head_size)
    key_lin = projected[:, query_width : query_width + kv_width].reshape(
        total_rows, kv_heads, head_size
    )
    value_lin = projected[:, query_width + kv_width :]
    query_rows = rotary_embed(query_lin, cosine_table, sine_table).astype(jnp.bfloat16)
    keys_own = (
        rotary_embed(key_lin, cosine_table, sine_table)
        .astype(jnp.bfloat16)
        .reshape(seq_group, rows_local, kv_width)
    )
    values_own = value_lin.astype(jnp.bfloat16).reshape(seq_group, rows_local, kv_width)
    all_keys, all_values = (
        lax.all_gather(keys_own, "row", axis=1, tiled=True),
        lax.all_gather(values_own, "row", axis=1, tiled=True),
    )
    query_split = query_rows.reshape(seq_group, rows_local, kv_heads, group_size, head_size)
    key_split = all_keys.reshape(seq_group, slot_len, kv_heads, head_size)
    value_split = all_values.reshape(seq_group, slot_len, kv_heads, head_size)

    def forward_seq(inputs):
        return attend(inputs, key_pos, local_pos)

    mixed_heads, row_max, row_sums = lax.map(
        forward_seq, (query_split, key_split, value_split, seq_lens)
    )
    heads_out = mixed_heads.reshape(total_rows, query_width).astype(jnp.bfloat16)
    attn_local = narrow_cols(expand_with(heads_out, "out"))
    resid = own_tokens.astype(jnp.float32) + RES_MULT * attn_local
    gain_two = lax.dynamic_slice_in_dim(
        gain_ffn.astype(jnp.float32), col_index * width_local, width_local
    )
    scale_two = lax.rsqrt(sum_over_cols(jnp.sum(resid * resid, axis=1)) / full_width + EPSILON)[
        :, None
    ]
    normed_two = resid * scale_two
    ffn_input = widen_cols((normed_two * gain_two).astype(jnp.bfloat16))
    gate_up = contract_with(ffn_input, "gate_up")
    gate = gate_up[:, 0]
    upward = gate_up[:, 1]
    sigmoid_gate = jax.nn.sigmoid(gate)
    silu_gate = gate * sigmoid_gate
    hidden = (silu_gate * upward).astype(jnp.bfloat16)
    ffn_local = narrow_cols(expand_with(hidden, "down"))
    layer_out = live_rows * (resid + RES_MULT * ffn_local)
    grad_rows = live_rows * own_cotangent.reshape(total_rows, width_local).astype(jnp.float32)
    grad_ffn = widen_cols((RES_MULT * grad_rows).astype(jnp.bfloat16))
    grad_hidden = contract_with(grad_ffn, "down")
    grad_down = token_outer(grad_ffn, hidden)
    slope = sigmoid_gate * (1.0 + gate * (1.0 - sigmoid_gate))
    grad_gate_rows = jnp.stack(
        [grad_hidden * upward * slope, grad_hidden * silu_gate], axis=1
    ).astype(jnp.bfloat16)
    grad_gate_up = token_outer(ffn_input, grad_gate_rows)
    grad_normed_two = narrow_cols(expand_with(grad_gate_rows, "gate_up"))
    weighted_two = grad_normed_two * gain_two
    inner_two = sum_over_cols(jnp.sum(weighted_two * resid, axis=1))[:, None]
    grad_resid = (
        grad_rows + scale_two * weighted_two - resid * scale_two**3 * inner_two / full_width
    )
    gain_two_part = jnp.sum(grad_normed_two * normed_two, axis=0)
    grad_attn = widen_cols((RES_MULT * grad_resid).astype(jnp.bfloat16))
    grad_heads = contract_with(grad_attn, "out").astype(jnp.bfloat16)
    grad_out = token_outer(grad_attn, heads_out)
    grad_split = grad_heads.reshape(seq_group, rows_local, kv_heads, group_size, head_size)

    def backward_seq(inputs):
        return attend_back(inputs, key_pos, local_pos)

    grad_query, grad_key, grad_value = lax.map(
        backward_seq, (query_split, key_split, value_split, grad_split, row_max, row_sums, seq_lens)
    )
    key_part, value_part = (
        lax.psum_scatter(
            grad_key.reshape(seq_group, slot_len, kv_width).astype(jnp.bfloat16),
            "row",
            scatter_dimension=1,
            tiled=True,
        ).astype(jnp.float32),
        lax.psum_scatter(
            grad_value.reshape(seq_group, slot_len, kv_width).astype(jnp.bfloat16),
            "row",
            scatter_dimension=1,
            tiled=True,
        ).astype(jnp.float32),
    )
    query_back = rotary_embed(
        grad_query.reshape(total_rows, query_width // head_size, head_size),
        cosine_table,
        -sine_table,
    ).reshape(total_rows, query_width)
    key_back = rotary_embed(
        key_part.reshape(total_rows, kv_heads, head_size), cosine_table, -sine_table
    ).reshape(total_rows, kv_width)
    grad_projected = jnp.concatenate(
        [query_back, key_back, value_part.reshape(total_rows, kv_width)], axis=1
    ).astype(jnp.bfloat16)
    grad_qkv = token_outer(attn_input, grad_projected)
    grad_normed_one = expand_with(grad_projected, "qkv")
    weighted_one = grad_normed_one * gain_one
    inner_one = jnp.sum(weighted_one * wide_float, axis=1, keepdims=True)
    input_part = scale_one * weighted_one - wide_float * scale_one**3 * inner_one / full_width
    input_grad = grad_resid + narrow_cols(input_part)
    gain_one_part = jnp.sum(grad_normed_one * first_normed, axis=0)
    gain_two_full = lax.dynamic_update_slice_in_dim(
        jnp.zeros((full_width,), jnp.float32), gain_two_part, col_index * width_local, 0
    )
    grad_gain_attn, grad_gain_ffn = lax.psum((gain_one_part, gain_two_full), ("dp", "row", "col"))
    sums_qkv, sums_out, sums_gate_up, sums_down = (
        lax.psum_scatter(
            grad_qkv.astype(jnp.bfloat16), ("dp", "row"), scatter_dimension=0, tiled=True
        ).astype(jnp.float32),
        lax.psum_scatter(
            grad_out.astype(jnp.bfloat16), ("dp", "row"), scatter_dimension=0, tiled=True
        ).astype(jnp.float32),
        lax.psum_scatter(
            grad_gate_up.astype(jnp.bfloat16), ("dp", "row"), scatter_dimension=0, tiled=True
        ).astype(jnp.float32),
        lax.psum_scatter(
            grad_down.astype(jnp.bfloat16), ("dp", "row"), scatter_dimension=0, tiled=True
        ).astype(jnp.float32),
    )
    out_query = sums_qkv[:, :query_width]
    out_kv = sums_qkv[:, query_width:].reshape(sums_qkv.shape[0], 2, kv_width)
    return (
        layer_out.reshape(seq_group, rows_local, width_local),
        input_grad.reshape(seq_group, rows_local, width_local),
        out_query,
        out_kv,
        sums_out,
        sums_gate_up,
        sums_down,
        grad_gain_attn,
        grad_gain_ffn,
    )


def body(tokens, cotangent, lengths, deal_order, gain_attn, gain_ffn, w_query, key_value_weight, *rest):
    sizes = (lax.axis_size("dp"), lax.axis_size("row"), lax.axis_size("col"))
    one_each = sizes == (4, 2, 4) and tokens.shape[0] == sizes[2]
    pairs = w_query.shape[1] == 8 * HEAD_SIZE and key_value_weight.shape[2] == 2 * HEAD_SIZE
    chosen = one_sequence_body if one_each and pairs else general_body
    return chosen(
        tokens, cotangent, lengths, deal_order, gain_attn, gain_ffn, w_query, key_value_weight, *rest
    )


def solution(mesh):
    placed = (
        P("dp", "row", "col"),
        P("dp", "row", "col"),
        P(),
        P(),
        P(),
        P(),
        P("row", "col"),
        P("row", None, "col"),
        P("row", "col"),
        P("row", None, "col"),
        P("row", "col"),
    )
    return jax.shard_map(
        body,
        mesh=mesh,
        in_specs=placed,
        out_specs=(
            P("dp", "row", "col"),
            P("dp", "row", "col"),
            P(("dp", "row"), "col"),
            P(("dp", "row"), None, "col"),
            P(("dp", "row"), "col"),
            P(("dp", "row"), None, "col"),
            P(("dp", "row"), "col"),
            P(),
            P(),
        ),
        check_vma=False,
    )
```

```python
import functools

import jax
import jax.numpy as jnp
from jax import lax
from jax.experimental import pallas as pl
from jax.experimental.pallas import tpu as pltpu
from jax.sharding import PartitionSpec as P

HEAD_SIZE = 64


EPSILON = 1e-05
THETA = 10000000.0
ATTN_MULT = 0.015625
RES_MULT = 0.22
MASKED = -1e30


def rope_tables(positions, head_size):
    halves = jnp.arange(head_size // 2, dtype=jnp.float32)
    inverse_freq = THETA ** (-(halves * 2.0) / head_size)
    angles = positions.astype(jnp.float32)[:, None] * inverse_freq[None, :]
    return (jnp.cos(angles), jnp.sin(angles))


def rotary_embed(value_rows, cosine_table, sine_table):
    middle = value_rows.shape[-1] // 2
    first_half = value_rows[..., :middle]
    second_half = value_rows[..., middle:]
    cos_part = cosine_table[:, None, :]
    sin_part = sine_table[:, None, :]
    return jnp.concatenate(
        [
            first_half * cos_part - second_half * sin_part,
            second_half * cos_part + first_half * sin_part,
        ],
        axis=-1,
    )


def widen_cols(value_rows):
    return lax.all_gather(value_rows, "col", axis=1, tiled=True)


def narrow_cols(value_rows):
    return lax.psum_scatter(value_rows, "col", scatter_dimension=1, tiled=True)


def sum_over_cols(value_rows):
    return lax.psum(value_rows, "col")


def contract_local(operand, matrix):
    return lax.dot_general(
        operand, matrix, (((1,), (0,)), ((), ())), preferred_element_type=jnp.float32
    )


def expand_local(operand, matrix):
    trailing = tuple(range(1, operand.ndim))
    return lax.dot_general(
        operand, matrix, ((trailing, trailing), ((), ())), preferred_element_type=jnp.float32
    )


def token_outer(features, grads):
    return lax.dot_general(
        features, grads, (((0,), (0,)), ((), ())), preferred_element_type=jnp.float32
    )


def contract_rows(operand, matrix):
    return contract_local(operand, lax.all_gather(matrix, "row", axis=0, tiled=True))


def expand_rows(operand, matrix):
    return expand_local(operand, lax.all_gather(matrix, "row", axis=0, tiled=True))


def split_keys(key_seq, value_seq, key_pos):
    slot_len = key_seq.shape[0]
    width = min(512, slot_len)
    count = slot_len // width
    return (
        key_seq.reshape(count, width, key_seq.shape[1], key_seq.shape[2]),
        value_seq.reshape(count, width, value_seq.shape[1], value_seq.shape[2]),
        key_pos.reshape(count, width),
    )


def block_scores(query_seq, key_block, pos_block, query_pos, length):
    scores = (
        jnp.einsum("qkgd,tkd->kgqt", query_seq, key_block, preferred_element_type=jnp.float32)
        * ATTN_MULT
    )
    allowed = (pos_block[None, :] <= query_pos[:, None]) & (pos_block[None, :] < length)
    return jnp.where(allowed, scores, MASKED)


def attend(inputs, key_pos, query_pos):
    query_seq, key_seq, value_seq, length = inputs
    key_blocks, value_blocks, pos_blocks = split_keys(key_seq, value_seq, key_pos)
    stat_shape = (query_seq.shape[1], query_seq.shape[2], query_seq.shape[0], 1)

    def gather_stats(carry, entry):
        running_max, running_sum = carry
        key_block, pos_block = entry
        scores = block_scores(query_seq, key_block, pos_block, query_pos, length)
        new_max = jnp.maximum(running_max, jnp.max(scores, axis=-1, keepdims=True))
        new_sum = running_sum * jnp.exp(running_max - new_max) + jnp.sum(
            jnp.exp(scores - new_max), axis=-1, keepdims=True
        )
        return ((new_max, new_sum), None)

    start_stats = (jnp.full(stat_shape, MASKED, jnp.float32), jnp.zeros(stat_shape, jnp.float32))
    (row_max, row_sums), unused = lax.scan(gather_stats, start_stats, (key_blocks, pos_blocks))

    def mix_values(running, entry):
        key_block, value_block, pos_block = entry
        scores = block_scores(query_seq, key_block, pos_block, query_pos, length)
        weights = jnp.exp(scores - row_max) / row_sums
        return (
            running
            + jnp.einsum(
                "kgqt,tkd->qkgd",
                weights.astype(jnp.bfloat16),
                value_block,
                preferred_element_type=jnp.float32,
            ),
            None,
        )

    start_mix = jnp.zeros(query_seq.shape, jnp.float32)
    mixed_heads, unused = lax.scan(mix_values, start_mix, (key_blocks, value_blocks, pos_blocks))
    return (mixed_heads, row_max, row_sums)


def attend_back(inputs, key_pos, query_pos):
    query_seq, key_seq, value_seq, grad_mixed, row_max, row_sums, length = inputs
    key_blocks, value_blocks, pos_blocks = split_keys(key_seq, value_seq, key_pos)

    def block_weights(key_block, value_block, pos_block):
        scores = block_scores(query_seq, key_block, pos_block, query_pos, length)
        weights = jnp.exp(scores - row_max) / row_sums
        grad_weights = jnp.einsum(
            "qkgd,tkd->kgqt", grad_mixed, value_block, preferred_element_type=jnp.float32
        )
        return (weights, grad_weights)

    def gather_centre(running, entry):
        weights, grad_weights = block_weights(*entry)
        return (running + jnp.sum(weights * grad_weights, axis=-1, keepdims=True), None)

    start_centre = jnp.zeros(row_max.shape, jnp.float32)
    centre, unused = lax.scan(gather_centre, start_centre, (key_blocks, value_blocks, pos_blocks))

    def grads_block(running, entry):
        key_block = entry[0]
        weights, grad_weights = block_weights(*entry)
        grad_scores = (weights * (grad_weights - centre)).astype(jnp.bfloat16)
        grad_query = (
            running
            + jnp.einsum(
                "kgqt,tkd->qkgd", grad_scores, key_block, preferred_element_type=jnp.float32
            )
            * ATTN_MULT
        )
        grad_key = (
            jnp.einsum("kgqt,qkgd->tkd", grad_scores, query_seq, preferred_element_type=jnp.float32)
            * ATTN_MULT
        )
        grad_value = jnp.einsum(
            "kgqt,qkgd->tkd",
            weights.astype(jnp.bfloat16),
            grad_mixed,
            preferred_element_type=jnp.float32,
        )
        return (grad_query, (grad_key, grad_value))

    start_query = jnp.zeros(query_seq.shape, jnp.float32)
    grad_query, (grad_key, grad_value) = lax.scan(
        grads_block, start_query, (key_blocks, value_blocks, pos_blocks)
    )
    return (grad_query, grad_key.reshape(key_seq.shape), grad_value.reshape(value_seq.shape))


MESH_IDS = pl.DeviceIdType.MESH
SIBLINGS = [(0, 1), (1, 0), (2, 3), (3, 2)]
OVER_X = [(0, 1), (1, 0)]
OVER_Y = [(0, 2), (2, 0), (1, 3), (3, 1)]
CROSSED = [((2 * y + c) * 2 + x, (2 * y + x) * 2 + c) for y in (0, 1) for c in (0, 1) for x in (0, 1)]


def pick_sequences(everyone, deal_order, first, count):
    slots = jnp.arange(deal_order.shape[0], dtype=jnp.int32)
    inverse = jnp.sum(jnp.where(deal_order[None, :] == slots[:, None], slots[None, :], 0), axis=1)
    return jnp.concatenate(
        [
            lax.dynamic_slice_in_dim(
                everyone, lax.dynamic_index_in_dim(inverse, first + at, keepdims=False), 1
            )
            for at in range(count)
        ]
    )


def bring_cotangent(cotangent, deal_order, first):
    everyone = lax.all_gather(cotangent, "dp", axis=0, tiled=True)
    return pick_sequences(everyone, deal_order, first, cotangent.shape[0])


def place():
    group = lax.axis_index("dp")
    core = lax.rem(group, 2)
    row = lax.axis_index("row")
    return group, core, group - core + row, row, lax.axis_index("col")


def lined(index, step, count):
    return lax.rem(index + step + count, count)


def aligned(block, size):
    return pl.ds(pl.multiple_of(block * size, size), size)


def greet(device):
    pl.semaphore_signal(
        pltpu.get_barrier_semaphore(), inc=1, device_id=device, device_id_type=MESH_IDS
    )


def remote(src, dst, sems, at, device):
    return pltpu.make_async_remote_copy(
        src_ref=src,
        dst_ref=dst,
        send_sem=sems.at[0, at],
        recv_sem=sems.at[1, at],
        device_id=device,
        device_id_type=MESH_IDS,
    )


def line_order(col, last, at):
    inner_low = jnp.where(at < 2, 1 - at, at)
    inner_high = jnp.where(at == 3, 0, jnp.where(at == 0, 2, jnp.where(at == 1, 1, 3)))
    return jnp.where(
        col == 0, at, jnp.where(col == last, last - at, jnp.where(col == 1, inner_low, inner_high))
    )


def start_kernel(
    cols, tok_ref, gain_ref, x_ref, a_ref, x_buf, a_buf, tok_sems, a_sems, local_sems
):
    group, core, mate, row, col = place()
    width = tok_ref.shape[2]
    length = x_buf.shape[0]
    sibling = (group + 1 - 2 * core, row, col)

    def line(step):
        return lined(col, step, cols)

    for step in range(1, cols):
        greet((mate, core, line(step)))
    greet(sibling)

    @pl.when(core != row)
    def _():
        greet((mate, core, col))

    pl.semaphore_wait(pltpu.get_barrier_semaphore(), cols + (core - row) * (core - row))

    def token_copy(step, into):
        return remote(
            tok_ref.at[line(step)],
            x_buf.at[:, aligned(into, width)],
            tok_sems,
            step,
            (mate, core, line(step)),
        )

    own_tokens = pltpu.make_async_copy(
        tok_ref.at[col], x_buf.at[:, aligned(col, width)], local_sems.at[0]
    )
    for step in range(1, cols):
        token_copy(step, col).start()

    @pl.when(core != row)
    def _():
        token_copy(0, col).start()

    @pl.when(core == row)
    def _():
        own_tokens.start()

    for step in range(1, cols):
        token_copy(step, line(-step)).wait_recv()

    @pl.when(core != row)
    def _():
        token_copy(0, col).wait_recv()

    @pl.when(core == row)
    def _():
        own_tokens.wait()

    keep_x = pltpu.make_async_copy(x_buf, x_ref, local_sems.at[1])
    keep_x.start()
    tall = min(64, length)

    @pl.loop(0, length // tall)
    def _(at):
        here = aligned(at, tall)
        now = x_buf[here, :].astype(jnp.float32)
        scale = lax.rsqrt(jnp.mean(now * now, axis=1, keepdims=True) + EPSILON)
        a_buf[here, :] = (now * scale * gain_ref[...]).astype(jnp.bfloat16)

    def a_copy(of_core):
        return remote(a_buf, a_ref.at[aligned(of_core, length)], a_sems, 0, sibling)

    own_a = pltpu.make_async_copy(a_buf, a_ref.at[aligned(core, length)], local_sems.at[2])
    a_copy(core).start()
    own_a.start()
    for step in range(1, cols):
        token_copy(step, col).wait_send()

    @pl.when(core != row)
    def _():
        token_copy(0, col).wait_send()

    keep_x.wait()
    own_a.wait()
    a_copy(core).wait_send()
    a_copy(1 - core).wait_recv()


def start_exchange(tokens, gain, cols):
    anywhere = pl.BlockSpec(memory_space=pl.ANY)
    seqs, length, width = tokens.shape
    full = width * cols
    return pl.pallas_call(
        functools.partial(start_kernel, cols),
        out_shape=(
            jax.ShapeDtypeStruct((length, full), tokens.dtype),
            jax.ShapeDtypeStruct((2 * length, full), tokens.dtype),
        ),
        in_specs=[anywhere, pl.BlockSpec(memory_space=pltpu.VMEM)],
        out_specs=(anywhere,) * 2,
        scratch_shapes=[
            pltpu.VMEM((length, full), tokens.dtype),
            pltpu.VMEM((length, full), tokens.dtype),
            pltpu.SemaphoreType.DMA((2, cols)),
            pltpu.SemaphoreType.DMA((2, 1)),
            pltpu.SemaphoreType.DMA((3,)),
        ],
        compiler_params=pltpu.CompilerParams(
            collective_id=1, has_side_effects=True, vmem_limit_bytes=60 << 20
        ),
        cost_estimate=pl.CostEstimate(flops=0, bytes_accessed=200 << 20, transcendentals=0),
        name="start_exchange",
    )(tokens, gain.reshape(1, full))


def gather_kernel(
    cols, q_ref, o_ref, after_ref, wq_ref, wo_ref, q_send, q_recv, q_over, o_send, o_recv, o_over, local_sems
):
    group, core, mate, row, col = place()
    last = cols - 1
    over = (group, 1 - row, col)
    greet(over)

    @pl.when(col < last)
    def _():
        greet((group, row, col + 1))

    @pl.when(col > 0)
    def _():
        greet((group, row, col - 1))

    pl.semaphore_wait(
        pltpu.get_barrier_semaphore(),
        1 + jnp.minimum(col, 1) + jnp.minimum(last - col, 1),
    )

    def moves(own, full, send, recv, over_sems):
        tall, wide = own.shape

        def block(of_row, of_col):
            return full.at[aligned(of_row, tall), aligned(of_col, wide)]

        def along(src, chunk, to, way):
            return pltpu.make_async_remote_copy(
                src_ref=src,
                dst_ref=block(row, chunk),
                send_sem=send.at[way, chunk],
                recv_sem=recv.at[chunk],
                device_id=(group, row, to),
                device_id_type=MESH_IDS,
            )

        def across(src, of_row, chunk):
            return remote(src, block(of_row, chunk), over_sems, chunk, over)

        return block, along, across

    both = (
        (q_ref, moves(q_ref, wq_ref, q_send, q_recv, q_over)),
        (o_ref, moves(o_ref, wo_ref, o_send, o_recv, o_over)),
    )
    own_copies = []
    for at, (own, (block, along, across)) in enumerate(both):

        @pl.when(col < last)
        def _():
            along(own, col, col + 1, 0).start()

        @pl.when(col > 0)
        def _():
            along(own, col, col - 1, 1).start()

        across(own, row, col).start()
        own_copies.append(pltpu.make_async_copy(own, block(row, col), local_sems.at[at]))
        own_copies[-1].start()
    for at in range(1, cols):
        chunk = line_order(col, last, at)
        for own, (block, along, across) in both:
            along(own, chunk, col, 0).wait_recv()

            @pl.when((chunk < col) & (col < last))
            def _():
                along(block(row, chunk), chunk, col + 1, 0).start()

            @pl.when((chunk > col) & (col > 0))
            def _():
                along(block(row, chunk), chunk, col - 1, 1).start()

            across(block(row, chunk), row, chunk).start()
    for copy in own_copies:
        copy.wait()
    for own, (block, along, across) in both:
        for chunk in range(cols):

            @pl.when((col >= chunk) & (col < last))
            def _():
                along(own, chunk, col + 1, 0).wait_send()

            @pl.when((col <= chunk) & (col > 0))
            def _():
                along(own, chunk, col - 1, 1).wait_send()

            across(own, row, chunk).wait_send()
            across(own, 1 - row, chunk).wait_recv()


def gather_weights(own_q, own_o, after, rows, cols):
    anywhere = pl.BlockSpec(memory_space=pl.ANY)

    def whole(own):
        return jax.ShapeDtypeStruct((own.shape[0] * rows, own.shape[1] * cols), own.dtype)

    return pl.pallas_call(
        functools.partial(gather_kernel, cols),
        out_shape=(whole(own_q), whole(own_o)),
        in_specs=[anywhere] * 3,
        out_specs=(anywhere,) * 2,
        scratch_shapes=[
            pltpu.SemaphoreType.DMA((2, cols)),
            pltpu.SemaphoreType.DMA((cols,)),
            pltpu.SemaphoreType.DMA((2, cols)),
        ]
        * 2
        + [pltpu.SemaphoreType.DMA((2,))],
        compiler_params=pltpu.CompilerParams(collective_id=4, has_side_effects=True),
        cost_estimate=pl.CostEstimate(flops=0, bytes_accessed=300 << 20, transcendentals=0),
        name="gather_weights",
    )(own_q, own_o, after)


def half_turn(wide):
    lanes = wide.shape[1]
    half = HEAD_SIZE // 2
    lane = lax.broadcasted_iota(jnp.int32, wide.shape, 1)
    return jnp.where(
        lax.rem(lane, HEAD_SIZE) < half,
        pltpu.roll(wide, lanes - half, 1),
        pltpu.roll(wide, half, 1),
    )


def both_heads(pair):
    lane = lax.broadcasted_iota(jnp.int32, pair.shape, 1)
    turned = pltpu.roll(pair, HEAD_SIZE, 1)
    low = lane < HEAD_SIZE
    return jnp.where(low, pair, turned), jnp.where(low, turned, pair)


def keep_head(pair, side):
    lane = lax.broadcasted_iota(jnp.int32, pair.shape, 1)
    mine = lane < HEAD_SIZE if side == 0 else lane >= HEAD_SIZE
    return jnp.where(mine, pair, jnp.zeros_like(pair))


def dot_nn(a, b):
    return lax.dot_general(a, b, (((1,), (0,)), ((), ())), preferred_element_type=jnp.float32)


def dot_nt(a, b):
    return lax.dot_general(a, b, (((1,), (1,)), ((), ())), preferred_element_type=jnp.float32)


def dot_tn(a, b):
    return lax.dot_general(a, b, (((0,), (0,)), ((), ())), preferred_element_type=jnp.float32)


PAIR = 2 * HEAD_SIZE


def attend_kernel(block, len_ref, a_ref, w_ref, cos_ref, sin_ref, qkv_ref, z_ref, q_all, k_two, v_two):
    rows = a_ref.shape[0]
    heads = q_all.shape[0]
    length = len_ref[0]

    @pl.loop(0, rows // block)
    def _(at):
        here = pl.ds(pl.multiple_of(at * block, block), block)
        lin = dot_nn(a_ref[here, :], w_ref[...])
        for part in range(heads // 2 + 1):
            lanes = slice(part * PAIR, (part + 1) * PAIR)
            now = lin[:, lanes]
            table = slice(0, PAIR) if part < heads // 2 else slice(PAIR, 2 * PAIR)
            now = now * cos_ref[here, table] + half_turn(now) * sin_ref[here, table]
            qkv_ref[here, lanes] = now.astype(jnp.bfloat16)
            if part < heads // 2:
                for side in range(2):
                    q_all[2 * part + side, here, :] = keep_head(now * ATTN_MULT, side).astype(
                        jnp.bfloat16
                    )
            else:
                keys, values = both_heads(now)
                k_two[here, :] = keys.astype(jnp.bfloat16)
                v_two[here, :] = values.astype(jnp.bfloat16)

    for at in range(rows // block):
        here = slice(at * block, (at + 1) * block)
        upto = (at + 1) * block
        row = lax.broadcasted_iota(jnp.int32, (block, upto), 0) + at * block
        key = lax.broadcasted_iota(jnp.int32, (block, upto), 1)
        allowed = key < jnp.minimum(row + 1, length)

        def one_head(head):
            scores = dot_nt(q_all[head, here, :], k_two[:upto, :])
            scores = jnp.where(allowed, scores, MASKED)
            top = jnp.max(scores, axis=1, keepdims=True)
            power = jnp.exp(scores - top)
            total = jnp.sum(power, axis=1, keepdims=True)
            return dot_nn(power.astype(jnp.bfloat16), v_two[:upto, :]) / total

        for pair in range(heads // 2):
            low = one_head(2 * pair)
            high = one_head(2 * pair + 1)
            lane = lax.broadcasted_iota(jnp.int32, low.shape, 1)
            z_ref[here, pair * PAIR : (pair + 1) * PAIR] = jnp.where(
                lane < HEAD_SIZE, low, high
            ).astype(jnp.bfloat16)


def attend_fast(length, inputs, weights, cosines, sines, groups):
    rows, depth = inputs.shape
    wide = weights.shape[1] // groups
    heads = (wide - PAIR) // HEAD_SIZE
    block = min(256, rows)
    return pl.pallas_call(
        functools.partial(attend_kernel, block),
        grid=(groups,),
        out_shape=(
            jax.ShapeDtypeStruct((rows, groups * wide), jnp.bfloat16),
            jax.ShapeDtypeStruct((rows, groups * heads * HEAD_SIZE), jnp.bfloat16),
        ),
        in_specs=[
            pl.BlockSpec(memory_space=pltpu.SMEM),
            pl.BlockSpec((rows, depth), lambda g: (0, 0)),
            pl.BlockSpec((depth, wide), lambda g: (0, g)),
            pl.BlockSpec((rows, 2 * PAIR), lambda g: (0, 0)),
            pl.BlockSpec((rows, 2 * PAIR), lambda g: (0, 0)),
        ],
        out_specs=(
            pl.BlockSpec((rows, wide), lambda g: (0, g)),
            pl.BlockSpec((rows, heads * HEAD_SIZE), lambda g: (0, g)),
        ),
        scratch_shapes=[
            pltpu.VMEM((heads, rows, PAIR), jnp.bfloat16),
            pltpu.VMEM((rows, PAIR), jnp.bfloat16),
            pltpu.VMEM((rows, PAIR), jnp.bfloat16),
        ],
        compiler_params=pltpu.CompilerParams(vmem_limit_bytes=48 << 20),
        cost_estimate=pl.CostEstimate(
            flops=2 * rows * depth * wide * groups + 2 * groups * heads * rows * rows * 128,
            bytes_accessed=2 * (rows * depth + depth * wide * groups + rows * wide * groups),
            transcendentals=groups * heads * rows * rows // 2,
        ),
        name="attend",
    )(length, inputs, weights, cosines, sines)


def attend_back_kernel(
    block, len_ref, qkv_ref, dz_ref, cos_ref, sin_ref, out_ref, q_all, z_all, k_two, v_two, k_acc, v_acc
):
    rows = qkv_ref.shape[0]
    heads = q_all.shape[0]
    length = len_ref[0]

    @pl.loop(0, rows // block)
    def _(at):
        here = pl.ds(pl.multiple_of(at * block, block), block)
        for part in range(heads // 2):
            lanes = slice(part * PAIR, (part + 1) * PAIR)
            queries = qkv_ref[here, lanes].astype(jnp.float32) * ATTN_MULT
            mixed = dz_ref[here, lanes].astype(jnp.float32)
            for side in range(2):
                q_all[2 * part + side, here, :] = keep_head(queries, side).astype(jnp.bfloat16)
                z_all[2 * part + side, here, :] = keep_head(mixed, side).astype(jnp.bfloat16)
        keys, values = both_heads(qkv_ref[here, heads * HEAD_SIZE :].astype(jnp.float32))
        k_two[here, :] = keys.astype(jnp.bfloat16)
        v_two[here, :] = values.astype(jnp.bfloat16)
        k_acc[here, :] = jnp.zeros((block, PAIR), jnp.float32)
        v_acc[here, :] = jnp.zeros((block, PAIR), jnp.float32)

    def turn_back(now, here, table):
        return (now * cos_ref[here, table] - half_turn(now) * sin_ref[here, table]).astype(
            jnp.bfloat16
        )

    for at in range(rows // block):
        here = slice(at * block, (at + 1) * block)
        upto = (at + 1) * block
        key = lax.broadcasted_iota(jnp.int32, (upto, block), 0)
        query = lax.broadcasted_iota(jnp.int32, (upto, block), 1) + at * block
        allowed = key < jnp.minimum(query + 1, length)

        def one_head(head):
            queries, mixed = q_all[head, here, :], z_all[head, here, :]
            scores = jnp.where(allowed, dot_nt(k_two[:upto, :], queries), MASKED)
            power = jnp.exp(scores - jnp.max(scores, axis=0, keepdims=True))
            weights = power * (1.0 / jnp.sum(power, axis=0, keepdims=True))
            back = dot_nt(v_two[:upto, :], mixed)
            centre = jnp.sum(weights * back, axis=0, keepdims=True)
            slope = (weights * (back - centre)).astype(jnp.bfloat16)
            k_acc[:upto, :] += dot_nn(slope, queries)
            v_acc[:upto, :] += dot_nn(weights.astype(jnp.bfloat16), mixed)
            return dot_tn(slope, k_two[:upto, :]) * ATTN_MULT

        for pair in range(heads // 2):
            low = one_head(2 * pair)
            high = one_head(2 * pair + 1)
            lane = lax.broadcasted_iota(jnp.int32, low.shape, 1)
            lanes = slice(pair * PAIR, (pair + 1) * PAIR)
            out_ref[here, lanes] = turn_back(
                jnp.where(lane < HEAD_SIZE, low, high), here, slice(0, PAIR)
            )

    @pl.loop(0, rows // block)
    def _(at):
        here = pl.ds(pl.multiple_of(at * block, block), block)
        keys, values = k_acc[here, :], v_acc[here, :]
        keys = keys + pltpu.roll(keys, HEAD_SIZE, 1)
        values = values + pltpu.roll(values, HEAD_SIZE, 1)
        lane = lax.broadcasted_iota(jnp.int32, keys.shape, 1)
        lanes = slice(heads * HEAD_SIZE, heads * HEAD_SIZE + PAIR)
        out_ref[here, lanes] = turn_back(
            jnp.where(lane < HEAD_SIZE, keys, values), here, slice(PAIR, 2 * PAIR)
        )


def attend_back_fast(length, projected, grad_mixed, cosines, sines, groups):
    rows = projected.shape[0]
    wide = projected.shape[1] // groups
    heads = (wide - PAIR) // HEAD_SIZE
    block = min(256, rows)
    return pl.pallas_call(
        functools.partial(attend_back_kernel, block),
        grid=(groups,),
        out_shape=jax.ShapeDtypeStruct((rows, groups * wide), jnp.bfloat16),
        in_specs=[
            pl.BlockSpec(memory_space=pltpu.SMEM),
            pl.BlockSpec((rows, wide), lambda g: (0, g)),
            pl.BlockSpec((rows, heads * HEAD_SIZE), lambda g: (0, g)),
            pl.BlockSpec((rows, 2 * PAIR), lambda g: (0, 0)),
            pl.BlockSpec((rows, 2 * PAIR), lambda g: (0, 0)),
        ],
        out_specs=pl.BlockSpec((rows, wide), lambda g: (0, g)),
        scratch_shapes=[
            pltpu.VMEM((heads, rows, PAIR), jnp.bfloat16),
            pltpu.VMEM((heads, rows, PAIR), jnp.bfloat16),
            pltpu.VMEM((rows, PAIR), jnp.bfloat16),
            pltpu.VMEM((rows, PAIR), jnp.bfloat16),
            pltpu.VMEM((rows, PAIR), jnp.float32),
            pltpu.VMEM((rows, PAIR), jnp.float32),
        ],
        compiler_params=pltpu.CompilerParams(vmem_limit_bytes=48 << 20),
        cost_estimate=pl.CostEstimate(
            flops=5 * groups * heads * rows * rows * 128,
            bytes_accessed=2 * (2 * rows * wide * groups + rows * heads * HEAD_SIZE * groups),
            transcendentals=groups * heads * rows * rows // 2,
        ),
        name="attend_back",
    )(length, projected, grad_mixed, cosines, sines)


def ffn_kernel(
    cols,
    own_ref,
    resid_ref,
    grad_ref,
    wg_own,
    wu_own,
    wd_own,
    wg_far,
    wu_far,
    wd_far,
    wg_far_y,
    wu_far_y,
    wd_far_y,
    wg_sib,
    wu_sib,
    wd_sib,
    wg_sib_y,
    wu_sib_y,
    wd_sib_y,
    u_all,
    dgu_all,
    mlp_all,
    back_all,
    relay_ref,
    land_ref,
    a_keep,
    a_send,
    b_keep,
    b_send,
    wg,
    wu,
    wd,
    b_all,
    b_turn,
    g_two,
    u_buf,
    dg_buf,
    du_buf,
    mlp_buf,
    back_buf,
    w_sems,
    ag_send,
    ag_recv,
    back_send,
    back_recv,
    relay_recv,
    pair_sems,
    lane_sems,
    tile_sems,
    io_sems,
):
    group, core, mate, row, col = place()
    sibling = (group + 1 - 2 * core, row, col)
    last = cols - 1
    depth = wg_own.shape[0]
    half = depth // 2
    units = wg_own.shape[1]
    rows = own_ref.shape[0]
    tile = units // cols
    beside = col + 1 - 2 * lax.rem(col, 2)
    facing = last - col
    inner = (col > 0) & (col < last)

    for step in range(1, cols):
        greet((group, row, lined(col, step, cols)))
    greet(sibling)
    pl.semaphore_wait(pltpu.get_barrier_semaphore(), cols)

    def pass_on(src, at, to, way):
        return pltpu.make_async_remote_copy(
            src_ref=src,
            dst_ref=b_all.at[at],
            send_sem=ag_send.at[way, at],
            recv_sem=ag_recv.at[at],
            device_id=(group, row, to),
            device_id_type=MESH_IDS,
        )

    @pl.when(col < last)
    def _():
        pass_on(own_ref, col, col + 1, 0).start()

    @pl.when(col > 0)
    def _():
        pass_on(own_ref, col, col - 1, 1).start()

    def order(at):
        return line_order(col, last, at)

    def load_g(at):
        side = lax.rem(at, 2)
        return pltpu.make_async_copy(grad_ref.at[order(at)], g_two.at[side], io_sems.at[6 + side])

    quarter = half // 2
    high = (group - core) // 2

    def rows_at(first, size):
        return pl.ds(pl.multiple_of(first, quarter), size)

    own_copy = pltpu.make_async_copy(own_ref, b_all.at[col], io_sems.at[0])
    own_copy.start()
    load_resid = pltpu.make_async_copy(resid_ref, mlp_buf, io_sems.at[8])
    far = (1 - row) * depth
    loads = []
    for full, mine, pieces in (
        (wg, wg_own, (wg_far, wg_far_y, wg_sib, wg_sib_y)),
        (wu, wu_own, (wu_far, wu_far_y, wu_sib, wu_sib_y)),
        (wd, wd_own, (wd_far, wd_far_y, wd_sib, wd_sib_y)),
    ):
        places = [
            far + of_core * half + of_plane * quarter
            for of_core in (core, 1 - core)
            for of_plane in (high, 1 - high)
        ]
        loads.append(
            pltpu.make_async_copy(
                mine, full.at[rows_at(row * depth, depth)], w_sems.at[len(loads)]
            )
        )
        for piece, first in zip(pieces, places):
            loads.append(
                pltpu.make_async_copy(
                    piece, full.at[rows_at(first, quarter)], w_sems.at[len(loads)]
                )
            )
    for load in loads:
        load.start()
    load_g(0).start()
    load_resid.start()
    own_copy.wait()
    for load in loads:
        load.wait()

    def arrive(chunk):
        pass_on(b_all.at[chunk], chunk, col, 0).wait_recv()

        @pl.when((chunk < col) & (col < last))
        def _():
            pass_on(b_all.at[chunk], chunk, col + 1, 0).start()

        @pl.when((chunk > col) & (col > 0))
        def _():
            pass_on(b_all.at[chunk], chunk, col - 1, 1).start()

    def outputs(chunk):
        return (
            pltpu.make_async_copy(u_buf, u_all.at[chunk], io_sems.at[1]),
            pltpu.make_async_copy(dg_buf, dgu_all.at[chunk, :, 0:units], io_sems.at[2]),
            pltpu.make_async_copy(du_buf, dgu_all.at[chunk, :, units : 2 * units], io_sems.at[3]),
        )

    def mlp_out(chunk):
        return pltpu.make_async_copy(mlp_buf, mlp_all.at[chunk], io_sems.at[4])

    def slot_of(at):
        return lax.rem(at, cols - 1)

    def deliver(slot, to, place_there, at):
        return pltpu.make_async_remote_copy(
            src_ref=back_buf.at[slot],
            dst_ref=back_all.at[place_there],
            send_sem=back_send.at[at],
            recv_sem=back_recv.at[place_there],
            device_id=(group, row, to),
            device_id_type=MESH_IDS,
        )

    def hand_over(slot, to, box, at):
        return pltpu.make_async_remote_copy(
            src_ref=back_buf.at[slot],
            dst_ref=relay_ref.at[box],
            send_sem=back_send.at[at],
            recv_sem=relay_recv.at[box],
            device_id=(group, row, to),
            device_id_type=MESH_IDS,
        )

    own_back = pltpu.make_async_copy(back_buf.at[0], back_all.at[0], io_sems.at[5])
    at_end = jnp.logical_not(inner)

    def one_chunk(at, unused):
        chunk = order(at)
        side = lax.rem(at, 2)

        @pl.when(at_end & (at > 0))
        def _():
            arrive(order(at))

        @pl.when(inner & (at == 1))
        def _():
            arrive(order(1))
            arrive(order(2))

        @pl.when(inner & (at == 3))
        def _():
            arrive(order(3))

        load_g(at).wait()

        @pl.when(at < last)
        def _():
            load_g(at + 1).start()

        @pl.when(at > 0)
        def _():
            for copy in outputs(order(at - 1)):
                copy.wait()

        @pl.loop(0, units // tile)
        def _(step):
            lanes = aligned(step, tile)
            gate = dot_nn(b_all[chunk], wg[:, lanes])
            upward = dot_nn(b_all[chunk], wu[:, lanes])
            back = RES_MULT * dot_nn(g_two[side], wd[:, lanes])
            opened = 1.0 / (1.0 + jnp.exp(-gate))
            silu = gate * opened
            u_buf[:, lanes] = (silu * upward).astype(jnp.bfloat16)
            slope = opened * (1.0 + gate * (1.0 - opened))
            dg_buf[:, lanes] = (back * upward * slope).astype(jnp.bfloat16)
            du_buf[:, lanes] = (back * silu).astype(jnp.bfloat16)

        for copy in outputs(chunk):
            copy.start()

        @pl.when(at > 0)
        def _():
            mlp_out(order(at - 1)).wait()

        @pl.when(at == 0)
        def _():
            load_resid.wait()

        @pl.when(at == last)
        def _():
            own_back.wait()

        @pl.loop(0, 2 * depth // tile)
        def _(step):
            here = aligned(step, tile)
            back = dot_nt(dg_buf[...], wg[here, :]) + dot_nt(du_buf[...], wu[here, :])
            back_buf[slot_of(at), :, here] = back.astype(jnp.bfloat16)
            added = jnp.where(at == 0, mlp_buf[:, here].astype(jnp.float32), 0.0)
            mlp_buf[:, here] = (added + RES_MULT * dot_nt(u_buf[...], wd[here, :])).astype(
                jnp.bfloat16
            )

        mlp_out(chunk).start()

        @pl.when(at == 0)
        def _():
            own_back.start()

        @pl.when(at_end & (at == 1))
        def _():
            deliver(1, beside, 1, 1).start()

        @pl.when(at_end & (at == 2))
        def _():
            hand_over(2, beside, 1, 2).start()

        @pl.when(at_end & (at == 3))
        def _():
            deliver(0, facing, 2, 3).start()

        @pl.when(inner & (at == 3))
        def _():
            hand_over(0, facing, 0, 3).start()

        return unused

    lax.fori_loop(0, cols, one_chunk, 0)
    for copy in outputs(order(last)):
        copy.wait()
    mlp_out(order(last)).wait()

    loads = []
    for chunk in range(cols):
        here = slice(chunk * rows, (chunk + 1) * rows)
        loads += [
            pltpu.make_async_copy(
                dgu_all.at[chunk, :, 0:units], wg.at[here], w_sems.at[chunk]
            ),
            pltpu.make_async_copy(
                dgu_all.at[chunk, :, units : 2 * units], wu.at[here], w_sems.at[cols + chunk]
            ),
            pltpu.make_async_copy(u_all.at[chunk], wd.at[here], w_sems.at[2 * cols + chunk]),
        ]
    for load in loads:
        load.start()

    def relay(box, slot):
        hand_over(slot, facing, box, 3).wait_recv()
        load = pltpu.make_async_copy(relay_ref.at[box], mlp_buf, io_sems.at[4])
        load.start()
        load.wait()
        tall = min(64, rows)

        @pl.loop(0, rows // tall)
        def _(at):
            here = aligned(at, tall)
            back_buf[slot, here, :] = (
                back_buf[slot, here, :].astype(jnp.float32)
                + mlp_buf[here, :].astype(jnp.float32)
            ).astype(jnp.bfloat16)

    buffers = (dg_buf, du_buf, u_buf)

    def to_sibling(at, part):
        return pltpu.make_async_remote_copy(
            src_ref=buffers[part],
            dst_ref=land_ref.at[at, part],
            send_sem=pair_sems.at[0, at, part],
            recv_sem=pair_sems.at[1, at, part],
            device_id=sibling,
            device_id_type=MESH_IDS,
        )

    def landed(at, part):
        return pltpu.make_async_copy(land_ref.at[at, part], buffers[part], io_sems.at[1 + part])

    halfway = units // 2
    small = rows // 2
    mine, others = aligned(row, small), aligned(1 - row, small)

    def x_lane(high):
        return (
            pltpu.make_async_copy(
                dg_buf.at[mine], a_keep.at[high, :, 0:units], lane_sems.at[0]
            ),
            pltpu.make_async_copy(
                dg_buf.at[others], a_send.at[high, :, 0:units], lane_sems.at[1]
            ),
            pltpu.make_async_copy(
                u_buf.at[mine, 0:halfway],
                a_keep.at[high, :, units : units + halfway],
                lane_sems.at[2],
            ),
            pltpu.make_async_copy(
                u_buf.at[others, 0:halfway],
                a_send.at[high, :, units : units + halfway],
                lane_sems.at[3],
            ),
        )

    def y_lane(target):
        copies = []
        for side in range(2):
            here = slice(side * small, (side + 1) * small)
            copies += [
                pltpu.make_async_copy(
                    du_buf.at[here], target.at[side, :, 0:units], lane_sems.at[4 + 2 * side]
                ),
                pltpu.make_async_copy(
                    u_buf.at[here, halfway:units],
                    target.at[side, :, units : units + halfway],
                    lane_sems.at[5 + 2 * side],
                ),
            ]
        return copies

    def put_results(high, act):
        for copy in x_lane(high):
            act(copy)

        @pl.when(high == (group - core) // 2)
        def _():
            for copy in y_lane(b_keep):
                act(copy)

        @pl.when(high != (group - core) // 2)
        def _():
            for copy in y_lane(b_send):
                act(copy)

    def start_it(copy):
        copy.start()

    def wait_for(copy):
        copy.wait()

    def part_of(chunk):
        return slice(chunk * rows, (chunk + 1) * rows)

    def grad_tile(block, chunk):
        return pltpu.make_async_copy(
            grad_ref.at[chunk, :, aligned(block, rows)],
            mlp_buf.at[:, part_of(chunk)],
            tile_sems.at[chunk],
        )

    parts = range(3)

    def block_of(at):
        return 2 * lax.rem(at, 2) + jnp.where(at >= 2, core, 1 - core)

    for chunk in range(cols):
        grad_tile(block_of(0), chunk).start()
    for chunk in range(cols):
        b_turn[0, :, part_of(chunk)] = b_all[chunk, :, aligned(block_of(0), rows)].T
    for chunk in range(cols):
        grad_tile(block_of(0), chunk).wait()
    for chunk in range(cols):
        g_two[0, :, part_of(chunk)] = mlp_buf[:, part_of(chunk)].T
    for load in loads:
        load.wait()

    def one_block(at, unused):
        high = lax.rem(at, 2)
        is_own = at >= 2
        side = lax.rem(at, 2)
        following = block_of(jnp.minimum(at + 1, 3))

        @pl.when(inner & (at == 1))
        def _():
            relay(0, col)
            deliver(col, beside, 1, 1).start()
            relay(1, last - col)
            deliver(last - col, facing, 2, 2).start()

        @pl.when(at < 3)
        def _():
            for chunk in range(cols):
                grad_tile(following, chunk).start()

        @pl.when((at == 1) | (at == 2))
        def _():
            for part in parts:
                to_sibling(at - 1, part).wait_send()

        @pl.when(at == 3)
        def _():
            put_results(0, wait_for)

        @pl.when(is_own)
        def _():
            for part in parts:
                to_sibling(high, part).wait_recv()
                landed(high, part).start()
            for part in parts:
                landed(high, part).wait()

        @pl.when(at < 3)
        def _():
            for chunk in range(cols):
                grad_tile(following, chunk).wait()

        @pl.loop(0, cols)
        def _(step):
            lanes = aligned(step, tile)
            tokens = aligned(step, rows)

            def put(buffer, value):
                other = jnp.where(is_own, buffer[:, lanes].astype(jnp.float32), 0.0)
                buffer[:, lanes] = (other + value).astype(jnp.bfloat16)

            put(dg_buf, dot_nn(b_turn[side], wg[:, lanes]))
            b_turn[1 - side, :, tokens] = b_all[step, :, aligned(following, rows)].T
            put(du_buf, dot_nn(b_turn[side], wu[:, lanes]))
            g_two[1 - side, :, tokens] = mlp_buf[:, tokens].T
            put(u_buf, RES_MULT * dot_nn(g_two[side], wd[:, lanes]))

        @pl.when(jnp.logical_not(is_own))
        def _():
            for part in parts:
                to_sibling(at, part).start()

        @pl.when(is_own)
        def _():
            put_results(high, start_it)

        return unused

    lax.fori_loop(0, 4, one_block, 0)
    put_results(1, wait_for)
    for at in range(1, cols):
        deliver(0, beside, 1, at).wait_send()
    for at in range(1, 3):
        deliver(0, beside, at, at).wait_recv()
    for chunk in range(cols):

        @pl.when((col >= chunk) & (col < last))
        def _():
            pass_on(own_ref, chunk, col + 1, 0).wait_send()

        @pl.when((col <= chunk) & (col > 0))
        def _():
            pass_on(own_ref, chunk, col - 1, 1).wait_send()


def feed_forward(own_input, resid, grad_rows, weights, cols):
    rows, width = own_input.shape
    units = weights[0].shape[1]
    anywhere = pl.BlockSpec(memory_space=pl.ANY)
    bf16 = jnp.bfloat16
    lane = jax.ShapeDtypeStruct((2, rows // 2, units + units // 2), bf16)
    return pl.pallas_call(
        functools.partial(ffn_kernel, cols),
        out_shape=(
            jax.ShapeDtypeStruct((cols, rows, units), bf16),
            jax.ShapeDtypeStruct((cols, rows, 2 * units), bf16),
            jax.ShapeDtypeStruct((cols, rows, width), bf16),
            jax.ShapeDtypeStruct((3, rows, width), bf16),
            jax.ShapeDtypeStruct((2, rows, width), bf16),
            jax.ShapeDtypeStruct((2, 3, rows, units), bf16),
        )
        + (lane,) * 4,
        in_specs=[anywhere] * 18,
        out_specs=(anywhere,) * 10,
        scratch_shapes=[
            pltpu.VMEM((width, units), bf16),
            pltpu.VMEM((width, units), bf16),
            pltpu.VMEM((width, units), bf16),
            pltpu.VMEM((cols, rows, width), bf16),
            pltpu.VMEM((2, rows, width), bf16),
            pltpu.VMEM((2, rows, width), bf16),
            pltpu.VMEM((rows, units), bf16),
            pltpu.VMEM((rows, units), bf16),
            pltpu.VMEM((rows, units), bf16),
            pltpu.VMEM((rows, width), bf16),
            pltpu.VMEM((cols - 1, rows, width), bf16),
            pltpu.SemaphoreType.DMA((15,)),
            pltpu.SemaphoreType.DMA((2, cols)),
            pltpu.SemaphoreType.DMA((cols,)),
            pltpu.SemaphoreType.DMA((cols,)),
            pltpu.SemaphoreType.DMA((cols,)),
            pltpu.SemaphoreType.DMA((2,)),
            pltpu.SemaphoreType.DMA((2, 2, 3)),
            pltpu.SemaphoreType.DMA((8,)),
            pltpu.SemaphoreType.DMA((cols,)),
            pltpu.SemaphoreType.DMA((9,)),
        ],
        compiler_params=pltpu.CompilerParams(
            collective_id=2, has_side_effects=True, vmem_limit_bytes=60 << 20
        ),
        cost_estimate=pl.CostEstimate(
            flops=18 * cols * rows * width * units,
            bytes_accessed=800 << 20,
            transcendentals=cols * rows * units,
        ),
        name="feed_forward",
    )(own_input, resid, grad_rows, *weights)


def finish_kernel(
    cols,
    ig_ref,
    gq_ref,
    go_ref,
    gain_ref,
    out_ref,
    gin_ref,
    crossed_ref,
    sq_ref,
    so_ref,
    gsum_ref,
    q_keep,
    q_sib,
    q_a1,
    q_a2,
    q_b1,
    q_b2,
    q_z,
    o_keep,
    o_sib,
    o_a1,
    o_a2,
    o_b1,
    o_b2,
    o_z,
    gain_now,
    gain_in,
    ig_sems,
    gain_sems,
    q_sems,
    o_sems,
    qz_sems,
    oz_sems,
    cross_sems,
    local_sems,
):
    group, core, mate, row, col = place()
    pair = group - core
    high = pair // 2
    sibling = (pair + 1 - core, row, col)
    over_x = (group, 1 - row, col)
    over_y = (2 * (1 - high) + core, row, col)
    width = gin_ref.shape[2]

    def line(step):
        return lax.rem(col + step + cols, cols)

    barrier = pltpu.get_barrier_semaphore()

    def greet(device):
        pl.semaphore_signal(barrier, inc=1, device_id=device, device_id_type=MESH_IDS)

    greet(sibling)
    greet(over_x)
    greet(over_y)
    for step in range(1, cols):
        greet((mate, core, line(step)))
        greet((group, row, line(step)))

    @pl.when(core != row)
    def _():
        greet((mate, core, col))

    pl.semaphore_wait(barrier, 2 * cols + 1 + (core - row) * (core - row))

    def remote(src, dst, sems, at, device):
        return pltpu.make_async_remote_copy(
            src_ref=src,
            dst_ref=dst,
            send_sem=sems.at[0, at],
            recv_sem=sems.at[1, at],
            device_id=device,
            device_id_type=MESH_IDS,
        )

    def lanes(block, size):
        return pl.ds(pl.multiple_of(block * size, size), size)

    matrices = (
        (gq_ref, sq_ref, q_keep, q_sib, q_a1, q_a2, q_b1, q_b2, q_z, q_sems, qz_sems),
        (go_ref, so_ref, o_keep, o_sib, o_a1, o_a2, o_b1, o_b2, o_z, o_sems, oz_sems),
    )

    def moves(m):
        grads, out, keep, sib, a1, a2, b1, b2, zb, sems, z_sems = matrices[m]
        return dict(
            s0=remote(grads.at[:, 1 - core], sib, sems, 0, sibling),
            a1=remote(grads.at[:, core, 1 - row], a1, sems, 1, over_x),
            a2=remote(keep.at[1 - high, row], a2, sems, 2, over_y),
            b1=remote(sib.at[1 - high], b1, sems, 3, over_y),
            b2=remote(sib.at[high, 1 - row], b2, sems, 4, over_x),
            own=pltpu.make_async_copy(grads.at[:, core], keep, local_sems.at[m]),
        )

    copies = (moves(0), moves(1))

    def rows_plus(into, more):
        rows = into.shape[0]
        step = min(32, rows)

        @pl.loop(0, rows // step)
        def _(at):
            here = pl.ds(pl.multiple_of(at * step, step), step)
            into[here, :] = (
                into[here, :].astype(jnp.float32) + more[here, :].astype(jnp.float32)
            ).astype(into.dtype)

    def token_copy(step, at):
        return remote(
            ig_ref.at[:, lanes(line(step), width)],
            gin_ref.at[at],
            ig_sems,
            step,
            (mate, core, line(step)),
        )

    own_tokens = pltpu.make_async_copy(
        ig_ref.at[:, lanes(col, width)], gin_ref.at[col], local_sems.at[2]
    )

    cross = remote(out_ref, crossed_ref, cross_sems, 0, (mate, core, col))
    stay = pltpu.make_async_copy(out_ref, crossed_ref, local_sems.at[4])
    for m in (1, 0):
        copies[m]["s0"].start()
        copies[m]["own"].start()
    copies[1]["a1"].start()
    @pl.when(core == row)
    def _():
        own_tokens.start()
        stay.start()
        for step in range(1, cols):
            token_copy(step, col).start()

    gain_load = pltpu.make_async_copy(gain_ref, gain_now.at[0], local_sems.at[3])
    gain_load.start()
    gain_load.wait()
    near = (
        sibling,
        over_x,
        over_y,
        (group, row, col + 1 - 2 * lax.rem(col, 2)),
        (group, row, lax.rem(col + cols // 2, cols)),
    )

    def gain_round(at):
        exchange = remote(gain_now.at[at], gain_in.at[at], gain_sems, at, near[at])
        exchange.start()
        exchange.wait()
        gain_now[at + 1] = gain_now[at] + gain_in[at]

    def z_moves(m, side, source):
        grads, out, keep, sib, a1, a2, b1, b2, zb, sems, z_sems = matrices[m]
        held = (keep, sib)[side]
        wide = zb.shape[3]
        return [
            pltpu.make_async_remote_copy(
                src_ref=held.at[high, row, :, lanes(line(step), wide)],
                dst_ref=zb.at[side, line(source(step))],
                send_sem=z_sems.at[0, side, step],
                recv_sem=z_sems.at[1, side, step],
                device_id=(group, row, line(step)),
                device_id_type=MESH_IDS,
            )
            for step in range(1, cols)
        ]

    def first_sums(m):
        grads, out, keep, sib, a1, a2, b1, b2, zb, sems, z_sems = matrices[m]
        copies[m]["own"].wait()
        copies[m]["a1"].wait()
        if m == 1:
            copies[0]["a1"].start()
        rows_plus(keep.at[1 - high, row], a1.at[1 - high])
        copies[m]["a2"].start()
        copies[m]["b1"].wait()
        if m == 1:
            copies[0]["b1"].start()
        rows_plus(sib.at[high, 1 - row], b1.at[1 - row])
        copies[m]["b2"].start()

    def last_sums(m):
        grads, out, keep, sib, a1, a2, b1, b2, zb, sems, z_sems = matrices[m]
        rows_plus(keep.at[high, row], a1.at[high])
        rows_plus(sib.at[high, row], b1.at[row])
        for side, last_copy in ((0, "a2"), (1, "b2")):
            copies[m][last_copy].wait()
            rows_plus((keep, sib)[side].at[high, row], (a2, b2)[side])
            for copy in z_moves(m, side, lambda step: 0):
                copy.start()

    copies[1]["s0"].wait()
    copies[1]["b1"].start()
    gain_round(0)
    copies[0]["s0"].wait()
    first_sums(1)
    gain_round(1)
    last_sums(1)
    gain_round(2)
    first_sums(0)

    @pl.when(core != row)
    def _():
        for step in range(cols):
            token_copy(step, col).start()
        cross.start()

    gain_round(3)
    last_sums(0)
    gain_round(4)
    gsum_ref[...] = gain_now[5]
    for m in (1, 0):
        for side in range(2):
            grads, out, keep, sib, a1, a2, b1, b2, zb, sems, z_sems = matrices[m]
            for copy in z_moves(m, side, lambda step: 0):
                copy.wait_send()
            for copy in z_moves(m, side, lambda step: -step):
                copy.wait_recv()
            held = (keep, sib)[side]
            wide = zb.shape[3]
            at_core = core if side == 0 else 1 - core
            rows = zb.shape[2]
            tall = min(32, rows)

            @pl.loop(0, rows // tall)
            def _(at):
                here = pl.ds(pl.multiple_of(at * tall, tall), tall)
                total = held[high, row, here, lanes(col, wide)].astype(jnp.float32)
                for step in range(1, cols):
                    total = total + zb[side, line(-step), here, :].astype(jnp.float32)
                out[at_core, here, :] = total

    for step in range(1, cols):
        token_copy(step, line(-step)).wait_recv()
        token_copy(step, col).wait_send()

    @pl.when(core != row)
    def _():
        token_copy(0, col).wait_recv()
        token_copy(0, col).wait_send()
        cross.wait()

    @pl.when(core == row)
    def _():
        own_tokens.wait()
        stay.wait()


def finish(input_grad, grad_q, grad_o, gains, output, cols):
    anywhere = pl.BlockSpec(memory_space=pl.ANY)
    in_vmem = pl.BlockSpec(memory_space=pltpu.VMEM)
    bf16, f32 = jnp.bfloat16, jnp.float32
    length, full = input_grad.shape
    rows = grad_q.shape[0] // 8

    def buffers(wide):
        return [
            pltpu.VMEM((2, 2, rows, wide), bf16),
            pltpu.VMEM((2, 2, rows, wide), bf16),
            pltpu.VMEM((2, rows, wide), bf16),
            pltpu.VMEM((rows, wide), bf16),
            pltpu.VMEM((2, rows, wide), bf16),
            pltpu.VMEM((rows, wide), bf16),
            pltpu.VMEM((2, cols, rows, wide // cols), bf16),
        ]

    wide_q, wide_o = grad_q.shape[1], grad_o.shape[1]
    return pl.pallas_call(
        functools.partial(finish_kernel, cols),
        out_shape=(
            jax.ShapeDtypeStruct((cols, length, full // cols), bf16),
            jax.ShapeDtypeStruct(output.shape, bf16),
            jax.ShapeDtypeStruct((2, rows, wide_q // cols), f32),
            jax.ShapeDtypeStruct((2, rows, wide_o // cols), f32),
            jax.ShapeDtypeStruct(gains.shape, f32),
        ),
        in_specs=[anywhere] * 5,
        out_specs=(anywhere, anywhere, in_vmem, in_vmem, in_vmem),
        scratch_shapes=buffers(wide_q)
        + buffers(wide_o)
        + [
            pltpu.VMEM((6,) + gains.shape, f32),
            pltpu.VMEM((5,) + gains.shape, f32),
            pltpu.SemaphoreType.DMA((2, cols)),
            pltpu.SemaphoreType.DMA((2, 5)),
            pltpu.SemaphoreType.DMA((2, 5)),
            pltpu.SemaphoreType.DMA((2, 5)),
            pltpu.SemaphoreType.DMA((2, 2, cols)),
            pltpu.SemaphoreType.DMA((2, 2, cols)),
            pltpu.SemaphoreType.DMA((2, 1)),
            pltpu.SemaphoreType.DMA((5,)),
        ],
        compiler_params=pltpu.CompilerParams(
            collective_id=3, has_side_effects=True, vmem_limit_bytes=60 << 20
        ),
        cost_estimate=pl.CostEstimate(flops=0, bytes_accessed=300 << 20, transcendentals=0),
        name="finish",
    )(
        input_grad,
        grad_q.reshape(2, 2, 2, rows, wide_q),
        grad_o.reshape(2, 2, 2, rows, wide_o),
        gains,
        output,
    )


def one_sequence_body(
    tokens,
    cotangent,
    lengths,
    deal_order,
    gain_attn,
    gain_ffn,
    w_query,
    key_value_weight,
    w_out,
    w_gate_up,
    w_down,
):
    seq_group, rows_local, width_local = tokens.shape
    row_count = lax.axis_size("row")
    col_count = lax.axis_size("col")
    full_width = width_local * col_count
    slot_len = rows_local * row_count
    group, core, mate, row, col = place()
    query_half = w_query.shape[1] // 2
    kv_half = key_value_weight.shape[2] // 2
    hidden = w_down.shape[1]

    def core_half(matrix, axis):
        width = matrix.shape[axis] // 2
        return lax.dynamic_slice_in_dim(matrix, core * width, width, axis)

    def joined(mine, other, at):
        return jnp.where(
            at == 0, jnp.concatenate([mine, other]), jnp.concatenate([other, mine])
        )

    def from_sibling(value):
        return lax.ppermute(value, "dp", SIBLINGS)

    def half_rows(matrix):
        return core_half(matrix, 0)

    pack_q = jnp.concatenate(
        [
            core_half(w_query, 1),
            core_half(key_value_weight[:, 0], 1),
            core_half(key_value_weight[:, 1], 1),
        ],
        axis=1,
    )
    pack_o = core_half(w_out, 1)
    gain_one = gain_attn.astype(jnp.float32)
    gain_two = gain_ffn.astype(jnp.float32)
    own_tokens, attn_input = start_exchange(tokens, gain_one, col_count)

    length = lax.dynamic_slice_in_dim(lengths, mate * seq_group + col, 1)
    given_pos = row * rows_local + jnp.arange(rows_local, dtype=jnp.int32)
    given_lengths = lax.dynamic_slice_in_dim(lengths, group * seq_group, seq_group)
    given_live = given_pos[None, :, None] < given_lengths[:, None, None]
    everyone = lax.all_gather(cotangent, "dp", axis=0, tiled=True)
    everyone, attn_input = lax.optimization_barrier((everyone, attn_input))
    picked = pick_sequences(everyone, deal_order, group * seq_group, seq_group)
    picked = jnp.where(given_live, picked, jnp.zeros_like(picked))
    given = lax.ppermute(picked, ("dp", "row"), CROSSED)
    weights_qkv, weights_out = gather_weights(pack_q, pack_o, picked, row_count, col_count)
    given, weights_qkv = lax.optimization_barrier((given, weights_qkv))
    line_cot = lax.all_gather(given, "col", axis=2, tiled=True)
    own_grad = lax.dynamic_index_in_dim(line_cot, col, keepdims=False).astype(jnp.float32)

    w_gate_up, w_down, weights_qkv = lax.optimization_barrier((w_gate_up, w_down, weights_qkv))
    def quarter_rows(matrix):
        count = matrix.shape[0] // 4
        return lax.dynamic_slice_in_dim(matrix, (2 * core + group // 2) * count, count)

    far_gate_up = lax.ppermute(quarter_rows(w_gate_up), "row", OVER_X)
    far_down = lax.ppermute(quarter_rows(w_down), "row", OVER_X)
    own_mats = (w_gate_up[:, 0], w_gate_up[:, 1], w_down)

    cosine_table, sine_table = rope_tables(jnp.arange(slot_len, dtype=jnp.int32), HEAD_SIZE)
    cosine_table, sine_table = lax.optimization_barrier((cosine_table, sine_table))
    cosines = jnp.concatenate(
        [jnp.tile(cosine_table, (1, 6)), jnp.ones((slot_len, HEAD_SIZE), jnp.float32)], axis=1
    )
    turning = jnp.concatenate([-sine_table, sine_table], axis=1)
    sines = jnp.concatenate(
        [jnp.tile(turning, (1, 3)), jnp.zeros((slot_len, HEAD_SIZE), jnp.float32)], axis=1
    )
    own_float = own_tokens.astype(jnp.float32)
    scale_one = lax.rsqrt(jnp.mean(own_float * own_float, axis=1, keepdims=True) + EPSILON)
    projected, heads_out = attend_fast(
        length, attn_input, weights_qkv, cosines, sines, col_count
    )

    def summed_rows(partial):
        count = partial.shape[0] // 2
        mine = lax.dynamic_slice_in_dim(partial, core * count, count)
        other = lax.dynamic_slice_in_dim(partial, (1 - core) * count, count)
        return mine.astype(jnp.float32) + from_sibling(other).astype(jnp.float32)

    attn_rows = summed_rows(expand_local(heads_out, weights_out).astype(jnp.bfloat16))
    resid = own_float + RES_MULT * attn_rows
    scale_two = lax.rsqrt(jnp.mean(resid * resid, axis=1, keepdims=True) + EPSILON)
    own_ffn = (resid * scale_two * gain_two).astype(jnp.bfloat16)

    shared_gate_up = lax.ppermute(far_gate_up, "dp", OVER_Y)
    shared_down = lax.ppermute(far_down, "dp", OVER_Y)
    own_ffn, own_mats, far_gate_up, far_down, shared_gate_up, shared_down = (
        lax.optimization_barrier(
            (own_ffn, own_mats, far_gate_up, far_down, shared_gate_up, shared_down)
        )
    )
    far_mats = (far_gate_up[:, 0], far_gate_up[:, 1], far_down)
    far_mats += (shared_gate_up[:, 0], shared_gate_up[:, 1], shared_down)
    sibling_mats = tuple(from_sibling(matrix) for matrix in far_mats)
    *unused, a_keep, a_send, b_keep, b_send = feed_forward(
        own_ffn,
        resid.astype(jnp.bfloat16),
        line_cot,
        own_mats + far_mats + sibling_mats,
        col_count,
    )
    mlp_part, back_part = unused[2:4]
    grad_normed_two = jnp.sum(back_part.astype(jnp.float32), axis=0)
    out_cols = lax.psum_scatter(mlp_part, "col", scatter_dimension=2, tiled=True)

    def plus(kept, came):
        return (kept.astype(jnp.float32) + came.astype(jnp.float32)).astype(jnp.bfloat16)

    a_came = lax.ppermute(a_send, "row", OVER_X)
    b_came = lax.ppermute(b_send, "dp", OVER_Y)

    weighted_two = grad_normed_two * gain_two
    inner_two = jnp.sum(weighted_two * resid, axis=1, keepdims=True)
    grad_resid = (
        own_grad + scale_two * weighted_two - resid * scale_two**3 * inner_two / full_width
    )
    gain_two_part = jnp.sum(grad_normed_two * resid * scale_two, axis=0)
    own_attn_grad = (RES_MULT * grad_resid).astype(jnp.bfloat16)
    grad_attn = joined(own_attn_grad, from_sibling(own_attn_grad), core)
    grad_heads = contract_local(grad_attn, weights_out).astype(jnp.bfloat16)
    grad_projected = attend_back_fast(
        length, projected, grad_heads, cosines, sines, col_count
    )
    a_sum, b_sum, grad_projected = lax.optimization_barrier(
        (plus(a_keep, a_came), plus(b_keep, b_came), grad_projected)
    )
    high = group // 2

    def one_of(pair, at):
        return lax.dynamic_index_in_dim(pair, at, keepdims=False)

    a_last = lax.ppermute(one_of(a_sum, 1 - high), "dp", OVER_Y)
    b_last = lax.ppermute(one_of(b_sum, 1 - row), "row", OVER_X)
    input_partial = expand_local(grad_projected, weights_qkv).astype(jnp.bfloat16)
    grad_attn, heads_out, input_partial = lax.optimization_barrier(
        (grad_attn, heads_out, input_partial)
    )
    grad_out = token_outer(grad_attn, heads_out).astype(jnp.bfloat16)
    grad_normed_one = summed_rows(input_partial)
    attn_input, grad_normed_one = lax.optimization_barrier((attn_input, grad_normed_one))
    grad_qkv = token_outer(attn_input, grad_projected).astype(jnp.bfloat16)
    weighted_one = grad_normed_one * gain_one
    inner_one = jnp.sum(weighted_one * own_float, axis=1, keepdims=True)
    own_input_grad = (
        grad_resid
        + scale_one * weighted_one
        - own_float * scale_one**3 * inner_one / full_width
    ).astype(jnp.bfloat16)
    gain_one_part = jnp.sum(grad_normed_one * own_float * scale_one, axis=0)
    a_total = one_of(a_sum, high).astype(jnp.float32) + a_last.astype(jnp.float32)
    b_total = one_of(b_sum, row).astype(jnp.float32) + b_last.astype(jnp.float32)
    sums_gate_up = jnp.stack([a_total[:, :hidden], b_total[:, :hidden]], axis=1)
    sums_down = jnp.concatenate([a_total[:, hidden:], b_total[:, hidden:]], axis=1)
    sums_gate_up, sums_down, own_input_grad = lax.optimization_barrier(
        (sums_gate_up, sums_down, own_input_grad)
    )
    gains = jnp.stack([gain_one_part, gain_two_part]).reshape(8, -1)
    given_grad, given_out, sums_q, sums_o, gain_sums = finish(
        own_input_grad, grad_qkv, grad_out, gains, out_cols, col_count
    )
    layer_out = jnp.where(given_live, given_out.astype(jnp.float32), 0.0)
    input_grad = given_grad.astype(jnp.float32)
    grad_gain_attn, grad_gain_ffn = gain_sums.reshape(2, full_width)

    def both_cores(sums):
        return jnp.concatenate([sums[0], sums[1]], axis=1)

    qk = query_half + kv_half
    out_query = both_cores(sums_q[:, :, :query_half])
    out_kv = jnp.stack(
        [
            both_cores(sums_q[:, :, query_half:qk]),
            both_cores(sums_q[:, :, qk:]),
        ],
        axis=1,
    )
    out_out = both_cores(sums_o)
    return (
        layer_out,
        input_grad,
        out_query,
        out_kv,
        out_out,
        sums_gate_up,
        sums_down,
        grad_gain_attn,
        grad_gain_ffn,
    )


def general_body(
    tokens,
    cotangent,
    lengths,
    deal_order,
    gain_attn,
    gain_ffn,
    w_query,
    key_value_weight,
    w_out,
    w_gate_up,
    w_down,
):
    seq_group, rows_local, width_local = tokens.shape
    row_count = lax.axis_size("row")
    col_count = lax.axis_size("col")
    full_width = width_local * col_count
    slot_len = rows_local * row_count
    total_rows = seq_group * rows_local
    head_size = HEAD_SIZE
    query_width = w_query.shape[1]
    kv_width = key_value_weight.shape[2]
    kv_heads = kv_width // head_size
    group_size = query_width // kv_width
    group_index = lax.axis_index("dp")
    row_index = lax.axis_index("row")
    col_index = lax.axis_index("col")
    matrices = {
        "qkv": jnp.concatenate(
            [w_query, key_value_weight.reshape(key_value_weight.shape[0], 2 * kv_width)], axis=1
        ),
        "out": w_out,
        "gate_up": w_gate_up,
        "down": w_down,
    }

    def contract_with(operand, which_one):
        return contract_rows(operand, matrices[which_one])

    def expand_with(operand, which_one):
        return expand_rows(operand, matrices[which_one])

    own_cotangent = bring_cotangent(cotangent, deal_order, group_index * seq_group)
    own_rows = tokens
    seq_lens = lax.dynamic_slice_in_dim(lengths, group_index * seq_group, seq_group)
    local_pos = row_index * rows_local + jnp.arange(rows_local, dtype=jnp.int32)
    key_pos = jnp.arange(slot_len, dtype=jnp.int32)
    live_rows = (local_pos[None, :] < seq_lens[:, None]).astype(jnp.float32).reshape(total_rows, 1)
    cosine_table, sine_table = rope_tables(jnp.tile(local_pos, seq_group), head_size)
    own_tokens = own_rows.reshape(total_rows, width_local)
    wide_float = widen_cols(own_tokens).astype(jnp.float32)
    scale_one = lax.rsqrt(jnp.mean(wide_float * wide_float, axis=1, keepdims=True) + EPSILON)
    gain_one = gain_attn.astype(jnp.float32)
    first_normed = wide_float * scale_one
    attn_input = (first_normed * gain_one).astype(jnp.bfloat16)
    projected = contract_with(attn_input, "qkv")
    query_lin = projected[:, :query_width].reshape(total_rows, query_width // head_size, head_size)
    key_lin = projected[:, query_width : query_width + kv_width].reshape(
        total_rows, kv_heads, head_size
    )
    value_lin = projected[:, query_width + kv_width :]
    query_rows = rotary_embed(query_lin, cosine_table, sine_table).astype(jnp.bfloat16)
    keys_own = (
        rotary_embed(key_lin, cosine_table, sine_table)
        .astype(jnp.bfloat16)
        .reshape(seq_group, rows_local, kv_width)
    )
    values_own = value_lin.astype(jnp.bfloat16).reshape(seq_group, rows_local, kv_width)
    all_keys, all_values = (
        lax.all_gather(keys_own, "row", axis=1, tiled=True),
        lax.all_gather(values_own, "row", axis=1, tiled=True),
    )
    query_split = query_rows.reshape(seq_group, rows_local, kv_heads, group_size, head_size)
    key_split = all_keys.reshape(seq_group, slot_len, kv_heads, head_size)
    value_split = all_values.reshape(seq_group, slot_len, kv_heads, head_size)

    def forward_seq(inputs):
        return attend(inputs, key_pos, local_pos)

    mixed_heads, row_max, row_sums = lax.map(
        forward_seq, (query_split, key_split, value_split, seq_lens)
    )
    heads_out = mixed_heads.reshape(total_rows, query_width).astype(jnp.bfloat16)
    attn_local = narrow_cols(expand_with(heads_out, "out"))
    resid = own_tokens.astype(jnp.float32) + RES_MULT * attn_local
    gain_two = lax.dynamic_slice_in_dim(
        gain_ffn.astype(jnp.float32), col_index * width_local, width_local
    )
    scale_two = lax.rsqrt(sum_over_cols(jnp.sum(resid * resid, axis=1)) / full_width + EPSILON)[
        :, None
    ]
    normed_two = resid * scale_two
    ffn_input = widen_cols((normed_two * gain_two).astype(jnp.bfloat16))
    gate_up = contract_with(ffn_input, "gate_up")
    gate = gate_up[:, 0]
    upward = gate_up[:, 1]
    sigmoid_gate = jax.nn.sigmoid(gate)
    silu_gate = gate * sigmoid_gate
    hidden = (silu_gate * upward).astype(jnp.bfloat16)
    ffn_local = narrow_cols(expand_with(hidden, "down"))
    layer_out = live_rows * (resid + RES_MULT * ffn_local)
    grad_rows = live_rows * own_cotangent.reshape(total_rows, width_local).astype(jnp.float32)
    grad_ffn = widen_cols((RES_MULT * grad_rows).astype(jnp.bfloat16))
    grad_hidden = contract_with(grad_ffn, "down")
    grad_down = token_outer(grad_ffn, hidden)
    slope = sigmoid_gate * (1.0 + gate * (1.0 - sigmoid_gate))
    grad_gate_rows = jnp.stack(
        [grad_hidden * upward * slope, grad_hidden * silu_gate], axis=1
    ).astype(jnp.bfloat16)
    grad_gate_up = token_outer(ffn_input, grad_gate_rows)
    grad_normed_two = narrow_cols(expand_with(grad_gate_rows, "gate_up"))
    weighted_two = grad_normed_two * gain_two
    inner_two = sum_over_cols(jnp.sum(weighted_two * resid, axis=1))[:, None]
    grad_resid = (
        grad_rows + scale_two * weighted_two - resid * scale_two**3 * inner_two / full_width
    )
    gain_two_part = jnp.sum(grad_normed_two * normed_two, axis=0)
    grad_attn = widen_cols((RES_MULT * grad_resid).astype(jnp.bfloat16))
    grad_heads = contract_with(grad_attn, "out").astype(jnp.bfloat16)
    grad_out = token_outer(grad_attn, heads_out)
    grad_split = grad_heads.reshape(seq_group, rows_local, kv_heads, group_size, head_size)

    def backward_seq(inputs):
        return attend_back(inputs, key_pos, local_pos)

    grad_query, grad_key, grad_value = lax.map(
        backward_seq, (query_split, key_split, value_split, grad_split, row_max, row_sums, seq_lens)
    )
    key_part, value_part = (
        lax.psum_scatter(
            grad_key.reshape(seq_group, slot_len, kv_width).astype(jnp.bfloat16),
            "row",
            scatter_dimension=1,
            tiled=True,
        ).astype(jnp.float32),
        lax.psum_scatter(
            grad_value.reshape(seq_group, slot_len, kv_width).astype(jnp.bfloat16),
            "row",
            scatter_dimension=1,
            tiled=True,
        ).astype(jnp.float32),
    )
    query_back = rotary_embed(
        grad_query.reshape(total_rows, query_width // head_size, head_size),
        cosine_table,
        -sine_table,
    ).reshape(total_rows, query_width)
    key_back = rotary_embed(
        key_part.reshape(total_rows, kv_heads, head_size), cosine_table, -sine_table
    ).reshape(total_rows, kv_width)
    grad_projected = jnp.concatenate(
        [query_back, key_back, value_part.reshape(total_rows, kv_width)], axis=1
    ).astype(jnp.bfloat16)
    grad_qkv = token_outer(attn_input, grad_projected)
    grad_normed_one = expand_with(grad_projected, "qkv")
    weighted_one = grad_normed_one * gain_one
    inner_one = jnp.sum(weighted_one * wide_float, axis=1, keepdims=True)
    input_part = scale_one * weighted_one - wide_float * scale_one**3 * inner_one / full_width
    input_grad = grad_resid + narrow_cols(input_part)
    gain_one_part = jnp.sum(grad_normed_one * first_normed, axis=0)
    gain_two_full = lax.dynamic_update_slice_in_dim(
        jnp.zeros((full_width,), jnp.float32), gain_two_part, col_index * width_local, 0
    )
    grad_gain_attn, grad_gain_ffn = lax.psum((gain_one_part, gain_two_full), ("dp", "row", "col"))
    sums_qkv, sums_out, sums_gate_up, sums_down = (
        lax.psum_scatter(
            grad_qkv.astype(jnp.bfloat16), ("dp", "row"), scatter_dimension=0, tiled=True
        ).astype(jnp.float32),
        lax.psum_scatter(
            grad_out.astype(jnp.bfloat16), ("dp", "row"), scatter_dimension=0, tiled=True
        ).astype(jnp.float32),
        lax.psum_scatter(
            grad_gate_up.astype(jnp.bfloat16), ("dp", "row"), scatter_dimension=0, tiled=True
        ).astype(jnp.float32),
        lax.psum_scatter(
            grad_down.astype(jnp.bfloat16), ("dp", "row"), scatter_dimension=0, tiled=True
        ).astype(jnp.float32),
    )
    out_query = sums_qkv[:, :query_width]
    out_kv = sums_qkv[:, query_width:].reshape(sums_qkv.shape[0], 2, kv_width)
    return (
        layer_out.reshape(seq_group, rows_local, width_local),
        input_grad.reshape(seq_group, rows_local, width_local),
        out_query,
        out_kv,
        sums_out,
        sums_gate_up,
        sums_down,
        grad_gain_attn,
        grad_gain_ffn,
    )


def body(tokens, cotangent, lengths, deal_order, gain_attn, gain_ffn, w_query, key_value_weight, *rest):
    sizes = (lax.axis_size("dp"), lax.axis_size("row"), lax.axis_size("col"))
    one_each = sizes == (4, 2, 4) and tokens.shape[0] == sizes[2]
    pairs = w_query.shape[1] == 8 * HEAD_SIZE and key_value_weight.shape[2] == 2 * HEAD_SIZE
    chosen = one_sequence_body if one_each and pairs else general_body
    return chosen(
        tokens, cotangent, lengths, deal_order, gain_attn, gain_ffn, w_query, key_value_weight, *rest
    )


def solution(mesh):
    placed = (
        P("dp", "row", "col"),
        P("dp", "row", "col"),
        P(),
        P(),
        P(),
        P(),
        P("row", "col"),
        P("row", None, "col"),
        P("row", "col"),
        P("row", None, "col"),
        P("row", "col"),
    )
    return jax.shard_map(
        body,
        mesh=mesh,
        in_specs=placed,
        out_specs=(
            P("dp", "row", "col"),
            P("dp", "row", "col"),
            P(("dp", "row"), "col"),
            P(("dp", "row"), None, "col"),
            P(("dp", "row"), "col"),
            P(("dp", "row"), None, "col"),
            P(("dp", "row"), "col"),
            P(),
            P(),
        ),
        check_vma=False,
    )
```

```python
import functools

import jax
import jax.numpy as jnp
from jax import lax
from jax.experimental import pallas as pl
from jax.experimental.pallas import tpu as pltpu
from jax.sharding import PartitionSpec as P

HEAD_SIZE = 64


EPSILON = 1e-05
THETA = 10000000.0
ATTN_MULT = 0.015625
RES_MULT = 0.22
MASKED = -1e30


def rope_tables(positions, head_size):
    halves = jnp.arange(head_size // 2, dtype=jnp.float32)
    inverse_freq = THETA ** (-(halves * 2.0) / head_size)
    angles = positions.astype(jnp.float32)[:, None] * inverse_freq[None, :]
    return (jnp.cos(angles), jnp.sin(angles))


def rotary_embed(value_rows, cosine_table, sine_table):
    middle = value_rows.shape[-1] // 2
    first_half = value_rows[..., :middle]
    second_half = value_rows[..., middle:]
    cos_part = cosine_table[:, None, :]
    sin_part = sine_table[:, None, :]
    return jnp.concatenate(
        [
            first_half * cos_part - second_half * sin_part,
            second_half * cos_part + first_half * sin_part,
        ],
        axis=-1,
    )


def widen_cols(value_rows):
    return lax.all_gather(value_rows, "col", axis=1, tiled=True)


def narrow_cols(value_rows):
    return lax.psum_scatter(value_rows, "col", scatter_dimension=1, tiled=True)


def sum_over_cols(value_rows):
    return lax.psum(value_rows, "col")


def contract_local(operand, matrix):
    return lax.dot_general(
        operand, matrix, (((1,), (0,)), ((), ())), preferred_element_type=jnp.float32
    )


def expand_local(operand, matrix):
    trailing = tuple(range(1, operand.ndim))
    return lax.dot_general(
        operand, matrix, ((trailing, trailing), ((), ())), preferred_element_type=jnp.float32
    )


def token_outer(features, grads):
    return lax.dot_general(
        features, grads, (((0,), (0,)), ((), ())), preferred_element_type=jnp.float32
    )


def contract_rows(operand, matrix):
    return contract_local(operand, lax.all_gather(matrix, "row", axis=0, tiled=True))


def expand_rows(operand, matrix):
    return expand_local(operand, lax.all_gather(matrix, "row", axis=0, tiled=True))


def split_keys(key_seq, value_seq, key_pos):
    slot_len = key_seq.shape[0]
    width = min(512, slot_len)
    count = slot_len // width
    return (
        key_seq.reshape(count, width, key_seq.shape[1], key_seq.shape[2]),
        value_seq.reshape(count, width, value_seq.shape[1], value_seq.shape[2]),
        key_pos.reshape(count, width),
    )


def block_scores(query_seq, key_block, pos_block, query_pos, length):
    scores = (
        jnp.einsum("qkgd,tkd->kgqt", query_seq, key_block, preferred_element_type=jnp.float32)
        * ATTN_MULT
    )
    allowed = (pos_block[None, :] <= query_pos[:, None]) & (pos_block[None, :] < length)
    return jnp.where(allowed, scores, MASKED)


def attend(inputs, key_pos, query_pos):
    query_seq, key_seq, value_seq, length = inputs
    key_blocks, value_blocks, pos_blocks = split_keys(key_seq, value_seq, key_pos)
    stat_shape = (query_seq.shape[1], query_seq.shape[2], query_seq.shape[0], 1)

    def gather_stats(carry, entry):
        running_max, running_sum = carry
        key_block, pos_block = entry
        scores = block_scores(query_seq, key_block, pos_block, query_pos, length)
        new_max = jnp.maximum(running_max, jnp.max(scores, axis=-1, keepdims=True))
        new_sum = running_sum * jnp.exp(running_max - new_max) + jnp.sum(
            jnp.exp(scores - new_max), axis=-1, keepdims=True
        )
        return ((new_max, new_sum), None)

    start_stats = (jnp.full(stat_shape, MASKED, jnp.float32), jnp.zeros(stat_shape, jnp.float32))
    (row_max, row_sums), unused = lax.scan(gather_stats, start_stats, (key_blocks, pos_blocks))

    def mix_values(running, entry):
        key_block, value_block, pos_block = entry
        scores = block_scores(query_seq, key_block, pos_block, query_pos, length)
        weights = jnp.exp(scores - row_max) / row_sums
        return (
            running
            + jnp.einsum(
                "kgqt,tkd->qkgd",
                weights.astype(jnp.bfloat16),
                value_block,
                preferred_element_type=jnp.float32,
            ),
            None,
        )

    start_mix = jnp.zeros(query_seq.shape, jnp.float32)
    mixed_heads, unused = lax.scan(mix_values, start_mix, (key_blocks, value_blocks, pos_blocks))
    return (mixed_heads, row_max, row_sums)


def attend_back(inputs, key_pos, query_pos):
    query_seq, key_seq, value_seq, grad_mixed, row_max, row_sums, length = inputs
    key_blocks, value_blocks, pos_blocks = split_keys(key_seq, value_seq, key_pos)

    def block_weights(key_block, value_block, pos_block):
        scores = block_scores(query_seq, key_block, pos_block, query_pos, length)
        weights = jnp.exp(scores - row_max) / row_sums
        grad_weights = jnp.einsum(
            "qkgd,tkd->kgqt", grad_mixed, value_block, preferred_element_type=jnp.float32
        )
        return (weights, grad_weights)

    def gather_centre(running, entry):
        weights, grad_weights = block_weights(*entry)
        return (running + jnp.sum(weights * grad_weights, axis=-1, keepdims=True), None)

    start_centre = jnp.zeros(row_max.shape, jnp.float32)
    centre, unused = lax.scan(gather_centre, start_centre, (key_blocks, value_blocks, pos_blocks))

    def grads_block(running, entry):
        key_block = entry[0]
        weights, grad_weights = block_weights(*entry)
        grad_scores = (weights * (grad_weights - centre)).astype(jnp.bfloat16)
        grad_query = (
            running
            + jnp.einsum(
                "kgqt,tkd->qkgd", grad_scores, key_block, preferred_element_type=jnp.float32
            )
            * ATTN_MULT
        )
        grad_key = (
            jnp.einsum("kgqt,qkgd->tkd", grad_scores, query_seq, preferred_element_type=jnp.float32)
            * ATTN_MULT
        )
        grad_value = jnp.einsum(
            "kgqt,qkgd->tkd",
            weights.astype(jnp.bfloat16),
            grad_mixed,
            preferred_element_type=jnp.float32,
        )
        return (grad_query, (grad_key, grad_value))

    start_query = jnp.zeros(query_seq.shape, jnp.float32)
    grad_query, (grad_key, grad_value) = lax.scan(
        grads_block, start_query, (key_blocks, value_blocks, pos_blocks)
    )
    return (grad_query, grad_key.reshape(key_seq.shape), grad_value.reshape(value_seq.shape))


MESH_IDS = pl.DeviceIdType.MESH
SIBLINGS = [(0, 1), (1, 0), (2, 3), (3, 2)]
OVER_X = [(0, 1), (1, 0)]
OVER_Y = [(0, 2), (2, 0), (1, 3), (3, 1)]
CROSSED = [((2 * y + c) * 2 + x, (2 * y + x) * 2 + c) for y in (0, 1) for c in (0, 1) for x in (0, 1)]


def pick_sequences(everyone, deal_order, first, count):
    slots = jnp.arange(deal_order.shape[0], dtype=jnp.int32)
    inverse = jnp.sum(jnp.where(deal_order[None, :] == slots[:, None], slots[None, :], 0), axis=1)
    return jnp.concatenate(
        [
            lax.dynamic_slice_in_dim(
                everyone, lax.dynamic_index_in_dim(inverse, first + at, keepdims=False), 1
            )
            for at in range(count)
        ]
    )


def bring_cotangent(cotangent, deal_order, first):
    everyone = lax.all_gather(cotangent, "dp", axis=0, tiled=True)
    return pick_sequences(everyone, deal_order, first, cotangent.shape[0])


def place():
    group = lax.axis_index("dp")
    core = lax.rem(group, 2)
    row = lax.axis_index("row")
    return group, core, group - core + row, row, lax.axis_index("col")


def lined(index, step, count):
    return lax.rem(index + step + count, count)


def aligned(block, size):
    return pl.ds(pl.multiple_of(block * size, size), size)


def greet(device):
    pl.semaphore_signal(
        pltpu.get_barrier_semaphore(), inc=1, device_id=device, device_id_type=MESH_IDS
    )


def remote(src, dst, sems, at, device):
    return pltpu.make_async_remote_copy(
        src_ref=src,
        dst_ref=dst,
        send_sem=sems.at[0, at],
        recv_sem=sems.at[1, at],
        device_id=device,
        device_id_type=MESH_IDS,
    )


def line_order(col, last, at):
    inner_low = jnp.where(at < 2, 1 - at, at)
    inner_high = jnp.where(at == 3, 0, jnp.where(at == 0, 2, jnp.where(at == 1, 1, 3)))
    return jnp.where(
        col == 0, at, jnp.where(col == last, last - at, jnp.where(col == 1, inner_low, inner_high))
    )


def start_kernel(
    cols, tok_ref, gain_ref, x_ref, a_ref, x_buf, a_buf, tok_sems, a_sems, local_sems
):
    group, core, mate, row, col = place()
    width = tok_ref.shape[2]
    length = x_buf.shape[0]
    sibling = (group + 1 - 2 * core, row, col)

    def line(step):
        return lined(col, step, cols)

    for step in range(1, cols):
        greet((mate, core, line(step)))
    greet(sibling)

    @pl.when(core != row)
    def _():
        greet((mate, core, col))

    pl.semaphore_wait(pltpu.get_barrier_semaphore(), cols + (core - row) * (core - row))

    def token_copy(step, into):
        return remote(
            tok_ref.at[line(step)],
            x_buf.at[:, aligned(into, width)],
            tok_sems,
            step,
            (mate, core, line(step)),
        )

    own_tokens = pltpu.make_async_copy(
        tok_ref.at[col], x_buf.at[:, aligned(col, width)], local_sems.at[0]
    )
    for step in range(1, cols):
        token_copy(step, col).start()

    @pl.when(core != row)
    def _():
        token_copy(0, col).start()

    @pl.when(core == row)
    def _():
        own_tokens.start()

    for step in range(1, cols):
        token_copy(step, line(-step)).wait_recv()

    @pl.when(core != row)
    def _():
        token_copy(0, col).wait_recv()

    @pl.when(core == row)
    def _():
        own_tokens.wait()

    keep_x = pltpu.make_async_copy(x_buf, x_ref, local_sems.at[1])
    keep_x.start()
    tall = min(64, length)

    @pl.loop(0, length // tall)
    def _(at):
        here = aligned(at, tall)
        now = x_buf[here, :].astype(jnp.float32)
        scale = lax.rsqrt(jnp.mean(now * now, axis=1, keepdims=True) + EPSILON)
        a_buf[here, :] = (now * scale * gain_ref[...]).astype(jnp.bfloat16)

    def a_copy(of_core):
        return remote(a_buf, a_ref.at[aligned(of_core, length)], a_sems, 0, sibling)

    own_a = pltpu.make_async_copy(a_buf, a_ref.at[aligned(core, length)], local_sems.at[2])
    a_copy(core).start()
    own_a.start()
    for step in range(1, cols):
        token_copy(step, col).wait_send()

    @pl.when(core != row)
    def _():
        token_copy(0, col).wait_send()

    keep_x.wait()
    own_a.wait()
    a_copy(core).wait_send()
    a_copy(1 - core).wait_recv()


def start_exchange(tokens, gain, cols):
    anywhere = pl.BlockSpec(memory_space=pl.ANY)
    seqs, length, width = tokens.shape
    full = width * cols
    return pl.pallas_call(
        functools.partial(start_kernel, cols),
        out_shape=(
            jax.ShapeDtypeStruct((length, full), tokens.dtype),
            jax.ShapeDtypeStruct((2 * length, full), tokens.dtype),
        ),
        in_specs=[anywhere, pl.BlockSpec(memory_space=pltpu.VMEM)],
        out_specs=(anywhere,) * 2,
        scratch_shapes=[
            pltpu.VMEM((length, full), tokens.dtype),
            pltpu.VMEM((length, full), tokens.dtype),
            pltpu.SemaphoreType.DMA((2, cols)),
            pltpu.SemaphoreType.DMA((2, 1)),
            pltpu.SemaphoreType.DMA((3,)),
        ],
        compiler_params=pltpu.CompilerParams(
            collective_id=1, has_side_effects=True, vmem_limit_bytes=60 << 20
        ),
        cost_estimate=pl.CostEstimate(flops=0, bytes_accessed=200 << 20, transcendentals=0),
        name="start_exchange",
    )(tokens, gain.reshape(1, full))


def gather_kernel(
    cols, q_ref, o_ref, after_ref, wq_ref, wo_ref, q_send, q_recv, q_over, o_send, o_recv, o_over, local_sems
):
    group, core, mate, row, col = place()
    last = cols - 1
    over = (group, 1 - row, col)
    greet(over)

    @pl.when(col < last)
    def _():
        greet((group, row, col + 1))

    @pl.when(col > 0)
    def _():
        greet((group, row, col - 1))

    pl.semaphore_wait(
        pltpu.get_barrier_semaphore(),
        1 + jnp.minimum(col, 1) + jnp.minimum(last - col, 1),
    )

    def moves(own, full, send, recv, over_sems):
        tall, wide = own.shape

        def block(of_row, of_col):
            return full.at[aligned(of_row, tall), aligned(of_col, wide)]

        def along(src, chunk, to, way):
            return pltpu.make_async_remote_copy(
                src_ref=src,
                dst_ref=block(row, chunk),
                send_sem=send.at[way, chunk],
                recv_sem=recv.at[chunk],
                device_id=(group, row, to),
                device_id_type=MESH_IDS,
            )

        def across(src, of_row, chunk):
            return remote(src, block(of_row, chunk), over_sems, chunk, over)

        return block, along, across

    both = (
        (q_ref, moves(q_ref, wq_ref, q_send, q_recv, q_over)),
        (o_ref, moves(o_ref, wo_ref, o_send, o_recv, o_over)),
    )
    own_copies = []
    for at, (own, (block, along, across)) in enumerate(both):

        @pl.when(col < last)
        def _():
            along(own, col, col + 1, 0).start()

        @pl.when(col > 0)
        def _():
            along(own, col, col - 1, 1).start()

        across(own, row, col).start()
        own_copies.append(pltpu.make_async_copy(own, block(row, col), local_sems.at[at]))
        own_copies[-1].start()
    for at in range(1, cols):
        chunk = line_order(col, last, at)
        for own, (block, along, across) in both:
            along(own, chunk, col, 0).wait_recv()

            @pl.when((chunk < col) & (col < last))
            def _():
                along(block(row, chunk), chunk, col + 1, 0).start()

            @pl.when((chunk > col) & (col > 0))
            def _():
                along(block(row, chunk), chunk, col - 1, 1).start()

            across(block(row, chunk), row, chunk).start()
    for copy in own_copies:
        copy.wait()
    for own, (block, along, across) in both:
        for chunk in range(cols):

            @pl.when((col >= chunk) & (col < last))
            def _():
                along(own, chunk, col + 1, 0).wait_send()

            @pl.when((col <= chunk) & (col > 0))
            def _():
                along(own, chunk, col - 1, 1).wait_send()

            across(own, row, chunk).wait_send()
            across(own, 1 - row, chunk).wait_recv()


def gather_weights(own_q, own_o, after, rows, cols):
    anywhere = pl.BlockSpec(memory_space=pl.ANY)

    def whole(own):
        return jax.ShapeDtypeStruct((own.shape[0] * rows, own.shape[1] * cols), own.dtype)

    return pl.pallas_call(
        functools.partial(gather_kernel, cols),
        out_shape=(whole(own_q), whole(own_o)),
        in_specs=[anywhere] * 3,
        out_specs=(anywhere,) * 2,
        scratch_shapes=[
            pltpu.SemaphoreType.DMA((2, cols)),
            pltpu.SemaphoreType.DMA((cols,)),
            pltpu.SemaphoreType.DMA((2, cols)),
        ]
        * 2
        + [pltpu.SemaphoreType.DMA((2,))],
        compiler_params=pltpu.CompilerParams(collective_id=4, has_side_effects=True),
        cost_estimate=pl.CostEstimate(flops=0, bytes_accessed=300 << 20, transcendentals=0),
        name="gather_weights",
    )(own_q, own_o, after)


def half_turn(wide):
    lanes = wide.shape[1]
    half = HEAD_SIZE // 2
    lane = lax.broadcasted_iota(jnp.int32, wide.shape, 1)
    return jnp.where(
        lax.rem(lane, HEAD_SIZE) < half,
        pltpu.roll(wide, lanes - half, 1),
        pltpu.roll(wide, half, 1),
    )


def both_heads(pair):
    lane = lax.broadcasted_iota(jnp.int32, pair.shape, 1)
    turned = pltpu.roll(pair, HEAD_SIZE, 1)
    low = lane < HEAD_SIZE
    return jnp.where(low, pair, turned), jnp.where(low, turned, pair)


def keep_head(pair, side):
    lane = lax.broadcasted_iota(jnp.int32, pair.shape, 1)
    mine = lane < HEAD_SIZE if side == 0 else lane >= HEAD_SIZE
    return jnp.where(mine, pair, jnp.zeros_like(pair))


def dot_nn(a, b):
    return lax.dot_general(a, b, (((1,), (0,)), ((), ())), preferred_element_type=jnp.float32)


def dot_nt(a, b):
    return lax.dot_general(a, b, (((1,), (1,)), ((), ())), preferred_element_type=jnp.float32)


def dot_tn(a, b):
    return lax.dot_general(a, b, (((0,), (0,)), ((), ())), preferred_element_type=jnp.float32)


PAIR = 2 * HEAD_SIZE


def attend_kernel(block, len_ref, a_ref, w_ref, cos_ref, sin_ref, qkv_ref, z_ref, q_all, k_two, v_two):
    rows = a_ref.shape[0]
    heads = q_all.shape[0]
    length = len_ref[0]

    @pl.loop(0, rows // block)
    def _(at):
        here = pl.ds(pl.multiple_of(at * block, block), block)
        lin = dot_nn(a_ref[here, :], w_ref[...])
        for part in range(heads // 2 + 1):
            lanes = slice(part * PAIR, (part + 1) * PAIR)
            now = lin[:, lanes]
            table = slice(0, PAIR) if part < heads // 2 else slice(PAIR, 2 * PAIR)
            now = now * cos_ref[here, table] + half_turn(now) * sin_ref[here, table]
            qkv_ref[here, lanes] = now.astype(jnp.bfloat16)
            if part < heads // 2:
                for side in range(2):
                    q_all[2 * part + side, here, :] = keep_head(now * ATTN_MULT, side).astype(
                        jnp.bfloat16
                    )
            else:
                keys, values = both_heads(now)
                k_two[here, :] = keys.astype(jnp.bfloat16)
                v_two[here, :] = values.astype(jnp.bfloat16)

    for at in range(rows // block):
        here = slice(at * block, (at + 1) * block)
        upto = (at + 1) * block
        row = lax.broadcasted_iota(jnp.int32, (block, upto), 0) + at * block
        key = lax.broadcasted_iota(jnp.int32, (block, upto), 1)
        allowed = key < jnp.minimum(row + 1, length)

        def one_head(head):
            scores = dot_nt(q_all[head, here, :], k_two[:upto, :])
            scores = jnp.where(allowed, scores, MASKED)
            top = jnp.max(scores, axis=1, keepdims=True)
            power = jnp.exp(scores - top)
            total = jnp.sum(power, axis=1, keepdims=True)
            return dot_nn(power.astype(jnp.bfloat16), v_two[:upto, :]) / total

        for pair in range(heads // 2):
            low = one_head(2 * pair)
            high = one_head(2 * pair + 1)
            lane = lax.broadcasted_iota(jnp.int32, low.shape, 1)
            z_ref[here, pair * PAIR : (pair + 1) * PAIR] = jnp.where(
                lane < HEAD_SIZE, low, high
            ).astype(jnp.bfloat16)


def attend_fast(length, inputs, weights, cosines, sines, groups):
    rows, depth = inputs.shape
    wide = weights.shape[1] // groups
    heads = (wide - PAIR) // HEAD_SIZE
    block = min(256, rows)
    return pl.pallas_call(
        functools.partial(attend_kernel, block),
        grid=(groups,),
        out_shape=(
            jax.ShapeDtypeStruct((rows, groups * wide), jnp.bfloat16),
            jax.ShapeDtypeStruct((rows, groups * heads * HEAD_SIZE), jnp.bfloat16),
        ),
        in_specs=[
            pl.BlockSpec(memory_space=pltpu.SMEM),
            pl.BlockSpec((rows, depth), lambda g: (0, 0)),
            pl.BlockSpec((depth, wide), lambda g: (0, g)),
            pl.BlockSpec((rows, 2 * PAIR), lambda g: (0, 0)),
            pl.BlockSpec((rows, 2 * PAIR), lambda g: (0, 0)),
        ],
        out_specs=(
            pl.BlockSpec((rows, wide), lambda g: (0, g)),
            pl.BlockSpec((rows, heads * HEAD_SIZE), lambda g: (0, g)),
        ),
        scratch_shapes=[
            pltpu.VMEM((heads, rows, PAIR), jnp.bfloat16),
            pltpu.VMEM((rows, PAIR), jnp.bfloat16),
            pltpu.VMEM((rows, PAIR), jnp.bfloat16),
        ],
        compiler_params=pltpu.CompilerParams(vmem_limit_bytes=48 << 20),
        cost_estimate=pl.CostEstimate(
            flops=2 * rows * depth * wide * groups + 2 * groups * heads * rows * rows * 128,
            bytes_accessed=2 * (rows * depth + depth * wide * groups + rows * wide * groups),
            transcendentals=groups * heads * rows * rows // 2,
        ),
        name="attend",
    )(length, inputs, weights, cosines, sines)


def attend_back_kernel(
    block, len_ref, qkv_ref, dz_ref, cos_ref, sin_ref, out_ref, q_all, z_all, k_two, v_two, k_acc, v_acc
):
    rows = qkv_ref.shape[0]
    heads = q_all.shape[0]
    length = len_ref[0]

    @pl.loop(0, rows // block)
    def _(at):
        here = pl.ds(pl.multiple_of(at * block, block), block)
        for part in range(heads // 2):
            lanes = slice(part * PAIR, (part + 1) * PAIR)
            queries = qkv_ref[here, lanes].astype(jnp.float32) * ATTN_MULT
            mixed = dz_ref[here, lanes].astype(jnp.float32)
            for side in range(2):
                q_all[2 * part + side, here, :] = keep_head(queries, side).astype(jnp.bfloat16)
                z_all[2 * part + side, here, :] = keep_head(mixed, side).astype(jnp.bfloat16)
        keys, values = both_heads(qkv_ref[here, heads * HEAD_SIZE :].astype(jnp.float32))
        k_two[here, :] = keys.astype(jnp.bfloat16)
        v_two[here, :] = values.astype(jnp.bfloat16)
        k_acc[here, :] = jnp.zeros((block, PAIR), jnp.float32)
        v_acc[here, :] = jnp.zeros((block, PAIR), jnp.float32)

    def turn_back(now, here, table):
        return (now * cos_ref[here, table] - half_turn(now) * sin_ref[here, table]).astype(
            jnp.bfloat16
        )

    for at in range(rows // block):
        here = slice(at * block, (at + 1) * block)
        upto = (at + 1) * block
        key = lax.broadcasted_iota(jnp.int32, (upto, block), 0)
        query = lax.broadcasted_iota(jnp.int32, (upto, block), 1) + at * block
        allowed = key < jnp.minimum(query + 1, length)

        def one_head(head):
            queries, mixed = q_all[head, here, :], z_all[head, here, :]
            scores = jnp.where(allowed, dot_nt(k_two[:upto, :], queries), MASKED)
            power = jnp.exp(scores - jnp.max(scores, axis=0, keepdims=True))
            weights = power * (1.0 / jnp.sum(power, axis=0, keepdims=True))
            back = dot_nt(v_two[:upto, :], mixed)
            centre = jnp.sum(weights * back, axis=0, keepdims=True)
            slope = (weights * (back - centre)).astype(jnp.bfloat16)
            k_acc[:upto, :] += dot_nn(slope, queries)
            v_acc[:upto, :] += dot_nn(weights.astype(jnp.bfloat16), mixed)
            return dot_tn(slope, k_two[:upto, :]) * ATTN_MULT

        for pair in range(heads // 2):
            low = one_head(2 * pair)
            high = one_head(2 * pair + 1)
            lane = lax.broadcasted_iota(jnp.int32, low.shape, 1)
            lanes = slice(pair * PAIR, (pair + 1) * PAIR)
            out_ref[here, lanes] = turn_back(
                jnp.where(lane < HEAD_SIZE, low, high), here, slice(0, PAIR)
            )

    @pl.loop(0, rows // block)
    def _(at):
        here = pl.ds(pl.multiple_of(at * block, block), block)
        keys, values = k_acc[here, :], v_acc[here, :]
        keys = keys + pltpu.roll(keys, HEAD_SIZE, 1)
        values = values + pltpu.roll(values, HEAD_SIZE, 1)
        lane = lax.broadcasted_iota(jnp.int32, keys.shape, 1)
        lanes = slice(heads * HEAD_SIZE, heads * HEAD_SIZE + PAIR)
        out_ref[here, lanes] = turn_back(
            jnp.where(lane < HEAD_SIZE, keys, values), here, slice(PAIR, 2 * PAIR)
        )


def attend_back_fast(length, projected, grad_mixed, cosines, sines, groups):
    rows = projected.shape[0]
    wide = projected.shape[1] // groups
    heads = (wide - PAIR) // HEAD_SIZE
    block = min(256, rows)
    return pl.pallas_call(
        functools.partial(attend_back_kernel, block),
        grid=(groups,),
        out_shape=jax.ShapeDtypeStruct((rows, groups * wide), jnp.bfloat16),
        in_specs=[
            pl.BlockSpec(memory_space=pltpu.SMEM),
            pl.BlockSpec((rows, wide), lambda g: (0, g)),
            pl.BlockSpec((rows, heads * HEAD_SIZE), lambda g: (0, g)),
            pl.BlockSpec((rows, 2 * PAIR), lambda g: (0, 0)),
            pl.BlockSpec((rows, 2 * PAIR), lambda g: (0, 0)),
        ],
        out_specs=pl.BlockSpec((rows, wide), lambda g: (0, g)),
        scratch_shapes=[
            pltpu.VMEM((heads, rows, PAIR), jnp.bfloat16),
            pltpu.VMEM((heads, rows, PAIR), jnp.bfloat16),
            pltpu.VMEM((rows, PAIR), jnp.bfloat16),
            pltpu.VMEM((rows, PAIR), jnp.bfloat16),
            pltpu.VMEM((rows, PAIR), jnp.float32),
            pltpu.VMEM((rows, PAIR), jnp.float32),
        ],
        compiler_params=pltpu.CompilerParams(vmem_limit_bytes=48 << 20),
        cost_estimate=pl.CostEstimate(
            flops=5 * groups * heads * rows * rows * 128,
            bytes_accessed=2 * (2 * rows * wide * groups + rows * heads * HEAD_SIZE * groups),
            transcendentals=groups * heads * rows * rows // 2,
        ),
        name="attend_back",
    )(length, projected, grad_mixed, cosines, sines)


def ffn_kernel(
    cols,
    own_ref,
    resid_ref,
    grad_ref,
    wg_own,
    wu_own,
    wd_own,
    wg_far,
    wu_far,
    wd_far,
    wg_far_y,
    wu_far_y,
    wd_far_y,
    wg_sib,
    wu_sib,
    wd_sib,
    wg_sib_y,
    wu_sib_y,
    wd_sib_y,
    u_all,
    dgu_all,
    mlp_all,
    back_all,
    relay_ref,
    land_ref,
    a_keep,
    a_send,
    b_keep,
    b_send,
    wg,
    wu,
    wd,
    b_all,
    b_turn,
    g_two,
    u_buf,
    dg_buf,
    du_buf,
    mlp_buf,
    back_buf,
    w_sems,
    ag_send,
    ag_recv,
    back_send,
    back_recv,
    relay_recv,
    pair_sems,
    lane_sems,
    tile_sems,
    io_sems,
):
    group, core, mate, row, col = place()
    sibling = (group + 1 - 2 * core, row, col)
    last = cols - 1
    depth = wg_own.shape[0]
    half = depth // 2
    units = wg_own.shape[1]
    rows = own_ref.shape[0]
    tile = units // cols
    beside = col + 1 - 2 * lax.rem(col, 2)
    facing = last - col
    inner = (col > 0) & (col < last)

    for step in range(1, cols):
        greet((group, row, lined(col, step, cols)))
    greet(sibling)
    pl.semaphore_wait(pltpu.get_barrier_semaphore(), cols)

    def pass_on(src, at, to, way):
        return pltpu.make_async_remote_copy(
            src_ref=src,
            dst_ref=b_all.at[at],
            send_sem=ag_send.at[way, at],
            recv_sem=ag_recv.at[at],
            device_id=(group, row, to),
            device_id_type=MESH_IDS,
        )

    @pl.when(col < last)
    def _():
        pass_on(own_ref, col, col + 1, 0).start()

    @pl.when(col > 0)
    def _():
        pass_on(own_ref, col, col - 1, 1).start()

    def order(at):
        return line_order(col, last, at)

    def load_g(at):
        side = lax.rem(at, 2)
        return pltpu.make_async_copy(grad_ref.at[order(at)], g_two.at[side], io_sems.at[6 + side])

    quarter = half // 2
    high = (group - core) // 2

    def rows_at(first, size):
        return pl.ds(pl.multiple_of(first, quarter), size)

    own_copy = pltpu.make_async_copy(own_ref, b_all.at[col], io_sems.at[0])
    own_copy.start()
    load_resid = pltpu.make_async_copy(resid_ref, mlp_buf, io_sems.at[8])
    far = (1 - row) * depth
    loads = []
    for full, mine, pieces in (
        (wg, wg_own, (wg_far, wg_far_y, wg_sib, wg_sib_y)),
        (wu, wu_own, (wu_far, wu_far_y, wu_sib, wu_sib_y)),
        (wd, wd_own, (wd_far, wd_far_y, wd_sib, wd_sib_y)),
    ):
        places = [
            far + of_core * half + of_plane * quarter
            for of_core in (core, 1 - core)
            for of_plane in (high, 1 - high)
        ]
        loads.append(
            pltpu.make_async_copy(
                mine, full.at[rows_at(row * depth, depth)], w_sems.at[len(loads)]
            )
        )
        for piece, first in zip(pieces, places):
            loads.append(
                pltpu.make_async_copy(
                    piece, full.at[rows_at(first, quarter)], w_sems.at[len(loads)]
                )
            )
    for load in loads:
        load.start()
    load_g(0).start()
    load_resid.start()
    own_copy.wait()
    for load in loads:
        load.wait()

    def arrive(chunk):
        pass_on(b_all.at[chunk], chunk, col, 0).wait_recv()

        @pl.when((chunk < col) & (col < last))
        def _():
            pass_on(b_all.at[chunk], chunk, col + 1, 0).start()

        @pl.when((chunk > col) & (col > 0))
        def _():
            pass_on(b_all.at[chunk], chunk, col - 1, 1).start()

    def outputs(chunk):
        return (
            pltpu.make_async_copy(u_buf, u_all.at[chunk], io_sems.at[1]),
            pltpu.make_async_copy(dg_buf, dgu_all.at[chunk, :, 0:units], io_sems.at[2]),
            pltpu.make_async_copy(du_buf, dgu_all.at[chunk, :, units : 2 * units], io_sems.at[3]),
        )

    def mlp_out(chunk):
        return pltpu.make_async_copy(mlp_buf, mlp_all.at[chunk], io_sems.at[4])

    def slot_of(at):
        return lax.rem(at, cols - 1)

    def deliver(slot, to, place_there, at):
        return pltpu.make_async_remote_copy(
            src_ref=back_buf.at[slot],
            dst_ref=back_all.at[place_there],
            send_sem=back_send.at[at],
            recv_sem=back_recv.at[place_there],
            device_id=(group, row, to),
            device_id_type=MESH_IDS,
        )

    def hand_over(slot, to, box, at):
        return pltpu.make_async_remote_copy(
            src_ref=back_buf.at[slot],
            dst_ref=relay_ref.at[box],
            send_sem=back_send.at[at],
            recv_sem=relay_recv.at[box],
            device_id=(group, row, to),
            device_id_type=MESH_IDS,
        )

    own_back = pltpu.make_async_copy(back_buf.at[0], back_all.at[0], io_sems.at[5])
    at_end = jnp.logical_not(inner)

    def one_chunk(at, unused):
        chunk = order(at)
        side = lax.rem(at, 2)

        @pl.when(at_end & (at > 0))
        def _():
            arrive(order(at))

        @pl.when(inner & (at == 1))
        def _():
            arrive(order(1))
            arrive(order(2))

        @pl.when(inner & (at == 3))
        def _():
            arrive(order(3))

        load_g(at).wait()

        @pl.when(at < last)
        def _():
            load_g(at + 1).start()

        @pl.when(at > 0)
        def _():
            for copy in outputs(order(at - 1)):
                copy.wait()

        @pl.loop(0, units // tile)
        def _(step):
            lanes = aligned(step, tile)
            gate = dot_nn(b_all[chunk], wg[:, lanes])
            upward = dot_nn(b_all[chunk], wu[:, lanes])
            back = RES_MULT * dot_nn(g_two[side], wd[:, lanes])
            opened = 1.0 / (1.0 + jnp.exp(-gate))
            silu = gate * opened
            u_buf[:, lanes] = (silu * upward).astype(jnp.bfloat16)
            slope = opened * (1.0 + gate * (1.0 - opened))
            dg_buf[:, lanes] = (back * upward * slope).astype(jnp.bfloat16)
            du_buf[:, lanes] = (back * silu).astype(jnp.bfloat16)

        for copy in outputs(chunk):
            copy.start()

        @pl.when(at > 0)
        def _():
            mlp_out(order(at - 1)).wait()

        @pl.when(at == 0)
        def _():
            load_resid.wait()

        @pl.when(at == last)
        def _():
            own_back.wait()

        @pl.loop(0, 2 * depth // tile)
        def _(step):
            here = aligned(step, tile)
            back = dot_nt(dg_buf[...], wg[here, :]) + dot_nt(du_buf[...], wu[here, :])
            back_buf[slot_of(at), :, here] = back.astype(jnp.bfloat16)
            added = jnp.where(at == 0, mlp_buf[:, here].astype(jnp.float32), 0.0)
            mlp_buf[:, here] = (added + RES_MULT * dot_nt(u_buf[...], wd[here, :])).astype(
                jnp.bfloat16
            )

        mlp_out(chunk).start()

        @pl.when(at == 0)
        def _():
            own_back.start()

        @pl.when(at_end & (at == 1))
        def _():
            deliver(1, beside, 1, 1).start()

        @pl.when(at_end & (at == 2))
        def _():
            hand_over(2, beside, 1, 2).start()

        @pl.when(at_end & (at == 3))
        def _():
            deliver(0, facing, 2, 3).start()

        @pl.when(inner & (at == 3))
        def _():
            hand_over(0, facing, 0, 3).start()

        return unused

    lax.fori_loop(0, cols, one_chunk, 0)
    for copy in outputs(order(last)):
        copy.wait()
    mlp_out(order(last)).wait()

    loads = []
    for chunk in range(cols):
        here = slice(chunk * rows, (chunk + 1) * rows)
        loads += [
            pltpu.make_async_copy(
                dgu_all.at[chunk, :, 0:units], wg.at[here], w_sems.at[chunk]
            ),
            pltpu.make_async_copy(
                dgu_all.at[chunk, :, units : 2 * units], wu.at[here], w_sems.at[cols + chunk]
            ),
            pltpu.make_async_copy(u_all.at[chunk], wd.at[here], w_sems.at[2 * cols + chunk]),
        ]
    for load in loads:
        load.start()

    def relay(box, slot):
        hand_over(slot, facing, box, 3).wait_recv()
        load = pltpu.make_async_copy(relay_ref.at[box], mlp_buf, io_sems.at[4])
        load.start()
        load.wait()
        tall = min(64, rows)

        @pl.loop(0, rows // tall)
        def _(at):
            here = aligned(at, tall)
            back_buf[slot, here, :] = (
                back_buf[slot, here, :].astype(jnp.float32)
                + mlp_buf[here, :].astype(jnp.float32)
            ).astype(jnp.bfloat16)

    buffers = (dg_buf, du_buf, u_buf)

    def to_sibling(at, part):
        return pltpu.make_async_remote_copy(
            src_ref=buffers[part],
            dst_ref=land_ref.at[at, part],
            send_sem=pair_sems.at[0, at, part],
            recv_sem=pair_sems.at[1, at, part],
            device_id=sibling,
            device_id_type=MESH_IDS,
        )

    def landed(at, part):
        return pltpu.make_async_copy(land_ref.at[at, part], buffers[part], io_sems.at[1 + part])

    halfway = units // 2
    small = rows // 2
    mine, others = aligned(row, small), aligned(1 - row, small)

    def x_lane(high):
        return (
            pltpu.make_async_copy(
                dg_buf.at[mine], a_keep.at[high, :, 0:units], lane_sems.at[0]
            ),
            pltpu.make_async_copy(
                dg_buf.at[others], a_send.at[high, :, 0:units], lane_sems.at[1]
            ),
            pltpu.make_async_copy(
                u_buf.at[mine, 0:halfway],
                a_keep.at[high, :, units : units + halfway],
                lane_sems.at[2],
            ),
            pltpu.make_async_copy(
                u_buf.at[others, 0:halfway],
                a_send.at[high, :, units : units + halfway],
                lane_sems.at[3],
            ),
        )

    def y_lane(target):
        copies = []
        for side in range(2):
            here = slice(side * small, (side + 1) * small)
            copies += [
                pltpu.make_async_copy(
                    du_buf.at[here], target.at[side, :, 0:units], lane_sems.at[4 + 2 * side]
                ),
                pltpu.make_async_copy(
                    u_buf.at[here, halfway:units],
                    target.at[side, :, units : units + halfway],
                    lane_sems.at[5 + 2 * side],
                ),
            ]
        return copies

    def put_results(high, act):
        for copy in x_lane(high):
            act(copy)

        @pl.when(high == (group - core) // 2)
        def _():
            for copy in y_lane(b_keep):
                act(copy)

        @pl.when(high != (group - core) // 2)
        def _():
            for copy in y_lane(b_send):
                act(copy)

    def start_it(copy):
        copy.start()

    def wait_for(copy):
        copy.wait()

    def part_of(chunk):
        return slice(chunk * rows, (chunk + 1) * rows)

    def grad_tile(block, chunk):
        return pltpu.make_async_copy(
            grad_ref.at[chunk, :, aligned(block, rows)],
            mlp_buf.at[:, part_of(chunk)],
            tile_sems.at[chunk],
        )

    parts = range(3)

    def block_of(at):
        return 2 * lax.rem(at, 2) + jnp.where(at >= 2, core, 1 - core)

    for chunk in range(cols):
        grad_tile(block_of(0), chunk).start()
    for chunk in range(cols):
        b_turn[0, :, part_of(chunk)] = b_all[chunk, :, aligned(block_of(0), rows)].T
    for chunk in range(cols):
        grad_tile(block_of(0), chunk).wait()
    for chunk in range(cols):
        g_two[0, :, part_of(chunk)] = mlp_buf[:, part_of(chunk)].T
    for load in loads:
        load.wait()

    def one_block(at, unused):
        high = lax.rem(at, 2)
        is_own = at >= 2
        side = lax.rem(at, 2)
        following = block_of(jnp.minimum(at + 1, 3))

        @pl.when(inner & (at == 1))
        def _():
            relay(0, col)
            deliver(col, beside, 1, 1).start()
            relay(1, last - col)
            deliver(last - col, facing, 2, 2).start()

        @pl.when(at < 3)
        def _():
            for chunk in range(cols):
                grad_tile(following, chunk).start()

        @pl.when((at == 1) | (at == 2))
        def _():
            for part in parts:
                to_sibling(at - 1, part).wait_send()

        @pl.when(at == 3)
        def _():
            put_results(0, wait_for)

        @pl.when(is_own)
        def _():
            for part in parts:
                to_sibling(high, part).wait_recv()
                landed(high, part).start()
            for part in parts:
                landed(high, part).wait()

        @pl.when(at < 3)
        def _():
            for chunk in range(cols):
                grad_tile(following, chunk).wait()

        @pl.loop(0, cols)
        def _(step):
            lanes = aligned(step, tile)
            tokens = aligned(step, rows)

            def put(buffer, value):
                other = jnp.where(is_own, buffer[:, lanes].astype(jnp.float32), 0.0)
                buffer[:, lanes] = (other + value).astype(jnp.bfloat16)

            put(dg_buf, dot_nn(b_turn[side], wg[:, lanes]))
            b_turn[1 - side, :, tokens] = b_all[step, :, aligned(following, rows)].T
            put(du_buf, dot_nn(b_turn[side], wu[:, lanes]))
            g_two[1 - side, :, tokens] = mlp_buf[:, tokens].T
            put(u_buf, RES_MULT * dot_nn(g_two[side], wd[:, lanes]))

        @pl.when(jnp.logical_not(is_own))
        def _():
            for part in parts:
                to_sibling(at, part).start()

        @pl.when(is_own)
        def _():
            put_results(high, start_it)

        return unused

    lax.fori_loop(0, 4, one_block, 0)
    put_results(1, wait_for)
    for at in range(1, cols):
        deliver(0, beside, 1, at).wait_send()
    for at in range(1, 3):
        deliver(0, beside, at, at).wait_recv()
    for chunk in range(cols):

        @pl.when((col >= chunk) & (col < last))
        def _():
            pass_on(own_ref, chunk, col + 1, 0).wait_send()

        @pl.when((col <= chunk) & (col > 0))
        def _():
            pass_on(own_ref, chunk, col - 1, 1).wait_send()


def feed_forward(own_input, resid, grad_rows, weights, cols):
    rows, width = own_input.shape
    units = weights[0].shape[1]
    anywhere = pl.BlockSpec(memory_space=pl.ANY)
    bf16 = jnp.bfloat16
    lane = jax.ShapeDtypeStruct((2, rows // 2, units + units // 2), bf16)
    return pl.pallas_call(
        functools.partial(ffn_kernel, cols),
        out_shape=(
            jax.ShapeDtypeStruct((cols, rows, units), bf16),
            jax.ShapeDtypeStruct((cols, rows, 2 * units), bf16),
            jax.ShapeDtypeStruct((cols, rows, width), bf16),
            jax.ShapeDtypeStruct((3, rows, width), bf16),
            jax.ShapeDtypeStruct((2, rows, width), bf16),
            jax.ShapeDtypeStruct((2, 3, rows, units), bf16),
        )
        + (lane,) * 4,
        in_specs=[anywhere] * 18,
        out_specs=(anywhere,) * 10,
        scratch_shapes=[
            pltpu.VMEM((width, units), bf16),
            pltpu.VMEM((width, units), bf16),
            pltpu.VMEM((width, units), bf16),
            pltpu.VMEM((cols, rows, width), bf16),
            pltpu.VMEM((2, rows, width), bf16),
            pltpu.VMEM((2, rows, width), bf16),
            pltpu.VMEM((rows, units), bf16),
            pltpu.VMEM((rows, units), bf16),
            pltpu.VMEM((rows, units), bf16),
            pltpu.VMEM((rows, width), bf16),
            pltpu.VMEM((cols - 1, rows, width), bf16),
            pltpu.SemaphoreType.DMA((15,)),
            pltpu.SemaphoreType.DMA((2, cols)),
            pltpu.SemaphoreType.DMA((cols,)),
            pltpu.SemaphoreType.DMA((cols,)),
            pltpu.SemaphoreType.DMA((cols,)),
            pltpu.SemaphoreType.DMA((2,)),
            pltpu.SemaphoreType.DMA((2, 2, 3)),
            pltpu.SemaphoreType.DMA((8,)),
            pltpu.SemaphoreType.DMA((cols,)),
            pltpu.SemaphoreType.DMA((9,)),
        ],
        compiler_params=pltpu.CompilerParams(
            collective_id=2, has_side_effects=True, vmem_limit_bytes=60 << 20
        ),
        cost_estimate=pl.CostEstimate(
            flops=18 * cols * rows * width * units,
            bytes_accessed=800 << 20,
            transcendentals=cols * rows * units,
        ),
        name="feed_forward",
    )(own_input, resid, grad_rows, *weights)


def finish_kernel(
    cols,
    ig_ref,
    gq_ref,
    go_ref,
    gain_ref,
    out_ref,
    gin_ref,
    crossed_ref,
    sq_ref,
    so_ref,
    gsum_ref,
    q_keep,
    q_sib,
    q_a1,
    q_a2,
    q_b1,
    q_b2,
    q_z,
    o_keep,
    o_sib,
    o_a1,
    o_a2,
    o_b1,
    o_b2,
    o_z,
    gain_now,
    gain_in,
    ig_sems,
    gain_sems,
    q_sems,
    o_sems,
    qz_sems,
    oz_sems,
    cross_sems,
    local_sems,
):
    group, core, mate, row, col = place()
    pair = group - core
    high = pair // 2
    sibling = (pair + 1 - core, row, col)
    over_x = (group, 1 - row, col)
    over_y = (2 * (1 - high) + core, row, col)
    width = gin_ref.shape[2]

    def line(step):
        return lax.rem(col + step + cols, cols)

    barrier = pltpu.get_barrier_semaphore()

    def greet(device):
        pl.semaphore_signal(barrier, inc=1, device_id=device, device_id_type=MESH_IDS)

    greet(sibling)
    greet(over_x)
    greet(over_y)
    for step in range(1, cols):
        greet((mate, core, line(step)))
        greet((group, row, line(step)))

    @pl.when(core != row)
    def _():
        greet((mate, core, col))

    pl.semaphore_wait(barrier, 2 * cols + 1 + (core - row) * (core - row))

    def remote(src, dst, sems, at, device):
        return pltpu.make_async_remote_copy(
            src_ref=src,
            dst_ref=dst,
            send_sem=sems.at[0, at],
            recv_sem=sems.at[1, at],
            device_id=device,
            device_id_type=MESH_IDS,
        )

    def lanes(block, size):
        return pl.ds(pl.multiple_of(block * size, size), size)

    matrices = (
        (gq_ref, sq_ref, q_keep, q_sib, q_a1, q_a2, q_b1, q_b2, q_z, q_sems, qz_sems),
        (go_ref, so_ref, o_keep, o_sib, o_a1, o_a2, o_b1, o_b2, o_z, o_sems, oz_sems),
    )

    def moves(m):
        grads, out, keep, sib, a1, a2, b1, b2, zb, sems, z_sems = matrices[m]
        return dict(
            s0=remote(grads.at[:, 1 - core], sib, sems, 0, sibling),
            a1=remote(grads.at[:, core, 1 - row], a1, sems, 1, over_x),
            a2=remote(keep.at[1 - high, row], a2, sems, 2, over_y),
            b1=remote(sib.at[1 - high], b1, sems, 3, over_y),
            b2=remote(sib.at[high, 1 - row], b2, sems, 4, over_x),
            own=pltpu.make_async_copy(grads.at[:, core], keep, local_sems.at[m]),
        )

    copies = (moves(0), moves(1))

    def rows_plus(into, more):
        rows = into.shape[0]
        step = min(32, rows)

        @pl.loop(0, rows // step)
        def _(at):
            here = pl.ds(pl.multiple_of(at * step, step), step)
            into[here, :] = (
                into[here, :].astype(jnp.float32) + more[here, :].astype(jnp.float32)
            ).astype(into.dtype)

    def token_copy(step, at):
        return remote(
            ig_ref.at[:, lanes(line(step), width)],
            gin_ref.at[at],
            ig_sems,
            step,
            (mate, core, line(step)),
        )

    own_tokens = pltpu.make_async_copy(
        ig_ref.at[:, lanes(col, width)], gin_ref.at[col], local_sems.at[2]
    )

    cross = remote(out_ref, crossed_ref, cross_sems, 0, (mate, core, col))
    stay = pltpu.make_async_copy(out_ref, crossed_ref, local_sems.at[4])
    for m in (1, 0):
        copies[m]["s0"].start()
        copies[m]["own"].start()
    copies[1]["a1"].start()
    @pl.when(core == row)
    def _():
        own_tokens.start()
        stay.start()
        for step in range(1, cols):
            token_copy(step, col).start()

    gain_load = pltpu.make_async_copy(gain_ref, gain_now.at[0], local_sems.at[3])
    gain_load.start()
    gain_load.wait()
    near = (
        sibling,
        over_x,
        over_y,
        (group, row, col + 1 - 2 * lax.rem(col, 2)),
        (group, row, lax.rem(col + cols // 2, cols)),
    )

    def gain_round(at):
        exchange = remote(gain_now.at[at], gain_in.at[at], gain_sems, at, near[at])
        exchange.start()
        exchange.wait()
        gain_now[at + 1] = gain_now[at] + gain_in[at]

    def z_moves(m, side, source):
        grads, out, keep, sib, a1, a2, b1, b2, zb, sems, z_sems = matrices[m]
        held = (keep, sib)[side]
        wide = zb.shape[3]
        return [
            pltpu.make_async_remote_copy(
                src_ref=held.at[high, row, :, lanes(line(step), wide)],
                dst_ref=zb.at[side, line(source(step))],
                send_sem=z_sems.at[0, side, step],
                recv_sem=z_sems.at[1, side, step],
                device_id=(group, row, line(step)),
                device_id_type=MESH_IDS,
            )
            for step in range(1, cols)
        ]

    def first_sums(m):
        grads, out, keep, sib, a1, a2, b1, b2, zb, sems, z_sems = matrices[m]
        copies[m]["own"].wait()
        copies[m]["a1"].wait()
        if m == 1:
            copies[0]["a1"].start()
        rows_plus(keep.at[1 - high, row], a1.at[1 - high])
        copies[m]["a2"].start()
        copies[m]["b1"].wait()
        if m == 1:
            copies[0]["b1"].start()
        rows_plus(sib.at[high, 1 - row], b1.at[1 - row])
        copies[m]["b2"].start()

    def last_sums(m):
        grads, out, keep, sib, a1, a2, b1, b2, zb, sems, z_sems = matrices[m]
        rows_plus(keep.at[high, row], a1.at[high])
        rows_plus(sib.at[high, row], b1.at[row])
        for side, last_copy in ((0, "a2"), (1, "b2")):
            copies[m][last_copy].wait()
            rows_plus((keep, sib)[side].at[high, row], (a2, b2)[side])
            for copy in z_moves(m, side, lambda step: 0):
                copy.start()

    copies[1]["s0"].wait()
    copies[1]["b1"].start()
    gain_round(0)
    copies[0]["s0"].wait()
    first_sums(1)
    gain_round(1)
    last_sums(1)
    gain_round(2)
    first_sums(0)

    @pl.when(core != row)
    def _():
        for step in range(cols):
            token_copy(step, col).start()
        cross.start()

    gain_round(3)
    last_sums(0)
    gain_round(4)
    gsum_ref[...] = gain_now[5]
    for m in (1, 0):
        for side in range(2):
            grads, out, keep, sib, a1, a2, b1, b2, zb, sems, z_sems = matrices[m]
            for copy in z_moves(m, side, lambda step: 0):
                copy.wait_send()
            for copy in z_moves(m, side, lambda step: -step):
                copy.wait_recv()
            held = (keep, sib)[side]
            wide = zb.shape[3]
            at_core = core if side == 0 else 1 - core
            rows = zb.shape[2]
            tall = min(32, rows)

            @pl.loop(0, rows // tall)
            def _(at):
                here = pl.ds(pl.multiple_of(at * tall, tall), tall)
                total = held[high, row, here, lanes(col, wide)].astype(jnp.float32)
                for step in range(1, cols):
                    total = total + zb[side, line(-step), here, :].astype(jnp.float32)
                out[at_core, here, :] = total

    for step in range(1, cols):
        token_copy(step, line(-step)).wait_recv()
        token_copy(step, col).wait_send()

    @pl.when(core != row)
    def _():
        token_copy(0, col).wait_recv()
        token_copy(0, col).wait_send()
        cross.wait()

    @pl.when(core == row)
    def _():
        own_tokens.wait()
        stay.wait()


def finish(input_grad, grad_q, grad_o, gains, output, cols):
    anywhere = pl.BlockSpec(memory_space=pl.ANY)
    in_vmem = pl.BlockSpec(memory_space=pltpu.VMEM)
    bf16, f32 = jnp.bfloat16, jnp.float32
    length, full = input_grad.shape
    rows = grad_q.shape[0] // 8

    def buffers(wide):
        return [
            pltpu.VMEM((2, 2, rows, wide), bf16),
            pltpu.VMEM((2, 2, rows, wide), bf16),
            pltpu.VMEM((2, rows, wide), bf16),
            pltpu.VMEM((rows, wide), bf16),
            pltpu.VMEM((2, rows, wide), bf16),
            pltpu.VMEM((rows, wide), bf16),
            pltpu.VMEM((2, cols, rows, wide // cols), bf16),
        ]

    wide_q, wide_o = grad_q.shape[1], grad_o.shape[1]
    return pl.pallas_call(
        functools.partial(finish_kernel, cols),
        out_shape=(
            jax.ShapeDtypeStruct((cols, length, full // cols), bf16),
            jax.ShapeDtypeStruct(output.shape, bf16),
            jax.ShapeDtypeStruct((2, rows, wide_q // cols), f32),
            jax.ShapeDtypeStruct((2, rows, wide_o // cols), f32),
            jax.ShapeDtypeStruct(gains.shape, f32),
        ),
        in_specs=[anywhere] * 5,
        out_specs=(anywhere, anywhere, in_vmem, in_vmem, in_vmem),
        scratch_shapes=buffers(wide_q)
        + buffers(wide_o)
        + [
            pltpu.VMEM((6,) + gains.shape, f32),
            pltpu.VMEM((5,) + gains.shape, f32),
            pltpu.SemaphoreType.DMA((2, cols)),
            pltpu.SemaphoreType.DMA((2, 5)),
            pltpu.SemaphoreType.DMA((2, 5)),
            pltpu.SemaphoreType.DMA((2, 5)),
            pltpu.SemaphoreType.DMA((2, 2, cols)),
            pltpu.SemaphoreType.DMA((2, 2, cols)),
            pltpu.SemaphoreType.DMA((2, 1)),
            pltpu.SemaphoreType.DMA((5,)),
        ],
        compiler_params=pltpu.CompilerParams(
            collective_id=3, has_side_effects=True, vmem_limit_bytes=60 << 20
        ),
        cost_estimate=pl.CostEstimate(flops=0, bytes_accessed=300 << 20, transcendentals=0),
        name="finish",
    )(
        input_grad,
        grad_q.reshape(2, 2, 2, rows, wide_q),
        grad_o.reshape(2, 2, 2, rows, wide_o),
        gains,
        output,
    )


def one_sequence_body(
    tokens,
    cotangent,
    lengths,
    deal_order,
    gain_attn,
    gain_ffn,
    w_query,
    key_value_weight,
    w_out,
    w_gate_up,
    w_down,
):
    seq_group, rows_local, width_local = tokens.shape
    row_count = lax.axis_size("row")
    col_count = lax.axis_size("col")
    full_width = width_local * col_count
    slot_len = rows_local * row_count
    group, core, mate, row, col = place()
    query_half = w_query.shape[1] // 2
    kv_half = key_value_weight.shape[2] // 2
    hidden = w_down.shape[1]

    def core_half(matrix, axis):
        width = matrix.shape[axis] // 2
        return lax.dynamic_slice_in_dim(matrix, core * width, width, axis)

    def joined(mine, other, at):
        return jnp.where(
            at == 0, jnp.concatenate([mine, other]), jnp.concatenate([other, mine])
        )

    def from_sibling(value):
        return lax.ppermute(value, "dp", SIBLINGS)

    def half_rows(matrix):
        return core_half(matrix, 0)

    pack_q = jnp.concatenate(
        [
            core_half(w_query, 1),
            core_half(key_value_weight[:, 0], 1),
            core_half(key_value_weight[:, 1], 1),
        ],
        axis=1,
    )
    pack_o = core_half(w_out, 1)
    gain_one = gain_attn.astype(jnp.float32)
    gain_two = gain_ffn.astype(jnp.float32)
    own_tokens, attn_input = start_exchange(tokens, gain_one, col_count)

    length = lax.dynamic_slice_in_dim(lengths, mate * seq_group + col, 1)
    given_pos = row * rows_local + jnp.arange(rows_local, dtype=jnp.int32)
    given_lengths = lax.dynamic_slice_in_dim(lengths, group * seq_group, seq_group)
    given_live = given_pos[None, :, None] < given_lengths[:, None, None]
    everyone = lax.all_gather(cotangent, "dp", axis=0, tiled=True)
    everyone, attn_input = lax.optimization_barrier((everyone, attn_input))
    picked = pick_sequences(everyone, deal_order, group * seq_group, seq_group)
    picked = jnp.where(given_live, picked, jnp.zeros_like(picked))
    given = lax.ppermute(picked, ("dp", "row"), CROSSED)
    weights_qkv, weights_out = gather_weights(pack_q, pack_o, picked, row_count, col_count)
    given, weights_qkv = lax.optimization_barrier((given, weights_qkv))
    line_cot = lax.all_gather(given, "col", axis=2, tiled=True)
    own_grad = lax.dynamic_index_in_dim(line_cot, col, keepdims=False).astype(jnp.float32)

    w_gate_up, w_down, weights_qkv = lax.optimization_barrier((w_gate_up, w_down, weights_qkv))
    def quarter_rows(matrix):
        count = matrix.shape[0] // 4
        return lax.dynamic_slice_in_dim(matrix, (2 * core + group // 2) * count, count)

    far_gate_up = lax.ppermute(quarter_rows(w_gate_up), "row", OVER_X)
    far_down = lax.ppermute(quarter_rows(w_down), "row", OVER_X)
    own_mats = (w_gate_up[:, 0], w_gate_up[:, 1], w_down)

    cosine_table, sine_table = rope_tables(jnp.arange(slot_len, dtype=jnp.int32), HEAD_SIZE)
    cosine_table, sine_table = lax.optimization_barrier((cosine_table, sine_table))
    cosines = jnp.concatenate(
        [jnp.tile(cosine_table, (1, 6)), jnp.ones((slot_len, HEAD_SIZE), jnp.float32)], axis=1
    )
    turning = jnp.concatenate([-sine_table, sine_table], axis=1)
    sines = jnp.concatenate(
        [jnp.tile(turning, (1, 3)), jnp.zeros((slot_len, HEAD_SIZE), jnp.float32)], axis=1
    )
    own_float = own_tokens.astype(jnp.float32)
    scale_one = lax.rsqrt(jnp.mean(own_float * own_float, axis=1, keepdims=True) + EPSILON)
    projected, heads_out = attend_fast(
        length, attn_input, weights_qkv, cosines, sines, col_count
    )

    def summed_rows(partial):
        count = partial.shape[0] // 2
        mine = lax.dynamic_slice_in_dim(partial, core * count, count)
        other = lax.dynamic_slice_in_dim(partial, (1 - core) * count, count)
        return mine.astype(jnp.float32) + from_sibling(other).astype(jnp.float32)

    attn_rows = summed_rows(expand_local(heads_out, weights_out).astype(jnp.bfloat16))
    resid = own_float + RES_MULT * attn_rows
    scale_two = lax.rsqrt(jnp.mean(resid * resid, axis=1, keepdims=True) + EPSILON)
    own_ffn = (resid * scale_two * gain_two).astype(jnp.bfloat16)

    shared_gate_up = lax.ppermute(far_gate_up, "dp", OVER_Y)
    shared_down = lax.ppermute(far_down, "dp", OVER_Y)
    own_ffn, own_mats, far_gate_up, far_down, shared_gate_up, shared_down = (
        lax.optimization_barrier(
            (own_ffn, own_mats, far_gate_up, far_down, shared_gate_up, shared_down)
        )
    )
    far_mats = (far_gate_up[:, 0], far_gate_up[:, 1], far_down)
    far_mats += (shared_gate_up[:, 0], shared_gate_up[:, 1], shared_down)
    sibling_mats = tuple(from_sibling(matrix) for matrix in far_mats)
    *unused, a_keep, a_send, b_keep, b_send = feed_forward(
        own_ffn,
        resid.astype(jnp.bfloat16),
        line_cot,
        own_mats + far_mats + sibling_mats,
        col_count,
    )
    mlp_part, back_part = unused[2:4]
    grad_normed_two = jnp.sum(back_part.astype(jnp.float32), axis=0)
    out_cols = lax.psum_scatter(mlp_part, "col", scatter_dimension=2, tiled=True)

    def plus(kept, came):
        return (kept.astype(jnp.float32) + came.astype(jnp.float32)).astype(jnp.bfloat16)

    a_came = lax.ppermute(a_send, "row", OVER_X)
    b_came = lax.ppermute(b_send, "dp", OVER_Y)

    weighted_two = grad_normed_two * gain_two
    inner_two = jnp.sum(weighted_two * resid, axis=1, keepdims=True)
    grad_resid = (
        own_grad + scale_two * weighted_two - resid * scale_two**3 * inner_two / full_width
    )
    gain_two_part = jnp.sum(grad_normed_two * resid * scale_two, axis=0)
    own_attn_grad = (RES_MULT * grad_resid).astype(jnp.bfloat16)
    grad_attn = joined(own_attn_grad, from_sibling(own_attn_grad), core)
    grad_heads = contract_local(grad_attn, weights_out).astype(jnp.bfloat16)
    grad_projected = attend_back_fast(
        length, projected, grad_heads, cosines, sines, col_count
    )
    a_sum, b_sum, grad_projected = lax.optimization_barrier(
        (plus(a_keep, a_came), plus(b_keep, b_came), grad_projected)
    )
    high = group // 2

    def one_of(pair, at):
        return lax.dynamic_index_in_dim(pair, at, keepdims=False)

    a_last = lax.ppermute(one_of(a_sum, 1 - high), "dp", OVER_Y)
    b_last = lax.ppermute(one_of(b_sum, 1 - row), "row", OVER_X)
    input_partial = expand_local(grad_projected, weights_qkv).astype(jnp.bfloat16)
    grad_attn, heads_out, input_partial = lax.optimization_barrier(
        (grad_attn, heads_out, input_partial)
    )
    grad_out = token_outer(grad_attn, heads_out).astype(jnp.bfloat16)
    grad_normed_one = summed_rows(input_partial)
    attn_input, grad_normed_one = lax.optimization_barrier((attn_input, grad_normed_one))
    grad_qkv = token_outer(attn_input, grad_projected).astype(jnp.bfloat16)
    weighted_one = grad_normed_one * gain_one
    inner_one = jnp.sum(weighted_one * own_float, axis=1, keepdims=True)
    own_input_grad = (
        grad_resid
        + scale_one * weighted_one
        - own_float * scale_one**3 * inner_one / full_width
    ).astype(jnp.bfloat16)
    gain_one_part = jnp.sum(grad_normed_one * own_float * scale_one, axis=0)
    a_last, b_last, grad_qkv, own_input_grad = lax.optimization_barrier(
        (a_last, b_last, grad_qkv, own_input_grad)
    )
    a_total = one_of(a_sum, high).astype(jnp.float32) + a_last.astype(jnp.float32)
    b_total = one_of(b_sum, row).astype(jnp.float32) + b_last.astype(jnp.float32)
    sums_gate_up = jnp.stack([a_total[:, :hidden], b_total[:, :hidden]], axis=1)
    sums_down = jnp.concatenate([a_total[:, hidden:], b_total[:, hidden:]], axis=1)
    sums_gate_up, sums_down, own_input_grad = lax.optimization_barrier(
        (sums_gate_up, sums_down, own_input_grad)
    )
    gains = jnp.stack([gain_one_part, gain_two_part]).reshape(8, -1)
    given_grad, given_out, sums_q, sums_o, gain_sums = finish(
        own_input_grad, grad_qkv, grad_out, gains, out_cols, col_count
    )
    layer_out = jnp.where(given_live, given_out.astype(jnp.float32), 0.0)
    input_grad = given_grad.astype(jnp.float32)
    grad_gain_attn, grad_gain_ffn = gain_sums.reshape(2, full_width)

    def both_cores(sums):
        return jnp.concatenate([sums[0], sums[1]], axis=1)

    qk = query_half + kv_half
    out_query = both_cores(sums_q[:, :, :query_half])
    out_kv = jnp.stack(
        [
            both_cores(sums_q[:, :, query_half:qk]),
            both_cores(sums_q[:, :, qk:]),
        ],
        axis=1,
    )
    out_out = both_cores(sums_o)
    return (
        layer_out,
        input_grad,
        out_query,
        out_kv,
        out_out,
        sums_gate_up,
        sums_down,
        grad_gain_attn,
        grad_gain_ffn,
    )


def general_body(
    tokens,
    cotangent,
    lengths,
    deal_order,
    gain_attn,
    gain_ffn,
    w_query,
    key_value_weight,
    w_out,
    w_gate_up,
    w_down,
):
    seq_group, rows_local, width_local = tokens.shape
    row_count = lax.axis_size("row")
    col_count = lax.axis_size("col")
    full_width = width_local * col_count
    slot_len = rows_local * row_count
    total_rows = seq_group * rows_local
    head_size = HEAD_SIZE
    query_width = w_query.shape[1]
    kv_width = key_value_weight.shape[2]
    kv_heads = kv_width // head_size
    group_size = query_width // kv_width
    group_index = lax.axis_index("dp")
    row_index = lax.axis_index("row")
    col_index = lax.axis_index("col")
    matrices = {
        "qkv": jnp.concatenate(
            [w_query, key_value_weight.reshape(key_value_weight.shape[0], 2 * kv_width)], axis=1
        ),
        "out": w_out,
        "gate_up": w_gate_up,
        "down": w_down,
    }

    def contract_with(operand, which_one):
        return contract_rows(operand, matrices[which_one])

    def expand_with(operand, which_one):
        return expand_rows(operand, matrices[which_one])

    own_cotangent = bring_cotangent(cotangent, deal_order, group_index * seq_group)
    own_rows = tokens
    seq_lens = lax.dynamic_slice_in_dim(lengths, group_index * seq_group, seq_group)
    local_pos = row_index * rows_local + jnp.arange(rows_local, dtype=jnp.int32)
    key_pos = jnp.arange(slot_len, dtype=jnp.int32)
    live_rows = (local_pos[None, :] < seq_lens[:, None]).astype(jnp.float32).reshape(total_rows, 1)
    cosine_table, sine_table = rope_tables(jnp.tile(local_pos, seq_group), head_size)
    own_tokens = own_rows.reshape(total_rows, width_local)
    wide_float = widen_cols(own_tokens).astype(jnp.float32)
    scale_one = lax.rsqrt(jnp.mean(wide_float * wide_float, axis=1, keepdims=True) + EPSILON)
    gain_one = gain_attn.astype(jnp.float32)
    first_normed = wide_float * scale_one
    attn_input = (first_normed * gain_one).astype(jnp.bfloat16)
    projected = contract_with(attn_input, "qkv")
    query_lin = projected[:, :query_width].reshape(total_rows, query_width // head_size, head_size)
    key_lin = projected[:, query_width : query_width + kv_width].reshape(
        total_rows, kv_heads, head_size
    )
    value_lin = projected[:, query_width + kv_width :]
    query_rows = rotary_embed(query_lin, cosine_table, sine_table).astype(jnp.bfloat16)
    keys_own = (
        rotary_embed(key_lin, cosine_table, sine_table)
        .astype(jnp.bfloat16)
        .reshape(seq_group, rows_local, kv_width)
    )
    values_own = value_lin.astype(jnp.bfloat16).reshape(seq_group, rows_local, kv_width)
    all_keys, all_values = (
        lax.all_gather(keys_own, "row", axis=1, tiled=True),
        lax.all_gather(values_own, "row", axis=1, tiled=True),
    )
    query_split = query_rows.reshape(seq_group, rows_local, kv_heads, group_size, head_size)
    key_split = all_keys.reshape(seq_group, slot_len, kv_heads, head_size)
    value_split = all_values.reshape(seq_group, slot_len, kv_heads, head_size)

    def forward_seq(inputs):
        return attend(inputs, key_pos, local_pos)

    mixed_heads, row_max, row_sums = lax.map(
        forward_seq, (query_split, key_split, value_split, seq_lens)
    )
    heads_out = mixed_heads.reshape(total_rows, query_width).astype(jnp.bfloat16)
    attn_local = narrow_cols(expand_with(heads_out, "out"))
    resid = own_tokens.astype(jnp.float32) + RES_MULT * attn_local
    gain_two = lax.dynamic_slice_in_dim(
        gain_ffn.astype(jnp.float32), col_index * width_local, width_local
    )
    scale_two = lax.rsqrt(sum_over_cols(jnp.sum(resid * resid, axis=1)) / full_width + EPSILON)[
        :, None
    ]
    normed_two = resid * scale_two
    ffn_input = widen_cols((normed_two * gain_two).astype(jnp.bfloat16))
    gate_up = contract_with(ffn_input, "gate_up")
    gate = gate_up[:, 0]
    upward = gate_up[:, 1]
    sigmoid_gate = jax.nn.sigmoid(gate)
    silu_gate = gate * sigmoid_gate
    hidden = (silu_gate * upward).astype(jnp.bfloat16)
    ffn_local = narrow_cols(expand_with(hidden, "down"))
    layer_out = live_rows * (resid + RES_MULT * ffn_local)
    grad_rows = live_rows * own_cotangent.reshape(total_rows, width_local).astype(jnp.float32)
    grad_ffn = widen_cols((RES_MULT * grad_rows).astype(jnp.bfloat16))
    grad_hidden = contract_with(grad_ffn, "down")
    grad_down = token_outer(grad_ffn, hidden)
    slope = sigmoid_gate * (1.0 + gate * (1.0 - sigmoid_gate))
    grad_gate_rows = jnp.stack(
        [grad_hidden * upward * slope, grad_hidden * silu_gate], axis=1
    ).astype(jnp.bfloat16)
    grad_gate_up = token_outer(ffn_input, grad_gate_rows)
    grad_normed_two = narrow_cols(expand_with(grad_gate_rows, "gate_up"))
    weighted_two = grad_normed_two * gain_two
    inner_two = sum_over_cols(jnp.sum(weighted_two * resid, axis=1))[:, None]
    grad_resid = (
        grad_rows + scale_two * weighted_two - resid * scale_two**3 * inner_two / full_width
    )
    gain_two_part = jnp.sum(grad_normed_two * normed_two, axis=0)
    grad_attn = widen_cols((RES_MULT * grad_resid).astype(jnp.bfloat16))
    grad_heads = contract_with(grad_attn, "out").astype(jnp.bfloat16)
    grad_out = token_outer(grad_attn, heads_out)
    grad_split = grad_heads.reshape(seq_group, rows_local, kv_heads, group_size, head_size)

    def backward_seq(inputs):
        return attend_back(inputs, key_pos, local_pos)

    grad_query, grad_key, grad_value = lax.map(
        backward_seq, (query_split, key_split, value_split, grad_split, row_max, row_sums, seq_lens)
    )
    key_part, value_part = (
        lax.psum_scatter(
            grad_key.reshape(seq_group, slot_len, kv_width).astype(jnp.bfloat16),
            "row",
            scatter_dimension=1,
            tiled=True,
        ).astype(jnp.float32),
        lax.psum_scatter(
            grad_value.reshape(seq_group, slot_len, kv_width).astype(jnp.bfloat16),
            "row",
            scatter_dimension=1,
            tiled=True,
        ).astype(jnp.float32),
    )
    query_back = rotary_embed(
        grad_query.reshape(total_rows, query_width // head_size, head_size),
        cosine_table,
        -sine_table,
    ).reshape(total_rows, query_width)
    key_back = rotary_embed(
        key_part.reshape(total_rows, kv_heads, head_size), cosine_table, -sine_table
    ).reshape(total_rows, kv_width)
    grad_projected = jnp.concatenate(
        [query_back, key_back, value_part.reshape(total_rows, kv_width)], axis=1
    ).astype(jnp.bfloat16)
    grad_qkv = token_outer(attn_input, grad_projected)
    grad_normed_one = expand_with(grad_projected, "qkv")
    weighted_one = grad_normed_one * gain_one
    inner_one = jnp.sum(weighted_one * wide_float, axis=1, keepdims=True)
    input_part = scale_one * weighted_one - wide_float * scale_one**3 * inner_one / full_width
    input_grad = grad_resid + narrow_cols(input_part)
    gain_one_part = jnp.sum(grad_normed_one * first_normed, axis=0)
    gain_two_full = lax.dynamic_update_slice_in_dim(
        jnp.zeros((full_width,), jnp.float32), gain_two_part, col_index * width_local, 0
    )
    grad_gain_attn, grad_gain_ffn = lax.psum((gain_one_part, gain_two_full), ("dp", "row", "col"))
    sums_qkv, sums_out, sums_gate_up, sums_down = (
        lax.psum_scatter(
            grad_qkv.astype(jnp.bfloat16), ("dp", "row"), scatter_dimension=0, tiled=True
        ).astype(jnp.float32),
        lax.psum_scatter(
            grad_out.astype(jnp.bfloat16), ("dp", "row"), scatter_dimension=0, tiled=True
        ).astype(jnp.float32),
        lax.psum_scatter(
            grad_gate_up.astype(jnp.bfloat16), ("dp", "row"), scatter_dimension=0, tiled=True
        ).astype(jnp.float32),
        lax.psum_scatter(
            grad_down.astype(jnp.bfloat16), ("dp", "row"), scatter_dimension=0, tiled=True
        ).astype(jnp.float32),
    )
    out_query = sums_qkv[:, :query_width]
    out_kv = sums_qkv[:, query_width:].reshape(sums_qkv.shape[0], 2, kv_width)
    return (
        layer_out.reshape(seq_group, rows_local, width_local),
        input_grad.reshape(seq_group, rows_local, width_local),
        out_query,
        out_kv,
        sums_out,
        sums_gate_up,
        sums_down,
        grad_gain_attn,
        grad_gain_ffn,
    )


def body(tokens, cotangent, lengths, deal_order, gain_attn, gain_ffn, w_query, key_value_weight, *rest):
    sizes = (lax.axis_size("dp"), lax.axis_size("row"), lax.axis_size("col"))
    one_each = sizes == (4, 2, 4) and tokens.shape[0] == sizes[2]
    pairs = w_query.shape[1] == 8 * HEAD_SIZE and key_value_weight.shape[2] == 2 * HEAD_SIZE
    chosen = one_sequence_body if one_each and pairs else general_body
    return chosen(
        tokens, cotangent, lengths, deal_order, gain_attn, gain_ffn, w_query, key_value_weight, *rest
    )


def solution(mesh):
    placed = (
        P("dp", "row", "col"),
        P("dp", "row", "col"),
        P(),
        P(),
        P(),
        P(),
        P("row", "col"),
        P("row", None, "col"),
        P("row", "col"),
        P("row", None, "col"),
        P("row", "col"),
    )
    return jax.shard_map(
        body,
        mesh=mesh,
        in_specs=placed,
        out_specs=(
            P("dp", "row", "col"),
            P("dp", "row", "col"),
            P(("dp", "row"), "col"),
            P(("dp", "row"), None, "col"),
            P(("dp", "row"), "col"),
            P(("dp", "row"), None, "col"),
            P(("dp", "row"), "col"),
            P(),
            P(),
        ),
        check_vma=False,
    )
```

```python
import functools

import jax
import jax.numpy as jnp
from jax import lax
from jax.experimental import pallas as pl
from jax.experimental.pallas import tpu as pltpu
from jax.sharding import PartitionSpec as P

HEAD_SIZE = 64


EPSILON = 1e-05
THETA = 10000000.0
ATTN_MULT = 0.015625
RES_MULT = 0.22
MASKED = -1e30


def rope_tables(positions, head_size):
    halves = jnp.arange(head_size // 2, dtype=jnp.float32)
    inverse_freq = THETA ** (-(halves * 2.0) / head_size)
    angles = positions.astype(jnp.float32)[:, None] * inverse_freq[None, :]
    return (jnp.cos(angles), jnp.sin(angles))


def rotary_embed(value_rows, cosine_table, sine_table):
    middle = value_rows.shape[-1] // 2
    first_half = value_rows[..., :middle]
    second_half = value_rows[..., middle:]
    cos_part = cosine_table[:, None, :]
    sin_part = sine_table[:, None, :]
    return jnp.concatenate(
        [
            first_half * cos_part - second_half * sin_part,
            second_half * cos_part + first_half * sin_part,
        ],
        axis=-1,
    )


def widen_cols(value_rows):
    return lax.all_gather(value_rows, "col", axis=1, tiled=True)


def narrow_cols(value_rows):
    return lax.psum_scatter(value_rows, "col", scatter_dimension=1, tiled=True)


def sum_over_cols(value_rows):
    return lax.psum(value_rows, "col")


def contract_local(operand, matrix):
    return lax.dot_general(
        operand, matrix, (((1,), (0,)), ((), ())), preferred_element_type=jnp.float32
    )


def expand_local(operand, matrix):
    trailing = tuple(range(1, operand.ndim))
    return lax.dot_general(
        operand, matrix, ((trailing, trailing), ((), ())), preferred_element_type=jnp.float32
    )


def token_outer(features, grads):
    return lax.dot_general(
        features, grads, (((0,), (0,)), ((), ())), preferred_element_type=jnp.float32
    )


def contract_rows(operand, matrix):
    return contract_local(operand, lax.all_gather(matrix, "row", axis=0, tiled=True))


def expand_rows(operand, matrix):
    return expand_local(operand, lax.all_gather(matrix, "row", axis=0, tiled=True))


def split_keys(key_seq, value_seq, key_pos):
    slot_len = key_seq.shape[0]
    width = min(512, slot_len)
    count = slot_len // width
    return (
        key_seq.reshape(count, width, key_seq.shape[1], key_seq.shape[2]),
        value_seq.reshape(count, width, value_seq.shape[1], value_seq.shape[2]),
        key_pos.reshape(count, width),
    )


def block_scores(query_seq, key_block, pos_block, query_pos, length):
    scores = (
        jnp.einsum("qkgd,tkd->kgqt", query_seq, key_block, preferred_element_type=jnp.float32)
        * ATTN_MULT
    )
    allowed = (pos_block[None, :] <= query_pos[:, None]) & (pos_block[None, :] < length)
    return jnp.where(allowed, scores, MASKED)


def attend(inputs, key_pos, query_pos):
    query_seq, key_seq, value_seq, length = inputs
    key_blocks, value_blocks, pos_blocks = split_keys(key_seq, value_seq, key_pos)
    stat_shape = (query_seq.shape[1], query_seq.shape[2], query_seq.shape[0], 1)

    def gather_stats(carry, entry):
        running_max, running_sum = carry
        key_block, pos_block = entry
        scores = block_scores(query_seq, key_block, pos_block, query_pos, length)
        new_max = jnp.maximum(running_max, jnp.max(scores, axis=-1, keepdims=True))
        new_sum = running_sum * jnp.exp(running_max - new_max) + jnp.sum(
            jnp.exp(scores - new_max), axis=-1, keepdims=True
        )
        return ((new_max, new_sum), None)

    start_stats = (jnp.full(stat_shape, MASKED, jnp.float32), jnp.zeros(stat_shape, jnp.float32))
    (row_max, row_sums), unused = lax.scan(gather_stats, start_stats, (key_blocks, pos_blocks))

    def mix_values(running, entry):
        key_block, value_block, pos_block = entry
        scores = block_scores(query_seq, key_block, pos_block, query_pos, length)
        weights = jnp.exp(scores - row_max) / row_sums
        return (
            running
            + jnp.einsum(
                "kgqt,tkd->qkgd",
                weights.astype(jnp.bfloat16),
                value_block,
                preferred_element_type=jnp.float32,
            ),
            None,
        )

    start_mix = jnp.zeros(query_seq.shape, jnp.float32)
    mixed_heads, unused = lax.scan(mix_values, start_mix, (key_blocks, value_blocks, pos_blocks))
    return (mixed_heads, row_max, row_sums)


def attend_back(inputs, key_pos, query_pos):
    query_seq, key_seq, value_seq, grad_mixed, row_max, row_sums, length = inputs
    key_blocks, value_blocks, pos_blocks = split_keys(key_seq, value_seq, key_pos)

    def block_weights(key_block, value_block, pos_block):
        scores = block_scores(query_seq, key_block, pos_block, query_pos, length)
        weights = jnp.exp(scores - row_max) / row_sums
        grad_weights = jnp.einsum(
            "qkgd,tkd->kgqt", grad_mixed, value_block, preferred_element_type=jnp.float32
        )
        return (weights, grad_weights)

    def gather_centre(running, entry):
        weights, grad_weights = block_weights(*entry)
        return (running + jnp.sum(weights * grad_weights, axis=-1, keepdims=True), None)

    start_centre = jnp.zeros(row_max.shape, jnp.float32)
    centre, unused = lax.scan(gather_centre, start_centre, (key_blocks, value_blocks, pos_blocks))

    def grads_block(running, entry):
        key_block = entry[0]
        weights, grad_weights = block_weights(*entry)
        grad_scores = (weights * (grad_weights - centre)).astype(jnp.bfloat16)
        grad_query = (
            running
            + jnp.einsum(
                "kgqt,tkd->qkgd", grad_scores, key_block, preferred_element_type=jnp.float32
            )
            * ATTN_MULT
        )
        grad_key = (
            jnp.einsum("kgqt,qkgd->tkd", grad_scores, query_seq, preferred_element_type=jnp.float32)
            * ATTN_MULT
        )
        grad_value = jnp.einsum(
            "kgqt,qkgd->tkd",
            weights.astype(jnp.bfloat16),
            grad_mixed,
            preferred_element_type=jnp.float32,
        )
        return (grad_query, (grad_key, grad_value))

    start_query = jnp.zeros(query_seq.shape, jnp.float32)
    grad_query, (grad_key, grad_value) = lax.scan(
        grads_block, start_query, (key_blocks, value_blocks, pos_blocks)
    )
    return (grad_query, grad_key.reshape(key_seq.shape), grad_value.reshape(value_seq.shape))


MESH_IDS = pl.DeviceIdType.MESH
SIBLINGS = [(0, 1), (1, 0), (2, 3), (3, 2)]
OVER_X = [(0, 1), (1, 0)]
OVER_Y = [(0, 2), (2, 0), (1, 3), (3, 1)]
CROSSED = [((2 * y + c) * 2 + x, (2 * y + x) * 2 + c) for y in (0, 1) for c in (0, 1) for x in (0, 1)]


def pick_sequences(everyone, deal_order, first, count):
    slots = jnp.arange(deal_order.shape[0], dtype=jnp.int32)
    inverse = jnp.sum(jnp.where(deal_order[None, :] == slots[:, None], slots[None, :], 0), axis=1)
    return jnp.concatenate(
        [
            lax.dynamic_slice_in_dim(
                everyone, lax.dynamic_index_in_dim(inverse, first + at, keepdims=False), 1
            )
            for at in range(count)
        ]
    )


def bring_cotangent(cotangent, deal_order, first):
    everyone = lax.all_gather(cotangent, "dp", axis=0, tiled=True)
    return pick_sequences(everyone, deal_order, first, cotangent.shape[0])


def place():
    group = lax.axis_index("dp")
    core = lax.rem(group, 2)
    row = lax.axis_index("row")
    return group, core, group - core + row, row, lax.axis_index("col")


def lined(index, step, count):
    return lax.rem(index + step + count, count)


def aligned(block, size):
    return pl.ds(pl.multiple_of(block * size, size), size)


def greet(device):
    pl.semaphore_signal(
        pltpu.get_barrier_semaphore(), inc=1, device_id=device, device_id_type=MESH_IDS
    )


def remote(src, dst, sems, at, device):
    return pltpu.make_async_remote_copy(
        src_ref=src,
        dst_ref=dst,
        send_sem=sems.at[0, at],
        recv_sem=sems.at[1, at],
        device_id=device,
        device_id_type=MESH_IDS,
    )


def line_order(col, last, at):
    inner_low = jnp.where(at < 2, 1 - at, at)
    inner_high = jnp.where(at == 3, 0, jnp.where(at == 0, 2, jnp.where(at == 1, 1, 3)))
    return jnp.where(
        col == 0, at, jnp.where(col == last, last - at, jnp.where(col == 1, inner_low, inner_high))
    )


def start_kernel(
    cols, tok_ref, gain_ref, x_ref, a_ref, x_buf, a_buf, tok_sems, a_sems, local_sems
):
    group, core, mate, row, col = place()
    width = tok_ref.shape[2]
    length = x_buf.shape[0]
    sibling = (group + 1 - 2 * core, row, col)

    def line(step):
        return lined(col, step, cols)

    for step in range(1, cols):
        greet((mate, core, line(step)))
    greet(sibling)

    @pl.when(core != row)
    def _():
        greet((mate, core, col))

    pl.semaphore_wait(pltpu.get_barrier_semaphore(), cols + (core - row) * (core - row))

    def token_copy(step, into):
        return remote(
            tok_ref.at[line(step)],
            x_buf.at[:, aligned(into, width)],
            tok_sems,
            step,
            (mate, core, line(step)),
        )

    own_tokens = pltpu.make_async_copy(
        tok_ref.at[col], x_buf.at[:, aligned(col, width)], local_sems.at[0]
    )
    for step in range(1, cols):
        token_copy(step, col).start()

    @pl.when(core != row)
    def _():
        token_copy(0, col).start()

    @pl.when(core == row)
    def _():
        own_tokens.start()

    for step in range(1, cols):
        token_copy(step, line(-step)).wait_recv()

    @pl.when(core != row)
    def _():
        token_copy(0, col).wait_recv()

    @pl.when(core == row)
    def _():
        own_tokens.wait()

    keep_x = pltpu.make_async_copy(x_buf, x_ref, local_sems.at[1])
    keep_x.start()
    tall = min(64, length)

    @pl.loop(0, length // tall)
    def _(at):
        here = aligned(at, tall)
        now = x_buf[here, :].astype(jnp.float32)
        scale = lax.rsqrt(jnp.mean(now * now, axis=1, keepdims=True) + EPSILON)
        a_buf[here, :] = (now * scale * gain_ref[...]).astype(jnp.bfloat16)

    def a_copy(of_core):
        return remote(a_buf, a_ref.at[aligned(of_core, length)], a_sems, 0, sibling)

    own_a = pltpu.make_async_copy(a_buf, a_ref.at[aligned(core, length)], local_sems.at[2])
    a_copy(core).start()
    own_a.start()
    for step in range(1, cols):
        token_copy(step, col).wait_send()

    @pl.when(core != row)
    def _():
        token_copy(0, col).wait_send()

    keep_x.wait()
    own_a.wait()
    a_copy(core).wait_send()
    a_copy(1 - core).wait_recv()


def start_exchange(tokens, gain, cols):
    anywhere = pl.BlockSpec(memory_space=pl.ANY)
    seqs, length, width = tokens.shape
    full = width * cols
    return pl.pallas_call(
        functools.partial(start_kernel, cols),
        out_shape=(
            jax.ShapeDtypeStruct((length, full), tokens.dtype),
            jax.ShapeDtypeStruct((2 * length, full), tokens.dtype),
        ),
        in_specs=[anywhere, pl.BlockSpec(memory_space=pltpu.VMEM)],
        out_specs=(anywhere,) * 2,
        scratch_shapes=[
            pltpu.VMEM((length, full), tokens.dtype),
            pltpu.VMEM((length, full), tokens.dtype),
            pltpu.SemaphoreType.DMA((2, cols)),
            pltpu.SemaphoreType.DMA((2, 1)),
            pltpu.SemaphoreType.DMA((3,)),
        ],
        compiler_params=pltpu.CompilerParams(
            collective_id=1, has_side_effects=True, vmem_limit_bytes=60 << 20
        ),
        cost_estimate=pl.CostEstimate(flops=0, bytes_accessed=200 << 20, transcendentals=0),
        name="start_exchange",
    )(tokens, gain.reshape(1, full))


def gather_kernel(
    cols, q_ref, o_ref, after_ref, wq_ref, wo_ref, q_send, q_recv, q_over, o_send, o_recv, o_over, local_sems
):
    group, core, mate, row, col = place()
    last = cols - 1
    over = (group, 1 - row, col)
    greet(over)

    @pl.when(col < last)
    def _():
        greet((group, row, col + 1))

    @pl.when(col > 0)
    def _():
        greet((group, row, col - 1))

    pl.semaphore_wait(
        pltpu.get_barrier_semaphore(),
        1 + jnp.minimum(col, 1) + jnp.minimum(last - col, 1),
    )

    def moves(own, full, send, recv, over_sems):
        tall, wide = own.shape

        def block(of_row, of_col):
            return full.at[aligned(of_row, tall), aligned(of_col, wide)]

        def along(src, chunk, to, way):
            return pltpu.make_async_remote_copy(
                src_ref=src,
                dst_ref=block(row, chunk),
                send_sem=send.at[way, chunk],
                recv_sem=recv.at[chunk],
                device_id=(group, row, to),
                device_id_type=MESH_IDS,
            )

        def across(src, of_row, chunk):
            return remote(src, block(of_row, chunk), over_sems, chunk, over)

        return block, along, across

    both = (
        (q_ref, moves(q_ref, wq_ref, q_send, q_recv, q_over)),
        (o_ref, moves(o_ref, wo_ref, o_send, o_recv, o_over)),
    )
    own_copies = []
    for at, (own, (block, along, across)) in enumerate(both):

        @pl.when(col < last)
        def _():
            along(own, col, col + 1, 0).start()

        @pl.when(col > 0)
        def _():
            along(own, col, col - 1, 1).start()

        across(own, row, col).start()
        own_copies.append(pltpu.make_async_copy(own, block(row, col), local_sems.at[at]))
        own_copies[-1].start()
    for at in range(1, cols):
        chunk = line_order(col, last, at)
        for own, (block, along, across) in both:
            along(own, chunk, col, 0).wait_recv()

            @pl.when((chunk < col) & (col < last))
            def _():
                along(block(row, chunk), chunk, col + 1, 0).start()

            @pl.when((chunk > col) & (col > 0))
            def _():
                along(block(row, chunk), chunk, col - 1, 1).start()

            across(block(row, chunk), row, chunk).start()
    for copy in own_copies:
        copy.wait()
    for own, (block, along, across) in both:
        for chunk in range(cols):

            @pl.when((col >= chunk) & (col < last))
            def _():
                along(own, chunk, col + 1, 0).wait_send()

            @pl.when((col <= chunk) & (col > 0))
            def _():
                along(own, chunk, col - 1, 1).wait_send()

            across(own, row, chunk).wait_send()
            across(own, 1 - row, chunk).wait_recv()


def gather_weights(own_q, own_o, after, rows, cols):
    anywhere = pl.BlockSpec(memory_space=pl.ANY)

    def whole(own):
        return jax.ShapeDtypeStruct((own.shape[0] * rows, own.shape[1] * cols), own.dtype)

    return pl.pallas_call(
        functools.partial(gather_kernel, cols),
        out_shape=(whole(own_q), whole(own_o)),
        in_specs=[anywhere] * 3,
        out_specs=(anywhere,) * 2,
        scratch_shapes=[
            pltpu.SemaphoreType.DMA((2, cols)),
            pltpu.SemaphoreType.DMA((cols,)),
            pltpu.SemaphoreType.DMA((2, cols)),
        ]
        * 2
        + [pltpu.SemaphoreType.DMA((2,))],
        compiler_params=pltpu.CompilerParams(collective_id=4, has_side_effects=True),
        cost_estimate=pl.CostEstimate(flops=0, bytes_accessed=300 << 20, transcendentals=0),
        name="gather_weights",
    )(own_q, own_o, after)


def half_turn(wide):
    lanes = wide.shape[1]
    half = HEAD_SIZE // 2
    lane = lax.broadcasted_iota(jnp.int32, wide.shape, 1)
    return jnp.where(
        lax.rem(lane, HEAD_SIZE) < half,
        pltpu.roll(wide, lanes - half, 1),
        pltpu.roll(wide, half, 1),
    )


def both_heads(pair):
    lane = lax.broadcasted_iota(jnp.int32, pair.shape, 1)
    turned = pltpu.roll(pair, HEAD_SIZE, 1)
    low = lane < HEAD_SIZE
    return jnp.where(low, pair, turned), jnp.where(low, turned, pair)


def keep_head(pair, side):
    lane = lax.broadcasted_iota(jnp.int32, pair.shape, 1)
    mine = lane < HEAD_SIZE if side == 0 else lane >= HEAD_SIZE
    return jnp.where(mine, pair, jnp.zeros_like(pair))


def dot_nn(a, b):
    return lax.dot_general(a, b, (((1,), (0,)), ((), ())), preferred_element_type=jnp.float32)


def dot_nt(a, b):
    return lax.dot_general(a, b, (((1,), (1,)), ((), ())), preferred_element_type=jnp.float32)


def dot_tn(a, b):
    return lax.dot_general(a, b, (((0,), (0,)), ((), ())), preferred_element_type=jnp.float32)


PAIR = 2 * HEAD_SIZE


def attend_kernel(block, len_ref, a_ref, w_ref, cos_ref, sin_ref, qkv_ref, z_ref, q_all, k_two, v_two):
    rows = a_ref.shape[0]
    heads = q_all.shape[0]
    length = len_ref[0]

    @pl.loop(0, rows // block)
    def _(at):
        here = pl.ds(pl.multiple_of(at * block, block), block)
        lin = dot_nn(a_ref[here, :], w_ref[...])
        for part in range(heads // 2 + 1):
            lanes = slice(part * PAIR, (part + 1) * PAIR)
            now = lin[:, lanes]
            table = slice(0, PAIR) if part < heads // 2 else slice(PAIR, 2 * PAIR)
            now = now * cos_ref[here, table] + half_turn(now) * sin_ref[here, table]
            qkv_ref[here, lanes] = now.astype(jnp.bfloat16)
            if part < heads // 2:
                for side in range(2):
                    q_all[2 * part + side, here, :] = keep_head(now * ATTN_MULT, side).astype(
                        jnp.bfloat16
                    )
            else:
                keys, values = both_heads(now)
                k_two[here, :] = keys.astype(jnp.bfloat16)
                v_two[here, :] = values.astype(jnp.bfloat16)

    for at in range(rows // block):
        here = slice(at * block, (at + 1) * block)
        upto = (at + 1) * block
        row = lax.broadcasted_iota(jnp.int32, (block, upto), 0) + at * block
        key = lax.broadcasted_iota(jnp.int32, (block, upto), 1)
        allowed = key < jnp.minimum(row + 1, length)

        def one_head(head):
            scores = dot_nt(q_all[head, here, :], k_two[:upto, :])
            scores = jnp.where(allowed, scores, MASKED)
            top = jnp.max(scores, axis=1, keepdims=True)
            power = jnp.exp(scores - top)
            total = jnp.sum(power, axis=1, keepdims=True)
            return dot_nn(power.astype(jnp.bfloat16), v_two[:upto, :]) / total

        for pair in range(heads // 2):
            low = one_head(2 * pair)
            high = one_head(2 * pair + 1)
            lane = lax.broadcasted_iota(jnp.int32, low.shape, 1)
            z_ref[here, pair * PAIR : (pair + 1) * PAIR] = jnp.where(
                lane < HEAD_SIZE, low, high
            ).astype(jnp.bfloat16)


def attend_fast(length, inputs, weights, cosines, sines, groups):
    rows, depth = inputs.shape
    wide = weights.shape[1] // groups
    heads = (wide - PAIR) // HEAD_SIZE
    block = min(256, rows)
    return pl.pallas_call(
        functools.partial(attend_kernel, block),
        grid=(groups,),
        out_shape=(
            jax.ShapeDtypeStruct((rows, groups * wide), jnp.bfloat16),
            jax.ShapeDtypeStruct((rows, groups * heads * HEAD_SIZE), jnp.bfloat16),
        ),
        in_specs=[
            pl.BlockSpec(memory_space=pltpu.SMEM),
            pl.BlockSpec((rows, depth), lambda g: (0, 0)),
            pl.BlockSpec((depth, wide), lambda g: (0, g)),
            pl.BlockSpec((rows, 2 * PAIR), lambda g: (0, 0)),
            pl.BlockSpec((rows, 2 * PAIR), lambda g: (0, 0)),
        ],
        out_specs=(
            pl.BlockSpec((rows, wide), lambda g: (0, g)),
            pl.BlockSpec((rows, heads * HEAD_SIZE), lambda g: (0, g)),
        ),
        scratch_shapes=[
            pltpu.VMEM((heads, rows, PAIR), jnp.bfloat16),
            pltpu.VMEM((rows, PAIR), jnp.bfloat16),
            pltpu.VMEM((rows, PAIR), jnp.bfloat16),
        ],
        compiler_params=pltpu.CompilerParams(vmem_limit_bytes=48 << 20),
        cost_estimate=pl.CostEstimate(
            flops=2 * rows * depth * wide * groups + 2 * groups * heads * rows * rows * 128,
            bytes_accessed=2 * (rows * depth + depth * wide * groups + rows * wide * groups),
            transcendentals=groups * heads * rows * rows // 2,
        ),
        name="attend",
    )(length, inputs, weights, cosines, sines)


def attend_back_kernel(
    block, len_ref, qkv_ref, dz_ref, cos_ref, sin_ref, out_ref, q_all, z_all, k_two, v_two, k_acc, v_acc
):
    rows = qkv_ref.shape[0]
    heads = q_all.shape[0]
    length = len_ref[0]

    @pl.loop(0, rows // block)
    def _(at):
        here = pl.ds(pl.multiple_of(at * block, block), block)
        for part in range(heads // 2):
            lanes = slice(part * PAIR, (part + 1) * PAIR)
            queries = qkv_ref[here, lanes].astype(jnp.float32) * ATTN_MULT
            mixed = dz_ref[here, lanes].astype(jnp.float32)
            for side in range(2):
                q_all[2 * part + side, here, :] = keep_head(queries, side).astype(jnp.bfloat16)
                z_all[2 * part + side, here, :] = keep_head(mixed, side).astype(jnp.bfloat16)
        keys, values = both_heads(qkv_ref[here, heads * HEAD_SIZE :].astype(jnp.float32))
        k_two[here, :] = keys.astype(jnp.bfloat16)
        v_two[here, :] = values.astype(jnp.bfloat16)
        k_acc[here, :] = jnp.zeros((block, PAIR), jnp.float32)
        v_acc[here, :] = jnp.zeros((block, PAIR), jnp.float32)

    def turn_back(now, here, table):
        return (now * cos_ref[here, table] - half_turn(now) * sin_ref[here, table]).astype(
            jnp.bfloat16
        )

    for at in range(rows // block):
        here = slice(at * block, (at + 1) * block)
        upto = (at + 1) * block
        key = lax.broadcasted_iota(jnp.int32, (upto, block), 0)
        query = lax.broadcasted_iota(jnp.int32, (upto, block), 1) + at * block
        allowed = key < jnp.minimum(query + 1, length)

        def one_head(head):
            queries, mixed = q_all[head, here, :], z_all[head, here, :]
            scores = jnp.where(allowed, dot_nt(k_two[:upto, :], queries), MASKED)
            power = jnp.exp(scores - jnp.max(scores, axis=0, keepdims=True))
            weights = power * (1.0 / jnp.sum(power, axis=0, keepdims=True))
            back = dot_nt(v_two[:upto, :], mixed)
            centre = jnp.sum(weights * back, axis=0, keepdims=True)
            slope = (weights * (back - centre)).astype(jnp.bfloat16)
            k_acc[:upto, :] += dot_nn(slope, queries)
            v_acc[:upto, :] += dot_nn(weights.astype(jnp.bfloat16), mixed)
            return dot_tn(slope, k_two[:upto, :]) * ATTN_MULT

        for pair in range(heads // 2):
            low = one_head(2 * pair)
            high = one_head(2 * pair + 1)
            lane = lax.broadcasted_iota(jnp.int32, low.shape, 1)
            lanes = slice(pair * PAIR, (pair + 1) * PAIR)
            out_ref[here, lanes] = turn_back(
                jnp.where(lane < HEAD_SIZE, low, high), here, slice(0, PAIR)
            )

    @pl.loop(0, rows // block)
    def _(at):
        here = pl.ds(pl.multiple_of(at * block, block), block)
        keys, values = k_acc[here, :], v_acc[here, :]
        keys = keys + pltpu.roll(keys, HEAD_SIZE, 1)
        values = values + pltpu.roll(values, HEAD_SIZE, 1)
        lane = lax.broadcasted_iota(jnp.int32, keys.shape, 1)
        lanes = slice(heads * HEAD_SIZE, heads * HEAD_SIZE + PAIR)
        out_ref[here, lanes] = turn_back(
            jnp.where(lane < HEAD_SIZE, keys, values), here, slice(PAIR, 2 * PAIR)
        )


def attend_back_fast(length, projected, grad_mixed, cosines, sines, groups):
    rows = projected.shape[0]
    wide = projected.shape[1] // groups
    heads = (wide - PAIR) // HEAD_SIZE
    block = min(256, rows)
    return pl.pallas_call(
        functools.partial(attend_back_kernel, block),
        grid=(groups,),
        out_shape=jax.ShapeDtypeStruct((rows, groups * wide), jnp.bfloat16),
        in_specs=[
            pl.BlockSpec(memory_space=pltpu.SMEM),
            pl.BlockSpec((rows, wide), lambda g: (0, g)),
            pl.BlockSpec((rows, heads * HEAD_SIZE), lambda g: (0, g)),
            pl.BlockSpec((rows, 2 * PAIR), lambda g: (0, 0)),
            pl.BlockSpec((rows, 2 * PAIR), lambda g: (0, 0)),
        ],
        out_specs=pl.BlockSpec((rows, wide), lambda g: (0, g)),
        scratch_shapes=[
            pltpu.VMEM((heads, rows, PAIR), jnp.bfloat16),
            pltpu.VMEM((heads, rows, PAIR), jnp.bfloat16),
            pltpu.VMEM((rows, PAIR), jnp.bfloat16),
            pltpu.VMEM((rows, PAIR), jnp.bfloat16),
            pltpu.VMEM((rows, PAIR), jnp.float32),
            pltpu.VMEM((rows, PAIR), jnp.float32),
        ],
        compiler_params=pltpu.CompilerParams(vmem_limit_bytes=48 << 20),
        cost_estimate=pl.CostEstimate(
            flops=5 * groups * heads * rows * rows * 128,
            bytes_accessed=2 * (2 * rows * wide * groups + rows * heads * HEAD_SIZE * groups),
            transcendentals=groups * heads * rows * rows // 2,
        ),
        name="attend_back",
    )(length, projected, grad_mixed, cosines, sines)


def ffn_kernel(
    cols,
    own_ref,
    resid_ref,
    grad_ref,
    wg_own,
    wu_own,
    wd_own,
    wg_far,
    wu_far,
    wd_far,
    wg_far_y,
    wu_far_y,
    wd_far_y,
    wg_sib,
    wu_sib,
    wd_sib,
    wg_sib_y,
    wu_sib_y,
    wd_sib_y,
    u_all,
    dgu_all,
    mlp_all,
    back_all,
    relay_ref,
    land_ref,
    a_keep,
    a_send,
    b_keep,
    b_send,
    wg,
    wu,
    wd,
    b_all,
    b_turn,
    g_two,
    u_buf,
    dg_buf,
    du_buf,
    mlp_buf,
    back_buf,
    w_sems,
    ag_send,
    ag_recv,
    back_send,
    back_recv,
    relay_recv,
    pair_sems,
    lane_sems,
    tile_sems,
    io_sems,
):
    group, core, mate, row, col = place()
    sibling = (group + 1 - 2 * core, row, col)
    last = cols - 1
    depth = wg_own.shape[0]
    half = depth // 2
    units = wg_own.shape[1]
    rows = own_ref.shape[0]
    tile = units // cols
    beside = col + 1 - 2 * lax.rem(col, 2)
    facing = last - col
    inner = (col > 0) & (col < last)

    for step in range(1, cols):
        greet((group, row, lined(col, step, cols)))
    greet(sibling)
    pl.semaphore_wait(pltpu.get_barrier_semaphore(), cols)

    def pass_on(src, at, to, way):
        return pltpu.make_async_remote_copy(
            src_ref=src,
            dst_ref=b_all.at[at],
            send_sem=ag_send.at[way, at],
            recv_sem=ag_recv.at[at],
            device_id=(group, row, to),
            device_id_type=MESH_IDS,
        )

    @pl.when(col < last)
    def _():
        pass_on(own_ref, col, col + 1, 0).start()

    @pl.when(col > 0)
    def _():
        pass_on(own_ref, col, col - 1, 1).start()

    def order(at):
        return line_order(col, last, at)

    def load_g(at):
        side = lax.rem(at, 2)
        return pltpu.make_async_copy(grad_ref.at[order(at)], g_two.at[side], io_sems.at[6 + side])

    quarter = half // 2
    high = (group - core) // 2

    def rows_at(first, size):
        return pl.ds(pl.multiple_of(first, quarter), size)

    own_copy = pltpu.make_async_copy(own_ref, b_all.at[col], io_sems.at[0])
    own_copy.start()
    load_resid = pltpu.make_async_copy(resid_ref, mlp_buf, io_sems.at[8])
    far = (1 - row) * depth
    loads = []
    for full, mine, pieces in (
        (wg, wg_own, (wg_far, wg_far_y, wg_sib, wg_sib_y)),
        (wu, wu_own, (wu_far, wu_far_y, wu_sib, wu_sib_y)),
        (wd, wd_own, (wd_far, wd_far_y, wd_sib, wd_sib_y)),
    ):
        places = [
            far + of_core * half + of_plane * quarter
            for of_core in (core, 1 - core)
            for of_plane in (high, 1 - high)
        ]
        loads.append(
            pltpu.make_async_copy(
                mine, full.at[rows_at(row * depth, depth)], w_sems.at[len(loads)]
            )
        )
        for piece, first in zip(pieces, places):
            loads.append(
                pltpu.make_async_copy(
                    piece, full.at[rows_at(first, quarter)], w_sems.at[len(loads)]
                )
            )
    for load in loads:
        load.start()
    load_g(0).start()
    load_resid.start()
    own_copy.wait()
    for load in loads:
        load.wait()

    def arrive(chunk):
        pass_on(b_all.at[chunk], chunk, col, 0).wait_recv()

        @pl.when((chunk < col) & (col < last))
        def _():
            pass_on(b_all.at[chunk], chunk, col + 1, 0).start()

        @pl.when((chunk > col) & (col > 0))
        def _():
            pass_on(b_all.at[chunk], chunk, col - 1, 1).start()

    def outputs(chunk):
        return (
            pltpu.make_async_copy(u_buf, u_all.at[chunk], io_sems.at[1]),
            pltpu.make_async_copy(dg_buf, dgu_all.at[chunk, :, 0:units], io_sems.at[2]),
            pltpu.make_async_copy(du_buf, dgu_all.at[chunk, :, units : 2 * units], io_sems.at[3]),
        )

    def mlp_out(chunk):
        return pltpu.make_async_copy(mlp_buf, mlp_all.at[chunk], io_sems.at[4])

    def slot_of(at):
        return lax.rem(at, cols - 1)

    def deliver(slot, to, place_there, at):
        return pltpu.make_async_remote_copy(
            src_ref=back_buf.at[slot],
            dst_ref=back_all.at[place_there],
            send_sem=back_send.at[at],
            recv_sem=back_recv.at[place_there],
            device_id=(group, row, to),
            device_id_type=MESH_IDS,
        )

    def hand_over(slot, to, box, at):
        return pltpu.make_async_remote_copy(
            src_ref=back_buf.at[slot],
            dst_ref=relay_ref.at[box],
            send_sem=back_send.at[at],
            recv_sem=relay_recv.at[box],
            device_id=(group, row, to),
            device_id_type=MESH_IDS,
        )

    own_back = pltpu.make_async_copy(back_buf.at[0], back_all.at[0], io_sems.at[5])
    at_end = jnp.logical_not(inner)

    def one_chunk(at, unused):
        chunk = order(at)
        side = lax.rem(at, 2)

        @pl.when(at_end & (at > 0))
        def _():
            arrive(order(at))

        @pl.when(inner & (at == 1))
        def _():
            arrive(order(1))
            arrive(order(2))

        @pl.when(inner & (at == 3))
        def _():
            arrive(order(3))

        load_g(at).wait()

        @pl.when(at < last)
        def _():
            load_g(at + 1).start()

        @pl.when(at > 0)
        def _():
            for copy in outputs(order(at - 1)):
                copy.wait()

        @pl.loop(0, units // tile)
        def _(step):
            lanes = aligned(step, tile)
            gate = dot_nn(b_all[chunk], wg[:, lanes])
            upward = dot_nn(b_all[chunk], wu[:, lanes])
            back = RES_MULT * dot_nn(g_two[side], wd[:, lanes])
            opened = 1.0 / (1.0 + jnp.exp(-gate))
            silu = gate * opened
            u_buf[:, lanes] = (silu * upward).astype(jnp.bfloat16)
            slope = opened * (1.0 + gate * (1.0 - opened))
            dg_buf[:, lanes] = (back * upward * slope).astype(jnp.bfloat16)
            du_buf[:, lanes] = (back * silu).astype(jnp.bfloat16)

        @pl.when(at < last)
        def _():
            for copy in outputs(chunk):
                copy.start()

        @pl.when(at > 0)
        def _():
            mlp_out(order(at - 1)).wait()

        @pl.when(at == 0)
        def _():
            load_resid.wait()

        @pl.when(at == last)
        def _():
            own_back.wait()

        @pl.loop(0, 2 * depth // tile)
        def _(step):
            here = aligned(step, tile)
            back = dot_nt(dg_buf[...], wg[here, :]) + dot_nt(du_buf[...], wu[here, :])
            back_buf[slot_of(at), :, here] = back.astype(jnp.bfloat16)
            added = jnp.where(at == 0, mlp_buf[:, here].astype(jnp.float32), 0.0)
            mlp_buf[:, here] = (added + RES_MULT * dot_nt(u_buf[...], wd[here, :])).astype(
                jnp.bfloat16
            )

        mlp_out(chunk).start()

        @pl.when(at == 0)
        def _():
            own_back.start()

        @pl.when(at_end & (at == 1))
        def _():
            deliver(1, beside, 1, 1).start()

        @pl.when(at_end & (at == 2))
        def _():
            hand_over(2, beside, 1, 2).start()

        @pl.when(at_end & (at == 3))
        def _():
            deliver(0, facing, 2, 3).start()

        @pl.when(inner & (at == 3))
        def _():
            hand_over(0, facing, 0, 3).start()

        return unused

    lax.fori_loop(0, cols, one_chunk, 0)

    loads = []
    for at in range(cols):
        chunk = order(at)
        here = aligned(chunk, rows)
        sources = (dg_buf, du_buf, u_buf)
        if at < last:
            sources = (
                dgu_all.at[chunk, :, 0:units],
                dgu_all.at[chunk, :, units : 2 * units],
                u_all.at[chunk],
            )
        for part, (source, full) in enumerate(zip(sources, (wg, wu, wd))):
            loads.append(
                pltpu.make_async_copy(source, full.at[here], w_sems.at[part * cols + at])
            )
    for load in loads:
        load.start()
    mlp_out(order(last)).wait()

    def relay(box, slot):
        hand_over(slot, facing, box, 3).wait_recv()
        load = pltpu.make_async_copy(relay_ref.at[box], mlp_buf, io_sems.at[4])
        load.start()
        load.wait()
        tall = min(64, rows)

        @pl.loop(0, rows // tall)
        def _(at):
            here = aligned(at, tall)
            back_buf[slot, here, :] = (
                back_buf[slot, here, :].astype(jnp.float32)
                + mlp_buf[here, :].astype(jnp.float32)
            ).astype(jnp.bfloat16)

    buffers = (dg_buf, du_buf, u_buf)

    def to_sibling(at, part):
        return pltpu.make_async_remote_copy(
            src_ref=buffers[part],
            dst_ref=land_ref.at[at, part],
            send_sem=pair_sems.at[0, at, part],
            recv_sem=pair_sems.at[1, at, part],
            device_id=sibling,
            device_id_type=MESH_IDS,
        )

    def landed(at, part):
        return pltpu.make_async_copy(land_ref.at[at, part], buffers[part], io_sems.at[1 + part])

    halfway = units // 2
    small = rows // 2
    mine, others = aligned(row, small), aligned(1 - row, small)

    def x_lane(high):
        return (
            pltpu.make_async_copy(
                dg_buf.at[mine], a_keep.at[high, :, 0:units], lane_sems.at[0]
            ),
            pltpu.make_async_copy(
                dg_buf.at[others], a_send.at[high, :, 0:units], lane_sems.at[1]
            ),
            pltpu.make_async_copy(
                u_buf.at[mine, 0:halfway],
                a_keep.at[high, :, units : units + halfway],
                lane_sems.at[2],
            ),
            pltpu.make_async_copy(
                u_buf.at[others, 0:halfway],
                a_send.at[high, :, units : units + halfway],
                lane_sems.at[3],
            ),
        )

    def y_lane(target):
        copies = []
        for side in range(2):
            here = slice(side * small, (side + 1) * small)
            copies += [
                pltpu.make_async_copy(
                    du_buf.at[here], target.at[side, :, 0:units], lane_sems.at[4 + 2 * side]
                ),
                pltpu.make_async_copy(
                    u_buf.at[here, halfway:units],
                    target.at[side, :, units : units + halfway],
                    lane_sems.at[5 + 2 * side],
                ),
            ]
        return copies

    def put_results(high, act):
        for copy in x_lane(high):
            act(copy)

        @pl.when(high == (group - core) // 2)
        def _():
            for copy in y_lane(b_keep):
                act(copy)

        @pl.when(high != (group - core) // 2)
        def _():
            for copy in y_lane(b_send):
                act(copy)

    def start_it(copy):
        copy.start()

    def wait_for(copy):
        copy.wait()

    def part_of(chunk):
        return slice(chunk * rows, (chunk + 1) * rows)

    def grad_tile(block, chunk):
        return pltpu.make_async_copy(
            grad_ref.at[chunk, :, aligned(block, rows)],
            mlp_buf.at[:, part_of(chunk)],
            tile_sems.at[chunk],
        )

    parts = range(3)

    def block_of(at):
        return 2 * lax.rem(at, 2) + jnp.where(at >= 2, core, 1 - core)

    for chunk in range(cols):
        grad_tile(block_of(0), chunk).start()
    for chunk in range(cols):
        b_turn[0, :, part_of(chunk)] = b_all[chunk, :, aligned(block_of(0), rows)].T
    for chunk in range(cols):
        grad_tile(block_of(0), chunk).wait()
    for chunk in range(cols):
        g_two[0, :, part_of(chunk)] = mlp_buf[:, part_of(chunk)].T
    for load in loads:
        load.wait()

    def one_block(at, unused):
        high = lax.rem(at, 2)
        is_own = at >= 2
        side = lax.rem(at, 2)
        following = block_of(jnp.minimum(at + 1, 3))

        @pl.when(inner & (at == 1))
        def _():
            relay(0, col)
            deliver(col, beside, 1, 1).start()
            relay(1, last - col)
            deliver(last - col, facing, 2, 2).start()

        @pl.when(at < 3)
        def _():
            for chunk in range(cols):
                grad_tile(following, chunk).start()

        @pl.when((at == 1) | (at == 2))
        def _():
            for part in parts:
                to_sibling(at - 1, part).wait_send()

        @pl.when(at == 3)
        def _():
            put_results(0, wait_for)

        @pl.when(is_own)
        def _():
            for part in parts:
                to_sibling(high, part).wait_recv()
                landed(high, part).start()
            for part in parts:
                landed(high, part).wait()

        @pl.when(at < 3)
        def _():
            for chunk in range(cols):
                grad_tile(following, chunk).wait()

        @pl.loop(0, cols)
        def _(step):
            lanes = aligned(step, tile)
            tokens = aligned(step, rows)

            def put(buffer, value):
                other = jnp.where(is_own, buffer[:, lanes].astype(jnp.float32), 0.0)
                buffer[:, lanes] = (other + value).astype(jnp.bfloat16)

            put(dg_buf, dot_nn(b_turn[side], wg[:, lanes]))
            b_turn[1 - side, :, tokens] = b_all[step, :, aligned(following, rows)].T
            put(du_buf, dot_nn(b_turn[side], wu[:, lanes]))
            g_two[1 - side, :, tokens] = mlp_buf[:, tokens].T
            put(u_buf, RES_MULT * dot_nn(g_two[side], wd[:, lanes]))

        @pl.when(jnp.logical_not(is_own))
        def _():
            for part in parts:
                to_sibling(at, part).start()

        @pl.when(is_own)
        def _():
            put_results(high, start_it)

        return unused

    lax.fori_loop(0, 4, one_block, 0)
    put_results(1, wait_for)
    for at in range(1, cols):
        deliver(0, beside, 1, at).wait_send()
    for at in range(1, 3):
        deliver(0, beside, at, at).wait_recv()
    for chunk in range(cols):

        @pl.when((col >= chunk) & (col < last))
        def _():
            pass_on(own_ref, chunk, col + 1, 0).wait_send()

        @pl.when((col <= chunk) & (col > 0))
        def _():
            pass_on(own_ref, chunk, col - 1, 1).wait_send()


def feed_forward(own_input, resid, grad_rows, weights, cols):
    rows, width = own_input.shape
    units = weights[0].shape[1]
    anywhere = pl.BlockSpec(memory_space=pl.ANY)
    bf16 = jnp.bfloat16
    lane = jax.ShapeDtypeStruct((2, rows // 2, units + units // 2), bf16)
    return pl.pallas_call(
        functools.partial(ffn_kernel, cols),
        out_shape=(
            jax.ShapeDtypeStruct((cols, rows, units), bf16),
            jax.ShapeDtypeStruct((cols, rows, 2 * units), bf16),
            jax.ShapeDtypeStruct((cols, rows, width), bf16),
            jax.ShapeDtypeStruct((3, rows, width), bf16),
            jax.ShapeDtypeStruct((2, rows, width), bf16),
            jax.ShapeDtypeStruct((2, 3, rows, units), bf16),
        )
        + (lane,) * 4,
        in_specs=[anywhere] * 18,
        out_specs=(anywhere,) * 10,
        scratch_shapes=[
            pltpu.VMEM((width, units), bf16),
            pltpu.VMEM((width, units), bf16),
            pltpu.VMEM((width, units), bf16),
            pltpu.VMEM((cols, rows, width), bf16),
            pltpu.VMEM((2, rows, width), bf16),
            pltpu.VMEM((2, rows, width), bf16),
            pltpu.VMEM((rows, units), bf16),
            pltpu.VMEM((rows, units), bf16),
            pltpu.VMEM((rows, units), bf16),
            pltpu.VMEM((rows, width), bf16),
            pltpu.VMEM((cols - 1, rows, width), bf16),
            pltpu.SemaphoreType.DMA((15,)),
            pltpu.SemaphoreType.DMA((2, cols)),
            pltpu.SemaphoreType.DMA((cols,)),
            pltpu.SemaphoreType.DMA((cols,)),
            pltpu.SemaphoreType.DMA((cols,)),
            pltpu.SemaphoreType.DMA((2,)),
            pltpu.SemaphoreType.DMA((2, 2, 3)),
            pltpu.SemaphoreType.DMA((8,)),
            pltpu.SemaphoreType.DMA((cols,)),
            pltpu.SemaphoreType.DMA((9,)),
        ],
        compiler_params=pltpu.CompilerParams(
            collective_id=2, has_side_effects=True, vmem_limit_bytes=60 << 20
        ),
        cost_estimate=pl.CostEstimate(
            flops=18 * cols * rows * width * units,
            bytes_accessed=800 << 20,
            transcendentals=cols * rows * units,
        ),
        name="feed_forward",
    )(own_input, resid, grad_rows, *weights)


def finish_kernel(
    cols,
    ig_ref,
    gq_ref,
    go_ref,
    gain_ref,
    out_ref,
    gin_ref,
    crossed_ref,
    sq_ref,
    so_ref,
    gsum_ref,
    q_keep,
    q_sib,
    q_a1,
    q_a2,
    q_b1,
    q_b2,
    q_z,
    o_keep,
    o_sib,
    o_a1,
    o_a2,
    o_b1,
    o_b2,
    o_z,
    gain_now,
    gain_in,
    ig_sems,
    gain_sems,
    q_sems,
    o_sems,
    qz_sems,
    oz_sems,
    cross_sems,
    local_sems,
):
    group, core, mate, row, col = place()
    pair = group - core
    high = pair // 2
    sibling = (pair + 1 - core, row, col)
    over_x = (group, 1 - row, col)
    over_y = (2 * (1 - high) + core, row, col)
    width = gin_ref.shape[2]

    def line(step):
        return lax.rem(col + step + cols, cols)

    barrier = pltpu.get_barrier_semaphore()

    def greet(device):
        pl.semaphore_signal(barrier, inc=1, device_id=device, device_id_type=MESH_IDS)

    greet(sibling)
    greet(over_x)
    greet(over_y)
    for step in range(1, cols):
        greet((mate, core, line(step)))
        greet((group, row, line(step)))

    @pl.when(core != row)
    def _():
        greet((mate, core, col))

    pl.semaphore_wait(barrier, 2 * cols + 1 + (core - row) * (core - row))

    def remote(src, dst, sems, at, device):
        return pltpu.make_async_remote_copy(
            src_ref=src,
            dst_ref=dst,
            send_sem=sems.at[0, at],
            recv_sem=sems.at[1, at],
            device_id=device,
            device_id_type=MESH_IDS,
        )

    def lanes(block, size):
        return pl.ds(pl.multiple_of(block * size, size), size)

    matrices = (
        (gq_ref, sq_ref, q_keep, q_sib, q_a1, q_a2, q_b1, q_b2, q_z, q_sems, qz_sems),
        (go_ref, so_ref, o_keep, o_sib, o_a1, o_a2, o_b1, o_b2, o_z, o_sems, oz_sems),
    )

    def moves(m):
        grads, out, keep, sib, a1, a2, b1, b2, zb, sems, z_sems = matrices[m]
        return dict(
            s0=remote(grads.at[:, 1 - core], sib, sems, 0, sibling),
            a1=remote(grads.at[:, core, 1 - row], a1, sems, 1, over_x),
            a2=remote(keep.at[1 - high, row], a2, sems, 2, over_y),
            b1=remote(sib.at[1 - high], b1, sems, 3, over_y),
            b2=remote(sib.at[high, 1 - row], b2, sems, 4, over_x),
            own=pltpu.make_async_copy(grads.at[:, core], keep, local_sems.at[m]),
        )

    copies = (moves(0), moves(1))

    def rows_plus(into, more):
        rows = into.shape[0]
        step = min(32, rows)

        @pl.loop(0, rows // step)
        def _(at):
            here = pl.ds(pl.multiple_of(at * step, step), step)
            into[here, :] = (
                into[here, :].astype(jnp.float32) + more[here, :].astype(jnp.float32)
            ).astype(into.dtype)

    def token_copy(step, at):
        return remote(
            ig_ref.at[:, lanes(line(step), width)],
            gin_ref.at[at],
            ig_sems,
            step,
            (mate, core, line(step)),
        )

    own_tokens = pltpu.make_async_copy(
        ig_ref.at[:, lanes(col, width)], gin_ref.at[col], local_sems.at[2]
    )

    cross = remote(out_ref, crossed_ref, cross_sems, 0, (mate, core, col))
    stay = pltpu.make_async_copy(out_ref, crossed_ref, local_sems.at[4])
    for m in (1, 0):
        copies[m]["s0"].start()
        copies[m]["own"].start()
    copies[1]["a1"].start()
    @pl.when(core == row)
    def _():
        own_tokens.start()
        stay.start()
        for step in range(1, cols):
            token_copy(step, col).start()

    gain_load = pltpu.make_async_copy(gain_ref, gain_now.at[0], local_sems.at[3])
    gain_load.start()
    gain_load.wait()
    near = (
        sibling,
        over_x,
        over_y,
        (group, row, col + 1 - 2 * lax.rem(col, 2)),
        (group, row, lax.rem(col + cols // 2, cols)),
    )

    def gain_round(at):
        exchange = remote(gain_now.at[at], gain_in.at[at], gain_sems, at, near[at])
        exchange.start()
        exchange.wait()
        gain_now[at + 1] = gain_now[at] + gain_in[at]

    def z_moves(m, side, source):
        grads, out, keep, sib, a1, a2, b1, b2, zb, sems, z_sems = matrices[m]
        held = (keep, sib)[side]
        wide = zb.shape[3]
        return [
            pltpu.make_async_remote_copy(
                src_ref=held.at[high, row, :, lanes(line(step), wide)],
                dst_ref=zb.at[side, line(source(step))],
                send_sem=z_sems.at[0, side, step],
                recv_sem=z_sems.at[1, side, step],
                device_id=(group, row, line(step)),
                device_id_type=MESH_IDS,
            )
            for step in range(1, cols)
        ]

    def first_sums(m):
        grads, out, keep, sib, a1, a2, b1, b2, zb, sems, z_sems = matrices[m]
        copies[m]["own"].wait()
        copies[m]["a1"].wait()
        if m == 1:
            copies[0]["a1"].start()
        rows_plus(keep.at[1 - high, row], a1.at[1 - high])
        copies[m]["a2"].start()
        copies[m]["b1"].wait()
        if m == 1:
            copies[0]["b1"].start()
        rows_plus(sib.at[high, 1 - row], b1.at[1 - row])
        copies[m]["b2"].start()

    def last_sums(m):
        grads, out, keep, sib, a1, a2, b1, b2, zb, sems, z_sems = matrices[m]
        rows_plus(keep.at[high, row], a1.at[high])
        rows_plus(sib.at[high, row], b1.at[row])
        for side, last_copy in ((0, "a2"), (1, "b2")):
            copies[m][last_copy].wait()
            rows_plus((keep, sib)[side].at[high, row], (a2, b2)[side])
            for copy in z_moves(m, side, lambda step: 0):
                copy.start()

    copies[1]["s0"].wait()
    copies[1]["b1"].start()
    gain_round(0)
    copies[0]["s0"].wait()
    first_sums(1)
    gain_round(1)
    last_sums(1)
    gain_round(2)
    first_sums(0)

    @pl.when(core != row)
    def _():
        for step in range(cols):
            token_copy(step, col).start()
        cross.start()

    gain_round(3)
    last_sums(0)
    gain_round(4)
    gsum_ref[...] = gain_now[5]
    for m in (1, 0):
        for side in range(2):
            grads, out, keep, sib, a1, a2, b1, b2, zb, sems, z_sems = matrices[m]
            for copy in z_moves(m, side, lambda step: 0):
                copy.wait_send()
            for copy in z_moves(m, side, lambda step: -step):
                copy.wait_recv()
            held = (keep, sib)[side]
            wide = zb.shape[3]
            at_core = core if side == 0 else 1 - core
            rows = zb.shape[2]
            tall = min(32, rows)

            @pl.loop(0, rows // tall)
            def _(at):
                here = pl.ds(pl.multiple_of(at * tall, tall), tall)
                total = held[high, row, here, lanes(col, wide)].astype(jnp.float32)
                for step in range(1, cols):
                    total = total + zb[side, line(-step), here, :].astype(jnp.float32)
                out[at_core, here, :] = total

    for step in range(1, cols):
        token_copy(step, line(-step)).wait_recv()
        token_copy(step, col).wait_send()

    @pl.when(core != row)
    def _():
        token_copy(0, col).wait_recv()
        token_copy(0, col).wait_send()
        cross.wait()

    @pl.when(core == row)
    def _():
        own_tokens.wait()
        stay.wait()


def finish(input_grad, grad_q, grad_o, gains, output, cols):
    anywhere = pl.BlockSpec(memory_space=pl.ANY)
    in_vmem = pl.BlockSpec(memory_space=pltpu.VMEM)
    bf16, f32 = jnp.bfloat16, jnp.float32
    length, full = input_grad.shape
    rows = grad_q.shape[0] // 8

    def buffers(wide):
        return [
            pltpu.VMEM((2, 2, rows, wide), bf16),
            pltpu.VMEM((2, 2, rows, wide), bf16),
            pltpu.VMEM((2, rows, wide), bf16),
            pltpu.VMEM((rows, wide), bf16),
            pltpu.VMEM((2, rows, wide), bf16),
            pltpu.VMEM((rows, wide), bf16),
            pltpu.VMEM((2, cols, rows, wide // cols), bf16),
        ]

    wide_q, wide_o = grad_q.shape[1], grad_o.shape[1]
    return pl.pallas_call(
        functools.partial(finish_kernel, cols),
        out_shape=(
            jax.ShapeDtypeStruct((cols, length, full // cols), bf16),
            jax.ShapeDtypeStruct(output.shape, bf16),
            jax.ShapeDtypeStruct((2, rows, wide_q // cols), f32),
            jax.ShapeDtypeStruct((2, rows, wide_o // cols), f32),
            jax.ShapeDtypeStruct(gains.shape, f32),
        ),
        in_specs=[anywhere] * 5,
        out_specs=(anywhere, anywhere, in_vmem, in_vmem, in_vmem),
        scratch_shapes=buffers(wide_q)
        + buffers(wide_o)
        + [
            pltpu.VMEM((6,) + gains.shape, f32),
            pltpu.VMEM((5,) + gains.shape, f32),
            pltpu.SemaphoreType.DMA((2, cols)),
            pltpu.SemaphoreType.DMA((2, 5)),
            pltpu.SemaphoreType.DMA((2, 5)),
            pltpu.SemaphoreType.DMA((2, 5)),
            pltpu.SemaphoreType.DMA((2, 2, cols)),
            pltpu.SemaphoreType.DMA((2, 2, cols)),
            pltpu.SemaphoreType.DMA((2, 1)),
            pltpu.SemaphoreType.DMA((5,)),
        ],
        compiler_params=pltpu.CompilerParams(
            collective_id=3, has_side_effects=True, vmem_limit_bytes=60 << 20
        ),
        cost_estimate=pl.CostEstimate(flops=0, bytes_accessed=300 << 20, transcendentals=0),
        name="finish",
    )(
        input_grad,
        grad_q.reshape(2, 2, 2, rows, wide_q),
        grad_o.reshape(2, 2, 2, rows, wide_o),
        gains,
        output,
    )


def one_sequence_body(
    tokens,
    cotangent,
    lengths,
    deal_order,
    gain_attn,
    gain_ffn,
    w_query,
    key_value_weight,
    w_out,
    w_gate_up,
    w_down,
):
    seq_group, rows_local, width_local = tokens.shape
    row_count = lax.axis_size("row")
    col_count = lax.axis_size("col")
    full_width = width_local * col_count
    slot_len = rows_local * row_count
    group, core, mate, row, col = place()
    query_half = w_query.shape[1] // 2
    kv_half = key_value_weight.shape[2] // 2
    hidden = w_down.shape[1]

    def core_half(matrix, axis):
        width = matrix.shape[axis] // 2
        return lax.dynamic_slice_in_dim(matrix, core * width, width, axis)

    def joined(mine, other, at):
        return jnp.where(
            at == 0, jnp.concatenate([mine, other]), jnp.concatenate([other, mine])
        )

    def from_sibling(value):
        return lax.ppermute(value, "dp", SIBLINGS)

    def half_rows(matrix):
        return core_half(matrix, 0)

    pack_q = jnp.concatenate(
        [
            core_half(w_query, 1),
            core_half(key_value_weight[:, 0], 1),
            core_half(key_value_weight[:, 1], 1),
        ],
        axis=1,
    )
    pack_o = core_half(w_out, 1)
    gain_one = gain_attn.astype(jnp.float32)
    gain_two = gain_ffn.astype(jnp.float32)
    own_tokens, attn_input = start_exchange(tokens, gain_one, col_count)

    length = lax.dynamic_slice_in_dim(lengths, mate * seq_group + col, 1)
    given_pos = row * rows_local + jnp.arange(rows_local, dtype=jnp.int32)
    given_lengths = lax.dynamic_slice_in_dim(lengths, group * seq_group, seq_group)
    given_live = given_pos[None, :, None] < given_lengths[:, None, None]
    everyone = lax.all_gather(cotangent, "dp", axis=0, tiled=True)
    everyone, attn_input = lax.optimization_barrier((everyone, attn_input))
    picked = pick_sequences(everyone, deal_order, group * seq_group, seq_group)
    picked = jnp.where(given_live, picked, jnp.zeros_like(picked))
    given = lax.ppermute(picked, ("dp", "row"), CROSSED)
    weights_qkv, weights_out = gather_weights(pack_q, pack_o, picked, row_count, col_count)
    given, weights_qkv = lax.optimization_barrier((given, weights_qkv))
    line_cot = lax.all_gather(given, "col", axis=2, tiled=True)
    own_grad = lax.dynamic_index_in_dim(line_cot, col, keepdims=False).astype(jnp.float32)

    w_gate_up, w_down, weights_qkv = lax.optimization_barrier((w_gate_up, w_down, weights_qkv))
    def quarter_rows(matrix):
        count = matrix.shape[0] // 4
        return lax.dynamic_slice_in_dim(matrix, (2 * core + group // 2) * count, count)

    far_gate_up = lax.ppermute(quarter_rows(w_gate_up), "row", OVER_X)
    far_down = lax.ppermute(quarter_rows(w_down), "row", OVER_X)
    own_mats = (w_gate_up[:, 0], w_gate_up[:, 1], w_down)

    cosine_table, sine_table = rope_tables(jnp.arange(slot_len, dtype=jnp.int32), HEAD_SIZE)
    cosine_table, sine_table = lax.optimization_barrier((cosine_table, sine_table))
    cosines = jnp.concatenate(
        [jnp.tile(cosine_table, (1, 6)), jnp.ones((slot_len, HEAD_SIZE), jnp.float32)], axis=1
    )
    turning = jnp.concatenate([-sine_table, sine_table], axis=1)
    sines = jnp.concatenate(
        [jnp.tile(turning, (1, 3)), jnp.zeros((slot_len, HEAD_SIZE), jnp.float32)], axis=1
    )
    own_float = own_tokens.astype(jnp.float32)
    scale_one = lax.rsqrt(jnp.mean(own_float * own_float, axis=1, keepdims=True) + EPSILON)
    projected, heads_out = attend_fast(
        length, attn_input, weights_qkv, cosines, sines, col_count
    )

    def summed_rows(partial):
        count = partial.shape[0] // 2
        mine = lax.dynamic_slice_in_dim(partial, core * count, count)
        other = lax.dynamic_slice_in_dim(partial, (1 - core) * count, count)
        return mine.astype(jnp.float32) + from_sibling(other).astype(jnp.float32)

    attn_rows = summed_rows(expand_local(heads_out, weights_out).astype(jnp.bfloat16))
    resid = own_float + RES_MULT * attn_rows
    scale_two = lax.rsqrt(jnp.mean(resid * resid, axis=1, keepdims=True) + EPSILON)
    own_ffn = (resid * scale_two * gain_two).astype(jnp.bfloat16)

    shared_gate_up = lax.ppermute(far_gate_up, "dp", OVER_Y)
    shared_down = lax.ppermute(far_down, "dp", OVER_Y)
    own_ffn, own_mats, far_gate_up, far_down, shared_gate_up, shared_down = (
        lax.optimization_barrier(
            (own_ffn, own_mats, far_gate_up, far_down, shared_gate_up, shared_down)
        )
    )
    far_mats = (far_gate_up[:, 0], far_gate_up[:, 1], far_down)
    far_mats += (shared_gate_up[:, 0], shared_gate_up[:, 1], shared_down)
    sibling_mats = tuple(from_sibling(matrix) for matrix in far_mats)
    *unused, a_keep, a_send, b_keep, b_send = feed_forward(
        own_ffn,
        resid.astype(jnp.bfloat16),
        line_cot,
        own_mats + far_mats + sibling_mats,
        col_count,
    )
    mlp_part, back_part = unused[2:4]
    grad_normed_two = jnp.sum(back_part.astype(jnp.float32), axis=0)
    out_cols = lax.psum_scatter(mlp_part, "col", scatter_dimension=2, tiled=True)

    def plus(kept, came):
        return (kept.astype(jnp.float32) + came.astype(jnp.float32)).astype(jnp.bfloat16)

    a_came = lax.ppermute(a_send, "row", OVER_X)
    b_came = lax.ppermute(b_send, "dp", OVER_Y)

    weighted_two = grad_normed_two * gain_two
    inner_two = jnp.sum(weighted_two * resid, axis=1, keepdims=True)
    grad_resid = (
        own_grad + scale_two * weighted_two - resid * scale_two**3 * inner_two / full_width
    )
    gain_two_part = jnp.sum(grad_normed_two * resid * scale_two, axis=0)
    own_attn_grad = (RES_MULT * grad_resid).astype(jnp.bfloat16)
    grad_attn = joined(own_attn_grad, from_sibling(own_attn_grad), core)
    grad_heads = contract_local(grad_attn, weights_out).astype(jnp.bfloat16)
    grad_projected = attend_back_fast(
        length, projected, grad_heads, cosines, sines, col_count
    )
    a_sum, b_sum, grad_projected = lax.optimization_barrier(
        (plus(a_keep, a_came), plus(b_keep, b_came), grad_projected)
    )
    high = group // 2

    def one_of(pair, at):
        return lax.dynamic_index_in_dim(pair, at, keepdims=False)

    a_last = lax.ppermute(one_of(a_sum, 1 - high), "dp", OVER_Y)
    b_last = lax.ppermute(one_of(b_sum, 1 - row), "row", OVER_X)
    input_partial = expand_local(grad_projected, weights_qkv).astype(jnp.bfloat16)
    grad_attn, heads_out, input_partial = lax.optimization_barrier(
        (grad_attn, heads_out, input_partial)
    )
    grad_out = token_outer(grad_attn, heads_out).astype(jnp.bfloat16)
    grad_normed_one = summed_rows(input_partial)
    attn_input, grad_normed_one = lax.optimization_barrier((attn_input, grad_normed_one))
    grad_qkv = token_outer(attn_input, grad_projected).astype(jnp.bfloat16)
    weighted_one = grad_normed_one * gain_one
    inner_one = jnp.sum(weighted_one * own_float, axis=1, keepdims=True)
    own_input_grad = (
        grad_resid
        + scale_one * weighted_one
        - own_float * scale_one**3 * inner_one / full_width
    ).astype(jnp.bfloat16)
    gain_one_part = jnp.sum(grad_normed_one * own_float * scale_one, axis=0)
    a_last, b_last, grad_qkv, own_input_grad = lax.optimization_barrier(
        (a_last, b_last, grad_qkv, own_input_grad)
    )
    a_total = one_of(a_sum, high).astype(jnp.float32) + a_last.astype(jnp.float32)
    b_total = one_of(b_sum, row).astype(jnp.float32) + b_last.astype(jnp.float32)
    sums_gate_up = jnp.stack([a_total[:, :hidden], b_total[:, :hidden]], axis=1)
    sums_down = jnp.concatenate([a_total[:, hidden:], b_total[:, hidden:]], axis=1)
    sums_gate_up, sums_down, own_input_grad = lax.optimization_barrier(
        (sums_gate_up, sums_down, own_input_grad)
    )
    gains = jnp.stack([gain_one_part, gain_two_part]).reshape(8, -1)
    given_grad, given_out, sums_q, sums_o, gain_sums = finish(
        own_input_grad, grad_qkv, grad_out, gains, out_cols, col_count
    )
    layer_out = jnp.where(given_live, given_out.astype(jnp.float32), 0.0)
    input_grad = given_grad.astype(jnp.float32)
    grad_gain_attn, grad_gain_ffn = gain_sums.reshape(2, full_width)

    def both_cores(sums):
        return jnp.concatenate([sums[0], sums[1]], axis=1)

    qk = query_half + kv_half
    out_query = both_cores(sums_q[:, :, :query_half])
    out_kv = jnp.stack(
        [
            both_cores(sums_q[:, :, query_half:qk]),
            both_cores(sums_q[:, :, qk:]),
        ],
        axis=1,
    )
    out_out = both_cores(sums_o)
    return (
        layer_out,
        input_grad,
        out_query,
        out_kv,
        out_out,
        sums_gate_up,
        sums_down,
        grad_gain_attn,
        grad_gain_ffn,
    )


def general_body(
    tokens,
    cotangent,
    lengths,
    deal_order,
    gain_attn,
    gain_ffn,
    w_query,
    key_value_weight,
    w_out,
    w_gate_up,
    w_down,
):
    seq_group, rows_local, width_local = tokens.shape
    row_count = lax.axis_size("row")
    col_count = lax.axis_size("col")
    full_width = width_local * col_count
    slot_len = rows_local * row_count
    total_rows = seq_group * rows_local
    head_size = HEAD_SIZE
    query_width = w_query.shape[1]
    kv_width = key_value_weight.shape[2]
    kv_heads = kv_width // head_size
    group_size = query_width // kv_width
    group_index = lax.axis_index("dp")
    row_index = lax.axis_index("row")
    col_index = lax.axis_index("col")
    matrices = {
        "qkv": jnp.concatenate(
            [w_query, key_value_weight.reshape(key_value_weight.shape[0], 2 * kv_width)], axis=1
        ),
        "out": w_out,
        "gate_up": w_gate_up,
        "down": w_down,
    }

    def contract_with(operand, which_one):
        return contract_rows(operand, matrices[which_one])

    def expand_with(operand, which_one):
        return expand_rows(operand, matrices[which_one])

    own_cotangent = bring_cotangent(cotangent, deal_order, group_index * seq_group)
    own_rows = tokens
    seq_lens = lax.dynamic_slice_in_dim(lengths, group_index * seq_group, seq_group)
    local_pos = row_index * rows_local + jnp.arange(rows_local, dtype=jnp.int32)
    key_pos = jnp.arange(slot_len, dtype=jnp.int32)
    live_rows = (local_pos[None, :] < seq_lens[:, None]).astype(jnp.float32).reshape(total_rows, 1)
    cosine_table, sine_table = rope_tables(jnp.tile(local_pos, seq_group), head_size)
    own_tokens = own_rows.reshape(total_rows, width_local)
    wide_float = widen_cols(own_tokens).astype(jnp.float32)
    scale_one = lax.rsqrt(jnp.mean(wide_float * wide_float, axis=1, keepdims=True) + EPSILON)
    gain_one = gain_attn.astype(jnp.float32)
    first_normed = wide_float * scale_one
    attn_input = (first_normed * gain_one).astype(jnp.bfloat16)
    projected = contract_with(attn_input, "qkv")
    query_lin = projected[:, :query_width].reshape(total_rows, query_width // head_size, head_size)
    key_lin = projected[:, query_width : query_width + kv_width].reshape(
        total_rows, kv_heads, head_size
    )
    value_lin = projected[:, query_width + kv_width :]
    query_rows = rotary_embed(query_lin, cosine_table, sine_table).astype(jnp.bfloat16)
    keys_own = (
        rotary_embed(key_lin, cosine_table, sine_table)
        .astype(jnp.bfloat16)
        .reshape(seq_group, rows_local, kv_width)
    )
    values_own = value_lin.astype(jnp.bfloat16).reshape(seq_group, rows_local, kv_width)
    all_keys, all_values = (
        lax.all_gather(keys_own, "row", axis=1, tiled=True),
        lax.all_gather(values_own, "row", axis=1, tiled=True),
    )
    query_split = query_rows.reshape(seq_group, rows_local, kv_heads, group_size, head_size)
    key_split = all_keys.reshape(seq_group, slot_len, kv_heads, head_size)
    value_split = all_values.reshape(seq_group, slot_len, kv_heads, head_size)

    def forward_seq(inputs):
        return attend(inputs, key_pos, local_pos)

    mixed_heads, row_max, row_sums = lax.map(
        forward_seq, (query_split, key_split, value_split, seq_lens)
    )
    heads_out = mixed_heads.reshape(total_rows, query_width).astype(jnp.bfloat16)
    attn_local = narrow_cols(expand_with(heads_out, "out"))
    resid = own_tokens.astype(jnp.float32) + RES_MULT * attn_local
    gain_two = lax.dynamic_slice_in_dim(
        gain_ffn.astype(jnp.float32), col_index * width_local, width_local
    )
    scale_two = lax.rsqrt(sum_over_cols(jnp.sum(resid * resid, axis=1)) / full_width + EPSILON)[
        :, None
    ]
    normed_two = resid * scale_two
    ffn_input = widen_cols((normed_two * gain_two).astype(jnp.bfloat16))
    gate_up = contract_with(ffn_input, "gate_up")
    gate = gate_up[:, 0]
    upward = gate_up[:, 1]
    sigmoid_gate = jax.nn.sigmoid(gate)
    silu_gate = gate * sigmoid_gate
    hidden = (silu_gate * upward).astype(jnp.bfloat16)
    ffn_local = narrow_cols(expand_with(hidden, "down"))
    layer_out = live_rows * (resid + RES_MULT * ffn_local)
    grad_rows = live_rows * own_cotangent.reshape(total_rows, width_local).astype(jnp.float32)
    grad_ffn = widen_cols((RES_MULT * grad_rows).astype(jnp.bfloat16))
    grad_hidden = contract_with(grad_ffn, "down")
    grad_down = token_outer(grad_ffn, hidden)
    slope = sigmoid_gate * (1.0 + gate * (1.0 - sigmoid_gate))
    grad_gate_rows = jnp.stack(
        [grad_hidden * upward * slope, grad_hidden * silu_gate], axis=1
    ).astype(jnp.bfloat16)
    grad_gate_up = token_outer(ffn_input, grad_gate_rows)
    grad_normed_two = narrow_cols(expand_with(grad_gate_rows, "gate_up"))
    weighted_two = grad_normed_two * gain_two
    inner_two = sum_over_cols(jnp.sum(weighted_two * resid, axis=1))[:, None]
    grad_resid = (
        grad_rows + scale_two * weighted_two - resid * scale_two**3 * inner_two / full_width
    )
    gain_two_part = jnp.sum(grad_normed_two * normed_two, axis=0)
    grad_attn = widen_cols((RES_MULT * grad_resid).astype(jnp.bfloat16))
    grad_heads = contract_with(grad_attn, "out").astype(jnp.bfloat16)
    grad_out = token_outer(grad_attn, heads_out)
    grad_split = grad_heads.reshape(seq_group, rows_local, kv_heads, group_size, head_size)

    def backward_seq(inputs):
        return attend_back(inputs, key_pos, local_pos)

    grad_query, grad_key, grad_value = lax.map(
        backward_seq, (query_split, key_split, value_split, grad_split, row_max, row_sums, seq_lens)
    )
    key_part, value_part = (
        lax.psum_scatter(
            grad_key.reshape(seq_group, slot_len, kv_width).astype(jnp.bfloat16),
            "row",
            scatter_dimension=1,
            tiled=True,
        ).astype(jnp.float32),
        lax.psum_scatter(
            grad_value.reshape(seq_group, slot_len, kv_width).astype(jnp.bfloat16),
            "row",
            scatter_dimension=1,
            tiled=True,
        ).astype(jnp.float32),
    )
    query_back = rotary_embed(
        grad_query.reshape(total_rows, query_width // head_size, head_size),
        cosine_table,
        -sine_table,
    ).reshape(total_rows, query_width)
    key_back = rotary_embed(
        key_part.reshape(total_rows, kv_heads, head_size), cosine_table, -sine_table
    ).reshape(total_rows, kv_width)
    grad_projected = jnp.concatenate(
        [query_back, key_back, value_part.reshape(total_rows, kv_width)], axis=1
    ).astype(jnp.bfloat16)
    grad_qkv = token_outer(attn_input, grad_projected)
    grad_normed_one = expand_with(grad_projected, "qkv")
    weighted_one = grad_normed_one * gain_one
    inner_one = jnp.sum(weighted_one * wide_float, axis=1, keepdims=True)
    input_part = scale_one * weighted_one - wide_float * scale_one**3 * inner_one / full_width
    input_grad = grad_resid + narrow_cols(input_part)
    gain_one_part = jnp.sum(grad_normed_one * first_normed, axis=0)
    gain_two_full = lax.dynamic_update_slice_in_dim(
        jnp.zeros((full_width,), jnp.float32), gain_two_part, col_index * width_local, 0
    )
    grad_gain_attn, grad_gain_ffn = lax.psum((gain_one_part, gain_two_full), ("dp", "row", "col"))
    sums_qkv, sums_out, sums_gate_up, sums_down = (
        lax.psum_scatter(
            grad_qkv.astype(jnp.bfloat16), ("dp", "row"), scatter_dimension=0, tiled=True
        ).astype(jnp.float32),
        lax.psum_scatter(
            grad_out.astype(jnp.bfloat16), ("dp", "row"), scatter_dimension=0, tiled=True
        ).astype(jnp.float32),
        lax.psum_scatter(
            grad_gate_up.astype(jnp.bfloat16), ("dp", "row"), scatter_dimension=0, tiled=True
        ).astype(jnp.float32),
        lax.psum_scatter(
            grad_down.astype(jnp.bfloat16), ("dp", "row"), scatter_dimension=0, tiled=True
        ).astype(jnp.float32),
    )
    out_query = sums_qkv[:, :query_width]
    out_kv = sums_qkv[:, query_width:].reshape(sums_qkv.shape[0], 2, kv_width)
    return (
        layer_out.reshape(seq_group, rows_local, width_local),
        input_grad.reshape(seq_group, rows_local, width_local),
        out_query,
        out_kv,
        sums_out,
        sums_gate_up,
        sums_down,
        grad_gain_attn,
        grad_gain_ffn,
    )


def body(tokens, cotangent, lengths, deal_order, gain_attn, gain_ffn, w_query, key_value_weight, *rest):
    sizes = (lax.axis_size("dp"), lax.axis_size("row"), lax.axis_size("col"))
    one_each = sizes == (4, 2, 4) and tokens.shape[0] == sizes[2]
    pairs = w_query.shape[1] == 8 * HEAD_SIZE and key_value_weight.shape[2] == 2 * HEAD_SIZE
    chosen = one_sequence_body if one_each and pairs else general_body
    return chosen(
        tokens, cotangent, lengths, deal_order, gain_attn, gain_ffn, w_query, key_value_weight, *rest
    )


def solution(mesh):
    placed = (
        P("dp", "row", "col"),
        P("dp", "row", "col"),
        P(),
        P(),
        P(),
        P(),
        P("row", "col"),
        P("row", None, "col"),
        P("row", "col"),
        P("row", None, "col"),
        P("row", "col"),
    )
    return jax.shard_map(
        body,
        mesh=mesh,
        in_specs=placed,
        out_specs=(
            P("dp", "row", "col"),
            P("dp", "row", "col"),
            P(("dp", "row"), "col"),
            P(("dp", "row"), None, "col"),
            P(("dp", "row"), "col"),
            P(("dp", "row"), None, "col"),
            P(("dp", "row"), "col"),
            P(),
            P(),
        ),
        check_vma=False,
    )
```
